32 devices in a mesh: dp: 4 (over z), expert: 8 (over y, x, core).
Axes of the slice: x: 2, y: 2, z: 4, core: 2. Of those that a mesh axis runs over, the one named last changes fastest.
Arguments:
- tokens: bfloat16 [4096, 2048], P(('dp', 'expert')), may hold values from -6 to 6
- cotangent: bfloat16 [4096, 2048], P(('dp', 'expert')), may hold values from -6 to 6
- lengths: int32 [32, 3], P(('dp', 'expert')), may hold values from 1 to 64, 128 in all within a row
- routes: int32 [4096, 8], P(('dp', 'expert')), may hold values from 0 to 63, all different within a row; in each aligned block of 128 rows (0 to 127, 128 to 255, ...) at most 24 rows name the same one
- w_query: bfloat16 [2048, 2048], P(('dp', 'expert')), may hold values from -0.125 to 0.125
- w_key: bfloat16 [2048, 2048], P(('dp', 'expert')), may hold values from -0.125 to 0.125
- w_value: bfloat16 [2048, 2048], P(('dp', 'expert')), may hold values from -0.125 to 0.125
- w_out: bfloat16 [2048, 2048], P(('dp', 'expert')), may hold values from -0.375 to 0.375
- w_router: bfloat16 [2048, 64], P(('dp', 'expert')), may hold values from -0.0625 to 0.0625
- gain_attn: bfloat16 [2048], P(('dp', 'expert')), may hold values from 0.5 to 1.5
- gain_query: bfloat16 [2048], P(('dp', 'expert')), may hold values from 0.5 to 1.5
- gain_key: bfloat16 [2048], P(('dp', 'expert')), may hold values from 0.5 to 1.5
- gain_mlp: bfloat16 [2048], P(('dp', 'expert')), may hold values from 0.5 to 1.5
- w_gate: bfloat16 [64, 2048, 1024], P('expert', 'dp'), may hold values from -0.125 to 0.125
- w_up: bfloat16 [64, 2048, 1024], P('expert', 'dp'), may hold values from -0.125 to 0.125
- w_down: bfloat16 [64, 1024, 2048], P('expert', 'dp'), may hold values from -2.5 to 2.5
Outputs:
- output: bfloat16 [4096, 2048], P(('dp', 'expert'))
- grad_tokens: float32 [4096, 2048], P(('dp', 'expert'))
- grad_query: float32 [2048, 2048], P(('dp', 'expert'))
- grad_key: float32 [2048, 2048], P(('dp', 'expert'))
- grad_value: float32 [2048, 2048], P(('dp', 'expert'))
- grad_out: float32 [2048, 2048], P(('dp', 'expert'))
- grad_router: float32 [2048, 64], P(('dp', 'expert'))
- grad_gain_attn: float32 [2048], P(('dp', 'expert'))
- grad_gain_query: float32 [2048], P(('dp', 'expert'))
- grad_gain_key: float32 [2048], P(('dp', 'expert'))
- grad_gain_mlp: float32 [2048], P(('dp', 'expert'))
- grad_gate: float32 [64, 2048, 1024], P('expert', 'dp')
- grad_up: float32 [64, 2048, 1024], P('expert', 'dp')
- grad_down: float32 [64, 1024, 2048], P('expert', 'dp')
The draws below stay inside these ranges and needn't reach their ends.
Inputs may be any that keep to these rules, and one draw needn't show every extreme that they name: The lengths of one device sum to 128; the longest of each device is exactly 64. `routes`: a token names 8 different experts; among the tokens of one device no expert is named more than 24 times, a bound that some block reaches.
All inputs are finite; a program needn't handle non-finite values.
Results may differ from the reference program's by a relative error of at most 0.015.
Values may be sent and summed in bfloat16 or wider, within the bound.
A program may use at most 640 MiB of HBM per device.

```python
import math
from functools import partial
import jax
import jax.numpy as jnp
import numpy as np
from jax import lax

D = 2048
HEADS = 16
HD = 128
EXPERTS = 64
FF = 1024
TOPK = 8
TOK_DEV = 128
NSEQ = 3
CAP = 24
GROUPS = 32
TOKENS = 4096
N_DP = 4
N_EXPERT = 8


def block_scale(own_key, shape, shards, least, high):
    loudness = 1.0
    for axis_at, parts in shards:
        draws = jax.random.uniform(jax.random.fold_in(jax.random.fold_in(own_key, 6), axis_at), (parts,), jnp.float32, least / len(shards), high / len(shards))
        loudness = loudness * jnp.repeat(jnp.exp(draws), shape[axis_at] // parts).reshape((-1,) + (1,) * (len(shape) - 1 - axis_at))
    return loudness


def profile(number_of, total, limit, skew):
    portions = [(1 << 20) // math.isqrt(grade ** skew) + 1 for grade in range(2, number_of + 1)]
    rest, given = total - limit - (number_of - 1), [1] * (number_of - 1)
    while rest > 0:
        movable = [i for i in range(number_of - 1) if given[i] < limit]
        mass, budget = sum([portions[i] for i in movable]), rest
        for i in movable:
            more = min(limit - given[i], max(1, budget * portions[i] // mass), rest)
            given[i] = given[i] + more
            rest = rest - more
    return np.array([limit] + given)


def ragged(own_key, number_of, total, reach, slope):
    if number_of == 2:
        one = jax.random.randint(own_key, (), max(1, total - reach), min(reach, total - 1) + 1)
        return jnp.stack([one, total - one])
    tallies = jnp.asarray(profile(number_of, total, reach, slope), jnp.int32)
    pairs = (number_of - 1) // 2
    giver, taker = tallies[1:1 + 2 * pairs:2], tallies[2:2 + 2 * pairs:2]
    room = jnp.minimum(giver - 1, reach - taker)
    moved = jax.random.randint(jax.random.fold_in(own_key, 1), (pairs,), 0, 1 << 20) % (room + 1)
    tallies = tallies.at[1:1 + 2 * pairs:2].set(giver - moved).at[2:2 + 2 * pairs:2].set(taker + moved)
    return tallies[jax.random.permutation(jax.random.fold_in(own_key, 2), number_of)]


def assign_block(key, own, number, rows, amount, top, most, slope):
    order = jax.random.permutation(key, amount)
    heavy_load, usual = portions_of(amount, rows * top, most, slope, True), portions_of(amount, rows * top, most, slope, False)
    places = jnp.arange(amount)

    def named(sizes, turn):
        used = int((sizes > 0).sum())
        fixed = max(1, used // 4)
        moved = fixed + (places - fixed + turn * (used - fixed)) % max(1, amount - fixed)
        return jnp.zeros((amount,), jnp.int32).at[order[jnp.where(places < fixed, places, moved)]].set(jnp.asarray(sizes, jnp.int32))

    sizes = jnp.where(number % 4 == 0, named(heavy_load, number // 4), named(usual, number - number // 4 - 1))
    mixed = jax.random.permutation(jax.random.fold_in(own, 3), amount)
    giver, taker = mixed[0:amount // 2 * 2:2], mixed[1:amount // 2 * 2:2]
    room = jnp.minimum(sizes[giver] - 1, most - sizes[taker]) // 2
    room = jnp.where((giver == order[0]) | (taker == order[0]) | (sizes[taker] == 0), 0, jnp.maximum(room, 0))
    moved = jax.random.randint(jax.random.fold_in(own, 4), (amount // 2,), 0, 1 << 20) % (room + 1)
    sizes = sizes.at[giver].add(-moved).at[taker].add(moved)
    members = jnp.searchsorted(jnp.cumsum(sizes), jnp.arange(rows * top), side="right").astype(jnp.int32)
    listing = members.reshape(top, rows).T
    listing = listing[jax.random.permutation(jax.random.fold_in(own, 1), rows)]
    turn = jax.random.randint(jax.random.fold_in(own, 2), (rows, 1), 0, top)
    return jnp.take_along_axis(listing, (jnp.arange(top)[None, :] + turn) % top, axis=1)


def portions_of(number_of, total, reach, lean, full):
    weights = [(1 << 20) // math.isqrt(grade ** lean) + 1 for grade in range(1, number_of + 1)]
    largest = reach if full else min(reach, max(-(-total // number_of), total * weights[0] // sum(weights)))
    least = 1 if total - largest >= number_of - 1 else 0
    given, surplus = [largest] + [least] * (number_of - 1), total - largest - least * (number_of - 1)
    while surplus > 0:
        movable = [i for i in range(1, number_of) if given[i] < largest] or [i for i in range(1, number_of) if given[i] < reach]
        pool, remaining = sum([weights[i] for i in movable]), surplus
        for i in movable:
            extra = min(reach - given[i], max(1, remaining * weights[i] // pool), surplus)
            given[i] = given[i] + extra
            surplus = surplus - extra
    return np.array(given)


def bell_draw(own_key, dims, deviation, limit, pieces=(), held_as=jnp.bfloat16):
    loudness = block_scale(own_key, dims, pieces, -0.22, 0.18) if pieces else 1.0
    values = jax.random.normal(own_key, dims, jnp.float32) * deviation * loudness
    return jnp.minimum(jnp.maximum(values, -limit), limit).astype(held_as)


def setup_inputs(seed: int = 0) -> dict:
    streams_of = jax.random.split(jax.random.key(seed), 17)
    tokens = bell_draw(streams_of[0], (TOKENS, D), 1.0, 6.0, ((0, 32),))
    cotangent = bell_draw(streams_of[1], (TOKENS, D), 1.0, 6.0, ((0, 32),))
    lengths = jax.vmap(lambda own: ragged(own, NSEQ, TOK_DEV, TOK_DEV // 2, 2))(jax.random.split(streams_of[2], (N_DP * N_EXPERT))).reshape((N_DP * N_EXPERT, NSEQ)).astype(jnp.int32)
    routes_keys = jax.random.split(jax.random.fold_in(streams_of[3], 1), TOKENS // TOK_DEV)
    routes_turns = jax.random.permutation(jax.random.fold_in(streams_of[3], 3), TOKENS // TOK_DEV)
    routes = jax.vmap(lambda own, number: assign_block(jax.random.fold_in(streams_of[3], 2), own, number, TOK_DEV, EXPERTS, TOPK, CAP, 1))(routes_keys, routes_turns).reshape((TOKENS, TOPK))
    w_query = bell_draw(streams_of[4], (D, D), D ** -0.5, 0.125, ((0, 32),))
    w_key = bell_draw(streams_of[5], (D, D), D ** -0.5, 0.125, ((0, 32),))
    w_value = bell_draw(streams_of[6], (D, D), D ** -0.5, 0.125, ((0, 32),))
    w_out = bell_draw(streams_of[7], (D, D), (D // 8) ** -0.5, 0.375, ((0, 32),))
    w_router = bell_draw(streams_of[8], (D, EXPERTS), (4 * D) ** -0.5, 0.0625, ((0, 32),))
    gain_attn = jnp.clip(1.0 + 0.1 * jax.random.normal(streams_of[9], (D,), jnp.float32), 0.5, 1.5).astype(jnp.bfloat16)
    gain_query = jnp.clip(1.0 + 0.1 * jax.random.normal(streams_of[10], (D,), jnp.float32), 0.5, 1.5).astype(jnp.bfloat16)
    gain_key = jnp.clip(1.0 + 0.1 * jax.random.normal(streams_of[11], (D,), jnp.float32), 0.5, 1.5).astype(jnp.bfloat16)
    gain_mlp = jnp.clip(1.0 + 0.1 * jax.random.normal(streams_of[12], (D,), jnp.float32), 0.5, 1.5).astype(jnp.bfloat16)
    w_gate = bell_draw(streams_of[13], (EXPERTS, D, FF), D ** -0.5, 0.125, ((0, 8), (1, 4)))
    w_up = bell_draw(streams_of[14], (EXPERTS, D, FF), D ** -0.5, 0.125, ((0, 8), (1, 4)))
    w_down = bell_draw(streams_of[15], (EXPERTS, FF, D), (FF // 256 + 1) ** -0.5, 2.5, ((0, 8), (1, 4)))
    return dict(tokens=tokens, cotangent=cotangent, lengths=lengths, routes=routes, w_query=w_query, w_key=w_key, w_value=w_value, w_out=w_out, w_router=w_router, gain_attn=gain_attn, gain_query=gain_query, gain_key=gain_key, gain_mlp=gain_mlp, w_gate=w_gate, w_up=w_up, w_down=w_down)


@jax.custom_vjp
def low(v):
    return lax.optimization_barrier(v.astype(jnp.bfloat16)).astype(jnp.float32)

@jax.custom_vjp
def low_back(v):
    return v

def low_keep(v):
    return (low(v), None)

def low_pass(kept, grad):
    return (grad,)

def back_keep(v):
    return (v, None)

def back_low(kept, grad):
    return (low(grad),)
low.defvjp(low_keep, low_pass)
low_back.defvjp(back_keep, back_low)
eps = 1e-05
highest = lax.Precision.HIGHEST

def mult(left, right):
    return jnp.dot(left, right, precision=highest, preferred_element_type=jnp.float32)

def rms_norm(values, gain):
    return values * lax.rsqrt(lax.optimization_barrier(jnp.mean(values * values, axis=-1, keepdims=True)) + eps) * gain

def layout(lengths_row):
    places = jnp.arange(TOK_DEV, dtype=jnp.int32)
    ends = jnp.cumsum(lengths_row, dtype=jnp.int32)
    passed = (places[:, None] >= ends[None, :]).astype(jnp.int32)
    segment = lax.optimization_barrier(jnp.sum(passed, axis=1, dtype=jnp.int32))
    start = lax.optimization_barrier(jnp.sum(passed * lengths_row[None, :], axis=1, dtype=jnp.int32))
    return (segment, places - start)

def angles(position):
    half = HD // 2
    freq = 10000.0 ** (-2.0 * jnp.arange(half, dtype=jnp.float32) / HD)
    angle = position.astype(jnp.float32)[:, None] * freq[None, :]
    return (jnp.cos(angle)[:, None, :], jnp.sin(angle)[:, None, :])

def rotate(values, cosine, sine):
    count = values.shape[0]
    heads = values.reshape(count, HEADS, HD)
    half = HD // 2
    first = heads[..., :half]
    second = heads[..., half:]
    turned = jnp.concatenate([first * cosine - second * sine, second * cosine + first * sine], axis=-1)
    return turned.reshape(count, D)

def attend_block(items):
    query, key, value, segment = items
    places = jnp.arange(TOK_DEV, dtype=jnp.int32)
    allowed = (segment[:, None] == segment[None, :]) & (places[None, :] <= places[:, None])
    query_heads = query.reshape(TOK_DEV, HEADS, HD)
    key_heads = key.reshape(TOK_DEV, HEADS, HD)
    value_heads = value.reshape(TOK_DEV, HEADS, HD)
    scores = jnp.einsum('qhd,khd->hqk', query_heads, key_heads, precision=highest) * HD ** (-0.5)
    scores = low_back(scores)
    scores = jnp.where(allowed[None], scores, -1e+30)
    probs = low(jax.nn.softmax(scores, axis=-1))
    return jnp.einsum('hqk,khd->qhd', probs, value_heads, precision=highest).reshape(TOK_DEV, D)

def slot_table(routes):
    flat = routes.reshape(GROUPS, TOK_DEV * TOPK)
    hits = (flat[:, :, None] == jnp.arange(EXPERTS, dtype=jnp.int32)[None, None, :]).astype(jnp.int32)
    before = jnp.cumsum(hits, axis=1, dtype=jnp.int32) - hits
    slot = lax.optimization_barrier(jnp.sum(before * hits, axis=2, dtype=jnp.int32))
    entry = jnp.arange(GROUPS * TOK_DEV * TOPK, dtype=jnp.int32).reshape(GROUPS, TOK_DEV * TOPK)
    group = jnp.broadcast_to(jnp.arange(GROUPS, dtype=jnp.int32)[:, None], flat.shape)
    table = jnp.full((GROUPS, EXPERTS, CAP), -1, jnp.int32).at[group, flat, slot].set(entry)
    return jnp.transpose(table, (1, 0, 2)).reshape(EXPERTS, GROUPS * CAP)

def expert_part(normed, gate_flat, items):
    weight_gate, weight_up, weight_down, chosen = items
    filled = chosen >= 0
    entry = jnp.where(filled, chosen, 0)
    token = entry // TOPK
    keep = filled.astype(jnp.float32)
    rows = low_back(normed[token] * keep[:, None])
    gate_mid = low_back(mult(rows, weight_gate))
    up_mid = low_back(mult(rows, weight_up))
    hidden = low(jax.nn.silu(gate_mid) * up_mid)
    result = low(low_back(mult(hidden, weight_down)))
    weighted = result * (gate_flat[entry] * keep)[:, None]
    return jnp.zeros((TOKENS, D), jnp.float32).at[token].add(weighted)

def mixture(normed, gate_flat, w_gate, w_up, w_down, table):
    part = jax.checkpoint(partial(expert_part, normed, gate_flat))

    def step(total, items):
        return (total + part(items), None)
    total, unused = lax.scan(step, jnp.zeros((TOKENS, D), jnp.float32), (w_gate, w_up, w_down, table))
    return total

def blocks(values):
    return values.reshape(GROUPS, TOK_DEV, D)

def forward(tokens, w_query, w_key, w_value, w_out, w_router, gain_attn, gain_query, gain_key, gain_mlp, w_gate, w_up, w_down, segment, cosine, sine, routes, table):
    normed = low(rms_norm(tokens, gain_attn))
    query = low(rotate(rms_norm(low_back(mult(normed, w_query)), gain_query), cosine, sine))
    key = low(rotate(rms_norm(low_back(mult(normed, w_key)), gain_key), cosine, sine))
    value = low(low_back(mult(normed, w_value)))
    attended = lax.map(jax.checkpoint(attend_block), (blocks(query), blocks(key), blocks(value), segment))
    attended = low(low_back(attended.reshape(TOKENS, D)))
    middle = tokens + low_back(mult(attended, w_out))
    normed_mlp = low(rms_norm(middle, gain_mlp))
    router = jax.nn.softmax(low_back(mult(normed_mlp, w_router)), axis=-1)
    gate_flat = jnp.take_along_axis(router, routes, axis=1).reshape(TOKENS * TOPK)
    return middle + mixture(normed_mlp, gate_flat, w_gate, w_up, w_down, table)

def reference(tokens, cotangent, lengths, routes, w_query, w_key, w_value, w_out, w_router, gain_attn, gain_query, gain_key, gain_mlp, w_gate, w_up, w_down):
    segment, position = jax.vmap(layout)(lengths)
    cosine, sine = angles(position.reshape(TOKENS))
    table = slot_table(routes)
    floats = [arr.astype(jnp.float32) for arr in (tokens, w_query, w_key, w_value, w_out, w_router, gain_attn, gain_query, gain_key, gain_mlp, w_gate, w_up, w_down)]

    def apply(*values):
        return forward(*values, segment, cosine, sine, routes, table)
    output, pullback = jax.vjp(apply, *floats)
    grads = pullback(cotangent.astype(jnp.float32))
    return (output.astype(jnp.bfloat16), grads[0], grads[1], grads[2], grads[3], grads[4], grads[5], grads[6], grads[7], grads[8], grads[9], grads[10], grads[11], grads[12])
```

```python
import functools

import jax
import jax.numpy as jnp
from jax import lax
from jax.sharding import PartitionSpec as P

D = 2048
HEADS = 16
HD = 128
TOPK = 8
CAP = 24


eps = 1e-05


def product(left, right, form):
    return jnp.einsum(form, left, right, preferred_element_type=jnp.float32)


def rms_forward(values, gain):
    inverse = lax.rsqrt(jnp.mean(values * values, axis=-1, keepdims=True) + eps)
    return (values * inverse * gain, inverse)


def rms_backward(values, inverse, gain, grad):
    scaled = grad * gain
    inner = jnp.mean(scaled * values, axis=-1, keepdims=True)
    grad_values = inverse * scaled - values * (inverse * inverse * inverse) * inner
    grad_gain = jnp.sum(grad * values * inverse, axis=0)
    return (grad_values, grad_gain)


def layout(lengths_row, count):
    places = jnp.arange(count, dtype=jnp.int32)
    ends = jnp.cumsum(lengths_row, dtype=jnp.int32)
    passed = (places[:, None] >= ends[None, :]).astype(jnp.int32)
    segment = jnp.sum(passed, axis=1, dtype=jnp.int32)
    start = jnp.sum(passed * lengths_row[None, :], axis=1, dtype=jnp.int32)
    return (segment, places - start, places)


def rotate(values, cosine, sine):
    count = values.shape[0]
    heads = values.reshape(count, HEADS, HD)
    half = HD // 2
    first = heads[..., :half]
    second = heads[..., half:]
    turned = jnp.concatenate(
        [first * cosine - second * sine, second * cosine + first * sine], axis=-1
    )
    return turned.reshape(count, D)


def spread(weights, axis, size):
    me = lax.axis_index(axis)
    experts, rows, columns = weights[0].shape
    part = columns // size
    whole = jnp.zeros((experts, size, rows, len(weights) * part), weights[0].dtype)
    for step in range(size):
        to = (me + step) % size
        piece = jnp.concatenate(
            [lax.dynamic_slice_in_dim(one, to * part, part, 2) for one in weights], axis=2
        )
        if step:
            piece = lax.ppermute(piece, axis, [(i, (i + step) % size) for i in range(size)])
        whole = lax.dynamic_update_slice_in_dim(whole, piece[:, None], (me - step) % size, 1)
    return whole.reshape(experts, size * rows, len(weights) * part)


def collect(grads, axis, size, number):
    me = lax.axis_index(axis)
    experts, rows, columns = grads.shape
    rows = rows // size
    part = columns // number
    wholes = [jnp.zeros((experts, rows, size, part), grads.dtype) for i in range(number)]
    for step in range(size):
        to = (me + step) % size
        piece = lax.dynamic_slice_in_dim(grads, to * rows, rows, 1)
        if step:
            piece = lax.ppermute(piece, axis, [(i, (i + step) % size) for i in range(size)])
        at = (me - step) % size
        wholes = [
            lax.dynamic_update_slice_in_dim(
                one, piece[:, :, None, i * part : (i + 1) * part], at, 2
            )
            for i, one in enumerate(wholes)
        ]
    return [one.reshape(experts, rows, size * part) for one in wholes]


def shards(
    n_dp,
    n_expert,
    tokens,
    cotangent,
    lengths,
    routes,
    w_query,
    w_key,
    w_value,
    w_out,
    w_router,
    gain_attn,
    gain_query,
    gain_key,
    gain_mlp,
    w_gate,
    w_up,
    w_down,
):
    both = ("dp", "expert")
    groups = n_dp * n_expert
    bf16 = jnp.bfloat16
    number = w_gate.shape[0]
    ff = w_gate.shape[2]
    part = ff // n_dp
    experts_all = w_router.shape[1]
    width = 128
    small = jnp.concatenate(
        [
            w_router,
            gain_attn[:, None],
            gain_query[:, None],
            gain_key[:, None],
            gain_mlp[:, None],
            jnp.zeros((w_router.shape[0], width - experts_all - 4), bf16),
        ],
        axis=1,
    )
    query_small = lax.all_gather(
        jnp.concatenate([w_query, small], axis=1), both, axis=0, tiled=True
    )
    query_weight = query_small[:, :D]
    small_all = query_small[:, D:]
    key_weight = lax.all_gather(w_key, both, axis=0, tiled=True)
    value_weight = lax.all_gather(w_value, both, axis=0, tiled=True)
    out_weight = lax.all_gather(w_out, both, axis=0, tiled=True)
    routes_all = lax.all_gather(routes, both, axis=0, tiled=True)
    cotangent_all = lax.all_gather(cotangent, both, axis=0, tiled=True)
    gate_up = spread([w_gate, w_up], "dp", n_dp)
    router_weight = small_all[:, :experts_all]
    gains = small_all[:, experts_all : experts_all + 4].astype(jnp.float32)
    attn_gain, query_gain, key_gain, mlp_gain = (gains[:, i] for i in range(4))
    inputs = tokens.astype(jnp.float32)
    count = inputs.shape[0]
    segment, position, places = layout(lengths[0], count)
    half = HD // 2
    freq = 10000.0 ** (-2.0 * jnp.arange(half, dtype=jnp.float32) / HD)
    angle = position.astype(jnp.float32)[:, None] * freq[None, :]
    cosine = jnp.cos(angle)[:, None, :]
    sine = jnp.sin(angle)[:, None, :]
    scale = HD ** (-0.5)
    normed, attn_inverse = rms_forward(inputs, attn_gain)
    normed_low = normed.astype(bf16)
    query_raw = product(normed_low, query_weight, "td,de->te")
    key_raw = product(normed_low, key_weight, "td,de->te")
    value_low = product(normed_low, value_weight, "td,de->te").astype(bf16)
    query_normed, query_inverse = rms_forward(query_raw, query_gain)
    key_normed, key_inverse = rms_forward(key_raw, key_gain)
    query_low = rotate(query_normed, cosine, sine).astype(bf16).reshape(count, HEADS, HD)
    key_low = rotate(key_normed, cosine, sine).astype(bf16).reshape(count, HEADS, HD)
    value_heads = value_low.reshape(count, HEADS, HD)
    allowed = (segment[:, None] == segment[None, :]) & (places[None, :] <= places[:, None])
    scores = product(query_low, key_low, "qhd,khd->hqk") * scale
    scores = jnp.where(allowed[None], scores, -1e30)
    probs = jax.nn.softmax(scores, axis=-1)
    probs_low = probs.astype(bf16)
    attended_low = product(probs_low, value_heads, "hqk,khd->qhd").reshape(count, D).astype(bf16)
    middle = inputs + product(attended_low, out_weight, "td,de->te")
    mlp_normed, mlp_inverse = rms_forward(middle, mlp_gain)
    mlp_low = mlp_normed.astype(bf16)
    router = jax.nn.softmax(product(mlp_low, router_weight, "td,de->te"), axis=-1)

    mlp_all = lax.all_gather(mlp_low, both, axis=0, tiled=True)
    router_all = jax.nn.softmax(product(mlp_all, router_weight, "td,de->te"), axis=-1)
    first = lax.axis_index("expert") * number
    own = lax.dynamic_slice_in_dim(router_all, first, number, 1).reshape(groups, count, number)
    names = first + jnp.arange(number, dtype=jnp.int32)
    hit = jnp.any(
        routes_all.reshape(groups, count, TOPK)[..., None] == names[None, None, None, :], axis=2
    )
    before = jnp.tril(jnp.ones((count, count), bf16), -1)
    slot = product(before, hit.astype(bf16), "ts,bse->bte").astype(jnp.int32)
    slot = jnp.where(hit, slot, -1)
    slots = jnp.arange(CAP, dtype=jnp.int32)
    table = jnp.transpose(slot, (0, 2, 1))[:, :, None, :] == slots[None, None, :, None]
    pick = table.astype(bf16)
    gates = jnp.sum(
        jnp.where(table, jnp.transpose(own, (0, 2, 1))[:, :, None, :], 0.0), axis=3
    )
    rows = product(pick, mlp_all.reshape(groups, count, D), "bect,btd->becd").astype(bf16)
    grows = product(pick, cotangent_all.reshape(groups, count, D), "bect,btd->becd").astype(bf16)
    mids = product(rows, gate_up, "becd,edf->becf")
    gate_mid = mids[..., :part]
    up_mid = mids[..., part:]
    sigmoid = jax.nn.sigmoid(gate_mid)
    silu = gate_mid * sigmoid
    hidden = silu * up_mid
    hidden_low = hidden.astype(bf16)
    result = product(hidden_low, w_down, "becf,efd->becd")
    weighted = (result * gates[..., None]).astype(bf16)
    part_out = product(pick, weighted, "bect,becd->btd").reshape(groups * count, D).astype(bf16)
    grad_plain = product(grows, w_down, "becd,efd->becf")
    grad_gates = jnp.sum(grad_plain * hidden_low.astype(jnp.float32), axis=3)
    grad_hidden = grad_plain * gates[..., None]
    grad_gate_low = (grad_hidden * up_mid * sigmoid * (1.0 + gate_mid * (1.0 - sigmoid))).astype(
        bf16
    )
    grad_up_low = (grad_hidden * silu).astype(bf16)
    grad_mids = jnp.concatenate([grad_gate_low, grad_up_low], axis=3)
    grad_rows = product(grad_mids, gate_up, "becf,edf->becd").astype(bf16)
    part_grad = product(pick, grad_rows, "bect,becd->btd").reshape(groups * count, D)
    part_probs = jnp.sum(
        jnp.where(table, grad_gates[..., None], 0.0), axis=2
    )
    part_probs = jnp.transpose(part_probs, (0, 2, 1)).reshape(groups * count, number)
    spare = jnp.zeros((groups * count, width), jnp.float32)
    part_probs = lax.dynamic_update_slice_in_dim(spare, part_probs, first, 1)
    back = lax.psum_scatter(
        jnp.concatenate([part_grad, part_probs], axis=1).astype(bf16),
        both,
        scatter_dimension=0,
        tiled=True,
    ).astype(jnp.float32)
    grad_down_part = product((hidden * gates[..., None]).astype(bf16), grows, "becf,becd->efd")
    grad_gate_up = product(rows, grad_mids, "becd,becf->edf").astype(bf16)
    grad_gate_part, grad_up_part = collect(grad_gate_up, "dp", n_dp, 2)
    grad_gate_part = grad_gate_part.astype(jnp.float32)
    grad_up_part = grad_up_part.astype(jnp.float32)
    summed = lax.psum_scatter(part_out, both, scatter_dimension=0, tiled=True)
    output = (middle + summed.astype(jnp.float32)).astype(bf16)

    grad_final = cotangent.astype(jnp.float32)
    grad_mlp = back[:, :D]
    grad_router_probs = back[:, D : D + experts_all]
    grad_logits = router * (
        grad_router_probs - jnp.sum(router * grad_router_probs, axis=1, keepdims=True)
    )
    grad_logits_low = grad_logits.astype(bf16)
    grad_router_full = product(mlp_low, grad_logits_low, "td,te->de")
    grad_mlp = grad_mlp + product(grad_logits_low, router_weight, "te,de->td")
    grad_middle_part, grad_mlp_gain = rms_backward(middle, mlp_inverse, mlp_gain, grad_mlp)
    grad_middle = grad_final + grad_middle_part
    grad_branch_low = grad_middle.astype(bf16)
    grad_out_full = product(attended_low, grad_branch_low, "td,te->de")
    grad_attended = (
        product(grad_branch_low, out_weight, "te,de->td").astype(bf16).reshape(count, HEADS, HD)
    )
    grad_weights = product(grad_attended, value_heads, "qhd,khd->hqk")
    grad_scores = probs * (grad_weights - jnp.sum(probs * grad_weights, axis=-1, keepdims=True))
    grad_scores_low = grad_scores.astype(bf16)
    grad_query_turn = product(grad_scores_low, key_low, "hqk,khd->qhd").reshape(count, D) * scale
    grad_key_turn = product(grad_scores_low, query_low, "hqk,qhd->khd").reshape(count, D) * scale
    grad_value_low = (
        product(probs_low, grad_attended, "hqk,qhd->khd").reshape(count, D).astype(bf16)
    )
    grad_query_raw, grad_query_gain = rms_backward(
        query_raw, query_inverse, query_gain, rotate(grad_query_turn, cosine, -sine)
    )
    grad_key_raw, grad_key_gain = rms_backward(
        key_raw, key_inverse, key_gain, rotate(grad_key_turn, cosine, -sine)
    )
    grad_query_low = grad_query_raw.astype(bf16)
    grad_key_low = grad_key_raw.astype(bf16)
    grad_query_full = product(normed_low, grad_query_low, "td,te->de")
    grad_key_full = product(normed_low, grad_key_low, "td,te->de")
    grad_value_full = product(normed_low, grad_value_low, "td,te->de")
    grad_normed = (
        product(grad_query_low, query_weight, "te,de->td")
        + product(grad_key_low, key_weight, "te,de->td")
        + product(grad_value_low, value_weight, "te,de->td")
    )
    grad_inputs_part, grad_attn_gain = rms_backward(inputs, attn_inverse, attn_gain, grad_normed)
    grad_inputs = grad_middle + grad_inputs_part

    def scattered(value):
        return lax.psum_scatter(value.astype(bf16), both, scatter_dimension=0, tiled=True).astype(
            jnp.float32
        )

    grad_out_part = scattered(grad_out_full)
    grad_value_part = scattered(grad_value_full)
    grad_key_part = scattered(grad_key_full)
    small_grads = jnp.concatenate(
        [
            grad_router_full,
            grad_attn_gain[:, None],
            grad_query_gain[:, None],
            grad_key_gain[:, None],
            grad_mlp_gain[:, None],
            jnp.zeros((D, width - experts_all - 4), jnp.float32),
        ],
        axis=1,
    )
    query_part = scattered(jnp.concatenate([grad_query_full, small_grads], axis=1))
    grad_query_part = query_part[:, :D]
    grad_router_part = query_part[:, D : D + experts_all]
    gain_parts = [query_part[:, D + experts_all + i] for i in range(4)]
    return (
        output,
        grad_inputs,
        grad_query_part,
        grad_key_part,
        grad_value_part,
        grad_out_part,
        grad_router_part,
        gain_parts[0],
        gain_parts[1],
        gain_parts[2],
        gain_parts[3],
        grad_gate_part,
        grad_up_part,
        grad_down_part,
    )


def solution(mesh):
    return jax.shard_map(
        functools.partial(shards, mesh.shape["dp"], mesh.shape["expert"]),
        mesh=mesh,
        in_specs=(
            P(("dp", "expert"), None),
            P(("dp", "expert"), None),
            P(("dp", "expert"), None),
            P(("dp", "expert"), None),
            P(("dp", "expert"), None),
            P(("dp", "expert"), None),
            P(("dp", "expert"), None),
            P(("dp", "expert"), None),
            P(("dp", "expert"), None),
            P(("dp", "expert")),
            P(("dp", "expert")),
            P(("dp", "expert")),
            P(("dp", "expert")),
            P("expert", "dp", None),
            P("expert", "dp", None),
            P("expert", "dp", None),
        ),
        out_specs=(
            P(("dp", "expert"), None),
            P(("dp", "expert"), None),
            P(("dp", "expert"), None),
            P(("dp", "expert"), None),
            P(("dp", "expert"), None),
            P(("dp", "expert"), None),
            P(("dp", "expert"), None),
            P(("dp", "expert")),
            P(("dp", "expert")),
            P(("dp", "expert")),
            P(("dp", "expert")),
            P("expert", "dp", None),
            P("expert", "dp", None),
            P("expert", "dp", None),
        ),
        check_vma=False,
    )
```

```python
import functools

import jax
import jax.numpy as jnp
from jax import lax
from jax.experimental import pallas as pl
from jax.experimental.pallas import tpu as pltpu
from jax.sharding import PartitionSpec as P

D = 2048
HEADS = 16
HD = 128
TOPK = 8
CAP = 24


eps = 1e-05


def product(left, right, form):
    return jnp.einsum(form, left, right, preferred_element_type=jnp.float32)


def rms_forward(values, gain):
    inverse = lax.rsqrt(jnp.mean(values * values, axis=-1, keepdims=True) + eps)
    return (values * inverse * gain, inverse)


def rms_backward(values, inverse, gain, grad):
    scaled = grad * gain
    inner = jnp.mean(scaled * values, axis=-1, keepdims=True)
    grad_values = inverse * scaled - values * (inverse * inverse * inverse) * inner
    grad_gain = jnp.sum(grad * values * inverse, axis=0)
    return (grad_values, grad_gain)


def layout(lengths_row, count):
    places = jnp.arange(count, dtype=jnp.int32)
    ends = jnp.cumsum(lengths_row, dtype=jnp.int32)
    passed = (places[:, None] >= ends[None, :]).astype(jnp.int32)
    segment = jnp.sum(passed, axis=1, dtype=jnp.int32)
    start = jnp.sum(passed * lengths_row[None, :], axis=1, dtype=jnp.int32)
    return (segment, places - start, places)


def rotate(values, cosine, sine):
    count = values.shape[0]
    heads = values.reshape(count, HEADS, HD)
    half = HD // 2
    first = heads[..., :half]
    second = heads[..., half:]
    turned = jnp.concatenate(
        [first * cosine - second * sine, second * cosine + first * sine], axis=-1
    )
    return turned.reshape(count, D)


MESH = pl.DeviceIdType.MESH


def place_of():
    z = lax.axis_index("dp")
    j = lax.axis_index("expert")
    return z, j, j // 2, j % 2


def greet(n_dp, n_expert):
    z, j, chip, core = place_of()
    chips = n_expert // 2
    barrier = pltpu.get_barrier_semaphore()
    for k in range(1, n_dp):
        pl.semaphore_signal(
            barrier, inc=1, device_id=((z + k) % n_dp, j), device_id_type=MESH
        )
    for k in range(1, chips):
        other = ((chip + k) % chips) * 2 + core
        pl.semaphore_signal(barrier, inc=1, device_id=(z, other), device_id_type=MESH)
    pl.semaphore_signal(
        barrier, inc=1, device_id=(z, chip * 2 + 1 - core), device_id_type=MESH
    )
    pl.semaphore_wait(barrier, n_dp - 1 + chips - 1 + 1)


def remote(source, target, send, receive, device):
    return pltpu.make_async_remote_copy(
        src_ref=source,
        dst_ref=target,
        send_sem=send,
        recv_sem=receive,
        device_id=device,
        device_id_type=MESH,
    )


def exchange(n_dp, pairs, send, receive, local):
    z, j, chip, core = place_of()
    copies = []
    for i, (source, target) in enumerate(pairs):
        for k in range(1, n_dp):
            to = (z + k) % n_dp
            copies.append(
                remote(source(to), target(z), send.at[i, k], receive.at[i, k], (to, j))
            )
        copies.append(pltpu.make_async_copy(source(z), target(z), local.at[i]))
    return copies


def gather_kernel(n_dp, n_expert, n_items, places, cuts, n_cut, n_out, *refs):
    z, j, chip, core = place_of()
    chips = n_expert // 2
    sources = refs[:n_items]
    cut_in = refs[n_items : n_items + n_cut]
    at = n_items + n_cut
    targets = refs[at : at + n_items]
    cut_out = refs[at + n_items : at + n_items + n_out]
    (
        send_c,
        recv_c,
        send_b,
        recv_b,
        send_a,
        recv_a,
        local,
        send_x,
        recv_x,
        local_x,
    ) = refs[at + n_items + n_out :]
    greet(n_dp, n_expert)
    mate = (z, chip * 2 + 1 - core)

    def slot(i, plane, column):
        return places[i](targets[i], plane * n_expert + column)

    def hand(i, plane, source):
        for k in range(1, chips):
            other = ((chip + k) % chips) * 2 + core
            remote(
                source, slot(i, plane, j), send_b.at[i, plane, k], recv_b.at[i, plane, k], (z, other)
            ).start()
        remote(
            source, slot(i, plane, j), send_a.at[i, plane, 0], recv_a.at[i, plane, 0], mate
        ).start()

    def along(i, plane, source, way, step):
        return remote(
            source, slot(i, plane, j), send_c.at[i, way, plane], recv_c.at[i, plane], (z + step, j)
        )

    for i in range(n_items):

        @pl.when(z < n_dp - 1)
        def _():
            along(i, z, sources[i], 0, 1).start()

        @pl.when(z > 0)
        def _():
            along(i, z, sources[i], 1, -1).start()

        hand(i, z, sources[i])
        pltpu.make_async_copy(sources[i], slot(i, z, j), local.at[i]).start()
    copies = exchange(n_dp, cuts(cut_in, cut_out), send_x, recv_x, local_x)
    for copy in copies:
        copy.start()

    def arrived(i, plane):
        for k in range(1, chips):
            column = ((chip + chips - k) % chips) * 2 + core
            block = slot(i, plane, column)
            remote(block, block, send_b.at[i, plane, k], recv_b.at[i, plane, k], mate).wait_recv()
            remote(block, block, send_a.at[i, plane, k], recv_a.at[i, plane, k], mate).start()

    for d in range(1, n_dp):

        @pl.when(z >= d)
        def _():
            for i in range(n_items):
                block = slot(i, z - d, j)
                along(i, z - d, block, 0, 1).wait_recv()

                @pl.when(z < n_dp - 1)
                def _():
                    along(i, z - d, block, 0, 1).start()

                hand(i, z - d, block)

        @pl.when(z + d < n_dp)
        def _():
            for i in range(n_items):
                block = slot(i, z + d, j)
                along(i, z + d, block, 1, -1).wait_recv()

                @pl.when(z > 0)
                def _():
                    along(i, z + d, block, 1, -1).start()

                hand(i, z + d, block)

        if d == 1:
            for i in range(n_items):
                arrived(i, z)
        else:

            @pl.when(z >= d - 1)
            def _():
                for i in range(n_items):
                    arrived(i, z - d + 1)

            @pl.when(z + d - 1 < n_dp)
            def _():
                for i in range(n_items):
                    arrived(i, z + d - 1)

    @pl.when(z >= n_dp - 1)
    def _():
        for i in range(n_items):
            arrived(i, z - n_dp + 1)

    @pl.when(z + n_dp - 1 < n_dp)
    def _():
        for i in range(n_items):
            arrived(i, z + n_dp - 1)

    for i in range(n_items):
        for plane in range(n_dp):
            for k in range(chips):
                column = ((chip + chips - k) % chips) * 2 + 1 - core
                block = slot(i, plane, column)
                remote(
                    block, block, send_a.at[i, plane, k], recv_a.at[i, plane, k], mate
                ).wait_recv()
    for i in range(n_items):
        for plane in range(n_dp):
            block = slot(i, plane, j)
            for k in range(1, chips):
                remote(
                    block, block, send_b.at[i, plane, k], recv_b.at[i, plane, k], mate
                ).wait_send()
            for k in range(chips):
                remote(
                    block, block, send_a.at[i, plane, k], recv_a.at[i, plane, k], mate
                ).wait_send()

            @pl.when((z < n_dp - 1) & (z >= plane))
            def _():
                along(i, plane, block, 0, 1).wait_send()

            @pl.when((z > 0) & (z <= plane))
            def _():
                along(i, plane, block, 1, -1).wait_send()

        pltpu.make_async_copy(sources[i], slot(i, z, j), local.at[i]).wait()
    for copy in copies:
        copy.wait()


def gather_call(n_dp, n_expert, items, shapes, places, cut_in, cut_shapes, cuts, aliases, number):
    chips = n_expert // 2
    n, m = len(items), len(cut_shapes)
    dma = pltpu.SemaphoreType.DMA
    anywhere = pl.BlockSpec(memory_space=pl.ANY)
    return pl.pallas_call(
        functools.partial(gather_kernel, n_dp, n_expert, n, places, cuts, len(cut_in), m),
        out_shape=[*shapes, *cut_shapes],
        in_specs=[anywhere] * (n + len(cut_in)),
        out_specs=[anywhere] * (n + m),
        scratch_shapes=[
            dma((n, 2, n_dp)),
            dma((n, n_dp)),
            dma((n, n_dp, chips)),
            dma((n, n_dp, chips)),
            dma((n, n_dp, chips)),
            dma((n, n_dp, chips)),
            dma((n,)),
            dma((max(m, 1), n_dp)),
            dma((max(m, 1), n_dp)),
            dma((max(m, 1),)),
        ],
        input_output_aliases=aliases,
        compiler_params=pltpu.CompilerParams(collective_id=number, has_side_effects=True),
    )(*items, *cut_in)


def scatter_kernel(n_dp, n_expert, n_items, n_cut, cuts, *refs):
    z, j, chip, core = place_of()
    chips = n_expert // 2
    sources = refs[:n_items]
    cut_in = refs[n_items : n_items + n_cut]
    at = n_items + n_cut
    targets = refs[at : at + n_items]
    cut_out = refs[at + n_items : at + n_items + n_cut]
    at = at + n_items + n_cut
    halves = refs[at : at + n_items]
    got_a = refs[at + n_items : at + 2 * n_items]
    got_b = refs[at + 2 * n_items : at + 3 * n_items]
    got_c = refs[at + 3 * n_items : at + 4 * n_items]
    (
        send_a,
        recv_a,
        send_b,
        recv_b,
        send_c,
        recv_c,
        local,
        send_x,
        recv_x,
        local_x,
    ) = refs[at + 4 * n_items :]
    greet(n_dp, n_expert)
    mate = (z, chip * 2 + 1 - core)
    order = [*range(1, chips), 0]

    def to_mate(i, k):
        column = ((chip + k) % chips) * 2
        return remote(
            sources[i].at[:, column + 1 - core],
            got_a[i].at[k],
            send_a.at[i, k],
            recv_a.at[i, k],
            mate,
        )

    def load(i, k):
        column = ((chip + k) % chips) * 2
        return pltpu.make_async_copy(
            sources[i].at[:, column + core], halves[i].at[k], local.at[i, k]
        )

    def to_chip(i, k):
        other = ((chip + k) % chips) * 2 + core
        return remote(
            halves[i].at[k], got_b[i].at[k - 1], send_b.at[i, k], recv_b.at[i, k], (z, other)
        )

    def to_plane(i, k):
        to = (z + k) % n_dp
        return remote(
            halves[i].at[0, to], got_c[i].at[k - 1], send_c.at[i, k], recv_c.at[i, k], (to, j)
        )

    for i in range(n_items):
        for k in order:
            to_mate(i, k).start()
            load(i, k).start()
    copies = exchange(n_dp, cuts(cut_in, cut_out), send_x, recv_x, local_x)
    for copy in copies:
        copy.start()

    def loop(rows, body):
        def step(n, unused):
            body(pl.ds(pl.multiple_of(n * 16, 16), 16))
            return unused

        lax.fori_loop(0, rows // 16, step, 0)

    f32 = jnp.float32
    for i in range(n_items):
        rows = halves[i].shape[2]
        for k in order:
            load(i, k).wait()
            to_mate(i, k).wait_recv()
            if k == 0:
                continue

            def one(n, unused):
                plane = n // (rows // 16)
                at = pl.ds(pl.multiple_of((n % (rows // 16)) * 16, 16), 16)
                total = halves[i][k, plane, at].astype(f32) + got_a[i][k, plane, at].astype(f32)
                halves[i][k, plane, at] = total.astype(halves[i].dtype)
                return unused

            lax.fori_loop(0, n_dp * (rows // 16), one, 0)
            to_chip(i, k).start()
    for i in range(n_items):
        rows = halves[i].shape[2]
        for k in range(1, chips):
            to_chip(i, k).wait_recv()
        for k in [*range(1, n_dp), 0]:
            plane = (z + k) % n_dp

            def body(at):
                total = halves[i][0, plane, at].astype(f32) + got_a[i][0, plane, at].astype(f32)
                for other in range(chips - 1):
                    total = total + got_b[i][other, plane, at].astype(f32)
                halves[i][0, plane, at] = total.astype(halves[i].dtype)

            loop(rows, body)
            if k:
                to_plane(i, k).start()
    for i in range(n_items):
        rows = halves[i].shape[2]
        for k in range(1, n_dp):
            to_plane(i, k).wait_recv()

        def body(at):
            total = halves[i][0, z, at].astype(f32)
            for k in range(n_dp - 1):
                total = total + got_c[i][k, at].astype(f32)
            targets[i][at] = total

        loop(rows, body)
    for i in range(n_items):
        for k in range(chips):
            to_mate(i, k).wait_send()
            if k:
                to_chip(i, k).wait_send()
        for k in range(1, n_dp):
            to_plane(i, k).wait_send()
    for copy in copies:
        copy.wait()


def scatter_call(n_dp, n_expert, items, cut_in, cut_shapes, cuts, number):
    chips = n_expert // 2
    n, m = len(items), len(cut_shapes)
    dma = pltpu.SemaphoreType.DMA
    anywhere = pl.BlockSpec(memory_space=pl.ANY)
    blocks = [item.shape[2:] for item in items]
    bf16 = jnp.bfloat16
    return pl.pallas_call(
        functools.partial(scatter_kernel, n_dp, n_expert, n, m, cuts),
        out_shape=[*[jax.ShapeDtypeStruct(block, jnp.float32) for block in blocks], *cut_shapes],
        in_specs=[anywhere] * (n + m),
        out_specs=[pl.BlockSpec(memory_space=pltpu.VMEM)] * n + [anywhere] * m,
        scratch_shapes=[
            *[pltpu.VMEM((chips, n_dp, *block), bf16) for block in blocks],
            *[pltpu.VMEM((chips, n_dp, *block), bf16) for block in blocks],
            *[pltpu.VMEM((chips - 1, n_dp, *block), bf16) for block in blocks],
            *[pltpu.VMEM((n_dp - 1, *block), bf16) for block in blocks],
            dma((n, chips)),
            dma((n, chips)),
            dma((n, chips)),
            dma((n, chips)),
            dma((n, n_dp)),
            dma((n, n_dp)),
            dma((n, chips)),
            dma((max(m, 1), n_dp)),
            dma((max(m, 1), n_dp)),
            dma((max(m, 1),)),
        ],
        compiler_params=pltpu.CompilerParams(
            collective_id=number, has_side_effects=True, vmem_limit_bytes=60 * 1024 * 1024
        ),
    )(*items, *cut_in)

def scatter_all(n_dp, n_expert, items, cut_in, cut_shapes, cuts, number):
    chips = n_expert // 2
    blocks = (3 * chips - 1) * n_dp + n_dp + 2
    need = sum(blocks * item.shape[2] * item.shape[3] * 2 for item in items)
    pieces = -(-need // (56 * 1024 * 1024))
    tiles = [item.shape[3] // 128 for item in items]
    results = [[] for item in items]
    extra = []
    for piece in range(pieces):
        ends = [(t * piece // pieces * 128, t * (piece + 1) // pieces * 128) for t in tiles]
        used = [i for i, (low, high) in enumerate(ends) if high > low]
        first = piece == 0
        outs = scatter_call(
            n_dp,
            n_expert,
            [items[i][..., ends[i][0] : ends[i][1]] if pieces > 1 else items[i] for i in used],
            cut_in if first else [],
            cut_shapes if first else [],
            cuts if first else lambda ins, outs: [],
            number + piece,
        )
        for i, out in zip(used, outs):
            results[i].append(out)
        if first:
            extra = outs[len(used) :]
    return [one[0] if len(one) == 1 else jnp.concatenate(one, axis=1) for one in results], extra


def shards(
    n_dp,
    n_expert,
    tokens,
    cotangent,
    lengths,
    routes,
    w_query,
    w_key,
    w_value,
    w_out,
    w_router,
    gain_attn,
    gain_query,
    gain_key,
    gain_mlp,
    w_gate,
    w_up,
    w_down,
):
    groups = n_dp * n_expert
    bf16 = jnp.bfloat16
    number = w_gate.shape[0]
    ff = w_gate.shape[2]
    part = ff // n_dp
    experts_all = w_router.shape[1]
    width = 128
    small = jnp.concatenate(
        [
            w_router,
            gain_attn[:, None],
            gain_query[:, None],
            gain_key[:, None],
            gain_mlp[:, None],
            jnp.zeros((w_router.shape[0], width - experts_all - 4), bf16),
        ],
        axis=1,
    )
    hits = jnp.any(
        routes[:, :, None] == jnp.arange(width, dtype=jnp.int32)[None, None, :], axis=1
    ).astype(bf16)
    count = tokens.shape[0]
    rows_each = w_query.shape[0]
    extras = jnp.concatenate(
        [cotangent, hits, jnp.pad(small, ((0, count - rows_each), (0, 0)))], axis=1
    )
    weights = jnp.stack([w_query, w_key, w_value, w_out])
    depth = w_gate.shape[1]
    early = number * 5 // 8
    cut_shape = jax.ShapeDtypeStruct((number, n_dp * depth, part), bf16)

    def row_block(size):
        return lambda ref, block: ref.at[pl.ds(pl.multiple_of(block * size, 16), size)]

    def recut(low, high):
        def cuts(ins, outs):
            def pair(n):
                def source(to):
                    columns = pl.ds(pl.multiple_of(to * part, part), part)
                    return ins[n].at[pl.ds(low, high - low), :, columns]

                def target(at):
                    here = pl.ds(pl.multiple_of(at * depth, depth), depth)
                    return outs[n].at[pl.ds(low, high - low), here]

                return source, target

            return [pair(0), pair(1)]

        return cuts

    weights_all, extras_all, gate_early, up_early = gather_call(
        n_dp,
        n_expert,
        [weights, extras],
        [
            jax.ShapeDtypeStruct((4, groups * rows_each, D), bf16),
            jax.ShapeDtypeStruct((groups * count, D + 2 * width), bf16),
        ],
        [
            lambda ref, block: ref.at[
                :, pl.ds(pl.multiple_of(block * rows_each, 16), rows_each)
            ],
            row_block(count),
        ],
        [w_gate, w_up],
        [cut_shape, cut_shape],
        recut(0, early),
        {},
        0,
    )
    query_weight, key_weight, value_weight, out_weight = (weights_all[i] for i in range(4))
    small_all = (
        extras_all[:, D + width :].reshape(groups, count, width)[:, :rows_each].reshape(-1, width)
    )
    cotangent_all = extras_all[:, :D]
    hits_all = extras_all[:, D : D + experts_all]
    router_weight = small_all[:, :experts_all]
    gains = small_all[:, experts_all : experts_all + 4].astype(jnp.float32)
    attn_gain, query_gain, key_gain, mlp_gain = (gains[:, i] for i in range(4))
    inputs = tokens.astype(jnp.float32)
    segment, position, places = layout(lengths[0], count)
    half = HD // 2
    freq = 10000.0 ** (-2.0 * jnp.arange(half, dtype=jnp.float32) / HD)
    angle = position.astype(jnp.float32)[:, None] * freq[None, :]
    cosine = jnp.cos(angle)[:, None, :]
    sine = jnp.sin(angle)[:, None, :]
    scale = HD ** (-0.5)
    normed, attn_inverse = rms_forward(inputs, attn_gain)
    normed_low = normed.astype(bf16)
    query_raw = product(normed_low, query_weight, "td,de->te")
    key_raw = product(normed_low, key_weight, "td,de->te")
    value_low = product(normed_low, value_weight, "td,de->te").astype(bf16)
    query_normed, query_inverse = rms_forward(query_raw, query_gain)
    key_normed, key_inverse = rms_forward(key_raw, key_gain)
    query_low = rotate(query_normed, cosine, sine).astype(bf16).reshape(count, HEADS, HD)
    key_low = rotate(key_normed, cosine, sine).astype(bf16).reshape(count, HEADS, HD)
    value_heads = value_low.reshape(count, HEADS, HD)
    allowed = (segment[:, None] == segment[None, :]) & (places[None, :] <= places[:, None])
    scores = product(query_low, key_low, "qhd,khd->hqk") * scale
    scores = jnp.where(allowed[None], scores, -1e30)
    probs = jax.nn.softmax(scores, axis=-1)
    probs_low = probs.astype(bf16)
    attended_low = product(probs_low, value_heads, "hqk,khd->qhd").reshape(count, D).astype(bf16)
    middle = inputs + product(attended_low, out_weight, "td,de->te")
    mlp_normed, mlp_inverse = rms_forward(middle, mlp_gain)
    mlp_low = mlp_normed.astype(bf16)
    router = jax.nn.softmax(product(mlp_low, router_weight, "td,de->te"), axis=-1)

    mlp_all, gate_cut, up_cut = gather_call(
        n_dp,
        n_expert,
        [mlp_low],
        [jax.ShapeDtypeStruct((groups * count, D), bf16)],
        [row_block(count)],
        [w_gate, w_up, gate_early, up_early],
        [cut_shape, cut_shape],
        recut(early, number),
        {3: 1, 4: 2},
        1,
    )
    gate_up = jnp.concatenate([gate_cut, up_cut], axis=2)
    router_all = jax.nn.softmax(product(mlp_all, router_weight, "td,de->te"), axis=-1)
    first = lax.axis_index("expert") * number
    own = lax.dynamic_slice_in_dim(router_all, first, number, 1).reshape(groups, count, number)
    hit = lax.dynamic_slice_in_dim(hits_all, first, number, 1).reshape(groups, count, number)
    before = jnp.tril(jnp.ones((count, count), bf16), -1)
    slot = product(before, hit, "ts,bse->bte").astype(jnp.int32)
    slot = jnp.where(hit > 0, slot, -1)
    slots = jnp.arange(CAP, dtype=jnp.int32)
    table = jnp.transpose(slot, (0, 2, 1))[:, :, None, :] == slots[None, None, :, None]
    pick = table.astype(bf16)
    gates = jnp.sum(
        jnp.where(table, jnp.transpose(own, (0, 2, 1))[:, :, None, :], 0.0), axis=3
    )
    rows = product(pick, mlp_all.reshape(groups, count, D), "bect,btd->becd").astype(bf16)
    grows = product(pick, cotangent_all.reshape(groups, count, D), "bect,btd->becd").astype(bf16)
    mids = product(rows, gate_up, "becd,edf->becf")
    gate_mid = mids[..., :part]
    up_mid = mids[..., part:]
    sigmoid = jax.nn.sigmoid(gate_mid)
    silu = gate_mid * sigmoid
    hidden = silu * up_mid
    hidden_low = hidden.astype(bf16)
    result = product(hidden_low, w_down, "becf,efd->becd")
    weighted = (result * gates[..., None]).astype(bf16)
    part_out = product(pick, weighted, "bect,becd->btd").reshape(groups * count, D).astype(bf16)
    grad_plain = product(grows, w_down, "becd,efd->becf")
    grad_gates = jnp.sum(grad_plain * hidden_low.astype(jnp.float32), axis=3)
    grad_hidden = grad_plain * gates[..., None]
    grad_gate_low = (grad_hidden * up_mid * sigmoid * (1.0 + gate_mid * (1.0 - sigmoid))).astype(
        bf16
    )
    grad_up_low = (grad_hidden * silu).astype(bf16)
    grad_mids = jnp.concatenate([grad_gate_low, grad_up_low], axis=3)
    grad_rows = product(grad_mids, gate_up, "becf,edf->becd").astype(bf16)
    part_grad = product(pick, grad_rows, "bect,becd->btd").reshape(groups * count, D)
    part_probs = jnp.sum(
        jnp.where(table, grad_gates[..., None], 0.0), axis=2
    )
    part_probs = jnp.transpose(part_probs, (0, 2, 1)).reshape(groups * count, number)
    spare = jnp.zeros((groups * count, width), jnp.float32)
    part_probs = lax.dynamic_update_slice_in_dim(spare, part_probs, first, 1)
    grad_down_part = product((hidden * gates[..., None]).astype(bf16), grows, "becf,becd->efd")
    grad_gate_up = product(rows, grad_mids, "becd,becf->edf").astype(bf16)
    grad_gate_cut = grad_gate_up[..., :part]
    grad_up_cut = grad_gate_up[..., part:]

    def way_back(low, high):
        def cuts(ins, outs):
            def pair(n):
                def source(to):
                    here = pl.ds(pl.multiple_of(to * depth, depth), depth)
                    return ins[n].at[pl.ds(low, high - low), here]

                def target(at):
                    columns = pl.ds(pl.multiple_of(at * part, part), part)
                    return outs[n].at[:, :, columns]

                return source, target

            return [pair(0), pair(1)]

        return cuts

    def way_shape(size):
        return jax.ShapeDtypeStruct((size, depth, ff), bf16)

    back_items = [
        jnp.concatenate([part_grad, part_probs], axis=1)
        .astype(bf16)
        .reshape(n_dp, n_expert, count, D + width),
        part_out.reshape(n_dp, n_expert, count, D),
    ]
    sooner = number * 3 // 8
    (back, summed), (gate_first, up_first) = scatter_all(
        n_dp,
        n_expert,
        back_items,
        [grad_gate_cut, grad_up_cut],
        [way_shape(sooner)] * 2,
        way_back(0, sooner),
        8,
    )
    output = (middle + summed).astype(bf16)

    grad_final = cotangent.astype(jnp.float32)
    grad_mlp = back[:, :D]
    grad_router_probs = back[:, D : D + experts_all]
    grad_logits = router * (
        grad_router_probs - jnp.sum(router * grad_router_probs, axis=1, keepdims=True)
    )
    grad_logits_low = grad_logits.astype(bf16)
    grad_router_full = product(mlp_low, grad_logits_low, "td,te->de")
    grad_mlp = grad_mlp + product(grad_logits_low, router_weight, "te,de->td")
    grad_middle_part, grad_mlp_gain = rms_backward(middle, mlp_inverse, mlp_gain, grad_mlp)
    grad_middle = grad_final + grad_middle_part
    grad_branch_low = grad_middle.astype(bf16)
    grad_out_full = product(attended_low, grad_branch_low, "td,te->de")
    grad_attended = (
        product(grad_branch_low, out_weight, "te,de->td").astype(bf16).reshape(count, HEADS, HD)
    )
    grad_weights = product(grad_attended, value_heads, "qhd,khd->hqk")
    grad_scores = probs * (grad_weights - jnp.sum(probs * grad_weights, axis=-1, keepdims=True))
    grad_scores_low = grad_scores.astype(bf16)
    grad_query_turn = product(grad_scores_low, key_low, "hqk,khd->qhd").reshape(count, D) * scale
    grad_key_turn = product(grad_scores_low, query_low, "hqk,qhd->khd").reshape(count, D) * scale
    grad_value_low = (
        product(probs_low, grad_attended, "hqk,qhd->khd").reshape(count, D).astype(bf16)
    )
    grad_query_raw, grad_query_gain = rms_backward(
        query_raw, query_inverse, query_gain, rotate(grad_query_turn, cosine, -sine)
    )
    grad_key_raw, grad_key_gain = rms_backward(
        key_raw, key_inverse, key_gain, rotate(grad_key_turn, cosine, -sine)
    )
    grad_query_low = grad_query_raw.astype(bf16)
    grad_key_low = grad_key_raw.astype(bf16)
    grad_query_full = product(normed_low, grad_query_low, "td,te->de")
    grad_key_full = product(normed_low, grad_key_low, "td,te->de")
    grad_value_full = product(normed_low, grad_value_low, "td,te->de")
    grad_normed = (
        product(grad_query_low, query_weight, "te,de->td")
        + product(grad_key_low, key_weight, "te,de->td")
        + product(grad_value_low, value_weight, "te,de->td")
    )
    grad_inputs_part, grad_attn_gain = rms_backward(inputs, attn_inverse, attn_gain, grad_normed)
    grad_inputs = grad_middle + grad_inputs_part

    small_grads = jnp.concatenate(
        [
            grad_router_full,
            grad_attn_gain[:, None],
            grad_query_gain[:, None],
            grad_key_gain[:, None],
            grad_mlp_gain[:, None],
            jnp.zeros((D, width - experts_all - 4), jnp.float32),
        ],
        axis=1,
    )

    def blocks_of(value):
        return value.astype(bf16).reshape(n_dp, n_expert, rows_each, -1)

    sums, (gate_last, up_last) = scatter_all(
        n_dp,
        n_expert,
        [
            blocks_of(value)
            for value in (
                grad_out_full,
                grad_value_full,
                grad_key_full,
                grad_query_full,
                small_grads,
            )
        ],
        [grad_gate_cut, grad_up_cut],
        [way_shape(number - sooner)] * 2,
        way_back(sooner, number),
        16,
    )
    grad_out_part, grad_value_part, grad_key_part, grad_query_part, small_part = sums
    grad_router_part = small_part[:, :experts_all]
    gain_parts = [small_part[:, experts_all + i] for i in range(4)]
    grad_gate_part = jnp.concatenate([gate_first, gate_last], axis=0).astype(jnp.float32)
    grad_up_part = jnp.concatenate([up_first, up_last], axis=0).astype(jnp.float32)
    return (
        output,
        grad_inputs,
        grad_query_part,
        grad_key_part,
        grad_value_part,
        grad_out_part,
        grad_router_part,
        gain_parts[0],
        gain_parts[1],
        gain_parts[2],
        gain_parts[3],
        grad_gate_part,
        grad_up_part,
        grad_down_part,
    )


def solution(mesh):
    return jax.shard_map(
        functools.partial(shards, mesh.shape["dp"], mesh.shape["expert"]),
        mesh=mesh,
        in_specs=(
            P(("dp", "expert"), None),
            P(("dp", "expert"), None),
            P(("dp", "expert"), None),
            P(("dp", "expert"), None),
            P(("dp", "expert"), None),
            P(("dp", "expert"), None),
            P(("dp", "expert"), None),
            P(("dp", "expert"), None),
            P(("dp", "expert"), None),
            P(("dp", "expert")),
            P(("dp", "expert")),
            P(("dp", "expert")),
            P(("dp", "expert")),
            P("expert", "dp", None),
            P("expert", "dp", None),
            P("expert", "dp", None),
        ),
        out_specs=(
            P(("dp", "expert"), None),
            P(("dp", "expert"), None),
            P(("dp", "expert"), None),
            P(("dp", "expert"), None),
            P(("dp", "expert"), None),
            P(("dp", "expert"), None),
            P(("dp", "expert"), None),
            P(("dp", "expert")),
            P(("dp", "expert")),
            P(("dp", "expert")),
            P(("dp", "expert")),
            P("expert", "dp", None),
            P("expert", "dp", None),
            P("expert", "dp", None),
        ),
        check_vma=False,
    )
```

```python
import functools

import jax
import jax.numpy as jnp
from jax import lax
from jax.experimental import pallas as pl
from jax.experimental.pallas import tpu as pltpu
from jax.sharding import PartitionSpec as P

D = 2048
HEADS = 16
HD = 128
TOPK = 8
CAP = 24


eps = 1e-05


def product(left, right, form):
    return jnp.einsum(form, left, right, preferred_element_type=jnp.float32)


def rms_forward(values, gain):
    inverse = lax.rsqrt(jnp.mean(values * values, axis=-1, keepdims=True) + eps)
    return (values * inverse * gain, inverse)


def rms_backward(values, inverse, gain, grad):
    scaled = grad * gain
    inner = jnp.mean(scaled * values, axis=-1, keepdims=True)
    grad_values = inverse * scaled - values * (inverse * inverse * inverse) * inner
    grad_gain = jnp.sum(grad * values * inverse, axis=0)
    return (grad_values, grad_gain)


def layout(lengths_row, count):
    places = jnp.arange(count, dtype=jnp.int32)
    ends = jnp.cumsum(lengths_row, dtype=jnp.int32)
    passed = (places[:, None] >= ends[None, :]).astype(jnp.int32)
    segment = jnp.sum(passed, axis=1, dtype=jnp.int32)
    start = jnp.sum(passed * lengths_row[None, :], axis=1, dtype=jnp.int32)
    return (segment, places - start, places)


def rotate(values, cosine, sine):
    count = values.shape[0]
    heads = values.reshape(count, HEADS, HD)
    half = HD // 2
    first = heads[..., :half]
    second = heads[..., half:]
    turned = jnp.concatenate(
        [first * cosine - second * sine, second * cosine + first * sine], axis=-1
    )
    return turned.reshape(count, D)


MESH = pl.DeviceIdType.MESH


def place_of():
    z = lax.axis_index("dp")
    j = lax.axis_index("expert")
    return z, j, j // 2, j % 2


def greet(n_dp, n_expert):
    z, j, chip, core = place_of()
    chips = n_expert // 2
    barrier = pltpu.get_barrier_semaphore()
    for k in range(1, n_dp):
        pl.semaphore_signal(
            barrier, inc=1, device_id=((z + k) % n_dp, j), device_id_type=MESH
        )
    for k in range(1, chips):
        other = ((chip + k) % chips) * 2 + core
        pl.semaphore_signal(barrier, inc=1, device_id=(z, other), device_id_type=MESH)
    pl.semaphore_signal(
        barrier, inc=1, device_id=(z, chip * 2 + 1 - core), device_id_type=MESH
    )
    pl.semaphore_wait(barrier, n_dp - 1 + chips - 1 + 1)


def remote(source, target, send, receive, device):
    return pltpu.make_async_remote_copy(
        src_ref=source,
        dst_ref=target,
        send_sem=send,
        recv_sem=receive,
        device_id=device,
        device_id_type=MESH,
    )


def exchange(n_dp, pairs, send, receive, local):
    z, j, chip, core = place_of()
    copies = []
    for i, (source, target) in enumerate(pairs):
        for k in range(1, n_dp):
            to = (z + k) % n_dp
            copies.append(
                remote(source(to), target(z), send.at[i, k], receive.at[i, k], (to, j))
            )
        copies.append(pltpu.make_async_copy(source(z), target(z), local.at[i]))
    return copies


def gather_kernel(n_dp, n_expert, n_items, places, cuts, n_cut, n_out, *refs):
    z, j, chip, core = place_of()
    chips = n_expert // 2
    sources = refs[:n_items]
    cut_in = refs[n_items : n_items + n_cut]
    at = n_items + n_cut
    targets = refs[at : at + n_items]
    cut_out = refs[at + n_items : at + n_items + n_out]
    (
        send_c,
        recv_c,
        send_b,
        recv_b,
        send_a,
        recv_a,
        local,
        send_x,
        recv_x,
        local_x,
    ) = refs[at + n_items + n_out :]
    greet(n_dp, n_expert)
    mate = (z, chip * 2 + 1 - core)

    def slot(i, plane, column):
        return places[i](targets[i], plane * n_expert + column)

    def hand(i, plane, source):
        for k in range(1, chips):
            other = ((chip + k) % chips) * 2 + core
            remote(
                source, slot(i, plane, j), send_b.at[i, plane, k], recv_b.at[i, plane, k], (z, other)
            ).start()
        remote(
            source, slot(i, plane, j), send_a.at[i, plane, 0], recv_a.at[i, plane, 0], mate
        ).start()

    def along(i, plane, source, way, step):
        return remote(
            source, slot(i, plane, j), send_c.at[i, way, plane], recv_c.at[i, plane], (z + step, j)
        )

    for i in range(n_items):

        @pl.when(z < n_dp - 1)
        def _():
            along(i, z, sources[i], 0, 1).start()

        @pl.when(z > 0)
        def _():
            along(i, z, sources[i], 1, -1).start()

        hand(i, z, sources[i])
        pltpu.make_async_copy(sources[i], slot(i, z, j), local.at[i]).start()
    copies = exchange(n_dp, cuts(cut_in, cut_out), send_x, recv_x, local_x)
    for copy in copies:
        copy.start()

    def arrived(i, plane):
        for k in range(1, chips):
            column = ((chip + chips - k) % chips) * 2 + core
            block = slot(i, plane, column)
            remote(block, block, send_b.at[i, plane, k], recv_b.at[i, plane, k], mate).wait_recv()
            remote(block, block, send_a.at[i, plane, k], recv_a.at[i, plane, k], mate).start()

    for d in range(1, n_dp):

        @pl.when(z >= d)
        def _():
            for i in range(n_items):
                block = slot(i, z - d, j)
                along(i, z - d, block, 0, 1).wait_recv()

                @pl.when(z < n_dp - 1)
                def _():
                    along(i, z - d, block, 0, 1).start()

                hand(i, z - d, block)

        @pl.when(z + d < n_dp)
        def _():
            for i in range(n_items):
                block = slot(i, z + d, j)
                along(i, z + d, block, 1, -1).wait_recv()

                @pl.when(z > 0)
                def _():
                    along(i, z + d, block, 1, -1).start()

                hand(i, z + d, block)

        if d == 1:
            for i in range(n_items):
                arrived(i, z)
        else:

            @pl.when(z >= d - 1)
            def _():
                for i in range(n_items):
                    arrived(i, z - d + 1)

            @pl.when(z + d - 1 < n_dp)
            def _():
                for i in range(n_items):
                    arrived(i, z + d - 1)

    @pl.when(z >= n_dp - 1)
    def _():
        for i in range(n_items):
            arrived(i, z - n_dp + 1)

    @pl.when(z + n_dp - 1 < n_dp)
    def _():
        for i in range(n_items):
            arrived(i, z + n_dp - 1)

    for i in range(n_items):
        for plane in range(n_dp):
            for k in range(chips):
                column = ((chip + chips - k) % chips) * 2 + 1 - core
                block = slot(i, plane, column)
                remote(
                    block, block, send_a.at[i, plane, k], recv_a.at[i, plane, k], mate
                ).wait_recv()
    for i in range(n_items):
        for plane in range(n_dp):
            block = slot(i, plane, j)
            for k in range(1, chips):
                remote(
                    block, block, send_b.at[i, plane, k], recv_b.at[i, plane, k], mate
                ).wait_send()
            for k in range(chips):
                remote(
                    block, block, send_a.at[i, plane, k], recv_a.at[i, plane, k], mate
                ).wait_send()

            @pl.when((z < n_dp - 1) & (z >= plane))
            def _():
                along(i, plane, block, 0, 1).wait_send()

            @pl.when((z > 0) & (z <= plane))
            def _():
                along(i, plane, block, 1, -1).wait_send()

        pltpu.make_async_copy(sources[i], slot(i, z, j), local.at[i]).wait()
    for copy in copies:
        copy.wait()


def gather_call(n_dp, n_expert, items, shapes, places, cut_in, cut_shapes, cuts, aliases, number):
    chips = n_expert // 2
    n, m = len(items), len(cut_shapes)
    dma = pltpu.SemaphoreType.DMA
    anywhere = pl.BlockSpec(memory_space=pl.ANY)
    return pl.pallas_call(
        functools.partial(gather_kernel, n_dp, n_expert, n, places, cuts, len(cut_in), m),
        out_shape=[*shapes, *cut_shapes],
        in_specs=[anywhere] * (n + len(cut_in)),
        out_specs=[anywhere] * (n + m),
        scratch_shapes=[
            dma((n, 2, n_dp)),
            dma((n, n_dp)),
            dma((n, n_dp, chips)),
            dma((n, n_dp, chips)),
            dma((n, n_dp, chips)),
            dma((n, n_dp, chips)),
            dma((n,)),
            dma((max(m, 1), n_dp)),
            dma((max(m, 1), n_dp)),
            dma((max(m, 1),)),
        ],
        input_output_aliases=aliases,
        compiler_params=pltpu.CompilerParams(collective_id=number, has_side_effects=True),
    )(*items, *cut_in)


def scatter_kernel(n_dp, n_expert, n_items, n_cut, cuts, *refs):
    z, j, chip, core = place_of()
    chips = n_expert // 2
    sources = refs[:n_items]
    cut_in = refs[n_items : n_items + n_cut]
    at = n_items + n_cut
    targets = refs[at : at + n_items]
    cut_out = refs[at + n_items : at + n_items + n_cut]
    at = at + n_items + n_cut
    halves = refs[at : at + n_items]
    got_a = refs[at + n_items : at + 2 * n_items]
    got_b = refs[at + 2 * n_items : at + 3 * n_items]
    got_c = refs[at + 3 * n_items : at + 4 * n_items]
    (
        send_a,
        recv_a,
        send_b,
        recv_b,
        send_c,
        recv_c,
        local,
        send_x,
        recv_x,
        local_x,
    ) = refs[at + 4 * n_items :]
    greet(n_dp, n_expert)
    mate = (z, chip * 2 + 1 - core)
    order = [*range(1, chips), 0]

    def to_mate(i, k):
        column = ((chip + k) % chips) * 2
        return remote(
            sources[i].at[:, column + 1 - core],
            got_a[i].at[k],
            send_a.at[i, k],
            recv_a.at[i, k],
            mate,
        )

    def load(i, k):
        column = ((chip + k) % chips) * 2
        return pltpu.make_async_copy(
            sources[i].at[:, column + core], halves[i].at[k], local.at[i, k]
        )

    def to_chip(i, k):
        other = ((chip + k) % chips) * 2 + core
        return remote(
            halves[i].at[k], got_b[i].at[k - 1], send_b.at[i, k], recv_b.at[i, k], (z, other)
        )

    def to_plane(i, k):
        to = (z + k) % n_dp
        return remote(
            halves[i].at[0, to], got_c[i].at[k - 1], send_c.at[i, k], recv_c.at[i, k], (to, j)
        )

    for i in range(n_items):
        for k in order:
            to_mate(i, k).start()
            load(i, k).start()
    copies = exchange(n_dp, cuts(cut_in, cut_out), send_x, recv_x, local_x)
    for copy in copies:
        copy.start()

    def loop(rows, body):
        def step(n, unused):
            body(pl.ds(pl.multiple_of(n * 16, 16), 16))
            return unused

        lax.fori_loop(0, rows // 16, step, 0)

    f32 = jnp.float32
    for i in range(n_items):
        rows = halves[i].shape[2]
        for k in order:
            load(i, k).wait()
            to_mate(i, k).wait_recv()
            if k == 0:
                continue

            def one(n, unused):
                plane = n // (rows // 16)
                at = pl.ds(pl.multiple_of((n % (rows // 16)) * 16, 16), 16)
                total = halves[i][k, plane, at].astype(f32) + got_a[i][k, plane, at].astype(f32)
                halves[i][k, plane, at] = total.astype(halves[i].dtype)
                return unused

            lax.fori_loop(0, n_dp * (rows // 16), one, 0)
            to_chip(i, k).start()
    for i in range(n_items):
        rows = halves[i].shape[2]
        for k in range(1, chips):
            to_chip(i, k).wait_recv()
        for k in [*range(1, n_dp), 0]:
            plane = (z + k) % n_dp

            def body(at):
                total = halves[i][0, plane, at].astype(f32) + got_a[i][0, plane, at].astype(f32)
                for other in range(chips - 1):
                    total = total + got_b[i][other, plane, at].astype(f32)
                halves[i][0, plane, at] = total.astype(halves[i].dtype)

            loop(rows, body)
            if k:
                to_plane(i, k).start()
    for i in range(n_items):
        rows = halves[i].shape[2]
        for k in range(1, n_dp):
            to_plane(i, k).wait_recv()

        def body(at):
            total = halves[i][0, z, at].astype(f32)
            for k in range(n_dp - 1):
                total = total + got_c[i][k, at].astype(f32)
            targets[i][at] = total

        loop(rows, body)
    for i in range(n_items):
        for k in range(chips):
            to_mate(i, k).wait_send()
            if k:
                to_chip(i, k).wait_send()
        for k in range(1, n_dp):
            to_plane(i, k).wait_send()
    for copy in copies:
        copy.wait()


def scatter_call(n_dp, n_expert, items, cut_in, cut_shapes, cuts, number):
    chips = n_expert // 2
    n, m = len(items), len(cut_shapes)
    dma = pltpu.SemaphoreType.DMA
    anywhere = pl.BlockSpec(memory_space=pl.ANY)
    blocks = [item.shape[2:] for item in items]
    bf16 = jnp.bfloat16
    return pl.pallas_call(
        functools.partial(scatter_kernel, n_dp, n_expert, n, m, cuts),
        out_shape=[*[jax.ShapeDtypeStruct(block, jnp.float32) for block in blocks], *cut_shapes],
        in_specs=[anywhere] * (n + m),
        out_specs=[pl.BlockSpec(memory_space=pltpu.VMEM)] * n + [anywhere] * m,
        scratch_shapes=[
            *[pltpu.VMEM((chips, n_dp, *block), bf16) for block in blocks],
            *[pltpu.VMEM((chips, n_dp, *block), bf16) for block in blocks],
            *[pltpu.VMEM((chips - 1, n_dp, *block), bf16) for block in blocks],
            *[pltpu.VMEM((n_dp - 1, *block), bf16) for block in blocks],
            dma((n, chips)),
            dma((n, chips)),
            dma((n, chips)),
            dma((n, chips)),
            dma((n, n_dp)),
            dma((n, n_dp)),
            dma((n, chips)),
            dma((max(m, 1), n_dp)),
            dma((max(m, 1), n_dp)),
            dma((max(m, 1),)),
        ],
        compiler_params=pltpu.CompilerParams(
            collective_id=number, has_side_effects=True, vmem_limit_bytes=60 * 1024 * 1024
        ),
    )(*items, *cut_in)

def scatter_all(n_dp, n_expert, items, cut_in, cut_shapes, cuts, number):
    chips = n_expert // 2
    blocks = (3 * chips - 1) * n_dp + n_dp + 2
    need = sum(blocks * item.shape[2] * item.shape[3] * 2 for item in items)
    pieces = -(-need // (56 * 1024 * 1024))
    tiles = [item.shape[3] // 128 for item in items]
    results = [[] for item in items]
    extra = []
    for piece in range(pieces):
        ends = [(t * piece // pieces * 128, t * (piece + 1) // pieces * 128) for t in tiles]
        used = [i for i, (low, high) in enumerate(ends) if high > low]
        first = piece == 0
        outs = scatter_call(
            n_dp,
            n_expert,
            [items[i][..., ends[i][0] : ends[i][1]] if pieces > 1 else items[i] for i in used],
            cut_in if first else [],
            cut_shapes if first else [],
            cuts if first else lambda ins, outs: [],
            number + piece,
        )
        for i, out in zip(used, outs):
            results[i].append(out)
        if first:
            extra = outs[len(used) :]
    return [one[0] if len(one) == 1 else jnp.concatenate(one, axis=1) for one in results], extra


def dot(left, right, dims):
    return lax.dot_general(
        left, right, ((dims[:1], dims[1:]), ((), ())), preferred_element_type=jnp.float32
    )


def picks(slots_ref, number):
    pair = slots_ref.shape[2]
    rows = lax.broadcasted_iota(jnp.int32, (2 * CAP, pair), 0)
    return [slots_ref[0, e : e + 1, :] == rows for e in range(number)]


def pick_kernel(number, experts_all, slots_ref, x_ref, g_ref, router_ref, rows_ref, grows_ref, gates_ref):
    chosen = picks(slots_ref, number)
    pick = jnp.concatenate(chosen, axis=0).astype(jnp.bfloat16)
    size = 2 * CAP
    x = x_ref[...]
    logits = dot(router_ref[...], x, (0, 1))
    names = lax.broadcasted_iota(jnp.int32, logits.shape, 0)
    logits = jnp.where(names < experts_all, logits, -1e30)
    weights = jnp.exp(logits - jnp.max(logits, axis=0, keepdims=True))
    probs = weights / jnp.sum(weights, axis=0, keepdims=True)
    for e in range(number):
        gate = jnp.sum(jnp.where(chosen[e], probs[e : e + 1, :], 0.0), axis=1, keepdims=True)
        gates_ref[e] = jnp.broadcast_to(gate, (size, 128))
    picked = dot(pick, x, (1, 0)).astype(jnp.bfloat16)
    for e in range(number):
        rows_ref[e] = picked[e * size : (e + 1) * size]
    picked = dot(pick, g_ref[...], (1, 0)).astype(jnp.bfloat16)
    for e in range(number):
        grows_ref[e] = picked[e * size : (e + 1) * size]


def expert_kernel(
    steps,
    half,
    first_ref,
    x_ref,
    g_ref,
    gates_ref,
    gate_ref,
    up_ref,
    down_ref,
    y_ref,
    dx_ref,
    probs_ref,
    dgate_ref,
    dup_ref,
    ddown_ref,
    sum_gate,
    sum_up,
):
    bf16 = jnp.bfloat16
    x, g = x_ref[0], g_ref[0]
    rows, width = x.shape
    gate = gates_ref[0][:, :1]
    gate_mid = dot(x, gate_ref[0], (1, 0))
    up_mid = dot(x, up_ref[0], (1, 0))
    sigmoid = 1.0 / (1.0 + jnp.exp(-gate_mid))
    silu = gate_mid * sigmoid
    hidden = silu * up_mid
    hidden_low = hidden.astype(bf16)
    grad_plain = dot(g, down_ref[0], (1, 1))
    grad_gates = jnp.sum(grad_plain * hidden_low.astype(jnp.float32), axis=1, keepdims=True)
    high = grad_gates.astype(bf16).astype(jnp.float32)
    lane = lax.broadcasted_iota(jnp.int32, (rows, 128), 1)
    name = first_ref[0] + pl.program_id(0)
    probs_ref[0] = (
        jnp.where(lane == name, high, 0.0) + jnp.where(lane == name + half, grad_gates - high, 0.0)
    ).astype(bf16)
    grad_hidden = grad_plain * gate
    grad_gate = (
        grad_hidden * up_mid * sigmoid * (1.0 + gate_mid * (1.0 - sigmoid))
    ).astype(bf16)
    grad_up = (grad_hidden * silu).astype(bf16)
    scaled = (hidden * gate).astype(bf16)
    piece = 512
    for at in range(0, width, piece):
        y_ref[0, :, at : at + piece] = (
            dot(hidden_low, down_ref[0, :, at : at + piece], (1, 0)) * gate
        ).astype(bf16)
        dx_ref[0, :, at : at + piece] = (
            dot(grad_gate, gate_ref[0, at : at + piece, :], (1, 1))
            + dot(grad_up, up_ref[0, at : at + piece, :], (1, 1))
        ).astype(bf16)
    step = pl.program_id(1)
    for at in range(0, width, piece):
        x_part = x_ref[0, :, at : at + piece]
        here_gate = dot(x_part, grad_gate, (0, 0))
        here_up = dot(x_part, grad_up, (0, 0))
        here_down = dot(scaled, g_ref[0, :, at : at + piece], (0, 0))
        if steps == 1:
            dgate_ref[0, at : at + piece, :] = here_gate.astype(bf16)
            dup_ref[0, at : at + piece, :] = here_up.astype(bf16)
            ddown_ref[0, :, at : at + piece] = here_down
            continue

        @pl.when(step == 0)
        def _():
            sum_gate[at : at + piece, :] = here_gate
            sum_up[at : at + piece, :] = here_up
            ddown_ref[0, :, at : at + piece] = here_down

        @pl.when(step > 0)
        def _():
            sum_gate[at : at + piece, :] += here_gate
            sum_up[at : at + piece, :] += here_up
            ddown_ref[0, :, at : at + piece] += here_down

        @pl.when(step == steps - 1)
        def _():
            dgate_ref[0, at : at + piece, :] = sum_gate[at : at + piece, :].astype(bf16)
            dup_ref[0, at : at + piece, :] = sum_up[at : at + piece, :].astype(bf16)


def place_kernel(number, slots_ref, y_ref, dx_ref, probs_ref, out_ref, back_ref):
    pick = jnp.concatenate(picks(slots_ref, number), axis=0).astype(jnp.bfloat16)
    width = out_ref.shape[1]
    piece = 512
    flat = number * 2 * CAP
    for at in range(0, width, piece):
        part = y_ref[:, :, at : at + piece].reshape(flat, piece)
        out_ref[:, at : at + piece] = dot(pick, part, (0, 0)).astype(jnp.bfloat16)
        part = dx_ref[:, :, at : at + piece].reshape(flat, piece)
        back_ref[:, at : at + piece] = dot(pick, part, (0, 0)).astype(jnp.bfloat16)
    part = probs_ref[...].reshape(flat, 128)
    back_ref[:, width:] = dot(pick, part, (0, 0)).astype(jnp.bfloat16)


BIG = 60 * 1024 * 1024


def pick_call(number, experts_all, slots, x_all, g_all, router):
    pairs, _, pair = slots.shape
    bf16 = jnp.bfloat16
    size = 2 * CAP
    rows = pl.BlockSpec((number, size, D), lambda p: (0, p, 0))
    tokens = pl.BlockSpec((pair, D), lambda p: (p, 0))
    return pl.pallas_call(
        functools.partial(pick_kernel, number, experts_all),
        grid=(pairs,),
        in_specs=[
            pl.BlockSpec((1, number, pair), lambda p: (p, 0, 0)),
            tokens,
            tokens,
            pl.BlockSpec(router.shape, lambda p: (0, 0)),
        ],
        out_specs=[rows, rows, pl.BlockSpec((number, size, 128), lambda p: (0, p, 0))],
        out_shape=[
            jax.ShapeDtypeStruct((number, pairs * size, D), bf16),
            jax.ShapeDtypeStruct((number, pairs * size, D), bf16),
            jax.ShapeDtypeStruct((number, pairs * size, 128), jnp.float32),
        ],
        compiler_params=pltpu.CompilerParams(vmem_limit_bytes=BIG),
    )(slots, x_all, g_all, router)


def expert_call(first, half, rows, grows, gates, gate, up, down):
    number, depth, _ = rows.shape
    part = gate.shape[2]
    size = depth
    while size > 768:
        size //= 2
    steps = depth // size
    bf16 = jnp.bfloat16
    f32 = jnp.float32

    def by_rows(width):
        return pl.BlockSpec((1, size, width), lambda e, r: (e, r, 0))

    def whole(*shape):
        return pl.BlockSpec((1, *shape), lambda e, r: (e, 0, 0))

    keep = (D, part) if steps > 1 else (16, 128)
    return pl.pallas_call(
        functools.partial(expert_kernel, steps, half),
        grid=(number, steps),
        in_specs=[
            pl.BlockSpec(memory_space=pltpu.SMEM),
            by_rows(D),
            by_rows(D),
            by_rows(128),
            whole(D, part),
            whole(D, part),
            whole(part, D),
        ],
        out_specs=[
            by_rows(D),
            by_rows(D),
            by_rows(128),
            whole(D, part),
            whole(D, part),
            whole(part, D),
        ],
        out_shape=[
            jax.ShapeDtypeStruct((number, depth, D), bf16),
            jax.ShapeDtypeStruct((number, depth, D), bf16),
            jax.ShapeDtypeStruct((number, depth, 128), bf16),
            jax.ShapeDtypeStruct((number, D, part), bf16),
            jax.ShapeDtypeStruct((number, D, part), bf16),
            jax.ShapeDtypeStruct((number, part, D), f32),
        ],
        scratch_shapes=[pltpu.VMEM(keep, f32), pltpu.VMEM(keep, f32)],
        compiler_params=pltpu.CompilerParams(vmem_limit_bytes=BIG),
    )(first, rows, grows, gates, gate, up, down)


def place_call(number, slots, y, dx, probs):
    pairs, _, pair = slots.shape
    bf16 = jnp.bfloat16
    size = 2 * CAP
    rows = pl.BlockSpec((number, size, D), lambda p: (0, p, 0))
    return pl.pallas_call(
        functools.partial(place_kernel, number),
        grid=(pairs,),
        in_specs=[
            pl.BlockSpec((1, number, pair), lambda p: (p, 0, 0)),
            rows,
            rows,
            pl.BlockSpec((number, size, 128), lambda p: (0, p, 0)),
        ],
        out_specs=[
            pl.BlockSpec((pair, D), lambda p: (p, 0)),
            pl.BlockSpec((pair, D + 128), lambda p: (p, 0)),
        ],
        out_shape=[
            jax.ShapeDtypeStruct((pairs * pair, D), bf16),
            jax.ShapeDtypeStruct((pairs * pair, D + 128), bf16),
        ],
        compiler_params=pltpu.CompilerParams(vmem_limit_bytes=BIG),
    )(slots, y, dx, probs)


def shards(
    n_dp,
    n_expert,
    tokens,
    cotangent,
    lengths,
    routes,
    w_query,
    w_key,
    w_value,
    w_out,
    w_router,
    gain_attn,
    gain_query,
    gain_key,
    gain_mlp,
    w_gate,
    w_up,
    w_down,
):
    groups = n_dp * n_expert
    bf16 = jnp.bfloat16
    number = w_gate.shape[0]
    ff = w_gate.shape[2]
    part = ff // n_dp
    experts_all = w_router.shape[1]
    width = 128
    small = jnp.concatenate(
        [
            w_router,
            gain_attn[:, None],
            gain_query[:, None],
            gain_key[:, None],
            gain_mlp[:, None],
            jnp.zeros((w_router.shape[0], width - experts_all - 4), bf16),
        ],
        axis=1,
    )
    hits = jnp.any(
        routes[:, :, None] == jnp.arange(width, dtype=jnp.int32)[None, None, :], axis=1
    ).astype(bf16)
    count = tokens.shape[0]
    rows_each = w_query.shape[0]
    extras = jnp.concatenate(
        [cotangent, hits, jnp.pad(small, ((0, count - rows_each), (0, 0)))], axis=1
    )
    weights = jnp.stack([w_query, w_key, w_value, w_out])
    depth = w_gate.shape[1]
    early = number * 5 // 8
    cut_shape = jax.ShapeDtypeStruct((number, n_dp * depth, part), bf16)

    def row_block(size):
        return lambda ref, block: ref.at[pl.ds(pl.multiple_of(block * size, 16), size)]

    def recut(low, high):
        def cuts(ins, outs):
            def pair(n):
                def source(to):
                    columns = pl.ds(pl.multiple_of(to * part, part), part)
                    return ins[n].at[pl.ds(low, high - low), :, columns]

                def target(at):
                    here = pl.ds(pl.multiple_of(at * depth, depth), depth)
                    return outs[n].at[pl.ds(low, high - low), here]

                return source, target

            return [pair(0), pair(1)]

        return cuts

    weights_all, extras_all, gate_early, up_early = gather_call(
        n_dp,
        n_expert,
        [weights, extras],
        [
            jax.ShapeDtypeStruct((4, groups * rows_each, D), bf16),
            jax.ShapeDtypeStruct((groups * count, D + 2 * width), bf16),
        ],
        [
            lambda ref, block: ref.at[
                :, pl.ds(pl.multiple_of(block * rows_each, 16), rows_each)
            ],
            row_block(count),
        ],
        [w_gate, w_up],
        [cut_shape, cut_shape],
        recut(0, early),
        {},
        0,
    )
    query_weight, key_weight, value_weight, out_weight = (weights_all[i] for i in range(4))
    small_all = (
        extras_all[:, D + width :].reshape(groups, count, width)[:, :rows_each].reshape(-1, width)
    )
    hits_all = extras_all[:, D : D + experts_all]
    router_weight = small_all[:, :experts_all]
    gains = small_all[:, experts_all : experts_all + 4].astype(jnp.float32)
    attn_gain, query_gain, key_gain, mlp_gain = (gains[:, i] for i in range(4))
    inputs = tokens.astype(jnp.float32)
    segment, position, places = layout(lengths[0], count)
    half = HD // 2
    freq = 10000.0 ** (-2.0 * jnp.arange(half, dtype=jnp.float32) / HD)
    angle = position.astype(jnp.float32)[:, None] * freq[None, :]
    cosine = jnp.cos(angle)[:, None, :]
    sine = jnp.sin(angle)[:, None, :]
    scale = HD ** (-0.5)
    normed, attn_inverse = rms_forward(inputs, attn_gain)
    normed_low = normed.astype(bf16)
    query_raw = product(normed_low, query_weight, "td,de->te")
    key_raw = product(normed_low, key_weight, "td,de->te")
    value_low = product(normed_low, value_weight, "td,de->te").astype(bf16)
    query_normed, query_inverse = rms_forward(query_raw, query_gain)
    key_normed, key_inverse = rms_forward(key_raw, key_gain)
    query_low = rotate(query_normed, cosine, sine).astype(bf16).reshape(count, HEADS, HD)
    key_low = rotate(key_normed, cosine, sine).astype(bf16).reshape(count, HEADS, HD)
    value_heads = value_low.reshape(count, HEADS, HD)
    allowed = (segment[:, None] == segment[None, :]) & (places[None, :] <= places[:, None])
    scores = product(query_low, key_low, "qhd,khd->hqk") * scale
    scores = jnp.where(allowed[None], scores, -1e30)
    probs = jax.nn.softmax(scores, axis=-1)
    probs_low = probs.astype(bf16)
    attended_low = product(probs_low, value_heads, "hqk,khd->qhd").reshape(count, D).astype(bf16)
    middle = inputs + product(attended_low, out_weight, "td,de->te")
    mlp_normed, mlp_inverse = rms_forward(middle, mlp_gain)
    mlp_low = mlp_normed.astype(bf16)
    router = jax.nn.softmax(product(mlp_low, router_weight, "td,de->te"), axis=-1)

    mlp_all, gate_cut, up_cut = gather_call(
        n_dp,
        n_expert,
        [mlp_low],
        [jax.ShapeDtypeStruct((groups * count, D), bf16)],
        [row_block(count)],
        [w_gate, w_up, gate_early, up_early],
        [cut_shape, cut_shape],
        recut(early, number),
        {3: 1, 4: 2},
        1,
    )
    first = lax.axis_index("expert") * number
    hit = lax.dynamic_slice_in_dim(hits_all, first, number, 1).reshape(groups, count, number)
    before = jnp.tril(jnp.ones((count, count), bf16), -1)
    slot = product(before, hit, "ts,bse->bet").astype(jnp.int32)
    slot = jnp.where(jnp.transpose(hit, (0, 2, 1)) > 0, slot, -1)
    slot = slot.reshape(groups // 2, 2, number, count)
    shift = jnp.array([0, CAP], jnp.int32)[None, :, None, None]
    slots = jnp.transpose(jnp.where(slot < 0, -1, slot + shift), (0, 2, 1, 3))
    slots = slots.reshape(groups // 2, number, 2 * count)
    router_own = jnp.pad(
        jnp.roll(router_weight, -first, axis=1), ((0, 0), (0, width - experts_all))
    )
    rows, grows, gates = pick_call(number, experts_all, slots, mlp_all, extras_all, router_own)
    weighted, grad_rows, grad_gates, grad_gate_cut, grad_up_cut, grad_down_part = expert_call(
        first[None], experts_all, rows, grows, gates, gate_cut, up_cut, w_down
    )
    part_out, part_back = place_call(number, slots, weighted, grad_rows, grad_gates)

    def way_back(low, high):
        def cuts(ins, outs):
            def pair(n):
                def source(to):
                    here = pl.ds(pl.multiple_of(to * depth, depth), depth)
                    return ins[n].at[pl.ds(low, high - low), here]

                def target(at):
                    columns = pl.ds(pl.multiple_of(at * part, part), part)
                    return outs[n].at[:, :, columns]

                return source, target

            return [pair(0), pair(1)]

        return cuts

    def way_shape(size):
        return jax.ShapeDtypeStruct((size, depth, ff), bf16)

    back_items = [
        part_back.reshape(n_dp, n_expert, count, D + width),
        part_out.reshape(n_dp, n_expert, count, D),
    ]
    sooner = number * 3 // 8
    (back, summed), (gate_first, up_first) = scatter_all(
        n_dp,
        n_expert,
        back_items,
        [grad_gate_cut, grad_up_cut],
        [way_shape(sooner)] * 2,
        way_back(0, sooner),
        8,
    )
    output = (middle + summed).astype(bf16)

    grad_final = cotangent.astype(jnp.float32)
    grad_mlp = back[:, :D]
    grad_router_probs = back[:, D : D + experts_all] + back[:, D + experts_all :]
    grad_logits = router * (
        grad_router_probs - jnp.sum(router * grad_router_probs, axis=1, keepdims=True)
    )
    grad_logits_low = grad_logits.astype(bf16)
    grad_router_full = product(mlp_low, grad_logits_low, "td,te->de")
    grad_mlp = grad_mlp + product(grad_logits_low, router_weight, "te,de->td")
    grad_middle_part, grad_mlp_gain = rms_backward(middle, mlp_inverse, mlp_gain, grad_mlp)
    grad_middle = grad_final + grad_middle_part
    grad_branch_low = grad_middle.astype(bf16)
    grad_out_full = product(attended_low, grad_branch_low, "td,te->de")
    grad_attended = (
        product(grad_branch_low, out_weight, "te,de->td").astype(bf16).reshape(count, HEADS, HD)
    )
    grad_weights = product(grad_attended, value_heads, "qhd,khd->hqk")
    grad_scores = probs * (grad_weights - jnp.sum(probs * grad_weights, axis=-1, keepdims=True))
    grad_scores_low = grad_scores.astype(bf16)
    grad_query_turn = product(grad_scores_low, key_low, "hqk,khd->qhd").reshape(count, D) * scale
    grad_key_turn = product(grad_scores_low, query_low, "hqk,qhd->khd").reshape(count, D) * scale
    grad_value_low = (
        product(probs_low, grad_attended, "hqk,qhd->khd").reshape(count, D).astype(bf16)
    )
    grad_query_raw, grad_query_gain = rms_backward(
        query_raw, query_inverse, query_gain, rotate(grad_query_turn, cosine, -sine)
    )
    grad_key_raw, grad_key_gain = rms_backward(
        key_raw, key_inverse, key_gain, rotate(grad_key_turn, cosine, -sine)
    )
    grad_query_low = grad_query_raw.astype(bf16)
    grad_key_low = grad_key_raw.astype(bf16)
    grad_query_full = product(normed_low, grad_query_low, "td,te->de")
    grad_key_full = product(normed_low, grad_key_low, "td,te->de")
    grad_value_full = product(normed_low, grad_value_low, "td,te->de")
    grad_normed = (
        product(grad_query_low, query_weight, "te,de->td")
        + product(grad_key_low, key_weight, "te,de->td")
        + product(grad_value_low, value_weight, "te,de->td")
    )
    grad_inputs_part, grad_attn_gain = rms_backward(inputs, attn_inverse, attn_gain, grad_normed)
    grad_inputs = grad_middle + grad_inputs_part

    small_grads = jnp.concatenate(
        [
            grad_router_full,
            grad_attn_gain[:, None],
            grad_query_gain[:, None],
            grad_key_gain[:, None],
            grad_mlp_gain[:, None],
            jnp.zeros((D, width - experts_all - 4), jnp.float32),
        ],
        axis=1,
    )

    def blocks_of(value):
        return value.astype(bf16).reshape(n_dp, n_expert, rows_each, -1)

    sums, (gate_last, up_last) = scatter_all(
        n_dp,
        n_expert,
        [
            blocks_of(value)
            for value in (
                grad_out_full,
                grad_value_full,
                grad_key_full,
                grad_query_full,
                small_grads,
            )
        ],
        [grad_gate_cut, grad_up_cut],
        [way_shape(number - sooner)] * 2,
        way_back(sooner, number),
        16,
    )
    grad_out_part, grad_value_part, grad_key_part, grad_query_part, small_part = sums
    grad_router_part = small_part[:, :experts_all]
    gain_parts = [small_part[:, experts_all + i] for i in range(4)]
    grad_gate_part = jnp.concatenate([gate_first, gate_last], axis=0).astype(jnp.float32)
    grad_up_part = jnp.concatenate([up_first, up_last], axis=0).astype(jnp.float32)
    return (
        output,
        grad_inputs,
        grad_query_part,
        grad_key_part,
        grad_value_part,
        grad_out_part,
        grad_router_part,
        gain_parts[0],
        gain_parts[1],
        gain_parts[2],
        gain_parts[3],
        grad_gate_part,
        grad_up_part,
        grad_down_part,
    )


def solution(mesh):
    return jax.shard_map(
        functools.partial(shards, mesh.shape["dp"], mesh.shape["expert"]),
        mesh=mesh,
        in_specs=(
            P(("dp", "expert"), None),
            P(("dp", "expert"), None),
            P(("dp", "expert"), None),
            P(("dp", "expert"), None),
            P(("dp", "expert"), None),
            P(("dp", "expert"), None),
            P(("dp", "expert"), None),
            P(("dp", "expert"), None),
            P(("dp", "expert"), None),
            P(("dp", "expert")),
            P(("dp", "expert")),
            P(("dp", "expert")),
            P(("dp", "expert")),
            P("expert", "dp", None),
            P("expert", "dp", None),
            P("expert", "dp", None),
        ),
        out_specs=(
            P(("dp", "expert"), None),
            P(("dp", "expert"), None),
            P(("dp", "expert"), None),
            P(("dp", "expert"), None),
            P(("dp", "expert"), None),
            P(("dp", "expert"), None),
            P(("dp", "expert"), None),
            P(("dp", "expert")),
            P(("dp", "expert")),
            P(("dp", "expert")),
            P(("dp", "expert")),
            P("expert", "dp", None),
            P("expert", "dp", None),
            P("expert", "dp", None),
        ),
        check_vma=False,
    )
```

```python
import functools

import jax
import jax.numpy as jnp
from jax import lax
from jax.experimental import pallas as pl
from jax.experimental.pallas import tpu as pltpu
from jax.sharding import PartitionSpec as P

D = 2048
HEADS = 16
HD = 128
TOPK = 8
CAP = 24


eps = 1e-05


def product(left, right, form):
    return jnp.einsum(form, left, right, preferred_element_type=jnp.float32)


def rms_forward(values, gain):
    inverse = lax.rsqrt(jnp.mean(values * values, axis=-1, keepdims=True) + eps)
    return (values * inverse * gain, inverse)


def rms_backward(values, inverse, gain, grad):
    scaled = grad * gain
    inner = jnp.mean(scaled * values, axis=-1, keepdims=True)
    grad_values = inverse * scaled - values * (inverse * inverse * inverse) * inner
    grad_gain = jnp.sum(grad * values * inverse, axis=0)
    return (grad_values, grad_gain)


def layout(lengths_row, count):
    places = jnp.arange(count, dtype=jnp.int32)
    ends = jnp.cumsum(lengths_row, dtype=jnp.int32)
    passed = (places[:, None] >= ends[None, :]).astype(jnp.int32)
    segment = jnp.sum(passed, axis=1, dtype=jnp.int32)
    start = jnp.sum(passed * lengths_row[None, :], axis=1, dtype=jnp.int32)
    return (segment, places - start, places)


def rotate(values, cosine, sine):
    count = values.shape[0]
    heads = values.reshape(count, HEADS, HD)
    half = HD // 2
    first = heads[..., :half]
    second = heads[..., half:]
    turned = jnp.concatenate(
        [first * cosine - second * sine, second * cosine + first * sine], axis=-1
    )
    return turned.reshape(count, D)


MESH = pl.DeviceIdType.MESH
BIG = 60 * 1024 * 1024


def place_of():
    z = lax.axis_index("dp")
    j = lax.axis_index("expert")
    return z, j, j // 2, j % 2


def other_chips(chip, chips):
    if chips == 4:
        square = [chip, chip + 1 - 2 * (chip % 2), chip + 2 - 4 * (chip // 2), 3 - chip]
        return lambda k: square[k], lambda k: square[k]
    return lambda k: (chip + k) % chips, lambda k: (chip + chips - k) % chips


def greet(n_dp, n_expert):
    z, j, chip, core = place_of()
    chips = n_expert // 2
    barrier = pltpu.get_barrier_semaphore()
    for k in range(1, n_dp):
        pl.semaphore_signal(
            barrier, inc=1, device_id=((z + k) % n_dp, j), device_id_type=MESH
        )
    for k in range(1, chips):
        other = ((chip + k) % chips) * 2 + core
        pl.semaphore_signal(barrier, inc=1, device_id=(z, other), device_id_type=MESH)
    pl.semaphore_signal(
        barrier, inc=1, device_id=(z, chip * 2 + 1 - core), device_id_type=MESH
    )
    pl.semaphore_wait(barrier, n_dp - 1 + chips - 1 + 1)


def remote(source, target, send, receive, device):
    return pltpu.make_async_remote_copy(
        src_ref=source,
        dst_ref=target,
        send_sem=send,
        recv_sem=receive,
        device_id=device,
        device_id_type=MESH,
    )


def exchange(n_dp, pairs, send, receive, local):
    z, j, chip, core = place_of()
    copies = []
    for i, (source, target) in enumerate(pairs):
        for k in range(1, n_dp):
            to = (z + k) % n_dp
            copies.append(
                remote(source(to), target(z), send.at[i, k], receive.at[i, k], (to, j))
            )
        copies.append(pltpu.make_async_copy(source(z), target(z), local.at[i]))
    return copies


def gather_kernel(n_dp, n_expert, n_items, places, cuts, n_cut, n_out, *refs):
    z, j, chip, core = place_of()
    chips = n_expert // 2
    square = chips == 4
    to_chip, from_chip = other_chips(chip, chips)
    sources = refs[:n_items]
    cut_in = refs[n_items : n_items + n_cut]
    at = n_items + n_cut
    targets = refs[at : at + n_items]
    cut_out = refs[at + n_items : at + n_items + n_out]
    (
        send_c,
        recv_c,
        send_b,
        recv_b,
        send_a,
        recv_a,
        local,
        send_x,
        recv_x,
        local_x,
    ) = refs[at + n_items + n_out :]
    greet(n_dp, n_expert)
    mate = (z, chip * 2 + 1 - core)
    near = (1, 2) if square else tuple(range(1, chips))

    def slot(i, plane, column):
        return places[i](targets[i], plane * n_expert + column)

    def pass_on(i, plane, source, column, k, chip_to):
        return remote(
            source,
            slot(i, plane, column),
            send_b.at[i, plane, k],
            recv_b.at[i, plane, k],
            (z, chip_to * 2 + core),
        )

    def hand(i, plane, source):
        for k in near:
            pass_on(i, plane, source, j, k, to_chip(k)).start()
        remote(
            source, slot(i, plane, j), send_a.at[i, plane, 0], recv_a.at[i, plane, 0], mate
        ).start()

    def along(i, plane, source, way, step):
        return remote(
            source, slot(i, plane, j), send_c.at[i, way, plane], recv_c.at[i, plane], (z + step, j)
        )

    def at_distance(d, body):
        if d == 0:
            body(z, 0)
            return

        @pl.when(z >= d)
        def _():
            body(z - d, 0)

        @pl.when(z + d < n_dp)
        def _():
            body(z + d, 1)

    for i in range(n_items):

        @pl.when(z < n_dp - 1)
        def _():
            along(i, z, sources[i], 0, 1).start()

        @pl.when(z > 0)
        def _():
            along(i, z, sources[i], 1, -1).start()

        hand(i, z, sources[i])
        pltpu.make_async_copy(sources[i], slot(i, z, j), local.at[i]).start()

    def relay(plane, way):
        step = -1 if way else 1
        for i in range(n_items):
            block = slot(i, plane, j)
            along(i, plane, block, way, step).wait_recv()

            @pl.when(z > 0 if way else z < n_dp - 1)
            def _():
                along(i, plane, block, way, step).start()

            hand(i, plane, block)

    for d in range(1, n_dp):
        at_distance(d, relay)
    copies = exchange(n_dp, cuts(cut_in, cut_out), send_x, recv_x, local_x)
    for copy in copies:
        copy.start()

    def arrive(i, plane, k):
        column = from_chip(k) * 2 + core
        block = slot(i, plane, column)
        pass_on(i, plane, block, column, k, chip).wait_recv()
        remote(block, block, send_a.at[i, plane, k], recv_a.at[i, plane, k], mate).start()
        return block, column

    def arrived(plane, way):
        for i in range(n_items):
            for k in near:
                block, column = arrive(i, plane, k)
                if square:

                    @pl.when(plane % 2 == k - 1)
                    def _():
                        pass_on(i, plane, block, column, 3, to_chip(3 - k)).start()

    def crossed(plane, way):
        for i in range(n_items):
            arrive(i, plane, 3)

    for d in range(n_dp):
        at_distance(d, arrived)
    if square:
        for d in range(n_dp):
            at_distance(d, crossed)

    for i in range(n_items):
        for plane in range(n_dp):
            for k in range(chips):
                column = (from_chip(k) if k else chip) * 2 + 1 - core
                block = slot(i, plane, column)
                remote(
                    block, block, send_a.at[i, plane, k], recv_a.at[i, plane, k], mate
                ).wait_recv()
    for i in range(n_items):
        for plane in range(n_dp):
            block = slot(i, plane, j)
            for k in range(1, chips):
                pass_on(i, plane, block, j, k, chip).wait_send()
            for k in range(chips):
                remote(
                    block, block, send_a.at[i, plane, k], recv_a.at[i, plane, k], mate
                ).wait_send()

            @pl.when((z < n_dp - 1) & (z >= plane))
            def _():
                along(i, plane, block, 0, 1).wait_send()

            @pl.when((z > 0) & (z <= plane))
            def _():
                along(i, plane, block, 1, -1).wait_send()

        pltpu.make_async_copy(sources[i], slot(i, z, j), local.at[i]).wait()
    for copy in copies:
        copy.wait()


def gather_call(n_dp, n_expert, items, shapes, places, cut_in, cut_shapes, cuts, aliases, number):
    chips = n_expert // 2
    n, m = len(items), len(cut_shapes)
    dma = pltpu.SemaphoreType.DMA
    anywhere = pl.BlockSpec(memory_space=pl.ANY)
    return pl.pallas_call(
        functools.partial(gather_kernel, n_dp, n_expert, n, places, cuts, len(cut_in), m),
        out_shape=[*shapes, *cut_shapes],
        in_specs=[anywhere] * (n + len(cut_in)),
        out_specs=[anywhere] * (n + m),
        scratch_shapes=[
            dma((n, 2, n_dp)),
            dma((n, n_dp)),
            dma((n, n_dp, chips)),
            dma((n, n_dp, chips)),
            dma((n, n_dp, chips)),
            dma((n, n_dp, chips)),
            dma((n,)),
            dma((max(m, 1), n_dp)),
            dma((max(m, 1), n_dp)),
            dma((max(m, 1),)),
        ],
        input_output_aliases=aliases,
        compiler_params=pltpu.CompilerParams(collective_id=number, has_side_effects=True),
    )(*items, *cut_in)


def scatter_kernel(n_dp, n_expert, n_items, n_cut, n_out, cuts, rings, n_rings, *refs):
    z, j, chip, core = place_of()
    chips = n_expert // 2
    square = chips == 4
    to_chip, from_chip = other_chips(chip, chips)
    refs = list(refs)

    def take(count):
        taken = refs[:count]
        del refs[:count]
        return taken

    sources, cut_in, targets, cut_out = take(n_items), take(n_cut), take(n_items), take(n_out)
    ring, got_a, got_b, got_c = take(n_rings), take(n_items), take(n_items), take(n_items)
    transit = take(n_items)
    (
        send_a,
        recv_a,
        send_b,
        recv_b,
        send_c,
        recv_c,
        send_t,
        recv_t,
        local,
        send_x,
        recv_x,
        local_x,
    ) = refs
    greet(n_dp, n_expert)
    mate = (z, chip * 2 + 1 - core)
    order = [3, 1, 2, 0] if square else [*range(1, chips), 0]
    half = n_dp // 2
    low, high = pl.ds(0, half), pl.ds(half, n_dp - half)

    def chip_of(k):
        return to_chip(k) if k else chip

    def to_mate(i, k):
        return remote(
            sources[i].at[:, chip_of(k) * 2 + 1 - core],
            got_a[i].at[k],
            send_a.at[i, k],
            recv_a.at[i, k],
            mate,
        )

    turn = [0] * n_rings
    loads = []
    for i in range(n_items):
        for k in order:
            loads.append((i, k, turn[rings[i]] % 2))
            turn[rings[i]] += 1

    def load(i, k, at):
        return pltpu.make_async_copy(
            sources[i].at[:, chip_of(k) * 2 + core], ring[rings[i]].at[at], local.at[rings[i], at]
        )

    def send_near(i, k, part, number):
        return remote(
            got_a[i].at[k, part],
            got_b[i].at[k - 1, part],
            send_b.at[i, number],
            recv_b.at[i, number],
            (z, to_chip(k) * 2 + core),
        )

    def send_over(i, k, part):
        return remote(
            got_a[i].at[3, part],
            transit[i].at[k - 1],
            send_t.at[i, k],
            recv_t.at[i, k],
            (z, to_chip(k) * 2 + core),
        )

    def send_far(i, k):
        return remote(
            got_a[i].at[k],
            got_b[i].at[k - 1],
            send_b.at[i, k],
            recv_b.at[i, k],
            (z, to_chip(k) * 2 + core),
        )

    def to_plane(i, k):
        to = (z + k) % n_dp
        return remote(
            got_a[i].at[0, to], got_c[i].at[k - 1], send_c.at[i, k], recv_c.at[i, k], (to, j)
        )

    f32 = jnp.float32

    def add(i, planes, target, terms):
        rows = got_a[i].shape[2]
        per = rows // 16

        def step(n, unused):
            plane = n // per
            at = pl.ds(pl.multiple_of((n % per) * 16, 16), 16)
            total = terms[0](plane, at).astype(f32)
            for term in terms[1:]:
                total = total + term(plane, at).astype(f32)
            target(plane, at, total)
            return unused

        lax.fori_loop(0, planes * per, step, 0)

    def grow(i, k, first, planes, term):
        def target(plane, at, total):
            got_a[i][k, plane + first, at] = total.astype(got_a[i].dtype)

        add(i, planes, target, [lambda plane, at: got_a[i][k, plane + first, at], term])

    for i in range(n_items):
        for k in order:
            to_mate(i, k).start()
    started = 0
    ahead = [0] * n_rings
    for i, k, at in loads:
        if ahead[rings[i]] < 2:
            load(i, k, at).start()
            ahead[rings[i]] += 1
    copies = exchange(n_dp, cuts(cut_in, cut_out), send_x, recv_x, local_x)
    for copy in copies:
        copy.start()

    for n, (i, k, at) in enumerate(loads):
        load(i, k, at).wait()
        to_mate(i, k).wait_recv()
        grow(i, k, 0, n_dp, lambda plane, rows: ring[rings[i]][at, plane, rows])
        later = [one for one in loads[n + 1 :] if rings[one[0]] == rings[i]]
        if len(later) >= 2:
            load(*later[1]).start()
        if not k:
            continue
        if not square:
            send_far(i, k).start()
        elif k == 3:
            send_over(i, 1, low).start()
            send_over(i, 2, high).start()
        elif k == 1:
            send_near(i, 1, low, 0).start()
        else:
            send_near(i, 2, high, 1).start()
    if square:
        for i in range(n_items):
            send_over(i, 2, high).wait_recv()
            grow(i, 1, half, n_dp - half, lambda plane, rows: transit[i][1, plane, rows])
            send_near(i, 1, high, 2).start()
            send_over(i, 1, low).wait_recv()
            grow(i, 2, 0, half, lambda plane, rows: transit[i][0, plane, rows])
            send_near(i, 2, low, 3).start()
    for i in range(n_items):
        if square:
            send_near(i, 1, low, 0).wait_recv()
            send_near(i, 2, high, 1).wait_recv()
            send_near(i, 1, high, 2).wait_recv()
            send_near(i, 2, low, 3).wait_recv()
        else:
            for k in range(1, chips):
                send_far(i, k).wait_recv()
        heard = 2 if square else chips - 1
        for k in [*range(1, n_dp), 0]:
            plane = (z + k) % n_dp

            def target(unused, at, total):
                got_a[i][0, plane, at] = total.astype(got_a[i].dtype)

            terms = [lambda unused, at: got_a[i][0, plane, at]]
            for other in range(heard):
                terms.append(lambda unused, at, other=other: got_b[i][other, plane, at])
            add(i, 1, target, terms)
            if k:
                to_plane(i, k).start()
    for i in range(n_items):
        for k in range(1, n_dp):
            to_plane(i, k).wait_recv()

        def target(unused, at, total):
            targets[i][at] = total

        terms = [lambda unused, at: got_a[i][0, z, at]]
        for k in range(n_dp - 1):
            terms.append(lambda unused, at, k=k: got_c[i][k, at])
        add(i, 1, target, terms)
    for i in range(n_items):
        for k in range(chips):
            to_mate(i, k).wait_send()
        if square:
            for k, part in ((1, low), (2, high)):
                send_over(i, k, part).wait_send()
            for k, part, number in ((1, low, 0), (2, high, 1), (1, high, 2), (2, low, 3)):
                send_near(i, k, part, number).wait_send()
        else:
            for k in range(1, chips):
                send_far(i, k).wait_send()
        for k in range(1, n_dp):
            to_plane(i, k).wait_send()
    for copy in copies:
        copy.wait()


def scatter_call(n_dp, n_expert, items, cut_in, cut_shapes, cuts, number):
    chips = n_expert // 2
    square = chips == 4
    n, m = len(items), len(cut_shapes)
    dma = pltpu.SemaphoreType.DMA
    anywhere = pl.BlockSpec(memory_space=pl.ANY)
    blocks = [item.shape[2:] for item in items]
    kinds = sorted(set(blocks))
    rings = [kinds.index(block) for block in blocks]
    bf16 = jnp.bfloat16
    heard = 2 if square else chips - 1
    return pl.pallas_call(
        functools.partial(
            scatter_kernel, n_dp, n_expert, n, len(cut_in), m, cuts, rings, len(kinds)
        ),
        out_shape=[*[jax.ShapeDtypeStruct(block, jnp.float32) for block in blocks], *cut_shapes],
        in_specs=[anywhere] * (n + len(cut_in)),
        out_specs=[pl.BlockSpec(memory_space=pltpu.VMEM)] * n + [anywhere] * m,
        scratch_shapes=[
            *[pltpu.VMEM((2, n_dp, *kind), bf16) for kind in kinds],
            *[pltpu.VMEM((chips, n_dp, *block), bf16) for block in blocks],
            *[pltpu.VMEM((heard, n_dp, *block), bf16) for block in blocks],
            *[pltpu.VMEM((n_dp - 1, *block), bf16) for block in blocks],
            *[pltpu.VMEM((2, n_dp // 2, *(block if square else (16, 128))), bf16) for block in blocks],
            dma((n, chips)),
            dma((n, chips)),
            dma((n, chips)),
            dma((n, chips)),
            dma((n, n_dp)),
            dma((n, n_dp)),
            dma((n, 3)),
            dma((n, 3)),
            dma((len(kinds), 2)),
            dma((max(m, 1), n_dp)),
            dma((max(m, 1), n_dp)),
            dma((max(m, 1),)),
        ],
        compiler_params=pltpu.CompilerParams(
            collective_id=number, has_side_effects=True, vmem_limit_bytes=62 * 1024 * 1024
        ),
    )(*items, *cut_in)


def scatter_all(n_dp, n_expert, items, cut_in, cut_shapes, cuts, number):
    chips = n_expert // 2
    blocks = (2 * chips if chips != 4 else 7) * n_dp + n_dp + 3
    need = sum(blocks * item.shape[2] * item.shape[3] * 2 for item in items)
    kinds = {item.shape[2:] for item in items}
    need += sum(2 * n_dp * kind[0] * kind[1] * 2 for kind in kinds)
    pieces = -(-need // (61 * 1024 * 1024))
    tiles = [item.shape[3] // 128 for item in items]
    results = [[] for item in items]
    extra = []
    for piece in range(pieces):
        ends = [(t * piece // pieces * 128, t * (piece + 1) // pieces * 128) for t in tiles]
        used = [i for i, (low, high) in enumerate(ends) if high > low]
        first = piece == 0
        outs = scatter_call(
            n_dp,
            n_expert,
            [items[i][..., ends[i][0] : ends[i][1]] if pieces > 1 else items[i] for i in used],
            cut_in if first else [],
            cut_shapes if first else [],
            cuts if first else lambda ins, outs: [],
            number + piece,
        )
        for i, out in zip(used, outs):
            results[i].append(out)
        if first:
            extra = outs[len(used) :]
    return [one[0] if len(one) == 1 else jnp.concatenate(one, axis=1) for one in results], extra


def dot(left, right, dims):
    return lax.dot_general(
        left, right, ((dims[:1], dims[1:]), ((), ())), preferred_element_type=jnp.float32
    )


def picks(slots_ref, number):
    pair = slots_ref.shape[2]
    rows = lax.broadcasted_iota(jnp.int32, (2 * CAP, pair), 0)
    return [slots_ref[0, e : e + 1, :] == rows for e in range(number)]


def pick_kernel(number, experts_all, slots_ref, x_ref, g_ref, router_ref, rows_ref, grows_ref, gates_ref):
    chosen = picks(slots_ref, number)
    pick = jnp.concatenate(chosen, axis=0).astype(jnp.bfloat16)
    size = 2 * CAP
    x = x_ref[...]
    logits = dot(router_ref[...], x, (0, 1))
    names = lax.broadcasted_iota(jnp.int32, logits.shape, 0)
    logits = jnp.where(names < experts_all, logits, -1e30)
    weights = jnp.exp(logits - jnp.max(logits, axis=0, keepdims=True))
    probs = weights / jnp.sum(weights, axis=0, keepdims=True)
    for e in range(number):
        gate = jnp.sum(jnp.where(chosen[e], probs[e : e + 1, :], 0.0), axis=1, keepdims=True)
        gates_ref[e] = jnp.broadcast_to(gate, (size, 128))
    picked = dot(pick, x, (1, 0)).astype(jnp.bfloat16)
    for e in range(number):
        rows_ref[e] = picked[e * size : (e + 1) * size]
    picked = dot(pick, g_ref[...], (1, 0)).astype(jnp.bfloat16)
    for e in range(number):
        grows_ref[e] = picked[e * size : (e + 1) * size]


def expert_kernel(
    steps,
    half,
    first_ref,
    x_ref,
    g_ref,
    gates_ref,
    gate_ref,
    up_ref,
    down_ref,
    y_ref,
    dx_ref,
    probs_ref,
    dgate_ref,
    dup_ref,
    ddown_ref,
    sum_gate,
    sum_up,
):
    bf16 = jnp.bfloat16
    x, g = x_ref[0], g_ref[0]
    rows, width = x.shape
    gate = gates_ref[0][:, :1]
    gate_mid = dot(x, gate_ref[0], (1, 0))
    up_mid = dot(x, up_ref[0], (1, 0))
    sigmoid = 1.0 / (1.0 + jnp.exp(-gate_mid))
    silu = gate_mid * sigmoid
    hidden = silu * up_mid
    hidden_low = hidden.astype(bf16)
    grad_plain = dot(g, down_ref[0], (1, 1))
    grad_gates = jnp.sum(grad_plain * hidden_low.astype(jnp.float32), axis=1, keepdims=True)
    high = grad_gates.astype(bf16).astype(jnp.float32)
    lane = lax.broadcasted_iota(jnp.int32, (rows, 128), 1)
    name = first_ref[0] + pl.program_id(0)
    probs_ref[0] = (
        jnp.where(lane == name, high, 0.0) + jnp.where(lane == name + half, grad_gates - high, 0.0)
    ).astype(bf16)
    grad_hidden = grad_plain * gate
    grad_gate = (
        grad_hidden * up_mid * sigmoid * (1.0 + gate_mid * (1.0 - sigmoid))
    ).astype(bf16)
    grad_up = (grad_hidden * silu).astype(bf16)
    scaled = (hidden * gate).astype(bf16)
    piece = 512
    for at in range(0, width, piece):
        y_ref[0, :, at : at + piece] = (
            dot(hidden_low, down_ref[0, :, at : at + piece], (1, 0)) * gate
        ).astype(bf16)
        dx_ref[0, :, at : at + piece] = (
            dot(grad_gate, gate_ref[0, at : at + piece, :], (1, 1))
            + dot(grad_up, up_ref[0, at : at + piece, :], (1, 1))
        ).astype(bf16)
    step = pl.program_id(1)
    for at in range(0, width, piece):
        x_part = x_ref[0, :, at : at + piece]
        here_gate = dot(x_part, grad_gate, (0, 0))
        here_up = dot(x_part, grad_up, (0, 0))
        here_down = dot(scaled, g_ref[0, :, at : at + piece], (0, 0))
        if steps == 1:
            dgate_ref[0, at : at + piece, :] = here_gate.astype(bf16)
            dup_ref[0, at : at + piece, :] = here_up.astype(bf16)
            ddown_ref[0, :, at : at + piece] = here_down
            continue

        @pl.when(step == 0)
        def _():
            sum_gate[at : at + piece, :] = here_gate
            sum_up[at : at + piece, :] = here_up
            ddown_ref[0, :, at : at + piece] = here_down

        @pl.when(step > 0)
        def _():
            sum_gate[at : at + piece, :] += here_gate
            sum_up[at : at + piece, :] += here_up
            ddown_ref[0, :, at : at + piece] += here_down

        @pl.when(step == steps - 1)
        def _():
            dgate_ref[0, at : at + piece, :] = sum_gate[at : at + piece, :].astype(bf16)
            dup_ref[0, at : at + piece, :] = sum_up[at : at + piece, :].astype(bf16)


def place_kernel(number, slots_ref, y_ref, dx_ref, probs_ref, out_ref, back_ref):
    pick = jnp.concatenate(picks(slots_ref, number), axis=0).astype(jnp.bfloat16)
    width = out_ref.shape[1]
    piece = 512
    flat = number * 2 * CAP
    for at in range(0, width, piece):
        part = y_ref[:, :, at : at + piece].reshape(flat, piece)
        out_ref[:, at : at + piece] = dot(pick, part, (0, 0)).astype(jnp.bfloat16)
        part = dx_ref[:, :, at : at + piece].reshape(flat, piece)
        back_ref[:, at : at + piece] = dot(pick, part, (0, 0)).astype(jnp.bfloat16)
    part = probs_ref[...].reshape(flat, 128)
    back_ref[:, width:] = dot(pick, part, (0, 0)).astype(jnp.bfloat16)


def pick_call(number, experts_all, slots, x_all, g_all, router):
    pairs, _, pair = slots.shape
    bf16 = jnp.bfloat16
    size = 2 * CAP
    rows = pl.BlockSpec((number, size, D), lambda p: (0, p, 0))
    tokens = pl.BlockSpec((pair, D), lambda p: (p, 0))
    return pl.pallas_call(
        functools.partial(pick_kernel, number, experts_all),
        grid=(pairs,),
        in_specs=[
            pl.BlockSpec((1, number, pair), lambda p: (p, 0, 0)),
            tokens,
            tokens,
            pl.BlockSpec(router.shape, lambda p: (0, 0)),
        ],
        out_specs=[rows, rows, pl.BlockSpec((number, size, 128), lambda p: (0, p, 0))],
        out_shape=[
            jax.ShapeDtypeStruct((number, pairs * size, D), bf16),
            jax.ShapeDtypeStruct((number, pairs * size, D), bf16),
            jax.ShapeDtypeStruct((number, pairs * size, 128), jnp.float32),
        ],
        compiler_params=pltpu.CompilerParams(vmem_limit_bytes=BIG),
    )(slots, x_all, g_all, router)


def expert_call(first, half, rows, grows, gates, gate, up, down):
    number, depth, _ = rows.shape
    part = gate.shape[2]
    size = depth
    while size > 768:
        size //= 2
    steps = depth // size
    bf16 = jnp.bfloat16
    f32 = jnp.float32

    def by_rows(width):
        return pl.BlockSpec((1, size, width), lambda e, r: (e, r, 0))

    def whole(*shape):
        return pl.BlockSpec((1, *shape), lambda e, r: (e, 0, 0))

    keep = (D, part) if steps > 1 else (16, 128)
    return pl.pallas_call(
        functools.partial(expert_kernel, steps, half),
        grid=(number, steps),
        in_specs=[
            pl.BlockSpec(memory_space=pltpu.SMEM),
            by_rows(D),
            by_rows(D),
            by_rows(128),
            whole(D, part),
            whole(D, part),
            whole(part, D),
        ],
        out_specs=[
            by_rows(D),
            by_rows(D),
            by_rows(128),
            whole(D, part),
            whole(D, part),
            whole(part, D),
        ],
        out_shape=[
            jax.ShapeDtypeStruct((number, depth, D), bf16),
            jax.ShapeDtypeStruct((number, depth, D), bf16),
            jax.ShapeDtypeStruct((number, depth, 128), bf16),
            jax.ShapeDtypeStruct((number, D, part), bf16),
            jax.ShapeDtypeStruct((number, D, part), bf16),
            jax.ShapeDtypeStruct((number, part, D), f32),
        ],
        scratch_shapes=[pltpu.VMEM(keep, f32), pltpu.VMEM(keep, f32)],
        compiler_params=pltpu.CompilerParams(vmem_limit_bytes=BIG),
    )(first, rows, grows, gates, gate, up, down)


def place_call(number, slots, y, dx, probs):
    pairs, _, pair = slots.shape
    bf16 = jnp.bfloat16
    size = 2 * CAP
    rows = pl.BlockSpec((number, size, D), lambda p: (0, p, 0))
    return pl.pallas_call(
        functools.partial(place_kernel, number),
        grid=(pairs,),
        in_specs=[
            pl.BlockSpec((1, number, pair), lambda p: (p, 0, 0)),
            rows,
            rows,
            pl.BlockSpec((number, size, 128), lambda p: (0, p, 0)),
        ],
        out_specs=[
            pl.BlockSpec((pair, D), lambda p: (p, 0)),
            pl.BlockSpec((pair, D + 128), lambda p: (p, 0)),
        ],
        out_shape=[
            jax.ShapeDtypeStruct((pairs * pair, D), bf16),
            jax.ShapeDtypeStruct((pairs * pair, D + 128), bf16),
        ],
        compiler_params=pltpu.CompilerParams(vmem_limit_bytes=BIG),
    )(slots, y, dx, probs)


def shards(
    n_dp,
    n_expert,
    tokens,
    cotangent,
    lengths,
    routes,
    w_query,
    w_key,
    w_value,
    w_out,
    w_router,
    gain_attn,
    gain_query,
    gain_key,
    gain_mlp,
    w_gate,
    w_up,
    w_down,
):
    groups = n_dp * n_expert
    bf16 = jnp.bfloat16
    number = w_gate.shape[0]
    ff = w_gate.shape[2]
    part = ff // n_dp
    experts_all = w_router.shape[1]
    width = 128
    small = jnp.concatenate(
        [
            w_router,
            gain_attn[:, None],
            gain_query[:, None],
            gain_key[:, None],
            gain_mlp[:, None],
            jnp.zeros((w_router.shape[0], width - experts_all - 4), bf16),
        ],
        axis=1,
    )
    hits = jnp.any(
        routes[:, :, None] == jnp.arange(width, dtype=jnp.int32)[None, None, :], axis=1
    ).astype(bf16)
    count = tokens.shape[0]
    rows_each = w_query.shape[0]
    extras = jnp.concatenate([hits, jnp.pad(small, ((0, count - rows_each), (0, 0)))], axis=1)
    weights = jnp.stack([w_query, w_key, w_value, w_out])
    depth = w_gate.shape[1]
    early = number // 4
    cut_shape = jax.ShapeDtypeStruct((number, n_dp * depth, part), bf16)

    def row_block(size):
        return lambda ref, block: ref.at[pl.ds(pl.multiple_of(block * size, 16), size)]

    def recut(low, high):
        def cuts(ins, outs):
            def pair(n):
                def source(to):
                    columns = pl.ds(pl.multiple_of(to * part, part), part)
                    return ins[n].at[pl.ds(low, high - low), :, columns]

                def target(at):
                    here = pl.ds(pl.multiple_of(at * depth, depth), depth)
                    return outs[n].at[pl.ds(low, high - low), here]

                return source, target

            return [pair(0), pair(1)]

        return cuts

    weights_all, extras_all, gate_early, up_early = gather_call(
        n_dp,
        n_expert,
        [weights, extras],
        [
            jax.ShapeDtypeStruct((4, groups * rows_each, D), bf16),
            jax.ShapeDtypeStruct((groups * count, 2 * width), bf16),
        ],
        [
            lambda ref, block: ref.at[
                :, pl.ds(pl.multiple_of(block * rows_each, 16), rows_each)
            ],
            row_block(count),
        ],
        [w_gate, w_up],
        [cut_shape, cut_shape],
        recut(0, early),
        {},
        0,
    )
    query_weight, key_weight, value_weight, out_weight = (weights_all[i] for i in range(4))
    small_all = (
        extras_all[:, width:].reshape(groups, count, width)[:, :rows_each].reshape(-1, width)
    )
    hits_all = extras_all[:, :experts_all]
    router_weight = small_all[:, :experts_all]
    gains = small_all[:, experts_all : experts_all + 4].astype(jnp.float32)
    attn_gain, query_gain, key_gain, mlp_gain = (gains[:, i] for i in range(4))
    inputs = tokens.astype(jnp.float32)
    segment, position, places = layout(lengths[0], count)
    half = HD // 2
    freq = 10000.0 ** (-2.0 * jnp.arange(half, dtype=jnp.float32) / HD)
    angle = position.astype(jnp.float32)[:, None] * freq[None, :]
    cosine = jnp.cos(angle)[:, None, :]
    sine = jnp.sin(angle)[:, None, :]
    scale = HD ** (-0.5)
    normed, attn_inverse = rms_forward(inputs, attn_gain)
    normed_low = normed.astype(bf16)
    query_raw = product(normed_low, query_weight, "td,de->te")
    key_raw = product(normed_low, key_weight, "td,de->te")
    value_low = product(normed_low, value_weight, "td,de->te").astype(bf16)
    query_normed, query_inverse = rms_forward(query_raw, query_gain)
    key_normed, key_inverse = rms_forward(key_raw, key_gain)
    query_low = rotate(query_normed, cosine, sine).astype(bf16).reshape(count, HEADS, HD)
    key_low = rotate(key_normed, cosine, sine).astype(bf16).reshape(count, HEADS, HD)
    value_heads = value_low.reshape(count, HEADS, HD)
    allowed = (segment[:, None] == segment[None, :]) & (places[None, :] <= places[:, None])
    scores = product(query_low, key_low, "qhd,khd->hqk") * scale
    scores = jnp.where(allowed[None], scores, -1e30)
    probs = jax.nn.softmax(scores, axis=-1)
    probs_low = probs.astype(bf16)
    attended_low = product(probs_low, value_heads, "hqk,khd->qhd").reshape(count, D).astype(bf16)
    middle = inputs + product(attended_low, out_weight, "td,de->te")
    mlp_normed, mlp_inverse = rms_forward(middle, mlp_gain)
    mlp_low = mlp_normed.astype(bf16)
    router = jax.nn.softmax(product(mlp_low, router_weight, "td,de->te"), axis=-1)

    mlp_all, cotangent_all, gate_cut, up_cut = gather_call(
        n_dp,
        n_expert,
        [mlp_low, cotangent],
        [jax.ShapeDtypeStruct((groups * count, D), bf16)] * 2,
        [row_block(count)] * 2,
        [w_gate, w_up, gate_early, up_early],
        [cut_shape, cut_shape],
        recut(early, number),
        {4: 2, 5: 3},
        1,
    )
    first = lax.axis_index("expert") * number
    hit = lax.dynamic_slice_in_dim(hits_all, first, number, 1).reshape(groups, count, number)
    before = jnp.tril(jnp.ones((count, count), bf16), -1)
    slot = product(before, hit, "ts,bse->bet").astype(jnp.int32)
    slot = jnp.where(jnp.transpose(hit, (0, 2, 1)) > 0, slot, -1)
    slot = slot.reshape(groups // 2, 2, number, count)
    shift = jnp.array([0, CAP], jnp.int32)[None, :, None, None]
    slots = jnp.transpose(jnp.where(slot < 0, -1, slot + shift), (0, 2, 1, 3))
    slots = slots.reshape(groups // 2, number, 2 * count)
    router_own = jnp.pad(
        jnp.roll(router_weight, -first, axis=1), ((0, 0), (0, width - experts_all))
    )
    rows, grows, gates = pick_call(number, experts_all, slots, mlp_all, cotangent_all, router_own)
    weighted, grad_rows, grad_gates, grad_gate_cut, grad_up_cut, grad_down_part = expert_call(
        first[None], experts_all, rows, grows, gates, gate_cut, up_cut, w_down
    )
    part_out, part_back = place_call(number, slots, weighted, grad_rows, grad_gates)

    def way_back(low, high):
        def cuts(ins, outs):
            def pair(n):
                def source(to):
                    here = pl.ds(pl.multiple_of(to * depth, depth), depth)
                    return ins[n].at[pl.ds(low, high - low), here]

                def target(at):
                    columns = pl.ds(pl.multiple_of(at * part, part), part)
                    return outs[n].at[:, :, columns]

                return source, target

            return [pair(0), pair(1)]

        return cuts

    def way_shape(size):
        return jax.ShapeDtypeStruct((size, depth, ff), bf16)

    back_items = [part_back.reshape(n_dp, n_expert, count, D + width)]
    sooner = number // 4
    (back,), (gate_first, up_first) = scatter_all(
        n_dp,
        n_expert,
        back_items,
        [grad_gate_cut, grad_up_cut],
        [way_shape(sooner)] * 2,
        way_back(0, sooner),
        8,
    )

    grad_final = cotangent.astype(jnp.float32)
    grad_mlp = back[:, :D]
    grad_router_probs = back[:, D : D + experts_all] + back[:, D + experts_all :]
    grad_logits = router * (
        grad_router_probs - jnp.sum(router * grad_router_probs, axis=1, keepdims=True)
    )
    grad_logits_low = grad_logits.astype(bf16)
    grad_router_full = product(mlp_low, grad_logits_low, "td,te->de")
    grad_mlp = grad_mlp + product(grad_logits_low, router_weight, "te,de->td")
    grad_middle_part, grad_mlp_gain = rms_backward(middle, mlp_inverse, mlp_gain, grad_mlp)
    grad_middle = grad_final + grad_middle_part
    grad_branch_low = grad_middle.astype(bf16)
    grad_out_full = product(attended_low, grad_branch_low, "td,te->de")
    grad_attended = (
        product(grad_branch_low, out_weight, "te,de->td").astype(bf16).reshape(count, HEADS, HD)
    )
    grad_weights = product(grad_attended, value_heads, "qhd,khd->hqk")
    grad_scores = probs * (grad_weights - jnp.sum(probs * grad_weights, axis=-1, keepdims=True))
    grad_scores_low = grad_scores.astype(bf16)
    grad_query_turn = product(grad_scores_low, key_low, "hqk,khd->qhd").reshape(count, D) * scale
    grad_key_turn = product(grad_scores_low, query_low, "hqk,qhd->khd").reshape(count, D) * scale
    grad_value_low = (
        product(probs_low, grad_attended, "hqk,qhd->khd").reshape(count, D).astype(bf16)
    )
    grad_query_raw, grad_query_gain = rms_backward(
        query_raw, query_inverse, query_gain, rotate(grad_query_turn, cosine, -sine)
    )
    grad_key_raw, grad_key_gain = rms_backward(
        key_raw, key_inverse, key_gain, rotate(grad_key_turn, cosine, -sine)
    )
    grad_query_low = grad_query_raw.astype(bf16)
    grad_key_low = grad_key_raw.astype(bf16)
    grad_query_full = product(normed_low, grad_query_low, "td,te->de")
    grad_key_full = product(normed_low, grad_key_low, "td,te->de")
    grad_value_full = product(normed_low, grad_value_low, "td,te->de")
    grad_normed = (
        product(grad_query_low, query_weight, "te,de->td")
        + product(grad_key_low, key_weight, "te,de->td")
        + product(grad_value_low, value_weight, "te,de->td")
    )
    grad_inputs_part, grad_attn_gain = rms_backward(inputs, attn_inverse, attn_gain, grad_normed)
    grad_inputs = grad_middle + grad_inputs_part

    small_grads = jnp.concatenate(
        [
            grad_router_full,
            grad_attn_gain[:, None],
            grad_query_gain[:, None],
            grad_key_gain[:, None],
            grad_mlp_gain[:, None],
            jnp.zeros((D, width - experts_all - 4), jnp.float32),
        ],
        axis=1,
    )

    def blocks_of(value):
        return value.astype(bf16).reshape(n_dp, n_expert, rows_each, -1)

    sums, (gate_last, up_last) = scatter_all(
        n_dp,
        n_expert,
        [
            blocks_of(value)
            for value in (
                grad_out_full,
                grad_value_full,
                grad_key_full,
                grad_query_full,
                small_grads,
            )
        ]
        + [part_out.reshape(n_dp, n_expert, count, D)],
        [grad_gate_cut, grad_up_cut],
        [way_shape(number - sooner)] * 2,
        way_back(sooner, number),
        16,
    )
    grad_out_part, grad_value_part, grad_key_part, grad_query_part, small_part, summed = sums
    output = (middle + summed).astype(bf16)
    grad_router_part = small_part[:, :experts_all]
    gain_parts = [small_part[:, experts_all + i] for i in range(4)]
    grad_gate_part = jnp.concatenate([gate_first, gate_last], axis=0).astype(jnp.float32)
    grad_up_part = jnp.concatenate([up_first, up_last], axis=0).astype(jnp.float32)
    return (
        output,
        grad_inputs,
        grad_query_part,
        grad_key_part,
        grad_value_part,
        grad_out_part,
        grad_router_part,
        gain_parts[0],
        gain_parts[1],
        gain_parts[2],
        gain_parts[3],
        grad_gate_part,
        grad_up_part,
        grad_down_part,
    )


def solution(mesh):
    return jax.shard_map(
        functools.partial(shards, mesh.shape["dp"], mesh.shape["expert"]),
        mesh=mesh,
        in_specs=(
            P(("dp", "expert"), None),
            P(("dp", "expert"), None),
            P(("dp", "expert"), None),
            P(("dp", "expert"), None),
            P(("dp", "expert"), None),
            P(("dp", "expert"), None),
            P(("dp", "expert"), None),
            P(("dp", "expert"), None),
            P(("dp", "expert"), None),
            P(("dp", "expert")),
            P(("dp", "expert")),
            P(("dp", "expert")),
            P(("dp", "expert")),
            P("expert", "dp", None),
            P("expert", "dp", None),
            P("expert", "dp", None),
        ),
        out_specs=(
            P(("dp", "expert"), None),
            P(("dp", "expert"), None),
            P(("dp", "expert"), None),
            P(("dp", "expert"), None),
            P(("dp", "expert"), None),
            P(("dp", "expert"), None),
            P(("dp", "expert"), None),
            P(("dp", "expert")),
            P(("dp", "expert")),
            P(("dp", "expert")),
            P(("dp", "expert")),
            P("expert", "dp", None),
            P("expert", "dp", None),
            P("expert", "dp", None),
        ),
        check_vma=False,
    )
```

```python
import functools

import jax
import jax.numpy as jnp
from jax import lax
from jax.experimental import pallas as pl
from jax.experimental.pallas import tpu as pltpu
from jax.sharding import PartitionSpec as P

D = 2048
HEADS = 16
HD = 128
TOPK = 8
CAP = 24


eps = 1e-05


def product(left, right, form):
    return jnp.einsum(form, left, right, preferred_element_type=jnp.float32)


def rms_forward(values, gain):
    inverse = lax.rsqrt(jnp.mean(values * values, axis=-1, keepdims=True) + eps)
    return (values * inverse * gain, inverse)


def rms_backward(values, inverse, gain, grad):
    scaled = grad * gain
    inner = jnp.mean(scaled * values, axis=-1, keepdims=True)
    grad_values = inverse * scaled - values * (inverse * inverse * inverse) * inner
    grad_gain = jnp.sum(grad * values * inverse, axis=0)
    return (grad_values, grad_gain)


def layout(lengths_row, count):
    places = jnp.arange(count, dtype=jnp.int32)
    ends = jnp.cumsum(lengths_row, dtype=jnp.int32)
    passed = (places[:, None] >= ends[None, :]).astype(jnp.int32)
    segment = jnp.sum(passed, axis=1, dtype=jnp.int32)
    start = jnp.sum(passed * lengths_row[None, :], axis=1, dtype=jnp.int32)
    return (segment, places - start, places)


def rotate(values, cosine, sine):
    count = values.shape[0]
    heads = values.reshape(count, HEADS, HD)
    half = HD // 2
    first = heads[..., :half]
    second = heads[..., half:]
    turned = jnp.concatenate(
        [first * cosine - second * sine, second * cosine + first * sine], axis=-1
    )
    return turned.reshape(count, D)


MESH = pl.DeviceIdType.MESH
BIG = 60 * 1024 * 1024


def place_of():
    z = lax.axis_index("dp")
    j = lax.axis_index("expert")
    return z, j, j // 2, j % 2


def other_chips(chip, chips):
    if chips == 4:
        square = [chip, chip + 1 - 2 * (chip % 2), chip + 2 - 4 * (chip // 2), 3 - chip]
        return lambda k: square[k], lambda k: square[k]
    return lambda k: (chip + k) % chips, lambda k: (chip + chips - k) % chips


def greet(n_dp, n_expert):
    z, j, chip, core = place_of()
    chips = n_expert // 2
    barrier = pltpu.get_barrier_semaphore()
    for k in range(1, n_dp):
        pl.semaphore_signal(
            barrier, inc=1, device_id=((z + k) % n_dp, j), device_id_type=MESH
        )
    for k in range(1, chips):
        other = ((chip + k) % chips) * 2 + core
        pl.semaphore_signal(barrier, inc=1, device_id=(z, other), device_id_type=MESH)
    pl.semaphore_signal(
        barrier, inc=1, device_id=(z, chip * 2 + 1 - core), device_id_type=MESH
    )
    pl.semaphore_wait(barrier, n_dp - 1 + chips - 1 + 1)


def remote(source, target, send, receive, device):
    return pltpu.make_async_remote_copy(
        src_ref=source,
        dst_ref=target,
        send_sem=send,
        recv_sem=receive,
        device_id=device,
        device_id_type=MESH,
    )


def exchange(n_dp, pairs, send, receive, local):
    z, j, chip, core = place_of()
    copies = []
    for i, (source, target) in enumerate(pairs):
        for k in range(1, n_dp):
            to = (z + k) % n_dp
            copies.append(
                remote(source(to), target(z), send.at[i, k], receive.at[i, k], (to, j))
            )
        copies.append(pltpu.make_async_copy(source(z), target(z), local.at[i]))
    return copies


def moves(pairs, local):
    return [
        pltpu.make_async_copy(source, target, local.at[i])
        for i, (source, target) in enumerate(pairs)
    ]


def nothing(ins, outs):
    return []


def gather_kernel(n_dp, n_expert, n_items, places, cuts, puts, n_cut, n_out, *refs):
    z, j, chip, core = place_of()
    chips = n_expert // 2
    square = chips == 4
    to_chip, from_chip = other_chips(chip, chips)
    sources = refs[:n_items]
    cut_in = refs[n_items : n_items + n_cut]
    at = n_items + n_cut
    targets = refs[at : at + n_items]
    cut_out = refs[at + n_items : at + n_items + n_out]
    (
        send_c,
        recv_c,
        send_b,
        recv_b,
        send_a,
        recv_a,
        local,
        send_x,
        recv_x,
        local_x,
        local_y,
    ) = refs[at + n_items + n_out :]
    greet(n_dp, n_expert)
    mate = (z, chip * 2 + 1 - core)
    near = (1, 2) if square else tuple(range(1, chips))

    def slot(i, plane, column):
        return places[i](targets[i], plane * n_expert + column)

    def pass_on(i, plane, source, column, k, chip_to):
        return remote(
            source,
            slot(i, plane, column),
            send_b.at[i, plane, k],
            recv_b.at[i, plane, k],
            (z, chip_to * 2 + core),
        )

    def hand(i, plane, source):
        for k in near:
            pass_on(i, plane, source, j, k, to_chip(k)).start()
        remote(
            source, slot(i, plane, j), send_a.at[i, plane, 0], recv_a.at[i, plane, 0], mate
        ).start()

    def along(i, plane, source, way, step):
        return remote(
            source, slot(i, plane, j), send_c.at[i, way, plane], recv_c.at[i, plane], (z + step, j)
        )

    def at_distance(d, body):
        if d == 0:
            body(z, 0)
            return

        @pl.when(z >= d)
        def _():
            body(z - d, 0)

        @pl.when(z + d < n_dp)
        def _():
            body(z + d, 1)

    for i in range(n_items):

        @pl.when(z < n_dp - 1)
        def _():
            along(i, z, sources[i], 0, 1).start()

        @pl.when(z > 0)
        def _():
            along(i, z, sources[i], 1, -1).start()

        hand(i, z, sources[i])
        pltpu.make_async_copy(sources[i], slot(i, z, j), local.at[i]).start()

    def relay(plane, way):
        step = -1 if way else 1
        for i in range(n_items):
            block = slot(i, plane, j)
            along(i, plane, block, way, step).wait_recv()

            @pl.when(z > 0 if way else z < n_dp - 1)
            def _():
                along(i, plane, block, way, step).start()

            hand(i, plane, block)

    for d in range(1, n_dp):
        at_distance(d, relay)
    copies = exchange(n_dp, cuts(cut_in, cut_out), send_x, recv_x, local_x)
    copies += moves(puts(cut_in, cut_out), local_y)
    for copy in copies:
        copy.start()

    def arrive(i, plane, k):
        column = from_chip(k) * 2 + core
        block = slot(i, plane, column)
        pass_on(i, plane, block, column, k, chip).wait_recv()
        remote(block, block, send_a.at[i, plane, k], recv_a.at[i, plane, k], mate).start()
        return block, column

    def arrived(plane, way):
        for i in range(n_items):
            for k in near:
                block, column = arrive(i, plane, k)
                if square:

                    @pl.when(plane % 2 == k - 1)
                    def _():
                        pass_on(i, plane, block, column, 3, to_chip(3 - k)).start()

    def crossed(plane, way):
        for i in range(n_items):
            arrive(i, plane, 3)

    for d in range(n_dp):
        at_distance(d, arrived)
    if square:
        for d in range(n_dp):
            at_distance(d, crossed)

    for i in range(n_items):
        for plane in range(n_dp):
            for k in range(chips):
                column = (from_chip(k) if k else chip) * 2 + 1 - core
                block = slot(i, plane, column)
                remote(
                    block, block, send_a.at[i, plane, k], recv_a.at[i, plane, k], mate
                ).wait_recv()
    for i in range(n_items):
        for plane in range(n_dp):
            block = slot(i, plane, j)
            for k in range(1, chips):
                pass_on(i, plane, block, j, k, chip).wait_send()
            for k in range(chips):
                remote(
                    block, block, send_a.at[i, plane, k], recv_a.at[i, plane, k], mate
                ).wait_send()

            @pl.when((z < n_dp - 1) & (z >= plane))
            def _():
                along(i, plane, block, 0, 1).wait_send()

            @pl.when((z > 0) & (z <= plane))
            def _():
                along(i, plane, block, 1, -1).wait_send()

        pltpu.make_async_copy(sources[i], slot(i, z, j), local.at[i]).wait()
    for copy in copies:
        copy.wait()


def gather_call(
    n_dp, n_expert, items, shapes, places, cut_in, cut_shapes, cuts, aliases, number, puts=nothing
):
    chips = n_expert // 2
    n, m = len(items), len(cut_shapes)
    dma = pltpu.SemaphoreType.DMA
    anywhere = pl.BlockSpec(memory_space=pl.ANY)
    return pl.pallas_call(
        functools.partial(gather_kernel, n_dp, n_expert, n, places, cuts, puts, len(cut_in), m),
        out_shape=[*shapes, *cut_shapes],
        in_specs=[anywhere] * (n + len(cut_in)),
        out_specs=[anywhere] * (n + m),
        scratch_shapes=[
            dma((n, 2, n_dp)),
            dma((n, n_dp)),
            dma((n, n_dp, chips)),
            dma((n, n_dp, chips)),
            dma((n, n_dp, chips)),
            dma((n, n_dp, chips)),
            dma((n,)),
            dma((4, n_dp)),
            dma((4, n_dp)),
            dma((4,)),
            dma((4 * n_dp,)),
        ],
        input_output_aliases=aliases,
        compiler_params=pltpu.CompilerParams(collective_id=number, has_side_effects=True),
    )(*items, *cut_in)


def scatter_kernel(n_dp, n_expert, n_items, n_cut, n_out, cuts, puts, rings, n_rings, *refs):
    z, j, chip, core = place_of()
    chips = n_expert // 2
    square = chips == 4
    to_chip, from_chip = other_chips(chip, chips)
    refs = list(refs)

    def take(count):
        taken = refs[:count]
        del refs[:count]
        return taken

    sources, cut_in, targets, cut_out = take(n_items), take(n_cut), take(n_items), take(n_out)
    ring, got_a, got_b, got_c = take(n_rings), take(n_items), take(n_items), take(n_items)
    transit = take(n_items)
    (
        send_a,
        recv_a,
        send_b,
        recv_b,
        send_c,
        recv_c,
        send_t,
        recv_t,
        local,
        send_x,
        recv_x,
        local_x,
        local_y,
    ) = refs
    greet(n_dp, n_expert)
    mate = (z, chip * 2 + 1 - core)
    order = [3, 1, 2, 0] if square else [*range(1, chips), 0]
    half = n_dp // 2
    low, high = pl.ds(0, half), pl.ds(half, n_dp - half)

    def chip_of(k):
        return to_chip(k) if k else chip

    def to_mate(i, k):
        return remote(
            sources[i].at[:, chip_of(k) * 2 + 1 - core],
            got_a[i].at[k],
            send_a.at[i, k],
            recv_a.at[i, k],
            mate,
        )

    turn = [0] * n_rings
    loads = []
    for i in range(n_items):
        for k in order:
            loads.append((i, k, turn[rings[i]] % 2))
            turn[rings[i]] += 1

    def load(i, k, at):
        return pltpu.make_async_copy(
            sources[i].at[:, chip_of(k) * 2 + core], ring[rings[i]].at[at], local.at[rings[i], at]
        )

    def send_near(i, k, part, number):
        return remote(
            got_a[i].at[k, part],
            got_b[i].at[k - 1, part],
            send_b.at[i, number],
            recv_b.at[i, number],
            (z, to_chip(k) * 2 + core),
        )

    def send_over(i, k, part):
        return remote(
            got_a[i].at[3, part],
            transit[i].at[k - 1],
            send_t.at[i, k],
            recv_t.at[i, k],
            (z, to_chip(k) * 2 + core),
        )

    def send_far(i, k):
        return remote(
            got_a[i].at[k],
            got_b[i].at[k - 1],
            send_b.at[i, k],
            recv_b.at[i, k],
            (z, to_chip(k) * 2 + core),
        )

    def along(i, plane, way):
        slot = n_dp - (z - 1) + plane if way else plane - (z + 1)
        return remote(
            got_a[i].at[0, plane],
            got_c[i].at[slot],
            send_c.at[i, plane],
            recv_c.at[i, slot],
            (z - 1 if way else z + 1, j),
        )

    def from_along(i, slot):
        return remote(
            got_c[i].at[slot], got_c[i].at[slot], send_c.at[i, 0], recv_c.at[i, slot], mate
        )

    f32 = jnp.float32

    def add(i, planes, target, terms):
        rows = got_a[i].shape[2]
        per = rows // 16

        def step(n, unused):
            plane = n // per
            at = pl.ds(pl.multiple_of((n % per) * 16, 16), 16)
            total = terms[0](plane, at).astype(f32)
            for term in terms[1:]:
                total = total + term(plane, at).astype(f32)
            target(plane, at, total)
            return unused

        lax.fori_loop(0, planes * per, step, 0)

    def grow(i, k, first, planes, term):
        def target(plane, at, total):
            got_a[i][k, plane + first, at] = total.astype(got_a[i].dtype)

        add(i, planes, target, [lambda plane, at: got_a[i][k, plane + first, at], term])

    for i in range(n_items):
        for k in order:
            to_mate(i, k).start()
    started = 0
    ahead = [0] * n_rings
    for i, k, at in loads:
        if ahead[rings[i]] < 2:
            load(i, k, at).start()
            ahead[rings[i]] += 1
    copies = exchange(n_dp, cuts(cut_in, cut_out), send_x, recv_x, local_x)
    copies += moves(puts(cut_in, cut_out), local_y)
    for copy in copies:
        copy.start()

    for n, (i, k, at) in enumerate(loads):
        load(i, k, at).wait()
        to_mate(i, k).wait_recv()
        grow(i, k, 0, n_dp, lambda plane, rows: ring[rings[i]][at, plane, rows])
        later = [one for one in loads[n + 1 :] if rings[one[0]] == rings[i]]
        if len(later) >= 2:
            load(*later[1]).start()
        if not k:
            continue
        if not square:
            send_far(i, k).start()
        elif k == 3:
            send_over(i, 1, low).start()
            send_over(i, 2, high).start()
        elif k == 1:
            send_near(i, 1, low, 0).start()
        else:
            send_near(i, 2, high, 1).start()
    if square:
        for i in range(n_items):
            send_over(i, 2, high).wait_recv()
            grow(i, 1, half, n_dp - half, lambda plane, rows: transit[i][1, plane, rows])
            send_near(i, 1, high, 2).start()
            send_over(i, 1, low).wait_recv()
            grow(i, 2, 0, half, lambda plane, rows: transit[i][0, plane, rows])
            send_near(i, 2, low, 3).start()
    for i in range(n_items):
        if square:
            send_near(i, 1, low, 0).wait_recv()
            send_near(i, 2, high, 1).wait_recv()
            send_near(i, 1, high, 2).wait_recv()
            send_near(i, 2, low, 3).wait_recv()
        else:
            for k in range(1, chips):
                send_far(i, k).wait_recv()
        heard = 2 if square else chips - 1

        def target(plane, at, total):
            got_a[i][0, plane, at] = total.astype(got_a[i].dtype)

        terms = [lambda plane, at: got_a[i][0, plane, at]]
        for other in range(heard):
            terms.append(lambda plane, at, other=other: got_b[i][other, plane, at])
        add(i, n_dp, target, terms)
        for d in range(n_dp - 1, 0, -1):
            for way in (0, 1):
                plane = z - d if way else z + d
                arrives = z < n_dp - 1 if way else z > 0
                slot = n_dp - z + plane if way else plane - z

                @pl.when(plane >= 0 if way else plane < n_dp)
                def _():
                    @pl.when(arrives)
                    def _():
                        from_along(i, slot).wait_recv()
                        grow(i, 0, plane, 1, lambda unused, at: got_c[i][slot, at])

                    along(i, plane, way).start()

    for i in range(n_items):

        def own(unused, at, total):
            targets[i][at] = total

        add(i, 1, own, [lambda unused, at: got_a[i][0, z, at]])
        for slot, arrives in ((0, z > 0), (n_dp, z < n_dp - 1)):

            @pl.when(arrives)
            def _():
                from_along(i, slot).wait_recv()
                add(
                    i,
                    1,
                    own,
                    [lambda unused, at: targets[i][at], lambda unused, at: got_c[i][slot, at]],
                )

    for i in range(n_items):
        for k in range(chips):
            to_mate(i, k).wait_send()
        if square:
            for k, part in ((1, low), (2, high)):
                send_over(i, k, part).wait_send()
            for k, part, number in ((1, low, 0), (2, high, 1), (1, high, 2), (2, low, 3)):
                send_near(i, k, part, number).wait_send()
        else:
            for k in range(1, chips):
                send_far(i, k).wait_send()
        for plane in range(n_dp):

            @pl.when(z != plane)
            def _():
                remote(
                    got_a[i].at[0, plane],
                    got_c[i].at[0],
                    send_c.at[i, plane],
                    recv_c.at[i, 0],
                    mate,
                ).wait_send()

    for copy in copies:
        copy.wait()


def scatter_call(
    n_dp, n_expert, items, cut_in, cut_shapes, cuts, number, aliases, puts=nothing
):
    chips = n_expert // 2
    square = chips == 4
    n, m = len(items), len(cut_shapes)
    dma = pltpu.SemaphoreType.DMA
    anywhere = pl.BlockSpec(memory_space=pl.ANY)
    blocks = [item.shape[2:] for item in items]
    kinds = sorted(set(blocks))
    rings = [kinds.index(block) for block in blocks]
    bf16 = jnp.bfloat16
    heard = 2 if square else chips - 1
    return pl.pallas_call(
        functools.partial(
            scatter_kernel, n_dp, n_expert, n, len(cut_in), m, cuts, puts, rings, len(kinds)
        ),
        out_shape=[*[jax.ShapeDtypeStruct(block, jnp.float32) for block in blocks], *cut_shapes],
        in_specs=[anywhere] * (n + len(cut_in)),
        out_specs=[pl.BlockSpec(memory_space=pltpu.VMEM)] * n + [anywhere] * m,
        scratch_shapes=[
            *[pltpu.VMEM((2, n_dp, *kind), bf16) for kind in kinds],
            *[pltpu.VMEM((chips, n_dp, *block), bf16) for block in blocks],
            *[pltpu.VMEM((heard, n_dp, *block), bf16) for block in blocks],
            *[pltpu.VMEM((n_dp + 1, *block), bf16) for block in blocks],
            *[pltpu.VMEM((2, n_dp // 2, *(block if square else (16, 128))), bf16) for block in blocks],
            dma((n, chips)),
            dma((n, chips)),
            dma((n, chips)),
            dma((n, chips)),
            dma((n, n_dp)),
            dma((n, n_dp + 1)),
            dma((n, 3)),
            dma((n, 3)),
            dma((len(kinds), 2)),
            dma((4, n_dp)),
            dma((4, n_dp)),
            dma((4,)),
            dma((4 * n_dp,)),
        ],
        input_output_aliases=aliases,
        compiler_params=pltpu.CompilerParams(
            collective_id=number, has_side_effects=True, vmem_limit_bytes=62 * 1024 * 1024
        ),
    )(*items, *cut_in)


def scatter_all(
    n_dp, n_expert, items, cut_in, cut_shapes, cuts, number, aliases=(), puts=nothing
):
    chips = n_expert // 2
    blocks = (2 * chips - 1 if chips != 4 else 7) * n_dp + n_dp + 3
    need = sum(blocks * item.shape[2] * item.shape[3] * 2 for item in items)
    kinds = {item.shape[2:] for item in items}
    need += sum(2 * n_dp * kind[0] * kind[1] * 2 for kind in kinds)
    pieces = -(-need // (61 * 1024 * 1024))
    tiles = [item.shape[3] // 128 for item in items]
    results = [[] for item in items]
    extra = []
    for piece in range(pieces):
        ends = [(t * piece // pieces * 128, t * (piece + 1) // pieces * 128) for t in tiles]
        used = [i for i, (low, high) in enumerate(ends) if high > low]
        first = piece == 0
        outs = scatter_call(
            n_dp,
            n_expert,
            [items[i][..., ends[i][0] : ends[i][1]] if pieces > 1 else items[i] for i in used],
            cut_in if first else [],
            cut_shapes if first else [],
            cuts if first else nothing,
            number + piece,
            {len(used) + a: len(used) + b for a, b in aliases} if first else {},
            puts if first else nothing,
        )
        for i, out in zip(used, outs):
            results[i].append(out)
        if first:
            extra = outs[len(used) :]
    return [one[0] if len(one) == 1 else jnp.concatenate(one, axis=1) for one in results], extra


def dot(left, right, dims):
    return lax.dot_general(
        left, right, ((dims[:1], dims[1:]), ((), ())), preferred_element_type=jnp.float32
    )


def picks(slots_ref, number):
    pair = slots_ref.shape[2]
    rows = lax.broadcasted_iota(jnp.int32, (2 * CAP, pair), 0)
    return [slots_ref[0, e : e + 1, :] == rows for e in range(number)]


def pick_kernel(number, experts_all, slots_ref, x_ref, g_ref, router_ref, rows_ref, grows_ref, gates_ref):
    chosen = picks(slots_ref, number)
    pick = jnp.concatenate(chosen, axis=0).astype(jnp.bfloat16)
    size = 2 * CAP
    x = x_ref[...]
    logits = dot(router_ref[...], x, (0, 1))
    names = lax.broadcasted_iota(jnp.int32, logits.shape, 0)
    logits = jnp.where(names < experts_all, logits, -1e30)
    weights = jnp.exp(logits - jnp.max(logits, axis=0, keepdims=True))
    probs = weights / jnp.sum(weights, axis=0, keepdims=True)
    for e in range(number):
        gate = jnp.sum(jnp.where(chosen[e], probs[e : e + 1, :], 0.0), axis=1, keepdims=True)
        gates_ref[e] = jnp.broadcast_to(gate, (size, 128))
    picked = dot(pick, x, (1, 0)).astype(jnp.bfloat16)
    for e in range(number):
        rows_ref[e] = picked[e * size : (e + 1) * size]
    picked = dot(pick, g_ref[...], (1, 0)).astype(jnp.bfloat16)
    for e in range(number):
        grows_ref[e] = picked[e * size : (e + 1) * size]


def expert_kernel(steps, half, n_weights, n_into, names_ref, x_ref, g_ref, gates_ref, *refs):
    weights, refs = refs[:n_weights], refs[n_weights:]
    down_ref, refs = refs[0], refs[1 + n_into :]
    (
        y_ref,
        dx_ref,
        probs_ref,
        dgate_ref,
        dup_ref,
        ddown_ref,
        sum_gate,
        sum_up,
    ) = refs
    bf16 = jnp.bfloat16
    g = g_ref[0]
    rows, width = x_ref.shape[1:]
    part = dgate_ref.shape[2]
    gate = gates_ref[0][:, :1]
    if n_weights == 2:
        piece = 512
        gate_ref, up_ref = weights
        gate_mid = dot(x_ref[0], gate_ref[0], (1, 0))
        up_mid = dot(x_ref[0], up_ref[0], (1, 0))
        spans = [
            (pl.ds(at, piece), gate_ref, up_ref, pl.ds(at, piece), pl.ds(0, part), pl.ds(0, part))
            for at in range(0, width, piece)
        ]
    else:
        piece = width // n_weights
        spans = []
        gate_mid = up_mid = 0.0
        for n, ref in enumerate(weights):
            span = pl.ds(pl.multiple_of(names_ref[1 + n], piece), piece)
            x_part = x_ref[0, :, span]
            gate_mid = gate_mid + dot(x_part, ref[0, :, :part], (1, 0))
            up_mid = up_mid + dot(x_part, ref[0, :, part:], (1, 0))
            spans.append((span, ref, ref, pl.ds(0, piece), pl.ds(0, part), pl.ds(part, part)))
    sigmoid = 1.0 / (1.0 + jnp.exp(-gate_mid))
    silu = gate_mid * sigmoid
    hidden = silu * up_mid
    hidden_low = hidden.astype(bf16)
    grad_plain = dot(g, down_ref[0], (1, 1))
    grad_gates = jnp.sum(grad_plain * hidden_low.astype(jnp.float32), axis=1, keepdims=True)
    high = grad_gates.astype(bf16).astype(jnp.float32)
    lane = lax.broadcasted_iota(jnp.int32, (rows, 128), 1)
    name = names_ref[0] + pl.program_id(0)
    probs_ref[0] = (
        jnp.where(lane == name, high, 0.0) + jnp.where(lane == name + half, grad_gates - high, 0.0)
    ).astype(bf16)
    grad_hidden = grad_plain * gate
    grad_gate = (
        grad_hidden * up_mid * sigmoid * (1.0 + gate_mid * (1.0 - sigmoid))
    ).astype(bf16)
    grad_up = (grad_hidden * silu).astype(bf16)
    scaled = (hidden * gate).astype(bf16)
    for at in range(0, width, piece):
        y_ref[0, :, at : at + piece] = (
            dot(hidden_low, down_ref[0, :, at : at + piece], (1, 0)) * gate
        ).astype(bf16)
    for span, gate_ref, up_ref, here, gate_columns, up_columns in spans:
        dx_ref[0, :, span] = (
            dot(grad_gate, gate_ref[0, here, gate_columns], (1, 1))
            + dot(grad_up, up_ref[0, here, up_columns], (1, 1))
        ).astype(bf16)
    step = pl.program_id(1)
    for span, *unused in spans:
        x_part = x_ref[0, :, span]
        here_gate = dot(x_part, grad_gate, (0, 0))
        here_up = dot(x_part, grad_up, (0, 0))
        here_down = dot(scaled, g_ref[0, :, span], (0, 0))
        if steps == 1:
            dgate_ref[0, span, :] = here_gate.astype(bf16)
            dup_ref[0, span, :] = here_up.astype(bf16)
            ddown_ref[0, :, span] = here_down
            continue

        @pl.when(step == 0)
        def _():
            sum_gate[span, :] = here_gate
            sum_up[span, :] = here_up
            ddown_ref[0, :, span] = here_down

        @pl.when(step > 0)
        def _():
            sum_gate[span, :] += here_gate
            sum_up[span, :] += here_up
            ddown_ref[0, :, span] += here_down

        @pl.when(step == steps - 1)
        def _():
            dgate_ref[0, span, :] = sum_gate[span, :].astype(bf16)
            dup_ref[0, span, :] = sum_up[span, :].astype(bf16)


def place_kernel(number, slots_ref, y_ref, dx_ref, probs_ref, out_ref, back_ref):
    pick = jnp.concatenate(picks(slots_ref, number), axis=0).astype(jnp.bfloat16)
    width = out_ref.shape[1]
    piece = 512
    flat = number * 2 * CAP
    for at in range(0, width, piece):
        part = y_ref[:, :, at : at + piece].reshape(flat, piece)
        out_ref[:, at : at + piece] = dot(pick, part, (0, 0)).astype(jnp.bfloat16)
        part = dx_ref[:, :, at : at + piece].reshape(flat, piece)
        back_ref[:, at : at + piece] = dot(pick, part, (0, 0)).astype(jnp.bfloat16)
    part = probs_ref[...].reshape(flat, 128)
    back_ref[:, width:] = dot(pick, part, (0, 0)).astype(jnp.bfloat16)


def pick_call(number, experts_all, slots, x_all, g_all, router):
    pairs, _, pair = slots.shape
    bf16 = jnp.bfloat16
    size = 2 * CAP
    rows = pl.BlockSpec((number, size, D), lambda p: (0, p, 0))
    tokens = pl.BlockSpec((pair, D), lambda p: (p, 0))
    return pl.pallas_call(
        functools.partial(pick_kernel, number, experts_all),
        grid=(pairs,),
        in_specs=[
            pl.BlockSpec((1, number, pair), lambda p: (p, 0, 0)),
            tokens,
            tokens,
            pl.BlockSpec(router.shape, lambda p: (0, 0)),
        ],
        out_specs=[rows, rows, pl.BlockSpec((number, size, 128), lambda p: (0, p, 0))],
        out_shape=[
            jax.ShapeDtypeStruct((number, pairs * size, D), bf16),
            jax.ShapeDtypeStruct((number, pairs * size, D), bf16),
            jax.ShapeDtypeStruct((number, pairs * size, 128), jnp.float32),
        ],
        compiler_params=pltpu.CompilerParams(vmem_limit_bytes=BIG),
    )(slots, x_all, g_all, router)


def expert_call(names, half, low, number, rows, grows, gates, weights, down, into=()):
    total, depth, _ = rows.shape
    part = down.shape[1]
    size = depth
    while size > 768:
        size //= 2
    steps = depth // size
    bf16 = jnp.bfloat16
    f32 = jnp.float32

    def from_rows(width):
        return pl.BlockSpec((1, size, width), lambda e, r: (e + low, r, 0))

    def whole(*shape):
        return pl.BlockSpec((1, *shape), lambda e, r: (e, 0, 0))

    def from_whole(*shape):
        return pl.BlockSpec((1, *shape), lambda e, r: (e + low, 0, 0))

    keep = (D, part) if steps > 1 else (16, 128)
    return pl.pallas_call(
        functools.partial(expert_kernel, steps, half, len(weights), len(into)),
        grid=(number, steps),
        in_specs=[
            pl.BlockSpec(memory_space=pltpu.SMEM),
            from_rows(D),
            from_rows(D),
            from_rows(128),
            *[(from_whole if len(weights) == 2 else whole)(*one.shape[1:]) for one in weights],
            from_whole(part, D),
            *[pl.BlockSpec(memory_space=pl.ANY)] * len(into),
        ],
        out_specs=[
            from_rows(D),
            from_rows(D),
            from_rows(128),
            whole(D, part),
            whole(D, part),
            from_whole(part, D),
        ],
        out_shape=[
            jax.ShapeDtypeStruct((total, depth, D), bf16),
            jax.ShapeDtypeStruct((total, depth, D), bf16),
            jax.ShapeDtypeStruct((total, depth, 128), bf16),
            jax.ShapeDtypeStruct((number, D, part), bf16),
            jax.ShapeDtypeStruct((number, D, part), bf16),
            jax.ShapeDtypeStruct((total, part, D), f32),
        ],
        input_output_aliases={
            5 + len(weights) + i: out for i, out in zip(range(len(into)), (0, 1, 2, 5))
        },
        scratch_shapes=[pltpu.VMEM(keep, f32), pltpu.VMEM(keep, f32)],
        compiler_params=pltpu.CompilerParams(vmem_limit_bytes=BIG),
    )(names, rows, grows, gates, *weights, down, *into)


def place_call(number, slots, y, dx, probs):
    pairs, _, pair = slots.shape
    bf16 = jnp.bfloat16
    size = 2 * CAP
    rows = pl.BlockSpec((number, size, D), lambda p: (0, p, 0))
    return pl.pallas_call(
        functools.partial(place_kernel, number),
        grid=(pairs,),
        in_specs=[
            pl.BlockSpec((1, number, pair), lambda p: (p, 0, 0)),
            rows,
            rows,
            pl.BlockSpec((number, size, 128), lambda p: (0, p, 0)),
        ],
        out_specs=[
            pl.BlockSpec((pair, D), lambda p: (p, 0)),
            pl.BlockSpec((pair, D + 128), lambda p: (p, 0)),
        ],
        out_shape=[
            jax.ShapeDtypeStruct((pairs * pair, D), bf16),
            jax.ShapeDtypeStruct((pairs * pair, D + 128), bf16),
        ],
        compiler_params=pltpu.CompilerParams(vmem_limit_bytes=BIG),
    )(slots, y, dx, probs)


def shards(
    n_dp,
    n_expert,
    tokens,
    cotangent,
    lengths,
    routes,
    w_query,
    w_key,
    w_value,
    w_out,
    w_router,
    gain_attn,
    gain_query,
    gain_key,
    gain_mlp,
    w_gate,
    w_up,
    w_down,
):
    groups = n_dp * n_expert
    bf16 = jnp.bfloat16
    number = w_gate.shape[0]
    ff = w_gate.shape[2]
    part = ff // n_dp
    experts_all = w_router.shape[1]
    width = 128
    small = jnp.concatenate(
        [
            w_router,
            gain_attn[:, None],
            gain_query[:, None],
            gain_key[:, None],
            gain_mlp[:, None],
            jnp.zeros((w_router.shape[0], width - experts_all - 4), bf16),
        ],
        axis=1,
    )
    hits = jnp.any(
        routes[:, :, None] == jnp.arange(width, dtype=jnp.int32)[None, None, :], axis=1
    ).astype(bf16)
    count = tokens.shape[0]
    rows_each = w_query.shape[0]
    extras = jnp.concatenate([hits, jnp.pad(small, ((0, count - rows_each), (0, 0)))], axis=1)
    weights = jnp.stack([w_query, w_key, w_value, w_out])
    depth = w_gate.shape[1]
    early = number // 4
    beside = early + number // 8
    late = number - number // 4
    back_beside = number // 8
    back_third = back_beside + number // 4
    back_late = back_third + number // 8
    me = lax.axis_index("dp")
    cut_shape = jax.ShapeDtypeStruct((number, n_dp * depth, part), bf16)

    def row_block(size):
        return lambda ref, block: ref.at[pl.ds(pl.multiple_of(block * size, 16), size)]

    def columns_at(at):
        return pl.ds(pl.multiple_of(at * part, part), part)

    def rows_at(at):
        return pl.ds(pl.multiple_of(at * depth, depth), depth)

    def recut(low, high):
        def cuts(ins, outs):
            def pair(n):
                chosen = pl.ds(low, high - low)
                return (
                    lambda to: ins[n].at[chosen, :, columns_at(to)],
                    lambda at: outs[n].at[chosen, rows_at(at)],
                )

            return [pair(0), pair(1)]

        return cuts

    def permuted(pieces, after):
        *pieces, unused = lax.optimization_barrier((*pieces, after))
        return [pieces[0]] + [
            lax.ppermute(pieces[k], "dp", [(i, (i + k) % n_dp) for i in range(n_dp)])
            for k in range(1, n_dp)
        ]

    def weight_pieces(low, high, after):
        return permuted(
            [
                jnp.concatenate(
                    [
                        lax.dynamic_slice_in_dim(one[low:high], (me + k) % n_dp * part, part, 2)
                        for one in (w_gate, w_up)
                    ],
                    axis=2,
                )
                for k in range(n_dp)
            ],
            after,
        )

    def grad_pieces(gate, up, low, high, after):
        return permuted(
            [
                jnp.concatenate(
                    [
                        lax.dynamic_slice_in_dim(one[low:high], (me + k) % n_dp * depth, depth, 1)
                        for one in (gate, up)
                    ],
                    axis=2,
                )
                for k in range(n_dp)
            ],
            after,
        )

    weights_all, extras_all, gate_early, up_early = gather_call(
        n_dp,
        n_expert,
        [weights, extras],
        [
            jax.ShapeDtypeStruct((4, groups * rows_each, D), bf16),
            jax.ShapeDtypeStruct((groups * count, 2 * width), bf16),
        ],
        [
            lambda ref, block: ref.at[
                :, pl.ds(pl.multiple_of(block * rows_each, 16), rows_each)
            ],
            row_block(count),
        ],
        [w_gate, w_up],
        [cut_shape, cut_shape],
        recut(0, early),
        {},
        0,
    )
    query_weight, key_weight, value_weight, out_weight = (weights_all[i] for i in range(4))
    small_all = (
        extras_all[:, width:].reshape(groups, count, width)[:, :rows_each].reshape(-1, width)
    )
    hits_all = extras_all[:, :experts_all]
    router_weight = small_all[:, :experts_all]
    gains = small_all[:, experts_all : experts_all + 4].astype(jnp.float32)
    attn_gain, query_gain, key_gain, mlp_gain = (gains[:, i] for i in range(4))
    inputs = tokens.astype(jnp.float32)
    segment, position, places = layout(lengths[0], count)
    half = HD // 2
    freq = 10000.0 ** (-2.0 * jnp.arange(half, dtype=jnp.float32) / HD)
    angle = position.astype(jnp.float32)[:, None] * freq[None, :]
    cosine = jnp.cos(angle)[:, None, :]
    sine = jnp.sin(angle)[:, None, :]
    scale = HD ** (-0.5)
    normed, attn_inverse = rms_forward(inputs, attn_gain)
    normed_low = normed.astype(bf16)
    query_raw = product(normed_low, query_weight, "td,de->te")
    key_raw = product(normed_low, key_weight, "td,de->te")
    value_low = product(normed_low, value_weight, "td,de->te").astype(bf16)
    query_normed, query_inverse = rms_forward(query_raw, query_gain)
    key_normed, key_inverse = rms_forward(key_raw, key_gain)
    query_low = rotate(query_normed, cosine, sine).astype(bf16).reshape(count, HEADS, HD)
    key_low = rotate(key_normed, cosine, sine).astype(bf16).reshape(count, HEADS, HD)
    value_heads = value_low.reshape(count, HEADS, HD)
    allowed = (segment[:, None] == segment[None, :]) & (places[None, :] <= places[:, None])
    scores = product(query_low, key_low, "qhd,khd->hqk") * scale
    scores = jnp.where(allowed[None], scores, -1e30)
    probs = jax.nn.softmax(scores, axis=-1)
    probs_low = probs.astype(bf16)
    attended_low = product(probs_low, value_heads, "hqk,khd->qhd").reshape(count, D).astype(bf16)
    middle = inputs + product(attended_low, out_weight, "td,de->te")
    mlp_normed, mlp_inverse = rms_forward(middle, mlp_gain)
    mlp_low = mlp_normed.astype(bf16)
    router = jax.nn.softmax(product(mlp_low, router_weight, "td,de->te"), axis=-1)

    pieces = []
    if beside > early:
        pieces = weight_pieces(early, beside, extras_all)
        mlp_low, *pieces = lax.optimization_barrier((mlp_low, *pieces))

    def put_weights(ins, outs):
        chosen = pl.ds(early, beside - early)
        pairs = []
        for k, piece in enumerate(ins[4:]):
            here = rows_at((lax.axis_index("dp") + n_dp - k) % n_dp)
            for n in range(2):
                columns = piece.at[:, :, pl.ds(n * part, part)]
                pairs.append((columns, outs[n].at[chosen, here]))
        return pairs

    mlp_all, cotangent_all, gate_cut, up_cut = gather_call(
        n_dp,
        n_expert,
        [mlp_low, cotangent],
        [jax.ShapeDtypeStruct((groups * count, D), bf16)] * 2,
        [row_block(count)] * 2,
        [w_gate, w_up, gate_early, up_early, *pieces],
        [cut_shape, cut_shape],
        recut(beside, late),
        {4: 2, 5: 3},
        1,
        put_weights,
    )
    late_pieces = weight_pieces(late, number, mlp_all)
    first = lax.axis_index("expert") * number
    hit = lax.dynamic_slice_in_dim(hits_all, first, number, 1).reshape(groups, count, number)
    before = jnp.tril(jnp.ones((count, count), bf16), -1)
    slot = product(before, hit, "ts,bse->bet").astype(jnp.int32)
    slot = jnp.where(jnp.transpose(hit, (0, 2, 1)) > 0, slot, -1)
    slot = slot.reshape(groups // 2, 2, number, count)
    shift = jnp.array([0, CAP], jnp.int32)[None, :, None, None]
    slots = jnp.transpose(jnp.where(slot < 0, -1, slot + shift), (0, 2, 1, 3))
    slots = slots.reshape(groups // 2, number, 2 * count)
    router_own = jnp.pad(
        jnp.roll(router_weight, -first, axis=1), ((0, 0), (0, width - experts_all))
    )
    rows, grows, gates = pick_call(number, experts_all, slots, mlp_all, cotangent_all, router_own)
    *outs, gate_soon, up_soon, down_soon = expert_call(
        first[None],
        experts_all,
        0,
        late,
        rows,
        grows,
        gates,
        [gate_cut, up_cut],
        w_down,
    )
    offsets = [(me + n_dp - k) % n_dp * depth for k in range(n_dp)]
    weighted, grad_rows, grad_gates, gate_rest, up_rest, grad_down_part = expert_call(
        jnp.stack([first + late, *offsets]),
        experts_all,
        late,
        number - late,
        rows,
        grows,
        gates,
        late_pieces,
        w_down,
        [*outs, down_soon],
    )
    part_out, part_back = place_call(number, slots, weighted, grad_rows, grad_gates)

    def ways(low, high, at, ins, outs):
        def pair(n):
            return (
                lambda to: ins[n].at[pl.ds(low, high - low), rows_at(to)],
                lambda here: outs[n].at[pl.ds(low + at, high - low), :, columns_at(here)],
            )

        return [pair(0), pair(1)]

    def put_grads(low, high, pieces, outs):
        pairs = []
        for k, piece in enumerate(pieces):
            here = columns_at((lax.axis_index("dp") + n_dp - k) % n_dp)
            for n in range(2):
                columns = piece.at[:, :, pl.ds(n * part, part)]
                pairs.append((columns, outs[n].at[pl.ds(low, high - low), :, here]))
        return pairs

    pieces = []
    if back_beside:
        pieces = grad_pieces(gate_soon, up_soon, 0, back_beside, gate_soon)
        part_back, *pieces = lax.optimization_barrier((part_back, *pieces))
    way_shapes = [jax.ShapeDtypeStruct((number, depth, ff), bf16)] * 2
    (back,), (gate_third, up_third) = scatter_all(
        n_dp,
        n_expert,
        [part_back.reshape(n_dp, n_expert, count, D + width)],
        [gate_soon, up_soon, *pieces],
        way_shapes,
        lambda ins, outs: ways(back_beside, back_third, 0, ins, outs),
        8,
        (),
        lambda ins, outs: put_grads(0, back_beside, ins[2:], outs),
    )
    pieces = []
    if back_late > back_third:
        pieces = grad_pieces(gate_soon, up_soon, back_third, back_late, back)
        part_out, *pieces = lax.optimization_barrier((part_out, *pieces))

    grad_final = cotangent.astype(jnp.float32)
    grad_mlp = back[:, :D]
    grad_router_probs = back[:, D : D + experts_all] + back[:, D + experts_all :]
    grad_logits = router * (
        grad_router_probs - jnp.sum(router * grad_router_probs, axis=1, keepdims=True)
    )
    grad_logits_low = grad_logits.astype(bf16)
    grad_router_full = product(mlp_low, grad_logits_low, "td,te->de")
    grad_mlp = grad_mlp + product(grad_logits_low, router_weight, "te,de->td")
    grad_middle_part, grad_mlp_gain = rms_backward(middle, mlp_inverse, mlp_gain, grad_mlp)
    grad_middle = grad_final + grad_middle_part
    grad_branch_low = grad_middle.astype(bf16)
    grad_out_full = product(attended_low, grad_branch_low, "td,te->de")
    grad_attended = (
        product(grad_branch_low, out_weight, "te,de->td").astype(bf16).reshape(count, HEADS, HD)
    )
    grad_weights = product(grad_attended, value_heads, "qhd,khd->hqk")
    grad_scores = probs * (grad_weights - jnp.sum(probs * grad_weights, axis=-1, keepdims=True))
    grad_scores_low = grad_scores.astype(bf16)
    grad_query_turn = product(grad_scores_low, key_low, "hqk,khd->qhd").reshape(count, D) * scale
    grad_key_turn = product(grad_scores_low, query_low, "hqk,qhd->khd").reshape(count, D) * scale
    grad_value_low = (
        product(probs_low, grad_attended, "hqk,qhd->khd").reshape(count, D).astype(bf16)
    )
    grad_query_raw, grad_query_gain = rms_backward(
        query_raw, query_inverse, query_gain, rotate(grad_query_turn, cosine, -sine)
    )
    grad_key_raw, grad_key_gain = rms_backward(
        key_raw, key_inverse, key_gain, rotate(grad_key_turn, cosine, -sine)
    )
    grad_query_low = grad_query_raw.astype(bf16)
    grad_key_low = grad_key_raw.astype(bf16)
    grad_query_full = product(normed_low, grad_query_low, "td,te->de")
    grad_key_full = product(normed_low, grad_key_low, "td,te->de")
    grad_value_full = product(normed_low, grad_value_low, "td,te->de")
    grad_normed = (
        product(grad_query_low, query_weight, "te,de->td")
        + product(grad_key_low, key_weight, "te,de->td")
        + product(grad_value_low, value_weight, "te,de->td")
    )
    grad_inputs_part, grad_attn_gain = rms_backward(inputs, attn_inverse, attn_gain, grad_normed)
    grad_inputs = grad_middle + grad_inputs_part

    small_grads = jnp.concatenate(
        [
            grad_router_full,
            grad_attn_gain[:, None],
            grad_query_gain[:, None],
            grad_key_gain[:, None],
            grad_mlp_gain[:, None],
            jnp.zeros((D, width - experts_all - 4), jnp.float32),
        ],
        axis=1,
    )

    def blocks_of(value):
        return value.astype(bf16).reshape(n_dp, n_expert, rows_each, -1)

    sums, (gate_back, up_back) = scatter_all(
        n_dp,
        n_expert,
        [
            blocks_of(value)
            for value in (
                grad_out_full,
                grad_value_full,
                grad_key_full,
                grad_query_full,
                small_grads,
            )
        ]
        + [part_out.reshape(n_dp, n_expert, count, D)],
        [gate_third, up_third, gate_soon, up_soon, gate_rest, up_rest, *pieces],
        way_shapes,
        lambda ins, outs: ways(back_late, late, 0, ins[2:4], outs)
        + ways(0, number - late, late, ins[4:6], outs),
        16,
        ((0, 0), (1, 1)),
        lambda ins, outs: put_grads(back_third, back_late, ins[6:], outs),
    )
    grad_out_part, grad_value_part, grad_key_part, grad_query_part, small_part, summed = sums
    output = (middle + summed).astype(bf16)
    grad_router_part = small_part[:, :experts_all]
    gain_parts = [small_part[:, experts_all + i] for i in range(4)]
    grad_gate_part = gate_back.astype(jnp.float32)
    grad_up_part = up_back.astype(jnp.float32)
    return (
        output,
        grad_inputs,
        grad_query_part,
        grad_key_part,
        grad_value_part,
        grad_out_part,
        grad_router_part,
        gain_parts[0],
        gain_parts[1],
        gain_parts[2],
        gain_parts[3],
        grad_gate_part,
        grad_up_part,
        grad_down_part,
    )


def solution(mesh):
    return jax.shard_map(
        functools.partial(shards, mesh.shape["dp"], mesh.shape["expert"]),
        mesh=mesh,
        in_specs=(
            P(("dp", "expert"), None),
            P(("dp", "expert"), None),
            P(("dp", "expert"), None),
            P(("dp", "expert"), None),
            P(("dp", "expert"), None),
            P(("dp", "expert"), None),
            P(("dp", "expert"), None),
            P(("dp", "expert"), None),
            P(("dp", "expert"), None),
            P(("dp", "expert")),
            P(("dp", "expert")),
            P(("dp", "expert")),
            P(("dp", "expert")),
            P("expert", "dp", None),
            P("expert", "dp", None),
            P("expert", "dp", None),
        ),
        out_specs=(
            P(("dp", "expert"), None),
            P(("dp", "expert"), None),
            P(("dp", "expert"), None),
            P(("dp", "expert"), None),
            P(("dp", "expert"), None),
            P(("dp", "expert"), None),
            P(("dp", "expert"), None),
            P(("dp", "expert")),
            P(("dp", "expert")),
            P(("dp", "expert")),
            P(("dp", "expert")),
            P("expert", "dp", None),
            P("expert", "dp", None),
            P("expert", "dp", None),
        ),
        check_vma=False,
    )
```

```python
import functools

import jax
import jax.numpy as jnp
from jax import lax
from jax.experimental import pallas as pl
from jax.experimental.pallas import tpu as pltpu
from jax.sharding import PartitionSpec as P

D = 2048
HEADS = 16
HD = 128
TOPK = 8
CAP = 24


eps = 1e-05


def product(left, right, form):
    return jnp.einsum(form, left, right, preferred_element_type=jnp.float32)


def rms_forward(values, gain):
    inverse = lax.rsqrt(jnp.mean(values * values, axis=-1, keepdims=True) + eps)
    return (values * inverse * gain, inverse)


def rms_backward(values, inverse, gain, grad):
    scaled = grad * gain
    inner = jnp.mean(scaled * values, axis=-1, keepdims=True)
    grad_values = inverse * scaled - values * (inverse * inverse * inverse) * inner
    grad_gain = jnp.sum(grad * values * inverse, axis=0)
    return (grad_values, grad_gain)


def layout(lengths_row, count):
    places = jnp.arange(count, dtype=jnp.int32)
    ends = jnp.cumsum(lengths_row, dtype=jnp.int32)
    passed = (places[:, None] >= ends[None, :]).astype(jnp.int32)
    segment = jnp.sum(passed, axis=1, dtype=jnp.int32)
    start = jnp.sum(passed * lengths_row[None, :], axis=1, dtype=jnp.int32)
    return (segment, places - start, places)


def rotate(values, cosine, sine):
    count = values.shape[0]
    heads = values.reshape(count, HEADS, HD)
    half = HD // 2
    first = heads[..., :half]
    second = heads[..., half:]
    turned = jnp.concatenate(
        [first * cosine - second * sine, second * cosine + first * sine], axis=-1
    )
    return turned.reshape(count, D)


MESH = pl.DeviceIdType.MESH
BIG = 60 * 1024 * 1024


def place_of():
    z = lax.axis_index("dp")
    j = lax.axis_index("expert")
    return z, j, j // 2, j % 2


def other_chips(chip, chips):
    if chips == 4:
        square = [chip, chip + 1 - 2 * (chip % 2), chip + 2 - 4 * (chip // 2), 3 - chip]
        return lambda k: square[k], lambda k: square[k]
    return lambda k: (chip + k) % chips, lambda k: (chip + chips - k) % chips


def partners(z, n_dp):
    if n_dp == 4:
        pairs = [z, (z + 2) % 4, 3 - z, z + 1 - 2 * (z % 2)]
        return lambda k: pairs[k], lambda k: pairs[k]
    return lambda k: (z + k) % n_dp, lambda k: (z + n_dp - k) % n_dp


def greet(n_dp, n_expert):
    z, j, chip, core = place_of()
    chips = n_expert // 2
    barrier = pltpu.get_barrier_semaphore()
    for k in range(1, n_dp):
        pl.semaphore_signal(
            barrier, inc=1, device_id=((z + k) % n_dp, j), device_id_type=MESH
        )
    for k in range(1, chips):
        other = ((chip + k) % chips) * 2 + core
        pl.semaphore_signal(barrier, inc=1, device_id=(z, other), device_id_type=MESH)
    pl.semaphore_signal(
        barrier, inc=1, device_id=(z, chip * 2 + 1 - core), device_id_type=MESH
    )
    pl.semaphore_wait(barrier, n_dp - 1 + chips - 1 + 1)


def remote(source, target, send, receive, device):
    return pltpu.make_async_remote_copy(
        src_ref=source,
        dst_ref=target,
        send_sem=send,
        recv_sem=receive,
        device_id=device,
        device_id_type=MESH,
    )


def exchange(n_dp, pairs, send, receive, local):
    z, j, chip, core = place_of()
    to_plane, unused = partners(z, n_dp)
    copies = []
    for i, (source, target) in enumerate(pairs):
        for k in range(1, n_dp):
            to = to_plane(k)
            copies.append(
                remote(source(to), target(z), send.at[i, k], receive.at[i, k], (to, j))
            )
        copies.append(pltpu.make_async_copy(source(z), target(z), local.at[i]))
    return copies


def moves(pairs, local):
    return [
        pltpu.make_async_copy(source, target, local.at[i])
        for i, (source, target) in enumerate(pairs)
    ]


def nothing(ins, outs):
    return []


def gather_kernel(n_dp, n_expert, n_items, places, cuts, puts, finish, n_cut, n_out, *refs):
    z, j, chip, core = place_of()
    chips = n_expert // 2
    square = chips == 4
    to_chip, from_chip = other_chips(chip, chips)
    sources = refs[:n_items]
    cut_in = refs[n_items : n_items + n_cut]
    at = n_items + n_cut
    targets = refs[at : at + n_items]
    cut_out = refs[at + n_items : at + n_items + n_out]
    (
        send_c,
        recv_c,
        send_b,
        recv_b,
        send_a,
        recv_a,
        local,
        send_x,
        recv_x,
        local_x,
        local_y,
    ) = refs[at + n_items + n_out :]
    greet(n_dp, n_expert)
    mate = (z, chip * 2 + 1 - core)
    near = (1, 2) if square else tuple(range(1, chips))

    def slot(i, plane, column):
        return places[i](targets[i], plane * n_expert + column)

    def pass_on(i, plane, source, column, k, chip_to):
        return remote(
            source,
            slot(i, plane, column),
            send_b.at[i, plane, k],
            recv_b.at[i, plane, k],
            (z, chip_to * 2 + core),
        )

    def hand(i, plane, source):
        for k in near:
            pass_on(i, plane, source, j, k, to_chip(k)).start()
        remote(
            source, slot(i, plane, j), send_a.at[i, plane, 0], recv_a.at[i, plane, 0], mate
        ).start()

    def along(i, plane, source, way, step):
        return remote(
            source, slot(i, plane, j), send_c.at[i, way, plane], recv_c.at[i, plane], (z + step, j)
        )

    def at_distance(d, body):
        if d == 0:
            body(z, 0)
            return

        @pl.when(z >= d)
        def _():
            body(z - d, 0)

        @pl.when(z + d < n_dp)
        def _():
            body(z + d, 1)

    for i in range(n_items):

        @pl.when(z < n_dp - 1)
        def _():
            along(i, z, sources[i], 0, 1).start()

        @pl.when(z > 0)
        def _():
            along(i, z, sources[i], 1, -1).start()

        hand(i, z, sources[i])
        pltpu.make_async_copy(sources[i], slot(i, z, j), local.at[i]).start()

    def relay(plane, way):
        step = -1 if way else 1
        for i in range(n_items):
            block = slot(i, plane, j)
            along(i, plane, block, way, step).wait_recv()

            @pl.when(z > 0 if way else z < n_dp - 1)
            def _():
                along(i, plane, block, way, step).start()

            hand(i, plane, block)

    for d in range(1, n_dp):
        at_distance(d, relay)
    copies = exchange(n_dp, cuts(cut_in, cut_out), send_x, recv_x, local_x)
    copies += moves(puts(cut_in, cut_out), local_y)
    for copy in copies:
        copy.start()

    def arrive(i, plane, k):
        column = from_chip(k) * 2 + core
        block = slot(i, plane, column)
        pass_on(i, plane, block, column, k, chip).wait_recv()
        remote(block, block, send_a.at[i, plane, k], recv_a.at[i, plane, k], mate).start()
        return block, column

    def arrived(plane, way):
        for i in range(n_items):
            for k in near:
                block, column = arrive(i, plane, k)
                if square:

                    @pl.when(plane % 2 == k - 1)
                    def _():
                        pass_on(i, plane, block, column, 3, to_chip(3 - k)).start()

    def crossed(plane, way):
        for i in range(n_items):
            arrive(i, plane, 3)

    for d in range(n_dp):
        at_distance(d, arrived)
    if square:
        for d in range(n_dp):
            at_distance(d, crossed)

    for i in range(n_items):
        for plane in range(n_dp):
            for k in range(chips):
                column = (from_chip(k) if k else chip) * 2 + 1 - core
                block = slot(i, plane, column)
                remote(
                    block, block, send_a.at[i, plane, k], recv_a.at[i, plane, k], mate
                ).wait_recv()
        pltpu.make_async_copy(sources[i], slot(i, z, j), local.at[i]).wait()
    finish(targets, cut_in, cut_out)
    for i in range(n_items):
        for plane in range(n_dp):
            block = slot(i, plane, j)
            for k in range(1, chips):
                pass_on(i, plane, block, j, k, chip).wait_send()
            for k in range(chips):
                remote(
                    block, block, send_a.at[i, plane, k], recv_a.at[i, plane, k], mate
                ).wait_send()

            @pl.when((z < n_dp - 1) & (z >= plane))
            def _():
                along(i, plane, block, 0, 1).wait_send()

            @pl.when((z > 0) & (z <= plane))
            def _():
                along(i, plane, block, 1, -1).wait_send()

    for copy in copies:
        copy.wait()


def gather_call(
    n_dp,
    n_expert,
    items,
    shapes,
    places,
    cut_in,
    cut_shapes,
    cuts,
    aliases,
    number,
    puts=nothing,
    finish=lambda items, ins, outs: None,
):
    chips = n_expert // 2
    n, m = len(items), len(cut_shapes)
    dma = pltpu.SemaphoreType.DMA
    anywhere = pl.BlockSpec(memory_space=pl.ANY)
    return pl.pallas_call(
        functools.partial(
            gather_kernel, n_dp, n_expert, n, places, cuts, puts, finish, len(cut_in), m
        ),
        out_shape=[*shapes, *cut_shapes],
        in_specs=[anywhere] * (n + len(cut_in)),
        out_specs=[anywhere] * (n + m),
        scratch_shapes=[
            dma((n, 2, n_dp)),
            dma((n, n_dp)),
            dma((n, n_dp, chips)),
            dma((n, n_dp, chips)),
            dma((n, n_dp, chips)),
            dma((n, n_dp, chips)),
            dma((n,)),
            dma((4, n_dp)),
            dma((4, n_dp)),
            dma((4,)),
            dma((4 * n_dp,)),
        ],
        input_output_aliases=aliases,
        compiler_params=pltpu.CompilerParams(
            collective_id=number, has_side_effects=True, vmem_limit_bytes=BIG
        ),
    )(*items, *cut_in)


def scatter_kernel(n_dp, n_expert, n_items, n_cut, n_out, cuts, puts, rings, n_rings, *refs):
    z, j, chip, core = place_of()
    chips = n_expert // 2
    square = chips == 4
    to_chip, from_chip = other_chips(chip, chips)
    refs = list(refs)

    def take(count):
        taken = refs[:count]
        del refs[:count]
        return taken

    sources, cut_in, targets, cut_out = take(n_items), take(n_cut), take(n_items), take(n_out)
    ring, got_a, got_b, got_c = take(n_rings), take(n_items), take(n_items), take(n_items)
    transit = take(n_items)
    (
        send_a,
        recv_a,
        send_b,
        recv_b,
        send_c,
        recv_c,
        send_t,
        recv_t,
        local,
        send_x,
        recv_x,
        local_x,
        local_y,
    ) = refs
    greet(n_dp, n_expert)
    mate = (z, chip * 2 + 1 - core)
    order = [3, 1, 2, 0] if square else [*range(1, chips), 0]
    half = n_dp // 2
    low, high = pl.ds(0, half), pl.ds(half, n_dp - half)

    def chip_of(k):
        return to_chip(k) if k else chip

    def to_mate(i, k):
        return remote(
            sources[i].at[:, chip_of(k) * 2 + 1 - core],
            got_a[i].at[k],
            send_a.at[i, k],
            recv_a.at[i, k],
            mate,
        )

    turn = [0] * n_rings
    loads = []
    for i in range(n_items):
        for k in order:
            loads.append((i, k, turn[rings[i]] % 2))
            turn[rings[i]] += 1

    def load(i, k, at):
        return pltpu.make_async_copy(
            sources[i].at[:, chip_of(k) * 2 + core], ring[rings[i]].at[at], local.at[rings[i], at]
        )

    def send_near(i, k, part, number):
        return remote(
            got_a[i].at[k, part],
            got_b[i].at[k - 1, part],
            send_b.at[i, number],
            recv_b.at[i, number],
            (z, to_chip(k) * 2 + core),
        )

    def send_over(i, k, part):
        return remote(
            got_a[i].at[3, part],
            transit[i].at[k - 1],
            send_t.at[i, k],
            recv_t.at[i, k],
            (z, to_chip(k) * 2 + core),
        )

    def send_far(i, k):
        return remote(
            got_a[i].at[k],
            got_b[i].at[k - 1],
            send_b.at[i, k],
            recv_b.at[i, k],
            (z, to_chip(k) * 2 + core),
        )

    def along(i, plane, way):
        slot = n_dp - (z - 1) + plane if way else plane - (z + 1)
        return remote(
            got_a[i].at[0, plane],
            got_c[i].at[slot],
            send_c.at[i, plane],
            recv_c.at[i, slot],
            (z - 1 if way else z + 1, j),
        )

    def from_along(i, slot):
        return remote(
            got_c[i].at[slot], got_c[i].at[slot], send_c.at[i, 0], recv_c.at[i, slot], mate
        )

    f32 = jnp.float32

    def add(i, planes, target, terms):
        rows = got_a[i].shape[2]
        per = rows // 16

        def step(n, unused):
            plane = n // per
            at = pl.ds(pl.multiple_of((n % per) * 16, 16), 16)
            total = terms[0](plane, at).astype(f32)
            for term in terms[1:]:
                total = total + term(plane, at).astype(f32)
            target(plane, at, total)
            return unused

        lax.fori_loop(0, planes * per, step, 0)

    def grow(i, k, first, planes, term):
        def target(plane, at, total):
            got_a[i][k, plane + first, at] = total.astype(got_a[i].dtype)

        add(i, planes, target, [lambda plane, at: got_a[i][k, plane + first, at], term])

    for i in range(n_items):
        for k in order:
            to_mate(i, k).start()
    started = 0
    ahead = [0] * n_rings
    for i, k, at in loads:
        if ahead[rings[i]] < 2:
            load(i, k, at).start()
            ahead[rings[i]] += 1
    copies = exchange(n_dp, cuts(cut_in, cut_out), send_x, recv_x, local_x)
    copies += moves(puts(cut_in, cut_out), local_y)
    for copy in copies:
        copy.start()

    for n, (i, k, at) in enumerate(loads):
        load(i, k, at).wait()
        to_mate(i, k).wait_recv()
        grow(i, k, 0, n_dp, lambda plane, rows: ring[rings[i]][at, plane, rows])
        later = [one for one in loads[n + 1 :] if rings[one[0]] == rings[i]]
        if len(later) >= 2:
            load(*later[1]).start()
        if not k:
            continue
        if not square:
            send_far(i, k).start()
        elif k == 3:
            send_over(i, 1, low).start()
            send_over(i, 2, high).start()
        elif k == 1:
            send_near(i, 1, low, 0).start()
        else:
            send_near(i, 2, high, 1).start()
    if square:
        for i in range(n_items):
            send_over(i, 2, high).wait_recv()
            grow(i, 1, half, n_dp - half, lambda plane, rows: transit[i][1, plane, rows])
            send_near(i, 1, high, 2).start()
            send_over(i, 1, low).wait_recv()
            grow(i, 2, 0, half, lambda plane, rows: transit[i][0, plane, rows])
            send_near(i, 2, low, 3).start()
    for i in range(n_items):
        if square:
            send_near(i, 1, low, 0).wait_recv()
            send_near(i, 2, high, 1).wait_recv()
            send_near(i, 1, high, 2).wait_recv()
            send_near(i, 2, low, 3).wait_recv()
        else:
            for k in range(1, chips):
                send_far(i, k).wait_recv()
        heard = 2 if square else chips - 1

        def target(plane, at, total):
            got_a[i][0, plane, at] = total.astype(got_a[i].dtype)

        terms = [lambda plane, at: got_a[i][0, plane, at]]
        for other in range(heard):
            terms.append(lambda plane, at, other=other: got_b[i][other, plane, at])
        add(i, n_dp, target, terms)
        for d in range(n_dp - 1, 0, -1):
            for way in (0, 1):
                plane = z - d if way else z + d
                arrives = z < n_dp - 1 if way else z > 0
                slot = n_dp - z + plane if way else plane - z

                @pl.when(plane >= 0 if way else plane < n_dp)
                def _():
                    @pl.when(arrives)
                    def _():
                        from_along(i, slot).wait_recv()
                        grow(i, 0, plane, 1, lambda unused, at: got_c[i][slot, at])

                    along(i, plane, way).start()

    for i in range(n_items):

        def own(unused, at, total):
            targets[i][at] = total

        add(i, 1, own, [lambda unused, at: got_a[i][0, z, at]])
        for slot, arrives in ((0, z > 0), (n_dp, z < n_dp - 1)):

            @pl.when(arrives)
            def _():
                from_along(i, slot).wait_recv()
                add(
                    i,
                    1,
                    own,
                    [lambda unused, at: targets[i][at], lambda unused, at: got_c[i][slot, at]],
                )

    for i in range(n_items):
        for k in range(chips):
            to_mate(i, k).wait_send()
        if square:
            for k, part in ((1, low), (2, high)):
                send_over(i, k, part).wait_send()
            for k, part, number in ((1, low, 0), (2, high, 1), (1, high, 2), (2, low, 3)):
                send_near(i, k, part, number).wait_send()
        else:
            for k in range(1, chips):
                send_far(i, k).wait_send()
        for plane in range(n_dp):

            @pl.when(z != plane)
            def _():
                remote(
                    got_a[i].at[0, plane],
                    got_c[i].at[0],
                    send_c.at[i, plane],
                    recv_c.at[i, 0],
                    mate,
                ).wait_send()

    for copy in copies:
        copy.wait()


def scatter_call(
    n_dp, n_expert, items, cut_in, cut_shapes, cuts, number, aliases, puts=nothing
):
    chips = n_expert // 2
    square = chips == 4
    n, m = len(items), len(cut_shapes)
    dma = pltpu.SemaphoreType.DMA
    anywhere = pl.BlockSpec(memory_space=pl.ANY)
    blocks = [item.shape[2:] for item in items]
    kinds = sorted(set(blocks))
    rings = [kinds.index(block) for block in blocks]
    bf16 = jnp.bfloat16
    heard = 2 if square else chips - 1
    return pl.pallas_call(
        functools.partial(
            scatter_kernel, n_dp, n_expert, n, len(cut_in), m, cuts, puts, rings, len(kinds)
        ),
        out_shape=[*[jax.ShapeDtypeStruct(block, jnp.float32) for block in blocks], *cut_shapes],
        in_specs=[anywhere] * (n + len(cut_in)),
        out_specs=[pl.BlockSpec(memory_space=pltpu.VMEM)] * n + [anywhere] * m,
        scratch_shapes=[
            *[pltpu.VMEM((2, n_dp, *kind), bf16) for kind in kinds],
            *[pltpu.VMEM((chips, n_dp, *block), bf16) for block in blocks],
            *[pltpu.VMEM((heard, n_dp, *block), bf16) for block in blocks],
            *[pltpu.VMEM((n_dp + 1, *block), bf16) for block in blocks],
            *[pltpu.VMEM((2, n_dp // 2, *(block if square else (16, 128))), bf16) for block in blocks],
            dma((n, chips)),
            dma((n, chips)),
            dma((n, chips)),
            dma((n, chips)),
            dma((n, n_dp)),
            dma((n, n_dp + 1)),
            dma((n, 3)),
            dma((n, 3)),
            dma((len(kinds), 2)),
            dma((4, n_dp)),
            dma((4, n_dp)),
            dma((4,)),
            dma((4 * n_dp,)),
        ],
        input_output_aliases=aliases,
        compiler_params=pltpu.CompilerParams(
            collective_id=number, has_side_effects=True, vmem_limit_bytes=62 * 1024 * 1024
        ),
    )(*items, *cut_in)


def scatter_all(
    n_dp, n_expert, items, cut_in, cut_shapes, cuts, number, aliases=(), puts=nothing
):
    chips = n_expert // 2
    blocks = (2 * chips - 1 if chips != 4 else 7) * n_dp + n_dp + 3
    need = sum(blocks * item.shape[2] * item.shape[3] * 2 for item in items)
    kinds = {item.shape[2:] for item in items}
    need += sum(2 * n_dp * kind[0] * kind[1] * 2 for kind in kinds)
    pieces = -(-need // (61 * 1024 * 1024))
    tiles = [item.shape[3] // 128 for item in items]
    results = [[] for item in items]
    extra = []
    for piece in range(pieces):
        ends = [(t * piece // pieces * 128, t * (piece + 1) // pieces * 128) for t in tiles]
        used = [i for i, (low, high) in enumerate(ends) if high > low]
        first = piece == 0
        outs = scatter_call(
            n_dp,
            n_expert,
            [items[i][..., ends[i][0] : ends[i][1]] if pieces > 1 else items[i] for i in used],
            cut_in if first else [],
            cut_shapes if first else [],
            cuts if first else nothing,
            number + piece,
            {len(used) + a: len(used) + b for a, b in aliases} if first else {},
            puts if first else nothing,
        )
        for i, out in zip(used, outs):
            results[i].append(out)
        if first:
            extra = outs[len(used) :]
    return [one[0] if len(one) == 1 else jnp.concatenate(one, axis=1) for one in results], extra


def dot(left, right, dims):
    return lax.dot_general(
        left, right, ((dims[:1], dims[1:]), ((), ())), preferred_element_type=jnp.float32
    )


def picks(slots_ref, number):
    pair = slots_ref.shape[2]
    rows = lax.broadcasted_iota(jnp.int32, (2 * CAP, pair), 0)
    return [slots_ref[0, e : e + 1, :] == rows for e in range(number)]


def pick_kernel(number, experts_all, slots_ref, x_ref, g_ref, router_ref, rows_ref, grows_ref, gates_ref):
    chosen = picks(slots_ref, number)
    pick = jnp.concatenate(chosen, axis=0).astype(jnp.bfloat16)
    size = 2 * CAP
    x = x_ref[...]
    logits = dot(router_ref[...], x, (0, 1))
    names = lax.broadcasted_iota(jnp.int32, logits.shape, 0)
    logits = jnp.where(names < experts_all, logits, -1e30)
    weights = jnp.exp(logits - jnp.max(logits, axis=0, keepdims=True))
    probs = weights / jnp.sum(weights, axis=0, keepdims=True)
    for e in range(number):
        gate = jnp.sum(jnp.where(chosen[e], probs[e : e + 1, :], 0.0), axis=1, keepdims=True)
        gates_ref[e] = jnp.broadcast_to(gate, (size, 128))
    picked = dot(pick, x, (1, 0)).astype(jnp.bfloat16)
    for e in range(number):
        rows_ref[e] = picked[e * size : (e + 1) * size]
    picked = dot(pick, g_ref[...], (1, 0)).astype(jnp.bfloat16)
    for e in range(number):
        grows_ref[e] = picked[e * size : (e + 1) * size]


def expert_kernel(steps, half, n_weights, n_into, n_pack, names_ref, x_ref, g_ref, gates_ref, *refs):
    weights, refs = refs[:n_weights], refs[n_weights:]
    down_ref, refs = refs[0], refs[1 + n_into :]
    (
        y_ref,
        dx_ref,
        probs_ref,
        dgate_ref,
        dup_ref,
        ddown_ref,
        *pack_refs,
        sum_gate,
        sum_up,
    ) = refs
    bf16 = jnp.bfloat16
    g = g_ref[0]
    rows, width = x_ref.shape[1:]
    part = dgate_ref.shape[2]
    gate = gates_ref[0][:, :1]
    if n_weights == 2:
        piece = 512
        gate_ref, up_ref = weights
        gate_mid = dot(x_ref[0], gate_ref[0], (1, 0))
        up_mid = dot(x_ref[0], up_ref[0], (1, 0))
        spans = [
            (pl.ds(at, piece), gate_ref, up_ref, pl.ds(at, piece), pl.ds(0, part), pl.ds(0, part))
            for at in range(0, width, piece)
        ]
    else:
        piece = width // n_weights
        spans = []
        gate_mid = up_mid = 0.0
        for n, ref in enumerate(weights):
            span = pl.ds(pl.multiple_of(names_ref[1 + n], piece), piece)
            x_part = x_ref[0, :, span]
            gate_mid = gate_mid + dot(x_part, ref[0, :, :part], (1, 0))
            up_mid = up_mid + dot(x_part, ref[0, :, part:], (1, 0))
            spans.append((span, ref, ref, pl.ds(0, piece), pl.ds(0, part), pl.ds(part, part)))
    sigmoid = 1.0 / (1.0 + jnp.exp(-gate_mid))
    silu = gate_mid * sigmoid
    hidden = silu * up_mid
    hidden_low = hidden.astype(bf16)
    grad_plain = dot(g, down_ref[0], (1, 1))
    grad_gates = jnp.sum(grad_plain * hidden_low.astype(jnp.float32), axis=1, keepdims=True)
    high = grad_gates.astype(bf16).astype(jnp.float32)
    lane = lax.broadcasted_iota(jnp.int32, (rows, 128), 1)
    name = names_ref[0] + pl.program_id(0)
    probs_ref[0] = (
        jnp.where(lane == name, high, 0.0) + jnp.where(lane == name + half, grad_gates - high, 0.0)
    ).astype(bf16)
    grad_hidden = grad_plain * gate
    grad_gate = (
        grad_hidden * up_mid * sigmoid * (1.0 + gate_mid * (1.0 - sigmoid))
    ).astype(bf16)
    grad_up = (grad_hidden * silu).astype(bf16)
    scaled = (hidden * gate).astype(bf16)
    for at in range(0, width, piece):
        y_ref[0, :, at : at + piece] = (
            dot(hidden_low, down_ref[0, :, at : at + piece], (1, 0)) * gate
        ).astype(bf16)
    for span, gate_ref, up_ref, here, gate_columns, up_columns in spans:
        dx_ref[0, :, span] = (
            dot(grad_gate, gate_ref[0, here, gate_columns], (1, 1))
            + dot(grad_up, up_ref[0, here, up_columns], (1, 1))
        ).astype(bf16)
    step = pl.program_id(1)
    for span, *unused in spans:
        x_part = x_ref[0, :, span]
        here_gate = dot(x_part, grad_gate, (0, 0))
        here_up = dot(x_part, grad_up, (0, 0))
        here_down = dot(scaled, g_ref[0, :, span], (0, 0))
        if steps == 1:
            dgate_ref[0, span, :] = here_gate.astype(bf16)
            dup_ref[0, span, :] = here_up.astype(bf16)
            ddown_ref[0, :, span] = here_down
            continue

        @pl.when(step == 0)
        def _():
            sum_gate[span, :] = here_gate
            sum_up[span, :] = here_up
            ddown_ref[0, :, span] = here_down

        @pl.when(step > 0)
        def _():
            sum_gate[span, :] += here_gate
            sum_up[span, :] += here_up
            ddown_ref[0, :, span] += here_down

        @pl.when(step == steps - 1)
        def _():
            dgate_ref[0, span, :] = sum_gate[span, :].astype(bf16)
            dup_ref[0, span, :] = sum_up[span, :].astype(bf16)

    if n_pack:

        @pl.when((step == steps - 1) & (pl.program_id(0) < n_pack))
        def _():
            pack_ref = pack_refs[0]
            depth = pack_ref.shape[2]
            for plane in range(pack_ref.shape[0]):
                here = pl.ds(plane * depth, depth)
                pack_ref[plane, 0, :, :part] = dgate_ref[0, here, :]
                pack_ref[plane, 0, :, part:] = dup_ref[0, here, :]


def place_kernel(number, slots_ref, y_ref, dx_ref, probs_ref, out_ref, back_ref):
    pick = jnp.concatenate(picks(slots_ref, number), axis=0).astype(jnp.bfloat16)
    width = out_ref.shape[1]
    piece = 512
    flat = number * 2 * CAP
    for at in range(0, width, piece):
        part = y_ref[:, :, at : at + piece].reshape(flat, piece)
        out_ref[:, at : at + piece] = dot(pick, part, (0, 0)).astype(jnp.bfloat16)
        part = dx_ref[:, :, at : at + piece].reshape(flat, piece)
        back_ref[:, at : at + piece] = dot(pick, part, (0, 0)).astype(jnp.bfloat16)
    part = probs_ref[...].reshape(flat, 128)
    back_ref[:, width:] = dot(pick, part, (0, 0)).astype(jnp.bfloat16)


def pick_shapes(number, pairs):
    bf16 = jnp.bfloat16
    size = 2 * CAP
    return [
        jax.ShapeDtypeStruct((number, pairs * size, D), bf16),
        jax.ShapeDtypeStruct((number, pairs * size, D), bf16),
        jax.ShapeDtypeStruct((number, pairs * size, 128), jnp.float32),
    ]


def pick_rows(number, experts_all, slots, x_all, g_all, router, rows, grows, gates):
    pairs, _, pair = slots.shape
    size = 2 * CAP
    tokens = pl.BlockSpec((pair, D), lambda p: (p, 0))
    picked = pl.BlockSpec((number, size, D), lambda p: (0, p, 0))
    pltpu.emit_pipeline(
        functools.partial(pick_kernel, number, experts_all),
        grid=(pairs,),
        in_specs=[
            pl.BlockSpec((1, number, pair), lambda p: (p, 0, 0)),
            tokens,
            tokens,
            pl.BlockSpec(router.shape, lambda p: (0, 0)),
        ],
        out_specs=[picked, picked, pl.BlockSpec((number, size, 128), lambda p: (0, p, 0))],
    )(slots, x_all, g_all, router, rows, grows, gates)


def expert_call(names, half, low, number, rows, grows, gates, weights, down, into=(), pack=()):
    total, depth, _ = rows.shape
    part = down.shape[1]
    size = depth
    while size > 768:
        size //= 2
    steps = depth // size
    bf16 = jnp.bfloat16
    f32 = jnp.float32

    def from_rows(width):
        return pl.BlockSpec((1, size, width), lambda e, r: (e + low, r, 0))

    def whole(*shape):
        return pl.BlockSpec((1, *shape), lambda e, r: (e, 0, 0))

    def from_whole(*shape):
        return pl.BlockSpec((1, *shape), lambda e, r: (e + low, 0, 0))

    packed = [
        pl.BlockSpec(
            (planes, 1, D // planes, 2 * part),
            lambda e, r, n=n: (0, lax.min(e, n - 1), 0, 0),
        )
        for n, planes in ([pack] if pack else [])
    ]
    keep = (D, part) if steps > 1 else (16, 128)
    return pl.pallas_call(
        functools.partial(
            expert_kernel, steps, half, len(weights), len(into), pack[0] if pack else 0
        ),
        grid=(number, steps),
        in_specs=[
            pl.BlockSpec(memory_space=pltpu.SMEM),
            from_rows(D),
            from_rows(D),
            from_rows(128),
            *[(from_whole if len(weights) == 2 else whole)(*one.shape[1:]) for one in weights],
            from_whole(part, D),
            *[pl.BlockSpec(memory_space=pl.ANY)] * len(into),
        ],
        out_specs=[
            from_rows(D),
            from_rows(D),
            from_rows(128),
            whole(D, part),
            whole(D, part),
            from_whole(part, D),
            *packed,
        ],
        out_shape=[
            jax.ShapeDtypeStruct((total, depth, D), bf16),
            jax.ShapeDtypeStruct((total, depth, D), bf16),
            jax.ShapeDtypeStruct((total, depth, 128), bf16),
            jax.ShapeDtypeStruct((number, D, part), bf16),
            jax.ShapeDtypeStruct((number, D, part), bf16),
            jax.ShapeDtypeStruct((total, part, D), f32),
            *[
                jax.ShapeDtypeStruct((planes, n, D // planes, 2 * part), bf16)
                for n, planes in ([pack] if pack else [])
            ],
        ],
        input_output_aliases={
            5 + len(weights) + i: out for i, out in zip(range(len(into)), (0, 1, 2, 5))
        },
        scratch_shapes=[pltpu.VMEM(keep, f32), pltpu.VMEM(keep, f32)],
        compiler_params=pltpu.CompilerParams(vmem_limit_bytes=BIG),
    )(names, rows, grows, gates, *weights, down, *into)


def place_call(number, slots, y, dx, probs):
    pairs, _, pair = slots.shape
    bf16 = jnp.bfloat16
    size = 2 * CAP
    rows = pl.BlockSpec((number, size, D), lambda p: (0, p, 0))
    return pl.pallas_call(
        functools.partial(place_kernel, number),
        grid=(pairs,),
        in_specs=[
            pl.BlockSpec((1, number, pair), lambda p: (p, 0, 0)),
            rows,
            rows,
            pl.BlockSpec((number, size, 128), lambda p: (0, p, 0)),
        ],
        out_specs=[
            pl.BlockSpec((pair, D), lambda p: (p, 0)),
            pl.BlockSpec((pair, D + 128), lambda p: (p, 0)),
        ],
        out_shape=[
            jax.ShapeDtypeStruct((pairs * pair, D), bf16),
            jax.ShapeDtypeStruct((pairs * pair, D + 128), bf16),
        ],
        compiler_params=pltpu.CompilerParams(vmem_limit_bytes=BIG),
    )(slots, y, dx, probs)


def widen_kernel(*refs):
    half = len(refs) // 2
    for source, target in zip(refs[:half], refs[half:]):
        target[...] = source[...].astype(jnp.float32)


def widen(values):
    number, rows, columns = values[0].shape
    block = pl.BlockSpec((1, rows, columns), lambda e: (e, 0, 0))
    return pl.pallas_call(
        widen_kernel,
        grid=(number,),
        in_specs=[block] * len(values),
        out_specs=[block] * len(values),
        out_shape=[jax.ShapeDtypeStruct(one.shape, jnp.float32) for one in values],
        compiler_params=pltpu.CompilerParams(vmem_limit_bytes=BIG),
    )(*values)


def shards(
    n_dp,
    n_expert,
    tokens,
    cotangent,
    lengths,
    routes,
    w_query,
    w_key,
    w_value,
    w_out,
    w_router,
    gain_attn,
    gain_query,
    gain_key,
    gain_mlp,
    w_gate,
    w_up,
    w_down,
):
    groups = n_dp * n_expert
    bf16 = jnp.bfloat16
    number = w_gate.shape[0]
    ff = w_gate.shape[2]
    part = ff // n_dp
    experts_all = w_router.shape[1]
    width = 128
    small = jnp.concatenate(
        [
            w_router,
            gain_attn[:, None],
            gain_query[:, None],
            gain_key[:, None],
            gain_mlp[:, None],
            jnp.zeros((w_router.shape[0], width - experts_all - 4), bf16),
        ],
        axis=1,
    )
    hits = jnp.any(
        routes[:, :, None] == jnp.arange(width, dtype=jnp.int32)[None, None, :], axis=1
    ).astype(bf16)
    count = tokens.shape[0]
    rows_each = w_query.shape[0]
    extras = jnp.concatenate([hits, jnp.pad(small, ((0, count - rows_each), (0, 0)))], axis=1)
    weights = jnp.stack([w_query, w_key, w_value, w_out])
    depth = w_gate.shape[1]
    early = number // 4
    beside = early + number // 8
    late = number - number // 4
    back_beside = number // 8
    back_third = back_beside + number // 4
    back_late = back_third + number // 4
    me = lax.axis_index("dp")
    cut_shape = jax.ShapeDtypeStruct((number, n_dp * depth, part), bf16)

    def row_block(size):
        return lambda ref, block: ref.at[pl.ds(pl.multiple_of(block * size, 16), size)]

    def columns_at(at):
        return pl.ds(pl.multiple_of(at * part, part), part)

    def rows_at(at):
        return pl.ds(pl.multiple_of(at * depth, depth), depth)

    def recut(low, high):
        def cuts(ins, outs):
            def pair(n):
                chosen = pl.ds(low, high - low)
                return (
                    lambda to: ins[n].at[chosen, :, columns_at(to)],
                    lambda at: outs[n].at[chosen, rows_at(at)],
                )

            return [pair(0), pair(1)]

        return cuts

    to_plane, from_plane = partners(me, n_dp)

    def permuted(pieces, chained=False):
        got = []
        for k, piece in enumerate(pieces, 1):
            if chained and got:
                piece, last = lax.optimization_barrier((piece, got.pop()))
                got.append(last)
            paths = [(i, partners(i, n_dp)[0](k)) for i in range(n_dp)]
            got.append(lax.ppermute(piece, "dp", paths))
        return got

    def cut_pieces(low, high, first_k, ins, outs):
        to, unused = partners(lax.axis_index("dp"), n_dp)
        pairs = []
        for k, piece in enumerate(outs, first_k):
            for n in range(2):
                source = ins[n].at[pl.ds(low, high - low), :, columns_at(to(k))]
                pairs.append((source, piece.at[:, :, pl.ds(n * part, part)]))
        return pairs

    def piece_shapes(size, first_k):
        shape = jax.ShapeDtypeStruct((size, depth, 2 * part), bf16)
        return [shape] * (n_dp - first_k if size else 0)

    soon_shapes = piece_shapes(beside - early, 1)
    late_shapes = piece_shapes(number - late, 0)
    n_soon = len(soon_shapes)

    weights_all, extras_all, gate_early, up_early, *pieces = gather_call(
        n_dp,
        n_expert,
        [weights, extras],
        [
            jax.ShapeDtypeStruct((4, groups * rows_each, D), bf16),
            jax.ShapeDtypeStruct((groups * count, 2 * width), bf16),
        ],
        [
            lambda ref, block: ref.at[
                :, pl.ds(pl.multiple_of(block * rows_each, 16), rows_each)
            ],
            row_block(count),
        ],
        [w_gate, w_up],
        [cut_shape, cut_shape, *soon_shapes, *late_shapes],
        recut(0, early),
        {},
        0,
        lambda ins, outs: cut_pieces(early, beside, 1, ins, outs[2 : 2 + n_soon])
        + cut_pieces(late, number, 0, ins, outs[2 + n_soon :]),
    )
    soon_pieces, late_pieces = pieces[:n_soon], pieces[n_soon:]
    query_weight, key_weight, value_weight, out_weight = (weights_all[i] for i in range(4))
    small_all = (
        extras_all[:, width:].reshape(groups, count, width)[:, :rows_each].reshape(-1, width)
    )
    hits_all = extras_all[:, :experts_all]
    router_weight = small_all[:, :experts_all]
    gains = small_all[:, experts_all : experts_all + 4].astype(jnp.float32)
    attn_gain, query_gain, key_gain, mlp_gain = (gains[:, i] for i in range(4))
    inputs = tokens.astype(jnp.float32)
    segment, position, places = layout(lengths[0], count)
    half = HD // 2
    freq = 10000.0 ** (-2.0 * jnp.arange(half, dtype=jnp.float32) / HD)
    angle = position.astype(jnp.float32)[:, None] * freq[None, :]
    cosine = jnp.cos(angle)[:, None, :]
    sine = jnp.sin(angle)[:, None, :]
    scale = HD ** (-0.5)
    normed, attn_inverse = rms_forward(inputs, attn_gain)
    normed_low = normed.astype(bf16)
    query_raw = product(normed_low, query_weight, "td,de->te")
    key_raw = product(normed_low, key_weight, "td,de->te")
    value_low = product(normed_low, value_weight, "td,de->te").astype(bf16)
    query_normed, query_inverse = rms_forward(query_raw, query_gain)
    key_normed, key_inverse = rms_forward(key_raw, key_gain)
    query_low = rotate(query_normed, cosine, sine).astype(bf16).reshape(count, HEADS, HD)
    key_low = rotate(key_normed, cosine, sine).astype(bf16).reshape(count, HEADS, HD)
    value_heads = value_low.reshape(count, HEADS, HD)
    allowed = (segment[:, None] == segment[None, :]) & (places[None, :] <= places[:, None])
    scores = product(query_low, key_low, "qhd,khd->hqk") * scale
    scores = jnp.where(allowed[None], scores, -1e30)
    probs = jax.nn.softmax(scores, axis=-1)
    probs_low = probs.astype(bf16)
    attended_low = product(probs_low, value_heads, "hqk,khd->qhd").reshape(count, D).astype(bf16)
    middle = inputs + product(attended_low, out_weight, "td,de->te")
    mlp_normed, mlp_inverse = rms_forward(middle, mlp_gain)
    mlp_low = mlp_normed.astype(bf16)
    router = jax.nn.softmax(product(mlp_low, router_weight, "td,de->te"), axis=-1)

    first = lax.axis_index("expert") * number
    hit = lax.dynamic_slice_in_dim(hits_all, first, number, 1).reshape(groups, count, number)
    before = jnp.tril(jnp.ones((count, count), bf16), -1)
    slot = product(before, hit, "ts,bse->bet").astype(jnp.int32)
    slot = jnp.where(jnp.transpose(hit, (0, 2, 1)) > 0, slot, -1)
    slot = slot.reshape(groups // 2, 2, number, count)
    shift = jnp.array([0, CAP], jnp.int32)[None, :, None, None]
    slots = jnp.transpose(jnp.where(slot < 0, -1, slot + shift), (0, 2, 1, 3))
    slots = slots.reshape(groups // 2, number, 2 * count)
    router_own = jnp.pad(
        jnp.roll(router_weight, -first, axis=1), ((0, 0), (0, width - experts_all))
    )
    if n_soon:
        mlp_low, *soon_pieces = lax.optimization_barrier((mlp_low, *permuted(soon_pieces)))

    def put_weights(ins, outs):
        chosen = pl.ds(early, beside - early)
        unused, heard = partners(lax.axis_index("dp"), n_dp)
        pairs = []
        if beside > early:
            own = lax.axis_index("dp")
            for n in range(2):
                source = ins[n].at[chosen, :, columns_at(own)]
                pairs.append((source, outs[n].at[chosen, rows_at(own)]))
        for k, piece in enumerate(ins[6:], 1):
            for n in range(2):
                columns = piece.at[:, :, pl.ds(n * part, part)]
                pairs.append((columns, outs[n].at[chosen, rows_at(heard(k))]))
        return pairs

    def pick_all(items, ins, outs):
        pick_rows(number, experts_all, ins[4], *items, ins[5], *outs[2:])

    unused, unused, gate_cut, up_cut, rows, grows, gates = gather_call(
        n_dp,
        n_expert,
        [mlp_low, cotangent],
        [jax.ShapeDtypeStruct((groups * count, D), bf16)] * 2,
        [row_block(count)] * 2,
        [w_gate, w_up, gate_early, up_early, slots, router_own, *soon_pieces],
        [cut_shape, cut_shape, *pick_shapes(number, groups // 2)],
        recut(beside, late),
        {4: 2, 5: 3},
        1,
        put_weights,
        pick_all,
    )
    *late_pieces, rows = lax.optimization_barrier((*late_pieces, rows))
    late_pieces = [late_pieces[0], *permuted(late_pieces[1:])]
    packing = back_beside > 0 and depth == 512
    *outs, gate_soon, up_soon, down_soon = expert_call(
        first[None],
        experts_all,
        0,
        late,
        rows,
        grows,
        gates,
        [gate_cut, up_cut],
        w_down,
        pack=(back_beside, n_dp) if packing else (),
    )
    if packing:
        *outs, gate_soon, up_soon, down_soon, packed = [*outs, gate_soon, up_soon, down_soon]
    offsets = [from_plane(k) * depth for k in range(n_dp)]
    weighted, grad_rows, grad_gates, gate_rest, up_rest, grad_down_part = expert_call(
        jnp.stack([first + late, *offsets]),
        experts_all,
        late,
        number - late,
        rows,
        grows,
        gates,
        late_pieces,
        w_down,
        [*outs, down_soon],
    )
    part_out, part_back = place_call(number, slots, weighted, grad_rows, grad_gates)

    def ways(low, high, at, ins, outs):
        def pair(n):
            return (
                lambda to: ins[n].at[pl.ds(low, high - low), rows_at(to)],
                lambda here: outs[n].at[pl.ds(low + at, high - low), :, columns_at(here)],
            )

        return [pair(0), pair(1)]

    def put_grads(low, high, ins, pieces, outs):
        own = lax.axis_index("dp")
        unused, heard = partners(own, n_dp)
        chosen = pl.ds(low, high - low)
        pairs = []
        if high > low:
            for n in range(2):
                source = ins[n].at[chosen, rows_at(own)]
                pairs.append((source, outs[n].at[chosen, :, columns_at(own)]))
        for k, piece in enumerate(pieces, 1):
            for n in range(2):
                columns = piece.at[:, :, pl.ds(n * part, part)]
                pairs.append((columns, outs[n].at[chosen, :, columns_at(heard(k))]))
        return pairs

    def cut_grads(low, high, ins, outs):
        to, unused = partners(lax.axis_index("dp"), n_dp)
        pairs = []
        for k, piece in enumerate(outs, 1):
            for n in range(2):
                source = ins[n].at[pl.ds(low, high - low), rows_at(to(k))]
                pairs.append((source, piece.at[:, :, pl.ds(n * part, part)]))
        return pairs

    pieces = []
    if back_beside:
        for k in range(1, n_dp):
            if packing:
                piece = lax.dynamic_index_in_dim(packed, to_plane(k), 0, False)
            else:
                piece = jnp.concatenate(
                    [
                        lax.dynamic_slice_in_dim(
                            one[:back_beside], to_plane(k) * depth, depth, 1
                        )
                        for one in (gate_soon, up_soon)
                    ],
                    axis=2,
                )
            pieces.append(piece)
        part_back, *pieces = lax.optimization_barrier((part_back, *permuted(pieces)))
    way_shapes = [jax.ShapeDtypeStruct((number, depth, ff), bf16)] * 2
    (back,), (gate_third, up_third, *pieces) = scatter_all(
        n_dp,
        n_expert,
        [part_back.reshape(n_dp, n_expert, count, D + width)],
        [gate_soon, up_soon, *pieces],
        way_shapes + piece_shapes(back_late - back_third, 1),
        lambda ins, outs: ways(back_beside, back_third, 0, ins, outs),
        8,
        (),
        lambda ins, outs: put_grads(0, back_beside, ins, ins[2:], outs)
        + cut_grads(back_third, back_late, ins, outs[2:]),
    )
    if pieces:
        part_out, *pieces = lax.optimization_barrier((part_out, *permuted(pieces, True)))

    grad_final = cotangent.astype(jnp.float32)
    grad_mlp = back[:, :D]
    grad_router_probs = back[:, D : D + experts_all] + back[:, D + experts_all :]
    grad_logits = router * (
        grad_router_probs - jnp.sum(router * grad_router_probs, axis=1, keepdims=True)
    )
    grad_logits_low = grad_logits.astype(bf16)
    grad_router_full = product(mlp_low, grad_logits_low, "td,te->de")
    grad_mlp = grad_mlp + product(grad_logits_low, router_weight, "te,de->td")
    grad_middle_part, grad_mlp_gain = rms_backward(middle, mlp_inverse, mlp_gain, grad_mlp)
    grad_middle = grad_final + grad_middle_part
    grad_branch_low = grad_middle.astype(bf16)
    grad_out_full = product(attended_low, grad_branch_low, "td,te->de")
    grad_attended = (
        product(grad_branch_low, out_weight, "te,de->td").astype(bf16).reshape(count, HEADS, HD)
    )
    grad_weights = product(grad_attended, value_heads, "qhd,khd->hqk")
    grad_scores = probs * (grad_weights - jnp.sum(probs * grad_weights, axis=-1, keepdims=True))
    grad_scores_low = grad_scores.astype(bf16)
    grad_query_turn = product(grad_scores_low, key_low, "hqk,khd->qhd").reshape(count, D) * scale
    grad_key_turn = product(grad_scores_low, query_low, "hqk,qhd->khd").reshape(count, D) * scale
    grad_value_low = (
        product(probs_low, grad_attended, "hqk,qhd->khd").reshape(count, D).astype(bf16)
    )
    grad_query_raw, grad_query_gain = rms_backward(
        query_raw, query_inverse, query_gain, rotate(grad_query_turn, cosine, -sine)
    )
    grad_key_raw, grad_key_gain = rms_backward(
        key_raw, key_inverse, key_gain, rotate(grad_key_turn, cosine, -sine)
    )
    grad_query_low = grad_query_raw.astype(bf16)
    grad_key_low = grad_key_raw.astype(bf16)
    grad_query_full = product(normed_low, grad_query_low, "td,te->de")
    grad_key_full = product(normed_low, grad_key_low, "td,te->de")
    grad_value_full = product(normed_low, grad_value_low, "td,te->de")
    grad_normed = (
        product(grad_query_low, query_weight, "te,de->td")
        + product(grad_key_low, key_weight, "te,de->td")
        + product(grad_value_low, value_weight, "te,de->td")
    )
    grad_inputs_part, grad_attn_gain = rms_backward(inputs, attn_inverse, attn_gain, grad_normed)
    grad_inputs = grad_middle + grad_inputs_part

    small_grads = jnp.concatenate(
        [
            grad_router_full,
            grad_attn_gain[:, None],
            grad_query_gain[:, None],
            grad_key_gain[:, None],
            grad_mlp_gain[:, None],
            jnp.zeros((D, width - experts_all - 4), jnp.float32),
        ],
        axis=1,
    )

    def blocks_of(value):
        return value.astype(bf16).reshape(n_dp, n_expert, rows_each, -1)

    sums, (gate_back, up_back) = scatter_all(
        n_dp,
        n_expert,
        [
            blocks_of(value)
            for value in (
                grad_out_full,
                grad_value_full,
                grad_key_full,
                grad_query_full,
                small_grads,
            )
        ]
        + [part_out.reshape(n_dp, n_expert, count, D)],
        [gate_third, up_third, gate_soon, up_soon, gate_rest, up_rest, *pieces],
        way_shapes,
        lambda ins, outs: ways(back_late, late, 0, ins[2:4], outs)
        + ways(0, number - late, late, ins[4:6], outs),
        16,
        ((0, 0), (1, 1)),
        lambda ins, outs: put_grads(back_third, back_late, ins[2:4], ins[6:], outs),
    )
    grad_out_part, grad_value_part, grad_key_part, grad_query_part, small_part, summed = sums
    output = (middle + summed).astype(bf16)
    grad_router_part = small_part[:, :experts_all]
    gain_parts = [small_part[:, experts_all + i] for i in range(4)]
    grad_gate_part, grad_up_part = widen([gate_back, up_back])
    return (
        output,
        grad_inputs,
        grad_query_part,
        grad_key_part,
        grad_value_part,
        grad_out_part,
        grad_router_part,
        gain_parts[0],
        gain_parts[1],
        gain_parts[2],
        gain_parts[3],
        grad_gate_part,
        grad_up_part,
        grad_down_part,
    )


def solution(mesh):
    return jax.shard_map(
        functools.partial(shards, mesh.shape["dp"], mesh.shape["expert"]),
        mesh=mesh,
        in_specs=(
            P(("dp", "expert"), None),
            P(("dp", "expert"), None),
            P(("dp", "expert"), None),
            P(("dp", "expert"), None),
            P(("dp", "expert"), None),
            P(("dp", "expert"), None),
            P(("dp", "expert"), None),
            P(("dp", "expert"), None),
            P(("dp", "expert"), None),
            P(("dp", "expert")),
            P(("dp", "expert")),
            P(("dp", "expert")),
            P(("dp", "expert")),
            P("expert", "dp", None),
            P("expert", "dp", None),
            P("expert", "dp", None),
        ),
        out_specs=(
            P(("dp", "expert"), None),
            P(("dp", "expert"), None),
            P(("dp", "expert"), None),
            P(("dp", "expert"), None),
            P(("dp", "expert"), None),
            P(("dp", "expert"), None),
            P(("dp", "expert"), None),
            P(("dp", "expert")),
            P(("dp", "expert")),
            P(("dp", "expert")),
            P(("dp", "expert")),
            P("expert", "dp", None),
            P("expert", "dp", None),
            P("expert", "dp", None),
        ),
        check_vma=False,
    )
```

```python
import functools

import jax
import jax.numpy as jnp
from jax import lax
from jax.experimental import pallas as pl
from jax.experimental.pallas import tpu as pltpu
from jax.sharding import PartitionSpec as P

D = 2048
HEADS = 16
HD = 128
TOPK = 8
CAP = 24


eps = 1e-05


def product(left, right, form):
    return jnp.einsum(form, left, right, preferred_element_type=jnp.float32)


def rms_forward(values, gain):
    inverse = lax.rsqrt(jnp.mean(values * values, axis=-1, keepdims=True) + eps)
    return (values * inverse * gain, inverse)


def rms_backward(values, inverse, gain, grad):
    scaled = grad * gain
    inner = jnp.mean(scaled * values, axis=-1, keepdims=True)
    grad_values = inverse * scaled - values * (inverse * inverse * inverse) * inner
    grad_gain = jnp.sum(grad * values * inverse, axis=0)
    return (grad_values, grad_gain)


def layout(lengths_row, count):
    places = jnp.arange(count, dtype=jnp.int32)
    ends = jnp.cumsum(lengths_row, dtype=jnp.int32)
    passed = (places[:, None] >= ends[None, :]).astype(jnp.int32)
    segment = jnp.sum(passed, axis=1, dtype=jnp.int32)
    start = jnp.sum(passed * lengths_row[None, :], axis=1, dtype=jnp.int32)
    return (segment, places - start, places)


def rotate(values, cosine, sine):
    count = values.shape[0]
    heads = values.reshape(count, HEADS, HD)
    half = HD // 2
    first = heads[..., :half]
    second = heads[..., half:]
    turned = jnp.concatenate(
        [first * cosine - second * sine, second * cosine + first * sine], axis=-1
    )
    return turned.reshape(count, D)


MESH = pl.DeviceIdType.MESH
BIG = 60 * 1024 * 1024


def place_of():
    z = lax.axis_index("dp")
    j = lax.axis_index("expert")
    return z, j, j // 2, j % 2


def other_chips(chip, chips):
    if chips == 4:
        square = [chip, chip + 1 - 2 * (chip % 2), chip + 2 - 4 * (chip // 2), 3 - chip]
        return lambda k: square[k], lambda k: square[k]
    return lambda k: (chip + k) % chips, lambda k: (chip + chips - k) % chips


def partners(z, n_dp):
    if n_dp == 4:
        pairs = [z, (z + 2) % 4, 3 - z, z + 1 - 2 * (z % 2)]
        return lambda k: pairs[k], lambda k: pairs[k]
    return lambda k: (z + k) % n_dp, lambda k: (z + n_dp - k) % n_dp


def greet(n_dp, n_expert):
    z, j, chip, core = place_of()
    chips = n_expert // 2
    barrier = pltpu.get_barrier_semaphore()
    for k in range(1, n_dp):
        pl.semaphore_signal(
            barrier, inc=1, device_id=((z + k) % n_dp, j), device_id_type=MESH
        )
    for k in range(1, chips):
        other = ((chip + k) % chips) * 2 + core
        pl.semaphore_signal(barrier, inc=1, device_id=(z, other), device_id_type=MESH)
    pl.semaphore_signal(
        barrier, inc=1, device_id=(z, chip * 2 + 1 - core), device_id_type=MESH
    )
    pl.semaphore_wait(barrier, n_dp - 1 + chips - 1 + 1)


def remote(source, target, send, receive, device):
    return pltpu.make_async_remote_copy(
        src_ref=source,
        dst_ref=target,
        send_sem=send,
        recv_sem=receive,
        device_id=device,
        device_id_type=MESH,
    )


def exchange(n_dp, pairs, send, receive):
    z, j, chip, core = place_of()
    to_plane, unused = partners(z, n_dp)
    copies = []
    for i, (source, target) in enumerate(pairs):
        for k in range(1, n_dp):
            to = to_plane(k)
            copies.append(
                remote(source(to), target(z), send.at[i, k], receive.at[i, k], (to, j))
            )
    return copies


def moves(pairs, stages, local):
    bring = [
        pltpu.make_async_copy(source, stages[i], local.at[i, 0])
        for i, (source, target) in enumerate(pairs)
    ]
    put = [
        pltpu.make_async_copy(stages[i], target, local.at[i, 1])
        for i, (source, target) in enumerate(pairs)
    ]
    return bring, put


def nothing(ins, outs):
    return []


def gather_kernel(
    n_dp, n_expert, n_items, places, cuts, puts, finish, n_cut, n_out, n_stages, *refs
):
    z, j, chip, core = place_of()
    chips = n_expert // 2
    square = chips == 4
    to_chip, from_chip = other_chips(chip, chips)
    sources = refs[:n_items]
    cut_in = refs[n_items : n_items + n_cut]
    at = n_items + n_cut
    targets = refs[at : at + n_items]
    cut_out = refs[at + n_items : at + n_items + n_out]
    (
        send_c,
        recv_c,
        send_b,
        recv_b,
        send_a,
        recv_a,
        local,
        send_x,
        recv_x,
        local_y,
        *stages,
    ) = refs[at + n_items + n_out :]
    greet(n_dp, n_expert)
    mate = (z, chip * 2 + 1 - core)
    near = (1, 2) if square else tuple(range(1, chips))

    def slot(i, plane, column):
        return places[i](targets[i], plane * n_expert + column)

    def pass_on(i, plane, source, column, k, chip_to):
        return remote(
            source,
            slot(i, plane, column),
            send_b.at[i, plane, k],
            recv_b.at[i, plane, k],
            (z, chip_to * 2 + core),
        )

    def hand(i, plane, source):
        for k in near:
            pass_on(i, plane, source, j, k, to_chip(k)).start()
        remote(
            source, slot(i, plane, j), send_a.at[i, plane, 0], recv_a.at[i, plane, 0], mate
        ).start()

    def along(i, plane, source, way, step):
        return remote(
            source, slot(i, plane, j), send_c.at[i, way, plane], recv_c.at[i, plane], (z + step, j)
        )

    def at_distance(d, body):
        if d == 0:
            body(z, 0)
            return

        @pl.when(z >= d)
        def _():
            body(z - d, 0)

        @pl.when(z + d < n_dp)
        def _():
            body(z + d, 1)

    for i in range(n_items):

        @pl.when(z < n_dp - 1)
        def _():
            along(i, z, sources[i], 0, 1).start()

        @pl.when(z > 0)
        def _():
            along(i, z, sources[i], 1, -1).start()

        hand(i, z, sources[i])
        pltpu.make_async_copy(sources[i], slot(i, z, j), local.at[i]).start()

    def relay(plane, way):
        step = -1 if way else 1
        for i in range(n_items):
            block = slot(i, plane, j)
            along(i, plane, block, way, step).wait_recv()

            @pl.when(z > 0 if way else z < n_dp - 1)
            def _():
                along(i, plane, block, way, step).start()

            hand(i, plane, block)

    for d in range(1, n_dp):
        at_distance(d, relay)
    pairs = cuts(cut_in, cut_out)
    copies = exchange(n_dp, pairs, send_x, recv_x)
    for copy in copies:
        copy.start()
    own = [(source(z), target(z)) for source, target in pairs]
    bring, put = moves(own + puts(cut_in, cut_out), stages, local_y)
    for copy in bring:
        copy.start()
    for one, other in zip(bring, put):
        one.wait()
        other.start()

    def arrive(i, plane, k):
        column = from_chip(k) * 2 + core
        block = slot(i, plane, column)
        pass_on(i, plane, block, column, k, chip).wait_recv()
        remote(block, block, send_a.at[i, plane, k], recv_a.at[i, plane, k], mate).start()
        return block, column

    def arrived(plane, way):
        for i in range(n_items):
            for k in near:
                block, column = arrive(i, plane, k)
                if square:

                    @pl.when(plane % 2 == k - 1)
                    def _():
                        pass_on(i, plane, block, column, 3, to_chip(3 - k)).start()

    def crossed(plane, way):
        for i in range(n_items):
            arrive(i, plane, 3)

    for d in range(n_dp):
        at_distance(d, arrived)
    if square:
        for d in range(n_dp):
            at_distance(d, crossed)

    for i in range(n_items):
        for plane in range(n_dp):
            for k in range(chips):
                column = (from_chip(k) if k else chip) * 2 + 1 - core
                block = slot(i, plane, column)
                remote(
                    block, block, send_a.at[i, plane, k], recv_a.at[i, plane, k], mate
                ).wait_recv()
        pltpu.make_async_copy(sources[i], slot(i, z, j), local.at[i]).wait()
    finish(targets, cut_in, cut_out)
    for i in range(n_items):
        for plane in range(n_dp):
            block = slot(i, plane, j)
            for k in range(1, chips):
                pass_on(i, plane, block, j, k, chip).wait_send()
            for k in range(chips):
                remote(
                    block, block, send_a.at[i, plane, k], recv_a.at[i, plane, k], mate
                ).wait_send()

            @pl.when((z < n_dp - 1) & (z >= plane))
            def _():
                along(i, plane, block, 0, 1).wait_send()

            @pl.when((z > 0) & (z <= plane))
            def _():
                along(i, plane, block, 1, -1).wait_send()

    for copy in copies + put:
        copy.wait()


def gather_call(
    n_dp,
    n_expert,
    items,
    shapes,
    places,
    cut_in,
    cut_shapes,
    cuts,
    aliases,
    number,
    stages,
    puts=nothing,
    finish=lambda items, ins, outs: None,
):
    chips = n_expert // 2
    n, m = len(items), len(cut_shapes)
    dma = pltpu.SemaphoreType.DMA
    anywhere = pl.BlockSpec(memory_space=pl.ANY)
    return pl.pallas_call(
        functools.partial(
            gather_kernel,
            n_dp,
            n_expert,
            n,
            places,
            cuts,
            puts,
            finish,
            len(cut_in),
            m,
            len(stages),
        ),
        out_shape=[*shapes, *cut_shapes],
        in_specs=[anywhere] * (n + len(cut_in)),
        out_specs=[anywhere] * (n + m),
        scratch_shapes=[
            dma((n, 2, n_dp)),
            dma((n, n_dp)),
            dma((n, n_dp, chips)),
            dma((n, n_dp, chips)),
            dma((n, n_dp, chips)),
            dma((n, n_dp, chips)),
            dma((n,)),
            dma((4, n_dp)),
            dma((4, n_dp)),
            dma((max(len(stages), 1), 2)),
            *[pltpu.VMEM(stage, jnp.bfloat16) for stage in stages],
        ],
        input_output_aliases=aliases,
        compiler_params=pltpu.CompilerParams(
            collective_id=number, has_side_effects=True, vmem_limit_bytes=BIG
        ),
    )(*items, *cut_in)


def scatter_kernel(
    n_dp, n_expert, n_items, n_cut, n_out, cuts, puts, rings, n_rings, *refs
):
    z, j, chip, core = place_of()
    chips = n_expert // 2
    square = chips == 4
    to_chip, from_chip = other_chips(chip, chips)
    refs = list(refs)

    def take(count):
        taken = refs[:count]
        del refs[:count]
        return taken

    sources, cut_in, targets, cut_out = take(n_items), take(n_cut), take(n_items), take(n_out)
    ring, got_a, got_b, got_c = take(n_rings), take(n_items), take(n_items), take(n_items)
    transit = take(n_items)
    (
        send_a,
        recv_a,
        send_b,
        recv_b,
        send_c,
        recv_c,
        send_t,
        recv_t,
        local,
        send_x,
        recv_x,
        local_y,
        *stages,
    ) = refs
    greet(n_dp, n_expert)
    mate = (z, chip * 2 + 1 - core)
    order = [3, 1, 2, 0] if square else [*range(1, chips), 0]
    half = n_dp // 2
    low, high = pl.ds(0, half), pl.ds(half, n_dp - half)

    def chip_of(k):
        return to_chip(k) if k else chip

    def to_mate(i, k):
        return remote(
            sources[i].at[:, chip_of(k) * 2 + 1 - core],
            got_a[i].at[k],
            send_a.at[i, k],
            recv_a.at[i, k],
            mate,
        )

    turn = [0] * n_rings
    loads = []
    for i in range(n_items):
        for k in order:
            loads.append((i, k, turn[rings[i]] % 2))
            turn[rings[i]] += 1

    def load(i, k, at):
        return pltpu.make_async_copy(
            sources[i].at[:, chip_of(k) * 2 + core], ring[rings[i]].at[at], local.at[rings[i], at]
        )

    def send_near(i, k, part, number):
        return remote(
            got_a[i].at[k, part],
            got_b[i].at[k - 1, part],
            send_b.at[i, number],
            recv_b.at[i, number],
            (z, to_chip(k) * 2 + core),
        )

    def send_over(i, k, part):
        return remote(
            got_a[i].at[3, part],
            transit[i].at[k - 1],
            send_t.at[i, k],
            recv_t.at[i, k],
            (z, to_chip(k) * 2 + core),
        )

    def send_far(i, k):
        return remote(
            got_a[i].at[k],
            got_b[i].at[k - 1],
            send_b.at[i, k],
            recv_b.at[i, k],
            (z, to_chip(k) * 2 + core),
        )

    def along(i, plane, way):
        slot = n_dp - (z - 1) + plane if way else plane - (z + 1)
        return remote(
            got_a[i].at[0, plane],
            got_c[i].at[slot],
            send_c.at[i, plane],
            recv_c.at[i, slot],
            (z - 1 if way else z + 1, j),
        )

    def from_along(i, slot):
        return remote(
            got_c[i].at[slot], got_c[i].at[slot], send_c.at[i, 0], recv_c.at[i, slot], mate
        )

    f32 = jnp.float32

    def add(i, planes, target, terms):
        rows = got_a[i].shape[2]
        per = rows // 16

        def step(n, unused):
            plane = n // per
            at = pl.ds(pl.multiple_of((n % per) * 16, 16), 16)
            total = terms[0](plane, at).astype(f32)
            for term in terms[1:]:
                total = total + term(plane, at).astype(f32)
            target(plane, at, total)
            return unused

        lax.fori_loop(0, planes * per, step, 0)

    def grow(i, k, first, planes, term):
        def target(plane, at, total):
            got_a[i][k, plane + first, at] = total.astype(got_a[i].dtype)

        add(i, planes, target, [lambda plane, at: got_a[i][k, plane + first, at], term])

    for i in range(n_items):
        for k in order:
            to_mate(i, k).start()
    started = 0
    ahead = [0] * n_rings
    for i, k, at in loads:
        if ahead[rings[i]] < 2:
            load(i, k, at).start()
            ahead[rings[i]] += 1
    pairs = cuts(cut_in, cut_out)
    copies = exchange(n_dp, pairs, send_x, recv_x)
    for copy in copies:
        copy.start()
    own = [(source(z), target(z)) for source, target in pairs]
    bring, put = moves(own + puts(cut_in, cut_out), stages, local_y)
    for copy in bring:
        copy.start()

    for n, (i, k, at) in enumerate(loads):
        load(i, k, at).wait()
        to_mate(i, k).wait_recv()
        grow(i, k, 0, n_dp, lambda plane, rows: ring[rings[i]][at, plane, rows])
        later = [one for one in loads[n + 1 :] if rings[one[0]] == rings[i]]
        if len(later) >= 2:
            load(*later[1]).start()
        if not k:
            continue
        if not square:
            send_far(i, k).start()
        elif k == 3:
            send_over(i, 1, low).start()
            send_over(i, 2, high).start()
        elif k == 1:
            send_near(i, 1, low, 0).start()
        else:
            send_near(i, 2, high, 1).start()
    for one, other in zip(bring, put):
        one.wait()
        other.start()
    if square:
        for i in range(n_items):
            send_over(i, 2, high).wait_recv()
            grow(i, 1, half, n_dp - half, lambda plane, rows: transit[i][1, plane, rows])
            send_near(i, 1, high, 2).start()
            send_over(i, 1, low).wait_recv()
            grow(i, 2, 0, half, lambda plane, rows: transit[i][0, plane, rows])
            send_near(i, 2, low, 3).start()
    for i in range(n_items):
        if square:
            send_near(i, 1, low, 0).wait_recv()
            send_near(i, 2, high, 1).wait_recv()
            send_near(i, 1, high, 2).wait_recv()
            send_near(i, 2, low, 3).wait_recv()
        else:
            for k in range(1, chips):
                send_far(i, k).wait_recv()
        heard = 2 if square else chips - 1

        def target(plane, at, total):
            got_a[i][0, plane, at] = total.astype(got_a[i].dtype)

        terms = [lambda plane, at: got_a[i][0, plane, at]]
        for other in range(heard):
            terms.append(lambda plane, at, other=other: got_b[i][other, plane, at])
        add(i, n_dp, target, terms)
        for d in range(n_dp - 1, 0, -1):
            for way in (0, 1):
                plane = z - d if way else z + d
                arrives = z < n_dp - 1 if way else z > 0
                slot = n_dp - z + plane if way else plane - z

                @pl.when(plane >= 0 if way else plane < n_dp)
                def _():
                    @pl.when(arrives)
                    def _():
                        from_along(i, slot).wait_recv()
                        grow(i, 0, plane, 1, lambda unused, at: got_c[i][slot, at])

                    along(i, plane, way).start()

    for i in range(n_items):

        def own(unused, at, total):
            targets[i][at] = total

        add(i, 1, own, [lambda unused, at: got_a[i][0, z, at]])
        for slot, arrives in ((0, z > 0), (n_dp, z < n_dp - 1)):

            @pl.when(arrives)
            def _():
                from_along(i, slot).wait_recv()
                add(
                    i,
                    1,
                    own,
                    [lambda unused, at: targets[i][at], lambda unused, at: got_c[i][slot, at]],
                )

    for i in range(n_items):
        for k in range(chips):
            to_mate(i, k).wait_send()
        if square:
            for k, part in ((1, low), (2, high)):
                send_over(i, k, part).wait_send()
            for k, part, number in ((1, low, 0), (2, high, 1), (1, high, 2), (2, low, 3)):
                send_near(i, k, part, number).wait_send()
        else:
            for k in range(1, chips):
                send_far(i, k).wait_send()
        for plane in range(n_dp):

            @pl.when(z != plane)
            def _():
                remote(
                    got_a[i].at[0, plane],
                    got_c[i].at[0],
                    send_c.at[i, plane],
                    recv_c.at[i, 0],
                    mate,
                ).wait_send()

    for copy in copies + put:
        copy.wait()


def scatter_call(
    n_dp, n_expert, items, cut_in, cut_shapes, cuts, number, aliases, stages, puts=nothing
):
    chips = n_expert // 2
    square = chips == 4
    n, m = len(items), len(cut_shapes)
    dma = pltpu.SemaphoreType.DMA
    anywhere = pl.BlockSpec(memory_space=pl.ANY)
    blocks = [item.shape[2:] for item in items]
    kinds = sorted(set(blocks))
    rings = [kinds.index(block) for block in blocks]
    bf16 = jnp.bfloat16
    heard = 2 if square else chips - 1
    return pl.pallas_call(
        functools.partial(
            scatter_kernel, n_dp, n_expert, n, len(cut_in), m, cuts, puts, rings, len(kinds)
        ),
        out_shape=[*[jax.ShapeDtypeStruct(block, jnp.float32) for block in blocks], *cut_shapes],
        in_specs=[anywhere] * (n + len(cut_in)),
        out_specs=[pl.BlockSpec(memory_space=pltpu.VMEM)] * n + [anywhere] * m,
        scratch_shapes=[
            *[pltpu.VMEM((2, n_dp, *kind), bf16) for kind in kinds],
            *[pltpu.VMEM((chips, n_dp, *block), bf16) for block in blocks],
            *[pltpu.VMEM((heard, n_dp, *block), bf16) for block in blocks],
            *[pltpu.VMEM((n_dp + 1, *block), bf16) for block in blocks],
            *[pltpu.VMEM((2, n_dp // 2, *(block if square else (16, 128))), bf16) for block in blocks],
            dma((n, chips)),
            dma((n, chips)),
            dma((n, chips)),
            dma((n, chips)),
            dma((n, n_dp)),
            dma((n, n_dp + 1)),
            dma((n, 3)),
            dma((n, 3)),
            dma((len(kinds), 2)),
            dma((4, n_dp)),
            dma((4, n_dp)),
            dma((max(len(stages), 1), 2)),
            *[pltpu.VMEM(stage, jnp.bfloat16) for stage in stages],
        ],
        input_output_aliases=aliases,
        compiler_params=pltpu.CompilerParams(
            collective_id=number, has_side_effects=True, vmem_limit_bytes=62 * 1024 * 1024
        ),
    )(*items, *cut_in)


def scatter_all(
    n_dp, n_expert, items, cut_in, cut_shapes, cuts, number, aliases, stages, puts=nothing
):
    chips = n_expert // 2
    blocks = (2 * chips - 1 if chips != 4 else 7) * n_dp + n_dp + 3
    need = sum(blocks * item.shape[2] * item.shape[3] * 2 for item in items)
    kinds = {item.shape[2:] for item in items}
    need += sum(2 * n_dp * kind[0] * kind[1] * 2 for kind in kinds)
    need += sum(stage[0] * stage[1] * stage[2] * 2 for stage in stages)
    pieces = -(-need // (61 * 1024 * 1024))
    tiles = [item.shape[3] // 128 for item in items]
    results = [[] for item in items]
    extra = []
    for piece in range(pieces):
        ends = [(t * piece // pieces * 128, t * (piece + 1) // pieces * 128) for t in tiles]
        used = [i for i, (low, high) in enumerate(ends) if high > low]
        first = piece == 0
        outs = scatter_call(
            n_dp,
            n_expert,
            [items[i][..., ends[i][0] : ends[i][1]] if pieces > 1 else items[i] for i in used],
            cut_in if first else [],
            cut_shapes if first else [],
            cuts if first else nothing,
            number + piece,
            {len(used) + a: len(used) + b for a, b in aliases} if first else {},
            stages if first else [],
            puts if first else nothing,
        )
        for i, out in zip(used, outs):
            results[i].append(out)
        if first:
            extra = outs[len(used) :]
    return [one[0] if len(one) == 1 else jnp.concatenate(one, axis=1) for one in results], extra


def dot(left, right, dims):
    return lax.dot_general(
        left, right, ((dims[:1], dims[1:]), ((), ())), preferred_element_type=jnp.float32
    )


def picks(slots_ref, number):
    pair = slots_ref.shape[2]
    rows = lax.broadcasted_iota(jnp.int32, (2 * CAP, pair), 0)
    return [slots_ref[0, e : e + 1, :] == rows for e in range(number)]


def pick_kernel(number, experts_all, slots_ref, x_ref, g_ref, router_ref, rows_ref, grows_ref, gates_ref):
    chosen = picks(slots_ref, number)
    pick = jnp.concatenate(chosen, axis=0).astype(jnp.bfloat16)
    size = 2 * CAP
    x = x_ref[...]
    logits = dot(router_ref[...], x, (0, 1))
    names = lax.broadcasted_iota(jnp.int32, logits.shape, 0)
    logits = jnp.where(names < experts_all, logits, -1e30)
    weights = jnp.exp(logits - jnp.max(logits, axis=0, keepdims=True))
    probs = weights / jnp.sum(weights, axis=0, keepdims=True)
    for e in range(number):
        gate = jnp.sum(jnp.where(chosen[e], probs[e : e + 1, :], 0.0), axis=1, keepdims=True)
        gates_ref[e] = jnp.broadcast_to(gate, (size, 128))
    picked = dot(pick, x, (1, 0)).astype(jnp.bfloat16)
    for e in range(number):
        rows_ref[e] = picked[e * size : (e + 1) * size]
    picked = dot(pick, g_ref[...], (1, 0)).astype(jnp.bfloat16)
    for e in range(number):
        grows_ref[e] = picked[e * size : (e + 1) * size]


def expert_kernel(steps, half, n_weights, n_into, n_pack, names_ref, x_ref, g_ref, gates_ref, *refs):
    weights, refs = refs[:n_weights], refs[n_weights:]
    down_ref, refs = refs[0], refs[1 + n_into :]
    (
        y_ref,
        dx_ref,
        probs_ref,
        dgate_ref,
        dup_ref,
        ddown_ref,
        *pack_refs,
        sum_gate,
        sum_up,
    ) = refs
    bf16 = jnp.bfloat16
    g = g_ref[0]
    rows, width = x_ref.shape[1:]
    part = dgate_ref.shape[2]
    gate = gates_ref[0][:, :1]
    if n_weights == 2:
        piece = 512
        gate_ref, up_ref = weights
        gate_mid = dot(x_ref[0], gate_ref[0], (1, 0))
        up_mid = dot(x_ref[0], up_ref[0], (1, 0))
        spans = [
            (pl.ds(at, piece), gate_ref, up_ref, pl.ds(at, piece), pl.ds(0, part), pl.ds(0, part))
            for at in range(0, width, piece)
        ]
    else:
        piece = width // n_weights
        spans = []
        gate_mid = up_mid = 0.0
        for n, ref in enumerate(weights):
            span = pl.ds(pl.multiple_of(names_ref[1 + n], piece), piece)
            x_part = x_ref[0, :, span]
            gate_mid = gate_mid + dot(x_part, ref[0, :, :part], (1, 0))
            up_mid = up_mid + dot(x_part, ref[0, :, part:], (1, 0))
            spans.append((span, ref, ref, pl.ds(0, piece), pl.ds(0, part), pl.ds(part, part)))
    sigmoid = 1.0 / (1.0 + jnp.exp(-gate_mid))
    silu = gate_mid * sigmoid
    hidden = silu * up_mid
    hidden_low = hidden.astype(bf16)
    grad_plain = dot(g, down_ref[0], (1, 1))
    grad_gates = jnp.sum(grad_plain * hidden_low.astype(jnp.float32), axis=1, keepdims=True)
    high = grad_gates.astype(bf16).astype(jnp.float32)
    lane = lax.broadcasted_iota(jnp.int32, (rows, 128), 1)
    name = names_ref[0] + pl.program_id(0)
    probs_ref[0] = (
        jnp.where(lane == name, high, 0.0) + jnp.where(lane == name + half, grad_gates - high, 0.0)
    ).astype(bf16)
    grad_hidden = grad_plain * gate
    grad_gate = (
        grad_hidden * up_mid * sigmoid * (1.0 + gate_mid * (1.0 - sigmoid))
    ).astype(bf16)
    grad_up = (grad_hidden * silu).astype(bf16)
    scaled = (hidden * gate).astype(bf16)
    for at in range(0, width, piece):
        y_ref[0, :, at : at + piece] = (
            dot(hidden_low, down_ref[0, :, at : at + piece], (1, 0)) * gate
        ).astype(bf16)
    for span, gate_ref, up_ref, here, gate_columns, up_columns in spans:
        dx_ref[0, :, span] = (
            dot(grad_gate, gate_ref[0, here, gate_columns], (1, 1))
            + dot(grad_up, up_ref[0, here, up_columns], (1, 1))
        ).astype(bf16)
    step = pl.program_id(1)
    for span, *unused in spans:
        x_part = x_ref[0, :, span]
        here_gate = dot(x_part, grad_gate, (0, 0))
        here_up = dot(x_part, grad_up, (0, 0))
        here_down = dot(scaled, g_ref[0, :, span], (0, 0))
        if steps == 1:
            dgate_ref[0, span, :] = here_gate.astype(bf16)
            dup_ref[0, span, :] = here_up.astype(bf16)
            ddown_ref[0, :, span] = here_down
            continue

        @pl.when(step == 0)
        def _():
            sum_gate[span, :] = here_gate
            sum_up[span, :] = here_up
            ddown_ref[0, :, span] = here_down

        @pl.when(step > 0)
        def _():
            sum_gate[span, :] += here_gate
            sum_up[span, :] += here_up
            ddown_ref[0, :, span] += here_down

        @pl.when(step == steps - 1)
        def _():
            dgate_ref[0, span, :] = sum_gate[span, :].astype(bf16)
            dup_ref[0, span, :] = sum_up[span, :].astype(bf16)

    if n_pack:

        @pl.when((step == steps - 1) & (pl.program_id(0) < n_pack))
        def _():
            pack_ref = pack_refs[0]
            depth = pack_ref.shape[2]
            for plane in range(pack_ref.shape[0]):
                here = pl.ds(plane * depth, depth)
                pack_ref[plane, 0, :, :part] = dgate_ref[0, here, :]
                pack_ref[plane, 0, :, part:] = dup_ref[0, here, :]


def place_kernel(number, slots_ref, y_ref, dx_ref, probs_ref, out_ref, back_ref):
    pick = jnp.concatenate(picks(slots_ref, number), axis=0).astype(jnp.bfloat16)
    width = out_ref.shape[1]
    piece = 512
    flat = number * 2 * CAP
    for at in range(0, width, piece):
        part = y_ref[:, :, at : at + piece].reshape(flat, piece)
        out_ref[:, at : at + piece] = dot(pick, part, (0, 0)).astype(jnp.bfloat16)
        part = dx_ref[:, :, at : at + piece].reshape(flat, piece)
        back_ref[:, at : at + piece] = dot(pick, part, (0, 0)).astype(jnp.bfloat16)
    part = probs_ref[...].reshape(flat, 128)
    back_ref[:, width:] = dot(pick, part, (0, 0)).astype(jnp.bfloat16)


def pick_shapes(number, pairs):
    bf16 = jnp.bfloat16
    size = 2 * CAP
    return [
        jax.ShapeDtypeStruct((number, pairs * size, D), bf16),
        jax.ShapeDtypeStruct((number, pairs * size, D), bf16),
        jax.ShapeDtypeStruct((number, pairs * size, 128), jnp.float32),
    ]


def pick_rows(number, experts_all, slots, x_all, g_all, router, rows, grows, gates):
    pairs, _, pair = slots.shape
    size = 2 * CAP
    tokens = pl.BlockSpec((pair, D), lambda p: (p, 0))
    picked = pl.BlockSpec((number, size, D), lambda p: (0, p, 0))
    pltpu.emit_pipeline(
        functools.partial(pick_kernel, number, experts_all),
        grid=(pairs,),
        in_specs=[
            pl.BlockSpec((1, number, pair), lambda p: (p, 0, 0)),
            tokens,
            tokens,
            pl.BlockSpec(router.shape, lambda p: (0, 0)),
        ],
        out_specs=[picked, picked, pl.BlockSpec((number, size, 128), lambda p: (0, p, 0))],
    )(slots, x_all, g_all, router, rows, grows, gates)


def expert_call(names, half, low, number, rows, grows, gates, weights, down, into=(), pack=()):
    total, depth, _ = rows.shape
    part = down.shape[1]
    size = depth
    while size > 768:
        size //= 2
    steps = depth // size
    bf16 = jnp.bfloat16
    f32 = jnp.float32

    def from_rows(width):
        return pl.BlockSpec((1, size, width), lambda e, r: (e + low, r, 0))

    def whole(*shape):
        return pl.BlockSpec((1, *shape), lambda e, r: (e, 0, 0))

    def from_whole(*shape):
        return pl.BlockSpec((1, *shape), lambda e, r: (e + low, 0, 0))

    packed = [
        pl.BlockSpec(
            (planes, 1, D // planes, 2 * part),
            lambda e, r, n=n: (0, lax.min(e, n - 1), 0, 0),
        )
        for n, planes in ([pack] if pack else [])
    ]
    keep = (D, part) if steps > 1 else (16, 128)
    return pl.pallas_call(
        functools.partial(
            expert_kernel, steps, half, len(weights), len(into), pack[0] if pack else 0
        ),
        grid=(number, steps),
        in_specs=[
            pl.BlockSpec(memory_space=pltpu.SMEM),
            from_rows(D),
            from_rows(D),
            from_rows(128),
            *[(from_whole if len(weights) == 2 else whole)(*one.shape[1:]) for one in weights],
            from_whole(part, D),
            *[pl.BlockSpec(memory_space=pl.ANY)] * len(into),
        ],
        out_specs=[
            from_rows(D),
            from_rows(D),
            from_rows(128),
            whole(D, part),
            whole(D, part),
            from_whole(part, D),
            *packed,
        ],
        out_shape=[
            jax.ShapeDtypeStruct((total, depth, D), bf16),
            jax.ShapeDtypeStruct((total, depth, D), bf16),
            jax.ShapeDtypeStruct((total, depth, 128), bf16),
            jax.ShapeDtypeStruct((number, D, part), bf16),
            jax.ShapeDtypeStruct((number, D, part), bf16),
            jax.ShapeDtypeStruct((total, part, D), f32),
            *[
                jax.ShapeDtypeStruct((planes, n, D // planes, 2 * part), bf16)
                for n, planes in ([pack] if pack else [])
            ],
        ],
        input_output_aliases={
            5 + len(weights) + i: out for i, out in zip(range(len(into)), (0, 1, 2, 5))
        },
        scratch_shapes=[pltpu.VMEM(keep, f32), pltpu.VMEM(keep, f32)],
        compiler_params=pltpu.CompilerParams(vmem_limit_bytes=BIG),
    )(names, rows, grows, gates, *weights, down, *into)


def place_call(number, slots, y, dx, probs):
    pairs, _, pair = slots.shape
    bf16 = jnp.bfloat16
    size = 2 * CAP
    rows = pl.BlockSpec((number, size, D), lambda p: (0, p, 0))
    return pl.pallas_call(
        functools.partial(place_kernel, number),
        grid=(pairs,),
        in_specs=[
            pl.BlockSpec((1, number, pair), lambda p: (p, 0, 0)),
            rows,
            rows,
            pl.BlockSpec((number, size, 128), lambda p: (0, p, 0)),
        ],
        out_specs=[
            pl.BlockSpec((pair, D), lambda p: (p, 0)),
            pl.BlockSpec((pair, D + 128), lambda p: (p, 0)),
        ],
        out_shape=[
            jax.ShapeDtypeStruct((pairs * pair, D), bf16),
            jax.ShapeDtypeStruct((pairs * pair, D + 128), bf16),
        ],
        compiler_params=pltpu.CompilerParams(vmem_limit_bytes=BIG),
    )(slots, y, dx, probs)


def widen_kernel(*refs):
    half = len(refs) // 2
    for source, target in zip(refs[:half], refs[half:]):
        target[...] = source[...].astype(jnp.float32)


def widen(low, values):
    number, rows, columns = values[0].shape
    block = pl.BlockSpec((1, rows, columns), lambda e: (e + low, 0, 0))
    return pl.pallas_call(
        widen_kernel,
        grid=(number - low,),
        in_specs=[block] * len(values),
        out_specs=[block] * len(values),
        out_shape=[jax.ShapeDtypeStruct(one.shape, jnp.float32) for one in values],
        compiler_params=pltpu.CompilerParams(vmem_limit_bytes=BIG),
    )(*values)


def widen_pieces_kernel(n_pieces, offsets_ref, *refs):
    pieces, refs = refs[:n_pieces], refs[n_pieces + 2 :]
    targets, wide, sems = refs[:2], refs[2], refs[3]
    part = wide.shape[4]
    copies = []
    for k, piece in enumerate(pieces):
        columns = pl.ds(pl.multiple_of(offsets_ref[k], part), part)
        for n in range(2):
            wide[k, n] = piece[:, :, n * part : (n + 1) * part].astype(jnp.float32)
            copy = pltpu.make_async_copy(
                wide.at[k, n], targets[n].at[pl.ds(0, piece.shape[0]), :, columns], sems.at[k, n]
            )
            copy.start()
            copies.append(copy)
    for copy in copies:
        copy.wait()


def widen_pieces(offsets, pieces, into):
    size, rows, columns = pieces[0].shape
    anywhere = pl.BlockSpec(memory_space=pl.ANY)
    count = len(pieces)
    return pl.pallas_call(
        functools.partial(widen_pieces_kernel, count),
        in_specs=[
            pl.BlockSpec(memory_space=pltpu.SMEM),
            *[pl.BlockSpec(memory_space=pltpu.VMEM)] * count,
            anywhere,
            anywhere,
        ],
        out_specs=[anywhere, anywhere],
        out_shape=[jax.ShapeDtypeStruct(one.shape, one.dtype) for one in into],
        scratch_shapes=[
            pltpu.VMEM((count, 2, size, rows, columns // 2), jnp.float32),
            pltpu.SemaphoreType.DMA((count, 2)),
        ],
        input_output_aliases={1 + count: 0, 2 + count: 1},
        compiler_params=pltpu.CompilerParams(vmem_limit_bytes=BIG),
    )(offsets, *pieces, *into)


def shards(
    n_dp,
    n_expert,
    tokens,
    cotangent,
    lengths,
    routes,
    w_query,
    w_key,
    w_value,
    w_out,
    w_router,
    gain_attn,
    gain_query,
    gain_key,
    gain_mlp,
    w_gate,
    w_up,
    w_down,
):
    groups = n_dp * n_expert
    bf16 = jnp.bfloat16
    number = w_gate.shape[0]
    ff = w_gate.shape[2]
    part = ff // n_dp
    experts_all = w_router.shape[1]
    width = 128
    small = jnp.concatenate(
        [
            w_router,
            gain_attn[:, None],
            gain_query[:, None],
            gain_key[:, None],
            gain_mlp[:, None],
            jnp.zeros((w_router.shape[0], width - experts_all - 4), bf16),
        ],
        axis=1,
    )
    hits = jnp.any(
        routes[:, :, None] == jnp.arange(width, dtype=jnp.int32)[None, None, :], axis=1
    ).astype(bf16)
    count = tokens.shape[0]
    rows_each = w_query.shape[0]
    extras = jnp.concatenate([hits, jnp.pad(small, ((0, count - rows_each), (0, 0)))], axis=1)
    weights = jnp.stack([w_query, w_key, w_value, w_out])
    depth = w_gate.shape[1]
    early = number // 4
    beside = early + number // 8
    late = number - number // 4
    back_beside = number // 8
    back_third = back_beside + number * 3 // 8
    me = lax.axis_index("dp")
    cut_shape = jax.ShapeDtypeStruct((number, n_dp * depth, part), bf16)

    def row_block(size):
        return lambda ref, block: ref.at[pl.ds(pl.multiple_of(block * size, 16), size)]

    def columns_at(at):
        return pl.ds(pl.multiple_of(at * part, part), part)

    def rows_at(at):
        return pl.ds(pl.multiple_of(at * depth, depth), depth)

    def recut(low, high):
        def cuts(ins, outs):
            def pair(n):
                chosen = pl.ds(low, high - low)
                return (
                    lambda to: ins[n].at[chosen, :, columns_at(to)],
                    lambda at: outs[n].at[chosen, rows_at(at)],
                )

            return [pair(0), pair(1)]

        return cuts

    to_plane, from_plane = partners(me, n_dp)

    def permuted(pieces, chained=False):
        got = []
        for k, piece in enumerate(pieces, 1):
            if chained and got:
                piece, last = lax.optimization_barrier((piece, got.pop()))
                got.append(last)
            paths = [(i, partners(i, n_dp)[0](k)) for i in range(n_dp)]
            got.append(lax.ppermute(piece, "dp", paths))
        return got

    def cut_pieces(low, high, first_k, ins, outs):
        to, unused = partners(lax.axis_index("dp"), n_dp)
        pairs = []
        for k, piece in enumerate(outs, first_k):
            for n in range(2):
                source = ins[n].at[pl.ds(low, high - low), :, columns_at(to(k))]
                pairs.append((source, piece.at[:, :, pl.ds(n * part, part)]))
        return pairs

    def piece_shapes(size, first_k):
        shape = jax.ShapeDtypeStruct((size, depth, 2 * part), bf16)
        return [shape] * (n_dp - first_k if size else 0)

    def stages(*sizes):
        return [(size, depth, part) for size in sizes]

    soon_shapes = piece_shapes(beside - early, 1)
    late_shapes = piece_shapes(number - late, 0)
    n_soon = len(soon_shapes)

    weights_all, extras_all, gate_early, up_early, *pieces = gather_call(
        n_dp,
        n_expert,
        [weights, extras],
        [
            jax.ShapeDtypeStruct((4, groups * rows_each, D), bf16),
            jax.ShapeDtypeStruct((groups * count, 2 * width), bf16),
        ],
        [
            lambda ref, block: ref.at[
                :, pl.ds(pl.multiple_of(block * rows_each, 16), rows_each)
            ],
            row_block(count),
        ],
        [w_gate, w_up],
        [cut_shape, cut_shape, *soon_shapes, *late_shapes],
        recut(0, early),
        {},
        0,
        stages(
            *[early] * 2,
            *[beside - early] * (2 * n_soon),
            *[number - late] * (2 * n_dp),
        ),
        lambda ins, outs: cut_pieces(early, beside, 1, ins, outs[2 : 2 + n_soon])
        + cut_pieces(late, number, 0, ins, outs[2 + n_soon :]),
    )
    soon_pieces, late_pieces = pieces[:n_soon], pieces[n_soon:]
    query_weight, key_weight, value_weight, out_weight = (weights_all[i] for i in range(4))
    small_all = (
        extras_all[:, width:].reshape(groups, count, width)[:, :rows_each].reshape(-1, width)
    )
    hits_all = extras_all[:, :experts_all]
    router_weight = small_all[:, :experts_all]
    gains = small_all[:, experts_all : experts_all + 4].astype(jnp.float32)
    attn_gain, query_gain, key_gain, mlp_gain = (gains[:, i] for i in range(4))
    inputs = tokens.astype(jnp.float32)
    segment, position, places = layout(lengths[0], count)
    half = HD // 2
    freq = 10000.0 ** (-2.0 * jnp.arange(half, dtype=jnp.float32) / HD)
    angle = position.astype(jnp.float32)[:, None] * freq[None, :]
    cosine = jnp.cos(angle)[:, None, :]
    sine = jnp.sin(angle)[:, None, :]
    scale = HD ** (-0.5)
    normed, attn_inverse = rms_forward(inputs, attn_gain)
    normed_low = normed.astype(bf16)
    query_raw = product(normed_low, query_weight, "td,de->te")
    key_raw = product(normed_low, key_weight, "td,de->te")
    value_low = product(normed_low, value_weight, "td,de->te").astype(bf16)
    query_normed, query_inverse = rms_forward(query_raw, query_gain)
    key_normed, key_inverse = rms_forward(key_raw, key_gain)
    query_low = rotate(query_normed, cosine, sine).astype(bf16).reshape(count, HEADS, HD)
    key_low = rotate(key_normed, cosine, sine).astype(bf16).reshape(count, HEADS, HD)
    value_heads = value_low.reshape(count, HEADS, HD)
    allowed = (segment[:, None] == segment[None, :]) & (places[None, :] <= places[:, None])
    scores = product(query_low, key_low, "qhd,khd->hqk") * scale
    scores = jnp.where(allowed[None], scores, -1e30)
    probs = jax.nn.softmax(scores, axis=-1)
    probs_low = probs.astype(bf16)
    attended_low = product(probs_low, value_heads, "hqk,khd->qhd").reshape(count, D).astype(bf16)
    middle = inputs + product(attended_low, out_weight, "td,de->te")
    mlp_normed, mlp_inverse = rms_forward(middle, mlp_gain)
    mlp_low = mlp_normed.astype(bf16)
    router = jax.nn.softmax(product(mlp_low, router_weight, "td,de->te"), axis=-1)

    first = lax.axis_index("expert") * number
    hit = lax.dynamic_slice_in_dim(hits_all, first, number, 1).reshape(groups, count, number)
    before = jnp.tril(jnp.ones((count, count), bf16), -1)
    slot = product(before, hit, "ts,bse->bet").astype(jnp.int32)
    slot = jnp.where(jnp.transpose(hit, (0, 2, 1)) > 0, slot, -1)
    slot = slot.reshape(groups // 2, 2, number, count)
    shift = jnp.array([0, CAP], jnp.int32)[None, :, None, None]
    slots = jnp.transpose(jnp.where(slot < 0, -1, slot + shift), (0, 2, 1, 3))
    slots = slots.reshape(groups // 2, number, 2 * count)
    router_own = jnp.pad(
        jnp.roll(router_weight, -first, axis=1), ((0, 0), (0, width - experts_all))
    )
    if n_soon:
        mlp_low, *soon_pieces = lax.optimization_barrier((mlp_low, *permuted(soon_pieces)))

    def put_weights(ins, outs):
        chosen = pl.ds(early, beside - early)
        unused, heard = partners(lax.axis_index("dp"), n_dp)
        pairs = []
        if beside > early:
            own = lax.axis_index("dp")
            for n in range(2):
                source = ins[n].at[chosen, :, columns_at(own)]
                pairs.append((source, outs[n].at[chosen, rows_at(own)]))
        for k, piece in enumerate(ins[6:], 1):
            for n in range(2):
                columns = piece.at[:, :, pl.ds(n * part, part)]
                pairs.append((columns, outs[n].at[chosen, rows_at(heard(k))]))
        return pairs

    def pick_all(items, ins, outs):
        pick_rows(number, experts_all, ins[4], *items, ins[5], *outs[2:])

    unused, unused, gate_cut, up_cut, rows, grows, gates = gather_call(
        n_dp,
        n_expert,
        [mlp_low, cotangent],
        [jax.ShapeDtypeStruct((groups * count, D), bf16)] * 2,
        [row_block(count)] * 2,
        [w_gate, w_up, gate_early, up_early, slots, router_own, *soon_pieces],
        [cut_shape, cut_shape, *pick_shapes(number, groups // 2)],
        recut(beside, late),
        {4: 2, 5: 3},
        1,
        stages(*[late - beside] * 2, *[beside - early] * (2 * n_dp if n_soon else 0)),
        put_weights,
        pick_all,
    )
    *late_pieces, rows = lax.optimization_barrier((*late_pieces, rows))
    late_pieces = [late_pieces[0], *permuted(late_pieces[1:])]
    packing = back_beside > 0 and depth == 512
    *outs, gate_soon, up_soon, down_soon = expert_call(
        first[None],
        experts_all,
        0,
        late,
        rows,
        grows,
        gates,
        [gate_cut, up_cut],
        w_down,
        pack=(back_beside, n_dp) if packing else (),
    )
    if packing:
        *outs, gate_soon, up_soon, down_soon, packed = [*outs, gate_soon, up_soon, down_soon]
    offsets = [from_plane(k) * depth for k in range(n_dp)]
    weighted, grad_rows, grad_gates, gate_rest, up_rest, grad_down_part = expert_call(
        jnp.stack([first + late, *offsets]),
        experts_all,
        late,
        number - late,
        rows,
        grows,
        gates,
        late_pieces,
        w_down,
        [*outs, down_soon],
    )
    part_out, part_back = place_call(number, slots, weighted, grad_rows, grad_gates)

    def ways(low, high, at, ins, outs):
        def pair(n):
            return (
                lambda to: ins[n].at[pl.ds(low, high - low), rows_at(to)],
                lambda here: outs[n].at[pl.ds(low + at, high - low), :, columns_at(here)],
            )

        return [pair(0), pair(1)]

    pieces = []
    if back_beside:
        for k in range(1, n_dp):
            if packing:
                piece = lax.dynamic_index_in_dim(packed, to_plane(k), 0, False)
            else:
                piece = jnp.concatenate(
                    [
                        lax.dynamic_slice_in_dim(
                            one[:back_beside], to_plane(k) * depth, depth, 1
                        )
                        for one in (gate_soon, up_soon)
                    ],
                    axis=2,
                )
            pieces.append(piece)
        pieces = permuted(pieces)
    way_shapes = [jax.ShapeDtypeStruct((number, depth, ff), bf16)] * 2
    (back,), (gate_third, up_third) = scatter_all(
        n_dp,
        n_expert,
        [part_back.reshape(n_dp, n_expert, count, D + width)],
        [gate_soon, up_soon],
        way_shapes,
        lambda ins, outs: ways(back_beside, back_third, 0, ins, outs),
        8,
        (),
        stages(*[back_third - back_beside] * 2),
    )

    grad_final = cotangent.astype(jnp.float32)
    grad_mlp = back[:, :D]
    grad_router_probs = back[:, D : D + experts_all] + back[:, D + experts_all :]
    grad_logits = router * (
        grad_router_probs - jnp.sum(router * grad_router_probs, axis=1, keepdims=True)
    )
    grad_logits_low = grad_logits.astype(bf16)
    grad_router_full = product(mlp_low, grad_logits_low, "td,te->de")
    grad_mlp = grad_mlp + product(grad_logits_low, router_weight, "te,de->td")
    grad_middle_part, grad_mlp_gain = rms_backward(middle, mlp_inverse, mlp_gain, grad_mlp)
    grad_middle = grad_final + grad_middle_part
    grad_branch_low = grad_middle.astype(bf16)
    grad_out_full = product(attended_low, grad_branch_low, "td,te->de")
    grad_attended = (
        product(grad_branch_low, out_weight, "te,de->td").astype(bf16).reshape(count, HEADS, HD)
    )
    grad_weights = product(grad_attended, value_heads, "qhd,khd->hqk")
    grad_scores = probs * (grad_weights - jnp.sum(probs * grad_weights, axis=-1, keepdims=True))
    grad_scores_low = grad_scores.astype(bf16)
    grad_query_turn = product(grad_scores_low, key_low, "hqk,khd->qhd").reshape(count, D) * scale
    grad_key_turn = product(grad_scores_low, query_low, "hqk,qhd->khd").reshape(count, D) * scale
    grad_value_low = (
        product(probs_low, grad_attended, "hqk,qhd->khd").reshape(count, D).astype(bf16)
    )
    grad_query_raw, grad_query_gain = rms_backward(
        query_raw, query_inverse, query_gain, rotate(grad_query_turn, cosine, -sine)
    )
    grad_key_raw, grad_key_gain = rms_backward(
        key_raw, key_inverse, key_gain, rotate(grad_key_turn, cosine, -sine)
    )
    grad_query_low = grad_query_raw.astype(bf16)
    grad_key_low = grad_key_raw.astype(bf16)
    grad_query_full = product(normed_low, grad_query_low, "td,te->de")
    grad_key_full = product(normed_low, grad_key_low, "td,te->de")
    grad_value_full = product(normed_low, grad_value_low, "td,te->de")
    grad_normed = (
        product(grad_query_low, query_weight, "te,de->td")
        + product(grad_key_low, key_weight, "te,de->td")
        + product(grad_value_low, value_weight, "te,de->td")
    )
    grad_inputs_part, grad_attn_gain = rms_backward(inputs, attn_inverse, attn_gain, grad_normed)
    grad_inputs = grad_middle + grad_inputs_part

    small_grads = jnp.concatenate(
        [
            grad_router_full,
            grad_attn_gain[:, None],
            grad_query_gain[:, None],
            grad_key_gain[:, None],
            grad_mlp_gain[:, None],
            jnp.zeros((D, width - experts_all - 4), jnp.float32),
        ],
        axis=1,
    )

    def blocks_of(value):
        return value.astype(bf16).reshape(n_dp, n_expert, rows_each, -1)

    sums, (gate_back, up_back) = scatter_all(
        n_dp,
        n_expert,
        [
            blocks_of(value)
            for value in (
                grad_out_full,
                grad_value_full,
                grad_key_full,
                grad_query_full,
                small_grads,
            )
        ]
        + [part_out.reshape(n_dp, n_expert, count, D)],
        [gate_third, up_third, gate_soon, up_soon, gate_rest, up_rest],
        way_shapes,
        lambda ins, outs: ways(back_third, late, 0, ins[2:4], outs)
        + ways(0, number - late, late, ins[4:6], outs),
        16,
        ((0, 0), (1, 1)),
        stages(*[late - back_third] * 2, *[number - late] * 2),
    )
    grad_out_part, grad_value_part, grad_key_part, grad_query_part, small_part, summed = sums
    output = (middle + summed).astype(bf16)
    grad_router_part = small_part[:, :experts_all]
    gain_parts = [small_part[:, experts_all + i] for i in range(4)]
    widened = widen(back_beside, [gate_back, up_back])
    if back_beside:
        own = jnp.concatenate(
            [
                lax.dynamic_slice_in_dim(one[:back_beside], me * depth, depth, 1)
                for one in (gate_soon, up_soon)
            ],
            axis=2,
        )
        offsets = jnp.stack([from_plane(k) * part for k in range(n_dp)])
        widened = widen_pieces(offsets, [own, *pieces], widened)
    grad_gate_part, grad_up_part = widened
    return (
        output,
        grad_inputs,
        grad_query_part,
        grad_key_part,
        grad_value_part,
        grad_out_part,
        grad_router_part,
        gain_parts[0],
        gain_parts[1],
        gain_parts[2],
        gain_parts[3],
        grad_gate_part,
        grad_up_part,
        grad_down_part,
    )


def solution(mesh):
    return jax.shard_map(
        functools.partial(shards, mesh.shape["dp"], mesh.shape["expert"]),
        mesh=mesh,
        in_specs=(
            P(("dp", "expert"), None),
            P(("dp", "expert"), None),
            P(("dp", "expert"), None),
            P(("dp", "expert"), None),
            P(("dp", "expert"), None),
            P(("dp", "expert"), None),
            P(("dp", "expert"), None),
            P(("dp", "expert"), None),
            P(("dp", "expert"), None),
            P(("dp", "expert")),
            P(("dp", "expert")),
            P(("dp", "expert")),
            P(("dp", "expert")),
            P("expert", "dp", None),
            P("expert", "dp", None),
            P("expert", "dp", None),
        ),
        out_specs=(
            P(("dp", "expert"), None),
            P(("dp", "expert"), None),
            P(("dp", "expert"), None),
            P(("dp", "expert"), None),
            P(("dp", "expert"), None),
            P(("dp", "expert"), None),
            P(("dp", "expert"), None),
            P(("dp", "expert")),
            P(("dp", "expert")),
            P(("dp", "expert")),
            P(("dp", "expert")),
            P("expert", "dp", None),
            P("expert", "dp", None),
            P("expert", "dp", None),
        ),
        check_vma=False,
    )
```

```python
import functools

import jax
import jax.numpy as jnp
from jax import lax
from jax.experimental import pallas as pl
from jax.experimental.pallas import tpu as pltpu
from jax.sharding import PartitionSpec as P

D = 2048
HEADS = 16
HD = 128
TOPK = 8
CAP = 24


eps = 1e-05


def product(left, right, form):
    return jnp.einsum(form, left, right, preferred_element_type=jnp.float32)


def rms_forward(values, gain):
    inverse = lax.rsqrt(jnp.mean(values * values, axis=-1, keepdims=True) + eps)
    return (values * inverse * gain, inverse)


def rms_backward(values, inverse, gain, grad):
    scaled = grad * gain
    inner = jnp.mean(scaled * values, axis=-1, keepdims=True)
    grad_values = inverse * scaled - values * (inverse * inverse * inverse) * inner
    grad_gain = jnp.sum(grad * values * inverse, axis=0)
    return (grad_values, grad_gain)


def layout(lengths_row, count):
    places = jnp.arange(count, dtype=jnp.int32)
    ends = jnp.cumsum(lengths_row, dtype=jnp.int32)
    passed = (places[:, None] >= ends[None, :]).astype(jnp.int32)
    segment = jnp.sum(passed, axis=1, dtype=jnp.int32)
    start = jnp.sum(passed * lengths_row[None, :], axis=1, dtype=jnp.int32)
    return (segment, places - start, places)


def rotate(values, cosine, sine):
    count = values.shape[0]
    heads = values.reshape(count, HEADS, HD)
    half = HD // 2
    first = heads[..., :half]
    second = heads[..., half:]
    turned = jnp.concatenate(
        [first * cosine - second * sine, second * cosine + first * sine], axis=-1
    )
    return turned.reshape(count, D)


MESH = pl.DeviceIdType.MESH
BIG = 60 * 1024 * 1024


def place_of():
    z = lax.axis_index("dp")
    j = lax.axis_index("expert")
    return z, j, j // 2, j % 2


def other_chips(chip, chips):
    if chips == 4:
        square = [chip, chip + 1 - 2 * (chip % 2), chip + 2 - 4 * (chip // 2), 3 - chip]
        return lambda k: square[k], lambda k: square[k]
    return lambda k: (chip + k) % chips, lambda k: (chip + chips - k) % chips


def partners(z, n_dp):
    if n_dp == 4:
        pairs = [z, (z + 2) % 4, 3 - z, z + 1 - 2 * (z % 2)]
        return lambda k: pairs[k], lambda k: pairs[k]
    return lambda k: (z + k) % n_dp, lambda k: (z + n_dp - k) % n_dp


def greet(n_dp, n_expert):
    z, j, chip, core = place_of()
    chips = n_expert // 2
    barrier = pltpu.get_barrier_semaphore()
    for k in range(1, n_dp):
        pl.semaphore_signal(
            barrier, inc=1, device_id=((z + k) % n_dp, j), device_id_type=MESH
        )
    for k in range(1, chips):
        other = ((chip + k) % chips) * 2 + core
        pl.semaphore_signal(barrier, inc=1, device_id=(z, other), device_id_type=MESH)
    pl.semaphore_signal(
        barrier, inc=1, device_id=(z, chip * 2 + 1 - core), device_id_type=MESH
    )
    pl.semaphore_wait(barrier, n_dp - 1 + chips - 1 + 1)


def remote(source, target, send, receive, device):
    return pltpu.make_async_remote_copy(
        src_ref=source,
        dst_ref=target,
        send_sem=send,
        recv_sem=receive,
        device_id=device,
        device_id_type=MESH,
    )


def exchange(n_dp, pairs, send, receive):
    z, j, chip, core = place_of()
    to_plane, unused = partners(z, n_dp)
    copies = []
    for i, (source, target) in enumerate(pairs):
        for k in range(1, n_dp):
            to = to_plane(k)
            copies.append(
                remote(source(to), target(z), send.at[i, k], receive.at[i, k], (to, j))
            )
    return copies


def moves(pairs, stages, local):
    if not stages:
        copies = [
            pltpu.make_async_copy(source, target, local.at[i, 0])
            for i, (source, target) in enumerate(pairs)
        ]
        for copy in copies:
            copy.start()
        return [], copies
    bring = [
        pltpu.make_async_copy(source, stages[i], local.at[i, 0])
        for i, (source, target) in enumerate(pairs)
    ]
    put = [
        pltpu.make_async_copy(stages[i], target, local.at[i, 1])
        for i, (source, target) in enumerate(pairs)
    ]
    return bring, put


def nothing(ins, outs):
    return []


def gather_kernel(
    n_dp, n_expert, n_items, places, cuts, puts, finish, n_cut, n_out, n_stages, *refs
):
    z, j, chip, core = place_of()
    chips = n_expert // 2
    square = chips == 4
    to_chip, from_chip = other_chips(chip, chips)
    sources = refs[:n_items]
    cut_in = refs[n_items : n_items + n_cut]
    at = n_items + n_cut
    targets = refs[at : at + n_items]
    cut_out = refs[at + n_items : at + n_items + n_out]
    (
        send_c,
        recv_c,
        send_b,
        recv_b,
        send_a,
        recv_a,
        local,
        send_x,
        recv_x,
        local_y,
        *stages,
    ) = refs[at + n_items + n_out :]
    greet(n_dp, n_expert)
    mate = (z, chip * 2 + 1 - core)
    near = (1, 2) if square else tuple(range(1, chips))

    def slot(i, plane, column):
        return places[i](targets[i], plane * n_expert + column)

    def pass_on(i, plane, source, column, k, chip_to):
        return remote(
            source,
            slot(i, plane, column),
            send_b.at[i, plane, k],
            recv_b.at[i, plane, k],
            (z, chip_to * 2 + core),
        )

    def hand(i, plane, source):
        for k in near:
            pass_on(i, plane, source, j, k, to_chip(k)).start()
        remote(
            source, slot(i, plane, j), send_a.at[i, plane, 0], recv_a.at[i, plane, 0], mate
        ).start()

    def along(i, plane, source, way, step):
        return remote(
            source, slot(i, plane, j), send_c.at[i, way, plane], recv_c.at[i, plane], (z + step, j)
        )

    def at_distance(d, body):
        if d == 0:
            body(z, 0)
            return

        @pl.when(z >= d)
        def _():
            body(z - d, 0)

        @pl.when(z + d < n_dp)
        def _():
            body(z + d, 1)

    for i in range(n_items):

        @pl.when(z < n_dp - 1)
        def _():
            along(i, z, sources[i], 0, 1).start()

        @pl.when(z > 0)
        def _():
            along(i, z, sources[i], 1, -1).start()

        hand(i, z, sources[i])
        pltpu.make_async_copy(sources[i], slot(i, z, j), local.at[i]).start()

    def relay(plane, way):
        step = -1 if way else 1
        for i in range(n_items):
            block = slot(i, plane, j)
            along(i, plane, block, way, step).wait_recv()

            @pl.when(z > 0 if way else z < n_dp - 1)
            def _():
                along(i, plane, block, way, step).start()

            hand(i, plane, block)

    for d in range(1, n_dp):
        at_distance(d, relay)
    pairs = cuts(cut_in, cut_out)
    copies = exchange(n_dp, pairs, send_x, recv_x)
    for copy in copies:
        copy.start()
    own = [(source(z), target(z)) for source, target in pairs]
    bring, put = moves(own + puts(cut_in, cut_out), stages, local_y)
    for copy in bring:
        copy.start()
    for one, other in zip(bring, put):
        one.wait()
        other.start()

    def arrive(i, plane, k):
        column = from_chip(k) * 2 + core
        block = slot(i, plane, column)
        pass_on(i, plane, block, column, k, chip).wait_recv()
        remote(block, block, send_a.at[i, plane, k], recv_a.at[i, plane, k], mate).start()
        return block, column

    def arrived(plane, way):
        for i in range(n_items):
            for k in near:
                block, column = arrive(i, plane, k)
                if square:

                    @pl.when(plane % 2 == k - 1)
                    def _():
                        pass_on(i, plane, block, column, 3, to_chip(3 - k)).start()

    def crossed(plane, way):
        for i in range(n_items):
            arrive(i, plane, 3)

    for d in range(n_dp):
        at_distance(d, arrived)
    if square:
        for d in range(n_dp):
            at_distance(d, crossed)

    for i in range(n_items):
        for plane in range(n_dp):
            for k in range(chips):
                column = (from_chip(k) if k else chip) * 2 + 1 - core
                block = slot(i, plane, column)
                remote(
                    block, block, send_a.at[i, plane, k], recv_a.at[i, plane, k], mate
                ).wait_recv()
        pltpu.make_async_copy(sources[i], slot(i, z, j), local.at[i]).wait()
    finish(targets, cut_in, cut_out)
    for i in range(n_items):
        for plane in range(n_dp):
            block = slot(i, plane, j)
            for k in range(1, chips):
                pass_on(i, plane, block, j, k, chip).wait_send()
            for k in range(chips):
                remote(
                    block, block, send_a.at[i, plane, k], recv_a.at[i, plane, k], mate
                ).wait_send()

            @pl.when((z < n_dp - 1) & (z >= plane))
            def _():
                along(i, plane, block, 0, 1).wait_send()

            @pl.when((z > 0) & (z <= plane))
            def _():
                along(i, plane, block, 1, -1).wait_send()

    for copy in copies + put:
        copy.wait()


def gather_call(
    n_dp,
    n_expert,
    items,
    shapes,
    places,
    cut_in,
    cut_shapes,
    cuts,
    aliases,
    number,
    stages,
    puts=nothing,
    finish=lambda items, ins, outs: None,
):
    chips = n_expert // 2
    n, m = len(items), len(cut_shapes)
    dma = pltpu.SemaphoreType.DMA
    anywhere = pl.BlockSpec(memory_space=pl.ANY)
    return pl.pallas_call(
        functools.partial(
            gather_kernel,
            n_dp,
            n_expert,
            n,
            places,
            cuts,
            puts,
            finish,
            len(cut_in),
            m,
            len(stages),
        ),
        out_shape=[*shapes, *cut_shapes],
        in_specs=[anywhere] * (n + len(cut_in)),
        out_specs=[anywhere] * (n + m),
        scratch_shapes=[
            dma((n, 2, n_dp)),
            dma((n, n_dp)),
            dma((n, n_dp, chips)),
            dma((n, n_dp, chips)),
            dma((n, n_dp, chips)),
            dma((n, n_dp, chips)),
            dma((n,)),
            dma((4, n_dp)),
            dma((4, n_dp)),
            dma((max(len(stages), 4), 2)),
            *[pltpu.VMEM(stage, jnp.bfloat16) for stage in stages],
        ],
        input_output_aliases=aliases,
        compiler_params=pltpu.CompilerParams(
            collective_id=number, has_side_effects=True, vmem_limit_bytes=BIG
        ),
    )(*items, *cut_in)


def scatter_kernel(
    n_dp, n_expert, n_items, n_cut, n_out, cuts, puts, rings, n_rings, *refs
):
    z, j, chip, core = place_of()
    chips = n_expert // 2
    square = chips == 4
    to_chip, from_chip = other_chips(chip, chips)
    refs = list(refs)

    def take(count):
        taken = refs[:count]
        del refs[:count]
        return taken

    sources, cut_in, targets, cut_out = take(n_items), take(n_cut), take(n_items), take(n_out)
    ring, got_a, got_b, got_c = take(n_rings), take(n_items), take(n_items), take(n_items)
    transit = take(n_items)
    (
        send_a,
        recv_a,
        send_b,
        recv_b,
        send_c,
        recv_c,
        send_t,
        recv_t,
        local,
        send_x,
        recv_x,
        local_y,
        *stages,
    ) = refs
    greet(n_dp, n_expert)
    mate = (z, chip * 2 + 1 - core)
    order = [3, 1, 2, 0] if square else [*range(1, chips), 0]
    half = n_dp // 2
    low, high = pl.ds(0, half), pl.ds(half, n_dp - half)

    def chip_of(k):
        return to_chip(k) if k else chip

    def to_mate(i, k):
        return remote(
            sources[i].at[:, chip_of(k) * 2 + 1 - core],
            got_a[i].at[k],
            send_a.at[i, k],
            recv_a.at[i, k],
            mate,
        )

    turn = [0] * n_rings
    loads = []
    for i in range(n_items):
        for k in order:
            loads.append((i, k, turn[rings[i]] % 2))
            turn[rings[i]] += 1

    def load(i, k, at):
        return pltpu.make_async_copy(
            sources[i].at[:, chip_of(k) * 2 + core], ring[rings[i]].at[at], local.at[rings[i], at]
        )

    def send_near(i, k, part, number):
        return remote(
            got_a[i].at[k, part],
            got_b[i].at[k - 1, part],
            send_b.at[i, number],
            recv_b.at[i, number],
            (z, to_chip(k) * 2 + core),
        )

    def send_over(i, k, part):
        return remote(
            got_a[i].at[3, part],
            transit[i].at[k - 1],
            send_t.at[i, k],
            recv_t.at[i, k],
            (z, to_chip(k) * 2 + core),
        )

    def send_far(i, k):
        return remote(
            got_a[i].at[k],
            got_b[i].at[k - 1],
            send_b.at[i, k],
            recv_b.at[i, k],
            (z, to_chip(k) * 2 + core),
        )

    def along(i, plane, way):
        slot = n_dp - (z - 1) + plane if way else plane - (z + 1)
        return remote(
            got_a[i].at[0, plane],
            got_c[i].at[slot],
            send_c.at[i, plane],
            recv_c.at[i, slot],
            (z - 1 if way else z + 1, j),
        )

    def from_along(i, slot):
        return remote(
            got_c[i].at[slot], got_c[i].at[slot], send_c.at[i, 0], recv_c.at[i, slot], mate
        )

    f32 = jnp.float32

    def add(i, planes, target, terms):
        rows = got_a[i].shape[2]
        per = rows // 16

        def step(n, unused):
            plane = n // per
            at = pl.ds(pl.multiple_of((n % per) * 16, 16), 16)
            total = terms[0](plane, at).astype(f32)
            for term in terms[1:]:
                total = total + term(plane, at).astype(f32)
            target(plane, at, total)
            return unused

        lax.fori_loop(0, planes * per, step, 0)

    def grow(i, k, first, planes, term):
        def target(plane, at, total):
            got_a[i][k, plane + first, at] = total.astype(got_a[i].dtype)

        add(i, planes, target, [lambda plane, at: got_a[i][k, plane + first, at], term])

    for i in range(n_items):
        for k in order:
            to_mate(i, k).start()
    started = 0
    ahead = [0] * n_rings
    for i, k, at in loads:
        if ahead[rings[i]] < 2:
            load(i, k, at).start()
            ahead[rings[i]] += 1
    pairs = cuts(cut_in, cut_out)
    copies = exchange(n_dp, pairs, send_x, recv_x)
    for copy in copies:
        copy.start()
    own = [(source(z), target(z)) for source, target in pairs]
    bring, put = moves(own + puts(cut_in, cut_out), stages, local_y)
    for copy in bring:
        copy.start()

    for n, (i, k, at) in enumerate(loads):
        load(i, k, at).wait()
        to_mate(i, k).wait_recv()
        grow(i, k, 0, n_dp, lambda plane, rows: ring[rings[i]][at, plane, rows])
        later = [one for one in loads[n + 1 :] if rings[one[0]] == rings[i]]
        if len(later) >= 2:
            load(*later[1]).start()
        if not k:
            continue
        if not square:
            send_far(i, k).start()
        elif k == 3:
            send_over(i, 1, low).start()
            send_over(i, 2, high).start()
        elif k == 1:
            send_near(i, 1, low, 0).start()
        else:
            send_near(i, 2, high, 1).start()
    for one, other in zip(bring, put):
        one.wait()
        other.start()
    if square:
        for i in range(n_items):
            send_over(i, 2, high).wait_recv()
            grow(i, 1, half, n_dp - half, lambda plane, rows: transit[i][1, plane, rows])
            send_near(i, 1, high, 2).start()
            send_over(i, 1, low).wait_recv()
            grow(i, 2, 0, half, lambda plane, rows: transit[i][0, plane, rows])
            send_near(i, 2, low, 3).start()
    for i in range(n_items):
        if square:
            send_near(i, 1, low, 0).wait_recv()
            send_near(i, 2, high, 1).wait_recv()
            send_near(i, 1, high, 2).wait_recv()
            send_near(i, 2, low, 3).wait_recv()
        else:
            for k in range(1, chips):
                send_far(i, k).wait_recv()
        heard = 2 if square else chips - 1

        def target(plane, at, total):
            got_a[i][0, plane, at] = total.astype(got_a[i].dtype)

        terms = [lambda plane, at: got_a[i][0, plane, at]]
        for other in range(heard):
            terms.append(lambda plane, at, other=other: got_b[i][other, plane, at])
        add(i, n_dp, target, terms)
        for d in range(n_dp - 1, 0, -1):
            for way in (0, 1):
                plane = z - d if way else z + d
                arrives = z < n_dp - 1 if way else z > 0
                slot = n_dp - z + plane if way else plane - z

                @pl.when(plane >= 0 if way else plane < n_dp)
                def _():
                    @pl.when(arrives)
                    def _():
                        from_along(i, slot).wait_recv()
                        grow(i, 0, plane, 1, lambda unused, at: got_c[i][slot, at])

                    along(i, plane, way).start()

    for i in range(n_items):

        def own(unused, at, total):
            targets[i][at] = total

        add(i, 1, own, [lambda unused, at: got_a[i][0, z, at]])
        for slot, arrives in ((0, z > 0), (n_dp, z < n_dp - 1)):

            @pl.when(arrives)
            def _():
                from_along(i, slot).wait_recv()
                add(
                    i,
                    1,
                    own,
                    [lambda unused, at: targets[i][at], lambda unused, at: got_c[i][slot, at]],
                )

    for i in range(n_items):
        for k in range(chips):
            to_mate(i, k).wait_send()
        if square:
            for k, part in ((1, low), (2, high)):
                send_over(i, k, part).wait_send()
            for k, part, number in ((1, low, 0), (2, high, 1), (1, high, 2), (2, low, 3)):
                send_near(i, k, part, number).wait_send()
        else:
            for k in range(1, chips):
                send_far(i, k).wait_send()
        for plane in range(n_dp):

            @pl.when(z != plane)
            def _():
                remote(
                    got_a[i].at[0, plane],
                    got_c[i].at[0],
                    send_c.at[i, plane],
                    recv_c.at[i, 0],
                    mate,
                ).wait_send()

    for copy in copies + put:
        copy.wait()


def scatter_call(
    n_dp, n_expert, items, cut_in, cut_shapes, cuts, number, aliases, stages, puts=nothing
):
    chips = n_expert // 2
    square = chips == 4
    n, m = len(items), len(cut_shapes)
    dma = pltpu.SemaphoreType.DMA
    anywhere = pl.BlockSpec(memory_space=pl.ANY)
    blocks = [item.shape[2:] for item in items]
    kinds = sorted(set(blocks))
    rings = [kinds.index(block) for block in blocks]
    bf16 = jnp.bfloat16
    heard = 2 if square else chips - 1
    return pl.pallas_call(
        functools.partial(
            scatter_kernel, n_dp, n_expert, n, len(cut_in), m, cuts, puts, rings, len(kinds)
        ),
        out_shape=[*[jax.ShapeDtypeStruct(block, jnp.float32) for block in blocks], *cut_shapes],
        in_specs=[anywhere] * (n + len(cut_in)),
        out_specs=[pl.BlockSpec(memory_space=pltpu.VMEM)] * n + [anywhere] * m,
        scratch_shapes=[
            *[pltpu.VMEM((2, n_dp, *kind), bf16) for kind in kinds],
            *[pltpu.VMEM((chips, n_dp, *block), bf16) for block in blocks],
            *[pltpu.VMEM((heard, n_dp, *block), bf16) for block in blocks],
            *[pltpu.VMEM((n_dp + 1, *block), bf16) for block in blocks],
            *[pltpu.VMEM((2, n_dp // 2, *(block if square else (16, 128))), bf16) for block in blocks],
            dma((n, chips)),
            dma((n, chips)),
            dma((n, chips)),
            dma((n, chips)),
            dma((n, n_dp)),
            dma((n, n_dp + 1)),
            dma((n, 3)),
            dma((n, 3)),
            dma((len(kinds), 2)),
            dma((4, n_dp)),
            dma((4, n_dp)),
            dma((max(len(stages), 4), 2)),
            *[pltpu.VMEM(stage, jnp.bfloat16) for stage in stages],
        ],
        input_output_aliases=aliases,
        compiler_params=pltpu.CompilerParams(
            collective_id=number, has_side_effects=True, vmem_limit_bytes=62 * 1024 * 1024
        ),
    )(*items, *cut_in)


def scatter_all(
    n_dp, n_expert, items, cut_in, cut_shapes, cuts, number, aliases, stages, puts=nothing
):
    chips = n_expert // 2
    blocks = (2 * chips - 1 if chips != 4 else 7) * n_dp + n_dp + 3
    need = sum(blocks * item.shape[2] * item.shape[3] * 2 for item in items)
    kinds = {item.shape[2:] for item in items}
    need += sum(2 * n_dp * kind[0] * kind[1] * 2 for kind in kinds)
    need += sum(stage[0] * stage[1] * stage[2] * 2 for stage in stages)
    pieces = -(-need // (61 * 1024 * 1024))
    tiles = [item.shape[3] // 128 for item in items]
    results = [[] for item in items]
    extra = []
    for piece in range(pieces):
        ends = [(t * piece // pieces * 128, t * (piece + 1) // pieces * 128) for t in tiles]
        used = [i for i, (low, high) in enumerate(ends) if high > low]
        first = piece == 0
        outs = scatter_call(
            n_dp,
            n_expert,
            [items[i][..., ends[i][0] : ends[i][1]] if pieces > 1 else items[i] for i in used],
            cut_in if first else [],
            cut_shapes if first else [],
            cuts if first else nothing,
            number + piece,
            {len(used) + a: len(used) + b for a, b in aliases} if first else {},
            stages if first else [],
            puts if first else nothing,
        )
        for i, out in zip(used, outs):
            results[i].append(out)
        if first:
            extra = outs[len(used) :]
    return [one[0] if len(one) == 1 else jnp.concatenate(one, axis=1) for one in results], extra


def dot(left, right, dims):
    return lax.dot_general(
        left, right, ((dims[:1], dims[1:]), ((), ())), preferred_element_type=jnp.float32
    )


def picks(slots_ref, number):
    pair = slots_ref.shape[2]
    rows = lax.broadcasted_iota(jnp.int32, (2 * CAP, pair), 0)
    return [slots_ref[0, e : e + 1, :] == rows for e in range(number)]


def pick_kernel(number, experts_all, slots_ref, x_ref, g_ref, router_ref, rows_ref, grows_ref, gates_ref):
    chosen = picks(slots_ref, number)
    pick = jnp.concatenate(chosen, axis=0).astype(jnp.bfloat16)
    size = 2 * CAP
    x = x_ref[...]
    logits = dot(router_ref[...], x, (0, 1))
    names = lax.broadcasted_iota(jnp.int32, logits.shape, 0)
    logits = jnp.where(names < experts_all, logits, -1e30)
    weights = jnp.exp(logits - jnp.max(logits, axis=0, keepdims=True))
    probs = weights / jnp.sum(weights, axis=0, keepdims=True)
    for e in range(number):
        gate = jnp.sum(jnp.where(chosen[e], probs[e : e + 1, :], 0.0), axis=1, keepdims=True)
        gates_ref[e] = jnp.broadcast_to(gate, (size, 128))
    picked = dot(pick, x, (1, 0)).astype(jnp.bfloat16)
    for e in range(number):
        rows_ref[e] = picked[e * size : (e + 1) * size]
    picked = dot(pick, g_ref[...], (1, 0)).astype(jnp.bfloat16)
    for e in range(number):
        grows_ref[e] = picked[e * size : (e + 1) * size]


def expert_kernel(steps, half, n_weights, n_into, n_pack, names_ref, x_ref, g_ref, gates_ref, *refs):
    weights, refs = refs[:n_weights], refs[n_weights:]
    down_ref, refs = refs[0], refs[1 + n_into :]
    (
        y_ref,
        dx_ref,
        probs_ref,
        dgate_ref,
        dup_ref,
        ddown_ref,
        *pack_refs,
        sum_gate,
        sum_up,
    ) = refs
    bf16 = jnp.bfloat16
    g = g_ref[0]
    rows, width = x_ref.shape[1:]
    part = dgate_ref.shape[2]
    gate = gates_ref[0][:, :1]
    if n_weights == 2:
        piece = 512
        gate_ref, up_ref = weights
        gate_mid = dot(x_ref[0], gate_ref[0], (1, 0))
        up_mid = dot(x_ref[0], up_ref[0], (1, 0))
        spans = [
            (pl.ds(at, piece), gate_ref, up_ref, pl.ds(at, piece), pl.ds(0, part), pl.ds(0, part))
            for at in range(0, width, piece)
        ]
    else:
        piece = width // n_weights
        spans = []
        gate_mid = up_mid = 0.0
        for n, ref in enumerate(weights):
            span = pl.ds(pl.multiple_of(names_ref[1 + n], piece), piece)
            x_part = x_ref[0, :, span]
            gate_mid = gate_mid + dot(x_part, ref[0, :, :part], (1, 0))
            up_mid = up_mid + dot(x_part, ref[0, :, part:], (1, 0))
            spans.append((span, ref, ref, pl.ds(0, piece), pl.ds(0, part), pl.ds(part, part)))
    sigmoid = 1.0 / (1.0 + jnp.exp(-gate_mid))
    silu = gate_mid * sigmoid
    hidden = silu * up_mid
    hidden_low = hidden.astype(bf16)
    grad_plain = dot(g, down_ref[0], (1, 1))
    grad_gates = jnp.sum(grad_plain * hidden_low.astype(jnp.float32), axis=1, keepdims=True)
    high = grad_gates.astype(bf16).astype(jnp.float32)
    lane = lax.broadcasted_iota(jnp.int32, (rows, 128), 1)
    name = names_ref[0] + pl.program_id(0)
    probs_ref[0] = (
        jnp.where(lane == name, high, 0.0) + jnp.where(lane == name + half, grad_gates - high, 0.0)
    ).astype(bf16)
    grad_hidden = grad_plain * gate
    grad_gate = (
        grad_hidden * up_mid * sigmoid * (1.0 + gate_mid * (1.0 - sigmoid))
    ).astype(bf16)
    grad_up = (grad_hidden * silu).astype(bf16)
    scaled = (hidden * gate).astype(bf16)
    for at in range(0, width, piece):
        y_ref[0, :, at : at + piece] = (
            dot(hidden_low, down_ref[0, :, at : at + piece], (1, 0)) * gate
        ).astype(bf16)
    for span, gate_ref, up_ref, here, gate_columns, up_columns in spans:
        dx_ref[0, :, span] = (
            dot(grad_gate, gate_ref[0, here, gate_columns], (1, 1))
            + dot(grad_up, up_ref[0, here, up_columns], (1, 1))
        ).astype(bf16)
    step = pl.program_id(1)
    for span, *unused in spans:
        x_part = x_ref[0, :, span]
        here_gate = dot(x_part, grad_gate, (0, 0))
        here_up = dot(x_part, grad_up, (0, 0))
        here_down = dot(scaled, g_ref[0, :, span], (0, 0))
        if steps == 1:
            dgate_ref[0, span, :] = here_gate.astype(bf16)
            dup_ref[0, span, :] = here_up.astype(bf16)
            ddown_ref[0, :, span] = here_down
            continue

        @pl.when(step == 0)
        def _():
            sum_gate[span, :] = here_gate
            sum_up[span, :] = here_up
            ddown_ref[0, :, span] = here_down

        @pl.when(step > 0)
        def _():
            sum_gate[span, :] += here_gate
            sum_up[span, :] += here_up
            ddown_ref[0, :, span] += here_down

        @pl.when(step == steps - 1)
        def _():
            dgate_ref[0, span, :] = sum_gate[span, :].astype(bf16)
            dup_ref[0, span, :] = sum_up[span, :].astype(bf16)

    if n_pack:

        @pl.when((step == steps - 1) & (pl.program_id(0) < n_pack))
        def _():
            pack_ref = pack_refs[0]
            depth = pack_ref.shape[2]
            for plane in range(pack_ref.shape[0]):
                here = pl.ds(plane * depth, depth)
                pack_ref[plane, 0, :, :part] = dgate_ref[0, here, :]
                pack_ref[plane, 0, :, part:] = dup_ref[0, here, :]


def place_kernel(number, slots_ref, y_ref, dx_ref, probs_ref, out_ref, back_ref):
    pick = jnp.concatenate(picks(slots_ref, number), axis=0).astype(jnp.bfloat16)
    width = out_ref.shape[1]
    piece = 512
    flat = number * 2 * CAP
    for at in range(0, width, piece):
        part = y_ref[:, :, at : at + piece].reshape(flat, piece)
        out_ref[:, at : at + piece] = dot(pick, part, (0, 0)).astype(jnp.bfloat16)
        part = dx_ref[:, :, at : at + piece].reshape(flat, piece)
        back_ref[:, at : at + piece] = dot(pick, part, (0, 0)).astype(jnp.bfloat16)
    part = probs_ref[...].reshape(flat, 128)
    back_ref[:, width:] = dot(pick, part, (0, 0)).astype(jnp.bfloat16)


def pick_shapes(number, pairs):
    bf16 = jnp.bfloat16
    size = 2 * CAP
    return [
        jax.ShapeDtypeStruct((number, pairs * size, D), bf16),
        jax.ShapeDtypeStruct((number, pairs * size, D), bf16),
        jax.ShapeDtypeStruct((number, pairs * size, 128), jnp.float32),
    ]


def pick_rows(number, experts_all, slots, x_all, g_all, router, rows, grows, gates):
    pairs, _, pair = slots.shape
    size = 2 * CAP
    tokens = pl.BlockSpec((pair, D), lambda p: (p, 0))
    picked = pl.BlockSpec((number, size, D), lambda p: (0, p, 0))
    pltpu.emit_pipeline(
        functools.partial(pick_kernel, number, experts_all),
        grid=(pairs,),
        in_specs=[
            pl.BlockSpec((1, number, pair), lambda p: (p, 0, 0)),
            tokens,
            tokens,
            pl.BlockSpec(router.shape, lambda p: (0, 0)),
        ],
        out_specs=[picked, picked, pl.BlockSpec((number, size, 128), lambda p: (0, p, 0))],
    )(slots, x_all, g_all, router, rows, grows, gates)


def expert_call(names, half, low, number, rows, grows, gates, weights, down, into=(), pack=()):
    total, depth, _ = rows.shape
    part = down.shape[1]
    size = depth
    while size > 768:
        size //= 2
    steps = depth // size
    bf16 = jnp.bfloat16
    f32 = jnp.float32

    def from_rows(width):
        return pl.BlockSpec((1, size, width), lambda e, r: (e + low, r, 0))

    def whole(*shape):
        return pl.BlockSpec((1, *shape), lambda e, r: (e, 0, 0))

    def from_whole(*shape):
        return pl.BlockSpec((1, *shape), lambda e, r: (e + low, 0, 0))

    packed = [
        pl.BlockSpec(
            (planes, 1, D // planes, 2 * part),
            lambda e, r, n=n: (0, lax.min(e, n - 1), 0, 0),
        )
        for n, planes in ([pack] if pack else [])
    ]
    keep = (D, part) if steps > 1 else (16, 128)
    return pl.pallas_call(
        functools.partial(
            expert_kernel, steps, half, len(weights), len(into), pack[0] if pack else 0
        ),
        grid=(number, steps),
        in_specs=[
            pl.BlockSpec(memory_space=pltpu.SMEM),
            from_rows(D),
            from_rows(D),
            from_rows(128),
            *[(from_whole if len(weights) == 2 else whole)(*one.shape[1:]) for one in weights],
            from_whole(part, D),
            *[pl.BlockSpec(memory_space=pl.ANY)] * len(into),
        ],
        out_specs=[
            from_rows(D),
            from_rows(D),
            from_rows(128),
            whole(D, part),
            whole(D, part),
            from_whole(part, D),
            *packed,
        ],
        out_shape=[
            jax.ShapeDtypeStruct((total, depth, D), bf16),
            jax.ShapeDtypeStruct((total, depth, D), bf16),
            jax.ShapeDtypeStruct((total, depth, 128), bf16),
            jax.ShapeDtypeStruct((number, D, part), bf16),
            jax.ShapeDtypeStruct((number, D, part), bf16),
            jax.ShapeDtypeStruct((total, part, D), f32),
            *[
                jax.ShapeDtypeStruct((planes, n, D // planes, 2 * part), bf16)
                for n, planes in ([pack] if pack else [])
            ],
        ],
        input_output_aliases={
            5 + len(weights) + i: out for i, out in zip(range(len(into)), (0, 1, 2, 5))
        },
        scratch_shapes=[pltpu.VMEM(keep, f32), pltpu.VMEM(keep, f32)],
        compiler_params=pltpu.CompilerParams(vmem_limit_bytes=BIG),
    )(names, rows, grows, gates, *weights, down, *into)


def place_call(number, slots, y, dx, probs):
    pairs, _, pair = slots.shape
    bf16 = jnp.bfloat16
    size = 2 * CAP
    rows = pl.BlockSpec((number, size, D), lambda p: (0, p, 0))
    return pl.pallas_call(
        functools.partial(place_kernel, number),
        grid=(pairs,),
        in_specs=[
            pl.BlockSpec((1, number, pair), lambda p: (p, 0, 0)),
            rows,
            rows,
            pl.BlockSpec((number, size, 128), lambda p: (0, p, 0)),
        ],
        out_specs=[
            pl.BlockSpec((pair, D), lambda p: (p, 0)),
            pl.BlockSpec((pair, D + 128), lambda p: (p, 0)),
        ],
        out_shape=[
            jax.ShapeDtypeStruct((pairs * pair, D), bf16),
            jax.ShapeDtypeStruct((pairs * pair, D + 128), bf16),
        ],
        compiler_params=pltpu.CompilerParams(vmem_limit_bytes=BIG),
    )(slots, y, dx, probs)


def widen_kernel(*refs):
    half = len(refs) // 2
    for source, target in zip(refs[:half], refs[half:]):
        target[...] = source[...].astype(jnp.float32)


def widen(spans, values):
    number, rows, columns = values[0].shape
    (low, high), (again, end) = spans

    def chosen(e):
        return (jnp.where(e < high - low, e + low, e - (high - low) + again), 0, 0)

    block = pl.BlockSpec((1, rows, columns), chosen)
    return pl.pallas_call(
        widen_kernel,
        grid=(high - low + end - again,),
        in_specs=[block] * len(values),
        out_specs=[block] * len(values),
        out_shape=[jax.ShapeDtypeStruct(one.shape, jnp.float32) for one in values],
        compiler_params=pltpu.CompilerParams(vmem_limit_bytes=BIG),
    )(*values)


def widen_pieces_kernel(low, n_pieces, offsets_ref, *refs):
    pieces, refs = refs[:n_pieces], refs[n_pieces + 2 :]
    targets, wide, sems = refs[:2], refs[2], refs[3]
    part = wide.shape[4]
    copies = []
    for k, piece in enumerate(pieces):
        columns = pl.ds(pl.multiple_of(offsets_ref[k], part), part)
        for n in range(2):
            wide[k, n] = piece[:, :, n * part : (n + 1) * part].astype(jnp.float32)
            copy = pltpu.make_async_copy(
                wide.at[k, n], targets[n].at[pl.ds(low, piece.shape[0]), :, columns], sems.at[k, n]
            )
            copy.start()
            copies.append(copy)
    for copy in copies:
        copy.wait()


def widen_pieces(offsets, low, pieces, into):
    size, rows, columns = pieces[0].shape
    anywhere = pl.BlockSpec(memory_space=pl.ANY)
    count = len(pieces)
    return pl.pallas_call(
        functools.partial(widen_pieces_kernel, low, count),
        in_specs=[
            pl.BlockSpec(memory_space=pltpu.SMEM),
            *[pl.BlockSpec(memory_space=pltpu.VMEM)] * count,
            anywhere,
            anywhere,
        ],
        out_specs=[anywhere, anywhere],
        out_shape=[jax.ShapeDtypeStruct(one.shape, one.dtype) for one in into],
        scratch_shapes=[
            pltpu.VMEM((count, 2, size, rows, columns // 2), jnp.float32),
            pltpu.SemaphoreType.DMA((count, 2)),
        ],
        input_output_aliases={1 + count: 0, 2 + count: 1},
        compiler_params=pltpu.CompilerParams(vmem_limit_bytes=BIG),
    )(offsets, *pieces, *into)


def shards(
    n_dp,
    n_expert,
    tokens,
    cotangent,
    lengths,
    routes,
    w_query,
    w_key,
    w_value,
    w_out,
    w_router,
    gain_attn,
    gain_query,
    gain_key,
    gain_mlp,
    w_gate,
    w_up,
    w_down,
):
    groups = n_dp * n_expert
    bf16 = jnp.bfloat16
    number = w_gate.shape[0]
    ff = w_gate.shape[2]
    part = ff // n_dp
    experts_all = w_router.shape[1]
    width = 128
    small = jnp.concatenate(
        [
            w_router,
            gain_attn[:, None],
            gain_query[:, None],
            gain_key[:, None],
            gain_mlp[:, None],
            jnp.zeros((w_router.shape[0], width - experts_all - 4), bf16),
        ],
        axis=1,
    )
    hits = jnp.any(
        routes[:, :, None] == jnp.arange(width, dtype=jnp.int32)[None, None, :], axis=1
    ).astype(bf16)
    count = tokens.shape[0]
    rows_each = w_query.shape[0]
    extras = jnp.concatenate([hits, jnp.pad(small, ((0, count - rows_each), (0, 0)))], axis=1)
    weights = jnp.stack([w_query, w_key, w_value, w_out])
    depth = w_gate.shape[1]
    early = number // 4
    beside = early + number // 8
    late = number - number // 4
    back_beside = number // 8
    back_third = back_beside + number // 4
    back_late = back_third + number // 4
    me = lax.axis_index("dp")
    cut_shape = jax.ShapeDtypeStruct((number, n_dp * depth, part), bf16)

    def row_block(size):
        return lambda ref, block: ref.at[pl.ds(pl.multiple_of(block * size, 16), size)]

    def columns_at(at):
        return pl.ds(pl.multiple_of(at * part, part), part)

    def rows_at(at):
        return pl.ds(pl.multiple_of(at * depth, depth), depth)

    def recut(low, high):
        def cuts(ins, outs):
            def pair(n):
                chosen = pl.ds(low, high - low)
                return (
                    lambda to: ins[n].at[chosen, :, columns_at(to)],
                    lambda at: outs[n].at[chosen, rows_at(at)],
                )

            return [pair(0), pair(1)]

        return cuts

    to_plane, from_plane = partners(me, n_dp)

    def permuted(pieces, chained=False):
        got = []
        for k, piece in enumerate(pieces, 1):
            if chained and got:
                piece, last = lax.optimization_barrier((piece, got.pop()))
                got.append(last)
            paths = [(i, partners(i, n_dp)[0](k)) for i in range(n_dp)]
            got.append(lax.ppermute(piece, "dp", paths))
        return got

    def cut_pieces(low, high, first_k, ins, outs):
        to, unused = partners(lax.axis_index("dp"), n_dp)
        pairs = []
        for k, piece in enumerate(outs, first_k):
            for n in range(2):
                source = ins[n].at[pl.ds(low, high - low), :, columns_at(to(k))]
                pairs.append((source, piece.at[:, :, pl.ds(n * part, part)]))
        return pairs

    def piece_shapes(size, first_k):
        shape = jax.ShapeDtypeStruct((size, depth, 2 * part), bf16)
        return [shape] * (n_dp - first_k if size else 0)

    def stages(*sizes):
        return [(size, depth, part) for size in sizes]

    soon_shapes = piece_shapes(beside - early, 1)
    late_shapes = piece_shapes(number - late, 0)
    n_soon = len(soon_shapes)

    weights_all, extras_all, gate_early, up_early, *pieces = gather_call(
        n_dp,
        n_expert,
        [weights, extras],
        [
            jax.ShapeDtypeStruct((4, groups * rows_each, D), bf16),
            jax.ShapeDtypeStruct((groups * count, 2 * width), bf16),
        ],
        [
            lambda ref, block: ref.at[
                :, pl.ds(pl.multiple_of(block * rows_each, 16), rows_each)
            ],
            row_block(count),
        ],
        [w_gate, w_up],
        [cut_shape, cut_shape, *soon_shapes, *late_shapes],
        recut(0, early),
        {},
        0,
        stages(
            *[early] * 2,
            *[beside - early] * (2 * n_soon),
            *[number - late] * (2 * n_dp),
        ),
        lambda ins, outs: cut_pieces(early, beside, 1, ins, outs[2 : 2 + n_soon])
        + cut_pieces(late, number, 0, ins, outs[2 + n_soon :]),
    )
    soon_pieces, late_pieces = pieces[:n_soon], pieces[n_soon:]
    query_weight, key_weight, value_weight, out_weight = (weights_all[i] for i in range(4))
    small_all = (
        extras_all[:, width:].reshape(groups, count, width)[:, :rows_each].reshape(-1, width)
    )
    hits_all = extras_all[:, :experts_all]
    router_weight = small_all[:, :experts_all]
    gains = small_all[:, experts_all : experts_all + 4].astype(jnp.float32)
    attn_gain, query_gain, key_gain, mlp_gain = (gains[:, i] for i in range(4))
    inputs = tokens.astype(jnp.float32)
    segment, position, places = layout(lengths[0], count)
    half = HD // 2
    freq = 10000.0 ** (-2.0 * jnp.arange(half, dtype=jnp.float32) / HD)
    angle = position.astype(jnp.float32)[:, None] * freq[None, :]
    cosine = jnp.cos(angle)[:, None, :]
    sine = jnp.sin(angle)[:, None, :]
    scale = HD ** (-0.5)
    normed, attn_inverse = rms_forward(inputs, attn_gain)
    normed_low = normed.astype(bf16)
    query_raw = product(normed_low, query_weight, "td,de->te")
    key_raw = product(normed_low, key_weight, "td,de->te")
    value_low = product(normed_low, value_weight, "td,de->te").astype(bf16)
    query_normed, query_inverse = rms_forward(query_raw, query_gain)
    key_normed, key_inverse = rms_forward(key_raw, key_gain)
    query_low = rotate(query_normed, cosine, sine).astype(bf16).reshape(count, HEADS, HD)
    key_low = rotate(key_normed, cosine, sine).astype(bf16).reshape(count, HEADS, HD)
    value_heads = value_low.reshape(count, HEADS, HD)
    allowed = (segment[:, None] == segment[None, :]) & (places[None, :] <= places[:, None])
    scores = product(query_low, key_low, "qhd,khd->hqk") * scale
    scores = jnp.where(allowed[None], scores, -1e30)
    probs = jax.nn.softmax(scores, axis=-1)
    probs_low = probs.astype(bf16)
    attended_low = product(probs_low, value_heads, "hqk,khd->qhd").reshape(count, D).astype(bf16)
    middle = inputs + product(attended_low, out_weight, "td,de->te")
    mlp_normed, mlp_inverse = rms_forward(middle, mlp_gain)
    mlp_low = mlp_normed.astype(bf16)
    router = jax.nn.softmax(product(mlp_low, router_weight, "td,de->te"), axis=-1)

    first = lax.axis_index("expert") * number
    hit = lax.dynamic_slice_in_dim(hits_all, first, number, 1).reshape(groups, count, number)
    before = jnp.tril(jnp.ones((count, count), bf16), -1)
    slot = product(before, hit, "ts,bse->bet").astype(jnp.int32)
    slot = jnp.where(jnp.transpose(hit, (0, 2, 1)) > 0, slot, -1)
    slot = slot.reshape(groups // 2, 2, number, count)
    shift = jnp.array([0, CAP], jnp.int32)[None, :, None, None]
    slots = jnp.transpose(jnp.where(slot < 0, -1, slot + shift), (0, 2, 1, 3))
    slots = slots.reshape(groups // 2, number, 2 * count)
    router_own = jnp.pad(
        jnp.roll(router_weight, -first, axis=1), ((0, 0), (0, width - experts_all))
    )
    if n_soon:
        mlp_low, *soon_pieces = lax.optimization_barrier((mlp_low, *permuted(soon_pieces)))

    def put_weights(ins, outs):
        chosen = pl.ds(early, beside - early)
        unused, heard = partners(lax.axis_index("dp"), n_dp)
        pairs = []
        if beside > early:
            own = lax.axis_index("dp")
            for n in range(2):
                source = ins[n].at[chosen, :, columns_at(own)]
                pairs.append((source, outs[n].at[chosen, rows_at(own)]))
        for k, piece in enumerate(ins[6:], 1):
            for n in range(2):
                columns = piece.at[:, :, pl.ds(n * part, part)]
                pairs.append((columns, outs[n].at[chosen, rows_at(heard(k))]))
        return pairs

    def pick_all(items, ins, outs):
        pick_rows(number, experts_all, ins[4], *items, ins[5], *outs[2:])

    unused, unused, gate_cut, up_cut, rows, grows, gates = gather_call(
        n_dp,
        n_expert,
        [mlp_low, cotangent],
        [jax.ShapeDtypeStruct((groups * count, D), bf16)] * 2,
        [row_block(count)] * 2,
        [w_gate, w_up, gate_early, up_early, slots, router_own, *soon_pieces],
        [cut_shape, cut_shape, *pick_shapes(number, groups // 2)],
        recut(beside, late),
        {4: 2, 5: 3},
        1,
        stages(*[late - beside] * 2, *[beside - early] * (2 * n_dp if n_soon else 0)),
        put_weights,
        pick_all,
    )
    *late_pieces, rows = lax.optimization_barrier((*late_pieces, rows))
    late_pieces = [late_pieces[0], *permuted(late_pieces[1:])]
    packing = back_beside > 0 and depth == 512
    *outs, gate_soon, up_soon, down_soon = expert_call(
        first[None],
        experts_all,
        0,
        late,
        rows,
        grows,
        gates,
        [gate_cut, up_cut],
        w_down,
        pack=(back_beside, n_dp) if packing else (),
    )
    if packing:
        *outs, gate_soon, up_soon, down_soon, packed = [*outs, gate_soon, up_soon, down_soon]
    offsets = [from_plane(k) * depth for k in range(n_dp)]
    weighted, grad_rows, grad_gates, gate_rest, up_rest, grad_down_part = expert_call(
        jnp.stack([first + late, *offsets]),
        experts_all,
        late,
        number - late,
        rows,
        grows,
        gates,
        late_pieces,
        w_down,
        [*outs, down_soon],
    )
    part_out, part_back = place_call(number, slots, weighted, grad_rows, grad_gates)

    def ways(low, high, at, ins, outs):
        def pair(n):
            return (
                lambda to: ins[n].at[pl.ds(low, high - low), rows_at(to)],
                lambda here: outs[n].at[pl.ds(low + at, high - low), :, columns_at(here)],
            )

        return [pair(0), pair(1)]

    def cut_grads(low, high, ins, outs):
        to, unused = partners(lax.axis_index("dp"), n_dp)
        pairs = []
        for k, piece in enumerate(outs, 1):
            for n in range(2):
                source = ins[n].at[pl.ds(low, high - low), rows_at(to(k))]
                pairs.append((source, piece.at[:, :, pl.ds(n * part, part)]))
        return pairs

    pieces = []
    if back_beside:
        for k in range(1, n_dp):
            if packing:
                piece = lax.dynamic_index_in_dim(packed, to_plane(k), 0, False)
            else:
                piece = jnp.concatenate(
                    [
                        lax.dynamic_slice_in_dim(
                            one[:back_beside], to_plane(k) * depth, depth, 1
                        )
                        for one in (gate_soon, up_soon)
                    ],
                    axis=2,
                )
            pieces.append(piece)
        pieces = permuted(pieces)
    way_shapes = [jax.ShapeDtypeStruct((number, depth, ff), bf16)] * 2
    piece_shape = jax.ShapeDtypeStruct((back_late - back_third, depth, 2 * part), bf16)
    (back,), (gate_third, up_third, *later_pieces) = scatter_all(
        n_dp,
        n_expert,
        [part_back.reshape(n_dp, n_expert, count, D + width)],
        [gate_soon, up_soon],
        way_shapes + [piece_shape] * (n_dp - 1),
        lambda ins, outs: ways(back_beside, back_third, 0, ins, outs),
        8,
        (),
        stages(
            *[back_third - back_beside] * 2, *[back_late - back_third] * (2 * (n_dp - 1))
        ),
        lambda ins, outs: cut_grads(back_third, back_late, ins, outs[2:]),
    )
    later_pieces = permuted(later_pieces)

    def attention_back(back):
        grad_final = cotangent.astype(jnp.float32)
        grad_mlp = back[:, :D]
        grad_router_probs = back[:, D : D + experts_all] + back[:, D + experts_all :]
        grad_logits = router * (
            grad_router_probs - jnp.sum(router * grad_router_probs, axis=1, keepdims=True)
        )
        grad_logits_low = grad_logits.astype(bf16)
        grad_router_full = product(mlp_low, grad_logits_low, "td,te->de")
        grad_mlp = grad_mlp + product(grad_logits_low, router_weight, "te,de->td")
        grad_middle_part, grad_mlp_gain = rms_backward(middle, mlp_inverse, mlp_gain, grad_mlp)
        grad_middle = grad_final + grad_middle_part
        grad_branch_low = grad_middle.astype(bf16)
        grad_out_full = product(attended_low, grad_branch_low, "td,te->de")
        grad_attended = (
            product(grad_branch_low, out_weight, "te,de->td").astype(bf16).reshape(count, HEADS, HD)
        )
        grad_weights = product(grad_attended, value_heads, "qhd,khd->hqk")
        grad_scores = probs * (grad_weights - jnp.sum(probs * grad_weights, axis=-1, keepdims=True))
        grad_scores_low = grad_scores.astype(bf16)
        grad_query_turn = product(grad_scores_low, key_low, "hqk,khd->qhd").reshape(count, D) * scale
        grad_key_turn = product(grad_scores_low, query_low, "hqk,qhd->khd").reshape(count, D) * scale
        grad_value_low = (
            product(probs_low, grad_attended, "hqk,qhd->khd").reshape(count, D).astype(bf16)
        )
        grad_query_raw, grad_query_gain = rms_backward(
            query_raw, query_inverse, query_gain, rotate(grad_query_turn, cosine, -sine)
        )
        grad_key_raw, grad_key_gain = rms_backward(
            key_raw, key_inverse, key_gain, rotate(grad_key_turn, cosine, -sine)
        )
        grad_query_low = grad_query_raw.astype(bf16)
        grad_key_low = grad_key_raw.astype(bf16)
        grad_query_full = product(normed_low, grad_query_low, "td,te->de")
        grad_key_full = product(normed_low, grad_key_low, "td,te->de")
        grad_value_full = product(normed_low, grad_value_low, "td,te->de")
        grad_normed = (
            product(grad_query_low, query_weight, "te,de->td")
            + product(grad_key_low, key_weight, "te,de->td")
            + product(grad_value_low, value_weight, "te,de->td")
        )
        grad_inputs_part, grad_attn_gain = rms_backward(inputs, attn_inverse, attn_gain, grad_normed)
        grad_inputs = grad_middle + grad_inputs_part

        small_grads = jnp.concatenate(
            [
                grad_router_full,
                grad_attn_gain[:, None],
                grad_query_gain[:, None],
                grad_key_gain[:, None],
                grad_mlp_gain[:, None],
                jnp.zeros((D, width - experts_all - 4), jnp.float32),
            ],
            axis=1,
        )
        grads = (grad_out_full, grad_value_full, grad_key_full, grad_query_full, small_grads)
        return grad_inputs, *[one.astype(bf16) for one in grads]

    def unreached(back):
        shapes = [(count, D)] + [(D, D)] * 4 + [(D, width)]
        kinds = [jnp.float32] + [bf16] * 5
        return tuple(jnp.zeros(shape, kind) for shape, kind in zip(shapes, kinds))

    grad_inputs, *weight_grads = lax.cond(lengths[0, 0] > 0, attention_back, unreached, back)

    def blocks_of(value):
        return value.reshape(n_dp, n_expert, rows_each, -1)

    sums, (gate_back, up_back) = scatter_all(
        n_dp,
        n_expert,
        [blocks_of(value) for value in weight_grads]
        + [part_out.reshape(n_dp, n_expert, count, D)],
        [gate_third, up_third, gate_soon, up_soon, gate_rest, up_rest],
        way_shapes,
        lambda ins, outs: ways(back_late, late, 0, ins[2:4], outs)
        + ways(0, number - late, late, ins[4:6], outs),
        16,
        ((0, 0), (1, 1)),
        [],
    )
    grad_out_part, grad_value_part, grad_key_part, grad_query_part, small_part, summed = sums
    output = (middle + summed).astype(bf16)
    grad_router_part = small_part[:, :experts_all]
    gain_parts = [small_part[:, experts_all + i] for i in range(4)]
    widened = widen([(back_beside, back_third), (back_late, number)], [gate_back, up_back])
    offsets = jnp.stack([from_plane(k) * part for k in range(n_dp)])
    for low, high, others in (
        (0, back_beside, pieces),
        (back_third, back_late, later_pieces),
    ):
        if high > low:
            own = jnp.concatenate(
                [
                    lax.dynamic_slice_in_dim(one[low:high], me * depth, depth, 1)
                    for one in (gate_soon, up_soon)
                ],
                axis=2,
            )
            widened = widen_pieces(offsets, low, [own, *others], widened)
    grad_gate_part, grad_up_part = widened
    return (
        output,
        grad_inputs,
        grad_query_part,
        grad_key_part,
        grad_value_part,
        grad_out_part,
        grad_router_part,
        gain_parts[0],
        gain_parts[1],
        gain_parts[2],
        gain_parts[3],
        grad_gate_part,
        grad_up_part,
        grad_down_part,
    )


def solution(mesh):
    return jax.shard_map(
        functools.partial(shards, mesh.shape["dp"], mesh.shape["expert"]),
        mesh=mesh,
        in_specs=(
            P(("dp", "expert"), None),
            P(("dp", "expert"), None),
            P(("dp", "expert"), None),
            P(("dp", "expert"), None),
            P(("dp", "expert"), None),
            P(("dp", "expert"), None),
            P(("dp", "expert"), None),
            P(("dp", "expert"), None),
            P(("dp", "expert"), None),
            P(("dp", "expert")),
            P(("dp", "expert")),
            P(("dp", "expert")),
            P(("dp", "expert")),
            P("expert", "dp", None),
            P("expert", "dp", None),
            P("expert", "dp", None),
        ),
        out_specs=(
            P(("dp", "expert"), None),
            P(("dp", "expert"), None),
            P(("dp", "expert"), None),
            P(("dp", "expert"), None),
            P(("dp", "expert"), None),
            P(("dp", "expert"), None),
            P(("dp", "expert"), None),
            P(("dp", "expert")),
            P(("dp", "expert")),
            P(("dp", "expert")),
            P(("dp", "expert")),
            P("expert", "dp", None),
            P("expert", "dp", None),
            P("expert", "dp", None),
        ),
        check_vma=False,
    )
```

```python
import functools

import jax
import jax.numpy as jnp
from jax import lax
from jax.experimental import pallas as pl
from jax.experimental.pallas import tpu as pltpu
from jax.sharding import PartitionSpec as P

D = 2048
HEADS = 16
HD = 128
TOPK = 8
CAP = 24


eps = 1e-05


def product(left, right, form):
    return jnp.einsum(form, left, right, preferred_element_type=jnp.float32)


def rms_forward(values, gain):
    inverse = lax.rsqrt(jnp.mean(values * values, axis=-1, keepdims=True) + eps)
    return (values * inverse * gain, inverse)


def rms_backward(values, inverse, gain, grad):
    scaled = grad * gain
    inner = jnp.mean(scaled * values, axis=-1, keepdims=True)
    grad_values = inverse * scaled - values * (inverse * inverse * inverse) * inner
    grad_gain = jnp.sum(grad * values * inverse, axis=0)
    return (grad_values, grad_gain)


def layout(lengths_row, count):
    places = jnp.arange(count, dtype=jnp.int32)
    ends = jnp.cumsum(lengths_row, dtype=jnp.int32)
    passed = (places[:, None] >= ends[None, :]).astype(jnp.int32)
    segment = jnp.sum(passed, axis=1, dtype=jnp.int32)
    start = jnp.sum(passed * lengths_row[None, :], axis=1, dtype=jnp.int32)
    return (segment, places - start, places)


def rotate(values, cosine, sine):
    count = values.shape[0]
    heads = values.reshape(count, HEADS, HD)
    half = HD // 2
    first = heads[..., :half]
    second = heads[..., half:]
    turned = jnp.concatenate(
        [first * cosine - second * sine, second * cosine + first * sine], axis=-1
    )
    return turned.reshape(count, D)


MESH = pl.DeviceIdType.MESH
BIG = 60 * 1024 * 1024


def place_of():
    z = lax.axis_index("dp")
    j = lax.axis_index("expert")
    return z, j, j // 2, j % 2


def other_chips(chip, chips):
    if chips == 4:
        square = [chip, chip + 1 - 2 * (chip % 2), chip + 2 - 4 * (chip // 2), 3 - chip]
        return lambda k: square[k], lambda k: square[k]
    return lambda k: (chip + k) % chips, lambda k: (chip + chips - k) % chips


def partners(z, n_dp):
    if n_dp == 4:
        pairs = [z, (z + 2) % 4, 3 - z, z + 1 - 2 * (z % 2)]
        return lambda k: pairs[k], lambda k: pairs[k]
    return lambda k: (z + k) % n_dp, lambda k: (z + n_dp - k) % n_dp


def greet(n_dp, n_expert):
    z, j, chip, core = place_of()
    chips = n_expert // 2
    barrier = pltpu.get_barrier_semaphore()
    for k in range(1, n_dp):
        pl.semaphore_signal(
            barrier, inc=1, device_id=((z + k) % n_dp, j), device_id_type=MESH
        )
    for k in range(1, chips):
        other = ((chip + k) % chips) * 2 + core
        pl.semaphore_signal(barrier, inc=1, device_id=(z, other), device_id_type=MESH)
    pl.semaphore_signal(
        barrier, inc=1, device_id=(z, chip * 2 + 1 - core), device_id_type=MESH
    )
    pl.semaphore_wait(barrier, n_dp - 1 + chips - 1 + 1)


def remote(source, target, send, receive, device):
    return pltpu.make_async_remote_copy(
        src_ref=source,
        dst_ref=target,
        send_sem=send,
        recv_sem=receive,
        device_id=device,
        device_id_type=MESH,
    )


def exchange(n_dp, pairs, send, receive):
    z, j, chip, core = place_of()
    to_plane, unused = partners(z, n_dp)
    copies = []
    for i, (source, target) in enumerate(pairs):
        for k in range(1, n_dp):
            to = to_plane(k)
            copies.append(
                remote(source(to), target(z), send.at[i, k], receive.at[i, k], (to, j))
            )
    return copies


def moves(pairs, stages, local):
    if not stages:
        copies = [
            pltpu.make_async_copy(source, target, local.at[i, 0])
            for i, (source, target) in enumerate(pairs)
        ]
        for copy in copies:
            copy.start()
        return [], copies
    bring = [
        pltpu.make_async_copy(source, stages[i], local.at[i, 0])
        for i, (source, target) in enumerate(pairs)
    ]
    put = [
        pltpu.make_async_copy(stages[i], target, local.at[i, 1])
        for i, (source, target) in enumerate(pairs)
    ]
    return bring, put


def nothing(ins, outs):
    return []


def gather_kernel(
    n_dp, n_expert, n_items, places, cuts, puts, finish, n_cut, n_out, n_stages, *refs
):
    z, j, chip, core = place_of()
    chips = n_expert // 2
    square = chips == 4
    to_chip, from_chip = other_chips(chip, chips)
    sources = refs[:n_items]
    cut_in = refs[n_items : n_items + n_cut]
    at = n_items + n_cut
    targets = refs[at : at + n_items]
    cut_out = refs[at + n_items : at + n_items + n_out]
    (
        send_c,
        recv_c,
        send_b,
        recv_b,
        send_a,
        recv_a,
        local,
        send_x,
        recv_x,
        local_y,
        *stages,
    ) = refs[at + n_items + n_out :]
    greet(n_dp, n_expert)
    mate = (z, chip * 2 + 1 - core)
    near = (1, 2) if square else tuple(range(1, chips))

    def slot(i, plane, column):
        return places[i](targets[i], plane * n_expert + column)

    def pass_on(i, plane, source, column, k, chip_to):
        return remote(
            source,
            slot(i, plane, column),
            send_b.at[i, plane, k],
            recv_b.at[i, plane, k],
            (z, chip_to * 2 + core),
        )

    def hand(i, plane, source):
        for k in near:
            pass_on(i, plane, source, j, k, to_chip(k)).start()
        remote(
            source, slot(i, plane, j), send_a.at[i, plane, 0], recv_a.at[i, plane, 0], mate
        ).start()

    def along(i, plane, source, way, step):
        return remote(
            source, slot(i, plane, j), send_c.at[i, way, plane], recv_c.at[i, plane], (z + step, j)
        )

    def at_distance(d, body):
        if d == 0:
            body(z, 0)
            return

        @pl.when(z >= d)
        def _():
            body(z - d, 0)

        @pl.when(z + d < n_dp)
        def _():
            body(z + d, 1)

    for i in range(n_items):

        @pl.when(z < n_dp - 1)
        def _():
            along(i, z, sources[i], 0, 1).start()

        @pl.when(z > 0)
        def _():
            along(i, z, sources[i], 1, -1).start()

        hand(i, z, sources[i])
        pltpu.make_async_copy(sources[i], slot(i, z, j), local.at[i]).start()

    def relay(plane, way):
        step = -1 if way else 1
        for i in range(n_items):
            block = slot(i, plane, j)
            along(i, plane, block, way, step).wait_recv()

            @pl.when(z > 0 if way else z < n_dp - 1)
            def _():
                along(i, plane, block, way, step).start()

            hand(i, plane, block)

    for d in range(1, n_dp):
        at_distance(d, relay)
    pairs = cuts(cut_in, cut_out)
    copies = exchange(n_dp, pairs, send_x, recv_x)
    for copy in copies:
        copy.start()
    own = [(source(z), target(z)) for source, target in pairs]
    bring, put = moves(own + puts(cut_in, cut_out), stages, local_y)
    for copy in bring:
        copy.start()
    for one, other in zip(bring, put):
        one.wait()
        other.start()

    def arrive(i, plane, k):
        column = from_chip(k) * 2 + core
        block = slot(i, plane, column)
        pass_on(i, plane, block, column, k, chip).wait_recv()
        remote(block, block, send_a.at[i, plane, k], recv_a.at[i, plane, k], mate).start()
        return block, column

    def arrived(plane, way):
        for i in range(n_items):
            for k in near:
                block, column = arrive(i, plane, k)
                if square:

                    @pl.when(plane % 2 == k - 1)
                    def _():
                        pass_on(i, plane, block, column, 3, to_chip(3 - k)).start()

    def crossed(plane, way):
        for i in range(n_items):
            arrive(i, plane, 3)

    for d in range(n_dp):
        at_distance(d, arrived)
    if square:
        for d in range(n_dp):
            at_distance(d, crossed)

    for i in range(n_items):
        for plane in range(n_dp):
            for k in range(chips):
                column = (from_chip(k) if k else chip) * 2 + 1 - core
                block = slot(i, plane, column)
                remote(
                    block, block, send_a.at[i, plane, k], recv_a.at[i, plane, k], mate
                ).wait_recv()
        pltpu.make_async_copy(sources[i], slot(i, z, j), local.at[i]).wait()
    finish(targets, cut_in, cut_out)
    for i in range(n_items):
        for plane in range(n_dp):
            block = slot(i, plane, j)
            for k in range(1, chips):
                pass_on(i, plane, block, j, k, chip).wait_send()
            for k in range(chips):
                remote(
                    block, block, send_a.at[i, plane, k], recv_a.at[i, plane, k], mate
                ).wait_send()

            @pl.when((z < n_dp - 1) & (z >= plane))
            def _():
                along(i, plane, block, 0, 1).wait_send()

            @pl.when((z > 0) & (z <= plane))
            def _():
                along(i, plane, block, 1, -1).wait_send()

    for copy in copies + put:
        copy.wait()


def gather_call(
    n_dp,
    n_expert,
    items,
    shapes,
    places,
    cut_in,
    cut_shapes,
    cuts,
    aliases,
    number,
    stages,
    puts=nothing,
    finish=lambda items, ins, outs: None,
):
    chips = n_expert // 2
    n, m = len(items), len(cut_shapes)
    dma = pltpu.SemaphoreType.DMA
    anywhere = pl.BlockSpec(memory_space=pl.ANY)
    return pl.pallas_call(
        functools.partial(
            gather_kernel,
            n_dp,
            n_expert,
            n,
            places,
            cuts,
            puts,
            finish,
            len(cut_in),
            m,
            len(stages),
        ),
        out_shape=[*shapes, *cut_shapes],
        in_specs=[anywhere] * (n + len(cut_in)),
        out_specs=[anywhere] * (n + m),
        scratch_shapes=[
            dma((n, 2, n_dp)),
            dma((n, n_dp)),
            dma((n, n_dp, chips)),
            dma((n, n_dp, chips)),
            dma((n, n_dp, chips)),
            dma((n, n_dp, chips)),
            dma((n,)),
            dma((4, n_dp)),
            dma((4, n_dp)),
            dma((max(len(stages), 4), 2)),
            *[pltpu.VMEM(stage, jnp.bfloat16) for stage in stages],
        ],
        input_output_aliases=aliases,
        compiler_params=pltpu.CompilerParams(
            collective_id=number, has_side_effects=True, vmem_limit_bytes=BIG
        ),
    )(*items, *cut_in)


def scatter_kernel(
    n_dp, n_expert, n_items, n_cut, n_out, cuts, puts, middle, rings, n_rings, *refs
):
    z, j, chip, core = place_of()
    chips = n_expert // 2
    square = chips == 4
    to_chip, from_chip = other_chips(chip, chips)
    refs = list(refs)

    def take(count):
        taken = refs[:count]
        del refs[:count]
        return taken

    sources, cut_in, targets, cut_out = take(n_items), take(n_cut), take(n_items), take(n_out)
    ring, got_a, got_b, got_c = take(n_rings), take(n_items), take(n_items), take(n_items)
    transit = take(n_items)
    (
        send_a,
        recv_a,
        send_b,
        recv_b,
        send_c,
        recv_c,
        send_t,
        recv_t,
        local,
        send_x,
        recv_x,
        local_y,
        *stages,
    ) = refs
    greet(n_dp, n_expert)
    mate = (z, chip * 2 + 1 - core)
    order = [3, 1, 2, 0] if square else [*range(1, chips), 0]
    half = n_dp // 2
    low, high = pl.ds(0, half), pl.ds(half, n_dp - half)

    def chip_of(k):
        return to_chip(k) if k else chip

    def to_mate(i, k):
        return remote(
            sources[i].at[:, chip_of(k) * 2 + 1 - core],
            got_a[i].at[k],
            send_a.at[i, k],
            recv_a.at[i, k],
            mate,
        )

    turn = [0] * n_rings
    loads = []
    for i in range(n_items):
        for k in order:
            loads.append((i, k, turn[rings[i]] % 2))
            turn[rings[i]] += 1

    def load(i, k, at):
        return pltpu.make_async_copy(
            sources[i].at[:, chip_of(k) * 2 + core], ring[rings[i]].at[at], local.at[rings[i], at]
        )

    def send_near(i, k, part, number):
        return remote(
            got_a[i].at[k, part],
            got_b[i].at[k - 1, part],
            send_b.at[i, number],
            recv_b.at[i, number],
            (z, to_chip(k) * 2 + core),
        )

    def send_over(i, k, part):
        return remote(
            got_a[i].at[3, part],
            transit[i].at[k - 1],
            send_t.at[i, k],
            recv_t.at[i, k],
            (z, to_chip(k) * 2 + core),
        )

    def send_far(i, k):
        return remote(
            got_a[i].at[k],
            got_b[i].at[k - 1],
            send_b.at[i, k],
            recv_b.at[i, k],
            (z, to_chip(k) * 2 + core),
        )

    def along(i, plane, way):
        slot = n_dp - (z - 1) + plane if way else plane - (z + 1)
        return remote(
            got_a[i].at[0, plane],
            got_c[i].at[slot],
            send_c.at[i, plane],
            recv_c.at[i, slot],
            (z - 1 if way else z + 1, j),
        )

    def from_along(i, slot):
        return remote(
            got_c[i].at[slot], got_c[i].at[slot], send_c.at[i, 0], recv_c.at[i, slot], mate
        )

    f32 = jnp.float32

    def add(i, planes, target, terms):
        rows = got_a[i].shape[2]
        per = rows // 16

        def step(n, unused):
            plane = n // per
            at = pl.ds(pl.multiple_of((n % per) * 16, 16), 16)
            total = terms[0](plane, at).astype(f32)
            for term in terms[1:]:
                total = total + term(plane, at).astype(f32)
            target(plane, at, total)
            return unused

        lax.fori_loop(0, planes * per, step, 0)

    def grow(i, k, first, planes, term):
        def target(plane, at, total):
            got_a[i][k, plane + first, at] = total.astype(got_a[i].dtype)

        add(i, planes, target, [lambda plane, at: got_a[i][k, plane + first, at], term])

    for i in range(n_items):
        for k in order:
            to_mate(i, k).start()
    started = 0
    ahead = [0] * n_rings
    for i, k, at in loads:
        if ahead[rings[i]] < 2:
            load(i, k, at).start()
            ahead[rings[i]] += 1
    pairs = cuts(cut_in, cut_out)
    copies = exchange(n_dp, pairs, send_x, recv_x)
    for copy in copies:
        copy.start()
    own = [(source(z), target(z)) for source, target in pairs]
    bring, put = moves(own + puts(cut_in, cut_out), stages, local_y)
    for copy in bring:
        copy.start()

    for n, (i, k, at) in enumerate(loads):
        load(i, k, at).wait()
        to_mate(i, k).wait_recv()
        grow(i, k, 0, n_dp, lambda plane, rows: ring[rings[i]][at, plane, rows])
        later = [one for one in loads[n + 1 :] if rings[one[0]] == rings[i]]
        if len(later) >= 2:
            load(*later[1]).start()
        if not k:
            continue
        if not square:
            send_far(i, k).start()
        elif k == 3:
            send_over(i, 1, low).start()
            send_over(i, 2, high).start()
        elif k == 1:
            send_near(i, 1, low, 0).start()
        else:
            send_near(i, 2, high, 1).start()
    for one, other in zip(bring, put):
        one.wait()
        other.start()
    middle(cut_in, cut_out)
    if square:
        for i in range(n_items):
            send_over(i, 2, high).wait_recv()
            grow(i, 1, half, n_dp - half, lambda plane, rows: transit[i][1, plane, rows])
            send_near(i, 1, high, 2).start()
            send_over(i, 1, low).wait_recv()
            grow(i, 2, 0, half, lambda plane, rows: transit[i][0, plane, rows])
            send_near(i, 2, low, 3).start()
    for i in range(n_items):
        if square:
            send_near(i, 1, low, 0).wait_recv()
            send_near(i, 2, high, 1).wait_recv()
            send_near(i, 1, high, 2).wait_recv()
            send_near(i, 2, low, 3).wait_recv()
        else:
            for k in range(1, chips):
                send_far(i, k).wait_recv()
        heard = 2 if square else chips - 1

        def target(plane, at, total):
            got_a[i][0, plane, at] = total.astype(got_a[i].dtype)

        terms = [lambda plane, at: got_a[i][0, plane, at]]
        for other in range(heard):
            terms.append(lambda plane, at, other=other: got_b[i][other, plane, at])
        add(i, n_dp, target, terms)
        for d in range(n_dp - 1, 0, -1):
            for way in (0, 1):
                plane = z - d if way else z + d
                arrives = z < n_dp - 1 if way else z > 0
                slot = n_dp - z + plane if way else plane - z

                @pl.when(plane >= 0 if way else plane < n_dp)
                def _():
                    @pl.when(arrives)
                    def _():
                        from_along(i, slot).wait_recv()
                        grow(i, 0, plane, 1, lambda unused, at: got_c[i][slot, at])

                    along(i, plane, way).start()

    for i in range(n_items):

        def own(unused, at, total):
            targets[i][at] = total

        add(i, 1, own, [lambda unused, at: got_a[i][0, z, at]])
        for slot, arrives in ((0, z > 0), (n_dp, z < n_dp - 1)):

            @pl.when(arrives)
            def _():
                from_along(i, slot).wait_recv()
                add(
                    i,
                    1,
                    own,
                    [lambda unused, at: targets[i][at], lambda unused, at: got_c[i][slot, at]],
                )

    for i in range(n_items):
        for k in range(chips):
            to_mate(i, k).wait_send()
        if square:
            for k, part in ((1, low), (2, high)):
                send_over(i, k, part).wait_send()
            for k, part, number in ((1, low, 0), (2, high, 1), (1, high, 2), (2, low, 3)):
                send_near(i, k, part, number).wait_send()
        else:
            for k in range(1, chips):
                send_far(i, k).wait_send()
        for plane in range(n_dp):

            @pl.when(z != plane)
            def _():
                remote(
                    got_a[i].at[0, plane],
                    got_c[i].at[0],
                    send_c.at[i, plane],
                    recv_c.at[i, 0],
                    mate,
                ).wait_send()

    for copy in copies + put:
        copy.wait()


def scatter_call(
    n_dp,
    n_expert,
    items,
    cut_in,
    cut_shapes,
    cuts,
    number,
    aliases,
    stages,
    puts=nothing,
    middle=nothing,
):
    chips = n_expert // 2
    square = chips == 4
    n, m = len(items), len(cut_shapes)
    dma = pltpu.SemaphoreType.DMA
    anywhere = pl.BlockSpec(memory_space=pl.ANY)
    blocks = [item.shape[2:] for item in items]
    kinds = sorted(set(blocks))
    rings = [kinds.index(block) for block in blocks]
    bf16 = jnp.bfloat16
    heard = 2 if square else chips - 1
    return pl.pallas_call(
        functools.partial(
            scatter_kernel,
            n_dp,
            n_expert,
            n,
            len(cut_in),
            m,
            cuts,
            puts,
            middle,
            rings,
            len(kinds),
        ),
        out_shape=[*[jax.ShapeDtypeStruct(block, jnp.float32) for block in blocks], *cut_shapes],
        in_specs=[anywhere] * (n + len(cut_in)),
        out_specs=[pl.BlockSpec(memory_space=pltpu.VMEM)] * n + [anywhere] * m,
        scratch_shapes=[
            *[pltpu.VMEM((2, n_dp, *kind), bf16) for kind in kinds],
            *[pltpu.VMEM((chips, n_dp, *block), bf16) for block in blocks],
            *[pltpu.VMEM((heard, n_dp, *block), bf16) for block in blocks],
            *[pltpu.VMEM((n_dp + 1, *block), bf16) for block in blocks],
            *[pltpu.VMEM((2, n_dp // 2, *(block if square else (16, 128))), bf16) for block in blocks],
            dma((n, chips)),
            dma((n, chips)),
            dma((n, chips)),
            dma((n, chips)),
            dma((n, n_dp)),
            dma((n, n_dp + 1)),
            dma((n, 3)),
            dma((n, 3)),
            dma((len(kinds), 2)),
            dma((4, n_dp)),
            dma((4, n_dp)),
            dma((max(len(stages), 4), 2)),
            *[pltpu.VMEM(stage, jnp.bfloat16) for stage in stages],
        ],
        input_output_aliases=aliases,
        compiler_params=pltpu.CompilerParams(
            collective_id=number, has_side_effects=True, vmem_limit_bytes=62 * 1024 * 1024
        ),
    )(*items, *cut_in)


def scatter_all(
    n_dp,
    n_expert,
    items,
    cut_in,
    cut_shapes,
    cuts,
    number,
    aliases,
    stages,
    puts=nothing,
    middle=nothing,
):
    chips = n_expert // 2
    blocks = (2 * chips - 1 if chips != 4 else 7) * n_dp + n_dp + 3
    need = sum(blocks * item.shape[2] * item.shape[3] * 2 for item in items)
    kinds = {item.shape[2:] for item in items}
    need += sum(2 * n_dp * kind[0] * kind[1] * 2 for kind in kinds)
    need += sum(stage[0] * stage[1] * stage[2] * 2 for stage in stages)
    pieces = -(-need // (61 * 1024 * 1024))
    tiles = [item.shape[3] // 128 for item in items]
    results = [[] for item in items]
    extra = []
    for piece in range(pieces):
        ends = [(t * piece // pieces * 128, t * (piece + 1) // pieces * 128) for t in tiles]
        used = [i for i, (low, high) in enumerate(ends) if high > low]
        first = piece == 0
        outs = scatter_call(
            n_dp,
            n_expert,
            [items[i][..., ends[i][0] : ends[i][1]] if pieces > 1 else items[i] for i in used],
            cut_in if first else [],
            cut_shapes if first else [],
            cuts if first else nothing,
            number + piece,
            {len(used) + a: len(used) + b for a, b in aliases} if first else {},
            stages if first else [],
            puts if first else nothing,
            middle if first else nothing,
        )
        for i, out in zip(used, outs):
            results[i].append(out)
        if first:
            extra = outs[len(used) :]
    return [one[0] if len(one) == 1 else jnp.concatenate(one, axis=1) for one in results], extra


def dot(left, right, dims):
    return lax.dot_general(
        left, right, ((dims[:1], dims[1:]), ((), ())), preferred_element_type=jnp.float32
    )


def picks(slots_ref, number):
    pair = slots_ref.shape[2]
    rows = lax.broadcasted_iota(jnp.int32, (2 * CAP, pair), 0)
    return [slots_ref[0, e : e + 1, :] == rows for e in range(number)]


def pick_kernel(number, experts_all, slots_ref, x_ref, g_ref, router_ref, rows_ref, grows_ref, gates_ref):
    chosen = picks(slots_ref, number)
    pick = jnp.concatenate(chosen, axis=0).astype(jnp.bfloat16)
    size = 2 * CAP
    x = x_ref[...]
    logits = dot(router_ref[...], x, (0, 1))
    names = lax.broadcasted_iota(jnp.int32, logits.shape, 0)
    logits = jnp.where(names < experts_all, logits, -1e30)
    weights = jnp.exp(logits - jnp.max(logits, axis=0, keepdims=True))
    probs = weights / jnp.sum(weights, axis=0, keepdims=True)
    for e in range(number):
        gate = jnp.sum(jnp.where(chosen[e], probs[e : e + 1, :], 0.0), axis=1, keepdims=True)
        gates_ref[e] = jnp.broadcast_to(gate, (size, 128))
    picked = dot(pick, x, (1, 0)).astype(jnp.bfloat16)
    for e in range(number):
        rows_ref[e] = picked[e * size : (e + 1) * size]
    picked = dot(pick, g_ref[...], (1, 0)).astype(jnp.bfloat16)
    for e in range(number):
        grows_ref[e] = picked[e * size : (e + 1) * size]


def expert_kernel(steps, half, n_weights, n_into, n_pack, names_ref, x_ref, g_ref, gates_ref, *refs):
    weights, refs = refs[:n_weights], refs[n_weights:]
    down_ref, refs = refs[0], refs[1 + n_into :]
    (
        y_ref,
        dx_ref,
        probs_ref,
        dgate_ref,
        dup_ref,
        ddown_ref,
        *pack_refs,
        sum_gate,
        sum_up,
    ) = refs
    bf16 = jnp.bfloat16
    g = g_ref[0]
    rows, width = x_ref.shape[1:]
    part = dgate_ref.shape[2]
    gate = gates_ref[0][:, :1]
    if n_weights == 2:
        piece = 512
        gate_ref, up_ref = weights
        gate_mid = dot(x_ref[0], gate_ref[0], (1, 0))
        up_mid = dot(x_ref[0], up_ref[0], (1, 0))
        spans = [
            (pl.ds(at, piece), gate_ref, up_ref, pl.ds(at, piece), pl.ds(0, part), pl.ds(0, part))
            for at in range(0, width, piece)
        ]
    else:
        piece = width // n_weights
        spans = []
        gate_mid = up_mid = 0.0
        for n, ref in enumerate(weights):
            span = pl.ds(pl.multiple_of(names_ref[1 + n], piece), piece)
            x_part = x_ref[0, :, span]
            gate_mid = gate_mid + dot(x_part, ref[0, :, :part], (1, 0))
            up_mid = up_mid + dot(x_part, ref[0, :, part:], (1, 0))
            spans.append((span, ref, ref, pl.ds(0, piece), pl.ds(0, part), pl.ds(part, part)))
    sigmoid = 1.0 / (1.0 + jnp.exp(-gate_mid))
    silu = gate_mid * sigmoid
    hidden = silu * up_mid
    hidden_low = hidden.astype(bf16)
    grad_plain = dot(g, down_ref[0], (1, 1))
    grad_gates = jnp.sum(grad_plain * hidden_low.astype(jnp.float32), axis=1, keepdims=True)
    high = grad_gates.astype(bf16).astype(jnp.float32)
    lane = lax.broadcasted_iota(jnp.int32, (rows, 128), 1)
    name = names_ref[0] + pl.program_id(0)
    probs_ref[0] = (
        jnp.where(lane == name, high, 0.0) + jnp.where(lane == name + half, grad_gates - high, 0.0)
    ).astype(bf16)
    grad_hidden = grad_plain * gate
    grad_gate = (
        grad_hidden * up_mid * sigmoid * (1.0 + gate_mid * (1.0 - sigmoid))
    ).astype(bf16)
    grad_up = (grad_hidden * silu).astype(bf16)
    scaled = (hidden * gate).astype(bf16)
    for at in range(0, width, piece):
        y_ref[0, :, at : at + piece] = (
            dot(hidden_low, down_ref[0, :, at : at + piece], (1, 0)) * gate
        ).astype(bf16)
    for span, gate_ref, up_ref, here, gate_columns, up_columns in spans:
        dx_ref[0, :, span] = (
            dot(grad_gate, gate_ref[0, here, gate_columns], (1, 1))
            + dot(grad_up, up_ref[0, here, up_columns], (1, 1))
        ).astype(bf16)
    step = pl.program_id(1)
    for span, *unused in spans:
        x_part = x_ref[0, :, span]
        here_gate = dot(x_part, grad_gate, (0, 0))
        here_up = dot(x_part, grad_up, (0, 0))
        here_down = dot(scaled, g_ref[0, :, span], (0, 0))
        if steps == 1:
            dgate_ref[0, span, :] = here_gate.astype(bf16)
            dup_ref[0, span, :] = here_up.astype(bf16)
            ddown_ref[0, :, span] = here_down
            continue

        @pl.when(step == 0)
        def _():
            sum_gate[span, :] = here_gate
            sum_up[span, :] = here_up
            ddown_ref[0, :, span] = here_down

        @pl.when(step > 0)
        def _():
            sum_gate[span, :] += here_gate
            sum_up[span, :] += here_up
            ddown_ref[0, :, span] += here_down

        @pl.when(step == steps - 1)
        def _():
            dgate_ref[0, span, :] = sum_gate[span, :].astype(bf16)
            dup_ref[0, span, :] = sum_up[span, :].astype(bf16)

    if n_pack:

        @pl.when((step == steps - 1) & (pl.program_id(0) < n_pack))
        def _():
            pack_ref = pack_refs[0]
            depth = pack_ref.shape[2]
            for plane in range(pack_ref.shape[0]):
                here = pl.ds(plane * depth, depth)
                pack_ref[plane, 0, :, :part] = dgate_ref[0, here, :]
                pack_ref[plane, 0, :, part:] = dup_ref[0, here, :]


def put_back(number, slots_ref, pairs):
    pick = jnp.concatenate(picks(slots_ref, number), axis=0).astype(jnp.bfloat16)
    piece = 512
    for source, target, first in pairs:
        width = source.shape[2]
        for at in range(0, width, piece):
            size = min(piece, width)
            part = source[:, :, at : at + size].reshape(-1, size)
            target[:, first + at : first + at + size] = dot(pick, part, (0, 0)).astype(
                jnp.bfloat16
            )


def place_back_kernel(number, slots_ref, dx_ref, probs_ref, back_ref):
    put_back(number, slots_ref, [(dx_ref, back_ref, 0), (probs_ref, back_ref, dx_ref.shape[2])])


def place_out_kernel(number, slots_ref, y_ref, out_ref):
    put_back(number, slots_ref, [(y_ref, out_ref, 0)])


def place_out(slots, y, out):
    pairs, number, pair = slots.shape
    pltpu.emit_pipeline(
        functools.partial(place_out_kernel, number),
        grid=(pairs,),
        in_specs=[
            pl.BlockSpec((1, number, pair), lambda p: (p, 0, 0)),
            pl.BlockSpec((number, 2 * CAP, D), lambda p: (0, p, 0)),
        ],
        out_specs=[pl.BlockSpec((pair, D), lambda p: (p, 0))],
    )(slots, y, out)


def pick_shapes(number, pairs):
    bf16 = jnp.bfloat16
    size = 2 * CAP
    return [
        jax.ShapeDtypeStruct((number, pairs * size, D), bf16),
        jax.ShapeDtypeStruct((number, pairs * size, D), bf16),
        jax.ShapeDtypeStruct((number, pairs * size, 128), jnp.float32),
    ]


def pick_rows(number, experts_all, slots, x_all, g_all, router, rows, grows, gates):
    pairs, _, pair = slots.shape
    size = 2 * CAP
    tokens = pl.BlockSpec((pair, D), lambda p: (p, 0))
    picked = pl.BlockSpec((number, size, D), lambda p: (0, p, 0))
    pltpu.emit_pipeline(
        functools.partial(pick_kernel, number, experts_all),
        grid=(pairs,),
        in_specs=[
            pl.BlockSpec((1, number, pair), lambda p: (p, 0, 0)),
            tokens,
            tokens,
            pl.BlockSpec(router.shape, lambda p: (0, 0)),
        ],
        out_specs=[picked, picked, pl.BlockSpec((number, size, 128), lambda p: (0, p, 0))],
    )(slots, x_all, g_all, router, rows, grows, gates)


def expert_call(names, half, low, number, rows, grows, gates, weights, down, into=(), pack=()):
    total, depth, _ = rows.shape
    part = down.shape[1]
    size = depth
    while size > 768:
        size //= 2
    steps = depth // size
    bf16 = jnp.bfloat16
    f32 = jnp.float32

    def from_rows(width):
        return pl.BlockSpec((1, size, width), lambda e, r: (e + low, r, 0))

    def whole(*shape):
        return pl.BlockSpec((1, *shape), lambda e, r: (e, 0, 0))

    def from_whole(*shape):
        return pl.BlockSpec((1, *shape), lambda e, r: (e + low, 0, 0))

    packed = [
        pl.BlockSpec(
            (planes, 1, D // planes, 2 * part),
            lambda e, r, n=n: (0, lax.min(e, n - 1), 0, 0),
        )
        for n, planes in ([pack] if pack else [])
    ]
    keep = (D, part) if steps > 1 else (16, 128)
    return pl.pallas_call(
        functools.partial(
            expert_kernel, steps, half, len(weights), len(into), pack[0] if pack else 0
        ),
        grid=(number, steps),
        in_specs=[
            pl.BlockSpec(memory_space=pltpu.SMEM),
            from_rows(D),
            from_rows(D),
            from_rows(128),
            *[(from_whole if len(weights) == 2 else whole)(*one.shape[1:]) for one in weights],
            from_whole(part, D),
            *[pl.BlockSpec(memory_space=pl.ANY)] * len(into),
        ],
        out_specs=[
            from_rows(D),
            from_rows(D),
            from_rows(128),
            whole(D, part),
            whole(D, part),
            from_whole(part, D),
            *packed,
        ],
        out_shape=[
            jax.ShapeDtypeStruct((total, depth, D), bf16),
            jax.ShapeDtypeStruct((total, depth, D), bf16),
            jax.ShapeDtypeStruct((total, depth, 128), bf16),
            jax.ShapeDtypeStruct((number, D, part), bf16),
            jax.ShapeDtypeStruct((number, D, part), bf16),
            jax.ShapeDtypeStruct((total, part, D), f32),
            *[
                jax.ShapeDtypeStruct((planes, n, D // planes, 2 * part), bf16)
                for n, planes in ([pack] if pack else [])
            ],
        ],
        input_output_aliases={
            5 + len(weights) + i: out for i, out in zip(range(len(into)), (0, 1, 2, 5))
        },
        scratch_shapes=[pltpu.VMEM(keep, f32), pltpu.VMEM(keep, f32)],
        compiler_params=pltpu.CompilerParams(vmem_limit_bytes=BIG),
    )(names, rows, grows, gates, *weights, down, *into)


def place_back(slots, dx, probs):
    pairs, number, pair = slots.shape
    size = 2 * CAP

    def rows(one):
        return pl.BlockSpec((number, size, one.shape[2]), lambda p: (0, p, 0))

    return pl.pallas_call(
        functools.partial(place_back_kernel, number),
        grid=(pairs,),
        in_specs=[pl.BlockSpec((1, number, pair), lambda p: (p, 0, 0)), rows(dx), rows(probs)],
        out_specs=pl.BlockSpec((pair, D + 128), lambda p: (p, 0)),
        out_shape=jax.ShapeDtypeStruct((pairs * pair, D + 128), jnp.bfloat16),
        compiler_params=pltpu.CompilerParams(vmem_limit_bytes=BIG),
    )(slots, dx, probs)


def widen_kernel(*refs):
    half = len(refs) // 2
    for source, target in zip(refs[:half], refs[half:]):
        target[...] = source[...].astype(jnp.float32)


def widen(spans, values):
    number, rows, columns = values[0].shape
    (low, high), (again, end) = spans

    def chosen(e):
        return (jnp.where(e < high - low, e + low, e - (high - low) + again), 0, 0)

    block = pl.BlockSpec((1, rows, columns), chosen)
    return pl.pallas_call(
        widen_kernel,
        grid=(high - low + end - again,),
        in_specs=[block] * len(values),
        out_specs=[block] * len(values),
        out_shape=[jax.ShapeDtypeStruct(one.shape, jnp.float32) for one in values],
        compiler_params=pltpu.CompilerParams(vmem_limit_bytes=BIG),
    )(*values)


def widen_pieces_kernel(low, n_pieces, offsets_ref, *refs):
    pieces, refs = refs[:n_pieces], refs[n_pieces + 2 :]
    targets, wide, sems = refs[:2], refs[2], refs[3]
    part = wide.shape[4]
    copies = []
    for k, piece in enumerate(pieces):
        columns = pl.ds(pl.multiple_of(offsets_ref[k], part), part)
        for n in range(2):
            wide[k, n] = piece[:, :, n * part : (n + 1) * part].astype(jnp.float32)
            copy = pltpu.make_async_copy(
                wide.at[k, n], targets[n].at[pl.ds(low, piece.shape[0]), :, columns], sems.at[k, n]
            )
            copy.start()
            copies.append(copy)
    for copy in copies:
        copy.wait()


def widen_pieces(offsets, low, pieces, into):
    size, rows, columns = pieces[0].shape
    anywhere = pl.BlockSpec(memory_space=pl.ANY)
    count = len(pieces)
    return pl.pallas_call(
        functools.partial(widen_pieces_kernel, low, count),
        in_specs=[
            pl.BlockSpec(memory_space=pltpu.SMEM),
            *[pl.BlockSpec(memory_space=pltpu.VMEM)] * count,
            anywhere,
            anywhere,
        ],
        out_specs=[anywhere, anywhere],
        out_shape=[jax.ShapeDtypeStruct(one.shape, one.dtype) for one in into],
        scratch_shapes=[
            pltpu.VMEM((count, 2, size, rows, columns // 2), jnp.float32),
            pltpu.SemaphoreType.DMA((count, 2)),
        ],
        input_output_aliases={1 + count: 0, 2 + count: 1},
        compiler_params=pltpu.CompilerParams(vmem_limit_bytes=BIG),
    )(offsets, *pieces, *into)


def shards(
    n_dp,
    n_expert,
    tokens,
    cotangent,
    lengths,
    routes,
    w_query,
    w_key,
    w_value,
    w_out,
    w_router,
    gain_attn,
    gain_query,
    gain_key,
    gain_mlp,
    w_gate,
    w_up,
    w_down,
):
    groups = n_dp * n_expert
    bf16 = jnp.bfloat16
    number = w_gate.shape[0]
    ff = w_gate.shape[2]
    part = ff // n_dp
    experts_all = w_router.shape[1]
    width = 128
    small = jnp.concatenate(
        [
            w_router,
            gain_attn[:, None],
            gain_query[:, None],
            gain_key[:, None],
            gain_mlp[:, None],
            jnp.zeros((w_router.shape[0], width - experts_all - 4), bf16),
        ],
        axis=1,
    )
    hits = jnp.any(
        routes[:, :, None] == jnp.arange(width, dtype=jnp.int32)[None, None, :], axis=1
    ).astype(bf16)
    count = tokens.shape[0]
    rows_each = w_query.shape[0]
    extras = jnp.concatenate([hits, jnp.pad(small, ((0, count - rows_each), (0, 0)))], axis=1)
    weights = jnp.stack([w_query, w_key, w_value, w_out])
    depth = w_gate.shape[1]
    early = number // 4
    beside = early + number // 8
    late = number - number // 4
    back_beside = number // 8
    back_third = back_beside + max(number // 8, 1)
    back_late = back_third + number // 4
    me = lax.axis_index("dp")
    cut_shape = jax.ShapeDtypeStruct((number, n_dp * depth, part), bf16)

    def row_block(size):
        return lambda ref, block: ref.at[pl.ds(pl.multiple_of(block * size, 16), size)]

    def columns_at(at):
        return pl.ds(pl.multiple_of(at * part, part), part)

    def rows_at(at):
        return pl.ds(pl.multiple_of(at * depth, depth), depth)

    def recut(low, high):
        def cuts(ins, outs):
            def pair(n):
                chosen = pl.ds(low, high - low)
                return (
                    lambda to: ins[n].at[chosen, :, columns_at(to)],
                    lambda at: outs[n].at[chosen, rows_at(at)],
                )

            return [pair(0), pair(1)]

        return cuts

    to_plane, from_plane = partners(me, n_dp)

    def permuted(pieces, chained=False):
        got = []
        for k, piece in enumerate(pieces, 1):
            if chained and got:
                piece, last = lax.optimization_barrier((piece, got.pop()))
                got.append(last)
            paths = [(i, partners(i, n_dp)[0](k)) for i in range(n_dp)]
            got.append(lax.ppermute(piece, "dp", paths))
        return got

    def cut_pieces(low, high, first_k, ins, outs):
        to, unused = partners(lax.axis_index("dp"), n_dp)
        pairs = []
        for k, piece in enumerate(outs, first_k):
            for n in range(2):
                source = ins[n].at[pl.ds(low, high - low), :, columns_at(to(k))]
                pairs.append((source, piece.at[:, :, pl.ds(n * part, part)]))
        return pairs

    def piece_shapes(size, first_k):
        shape = jax.ShapeDtypeStruct((size, depth, 2 * part), bf16)
        return [shape] * (n_dp - first_k if size else 0)

    def stages(*sizes):
        return [(size, depth, part) for size in sizes]

    soon_shapes = piece_shapes(beside - early, 1)
    late_shapes = piece_shapes(number - late, 0)
    n_soon = len(soon_shapes)

    weights_all, extras_all, gate_early, up_early, *pieces = gather_call(
        n_dp,
        n_expert,
        [weights, extras],
        [
            jax.ShapeDtypeStruct((4, groups * rows_each, D), bf16),
            jax.ShapeDtypeStruct((groups * count, 2 * width), bf16),
        ],
        [
            lambda ref, block: ref.at[
                :, pl.ds(pl.multiple_of(block * rows_each, 16), rows_each)
            ],
            row_block(count),
        ],
        [w_gate, w_up],
        [cut_shape, cut_shape, *soon_shapes, *late_shapes],
        recut(0, early),
        {},
        0,
        stages(
            *[early] * 2,
            *[beside - early] * (2 * n_soon),
            *[number - late] * (2 * n_dp),
        ),
        lambda ins, outs: cut_pieces(early, beside, 1, ins, outs[2 : 2 + n_soon])
        + cut_pieces(late, number, 0, ins, outs[2 + n_soon :]),
    )
    soon_pieces, late_pieces = pieces[:n_soon], pieces[n_soon:]
    query_weight, key_weight, value_weight, out_weight = (weights_all[i] for i in range(4))
    small_all = (
        extras_all[:, width:].reshape(groups, count, width)[:, :rows_each].reshape(-1, width)
    )
    hits_all = extras_all[:, :experts_all]
    router_weight = small_all[:, :experts_all]
    gains = small_all[:, experts_all : experts_all + 4].astype(jnp.float32)
    attn_gain, query_gain, key_gain, mlp_gain = (gains[:, i] for i in range(4))
    inputs = tokens.astype(jnp.float32)
    segment, position, places = layout(lengths[0], count)
    half = HD // 2
    freq = 10000.0 ** (-2.0 * jnp.arange(half, dtype=jnp.float32) / HD)
    angle = position.astype(jnp.float32)[:, None] * freq[None, :]
    cosine = jnp.cos(angle)[:, None, :]
    sine = jnp.sin(angle)[:, None, :]
    scale = HD ** (-0.5)
    normed, attn_inverse = rms_forward(inputs, attn_gain)
    normed_low = normed.astype(bf16)
    query_raw = product(normed_low, query_weight, "td,de->te")
    key_raw = product(normed_low, key_weight, "td,de->te")
    value_low = product(normed_low, value_weight, "td,de->te").astype(bf16)
    query_normed, query_inverse = rms_forward(query_raw, query_gain)
    key_normed, key_inverse = rms_forward(key_raw, key_gain)
    query_low = rotate(query_normed, cosine, sine).astype(bf16).reshape(count, HEADS, HD)
    key_low = rotate(key_normed, cosine, sine).astype(bf16).reshape(count, HEADS, HD)
    value_heads = value_low.reshape(count, HEADS, HD)
    allowed = (segment[:, None] == segment[None, :]) & (places[None, :] <= places[:, None])
    scores = product(query_low, key_low, "qhd,khd->hqk") * scale
    scores = jnp.where(allowed[None], scores, -1e30)
    probs = jax.nn.softmax(scores, axis=-1)
    probs_low = probs.astype(bf16)
    attended_low = product(probs_low, value_heads, "hqk,khd->qhd").reshape(count, D).astype(bf16)
    middle = inputs + product(attended_low, out_weight, "td,de->te")
    mlp_normed, mlp_inverse = rms_forward(middle, mlp_gain)
    mlp_low = mlp_normed.astype(bf16)
    router = jax.nn.softmax(product(mlp_low, router_weight, "td,de->te"), axis=-1)

    first = lax.axis_index("expert") * number
    hit = lax.dynamic_slice_in_dim(hits_all, first, number, 1).reshape(groups, count, number)
    before = jnp.tril(jnp.ones((count, count), bf16), -1)
    slot = product(before, hit, "ts,bse->bet").astype(jnp.int32)
    slot = jnp.where(jnp.transpose(hit, (0, 2, 1)) > 0, slot, -1)
    slot = slot.reshape(groups // 2, 2, number, count)
    shift = jnp.array([0, CAP], jnp.int32)[None, :, None, None]
    slots = jnp.transpose(jnp.where(slot < 0, -1, slot + shift), (0, 2, 1, 3))
    slots = slots.reshape(groups // 2, number, 2 * count)
    router_own = jnp.pad(
        jnp.roll(router_weight, -first, axis=1), ((0, 0), (0, width - experts_all))
    )
    if n_soon:
        mlp_low, *soon_pieces = lax.optimization_barrier((mlp_low, *permuted(soon_pieces)))

    def put_weights(ins, outs):
        chosen = pl.ds(early, beside - early)
        unused, heard = partners(lax.axis_index("dp"), n_dp)
        pairs = []
        if beside > early:
            own = lax.axis_index("dp")
            for n in range(2):
                source = ins[n].at[chosen, :, columns_at(own)]
                pairs.append((source, outs[n].at[chosen, rows_at(own)]))
        for k, piece in enumerate(ins[6:], 1):
            for n in range(2):
                columns = piece.at[:, :, pl.ds(n * part, part)]
                pairs.append((columns, outs[n].at[chosen, rows_at(heard(k))]))
        return pairs

    def pick_all(items, ins, outs):
        pick_rows(number, experts_all, ins[4], *items, ins[5], *outs[2:])

    unused, unused, gate_cut, up_cut, rows, grows, gates = gather_call(
        n_dp,
        n_expert,
        [mlp_low, cotangent],
        [jax.ShapeDtypeStruct((groups * count, D), bf16)] * 2,
        [row_block(count)] * 2,
        [w_gate, w_up, gate_early, up_early, slots, router_own, *soon_pieces],
        [cut_shape, cut_shape, *pick_shapes(number, groups // 2)],
        recut(beside, late),
        {4: 2, 5: 3},
        1,
        stages(*[late - beside] * 2, *[beside - early] * (2 * n_dp if n_soon else 0)),
        put_weights,
        pick_all,
    )
    *late_pieces, rows = lax.optimization_barrier((*late_pieces, rows))
    late_pieces = [late_pieces[0], *permuted(late_pieces[1:])]
    packing = back_beside > 0 and depth == 512
    *outs, gate_soon, up_soon, down_soon = expert_call(
        first[None],
        experts_all,
        0,
        late,
        rows,
        grows,
        gates,
        [gate_cut, up_cut],
        w_down,
        pack=(back_beside, n_dp) if packing else (),
    )
    if packing:
        *outs, gate_soon, up_soon, down_soon, packed = [*outs, gate_soon, up_soon, down_soon]
    offsets = [from_plane(k) * depth for k in range(n_dp)]
    weighted, grad_rows, grad_gates, gate_rest, up_rest, grad_down_part = expert_call(
        jnp.stack([first + late, *offsets]),
        experts_all,
        late,
        number - late,
        rows,
        grows,
        gates,
        late_pieces,
        w_down,
        [*outs, down_soon],
    )
    part_back = place_back(slots, grad_rows, grad_gates)

    def ways(low, high, at, ins, outs):
        def pair(n):
            return (
                lambda to: ins[n].at[pl.ds(low, high - low), rows_at(to)],
                lambda here: outs[n].at[pl.ds(low + at, high - low), :, columns_at(here)],
            )

        return [pair(0), pair(1)]

    def cut_grads(low, high, ins, outs):
        to, unused = partners(lax.axis_index("dp"), n_dp)
        pairs = []
        for k, piece in enumerate(outs, 1):
            for n in range(2):
                source = ins[n].at[pl.ds(low, high - low), rows_at(to(k))]
                pairs.append((source, piece.at[:, :, pl.ds(n * part, part)]))
        return pairs

    pieces = []
    if back_beside:
        for k in range(1, n_dp):
            if packing:
                piece = lax.dynamic_index_in_dim(packed, to_plane(k), 0, False)
            else:
                piece = jnp.concatenate(
                    [
                        lax.dynamic_slice_in_dim(
                            one[:back_beside], to_plane(k) * depth, depth, 1
                        )
                        for one in (gate_soon, up_soon)
                    ],
                    axis=2,
                )
            pieces.append(piece)
        ahead = lax.optimization_barrier((*pieces, *late_pieces[1:]))
        pieces = permuted(ahead[: n_dp - 1])
        part_back, *pieces = lax.optimization_barrier((part_back, *pieces))
    way_shapes = [jax.ShapeDtypeStruct((number, depth, ff), bf16)] * 2
    piece_shape = jax.ShapeDtypeStruct((back_late - back_third, depth, 2 * part), bf16)
    (back,), (gate_third, up_third, part_out, *later_pieces) = scatter_all(
        n_dp,
        n_expert,
        [part_back.reshape(n_dp, n_expert, count, D + width)],
        [gate_soon, up_soon, slots, weighted],
        [
            *way_shapes,
            jax.ShapeDtypeStruct((groups * count, D), bf16),
            *[piece_shape] * (n_dp - 1),
        ],
        lambda ins, outs: ways(back_beside, back_third, 0, ins, outs),
        8,
        (),
        stages(
            *[back_third - back_beside] * 2, *[back_late - back_third] * (2 * (n_dp - 1))
        ),
        lambda ins, outs: cut_grads(back_third, back_late, ins, outs[3:]),
        lambda ins, outs: place_out(ins[2], ins[3], outs[2]),
    )
    later_pieces = permuted(later_pieces)

    def attention_back(back):
        query_weight, key_weight, value_weight, out_weight = (weights_all[i] for i in range(4))
        grad_final = cotangent.astype(jnp.float32)
        grad_mlp = back[:, :D]
        grad_router_probs = back[:, D : D + experts_all] + back[:, D + experts_all :]
        grad_logits = router * (
            grad_router_probs - jnp.sum(router * grad_router_probs, axis=1, keepdims=True)
        )
        grad_logits_low = grad_logits.astype(bf16)
        grad_router_full = product(mlp_low, grad_logits_low, "td,te->de")
        grad_mlp = grad_mlp + product(grad_logits_low, router_weight, "te,de->td")
        grad_middle_part, grad_mlp_gain = rms_backward(middle, mlp_inverse, mlp_gain, grad_mlp)
        grad_middle = grad_final + grad_middle_part
        grad_branch_low = grad_middle.astype(bf16)
        grad_out_full = product(attended_low, grad_branch_low, "td,te->de")
        grad_attended = (
            product(grad_branch_low, out_weight, "te,de->td").astype(bf16).reshape(count, HEADS, HD)
        )
        grad_weights = product(grad_attended, value_heads, "qhd,khd->hqk")
        grad_scores = probs * (grad_weights - jnp.sum(probs * grad_weights, axis=-1, keepdims=True))
        grad_scores_low = grad_scores.astype(bf16)
        grad_query_turn = product(grad_scores_low, key_low, "hqk,khd->qhd").reshape(count, D) * scale
        grad_key_turn = product(grad_scores_low, query_low, "hqk,qhd->khd").reshape(count, D) * scale
        grad_value_low = (
            product(probs_low, grad_attended, "hqk,qhd->khd").reshape(count, D).astype(bf16)
        )
        grad_query_raw, grad_query_gain = rms_backward(
            query_raw, query_inverse, query_gain, rotate(grad_query_turn, cosine, -sine)
        )
        grad_key_raw, grad_key_gain = rms_backward(
            key_raw, key_inverse, key_gain, rotate(grad_key_turn, cosine, -sine)
        )
        grad_query_low = grad_query_raw.astype(bf16)
        grad_key_low = grad_key_raw.astype(bf16)
        grad_query_full = product(normed_low, grad_query_low, "td,te->de")
        grad_key_full = product(normed_low, grad_key_low, "td,te->de")
        grad_value_full = product(normed_low, grad_value_low, "td,te->de")
        grad_normed = (
            product(grad_query_low, query_weight, "te,de->td")
            + product(grad_key_low, key_weight, "te,de->td")
            + product(grad_value_low, value_weight, "te,de->td")
        )
        grad_inputs_part, grad_attn_gain = rms_backward(inputs, attn_inverse, attn_gain, grad_normed)
        grad_inputs = grad_middle + grad_inputs_part

        small_grads = jnp.concatenate(
            [
                grad_router_full,
                grad_attn_gain[:, None],
                grad_query_gain[:, None],
                grad_key_gain[:, None],
                grad_mlp_gain[:, None],
                jnp.zeros((D, width - experts_all - 4), jnp.float32),
            ],
            axis=1,
        )
        grads = (grad_out_full, grad_value_full, grad_key_full, grad_query_full, small_grads)
        return grad_inputs, *[one.astype(bf16) for one in grads]

    def unreached(back):
        shapes = [(count, D)] + [(D, D)] * 4 + [(D, width)]
        kinds = [jnp.float32] + [bf16] * 5
        return tuple(jnp.zeros(shape, kind) for shape, kind in zip(shapes, kinds))

    grad_inputs, *weight_grads = lax.cond(lengths[0, 0] > 0, attention_back, unreached, back)

    def blocks_of(value):
        return value.reshape(n_dp, n_expert, rows_each, -1)

    sums, (gate_back, up_back) = scatter_all(
        n_dp,
        n_expert,
        [blocks_of(value) for value in weight_grads]
        + [part_out.reshape(n_dp, n_expert, count, D)],
        [gate_third, up_third, gate_soon, up_soon, gate_rest, up_rest],
        way_shapes,
        lambda ins, outs: ways(back_late, late, 0, ins[2:4], outs)
        + ways(0, number - late, late, ins[4:6], outs),
        16,
        ((0, 0), (1, 1)),
        [],
    )
    grad_out_part, grad_value_part, grad_key_part, grad_query_part, small_part, summed = sums
    output = (middle + summed).astype(bf16)
    grad_router_part = small_part[:, :experts_all]
    gain_parts = [small_part[:, experts_all + i] for i in range(4)]
    widened = widen([(back_beside, back_third), (back_late, number)], [gate_back, up_back])
    offsets = jnp.stack([from_plane(k) * part for k in range(n_dp)])
    for low, high, others in (
        (0, back_beside, pieces),
        (back_third, back_late, later_pieces),
    ):
        if high > low:
            own = jnp.concatenate(
                [
                    lax.dynamic_slice_in_dim(one[low:high], me * depth, depth, 1)
                    for one in (gate_soon, up_soon)
                ],
                axis=2,
            )
            widened = widen_pieces(offsets, low, [own, *others], widened)
    grad_gate_part, grad_up_part = widened
    return (
        output,
        grad_inputs,
        grad_query_part,
        grad_key_part,
        grad_value_part,
        grad_out_part,
        grad_router_part,
        gain_parts[0],
        gain_parts[1],
        gain_parts[2],
        gain_parts[3],
        grad_gate_part,
        grad_up_part,
        grad_down_part,
    )


def solution(mesh):
    return jax.shard_map(
        functools.partial(shards, mesh.shape["dp"], mesh.shape["expert"]),
        mesh=mesh,
        in_specs=(
            P(("dp", "expert"), None),
            P(("dp", "expert"), None),
            P(("dp", "expert"), None),
            P(("dp", "expert"), None),
            P(("dp", "expert"), None),
            P(("dp", "expert"), None),
            P(("dp", "expert"), None),
            P(("dp", "expert"), None),
            P(("dp", "expert"), None),
            P(("dp", "expert")),
            P(("dp", "expert")),
            P(("dp", "expert")),
            P(("dp", "expert")),
            P("expert", "dp", None),
            P("expert", "dp", None),
            P("expert", "dp", None),
        ),
        out_specs=(
            P(("dp", "expert"), None),
            P(("dp", "expert"), None),
            P(("dp", "expert"), None),
            P(("dp", "expert"), None),
            P(("dp", "expert"), None),
            P(("dp", "expert"), None),
            P(("dp", "expert"), None),
            P(("dp", "expert")),
            P(("dp", "expert")),
            P(("dp", "expert")),
            P(("dp", "expert")),
            P("expert", "dp", None),
            P("expert", "dp", None),
            P("expert", "dp", None),
        ),
        check_vma=False,
    )
```

```python
import functools

import jax
import jax.numpy as jnp
from jax import lax
from jax.experimental import pallas as pl
from jax.experimental.pallas import tpu as pltpu
from jax.sharding import PartitionSpec as P

D = 2048
HEADS = 16
HD = 128
TOPK = 8
CAP = 24


eps = 1e-05


def product(left, right, form):
    return jnp.einsum(form, left, right, preferred_element_type=jnp.float32)


def rms_forward(values, gain):
    inverse = lax.rsqrt(jnp.mean(values * values, axis=-1, keepdims=True) + eps)
    return (values * inverse * gain, inverse)


def rms_backward(values, inverse, gain, grad):
    scaled = grad * gain
    inner = jnp.mean(scaled * values, axis=-1, keepdims=True)
    grad_values = inverse * scaled - values * (inverse * inverse * inverse) * inner
    grad_gain = jnp.sum(grad * values * inverse, axis=0)
    return (grad_values, grad_gain)


def layout(lengths_row, count):
    places = jnp.arange(count, dtype=jnp.int32)
    ends = jnp.cumsum(lengths_row, dtype=jnp.int32)
    passed = (places[:, None] >= ends[None, :]).astype(jnp.int32)
    segment = jnp.sum(passed, axis=1, dtype=jnp.int32)
    start = jnp.sum(passed * lengths_row[None, :], axis=1, dtype=jnp.int32)
    return (segment, places - start, places)


def rotate(values, cosine, sine):
    count = values.shape[0]
    heads = values.reshape(count, HEADS, HD)
    half = HD // 2
    first = heads[..., :half]
    second = heads[..., half:]
    turned = jnp.concatenate(
        [first * cosine - second * sine, second * cosine + first * sine], axis=-1
    )
    return turned.reshape(count, D)


MESH = pl.DeviceIdType.MESH
BIG = 60 * 1024 * 1024


def place_of():
    z = lax.axis_index("dp")
    j = lax.axis_index("expert")
    return z, j, j // 2, j % 2


def other_chips(chip, chips):
    if chips == 4:
        square = [chip, chip + 1 - 2 * (chip % 2), chip + 2 - 4 * (chip // 2), 3 - chip]
        return lambda k: square[k], lambda k: square[k]
    return lambda k: (chip + k) % chips, lambda k: (chip + chips - k) % chips


def partners(z, n_dp):
    if n_dp == 4:
        pairs = [z, (z + 2) % 4, 3 - z, z + 1 - 2 * (z % 2)]
        return lambda k: pairs[k], lambda k: pairs[k]
    return lambda k: (z + k) % n_dp, lambda k: (z + n_dp - k) % n_dp


def greet(n_dp, n_expert):
    z, j, chip, core = place_of()
    chips = n_expert // 2
    barrier = pltpu.get_barrier_semaphore()
    for k in range(1, n_dp):
        pl.semaphore_signal(
            barrier, inc=1, device_id=((z + k) % n_dp, j), device_id_type=MESH
        )
    for k in range(1, chips):
        other = ((chip + k) % chips) * 2 + core
        pl.semaphore_signal(barrier, inc=1, device_id=(z, other), device_id_type=MESH)
    pl.semaphore_signal(
        barrier, inc=1, device_id=(z, chip * 2 + 1 - core), device_id_type=MESH
    )
    pl.semaphore_wait(barrier, n_dp - 1 + chips - 1 + 1)


def remote(source, target, send, receive, device):
    return pltpu.make_async_remote_copy(
        src_ref=source,
        dst_ref=target,
        send_sem=send,
        recv_sem=receive,
        device_id=device,
        device_id_type=MESH,
    )


def exchange(n_dp, pairs, send, receive):
    z, j, chip, core = place_of()
    to_plane, unused = partners(z, n_dp)
    copies = []
    for i, (source, target) in enumerate(pairs):
        for k in range(1, n_dp):
            to = to_plane(k)
            copies.append(
                remote(source(to), target(z), send.at[i, k], receive.at[i, k], (to, j))
            )
    return copies


def moves(pairs, stages, local):
    if not stages:
        copies = [
            pltpu.make_async_copy(source, target, local.at[i, 0])
            for i, (source, target) in enumerate(pairs)
        ]
        for copy in copies:
            copy.start()
        return [], copies
    bring = [
        pltpu.make_async_copy(source, stages[i], local.at[i, 0])
        for i, (source, target) in enumerate(pairs)
    ]
    put = [
        pltpu.make_async_copy(stages[i], target, local.at[i, 1])
        for i, (source, target) in enumerate(pairs)
    ]
    return bring, put


def nothing(ins, outs):
    return []


def gather_kernel(
    n_dp, n_expert, n_items, places, cuts, puts, finish, n_cut, n_out, n_stages, *refs
):
    z, j, chip, core = place_of()
    chips = n_expert // 2
    square = chips == 4
    to_chip, from_chip = other_chips(chip, chips)
    sources = refs[:n_items]
    cut_in = refs[n_items : n_items + n_cut]
    at = n_items + n_cut
    targets = refs[at : at + n_items]
    cut_out = refs[at + n_items : at + n_items + n_out]
    (
        send_c,
        recv_c,
        send_b,
        recv_b,
        send_a,
        recv_a,
        local,
        send_x,
        recv_x,
        local_y,
        *stages,
    ) = refs[at + n_items + n_out :]
    greet(n_dp, n_expert)
    mate = (z, chip * 2 + 1 - core)
    near = (1, 2) if square else tuple(range(1, chips))

    def slot(i, plane, column):
        return places[i](targets[i], plane * n_expert + column)

    def pass_on(i, plane, source, column, k, chip_to):
        return remote(
            source,
            slot(i, plane, column),
            send_b.at[i, plane, k],
            recv_b.at[i, plane, k],
            (z, chip_to * 2 + core),
        )

    def hand(i, plane, source):
        for k in near:
            pass_on(i, plane, source, j, k, to_chip(k)).start()
        remote(
            source, slot(i, plane, j), send_a.at[i, plane, 0], recv_a.at[i, plane, 0], mate
        ).start()

    def along(i, plane, source, way, step):
        return remote(
            source, slot(i, plane, j), send_c.at[i, way, plane], recv_c.at[i, plane], (z + step, j)
        )

    def at_distance(d, body):
        if d == 0:
            body(z, 0)
            return

        @pl.when(z >= d)
        def _():
            body(z - d, 0)

        @pl.when(z + d < n_dp)
        def _():
            body(z + d, 1)

    for i in range(n_items):

        @pl.when(z < n_dp - 1)
        def _():
            along(i, z, sources[i], 0, 1).start()

        @pl.when(z > 0)
        def _():
            along(i, z, sources[i], 1, -1).start()

        hand(i, z, sources[i])
        pltpu.make_async_copy(sources[i], slot(i, z, j), local.at[i]).start()

    def relay(plane, way):
        step = -1 if way else 1
        for i in range(n_items):
            block = slot(i, plane, j)
            along(i, plane, block, way, step).wait_recv()

            @pl.when(z > 0 if way else z < n_dp - 1)
            def _():
                along(i, plane, block, way, step).start()

            hand(i, plane, block)

    for d in range(1, n_dp):
        at_distance(d, relay)
    pairs = cuts(cut_in, cut_out)
    copies = exchange(n_dp, pairs, send_x, recv_x)
    for copy in copies:
        copy.start()
    own = [(source(z), target(z)) for source, target in pairs]
    bring, put = moves(own + puts(cut_in, cut_out), stages, local_y)
    for copy in bring:
        copy.start()
    for one, other in zip(bring, put):
        one.wait()
        other.start()

    def arrive(i, plane, k):
        column = from_chip(k) * 2 + core
        block = slot(i, plane, column)
        pass_on(i, plane, block, column, k, chip).wait_recv()
        remote(block, block, send_a.at[i, plane, k], recv_a.at[i, plane, k], mate).start()
        return block, column

    def arrived(plane, way):
        for i in range(n_items):
            for k in near:
                block, column = arrive(i, plane, k)
                if square:

                    @pl.when(plane % 2 == k - 1)
                    def _():
                        pass_on(i, plane, block, column, 3, to_chip(3 - k)).start()

    def crossed(plane, way):
        for i in range(n_items):
            arrive(i, plane, 3)

    for d in range(n_dp):
        at_distance(d, arrived)
    if square:
        for d in range(n_dp):
            at_distance(d, crossed)

    for i in range(n_items):
        for plane in range(n_dp):
            for k in range(chips):
                column = (from_chip(k) if k else chip) * 2 + 1 - core
                block = slot(i, plane, column)
                remote(
                    block, block, send_a.at[i, plane, k], recv_a.at[i, plane, k], mate
                ).wait_recv()
        pltpu.make_async_copy(sources[i], slot(i, z, j), local.at[i]).wait()
    finish(targets, cut_in, cut_out)
    for i in range(n_items):
        for plane in range(n_dp):
            block = slot(i, plane, j)
            for k in range(1, chips):
                pass_on(i, plane, block, j, k, chip).wait_send()
            for k in range(chips):
                remote(
                    block, block, send_a.at[i, plane, k], recv_a.at[i, plane, k], mate
                ).wait_send()

            @pl.when((z < n_dp - 1) & (z >= plane))
            def _():
                along(i, plane, block, 0, 1).wait_send()

            @pl.when((z > 0) & (z <= plane))
            def _():
                along(i, plane, block, 1, -1).wait_send()

    for copy in copies + put:
        copy.wait()


def gather_call(
    n_dp,
    n_expert,
    items,
    shapes,
    places,
    cut_in,
    cut_shapes,
    cuts,
    aliases,
    number,
    stages,
    puts=nothing,
    finish=lambda items, ins, outs: None,
):
    chips = n_expert // 2
    n, m = len(items), len(cut_shapes)
    dma = pltpu.SemaphoreType.DMA
    anywhere = pl.BlockSpec(memory_space=pl.ANY)
    return pl.pallas_call(
        functools.partial(
            gather_kernel,
            n_dp,
            n_expert,
            n,
            places,
            cuts,
            puts,
            finish,
            len(cut_in),
            m,
            len(stages),
        ),
        out_shape=[*shapes, *cut_shapes],
        in_specs=[anywhere] * (n + len(cut_in)),
        out_specs=[anywhere] * (n + m),
        scratch_shapes=[
            dma((n, 2, n_dp)),
            dma((n, n_dp)),
            dma((n, n_dp, chips)),
            dma((n, n_dp, chips)),
            dma((n, n_dp, chips)),
            dma((n, n_dp, chips)),
            dma((n,)),
            dma((4, n_dp)),
            dma((4, n_dp)),
            dma((max(len(stages), 4), 2)),
            *[pltpu.VMEM(stage, jnp.bfloat16) for stage in stages],
        ],
        input_output_aliases=aliases,
        compiler_params=pltpu.CompilerParams(
            collective_id=number, has_side_effects=True, vmem_limit_bytes=BIG
        ),
    )(*items, *cut_in)


def scatter_kernel(
    n_dp, n_expert, n_arrays, items, n_cut, n_out, cuts, puts, middle, rings, n_rings, *refs
):
    n_items = len(items)
    z, j, chip, core = place_of()
    chips = n_expert // 2
    square = chips == 4
    to_chip, from_chip = other_chips(chip, chips)
    refs = list(refs)

    def take(count):
        taken = refs[:count]
        del refs[:count]
        return taken

    sources, cut_in, targets, cut_out = take(n_arrays), take(n_cut), take(n_arrays), take(n_out)
    ring, got_a, got_b, got_c = take(n_rings), take(n_items), take(n_items), take(n_items)
    transit = take(n_items)
    (
        send_a,
        recv_a,
        send_b,
        recv_b,
        send_c,
        recv_c,
        send_t,
        recv_t,
        local,
        send_x,
        recv_x,
        local_y,
        *stages,
    ) = refs
    greet(n_dp, n_expert)
    mate = (z, chip * 2 + 1 - core)
    order = [3, 1, 2, 0] if square else [*range(1, chips), 0]
    half = n_dp // 2
    low, high = pl.ds(0, half), pl.ds(half, n_dp - half)

    def chip_of(k):
        return to_chip(k) if k else chip

    def source(i, column):
        array, first, rows = items[i]
        return sources[array].at[:, column, pl.ds(first, rows)]

    def to_mate(i, k):
        return remote(
            source(i, chip_of(k) * 2 + 1 - core),
            got_a[i].at[k],
            send_a.at[i, k],
            recv_a.at[i, k],
            mate,
        )

    turn = [0] * n_rings
    loads = []
    for i in range(n_items):
        for k in order:
            loads.append((i, k, turn[rings[i]] % 2))
            turn[rings[i]] += 1

    def load(i, k, at):
        return pltpu.make_async_copy(
            source(i, chip_of(k) * 2 + core), ring[rings[i]].at[at], local.at[rings[i], at]
        )

    def send_near(i, k, part, number):
        return remote(
            got_a[i].at[k, part],
            got_b[i].at[k - 1, part],
            send_b.at[i, number],
            recv_b.at[i, number],
            (z, to_chip(k) * 2 + core),
        )

    def send_over(i, k, part):
        return remote(
            got_a[i].at[3, part],
            transit[i].at[k - 1],
            send_t.at[i, k],
            recv_t.at[i, k],
            (z, to_chip(k) * 2 + core),
        )

    def send_far(i, k):
        return remote(
            got_a[i].at[k],
            got_b[i].at[k - 1],
            send_b.at[i, k],
            recv_b.at[i, k],
            (z, to_chip(k) * 2 + core),
        )

    def along(i, plane, way):
        slot = n_dp - (z - 1) + plane if way else plane - (z + 1)
        return remote(
            got_a[i].at[0, plane],
            got_c[i].at[slot],
            send_c.at[i, plane],
            recv_c.at[i, slot],
            (z - 1 if way else z + 1, j),
        )

    def from_along(i, slot):
        return remote(
            got_c[i].at[slot], got_c[i].at[slot], send_c.at[i, 0], recv_c.at[i, slot], mate
        )

    f32 = jnp.float32

    def add(i, planes, target, terms):
        rows = got_a[i].shape[2]
        per = rows // 16

        def step(n, unused):
            plane = n // per
            at = pl.ds(pl.multiple_of((n % per) * 16, 16), 16)
            total = terms[0](plane, at).astype(f32)
            for term in terms[1:]:
                total = total + term(plane, at).astype(f32)
            target(plane, at, total)
            return unused

        lax.fori_loop(0, planes * per, step, 0)

    def grow(i, k, first, planes, term):
        def target(plane, at, total):
            got_a[i][k, plane + first, at] = total.astype(got_a[i].dtype)

        add(i, planes, target, [lambda plane, at: got_a[i][k, plane + first, at], term])

    for i in range(n_items):
        for k in order:
            to_mate(i, k).start()
    started = 0
    ahead = [0] * n_rings
    for i, k, at in loads:
        if ahead[rings[i]] < 2:
            load(i, k, at).start()
            ahead[rings[i]] += 1
    pairs = cuts(cut_in, cut_out)
    copies = exchange(n_dp, pairs, send_x, recv_x)
    for copy in copies:
        copy.start()
    own = [(source(z), target(z)) for source, target in pairs]
    bring, put = moves(own + puts(cut_in, cut_out), stages, local_y)
    for copy in bring:
        copy.start()

    def over_cores(i):
        for n, (item, k, at) in enumerate(loads):
            if item != i:
                continue
            load(i, k, at).wait()
            to_mate(i, k).wait_recv()
            grow(i, k, 0, n_dp, lambda plane, rows: ring[rings[i]][at, plane, rows])
            later = [one for one in loads[n + 1 :] if rings[one[0]] == rings[i]]
            if len(later) >= 2:
                load(*later[1]).start()
            if not k:
                continue
            if not square:
                send_far(i, k).start()
            elif k == 3:
                send_over(i, 1, low).start()
                send_over(i, 2, high).start()
            elif k == 1:
                send_near(i, 1, low, 0).start()
            else:
                send_near(i, 2, high, 1).start()

    def pass_over(i):
        if not square:
            return
        send_over(i, 2, high).wait_recv()
        grow(i, 1, half, n_dp - half, lambda plane, rows: transit[i][1, plane, rows])
        send_near(i, 1, high, 2).start()
        send_over(i, 1, low).wait_recv()
        grow(i, 2, 0, half, lambda plane, rows: transit[i][0, plane, rows])
        send_near(i, 2, low, 3).start()

    def over_chips(i):
        if square:
            send_near(i, 1, low, 0).wait_recv()
            send_near(i, 2, high, 1).wait_recv()
            send_near(i, 1, high, 2).wait_recv()
            send_near(i, 2, low, 3).wait_recv()
        else:
            for k in range(1, chips):
                send_far(i, k).wait_recv()
        heard = 2 if square else chips - 1

        def target(plane, at, total):
            got_a[i][0, plane, at] = total.astype(got_a[i].dtype)

        terms = [lambda plane, at: got_a[i][0, plane, at]]
        for other in range(heard):
            terms.append(lambda plane, at, other=other: got_b[i][other, plane, at])
        add(i, n_dp, target, terms)
        for d in range(n_dp - 1, 0, -1):
            for way in (0, 1):
                plane = z - d if way else z + d

                @pl.when(z == (n_dp - 1 if way else 0))
                def _():
                    along(i, plane, way).start()

    def over_planes(i):
        for d in range(n_dp - 2, 0, -1):
            for way in (0, 1):
                plane = z - d if way else z + d
                slot = n_dp - d if way else d

                @pl.when((plane >= 0) & (z < n_dp - 1) if way else (plane < n_dp) & (z > 0))
                def _():
                    from_along(i, slot).wait_recv()
                    grow(i, 0, plane, 1, lambda unused, at: got_c[i][slot, at])
                    along(i, plane, way).start()

    def finish(i):
        array, first, rows = items[i]

        def here(at):
            return pl.ds(pl.multiple_of(first + at.start, 16), 16)

        def own(unused, at, total):
            targets[array][here(at)] = total

        add(i, 1, own, [lambda unused, at: got_a[i][0, z, at]])
        for slot, arrives in ((0, z > 0), (n_dp, z < n_dp - 1)):

            @pl.when(arrives)
            def _():
                from_along(i, slot).wait_recv()
                add(
                    i,
                    1,
                    own,
                    [
                        lambda unused, at: targets[array][here(at)],
                        lambda unused, at: got_c[i][slot, at],
                    ],
                )

    steps = (over_cores, pass_over, over_chips, over_planes, finish)
    for n in range(n_items + len(steps) - 1):
        for late, step in enumerate(steps):
            if 0 <= n - late < n_items:
                step(n - late)
        if n == min(1, n_items - 1):
            for one, other in zip(bring, put):
                one.wait()
                other.start()
            middle(cut_in, cut_out)
    for i in range(n_items):
        for k in range(chips):
            to_mate(i, k).wait_send()
        if square:
            for k, part in ((1, low), (2, high)):
                send_over(i, k, part).wait_send()
            for k, part, number in ((1, low, 0), (2, high, 1), (1, high, 2), (2, low, 3)):
                send_near(i, k, part, number).wait_send()
        else:
            for k in range(1, chips):
                send_far(i, k).wait_send()
        for plane in range(n_dp):

            @pl.when(z != plane)
            def _():
                remote(
                    got_a[i].at[0, plane],
                    got_c[i].at[0],
                    send_c.at[i, plane],
                    recv_c.at[i, 0],
                    mate,
                ).wait_send()

    for copy in copies + put:
        copy.wait()


def scatter_call(
    n_dp,
    n_expert,
    arrays,
    splits,
    cut_in,
    cut_shapes,
    cuts,
    number,
    aliases,
    stages,
    puts=nothing,
    middle=nothing,
):
    chips = n_expert // 2
    square = chips == 4
    items = []
    for array, (one, split) in enumerate(zip(arrays, splits)):
        rows = one.shape[2] // split
        items += [(array, first, rows) for first in range(0, one.shape[2], rows)]
    n, m = len(items), len(cut_shapes)
    count = len(arrays)
    dma = pltpu.SemaphoreType.DMA
    anywhere = pl.BlockSpec(memory_space=pl.ANY)
    blocks = [(rows, arrays[array].shape[3]) for array, unused, rows in items]
    kinds = sorted(set(blocks))
    rings = [kinds.index(block) for block in blocks]
    bf16 = jnp.bfloat16
    heard = 2 if square else chips - 1
    return pl.pallas_call(
        functools.partial(
            scatter_kernel,
            n_dp,
            n_expert,
            count,
            items,
            len(cut_in),
            m,
            cuts,
            puts,
            middle,
            rings,
            len(kinds),
        ),
        out_shape=[
            *[jax.ShapeDtypeStruct(one.shape[2:], jnp.float32) for one in arrays],
            *cut_shapes,
        ],
        in_specs=[anywhere] * (count + len(cut_in)),
        out_specs=[pl.BlockSpec(memory_space=pltpu.VMEM)] * count + [anywhere] * m,
        scratch_shapes=[
            *[pltpu.VMEM((2, n_dp, *kind), bf16) for kind in kinds],
            *[pltpu.VMEM((chips, n_dp, *block), bf16) for block in blocks],
            *[pltpu.VMEM((heard, n_dp, *block), bf16) for block in blocks],
            *[pltpu.VMEM((n_dp + 1, *block), bf16) for block in blocks],
            *[pltpu.VMEM((2, n_dp // 2, *(block if square else (16, 128))), bf16) for block in blocks],
            dma((n, chips)),
            dma((n, chips)),
            dma((n, chips)),
            dma((n, chips)),
            dma((n, n_dp)),
            dma((n, n_dp + 1)),
            dma((n, 3)),
            dma((n, 3)),
            dma((len(kinds), 2)),
            dma((4, n_dp)),
            dma((4, n_dp)),
            dma((max(len(stages), 4), 2)),
            *[pltpu.VMEM(stage, jnp.bfloat16) for stage in stages],
        ],
        input_output_aliases=aliases,
        compiler_params=pltpu.CompilerParams(
            collective_id=number, has_side_effects=True, vmem_limit_bytes=62 * 1024 * 1024
        ),
    )(*arrays, *cut_in)


def scatter_all(
    n_dp,
    n_expert,
    items,
    splits,
    cut_in,
    cut_shapes,
    cuts,
    number,
    aliases,
    stages,
    puts=nothing,
    middle=nothing,
):
    chips = n_expert // 2
    blocks = (2 * chips - 1 if chips != 4 else 7) * n_dp + n_dp + 3
    need = sum(blocks * item.shape[2] * item.shape[3] * 2 for item in items)
    kinds = {(item.shape[2] // split, item.shape[3]) for item, split in zip(items, splits)}
    need += sum(2 * n_dp * kind[0] * kind[1] * 2 for kind in kinds)
    need += sum(stage[0] * stage[1] * stage[2] * 2 for stage in stages)
    pieces = -(-need // (61 * 1024 * 1024))
    tiles = [item.shape[3] // 128 for item in items]
    results = [[] for item in items]
    extra = []
    for piece in range(pieces):
        ends = [(t * piece // pieces * 128, t * (piece + 1) // pieces * 128) for t in tiles]
        used = [i for i, (low, high) in enumerate(ends) if high > low]
        first = piece == 0
        outs = scatter_call(
            n_dp,
            n_expert,
            [items[i][..., ends[i][0] : ends[i][1]] if pieces > 1 else items[i] for i in used],
            [splits[i] for i in used],
            cut_in if first else [],
            cut_shapes if first else [],
            cuts if first else nothing,
            number + piece,
            {len(used) + a: len(used) + b for a, b in aliases} if first else {},
            stages if first else [],
            puts if first else nothing,
            middle if first else nothing,
        )
        for i, out in zip(used, outs):
            results[i].append(out)
        if first:
            extra = outs[len(used) :]
    return [one[0] if len(one) == 1 else jnp.concatenate(one, axis=1) for one in results], extra


def dot(left, right, dims):
    return lax.dot_general(
        left, right, ((dims[:1], dims[1:]), ((), ())), preferred_element_type=jnp.float32
    )


def picks(slots_ref, number):
    pair = slots_ref.shape[2]
    rows = lax.broadcasted_iota(jnp.int32, (2 * CAP, pair), 0)
    return [slots_ref[0, e : e + 1, :] == rows for e in range(number)]


def pick_kernel(number, experts_all, slots_ref, x_ref, g_ref, router_ref, rows_ref, grows_ref, gates_ref):
    chosen = picks(slots_ref, number)
    pick = jnp.concatenate(chosen, axis=0).astype(jnp.bfloat16)
    size = 2 * CAP
    x = x_ref[...]
    logits = dot(router_ref[...], x, (0, 1))
    names = lax.broadcasted_iota(jnp.int32, logits.shape, 0)
    logits = jnp.where(names < experts_all, logits, -1e30)
    weights = jnp.exp(logits - jnp.max(logits, axis=0, keepdims=True))
    probs = weights / jnp.sum(weights, axis=0, keepdims=True)
    for e in range(number):
        gate = jnp.sum(jnp.where(chosen[e], probs[e : e + 1, :], 0.0), axis=1, keepdims=True)
        gates_ref[e] = jnp.broadcast_to(gate, (size, 128))
    picked = dot(pick, x, (1, 0)).astype(jnp.bfloat16)
    for e in range(number):
        rows_ref[e] = picked[e * size : (e + 1) * size]
    picked = dot(pick, g_ref[...], (1, 0)).astype(jnp.bfloat16)
    for e in range(number):
        grows_ref[e] = picked[e * size : (e + 1) * size]


def expert_kernel(steps, half, n_weights, n_into, n_pack, names_ref, x_ref, g_ref, gates_ref, *refs):
    weights, refs = refs[:n_weights], refs[n_weights:]
    down_ref, refs = refs[0], refs[1 + n_into :]
    (
        y_ref,
        dx_ref,
        probs_ref,
        dgate_ref,
        dup_ref,
        ddown_ref,
        *pack_refs,
        sum_gate,
        sum_up,
    ) = refs
    bf16 = jnp.bfloat16
    g = g_ref[0]
    rows, width = x_ref.shape[1:]
    part = dgate_ref.shape[2]
    gate = gates_ref[0][:, :1]
    if n_weights == 2:
        piece = 512
        gate_ref, up_ref = weights
        gate_mid = dot(x_ref[0], gate_ref[0], (1, 0))
        up_mid = dot(x_ref[0], up_ref[0], (1, 0))
        spans = [
            (pl.ds(at, piece), gate_ref, up_ref, pl.ds(at, piece), pl.ds(0, part), pl.ds(0, part))
            for at in range(0, width, piece)
        ]
    else:
        piece = width // n_weights
        spans = []
        gate_mid = up_mid = 0.0
        for n, ref in enumerate(weights):
            span = pl.ds(pl.multiple_of(names_ref[1 + n], piece), piece)
            x_part = x_ref[0, :, span]
            gate_mid = gate_mid + dot(x_part, ref[0, :, :part], (1, 0))
            up_mid = up_mid + dot(x_part, ref[0, :, part:], (1, 0))
            spans.append((span, ref, ref, pl.ds(0, piece), pl.ds(0, part), pl.ds(part, part)))
    sigmoid = 1.0 / (1.0 + jnp.exp(-gate_mid))
    silu = gate_mid * sigmoid
    hidden = silu * up_mid
    hidden_low = hidden.astype(bf16)
    grad_plain = dot(g, down_ref[0], (1, 1))
    grad_gates = jnp.sum(grad_plain * hidden_low.astype(jnp.float32), axis=1, keepdims=True)
    high = grad_gates.astype(bf16).astype(jnp.float32)
    lane = lax.broadcasted_iota(jnp.int32, (rows, 128), 1)
    name = names_ref[0] + pl.program_id(0)
    probs_ref[0] = (
        jnp.where(lane == name, high, 0.0) + jnp.where(lane == name + half, grad_gates - high, 0.0)
    ).astype(bf16)
    grad_hidden = grad_plain * gate
    grad_gate = (
        grad_hidden * up_mid * sigmoid * (1.0 + gate_mid * (1.0 - sigmoid))
    ).astype(bf16)
    grad_up = (grad_hidden * silu).astype(bf16)
    scaled = (hidden * gate).astype(bf16)
    for at in range(0, width, piece):
        y_ref[0, :, at : at + piece] = (
            dot(hidden_low, down_ref[0, :, at : at + piece], (1, 0)) * gate
        ).astype(bf16)
    for span, gate_ref, up_ref, here, gate_columns, up_columns in spans:
        dx_ref[0, :, span] = (
            dot(grad_gate, gate_ref[0, here, gate_columns], (1, 1))
            + dot(grad_up, up_ref[0, here, up_columns], (1, 1))
        ).astype(bf16)
    step = pl.program_id(1)
    for span, *unused in spans:
        x_part = x_ref[0, :, span]
        here_gate = dot(x_part, grad_gate, (0, 0))
        here_up = dot(x_part, grad_up, (0, 0))
        here_down = dot(scaled, g_ref[0, :, span], (0, 0))
        if steps == 1:
            dgate_ref[0, span, :] = here_gate.astype(bf16)
            dup_ref[0, span, :] = here_up.astype(bf16)
            ddown_ref[0, :, span] = here_down
            continue

        @pl.when(step == 0)
        def _():
            sum_gate[span, :] = here_gate
            sum_up[span, :] = here_up
            ddown_ref[0, :, span] = here_down

        @pl.when(step > 0)
        def _():
            sum_gate[span, :] += here_gate
            sum_up[span, :] += here_up
            ddown_ref[0, :, span] += here_down

        @pl.when(step == steps - 1)
        def _():
            dgate_ref[0, span, :] = sum_gate[span, :].astype(bf16)
            dup_ref[0, span, :] = sum_up[span, :].astype(bf16)

    if n_pack:

        @pl.when((step == steps - 1) & (pl.program_id(0) < n_pack))
        def _():
            pack_ref = pack_refs[0]
            depth = pack_ref.shape[2]
            for plane in range(pack_ref.shape[0]):
                here = pl.ds(plane * depth, depth)
                pack_ref[plane, 0, :, :part] = dgate_ref[0, here, :]
                pack_ref[plane, 0, :, part:] = dup_ref[0, here, :]


def put_back(number, slots_ref, pairs):
    pick = jnp.concatenate(picks(slots_ref, number), axis=0).astype(jnp.bfloat16)
    piece = 512
    for source, target, first in pairs:
        width = source.shape[2]
        for at in range(0, width, piece):
            size = min(piece, width)
            part = source[:, :, at : at + size].reshape(-1, size)
            target[:, first + at : first + at + size] = dot(pick, part, (0, 0)).astype(
                jnp.bfloat16
            )


def place_back_kernel(number, slots_ref, dx_ref, probs_ref, back_ref):
    put_back(number, slots_ref, [(dx_ref, back_ref, 0), (probs_ref, back_ref, dx_ref.shape[2])])


def place_out_kernel(number, slots_ref, y_ref, out_ref):
    put_back(number, slots_ref, [(y_ref, out_ref, 0)])


def place_out(slots, y, out):
    pairs, number, pair = slots.shape
    pltpu.emit_pipeline(
        functools.partial(place_out_kernel, number),
        grid=(pairs,),
        in_specs=[
            pl.BlockSpec((1, number, pair), lambda p: (p, 0, 0)),
            pl.BlockSpec((number, 2 * CAP, D), lambda p: (0, p, 0)),
        ],
        out_specs=[pl.BlockSpec((pair, D), lambda p: (p, 0))],
    )(slots, y, out)


def pick_shapes(number, pairs):
    bf16 = jnp.bfloat16
    size = 2 * CAP
    return [
        jax.ShapeDtypeStruct((number, pairs * size, D), bf16),
        jax.ShapeDtypeStruct((number, pairs * size, D), bf16),
        jax.ShapeDtypeStruct((number, pairs * size, 128), jnp.float32),
    ]


def pick_rows(number, experts_all, slots, x_all, g_all, router, rows, grows, gates):
    pairs, _, pair = slots.shape
    size = 2 * CAP
    tokens = pl.BlockSpec((pair, D), lambda p: (p, 0))
    picked = pl.BlockSpec((number, size, D), lambda p: (0, p, 0))
    pltpu.emit_pipeline(
        functools.partial(pick_kernel, number, experts_all),
        grid=(pairs,),
        in_specs=[
            pl.BlockSpec((1, number, pair), lambda p: (p, 0, 0)),
            tokens,
            tokens,
            pl.BlockSpec(router.shape, lambda p: (0, 0)),
        ],
        out_specs=[picked, picked, pl.BlockSpec((number, size, 128), lambda p: (0, p, 0))],
    )(slots, x_all, g_all, router, rows, grows, gates)


def expert_call(names, half, low, number, rows, grows, gates, weights, down, into=(), pack=()):
    total, depth, _ = rows.shape
    part = down.shape[1]
    size = depth
    while size > 768:
        size //= 2
    steps = depth // size
    bf16 = jnp.bfloat16
    f32 = jnp.float32

    def from_rows(width):
        return pl.BlockSpec((1, size, width), lambda e, r: (e + low, r, 0))

    def whole(*shape):
        return pl.BlockSpec((1, *shape), lambda e, r: (e, 0, 0))

    def from_whole(*shape):
        return pl.BlockSpec((1, *shape), lambda e, r: (e + low, 0, 0))

    packed = [
        pl.BlockSpec(
            (planes, 1, D // planes, 2 * part),
            lambda e, r, n=n: (0, lax.min(e, n - 1), 0, 0),
        )
        for n, planes in ([pack] if pack else [])
    ]
    keep = (D, part) if steps > 1 else (16, 128)
    return pl.pallas_call(
        functools.partial(
            expert_kernel, steps, half, len(weights), len(into), pack[0] if pack else 0
        ),
        grid=(number, steps),
        in_specs=[
            pl.BlockSpec(memory_space=pltpu.SMEM),
            from_rows(D),
            from_rows(D),
            from_rows(128),
            *[(from_whole if len(weights) == 2 else whole)(*one.shape[1:]) for one in weights],
            from_whole(part, D),
            *[pl.BlockSpec(memory_space=pl.ANY)] * len(into),
        ],
        out_specs=[
            from_rows(D),
            from_rows(D),
            from_rows(128),
            whole(D, part),
            whole(D, part),
            from_whole(part, D),
            *packed,
        ],
        out_shape=[
            jax.ShapeDtypeStruct((total, depth, D), bf16),
            jax.ShapeDtypeStruct((total, depth, D), bf16),
            jax.ShapeDtypeStruct((total, depth, 128), bf16),
            jax.ShapeDtypeStruct((number, D, part), bf16),
            jax.ShapeDtypeStruct((number, D, part), bf16),
            jax.ShapeDtypeStruct((total, part, D), f32),
            *[
                jax.ShapeDtypeStruct((planes, n, D // planes, 2 * part), bf16)
                for n, planes in ([pack] if pack else [])
            ],
        ],
        input_output_aliases={
            5 + len(weights) + i: out for i, out in zip(range(len(into)), (0, 1, 2, 5))
        },
        scratch_shapes=[pltpu.VMEM(keep, f32), pltpu.VMEM(keep, f32)],
        compiler_params=pltpu.CompilerParams(vmem_limit_bytes=BIG),
    )(names, rows, grows, gates, *weights, down, *into)


def place_back(slots, dx, probs):
    pairs, number, pair = slots.shape
    size = 2 * CAP

    def rows(one):
        return pl.BlockSpec((number, size, one.shape[2]), lambda p: (0, p, 0))

    return pl.pallas_call(
        functools.partial(place_back_kernel, number),
        grid=(pairs,),
        in_specs=[pl.BlockSpec((1, number, pair), lambda p: (p, 0, 0)), rows(dx), rows(probs)],
        out_specs=pl.BlockSpec((pair, D + 128), lambda p: (p, 0)),
        out_shape=jax.ShapeDtypeStruct((pairs * pair, D + 128), jnp.bfloat16),
        compiler_params=pltpu.CompilerParams(vmem_limit_bytes=BIG),
    )(slots, dx, probs)


def widen_kernel(*refs):
    half = len(refs) // 2
    for source, target in zip(refs[:half], refs[half:]):
        target[...] = source[...].astype(jnp.float32)


def widen(spans, values):
    number, rows, columns = values[0].shape
    (low, high), (again, end) = spans

    def chosen(e):
        return (jnp.where(e < high - low, e + low, e - (high - low) + again), 0, 0)

    block = pl.BlockSpec((1, rows, columns), chosen)
    return pl.pallas_call(
        widen_kernel,
        grid=(high - low + end - again,),
        in_specs=[block] * len(values),
        out_specs=[block] * len(values),
        out_shape=[jax.ShapeDtypeStruct(one.shape, jnp.float32) for one in values],
        compiler_params=pltpu.CompilerParams(vmem_limit_bytes=BIG),
    )(*values)


def widen_pieces_kernel(low, n_pieces, offsets_ref, *refs):
    pieces, refs = refs[:n_pieces], refs[n_pieces + 2 :]
    targets, wide, sems = refs[:2], refs[2], refs[3]
    part = wide.shape[4]
    copies = []
    for k, piece in enumerate(pieces):
        columns = pl.ds(pl.multiple_of(offsets_ref[k], part), part)
        for n in range(2):
            wide[k, n] = piece[:, :, n * part : (n + 1) * part].astype(jnp.float32)
            copy = pltpu.make_async_copy(
                wide.at[k, n], targets[n].at[pl.ds(low, piece.shape[0]), :, columns], sems.at[k, n]
            )
            copy.start()
            copies.append(copy)
    for copy in copies:
        copy.wait()


def widen_pieces(offsets, low, pieces, into):
    size, rows, columns = pieces[0].shape
    anywhere = pl.BlockSpec(memory_space=pl.ANY)
    count = len(pieces)
    return pl.pallas_call(
        functools.partial(widen_pieces_kernel, low, count),
        in_specs=[
            pl.BlockSpec(memory_space=pltpu.SMEM),
            *[pl.BlockSpec(memory_space=pltpu.VMEM)] * count,
            anywhere,
            anywhere,
        ],
        out_specs=[anywhere, anywhere],
        out_shape=[jax.ShapeDtypeStruct(one.shape, one.dtype) for one in into],
        scratch_shapes=[
            pltpu.VMEM((count, 2, size, rows, columns // 2), jnp.float32),
            pltpu.SemaphoreType.DMA((count, 2)),
        ],
        input_output_aliases={1 + count: 0, 2 + count: 1},
        compiler_params=pltpu.CompilerParams(vmem_limit_bytes=BIG),
    )(offsets, *pieces, *into)


def shards(
    n_dp,
    n_expert,
    tokens,
    cotangent,
    lengths,
    routes,
    w_query,
    w_key,
    w_value,
    w_out,
    w_router,
    gain_attn,
    gain_query,
    gain_key,
    gain_mlp,
    w_gate,
    w_up,
    w_down,
):
    groups = n_dp * n_expert
    bf16 = jnp.bfloat16
    number = w_gate.shape[0]
    ff = w_gate.shape[2]
    part = ff // n_dp
    experts_all = w_router.shape[1]
    width = 128
    small = jnp.concatenate(
        [
            w_router,
            gain_attn[:, None],
            gain_query[:, None],
            gain_key[:, None],
            gain_mlp[:, None],
            jnp.zeros((w_router.shape[0], width - experts_all - 4), bf16),
        ],
        axis=1,
    )
    hits = jnp.any(
        routes[:, :, None] == jnp.arange(width, dtype=jnp.int32)[None, None, :], axis=1
    ).astype(bf16)
    count = tokens.shape[0]
    rows_each = w_query.shape[0]
    extras = jnp.concatenate([hits, jnp.pad(small, ((0, count - rows_each), (0, 0)))], axis=1)
    weights = jnp.stack([w_query, w_key, w_value, w_out])
    depth = w_gate.shape[1]
    early = number // 4
    beside = early + number // 8
    late = number - number // 4
    back_beside = number // 8
    back_third = back_beside + max(number // 4, 1)
    back_late = back_third + number // 4
    me = lax.axis_index("dp")
    cut_shape = jax.ShapeDtypeStruct((number, n_dp * depth, part), bf16)

    def row_block(size):
        return lambda ref, block: ref.at[pl.ds(pl.multiple_of(block * size, 16), size)]

    def columns_at(at):
        return pl.ds(pl.multiple_of(at * part, part), part)

    def rows_at(at):
        return pl.ds(pl.multiple_of(at * depth, depth), depth)

    def recut(low, high):
        def cuts(ins, outs):
            def pair(n):
                chosen = pl.ds(low, high - low)
                return (
                    lambda to: ins[n].at[chosen, :, columns_at(to)],
                    lambda at: outs[n].at[chosen, rows_at(at)],
                )

            return [pair(0), pair(1)]

        return cuts

    to_plane, from_plane = partners(me, n_dp)

    def permuted(pieces, chained=False):
        got = []
        for k, piece in enumerate(pieces, 1):
            if chained and got:
                piece, last = lax.optimization_barrier((piece, got.pop()))
                got.append(last)
            paths = [(i, partners(i, n_dp)[0](k)) for i in range(n_dp)]
            got.append(lax.ppermute(piece, "dp", paths))
        return got

    def cut_pieces(low, high, first_k, ins, outs):
        to, unused = partners(lax.axis_index("dp"), n_dp)
        pairs = []
        for k, piece in enumerate(outs, first_k):
            for n in range(2):
                source = ins[n].at[pl.ds(low, high - low), :, columns_at(to(k))]
                pairs.append((source, piece.at[:, :, pl.ds(n * part, part)]))
        return pairs

    def piece_shapes(size, first_k):
        shape = jax.ShapeDtypeStruct((size, depth, 2 * part), bf16)
        return [shape] * (n_dp - first_k if size else 0)

    def stages(*sizes):
        return [(size, depth, part) for size in sizes]

    soon_shapes = piece_shapes(beside - early, 1)
    late_shapes = piece_shapes(number - late, 0)
    n_soon = len(soon_shapes)

    weights_all, extras_all, gate_early, up_early, *pieces = gather_call(
        n_dp,
        n_expert,
        [weights, extras],
        [
            jax.ShapeDtypeStruct((4, groups * rows_each, D), bf16),
            jax.ShapeDtypeStruct((groups * count, 2 * width), bf16),
        ],
        [
            lambda ref, block: ref.at[
                :, pl.ds(pl.multiple_of(block * rows_each, 16), rows_each)
            ],
            row_block(count),
        ],
        [w_gate, w_up],
        [cut_shape, cut_shape, *soon_shapes, *late_shapes],
        recut(0, early),
        {},
        0,
        stages(
            *[early] * 2,
            *[beside - early] * (2 * n_soon),
            *[number - late] * (2 * n_dp),
        ),
        lambda ins, outs: cut_pieces(early, beside, 1, ins, outs[2 : 2 + n_soon])
        + cut_pieces(late, number, 0, ins, outs[2 + n_soon :]),
    )
    soon_pieces, late_pieces = pieces[:n_soon], pieces[n_soon:]
    query_weight, key_weight, value_weight, out_weight = (weights_all[i] for i in range(4))
    small_all = (
        extras_all[:, width:].reshape(groups, count, width)[:, :rows_each].reshape(-1, width)
    )
    hits_all = extras_all[:, :experts_all]
    router_weight = small_all[:, :experts_all]
    gains = small_all[:, experts_all : experts_all + 4].astype(jnp.float32)
    attn_gain, query_gain, key_gain, mlp_gain = (gains[:, i] for i in range(4))
    inputs = tokens.astype(jnp.float32)
    segment, position, places = layout(lengths[0], count)
    half = HD // 2
    freq = 10000.0 ** (-2.0 * jnp.arange(half, dtype=jnp.float32) / HD)
    angle = position.astype(jnp.float32)[:, None] * freq[None, :]
    cosine = jnp.cos(angle)[:, None, :]
    sine = jnp.sin(angle)[:, None, :]
    scale = HD ** (-0.5)
    normed, attn_inverse = rms_forward(inputs, attn_gain)
    normed_low = normed.astype(bf16)
    query_raw = product(normed_low, query_weight, "td,de->te")
    key_raw = product(normed_low, key_weight, "td,de->te")
    value_low = product(normed_low, value_weight, "td,de->te").astype(bf16)
    query_normed, query_inverse = rms_forward(query_raw, query_gain)
    key_normed, key_inverse = rms_forward(key_raw, key_gain)
    query_low = rotate(query_normed, cosine, sine).astype(bf16).reshape(count, HEADS, HD)
    key_low = rotate(key_normed, cosine, sine).astype(bf16).reshape(count, HEADS, HD)
    value_heads = value_low.reshape(count, HEADS, HD)
    allowed = (segment[:, None] == segment[None, :]) & (places[None, :] <= places[:, None])
    scores = product(query_low, key_low, "qhd,khd->hqk") * scale
    scores = jnp.where(allowed[None], scores, -1e30)
    probs = jax.nn.softmax(scores, axis=-1)
    probs_low = probs.astype(bf16)
    attended_low = product(probs_low, value_heads, "hqk,khd->qhd").reshape(count, D).astype(bf16)
    middle = inputs + product(attended_low, out_weight, "td,de->te")
    mlp_normed, mlp_inverse = rms_forward(middle, mlp_gain)
    mlp_low = mlp_normed.astype(bf16)
    router = jax.nn.softmax(product(mlp_low, router_weight, "td,de->te"), axis=-1)

    first = lax.axis_index("expert") * number
    hit = lax.dynamic_slice_in_dim(hits_all, first, number, 1).reshape(groups, count, number)
    before = jnp.tril(jnp.ones((count, count), bf16), -1)
    slot = product(before, hit, "ts,bse->bet").astype(jnp.int32)
    slot = jnp.where(jnp.transpose(hit, (0, 2, 1)) > 0, slot, -1)
    slot = slot.reshape(groups // 2, 2, number, count)
    shift = jnp.array([0, CAP], jnp.int32)[None, :, None, None]
    slots = jnp.transpose(jnp.where(slot < 0, -1, slot + shift), (0, 2, 1, 3))
    slots = slots.reshape(groups // 2, number, 2 * count)
    router_own = jnp.pad(
        jnp.roll(router_weight, -first, axis=1), ((0, 0), (0, width - experts_all))
    )
    if n_soon:
        mlp_low, *soon_pieces = lax.optimization_barrier((mlp_low, *permuted(soon_pieces)))

    def put_weights(ins, outs):
        chosen = pl.ds(early, beside - early)
        unused, heard = partners(lax.axis_index("dp"), n_dp)
        pairs = []
        if beside > early:
            own = lax.axis_index("dp")
            for n in range(2):
                source = ins[n].at[chosen, :, columns_at(own)]
                pairs.append((source, outs[n].at[chosen, rows_at(own)]))
        for k, piece in enumerate(ins[6:], 1):
            for n in range(2):
                columns = piece.at[:, :, pl.ds(n * part, part)]
                pairs.append((columns, outs[n].at[chosen, rows_at(heard(k))]))
        return pairs

    def pick_all(items, ins, outs):
        pick_rows(number, experts_all, ins[4], *items, ins[5], *outs[2:])

    unused, unused, gate_cut, up_cut, rows, grows, gates = gather_call(
        n_dp,
        n_expert,
        [mlp_low, cotangent],
        [jax.ShapeDtypeStruct((groups * count, D), bf16)] * 2,
        [row_block(count)] * 2,
        [w_gate, w_up, gate_early, up_early, slots, router_own, *soon_pieces],
        [cut_shape, cut_shape, *pick_shapes(number, groups // 2)],
        recut(beside, late),
        {4: 2, 5: 3},
        1,
        stages(*[late - beside] * 2, *[beside - early] * (2 * n_dp if n_soon else 0)),
        put_weights,
        pick_all,
    )
    *late_pieces, rows = lax.optimization_barrier((*late_pieces, rows))
    late_pieces = [late_pieces[0], *permuted(late_pieces[1:])]
    packing = back_beside > 0 and depth == 512
    *outs, gate_soon, up_soon, down_soon = expert_call(
        first[None],
        experts_all,
        0,
        late,
        rows,
        grows,
        gates,
        [gate_cut, up_cut],
        w_down,
        pack=(back_beside, n_dp) if packing else (),
    )
    if packing:
        *outs, gate_soon, up_soon, down_soon, packed = [*outs, gate_soon, up_soon, down_soon]
    offsets = [from_plane(k) * depth for k in range(n_dp)]
    weighted, grad_rows, grad_gates, gate_rest, up_rest, grad_down_part = expert_call(
        jnp.stack([first + late, *offsets]),
        experts_all,
        late,
        number - late,
        rows,
        grows,
        gates,
        late_pieces,
        w_down,
        [*outs, down_soon],
    )
    part_back = place_back(slots, grad_rows, grad_gates)

    def ways(low, high, at, ins, outs):
        def pair(n):
            return (
                lambda to: ins[n].at[pl.ds(low, high - low), rows_at(to)],
                lambda here: outs[n].at[pl.ds(low + at, high - low), :, columns_at(here)],
            )

        return [pair(0), pair(1)]

    def cut_grads(low, high, ins, outs):
        to, unused = partners(lax.axis_index("dp"), n_dp)
        pairs = []
        for k, piece in enumerate(outs, 1):
            for n in range(2):
                source = ins[n].at[pl.ds(low, high - low), rows_at(to(k))]
                pairs.append((source, piece.at[:, :, pl.ds(n * part, part)]))
        return pairs

    pieces = []
    if back_beside:
        for k in range(1, n_dp):
            if packing:
                piece = lax.dynamic_index_in_dim(packed, to_plane(k), 0, False)
            else:
                piece = jnp.concatenate(
                    [
                        lax.dynamic_slice_in_dim(
                            one[:back_beside], to_plane(k) * depth, depth, 1
                        )
                        for one in (gate_soon, up_soon)
                    ],
                    axis=2,
                )
            pieces.append(piece)
        ahead = lax.optimization_barrier((*pieces, *late_pieces[1:]))
        pieces = permuted(ahead[: n_dp - 1])
        part_back, *pieces = lax.optimization_barrier((part_back, *pieces))
    way_shapes = [jax.ShapeDtypeStruct((number, depth, ff), bf16)] * 2
    piece_shape = jax.ShapeDtypeStruct((back_late - back_third, depth, 2 * part), bf16)
    (back,), (gate_third, up_third, part_out, *later_pieces) = scatter_all(
        n_dp,
        n_expert,
        [part_back.reshape(n_dp, n_expert, count, D + width)],
        [4],
        [gate_soon, up_soon, slots, weighted],
        [
            *way_shapes,
            jax.ShapeDtypeStruct((groups * count, D), bf16),
            *[piece_shape] * (n_dp - 1),
        ],
        lambda ins, outs: ways(back_beside, back_third, 0, ins, outs),
        8,
        (),
        stages(
            *[back_third - back_beside] * 2, *[back_late - back_third] * (2 * (n_dp - 1))
        ),
        lambda ins, outs: cut_grads(back_third, back_late, ins, outs[3:]),
        lambda ins, outs: place_out(ins[2], ins[3], outs[2]),
    )
    later_pieces = permuted(later_pieces)

    def attention_back(back):
        query_weight, key_weight, value_weight, out_weight = (weights_all[i] for i in range(4))
        grad_final = cotangent.astype(jnp.float32)
        grad_mlp = back[:, :D]
        grad_router_probs = back[:, D : D + experts_all] + back[:, D + experts_all :]
        grad_logits = router * (
            grad_router_probs - jnp.sum(router * grad_router_probs, axis=1, keepdims=True)
        )
        grad_logits_low = grad_logits.astype(bf16)
        grad_router_full = product(mlp_low, grad_logits_low, "td,te->de")
        grad_mlp = grad_mlp + product(grad_logits_low, router_weight, "te,de->td")
        grad_middle_part, grad_mlp_gain = rms_backward(middle, mlp_inverse, mlp_gain, grad_mlp)
        grad_middle = grad_final + grad_middle_part
        grad_branch_low = grad_middle.astype(bf16)
        grad_out_full = product(attended_low, grad_branch_low, "td,te->de")
        grad_attended = (
            product(grad_branch_low, out_weight, "te,de->td").astype(bf16).reshape(count, HEADS, HD)
        )
        grad_weights = product(grad_attended, value_heads, "qhd,khd->hqk")
        grad_scores = probs * (grad_weights - jnp.sum(probs * grad_weights, axis=-1, keepdims=True))
        grad_scores_low = grad_scores.astype(bf16)
        grad_query_turn = product(grad_scores_low, key_low, "hqk,khd->qhd").reshape(count, D) * scale
        grad_key_turn = product(grad_scores_low, query_low, "hqk,qhd->khd").reshape(count, D) * scale
        grad_value_low = (
            product(probs_low, grad_attended, "hqk,qhd->khd").reshape(count, D).astype(bf16)
        )
        grad_query_raw, grad_query_gain = rms_backward(
            query_raw, query_inverse, query_gain, rotate(grad_query_turn, cosine, -sine)
        )
        grad_key_raw, grad_key_gain = rms_backward(
            key_raw, key_inverse, key_gain, rotate(grad_key_turn, cosine, -sine)
        )
        grad_query_low = grad_query_raw.astype(bf16)
        grad_key_low = grad_key_raw.astype(bf16)
        grad_query_full = product(normed_low, grad_query_low, "td,te->de")
        grad_key_full = product(normed_low, grad_key_low, "td,te->de")
        grad_value_full = product(normed_low, grad_value_low, "td,te->de")
        grad_normed = (
            product(grad_query_low, query_weight, "te,de->td")
            + product(grad_key_low, key_weight, "te,de->td")
            + product(grad_value_low, value_weight, "te,de->td")
        )
        grad_inputs_part, grad_attn_gain = rms_backward(inputs, attn_inverse, attn_gain, grad_normed)
        grad_inputs = grad_middle + grad_inputs_part

        small_grads = jnp.concatenate(
            [
                grad_router_full,
                grad_attn_gain[:, None],
                grad_query_gain[:, None],
                grad_key_gain[:, None],
                grad_mlp_gain[:, None],
                jnp.zeros((D, width - experts_all - 4), jnp.float32),
            ],
            axis=1,
        )
        grads = (grad_out_full, grad_value_full, grad_key_full, grad_query_full, small_grads)
        return grad_inputs, *[one.astype(bf16) for one in grads]

    def unreached(back):
        shapes = [(count, D)] + [(D, D)] * 4 + [(D, width)]
        kinds = [jnp.float32] + [bf16] * 5
        return tuple(jnp.zeros(shape, kind) for shape, kind in zip(shapes, kinds))

    grad_inputs, *weight_grads = lax.cond(lengths[0, 0] > 0, attention_back, unreached, back)

    def blocks_of(value):
        return value.reshape(n_dp, n_expert, rows_each, -1)

    sums, (gate_back, up_back) = scatter_all(
        n_dp,
        n_expert,
        [part_out.reshape(n_dp, n_expert, count, D)]
        + [blocks_of(value) for value in weight_grads],
        [2] + [1] * len(weight_grads),
        [gate_third, up_third, gate_soon, up_soon, gate_rest, up_rest],
        way_shapes,
        lambda ins, outs: ways(back_late, late, 0, ins[2:4], outs)
        + ways(0, number - late, late, ins[4:6], outs),
        16,
        ((0, 0), (1, 1)),
        [],
    )
    summed, grad_out_part, grad_value_part, grad_key_part, grad_query_part, small_part = sums
    output = (middle + summed).astype(bf16)
    grad_router_part = small_part[:, :experts_all]
    gain_parts = [small_part[:, experts_all + i] for i in range(4)]
    widened = widen([(back_beside, back_third), (back_late, number)], [gate_back, up_back])
    offsets = jnp.stack([from_plane(k) * part for k in range(n_dp)])
    for low, high, others in (
        (0, back_beside, pieces),
        (back_third, back_late, later_pieces),
    ):
        if high > low:
            own = jnp.concatenate(
                [
                    lax.dynamic_slice_in_dim(one[low:high], me * depth, depth, 1)
                    for one in (gate_soon, up_soon)
                ],
                axis=2,
            )
            widened = widen_pieces(offsets, low, [own, *others], widened)
    grad_gate_part, grad_up_part = widened
    return (
        output,
        grad_inputs,
        grad_query_part,
        grad_key_part,
        grad_value_part,
        grad_out_part,
        grad_router_part,
        gain_parts[0],
        gain_parts[1],
        gain_parts[2],
        gain_parts[3],
        grad_gate_part,
        grad_up_part,
        grad_down_part,
    )


def solution(mesh):
    return jax.shard_map(
        functools.partial(shards, mesh.shape["dp"], mesh.shape["expert"]),
        mesh=mesh,
        in_specs=(
            P(("dp", "expert"), None),
            P(("dp", "expert"), None),
            P(("dp", "expert"), None),
            P(("dp", "expert"), None),
            P(("dp", "expert"), None),
            P(("dp", "expert"), None),
            P(("dp", "expert"), None),
            P(("dp", "expert"), None),
            P(("dp", "expert"), None),
            P(("dp", "expert")),
            P(("dp", "expert")),
            P(("dp", "expert")),
            P(("dp", "expert")),
            P("expert", "dp", None),
            P("expert", "dp", None),
            P("expert", "dp", None),
        ),
        out_specs=(
            P(("dp", "expert"), None),
            P(("dp", "expert"), None),
            P(("dp", "expert"), None),
            P(("dp", "expert"), None),
            P(("dp", "expert"), None),
            P(("dp", "expert"), None),
            P(("dp", "expert"), None),
            P(("dp", "expert")),
            P(("dp", "expert")),
            P(("dp", "expert")),
            P(("dp", "expert")),
            P("expert", "dp", None),
            P("expert", "dp", None),
            P("expert", "dp", None),
        ),
        check_vma=False,
    )
```

```python
import functools

import jax
import jax.numpy as jnp
from jax import lax
from jax.experimental import pallas as pl
from jax.experimental.pallas import tpu as pltpu
from jax.sharding import PartitionSpec as P

D = 2048
HEADS = 16
HD = 128
TOPK = 8
CAP = 24


eps = 1e-05


def product(left, right, form):
    return jnp.einsum(form, left, right, preferred_element_type=jnp.float32)


def rms_forward(values, gain):
    inverse = lax.rsqrt(jnp.mean(values * values, axis=-1, keepdims=True) + eps)
    return (values * inverse * gain, inverse)


def rms_backward(values, inverse, gain, grad):
    scaled = grad * gain
    inner = jnp.mean(scaled * values, axis=-1, keepdims=True)
    grad_values = inverse * scaled - values * (inverse * inverse * inverse) * inner
    grad_gain = jnp.sum(grad * values * inverse, axis=0)
    return (grad_values, grad_gain)


def layout(lengths_row, count):
    places = jnp.arange(count, dtype=jnp.int32)
    ends = jnp.cumsum(lengths_row, dtype=jnp.int32)
    passed = (places[:, None] >= ends[None, :]).astype(jnp.int32)
    segment = jnp.sum(passed, axis=1, dtype=jnp.int32)
    start = jnp.sum(passed * lengths_row[None, :], axis=1, dtype=jnp.int32)
    return (segment, places - start, places)


def rotate(values, cosine, sine):
    count = values.shape[0]
    heads = values.reshape(count, HEADS, HD)
    half = HD // 2
    first = heads[..., :half]
    second = heads[..., half:]
    turned = jnp.concatenate(
        [first * cosine - second * sine, second * cosine + first * sine], axis=-1
    )
    return turned.reshape(count, D)


MESH = pl.DeviceIdType.MESH
BIG = 60 * 1024 * 1024


def place_of():
    z = lax.axis_index("dp")
    j = lax.axis_index("expert")
    return z, j, j // 2, j % 2


def other_chips(chip, chips):
    if chips == 4:
        square = [chip, chip + 1 - 2 * (chip % 2), chip + 2 - 4 * (chip // 2), 3 - chip]
        return lambda k: square[k], lambda k: square[k]
    return lambda k: (chip + k) % chips, lambda k: (chip + chips - k) % chips


def partners(z, n_dp):
    if n_dp == 4:
        pairs = [z, 3 - z, (z + 2) % 4, z + 1 - 2 * (z % 2)]
        return lambda k: pairs[k], lambda k: pairs[k]
    return lambda k: (z + k) % n_dp, lambda k: (z + n_dp - k) % n_dp


def greet(n_dp, n_expert):
    z, j, chip, core = place_of()
    chips = n_expert // 2
    barrier = pltpu.get_barrier_semaphore()
    for k in range(1, n_dp):
        pl.semaphore_signal(
            barrier, inc=1, device_id=((z + k) % n_dp, j), device_id_type=MESH
        )
    for k in range(1, chips):
        other = ((chip + k) % chips) * 2 + core
        pl.semaphore_signal(barrier, inc=1, device_id=(z, other), device_id_type=MESH)
    pl.semaphore_signal(
        barrier, inc=1, device_id=(z, chip * 2 + 1 - core), device_id_type=MESH
    )
    pl.semaphore_wait(barrier, n_dp - 1 + chips - 1 + 1)


def remote(source, target, send, receive, device):
    return pltpu.make_async_remote_copy(
        src_ref=source,
        dst_ref=target,
        send_sem=send,
        recv_sem=receive,
        device_id=device,
        device_id_type=MESH,
    )


def exchange(n_dp, pairs, send, receive):
    z, j, chip, core = place_of()
    to_plane, unused = partners(z, n_dp)
    copies = []
    for i, (source, target) in enumerate(pairs):
        for k in range(1, n_dp):
            to = to_plane(k)
            copies.append(
                remote(source(to), target(z), send.at[i, k], receive.at[i, k], (to, j))
            )
    return copies


def moves(pairs, stages, local):
    if not stages:
        copies = [
            pltpu.make_async_copy(source, target, local.at[i, 0])
            for i, (source, target) in enumerate(pairs)
        ]
        for copy in copies:
            copy.start()
        return [], copies
    bring = [
        pltpu.make_async_copy(source, stages[i], local.at[i, 0])
        for i, (source, target) in enumerate(pairs)
    ]
    put = [
        pltpu.make_async_copy(stages[i], target, local.at[i, 1])
        for i, (source, target) in enumerate(pairs)
    ]
    return bring, put


def nothing(ins, outs):
    return []


def gather_kernel(
    n_dp, n_expert, n_items, places, cuts, puts, finish, n_cut, n_out, n_stages, *refs
):
    z, j, chip, core = place_of()
    chips = n_expert // 2
    square = chips == 4
    to_chip, from_chip = other_chips(chip, chips)
    sources = refs[:n_items]
    cut_in = refs[n_items : n_items + n_cut]
    at = n_items + n_cut
    targets = refs[at : at + n_items]
    cut_out = refs[at + n_items : at + n_items + n_out]
    (
        send_c,
        recv_c,
        send_b,
        recv_b,
        send_a,
        recv_a,
        local,
        send_x,
        recv_x,
        local_y,
        *stages,
    ) = refs[at + n_items + n_out :]
    greet(n_dp, n_expert)
    mate = (z, chip * 2 + 1 - core)
    near = (1, 2) if square else tuple(range(1, chips))

    def slot(i, plane, column):
        return places[i](targets[i], plane * n_expert + column)

    def pass_on(i, plane, source, column, k, chip_to):
        return remote(
            source,
            slot(i, plane, column),
            send_b.at[i, plane, k],
            recv_b.at[i, plane, k],
            (z, chip_to * 2 + core),
        )

    def hand(i, plane, source):
        for k in near:
            pass_on(i, plane, source, j, k, to_chip(k)).start()
        remote(
            source, slot(i, plane, j), send_a.at[i, plane, 0], recv_a.at[i, plane, 0], mate
        ).start()

    def along(i, plane, source, way, step):
        return remote(
            source, slot(i, plane, j), send_c.at[i, way, plane], recv_c.at[i, plane], (z + step, j)
        )

    def at_distance(d, body):
        if d == 0:
            body(z, 0)
            return

        @pl.when(z >= d)
        def _():
            body(z - d, 0)

        @pl.when(z + d < n_dp)
        def _():
            body(z + d, 1)

    for i in range(n_items):

        @pl.when(z < n_dp - 1)
        def _():
            along(i, z, sources[i], 0, 1).start()

        @pl.when(z > 0)
        def _():
            along(i, z, sources[i], 1, -1).start()

        hand(i, z, sources[i])
        pltpu.make_async_copy(sources[i], slot(i, z, j), local.at[i]).start()

    def relay(plane, way):
        step = -1 if way else 1
        for i in range(n_items):
            block = slot(i, plane, j)
            along(i, plane, block, way, step).wait_recv()

            @pl.when(z > 0 if way else z < n_dp - 1)
            def _():
                along(i, plane, block, way, step).start()

            hand(i, plane, block)

    for d in range(1, n_dp):
        at_distance(d, relay)
    pairs = cuts(cut_in, cut_out)
    copies = exchange(n_dp, pairs, send_x, recv_x)
    for copy in copies:
        copy.start()
    own = [(source(z), target(z)) for source, target in pairs]
    bring, put = moves(own + puts(cut_in, cut_out), stages, local_y)
    for copy in bring:
        copy.start()
    for one, other in zip(bring, put):
        one.wait()
        other.start()

    def arrive(i, plane, k):
        column = from_chip(k) * 2 + core
        block = slot(i, plane, column)
        pass_on(i, plane, block, column, k, chip).wait_recv()
        remote(block, block, send_a.at[i, plane, k], recv_a.at[i, plane, k], mate).start()
        return block, column

    def arrived(plane, way):
        for i in range(n_items):
            for k in near:
                block, column = arrive(i, plane, k)
                if square:

                    @pl.when(plane % 2 == k - 1)
                    def _():
                        pass_on(i, plane, block, column, 3, to_chip(3 - k)).start()

    def crossed(plane, way):
        for i in range(n_items):
            arrive(i, plane, 3)

    for d in range(n_dp):
        at_distance(d, arrived)
    if square:
        for d in range(n_dp):
            at_distance(d, crossed)

    for i in range(n_items):
        for plane in range(n_dp):
            for k in range(chips):
                column = (from_chip(k) if k else chip) * 2 + 1 - core
                block = slot(i, plane, column)
                remote(
                    block, block, send_a.at[i, plane, k], recv_a.at[i, plane, k], mate
                ).wait_recv()
        pltpu.make_async_copy(sources[i], slot(i, z, j), local.at[i]).wait()
    finish(targets, cut_in, cut_out)
    for i in range(n_items):
        for plane in range(n_dp):
            block = slot(i, plane, j)
            for k in range(1, chips):
                pass_on(i, plane, block, j, k, chip).wait_send()
            for k in range(chips):
                remote(
                    block, block, send_a.at[i, plane, k], recv_a.at[i, plane, k], mate
                ).wait_send()

            @pl.when((z < n_dp - 1) & (z >= plane))
            def _():
                along(i, plane, block, 0, 1).wait_send()

            @pl.when((z > 0) & (z <= plane))
            def _():
                along(i, plane, block, 1, -1).wait_send()

    for copy in copies + put:
        copy.wait()


def gather_call(
    n_dp,
    n_expert,
    items,
    shapes,
    places,
    cut_in,
    cut_shapes,
    cuts,
    aliases,
    number,
    stages,
    puts=nothing,
    finish=lambda items, ins, outs: None,
):
    chips = n_expert // 2
    n, m = len(items), len(cut_shapes)
    dma = pltpu.SemaphoreType.DMA
    anywhere = pl.BlockSpec(memory_space=pl.ANY)
    return pl.pallas_call(
        functools.partial(
            gather_kernel,
            n_dp,
            n_expert,
            n,
            places,
            cuts,
            puts,
            finish,
            len(cut_in),
            m,
            len(stages),
        ),
        out_shape=[*shapes, *cut_shapes],
        in_specs=[anywhere] * (n + len(cut_in)),
        out_specs=[anywhere] * (n + m),
        scratch_shapes=[
            dma((n, 2, n_dp)),
            dma((n, n_dp)),
            dma((n, n_dp, chips)),
            dma((n, n_dp, chips)),
            dma((n, n_dp, chips)),
            dma((n, n_dp, chips)),
            dma((n,)),
            dma((4, n_dp)),
            dma((4, n_dp)),
            dma((max(len(stages), 4), 2)),
            *[pltpu.VMEM(stage, jnp.bfloat16) for stage in stages],
        ],
        input_output_aliases=aliases,
        compiler_params=pltpu.CompilerParams(
            collective_id=number, has_side_effects=True, vmem_limit_bytes=BIG
        ),
    )(*items, *cut_in)


def scatter_kernel(
    n_dp, n_expert, n_arrays, items, n_cut, n_out, cuts, puts, middle, rings, n_rings, *refs
):
    n_items = len(items)
    z, j, chip, core = place_of()
    chips = n_expert // 2
    square = chips == 4
    to_chip, from_chip = other_chips(chip, chips)
    refs = list(refs)

    def take(count):
        taken = refs[:count]
        del refs[:count]
        return taken

    sources, cut_in, targets, cut_out = take(n_arrays), take(n_cut), take(n_arrays), take(n_out)
    ring, got_a, got_b, got_c = take(n_rings), take(n_items), take(n_items), take(n_items)
    transit = take(n_items)
    (
        send_a,
        recv_a,
        send_b,
        recv_b,
        send_c,
        recv_c,
        send_t,
        recv_t,
        local,
        send_x,
        recv_x,
        local_y,
        *stages,
    ) = refs
    greet(n_dp, n_expert)
    mate = (z, chip * 2 + 1 - core)
    order = [3, 1, 2, 0] if square else [*range(1, chips), 0]
    half = n_dp // 2
    low, high = pl.ds(0, half), pl.ds(half, n_dp - half)

    def chip_of(k):
        return to_chip(k) if k else chip

    def source(i, column):
        array, first, rows = items[i]
        return sources[array].at[:, column, pl.ds(first, rows)]

    def to_mate(i, k):
        return remote(
            source(i, chip_of(k) * 2 + 1 - core),
            got_a[i].at[k],
            send_a.at[i, k],
            recv_a.at[i, k],
            mate,
        )

    turn = [0] * n_rings
    loads = []
    for i in range(n_items):
        for k in order:
            loads.append((i, k, turn[rings[i]] % 2))
            turn[rings[i]] += 1

    def load(i, k, at):
        return pltpu.make_async_copy(
            source(i, chip_of(k) * 2 + core), ring[rings[i]].at[at], local.at[rings[i], at]
        )

    def send_near(i, k, part, number):
        return remote(
            got_a[i].at[k, part],
            got_b[i].at[k - 1, part],
            send_b.at[i, number],
            recv_b.at[i, number],
            (z, to_chip(k) * 2 + core),
        )

    def send_over(i, k, part):
        return remote(
            got_a[i].at[3, part],
            transit[i].at[k - 1],
            send_t.at[i, k],
            recv_t.at[i, k],
            (z, to_chip(k) * 2 + core),
        )

    def send_far(i, k):
        return remote(
            got_a[i].at[k],
            got_b[i].at[k - 1],
            send_b.at[i, k],
            recv_b.at[i, k],
            (z, to_chip(k) * 2 + core),
        )

    def along(i, plane, way):
        slot = n_dp - (z - 1) + plane if way else plane - (z + 1)
        return remote(
            got_a[i].at[0, plane],
            got_c[i].at[slot],
            send_c.at[i, plane],
            recv_c.at[i, slot],
            (z - 1 if way else z + 1, j),
        )

    def from_along(i, slot):
        return remote(
            got_c[i].at[slot], got_c[i].at[slot], send_c.at[i, 0], recv_c.at[i, slot], mate
        )

    f32 = jnp.float32

    def add(i, planes, target, terms):
        rows = got_a[i].shape[2]
        per = rows // 16

        def step(n, unused):
            plane = n // per
            at = pl.ds(pl.multiple_of((n % per) * 16, 16), 16)
            total = terms[0](plane, at).astype(f32)
            for term in terms[1:]:
                total = total + term(plane, at).astype(f32)
            target(plane, at, total)
            return unused

        lax.fori_loop(0, planes * per, step, 0)

    def grow(i, k, first, planes, term):
        def target(plane, at, total):
            got_a[i][k, plane + first, at] = total.astype(got_a[i].dtype)

        add(i, planes, target, [lambda plane, at: got_a[i][k, plane + first, at], term])

    for i in range(n_items):
        for k in order:
            to_mate(i, k).start()
    started = 0
    ahead = [0] * n_rings
    for i, k, at in loads:
        if ahead[rings[i]] < 2:
            load(i, k, at).start()
            ahead[rings[i]] += 1
    pairs = cuts(cut_in, cut_out)
    copies = exchange(n_dp, pairs, send_x, recv_x)
    for copy in copies:
        copy.start()
    own = [(source(z), target(z)) for source, target in pairs]
    bring, put = moves(own + puts(cut_in, cut_out), stages, local_y)
    for copy in bring:
        copy.start()

    def over_cores(i):
        for n, (item, k, at) in enumerate(loads):
            if item != i:
                continue
            load(i, k, at).wait()
            to_mate(i, k).wait_recv()
            grow(i, k, 0, n_dp, lambda plane, rows: ring[rings[i]][at, plane, rows])
            later = [one for one in loads[n + 1 :] if rings[one[0]] == rings[i]]
            if len(later) >= 2:
                load(*later[1]).start()
            if not k:
                continue
            if not square:
                send_far(i, k).start()
            elif k == 3:
                send_over(i, 1, low).start()
                send_over(i, 2, high).start()
            elif k == 1:
                send_near(i, 1, low, 0).start()
            else:
                send_near(i, 2, high, 1).start()

    def pass_over(i):
        if not square:
            return
        send_over(i, 2, high).wait_recv()
        grow(i, 1, half, n_dp - half, lambda plane, rows: transit[i][1, plane, rows])
        send_near(i, 1, high, 2).start()
        send_over(i, 1, low).wait_recv()
        grow(i, 2, 0, half, lambda plane, rows: transit[i][0, plane, rows])
        send_near(i, 2, low, 3).start()

    def over_chips(i):
        if square:
            send_near(i, 1, low, 0).wait_recv()
            send_near(i, 2, high, 1).wait_recv()
            send_near(i, 1, high, 2).wait_recv()
            send_near(i, 2, low, 3).wait_recv()
        else:
            for k in range(1, chips):
                send_far(i, k).wait_recv()
        heard = 2 if square else chips - 1

        def target(plane, at, total):
            got_a[i][0, plane, at] = total.astype(got_a[i].dtype)

        terms = [lambda plane, at: got_a[i][0, plane, at]]
        for other in range(heard):
            terms.append(lambda plane, at, other=other: got_b[i][other, plane, at])
        add(i, n_dp, target, terms)
        for d in range(n_dp - 1, 0, -1):
            for way in (0, 1):
                plane = z - d if way else z + d

                @pl.when(z == (n_dp - 1 if way else 0))
                def _():
                    along(i, plane, way).start()

    def over_planes(i):
        for d in range(n_dp - 2, 0, -1):
            for way in (0, 1):
                plane = z - d if way else z + d
                slot = n_dp - d if way else d

                @pl.when((plane >= 0) & (z < n_dp - 1) if way else (plane < n_dp) & (z > 0))
                def _():
                    from_along(i, slot).wait_recv()
                    grow(i, 0, plane, 1, lambda unused, at: got_c[i][slot, at])
                    along(i, plane, way).start()

    def finish(i):
        array, first, rows = items[i]

        def here(at):
            return pl.ds(pl.multiple_of(first + at.start, 16), 16)

        def own(unused, at, total):
            targets[array][here(at)] = total

        add(i, 1, own, [lambda unused, at: got_a[i][0, z, at]])
        for slot, arrives in ((0, z > 0), (n_dp, z < n_dp - 1)):

            @pl.when(arrives)
            def _():
                from_along(i, slot).wait_recv()
                add(
                    i,
                    1,
                    own,
                    [
                        lambda unused, at: targets[array][here(at)],
                        lambda unused, at: got_c[i][slot, at],
                    ],
                )

    steps = (over_cores, pass_over, over_chips, over_planes, finish)
    for n in range(n_items + len(steps) - 1):
        for late, step in enumerate(steps):
            if 0 <= n - late < n_items:
                step(n - late)
        if n == min(1, n_items - 1):
            for one, other in zip(bring, put):
                one.wait()
                other.start()
            middle(cut_in, cut_out)
    for i in range(n_items):
        for k in range(chips):
            to_mate(i, k).wait_send()
        if square:
            for k, part in ((1, low), (2, high)):
                send_over(i, k, part).wait_send()
            for k, part, number in ((1, low, 0), (2, high, 1), (1, high, 2), (2, low, 3)):
                send_near(i, k, part, number).wait_send()
        else:
            for k in range(1, chips):
                send_far(i, k).wait_send()
        for plane in range(n_dp):

            @pl.when(z != plane)
            def _():
                remote(
                    got_a[i].at[0, plane],
                    got_c[i].at[0],
                    send_c.at[i, plane],
                    recv_c.at[i, 0],
                    mate,
                ).wait_send()

    for copy in copies + put:
        copy.wait()


def scatter_call(
    n_dp,
    n_expert,
    arrays,
    splits,
    cut_in,
    cut_shapes,
    cuts,
    number,
    aliases,
    stages,
    puts=nothing,
    middle=nothing,
):
    chips = n_expert // 2
    square = chips == 4
    items = []
    for array, (one, split) in enumerate(zip(arrays, splits)):
        rows = one.shape[2] // split
        items += [(array, first, rows) for first in range(0, one.shape[2], rows)]
    n, m = len(items), len(cut_shapes)
    count = len(arrays)
    dma = pltpu.SemaphoreType.DMA
    anywhere = pl.BlockSpec(memory_space=pl.ANY)
    blocks = [(rows, arrays[array].shape[3]) for array, unused, rows in items]
    kinds = sorted(set(blocks))
    rings = [kinds.index(block) for block in blocks]
    bf16 = jnp.bfloat16
    heard = 2 if square else chips - 1
    return pl.pallas_call(
        functools.partial(
            scatter_kernel,
            n_dp,
            n_expert,
            count,
            items,
            len(cut_in),
            m,
            cuts,
            puts,
            middle,
            rings,
            len(kinds),
        ),
        out_shape=[
            *[jax.ShapeDtypeStruct(one.shape[2:], jnp.float32) for one in arrays],
            *cut_shapes,
        ],
        in_specs=[anywhere] * (count + len(cut_in)),
        out_specs=[pl.BlockSpec(memory_space=pltpu.VMEM)] * count + [anywhere] * m,
        scratch_shapes=[
            *[pltpu.VMEM((2, n_dp, *kind), bf16) for kind in kinds],
            *[pltpu.VMEM((chips, n_dp, *block), bf16) for block in blocks],
            *[pltpu.VMEM((heard, n_dp, *block), bf16) for block in blocks],
            *[pltpu.VMEM((n_dp + 1, *block), bf16) for block in blocks],
            *[pltpu.VMEM((2, n_dp // 2, *(block if square else (16, 128))), bf16) for block in blocks],
            dma((n, chips)),
            dma((n, chips)),
            dma((n, chips)),
            dma((n, chips)),
            dma((n, n_dp)),
            dma((n, n_dp + 1)),
            dma((n, 3)),
            dma((n, 3)),
            dma((len(kinds), 2)),
            dma((4, n_dp)),
            dma((4, n_dp)),
            dma((max(len(stages), 4), 2)),
            *[pltpu.VMEM(stage, jnp.bfloat16) for stage in stages],
        ],
        input_output_aliases=aliases,
        compiler_params=pltpu.CompilerParams(
            collective_id=number, has_side_effects=True, vmem_limit_bytes=62 * 1024 * 1024
        ),
    )(*arrays, *cut_in)


def scatter_all(
    n_dp,
    n_expert,
    items,
    splits,
    cut_in,
    cut_shapes,
    cuts,
    number,
    aliases,
    stages,
    puts=nothing,
    middle=nothing,
):
    chips = n_expert // 2
    blocks = (2 * chips - 1 if chips != 4 else 7) * n_dp + n_dp + 3
    need = sum(blocks * item.shape[2] * item.shape[3] * 2 for item in items)
    kinds = {(item.shape[2] // split, item.shape[3]) for item, split in zip(items, splits)}
    need += sum(2 * n_dp * kind[0] * kind[1] * 2 for kind in kinds)
    need += sum(stage[0] * stage[1] * stage[2] * 2 for stage in stages)
    pieces = -(-need // (61 * 1024 * 1024))
    tiles = [item.shape[3] // 128 for item in items]
    results = [[] for item in items]
    extra = []
    for piece in range(pieces):
        ends = [(t * piece // pieces * 128, t * (piece + 1) // pieces * 128) for t in tiles]
        used = [i for i, (low, high) in enumerate(ends) if high > low]
        first = piece == 0
        outs = scatter_call(
            n_dp,
            n_expert,
            [items[i][..., ends[i][0] : ends[i][1]] if pieces > 1 else items[i] for i in used],
            [splits[i] for i in used],
            cut_in if first else [],
            cut_shapes if first else [],
            cuts if first else nothing,
            number + piece,
            {len(used) + a: len(used) + b for a, b in aliases} if first else {},
            stages if first else [],
            puts if first else nothing,
            middle if first else nothing,
        )
        for i, out in zip(used, outs):
            results[i].append(out)
        if first:
            extra = outs[len(used) :]
    return [one[0] if len(one) == 1 else jnp.concatenate(one, axis=1) for one in results], extra


def dot(left, right, dims):
    return lax.dot_general(
        left, right, ((dims[:1], dims[1:]), ((), ())), preferred_element_type=jnp.float32
    )


def picks(slots_ref, number):
    pair = slots_ref.shape[2]
    rows = lax.broadcasted_iota(jnp.int32, (2 * CAP, pair), 0)
    return [slots_ref[0, e : e + 1, :] == rows for e in range(number)]


def pick_kernel(number, experts_all, slots_ref, x_ref, g_ref, router_ref, rows_ref, grows_ref, gates_ref):
    chosen = picks(slots_ref, number)
    pick = jnp.concatenate(chosen, axis=0).astype(jnp.bfloat16)
    size = 2 * CAP
    x = x_ref[...]
    logits = dot(router_ref[...], x, (0, 1))
    names = lax.broadcasted_iota(jnp.int32, logits.shape, 0)
    logits = jnp.where(names < experts_all, logits, -1e30)
    weights = jnp.exp(logits - jnp.max(logits, axis=0, keepdims=True))
    probs = weights / jnp.sum(weights, axis=0, keepdims=True)
    for e in range(number):
        gate = jnp.sum(jnp.where(chosen[e], probs[e : e + 1, :], 0.0), axis=1, keepdims=True)
        gates_ref[e] = jnp.broadcast_to(gate, (size, 128))
    picked = dot(pick, x, (1, 0)).astype(jnp.bfloat16)
    for e in range(number):
        rows_ref[e] = picked[e * size : (e + 1) * size]
    picked = dot(pick, g_ref[...], (1, 0)).astype(jnp.bfloat16)
    for e in range(number):
        grows_ref[e] = picked[e * size : (e + 1) * size]


def expert_kernel(steps, half, n_weights, n_into, n_pack, names_ref, x_ref, g_ref, gates_ref, *refs):
    weights, refs = refs[:n_weights], refs[n_weights:]
    down_ref, refs = refs[0], refs[1 + n_into :]
    (
        y_ref,
        dx_ref,
        probs_ref,
        dgate_ref,
        dup_ref,
        ddown_ref,
        *pack_refs,
        sum_gate,
        sum_up,
    ) = refs
    bf16 = jnp.bfloat16
    g = g_ref[0]
    rows, width = x_ref.shape[1:]
    part = dgate_ref.shape[2]
    gate = gates_ref[0][:, :1]
    if n_weights == 2:
        piece = 512
        gate_ref, up_ref = weights
        gate_mid = dot(x_ref[0], gate_ref[0], (1, 0))
        up_mid = dot(x_ref[0], up_ref[0], (1, 0))
        spans = [
            (pl.ds(at, piece), gate_ref, up_ref, pl.ds(at, piece), pl.ds(0, part), pl.ds(0, part))
            for at in range(0, width, piece)
        ]
    else:
        piece = width // n_weights
        spans = []
        gate_mid = up_mid = 0.0
        for n, ref in enumerate(weights):
            span = pl.ds(pl.multiple_of(names_ref[1 + n], piece), piece)
            x_part = x_ref[0, :, span]
            gate_mid = gate_mid + dot(x_part, ref[0, :, :part], (1, 0))
            up_mid = up_mid + dot(x_part, ref[0, :, part:], (1, 0))
            spans.append((span, ref, ref, pl.ds(0, piece), pl.ds(0, part), pl.ds(part, part)))
    sigmoid = 1.0 / (1.0 + jnp.exp(-gate_mid))
    silu = gate_mid * sigmoid
    hidden = silu * up_mid
    hidden_low = hidden.astype(bf16)
    grad_plain = dot(g, down_ref[0], (1, 1))
    grad_gates = jnp.sum(grad_plain * hidden_low.astype(jnp.float32), axis=1, keepdims=True)
    high = grad_gates.astype(bf16).astype(jnp.float32)
    lane = lax.broadcasted_iota(jnp.int32, (rows, 128), 1)
    name = names_ref[0] + pl.program_id(0)
    probs_ref[0] = (
        jnp.where(lane == name, high, 0.0) + jnp.where(lane == name + half, grad_gates - high, 0.0)
    ).astype(bf16)
    grad_hidden = grad_plain * gate
    grad_gate = (
        grad_hidden * up_mid * sigmoid * (1.0 + gate_mid * (1.0 - sigmoid))
    ).astype(bf16)
    grad_up = (grad_hidden * silu).astype(bf16)
    scaled = (hidden * gate).astype(bf16)
    for at in range(0, width, piece):
        y_ref[0, :, at : at + piece] = (
            dot(hidden_low, down_ref[0, :, at : at + piece], (1, 0)) * gate
        ).astype(bf16)
    for span, gate_ref, up_ref, here, gate_columns, up_columns in spans:
        dx_ref[0, :, span] = (
            dot(grad_gate, gate_ref[0, here, gate_columns], (1, 1))
            + dot(grad_up, up_ref[0, here, up_columns], (1, 1))
        ).astype(bf16)
    step = pl.program_id(1)
    for span, *unused in spans:
        x_part = x_ref[0, :, span]
        here_gate = dot(x_part, grad_gate, (0, 0))
        here_up = dot(x_part, grad_up, (0, 0))
        here_down = dot(scaled, g_ref[0, :, span], (0, 0))
        if steps == 1:
            dgate_ref[0, span, :] = here_gate.astype(bf16)
            dup_ref[0, span, :] = here_up.astype(bf16)
            ddown_ref[0, :, span] = here_down
            continue

        @pl.when(step == 0)
        def _():
            sum_gate[span, :] = here_gate
            sum_up[span, :] = here_up
            ddown_ref[0, :, span] = here_down

        @pl.when(step > 0)
        def _():
            sum_gate[span, :] += here_gate
            sum_up[span, :] += here_up
            ddown_ref[0, :, span] += here_down

        @pl.when(step == steps - 1)
        def _():
            dgate_ref[0, span, :] = sum_gate[span, :].astype(bf16)
            dup_ref[0, span, :] = sum_up[span, :].astype(bf16)

    if n_pack:

        @pl.when((step == steps - 1) & (pl.program_id(0) < n_pack))
        def _():
            pack_ref = pack_refs[0]
            depth = pack_ref.shape[2]
            for plane in range(pack_ref.shape[0]):
                here = pl.ds(plane * depth, depth)
                pack_ref[plane, 0, :, :part] = dgate_ref[0, here, :]
                pack_ref[plane, 0, :, part:] = dup_ref[0, here, :]


def put_back(number, slots_ref, pairs):
    pick = jnp.concatenate(picks(slots_ref, number), axis=0).astype(jnp.bfloat16)
    piece = 512
    for source, target, first in pairs:
        width = source.shape[2]
        for at in range(0, width, piece):
            size = min(piece, width)
            part = source[:, :, at : at + size].reshape(-1, size)
            target[:, first + at : first + at + size] = dot(pick, part, (0, 0)).astype(
                jnp.bfloat16
            )


def place_back_kernel(number, slots_ref, dx_ref, probs_ref, back_ref):
    put_back(number, slots_ref, [(dx_ref, back_ref, 0), (probs_ref, back_ref, dx_ref.shape[2])])


def place_out_kernel(number, slots_ref, y_ref, out_ref):
    put_back(number, slots_ref, [(y_ref, out_ref, 0)])


def place_out(slots, y, out):
    pairs, number, pair = slots.shape
    pltpu.emit_pipeline(
        functools.partial(place_out_kernel, number),
        grid=(pairs,),
        in_specs=[
            pl.BlockSpec((1, number, pair), lambda p: (p, 0, 0)),
            pl.BlockSpec((number, 2 * CAP, D), lambda p: (0, p, 0)),
        ],
        out_specs=[pl.BlockSpec((pair, D), lambda p: (p, 0))],
    )(slots, y, out)


def pick_shapes(number, pairs):
    bf16 = jnp.bfloat16
    size = 2 * CAP
    return [
        jax.ShapeDtypeStruct((number, pairs * size, D), bf16),
        jax.ShapeDtypeStruct((number, pairs * size, D), bf16),
        jax.ShapeDtypeStruct((number, pairs * size, 128), jnp.float32),
    ]


def pick_rows(number, experts_all, slots, x_all, g_all, router, rows, grows, gates):
    pairs, _, pair = slots.shape
    size = 2 * CAP
    tokens = pl.BlockSpec((pair, D), lambda p: (p, 0))
    picked = pl.BlockSpec((number, size, D), lambda p: (0, p, 0))
    pltpu.emit_pipeline(
        functools.partial(pick_kernel, number, experts_all),
        grid=(pairs,),
        in_specs=[
            pl.BlockSpec((1, number, pair), lambda p: (p, 0, 0)),
            tokens,
            tokens,
            pl.BlockSpec(router.shape, lambda p: (0, 0)),
        ],
        out_specs=[picked, picked, pl.BlockSpec((number, size, 128), lambda p: (0, p, 0))],
    )(slots, x_all, g_all, router, rows, grows, gates)


def expert_call(names, half, low, number, rows, grows, gates, weights, down, into=(), pack=()):
    total, depth, _ = rows.shape
    part = down.shape[1]
    size = depth
    while size > 768:
        size //= 2
    steps = depth // size
    bf16 = jnp.bfloat16
    f32 = jnp.float32

    def from_rows(width):
        return pl.BlockSpec((1, size, width), lambda e, r: (e + low, r, 0))

    def whole(*shape):
        return pl.BlockSpec((1, *shape), lambda e, r: (e, 0, 0))

    def from_whole(*shape):
        return pl.BlockSpec((1, *shape), lambda e, r: (e + low, 0, 0))

    packed = [
        pl.BlockSpec(
            (planes, 1, D // planes, 2 * part),
            lambda e, r, n=n: (0, lax.min(e, n - 1), 0, 0),
        )
        for n, planes in ([pack] if pack else [])
    ]
    keep = (D, part) if steps > 1 else (16, 128)
    return pl.pallas_call(
        functools.partial(
            expert_kernel, steps, half, len(weights), len(into), pack[0] if pack else 0
        ),
        grid=(number, steps),
        in_specs=[
            pl.BlockSpec(memory_space=pltpu.SMEM),
            from_rows(D),
            from_rows(D),
            from_rows(128),
            *[(from_whole if len(weights) == 2 else whole)(*one.shape[1:]) for one in weights],
            from_whole(part, D),
            *[pl.BlockSpec(memory_space=pl.ANY)] * len(into),
        ],
        out_specs=[
            from_rows(D),
            from_rows(D),
            from_rows(128),
            whole(D, part),
            whole(D, part),
            from_whole(part, D),
            *packed,
        ],
        out_shape=[
            jax.ShapeDtypeStruct((total, depth, D), bf16),
            jax.ShapeDtypeStruct((total, depth, D), bf16),
            jax.ShapeDtypeStruct((total, depth, 128), bf16),
            jax.ShapeDtypeStruct((number, D, part), bf16),
            jax.ShapeDtypeStruct((number, D, part), bf16),
            jax.ShapeDtypeStruct((total, part, D), f32),
            *[
                jax.ShapeDtypeStruct((planes, n, D // planes, 2 * part), bf16)
                for n, planes in ([pack] if pack else [])
            ],
        ],
        input_output_aliases={
            5 + len(weights) + i: out for i, out in zip(range(len(into)), (0, 1, 2, 5))
        },
        scratch_shapes=[pltpu.VMEM(keep, f32), pltpu.VMEM(keep, f32)],
        compiler_params=pltpu.CompilerParams(vmem_limit_bytes=BIG),
    )(names, rows, grows, gates, *weights, down, *into)


def place_back(slots, dx, probs):
    pairs, number, pair = slots.shape
    size = 2 * CAP

    def rows(one):
        return pl.BlockSpec((number, size, one.shape[2]), lambda p: (0, p, 0))

    return pl.pallas_call(
        functools.partial(place_back_kernel, number),
        grid=(pairs,),
        in_specs=[pl.BlockSpec((1, number, pair), lambda p: (p, 0, 0)), rows(dx), rows(probs)],
        out_specs=pl.BlockSpec((pair, D + 128), lambda p: (p, 0)),
        out_shape=jax.ShapeDtypeStruct((pairs * pair, D + 128), jnp.bfloat16),
        compiler_params=pltpu.CompilerParams(vmem_limit_bytes=BIG),
    )(slots, dx, probs)


def widen_kernel(*refs):
    half = len(refs) // 2
    for source, target in zip(refs[:half], refs[half:]):
        target[...] = source[...].astype(jnp.float32)


def widen(spans, values):
    number, rows, columns = values[0].shape
    (low, high), (again, end) = spans

    def chosen(e):
        return (jnp.where(e < high - low, e + low, e - (high - low) + again), 0, 0)

    block = pl.BlockSpec((1, rows, columns), chosen)
    return pl.pallas_call(
        widen_kernel,
        grid=(high - low + end - again,),
        in_specs=[block] * len(values),
        out_specs=[block] * len(values),
        out_shape=[jax.ShapeDtypeStruct(one.shape, jnp.float32) for one in values],
        compiler_params=pltpu.CompilerParams(vmem_limit_bytes=BIG),
    )(*values)


def widen_pieces_kernel(low, n_pieces, offsets_ref, *refs):
    pieces, refs = refs[:n_pieces], refs[n_pieces + 2 :]
    targets, wide, sems = refs[:2], refs[2], refs[3]
    part = wide.shape[4]
    copies = []
    for k, piece in enumerate(pieces):
        columns = pl.ds(pl.multiple_of(offsets_ref[k], part), part)
        for n in range(2):
            wide[k, n] = piece[:, :, n * part : (n + 1) * part].astype(jnp.float32)
            copy = pltpu.make_async_copy(
                wide.at[k, n], targets[n].at[pl.ds(low, piece.shape[0]), :, columns], sems.at[k, n]
            )
            copy.start()
            copies.append(copy)
    for copy in copies:
        copy.wait()


def widen_pieces(offsets, low, pieces, into):
    size, rows, columns = pieces[0].shape
    anywhere = pl.BlockSpec(memory_space=pl.ANY)
    count = len(pieces)
    return pl.pallas_call(
        functools.partial(widen_pieces_kernel, low, count),
        in_specs=[
            pl.BlockSpec(memory_space=pltpu.SMEM),
            *[pl.BlockSpec(memory_space=pltpu.VMEM)] * count,
            anywhere,
            anywhere,
        ],
        out_specs=[anywhere, anywhere],
        out_shape=[jax.ShapeDtypeStruct(one.shape, one.dtype) for one in into],
        scratch_shapes=[
            pltpu.VMEM((count, 2, size, rows, columns // 2), jnp.float32),
            pltpu.SemaphoreType.DMA((count, 2)),
        ],
        input_output_aliases={1 + count: 0, 2 + count: 1},
        compiler_params=pltpu.CompilerParams(vmem_limit_bytes=BIG),
    )(offsets, *pieces, *into)


def shards(
    n_dp,
    n_expert,
    tokens,
    cotangent,
    lengths,
    routes,
    w_query,
    w_key,
    w_value,
    w_out,
    w_router,
    gain_attn,
    gain_query,
    gain_key,
    gain_mlp,
    w_gate,
    w_up,
    w_down,
):
    groups = n_dp * n_expert
    bf16 = jnp.bfloat16
    number = w_gate.shape[0]
    ff = w_gate.shape[2]
    part = ff // n_dp
    experts_all = w_router.shape[1]
    width = 128
    small = jnp.concatenate(
        [
            w_router,
            gain_attn[:, None],
            gain_query[:, None],
            gain_key[:, None],
            gain_mlp[:, None],
            jnp.zeros((w_router.shape[0], width - experts_all - 4), bf16),
        ],
        axis=1,
    )
    hits = jnp.any(
        routes[:, :, None] == jnp.arange(width, dtype=jnp.int32)[None, None, :], axis=1
    ).astype(bf16)
    count = tokens.shape[0]
    rows_each = w_query.shape[0]
    extras = jnp.concatenate([hits, jnp.pad(small, ((0, count - rows_each), (0, 0)))], axis=1)
    weights = jnp.stack([w_query, w_key, w_value, w_out])
    depth = w_gate.shape[1]
    early = number // 4
    beside = early + number // 8
    late = number - number // 4
    back_beside = number // 8
    back_third = back_beside + max(number // 8, 1)
    back_late = back_third + number // 4
    me = lax.axis_index("dp")
    cut_shape = jax.ShapeDtypeStruct((number, n_dp * depth, part), bf16)

    def row_block(size):
        return lambda ref, block: ref.at[pl.ds(pl.multiple_of(block * size, 16), size)]

    def columns_at(at):
        return pl.ds(pl.multiple_of(at * part, part), part)

    def rows_at(at):
        return pl.ds(pl.multiple_of(at * depth, depth), depth)

    def recut(low, high):
        def cuts(ins, outs):
            def pair(n):
                chosen = pl.ds(low, high - low)
                return (
                    lambda to: ins[n].at[chosen, :, columns_at(to)],
                    lambda at: outs[n].at[chosen, rows_at(at)],
                )

            return [pair(0), pair(1)]

        return cuts

    to_plane, from_plane = partners(me, n_dp)

    def permuted(pieces, chained=False):
        got = []
        for k, piece in enumerate(pieces, 1):
            if chained and got:
                piece, last = lax.optimization_barrier((piece, got.pop()))
                got.append(last)
            paths = [(i, partners(i, n_dp)[0](k)) for i in range(n_dp)]
            got.append(lax.ppermute(piece, "dp", paths))
        return got

    def cut_pieces(low, high, first_k, ins, outs):
        to, unused = partners(lax.axis_index("dp"), n_dp)
        pairs = []
        for k, piece in enumerate(outs, first_k):
            for n in range(2):
                source = ins[n].at[pl.ds(low, high - low), :, columns_at(to(k))]
                pairs.append((source, piece.at[:, :, pl.ds(n * part, part)]))
        return pairs

    def piece_shapes(size, first_k):
        shape = jax.ShapeDtypeStruct((size, depth, 2 * part), bf16)
        return [shape] * (n_dp - first_k if size else 0)

    def stages(*sizes):
        return [(size, depth, part) for size in sizes]

    soon_shapes = piece_shapes(beside - early, 1)
    late_shapes = piece_shapes(number - late, 0)
    n_soon = len(soon_shapes)

    weights_all, extras_all, gate_early, up_early, *pieces = gather_call(
        n_dp,
        n_expert,
        [weights, extras],
        [
            jax.ShapeDtypeStruct((4, groups * rows_each, D), bf16),
            jax.ShapeDtypeStruct((groups * count, 2 * width), bf16),
        ],
        [
            lambda ref, block: ref.at[
                :, pl.ds(pl.multiple_of(block * rows_each, 16), rows_each)
            ],
            row_block(count),
        ],
        [w_gate, w_up],
        [cut_shape, cut_shape, *soon_shapes, *late_shapes],
        recut(0, early),
        {},
        0,
        stages(
            *[early] * 2,
            *[beside - early] * (2 * n_soon),
            *[number - late] * (2 * n_dp),
        ),
        lambda ins, outs: cut_pieces(early, beside, 1, ins, outs[2 : 2 + n_soon])
        + cut_pieces(late, number, 0, ins, outs[2 + n_soon :]),
    )
    soon_pieces, late_pieces = pieces[:n_soon], pieces[n_soon:]
    query_weight, key_weight, value_weight, out_weight = (weights_all[i] for i in range(4))
    small_all = (
        extras_all[:, width:].reshape(groups, count, width)[:, :rows_each].reshape(-1, width)
    )
    hits_all = extras_all[:, :experts_all]
    router_weight = small_all[:, :experts_all]
    gains = small_all[:, experts_all : experts_all + 4].astype(jnp.float32)
    attn_gain, query_gain, key_gain, mlp_gain = (gains[:, i] for i in range(4))
    inputs = tokens.astype(jnp.float32)
    segment, position, places = layout(lengths[0], count)
    half = HD // 2
    freq = 10000.0 ** (-2.0 * jnp.arange(half, dtype=jnp.float32) / HD)
    angle = position.astype(jnp.float32)[:, None] * freq[None, :]
    cosine = jnp.cos(angle)[:, None, :]
    sine = jnp.sin(angle)[:, None, :]
    scale = HD ** (-0.5)
    normed, attn_inverse = rms_forward(inputs, attn_gain)
    normed_low = normed.astype(bf16)
    query_raw = product(normed_low, query_weight, "td,de->te")
    key_raw = product(normed_low, key_weight, "td,de->te")
    value_low = product(normed_low, value_weight, "td,de->te").astype(bf16)
    query_normed, query_inverse = rms_forward(query_raw, query_gain)
    key_normed, key_inverse = rms_forward(key_raw, key_gain)
    query_low = rotate(query_normed, cosine, sine).astype(bf16).reshape(count, HEADS, HD)
    key_low = rotate(key_normed, cosine, sine).astype(bf16).reshape(count, HEADS, HD)
    value_heads = value_low.reshape(count, HEADS, HD)
    allowed = (segment[:, None] == segment[None, :]) & (places[None, :] <= places[:, None])
    scores = product(query_low, key_low, "qhd,khd->hqk") * scale
    scores = jnp.where(allowed[None], scores, -1e30)
    probs = jax.nn.softmax(scores, axis=-1)
    probs_low = probs.astype(bf16)
    attended_low = product(probs_low, value_heads, "hqk,khd->qhd").reshape(count, D).astype(bf16)
    middle = inputs + product(attended_low, out_weight, "td,de->te")
    mlp_normed, mlp_inverse = rms_forward(middle, mlp_gain)
    mlp_low = mlp_normed.astype(bf16)
    router = jax.nn.softmax(product(mlp_low, router_weight, "td,de->te"), axis=-1)

    first = lax.axis_index("expert") * number
    hit = lax.dynamic_slice_in_dim(hits_all, first, number, 1).reshape(groups, count, number)
    before = jnp.tril(jnp.ones((count, count), bf16), -1)
    slot = product(before, hit, "ts,bse->bet").astype(jnp.int32)
    slot = jnp.where(jnp.transpose(hit, (0, 2, 1)) > 0, slot, -1)
    slot = slot.reshape(groups // 2, 2, number, count)
    shift = jnp.array([0, CAP], jnp.int32)[None, :, None, None]
    slots = jnp.transpose(jnp.where(slot < 0, -1, slot + shift), (0, 2, 1, 3))
    slots = slots.reshape(groups // 2, number, 2 * count)
    router_own = jnp.pad(
        jnp.roll(router_weight, -first, axis=1), ((0, 0), (0, width - experts_all))
    )
    if n_soon:
        mlp_low, *soon_pieces = lax.optimization_barrier((mlp_low, *permuted(soon_pieces)))

    def put_weights(ins, outs):
        chosen = pl.ds(early, beside - early)
        unused, heard = partners(lax.axis_index("dp"), n_dp)
        pairs = []
        if beside > early:
            own = lax.axis_index("dp")
            for n in range(2):
                source = ins[n].at[chosen, :, columns_at(own)]
                pairs.append((source, outs[n].at[chosen, rows_at(own)]))
        for k, piece in enumerate(ins[6:], 1):
            for n in range(2):
                columns = piece.at[:, :, pl.ds(n * part, part)]
                pairs.append((columns, outs[n].at[chosen, rows_at(heard(k))]))
        return pairs

    def pick_all(items, ins, outs):
        pick_rows(number, experts_all, ins[4], *items, ins[5], *outs[2:])

    unused, unused, gate_cut, up_cut, rows, grows, gates = gather_call(
        n_dp,
        n_expert,
        [mlp_low, cotangent],
        [jax.ShapeDtypeStruct((groups * count, D), bf16)] * 2,
        [row_block(count)] * 2,
        [w_gate, w_up, gate_early, up_early, slots, router_own, *soon_pieces],
        [cut_shape, cut_shape, *pick_shapes(number, groups // 2)],
        recut(beside, late),
        {4: 2, 5: 3},
        1,
        stages(*[late - beside] * 2, *[beside - early] * (2 * n_dp if n_soon else 0)),
        put_weights,
        pick_all,
    )
    *late_pieces, rows = lax.optimization_barrier((*late_pieces, rows))
    late_pieces = [late_pieces[0], *permuted(late_pieces[1:])]
    packing = back_beside > 0 and depth == 512
    *outs, gate_soon, up_soon, down_soon = expert_call(
        first[None],
        experts_all,
        0,
        late,
        rows,
        grows,
        gates,
        [gate_cut, up_cut],
        w_down,
        pack=(back_beside, n_dp) if packing else (),
    )
    if packing:
        *outs, gate_soon, up_soon, down_soon, packed = [*outs, gate_soon, up_soon, down_soon]
    offsets = [from_plane(k) * depth for k in range(n_dp)]
    weighted, grad_rows, grad_gates, gate_rest, up_rest, grad_down_part = expert_call(
        jnp.stack([first + late, *offsets]),
        experts_all,
        late,
        number - late,
        rows,
        grows,
        gates,
        late_pieces,
        w_down,
        [*outs, down_soon],
    )
    part_back = place_back(slots, grad_rows, grad_gates)

    def ways(low, high, at, ins, outs):
        def pair(n):
            return (
                lambda to: ins[n].at[pl.ds(low, high - low), rows_at(to)],
                lambda here: outs[n].at[pl.ds(low + at, high - low), :, columns_at(here)],
            )

        return [pair(0), pair(1)]

    def cut_grads(low, high, ins, outs):
        to, unused = partners(lax.axis_index("dp"), n_dp)
        pairs = []
        for k, piece in enumerate(outs, 1):
            for n in range(2):
                source = ins[n].at[pl.ds(low, high - low), rows_at(to(k))]
                pairs.append((source, piece.at[:, :, pl.ds(n * part, part)]))
        return pairs

    pieces = []
    if back_beside:
        for k in range(1, n_dp):
            if packing:
                piece = lax.dynamic_index_in_dim(packed, to_plane(k), 0, False)
            else:
                piece = jnp.concatenate(
                    [
                        lax.dynamic_slice_in_dim(
                            one[:back_beside], to_plane(k) * depth, depth, 1
                        )
                        for one in (gate_soon, up_soon)
                    ],
                    axis=2,
                )
            pieces.append(piece)
        ahead = lax.optimization_barrier((*pieces, *late_pieces[1:]))
        pieces = permuted(ahead[: n_dp - 1])
        part_back, *pieces = lax.optimization_barrier((part_back, *pieces))
    way_shapes = [jax.ShapeDtypeStruct((number, depth, ff), bf16)] * 2
    piece_shape = jax.ShapeDtypeStruct((back_late - back_third, depth, 2 * part), bf16)
    (back,), (gate_third, up_third, part_out, *later_pieces) = scatter_all(
        n_dp,
        n_expert,
        [part_back.reshape(n_dp, n_expert, count, D + width)],
        [8],
        [gate_soon, up_soon, slots, weighted],
        [
            *way_shapes,
            jax.ShapeDtypeStruct((groups * count, D), bf16),
            *[piece_shape] * (n_dp - 1),
        ],
        lambda ins, outs: ways(back_beside, back_third, 0, ins, outs),
        8,
        (),
        stages(
            *[back_third - back_beside] * 2, *[back_late - back_third] * (2 * (n_dp - 1))
        ),
        lambda ins, outs: cut_grads(back_third, back_late, ins, outs[3:]),
        lambda ins, outs: place_out(ins[2], ins[3], outs[2]),
    )
    later_pieces = permuted(later_pieces)

    def attention_back(back):
        query_weight, key_weight, value_weight, out_weight = (weights_all[i] for i in range(4))
        grad_final = cotangent.astype(jnp.float32)
        grad_mlp = back[:, :D]
        grad_router_probs = back[:, D : D + experts_all] + back[:, D + experts_all :]
        grad_logits = router * (
            grad_router_probs - jnp.sum(router * grad_router_probs, axis=1, keepdims=True)
        )
        grad_logits_low = grad_logits.astype(bf16)
        grad_router_full = product(mlp_low, grad_logits_low, "td,te->de")
        grad_mlp = grad_mlp + product(grad_logits_low, router_weight, "te,de->td")
        grad_middle_part, grad_mlp_gain = rms_backward(middle, mlp_inverse, mlp_gain, grad_mlp)
        grad_middle = grad_final + grad_middle_part
        grad_branch_low = grad_middle.astype(bf16)
        grad_out_full = product(attended_low, grad_branch_low, "td,te->de")
        grad_attended = (
            product(grad_branch_low, out_weight, "te,de->td").astype(bf16).reshape(count, HEADS, HD)
        )
        grad_weights = product(grad_attended, value_heads, "qhd,khd->hqk")
        grad_scores = probs * (grad_weights - jnp.sum(probs * grad_weights, axis=-1, keepdims=True))
        grad_scores_low = grad_scores.astype(bf16)
        grad_query_turn = product(grad_scores_low, key_low, "hqk,khd->qhd").reshape(count, D) * scale
        grad_key_turn = product(grad_scores_low, query_low, "hqk,qhd->khd").reshape(count, D) * scale
        grad_value_low = (
            product(probs_low, grad_attended, "hqk,qhd->khd").reshape(count, D).astype(bf16)
        )
        grad_query_raw, grad_query_gain = rms_backward(
            query_raw, query_inverse, query_gain, rotate(grad_query_turn, cosine, -sine)
        )
        grad_key_raw, grad_key_gain = rms_backward(
            key_raw, key_inverse, key_gain, rotate(grad_key_turn, cosine, -sine)
        )
        grad_query_low = grad_query_raw.astype(bf16)
        grad_key_low = grad_key_raw.astype(bf16)
        grad_query_full = product(normed_low, grad_query_low, "td,te->de")
        grad_key_full = product(normed_low, grad_key_low, "td,te->de")
        grad_value_full = product(normed_low, grad_value_low, "td,te->de")
        grad_normed = (
            product(grad_query_low, query_weight, "te,de->td")
            + product(grad_key_low, key_weight, "te,de->td")
            + product(grad_value_low, value_weight, "te,de->td")
        )
        grad_inputs_part, grad_attn_gain = rms_backward(inputs, attn_inverse, attn_gain, grad_normed)
        grad_inputs = grad_middle + grad_inputs_part

        small_grads = jnp.concatenate(
            [
                grad_router_full,
                grad_attn_gain[:, None],
                grad_query_gain[:, None],
                grad_key_gain[:, None],
                grad_mlp_gain[:, None],
                jnp.zeros((D, width - experts_all - 4), jnp.float32),
            ],
            axis=1,
        )
        grads = (grad_out_full, grad_value_full, grad_key_full, grad_query_full, small_grads)
        return grad_inputs, *[one.astype(bf16) for one in grads]

    def unreached(back):
        shapes = [(count, D)] + [(D, D)] * 4 + [(D, width)]
        kinds = [jnp.float32] + [bf16] * 5
        return tuple(jnp.zeros(shape, kind) for shape, kind in zip(shapes, kinds))

    grad_inputs, *weight_grads = lax.cond(lengths[0, 0] > 0, attention_back, unreached, back)

    def blocks_of(value):
        return value.reshape(n_dp, n_expert, rows_each, -1)

    sums, (gate_back, up_back) = scatter_all(
        n_dp,
        n_expert,
        [part_out.reshape(n_dp, n_expert, count, D)]
        + [blocks_of(value) for value in weight_grads],
        [4] + [2 if rows_each > 16 else 1] * (len(weight_grads) - 1) + [1],
        [gate_third, up_third, gate_soon, up_soon, gate_rest, up_rest],
        way_shapes,
        lambda ins, outs: ways(back_late, late, 0, ins[2:4], outs)
        + ways(0, number - late, late, ins[4:6], outs),
        16,
        ((0, 0), (1, 1)),
        [],
    )
    summed, grad_out_part, grad_value_part, grad_key_part, grad_query_part, small_part = sums
    output = (middle + summed).astype(bf16)
    grad_router_part = small_part[:, :experts_all]
    gain_parts = [small_part[:, experts_all + i] for i in range(4)]
    widened = widen([(back_beside, back_third), (back_late, number)], [gate_back, up_back])
    offsets = jnp.stack([from_plane(k) * part for k in range(n_dp)])
    for low, high, others in (
        (0, back_beside, pieces),
        (back_third, back_late, later_pieces),
    ):
        if high > low:
            own = jnp.concatenate(
                [
                    lax.dynamic_slice_in_dim(one[low:high], me * depth, depth, 1)
                    for one in (gate_soon, up_soon)
                ],
                axis=2,
            )
            widened = widen_pieces(offsets, low, [own, *others], widened)
    grad_gate_part, grad_up_part = widened
    return (
        output,
        grad_inputs,
        grad_query_part,
        grad_key_part,
        grad_value_part,
        grad_out_part,
        grad_router_part,
        gain_parts[0],
        gain_parts[1],
        gain_parts[2],
        gain_parts[3],
        grad_gate_part,
        grad_up_part,
        grad_down_part,
    )


def solution(mesh):
    return jax.shard_map(
        functools.partial(shards, mesh.shape["dp"], mesh.shape["expert"]),
        mesh=mesh,
        in_specs=(
            P(("dp", "expert"), None),
            P(("dp", "expert"), None),
            P(("dp", "expert"), None),
            P(("dp", "expert"), None),
            P(("dp", "expert"), None),
            P(("dp", "expert"), None),
            P(("dp", "expert"), None),
            P(("dp", "expert"), None),
            P(("dp", "expert"), None),
            P(("dp", "expert")),
            P(("dp", "expert")),
            P(("dp", "expert")),
            P(("dp", "expert")),
            P("expert", "dp", None),
            P("expert", "dp", None),
            P("expert", "dp", None),
        ),
        out_specs=(
            P(("dp", "expert"), None),
            P(("dp", "expert"), None),
            P(("dp", "expert"), None),
            P(("dp", "expert"), None),
            P(("dp", "expert"), None),
            P(("dp", "expert"), None),
            P(("dp", "expert"), None),
            P(("dp", "expert")),
            P(("dp", "expert")),
            P(("dp", "expert")),
            P(("dp", "expert")),
            P("expert", "dp", None),
            P("expert", "dp", None),
            P("expert", "dp", None),
        ),
        check_vma=False,
    )
```

```python
import functools

import jax
import jax.numpy as jnp
from jax import lax
from jax.experimental import pallas as pl
from jax.experimental.pallas import tpu as pltpu
from jax.sharding import PartitionSpec as P

D = 2048
HEADS = 16
HD = 128
TOPK = 8
CAP = 24


eps = 1e-05


def product(left, right, form):
    return jnp.einsum(form, left, right, preferred_element_type=jnp.float32)


def rms_forward(values, gain):
    inverse = lax.rsqrt(jnp.mean(values * values, axis=-1, keepdims=True) + eps)
    return (values * inverse * gain, inverse)


def rms_backward(values, inverse, gain, grad):
    scaled = grad * gain
    inner = jnp.mean(scaled * values, axis=-1, keepdims=True)
    grad_values = inverse * scaled - values * (inverse * inverse * inverse) * inner
    grad_gain = jnp.sum(grad * values * inverse, axis=0)
    return (grad_values, grad_gain)


def layout(lengths_row, count):
    places = jnp.arange(count, dtype=jnp.int32)
    ends = jnp.cumsum(lengths_row, dtype=jnp.int32)
    passed = (places[:, None] >= ends[None, :]).astype(jnp.int32)
    segment = jnp.sum(passed, axis=1, dtype=jnp.int32)
    start = jnp.sum(passed * lengths_row[None, :], axis=1, dtype=jnp.int32)
    return (segment, places - start, places)


def rotate(values, cosine, sine):
    count = values.shape[0]
    heads = values.reshape(count, HEADS, HD)
    half = HD // 2
    first = heads[..., :half]
    second = heads[..., half:]
    turned = jnp.concatenate(
        [first * cosine - second * sine, second * cosine + first * sine], axis=-1
    )
    return turned.reshape(count, D)


MESH = pl.DeviceIdType.MESH
BIG = 60 * 1024 * 1024


def place_of():
    z = lax.axis_index("dp")
    j = lax.axis_index("expert")
    return z, j, j // 2, j % 2


def other_chips(chip, chips):
    if chips == 4:
        square = [chip, chip + 1 - 2 * (chip % 2), chip + 2 - 4 * (chip // 2), 3 - chip]
        return lambda k: square[k], lambda k: square[k]
    return lambda k: (chip + k) % chips, lambda k: (chip + chips - k) % chips


def partners(z, n_dp):
    if n_dp == 4:
        pairs = [z, 3 - z, (z + 2) % 4, z + 1 - 2 * (z % 2)]
        return lambda k: pairs[k], lambda k: pairs[k]
    return lambda k: (z + k) % n_dp, lambda k: (z + n_dp - k) % n_dp


def greet(n_dp, n_expert):
    z, j, chip, core = place_of()
    chips = n_expert // 2
    barrier = pltpu.get_barrier_semaphore()
    for k in range(1, n_dp):
        pl.semaphore_signal(
            barrier, inc=1, device_id=((z + k) % n_dp, j), device_id_type=MESH
        )
    for k in range(1, chips):
        other = ((chip + k) % chips) * 2 + core
        pl.semaphore_signal(barrier, inc=1, device_id=(z, other), device_id_type=MESH)
    pl.semaphore_signal(
        barrier, inc=1, device_id=(z, chip * 2 + 1 - core), device_id_type=MESH
    )
    pl.semaphore_wait(barrier, n_dp - 1 + chips - 1 + 1)


def remote(source, target, send, receive, device):
    return pltpu.make_async_remote_copy(
        src_ref=source,
        dst_ref=target,
        send_sem=send,
        recv_sem=receive,
        device_id=device,
        device_id_type=MESH,
    )


def exchange(n_dp, pairs, send, receive):
    z, j, chip, core = place_of()
    to_plane, unused = partners(z, n_dp)
    copies = []
    for i, (source, target) in enumerate(pairs):
        for k in range(1, n_dp):
            to = to_plane(k)
            copies.append(
                remote(source(to), target(z), send.at[i, k], receive.at[i, k], (to, j))
            )
    return copies


def moves(pairs, stages, local):
    if not stages:
        copies = [
            pltpu.make_async_copy(source, target, local.at[i, 0])
            for i, (source, target) in enumerate(pairs)
        ]
        for copy in copies:
            copy.start()
        return [], copies
    bring = [
        pltpu.make_async_copy(source, stages[i], local.at[i, 0])
        for i, (source, target) in enumerate(pairs)
    ]
    put = [
        pltpu.make_async_copy(stages[i], target, local.at[i, 1])
        for i, (source, target) in enumerate(pairs)
    ]
    return bring, put


def nothing(ins, outs):
    return []


def gather_kernel(
    n_dp, n_expert, n_items, places, cuts, puts, finish, n_cut, n_out, n_stages, *refs
):
    z, j, chip, core = place_of()
    chips = n_expert // 2
    square = chips == 4
    to_chip, from_chip = other_chips(chip, chips)
    sources = refs[:n_items]
    cut_in = refs[n_items : n_items + n_cut]
    at = n_items + n_cut
    targets = refs[at : at + n_items]
    cut_out = refs[at + n_items : at + n_items + n_out]
    (
        send_c,
        recv_c,
        send_b,
        recv_b,
        send_a,
        recv_a,
        local,
        send_x,
        recv_x,
        local_y,
        *stages,
    ) = refs[at + n_items + n_out :]
    greet(n_dp, n_expert)
    mate = (z, chip * 2 + 1 - core)
    near = (1, 2) if square else tuple(range(1, chips))

    def slot(i, plane, column):
        return places[i](targets[i], plane * n_expert + column)

    def pass_on(i, plane, source, column, k, chip_to):
        return remote(
            source,
            slot(i, plane, column),
            send_b.at[i, plane, k],
            recv_b.at[i, plane, k],
            (z, chip_to * 2 + core),
        )

    def hand(i, plane, source):
        for k in near:
            pass_on(i, plane, source, j, k, to_chip(k)).start()
        remote(
            source, slot(i, plane, j), send_a.at[i, plane, 0], recv_a.at[i, plane, 0], mate
        ).start()

    def along(i, plane, source, way, step):
        return remote(
            source, slot(i, plane, j), send_c.at[i, way, plane], recv_c.at[i, plane], (z + step, j)
        )

    def at_distance(d, body):
        if d == 0:
            body(z, 0)
            return

        @pl.when(z >= d)
        def _():
            body(z - d, 0)

        @pl.when(z + d < n_dp)
        def _():
            body(z + d, 1)

    for i in range(n_items):

        @pl.when(z < n_dp - 1)
        def _():
            along(i, z, sources[i], 0, 1).start()

        @pl.when(z > 0)
        def _():
            along(i, z, sources[i], 1, -1).start()

        hand(i, z, sources[i])
        pltpu.make_async_copy(sources[i], slot(i, z, j), local.at[i]).start()

    def relay(plane, way):
        step = -1 if way else 1
        for i in range(n_items):
            block = slot(i, plane, j)
            along(i, plane, block, way, step).wait_recv()

            @pl.when(z > 0 if way else z < n_dp - 1)
            def _():
                along(i, plane, block, way, step).start()

            hand(i, plane, block)

    for d in range(1, n_dp):
        at_distance(d, relay)
    pairs = cuts(cut_in, cut_out)
    copies = exchange(n_dp, pairs, send_x, recv_x)
    for copy in copies:
        copy.start()
    own = [(source(z), target(z)) for source, target in pairs]
    bring, put = moves(own + puts(cut_in, cut_out), stages, local_y)
    for copy in bring:
        copy.start()
    for one, other in zip(bring, put):
        one.wait()
        other.start()

    def arrive(i, plane, k):
        column = from_chip(k) * 2 + core
        block = slot(i, plane, column)
        pass_on(i, plane, block, column, k, chip).wait_recv()
        remote(block, block, send_a.at[i, plane, k], recv_a.at[i, plane, k], mate).start()
        return block, column

    def arrived(plane, way):
        for i in range(n_items):
            for k in near:
                block, column = arrive(i, plane, k)
                if square:

                    @pl.when(plane % 2 == k - 1)
                    def _():
                        pass_on(i, plane, block, column, 3, to_chip(3 - k)).start()

    def crossed(plane, way):
        for i in range(n_items):
            arrive(i, plane, 3)

    for d in range(n_dp):
        at_distance(d, arrived)
    if square:
        for d in range(n_dp):
            at_distance(d, crossed)

    for i in range(n_items):
        for plane in range(n_dp):
            for k in range(chips):
                column = (from_chip(k) if k else chip) * 2 + 1 - core
                block = slot(i, plane, column)
                remote(
                    block, block, send_a.at[i, plane, k], recv_a.at[i, plane, k], mate
                ).wait_recv()
        pltpu.make_async_copy(sources[i], slot(i, z, j), local.at[i]).wait()
    finish(targets, cut_in, cut_out)
    for i in range(n_items):
        for plane in range(n_dp):
            block = slot(i, plane, j)
            for k in range(1, chips):
                pass_on(i, plane, block, j, k, chip).wait_send()
            for k in range(chips):
                remote(
                    block, block, send_a.at[i, plane, k], recv_a.at[i, plane, k], mate
                ).wait_send()

            @pl.when((z < n_dp - 1) & (z >= plane))
            def _():
                along(i, plane, block, 0, 1).wait_send()

            @pl.when((z > 0) & (z <= plane))
            def _():
                along(i, plane, block, 1, -1).wait_send()

    for copy in copies + put:
        copy.wait()


def gather_call(
    n_dp,
    n_expert,
    items,
    shapes,
    places,
    cut_in,
    cut_shapes,
    cuts,
    aliases,
    number,
    stages,
    puts=nothing,
    finish=lambda items, ins, outs: None,
):
    chips = n_expert // 2
    n, m = len(items), len(cut_shapes)
    dma = pltpu.SemaphoreType.DMA
    anywhere = pl.BlockSpec(memory_space=pl.ANY)
    return pl.pallas_call(
        functools.partial(
            gather_kernel,
            n_dp,
            n_expert,
            n,
            places,
            cuts,
            puts,
            finish,
            len(cut_in),
            m,
            len(stages),
        ),
        out_shape=[*shapes, *cut_shapes],
        in_specs=[anywhere] * (n + len(cut_in)),
        out_specs=[anywhere] * (n + m),
        scratch_shapes=[
            dma((n, 2, n_dp)),
            dma((n, n_dp)),
            dma((n, n_dp, chips)),
            dma((n, n_dp, chips)),
            dma((n, n_dp, chips)),
            dma((n, n_dp, chips)),
            dma((n,)),
            dma((4, n_dp)),
            dma((4, n_dp)),
            dma((max(len(stages), 4), 2)),
            *[pltpu.VMEM(stage, jnp.bfloat16) for stage in stages],
        ],
        input_output_aliases=aliases,
        compiler_params=pltpu.CompilerParams(
            collective_id=number, has_side_effects=True, vmem_limit_bytes=BIG
        ),
    )(*items, *cut_in)


def scatter_kernel(
    n_dp, n_expert, n_arrays, items, n_cut, n_out, cuts, puts, middle, rings, n_rings, *refs
):
    n_items = len(items)
    z, j, chip, core = place_of()
    chips = n_expert // 2
    square = chips == 4
    to_chip, from_chip = other_chips(chip, chips)
    refs = list(refs)

    def take(count):
        taken = refs[:count]
        del refs[:count]
        return taken

    sources, cut_in, targets, cut_out = take(n_arrays), take(n_cut), take(n_arrays), take(n_out)
    ring, got_a, got_b, got_c = take(n_rings), take(n_items), take(n_items), take(n_items)
    transit = take(n_items)
    (
        send_a,
        recv_a,
        send_b,
        recv_b,
        send_c,
        recv_c,
        send_t,
        recv_t,
        local,
        send_x,
        recv_x,
        local_y,
        *stages,
    ) = refs
    greet(n_dp, n_expert)
    mate = (z, chip * 2 + 1 - core)
    order = [3, 1, 2, 0] if square else [*range(1, chips), 0]
    half = n_dp // 2
    low, high = pl.ds(0, half), pl.ds(half, n_dp - half)

    def chip_of(k):
        return to_chip(k) if k else chip

    def source(i, column):
        array, first, rows = items[i]
        return sources[array].at[:, column, pl.ds(first, rows)]

    def to_mate(i, k):
        return remote(
            source(i, chip_of(k) * 2 + 1 - core),
            got_a[i].at[k],
            send_a.at[i, k],
            recv_a.at[i, k],
            mate,
        )

    turn = [0] * n_rings
    loads = []
    for i in range(n_items):
        for k in order:
            loads.append((i, k, turn[rings[i]] % 2))
            turn[rings[i]] += 1

    def load(i, k, at):
        return pltpu.make_async_copy(
            source(i, chip_of(k) * 2 + core), ring[rings[i]].at[at], local.at[rings[i], at]
        )

    def send_near(i, k, part, number):
        return remote(
            got_a[i].at[k, part],
            got_b[i].at[k - 1, part],
            send_b.at[i, number],
            recv_b.at[i, number],
            (z, to_chip(k) * 2 + core),
        )

    def send_over(i, k, part):
        return remote(
            got_a[i].at[3, part],
            transit[i].at[k - 1],
            send_t.at[i, k],
            recv_t.at[i, k],
            (z, to_chip(k) * 2 + core),
        )

    def send_far(i, k):
        return remote(
            got_a[i].at[k],
            got_b[i].at[k - 1],
            send_b.at[i, k],
            recv_b.at[i, k],
            (z, to_chip(k) * 2 + core),
        )

    def along(i, plane, way):
        slot = n_dp - (z - 1) + plane if way else plane - (z + 1)
        return remote(
            got_a[i].at[0, plane],
            got_c[i].at[slot],
            send_c.at[i, plane],
            recv_c.at[i, slot],
            (z - 1 if way else z + 1, j),
        )

    def from_along(i, slot):
        return remote(
            got_c[i].at[slot], got_c[i].at[slot], send_c.at[i, 0], recv_c.at[i, slot], mate
        )

    f32 = jnp.float32

    def add(i, planes, target, terms):
        rows = got_a[i].shape[2]
        per = rows // 16

        def step(n, unused):
            plane = n // per
            at = pl.ds(pl.multiple_of((n % per) * 16, 16), 16)
            total = terms[0](plane, at).astype(f32)
            for term in terms[1:]:
                total = total + term(plane, at).astype(f32)
            target(plane, at, total)
            return unused

        lax.fori_loop(0, planes * per, step, 0)

    def grow(i, k, first, planes, term):
        def target(plane, at, total):
            got_a[i][k, plane + first, at] = total.astype(got_a[i].dtype)

        add(i, planes, target, [lambda plane, at: got_a[i][k, plane + first, at], term])

    for i in range(n_items):
        for k in order:
            to_mate(i, k).start()
    started = 0
    ahead = [0] * n_rings
    for i, k, at in loads:
        if ahead[rings[i]] < 2:
            load(i, k, at).start()
            ahead[rings[i]] += 1
    pairs = cuts(cut_in, cut_out)
    copies = exchange(n_dp, pairs, send_x, recv_x)
    own = [(source(z), target(z)) for source, target in pairs]
    bring, put = moves(own + puts(cut_in, cut_out), stages, local_y)
    for copy in bring:
        copy.start()

    def over_cores(i):
        for n, (item, k, at) in enumerate(loads):
            if item != i:
                continue
            load(i, k, at).wait()
            to_mate(i, k).wait_recv()
            grow(i, k, 0, n_dp, lambda plane, rows: ring[rings[i]][at, plane, rows])
            later = [one for one in loads[n + 1 :] if rings[one[0]] == rings[i]]
            if len(later) >= 2:
                load(*later[1]).start()
            if not k:
                continue
            if not square:
                send_far(i, k).start()
            elif k == 3:
                send_over(i, 1, low).start()
                send_over(i, 2, high).start()
            elif k == 1:
                send_near(i, 1, low, 0).start()
            else:
                send_near(i, 2, high, 1).start()

    def pass_over(i):
        if not square:
            return
        send_over(i, 2, high).wait_recv()
        grow(i, 1, half, n_dp - half, lambda plane, rows: transit[i][1, plane, rows])
        send_near(i, 1, high, 2).start()
        send_over(i, 1, low).wait_recv()
        grow(i, 2, 0, half, lambda plane, rows: transit[i][0, plane, rows])
        send_near(i, 2, low, 3).start()

    def over_chips(i):
        if square:
            send_near(i, 1, low, 0).wait_recv()
            send_near(i, 2, high, 1).wait_recv()
            send_near(i, 1, high, 2).wait_recv()
            send_near(i, 2, low, 3).wait_recv()
        else:
            for k in range(1, chips):
                send_far(i, k).wait_recv()
        heard = 2 if square else chips - 1

        def target(plane, at, total):
            got_a[i][0, plane, at] = total.astype(got_a[i].dtype)

        terms = [lambda plane, at: got_a[i][0, plane, at]]
        for other in range(heard):
            terms.append(lambda plane, at, other=other: got_b[i][other, plane, at])
        add(i, n_dp, target, terms)
        for d in range(n_dp - 1, 0, -1):
            for way in (0, 1):
                plane = z - d if way else z + d

                @pl.when(z == (n_dp - 1 if way else 0))
                def _():
                    along(i, plane, way).start()

    def over_planes(i):
        for d in range(n_dp - 2, 0, -1):
            for way in (0, 1):
                plane = z - d if way else z + d
                slot = n_dp - d if way else d

                @pl.when((plane >= 0) & (z < n_dp - 1) if way else (plane < n_dp) & (z > 0))
                def _():
                    from_along(i, slot).wait_recv()
                    grow(i, 0, plane, 1, lambda unused, at: got_c[i][slot, at])
                    along(i, plane, way).start()

    def finish(i):
        array, first, rows = items[i]

        def here(at):
            return pl.ds(pl.multiple_of(first + at.start, 16), 16)

        def own(unused, at, total):
            targets[array][here(at)] = total

        add(i, 1, own, [lambda unused, at: got_a[i][0, z, at]])
        for slot, arrives in ((0, z > 0), (n_dp, z < n_dp - 1)):

            @pl.when(arrives)
            def _():
                from_along(i, slot).wait_recv()
                add(
                    i,
                    1,
                    own,
                    [
                        lambda unused, at: targets[array][here(at)],
                        lambda unused, at: got_c[i][slot, at],
                    ],
                )

    steps = (over_cores, pass_over, over_chips, over_planes, finish)
    share = -(-len(copies) // n_items)
    for n in range(n_items + len(steps) - 1):
        for copy in copies[n * share : (n + 1) * share]:
            copy.start()
        for late, step in enumerate(steps):
            if 0 <= n - late < n_items:
                step(n - late)
        if n == min(1, n_items - 1):
            for one, other in zip(bring, put):
                one.wait()
                other.start()
            middle(cut_in, cut_out)
    for i in range(n_items):
        for k in range(chips):
            to_mate(i, k).wait_send()
        if square:
            for k, part in ((1, low), (2, high)):
                send_over(i, k, part).wait_send()
            for k, part, number in ((1, low, 0), (2, high, 1), (1, high, 2), (2, low, 3)):
                send_near(i, k, part, number).wait_send()
        else:
            for k in range(1, chips):
                send_far(i, k).wait_send()
        for plane in range(n_dp):

            @pl.when(z != plane)
            def _():
                remote(
                    got_a[i].at[0, plane],
                    got_c[i].at[0],
                    send_c.at[i, plane],
                    recv_c.at[i, 0],
                    mate,
                ).wait_send()

    for copy in copies + put:
        copy.wait()


def scatter_call(
    n_dp,
    n_expert,
    arrays,
    splits,
    cut_in,
    cut_shapes,
    cuts,
    number,
    aliases,
    stages,
    puts=nothing,
    middle=nothing,
):
    chips = n_expert // 2
    square = chips == 4
    items = []
    for array, (one, split) in enumerate(zip(arrays, splits)):
        rows = one.shape[2] // split
        items += [(array, first, rows) for first in range(0, one.shape[2], rows)]
    n, m = len(items), len(cut_shapes)
    count = len(arrays)
    dma = pltpu.SemaphoreType.DMA
    anywhere = pl.BlockSpec(memory_space=pl.ANY)
    blocks = [(rows, arrays[array].shape[3]) for array, unused, rows in items]
    kinds = sorted(set(blocks))
    rings = [kinds.index(block) for block in blocks]
    bf16 = jnp.bfloat16
    heard = 2 if square else chips - 1
    return pl.pallas_call(
        functools.partial(
            scatter_kernel,
            n_dp,
            n_expert,
            count,
            items,
            len(cut_in),
            m,
            cuts,
            puts,
            middle,
            rings,
            len(kinds),
        ),
        out_shape=[
            *[jax.ShapeDtypeStruct(one.shape[2:], jnp.float32) for one in arrays],
            *cut_shapes,
        ],
        in_specs=[anywhere] * (count + len(cut_in)),
        out_specs=[pl.BlockSpec(memory_space=pltpu.VMEM)] * count + [anywhere] * m,
        scratch_shapes=[
            *[pltpu.VMEM((2, n_dp, *kind), bf16) for kind in kinds],
            *[pltpu.VMEM((chips, n_dp, *block), bf16) for block in blocks],
            *[pltpu.VMEM((heard, n_dp, *block), bf16) for block in blocks],
            *[pltpu.VMEM((n_dp + 1, *block), bf16) for block in blocks],
            *[pltpu.VMEM((2, n_dp // 2, *(block if square else (16, 128))), bf16) for block in blocks],
            dma((n, chips)),
            dma((n, chips)),
            dma((n, chips)),
            dma((n, chips)),
            dma((n, n_dp)),
            dma((n, n_dp + 1)),
            dma((n, 3)),
            dma((n, 3)),
            dma((len(kinds), 2)),
            dma((16, n_dp)),
            dma((16, n_dp)),
            dma((max(len(stages), 16), 2)),
            *[pltpu.VMEM(stage, jnp.bfloat16) for stage in stages],
        ],
        input_output_aliases=aliases,
        compiler_params=pltpu.CompilerParams(
            collective_id=number, has_side_effects=True, vmem_limit_bytes=62 * 1024 * 1024
        ),
    )(*arrays, *cut_in)


def scatter_all(
    n_dp,
    n_expert,
    items,
    splits,
    cut_in,
    cut_shapes,
    cuts,
    number,
    aliases,
    stages,
    puts=nothing,
    middle=nothing,
):
    chips = n_expert // 2
    blocks = (2 * chips - 1 if chips != 4 else 7) * n_dp + n_dp + 3
    need = sum(blocks * item.shape[2] * item.shape[3] * 2 for item in items)
    kinds = {(item.shape[2] // split, item.shape[3]) for item, split in zip(items, splits)}
    need += sum(2 * n_dp * kind[0] * kind[1] * 2 for kind in kinds)
    need += sum(stage[0] * stage[1] * stage[2] * 2 for stage in stages)
    pieces = -(-need // (61 * 1024 * 1024))
    tiles = [item.shape[3] // 128 for item in items]
    results = [[] for item in items]
    extra = []
    for piece in range(pieces):
        ends = [(t * piece // pieces * 128, t * (piece + 1) // pieces * 128) for t in tiles]
        used = [i for i, (low, high) in enumerate(ends) if high > low]
        first = piece == 0
        outs = scatter_call(
            n_dp,
            n_expert,
            [items[i][..., ends[i][0] : ends[i][1]] if pieces > 1 else items[i] for i in used],
            [splits[i] for i in used],
            cut_in if first else [],
            cut_shapes if first else [],
            cuts if first else nothing,
            number + piece,
            {len(used) + a: len(used) + b for a, b in aliases} if first else {},
            stages if first else [],
            puts if first else nothing,
            middle if first else nothing,
        )
        for i, out in zip(used, outs):
            results[i].append(out)
        if first:
            extra = outs[len(used) :]
    return [one[0] if len(one) == 1 else jnp.concatenate(one, axis=1) for one in results], extra


def dot(left, right, dims):
    return lax.dot_general(
        left, right, ((dims[:1], dims[1:]), ((), ())), preferred_element_type=jnp.float32
    )


def picks(slots_ref, number):
    pair = slots_ref.shape[2]
    rows = lax.broadcasted_iota(jnp.int32, (2 * CAP, pair), 0)
    return [slots_ref[0, e : e + 1, :] == rows for e in range(number)]


def pick_kernel(number, experts_all, slots_ref, x_ref, g_ref, router_ref, rows_ref, grows_ref, gates_ref):
    chosen = picks(slots_ref, number)
    pick = jnp.concatenate(chosen, axis=0).astype(jnp.bfloat16)
    size = 2 * CAP
    x = x_ref[...]
    logits = dot(router_ref[...], x, (0, 1))
    names = lax.broadcasted_iota(jnp.int32, logits.shape, 0)
    logits = jnp.where(names < experts_all, logits, -1e30)
    weights = jnp.exp(logits - jnp.max(logits, axis=0, keepdims=True))
    probs = weights / jnp.sum(weights, axis=0, keepdims=True)
    for e in range(number):
        gate = jnp.sum(jnp.where(chosen[e], probs[e : e + 1, :], 0.0), axis=1, keepdims=True)
        gates_ref[e] = jnp.broadcast_to(gate, (size, 128))
    picked = dot(pick, x, (1, 0)).astype(jnp.bfloat16)
    for e in range(number):
        rows_ref[e] = picked[e * size : (e + 1) * size]
    picked = dot(pick, g_ref[...], (1, 0)).astype(jnp.bfloat16)
    for e in range(number):
        grows_ref[e] = picked[e * size : (e + 1) * size]


def expert_kernel(steps, half, n_weights, n_into, n_pack, names_ref, x_ref, g_ref, gates_ref, *refs):
    weights, refs = refs[:n_weights], refs[n_weights:]
    down_ref, refs = refs[0], refs[1 + n_into :]
    (
        y_ref,
        dx_ref,
        probs_ref,
        dgate_ref,
        dup_ref,
        ddown_ref,
        *pack_refs,
        sum_gate,
        sum_up,
    ) = refs
    bf16 = jnp.bfloat16
    g = g_ref[0]
    rows, width = x_ref.shape[1:]
    part = dgate_ref.shape[2]
    gate = gates_ref[0][:, :1]
    if n_weights == 2:
        piece = 512
        gate_ref, up_ref = weights
        gate_mid = dot(x_ref[0], gate_ref[0], (1, 0))
        up_mid = dot(x_ref[0], up_ref[0], (1, 0))
        spans = [
            (pl.ds(at, piece), gate_ref, up_ref, pl.ds(at, piece), pl.ds(0, part), pl.ds(0, part))
            for at in range(0, width, piece)
        ]
    else:
        piece = width // n_weights
        spans = []
        gate_mid = up_mid = 0.0
        for n, ref in enumerate(weights):
            span = pl.ds(pl.multiple_of(names_ref[1 + n], piece), piece)
            x_part = x_ref[0, :, span]
            gate_mid = gate_mid + dot(x_part, ref[0, :, :part], (1, 0))
            up_mid = up_mid + dot(x_part, ref[0, :, part:], (1, 0))
            spans.append((span, ref, ref, pl.ds(0, piece), pl.ds(0, part), pl.ds(part, part)))
    sigmoid = 1.0 / (1.0 + jnp.exp(-gate_mid))
    silu = gate_mid * sigmoid
    hidden = silu * up_mid
    hidden_low = hidden.astype(bf16)
    grad_plain = dot(g, down_ref[0], (1, 1))
    grad_gates = jnp.sum(grad_plain * hidden_low.astype(jnp.float32), axis=1, keepdims=True)
    high = grad_gates.astype(bf16).astype(jnp.float32)
    lane = lax.broadcasted_iota(jnp.int32, (rows, 128), 1)
    name = names_ref[0] + pl.program_id(0)
    probs_ref[0] = (
        jnp.where(lane == name, high, 0.0) + jnp.where(lane == name + half, grad_gates - high, 0.0)
    ).astype(bf16)
    grad_hidden = grad_plain * gate
    grad_gate = (
        grad_hidden * up_mid * sigmoid * (1.0 + gate_mid * (1.0 - sigmoid))
    ).astype(bf16)
    grad_up = (grad_hidden * silu).astype(bf16)
    scaled = (hidden * gate).astype(bf16)
    for at in range(0, width, piece):
        y_ref[0, :, at : at + piece] = (
            dot(hidden_low, down_ref[0, :, at : at + piece], (1, 0)) * gate
        ).astype(bf16)
    for span, gate_ref, up_ref, here, gate_columns, up_columns in spans:
        dx_ref[0, :, span] = (
            dot(grad_gate, gate_ref[0, here, gate_columns], (1, 1))
            + dot(grad_up, up_ref[0, here, up_columns], (1, 1))
        ).astype(bf16)
    step = pl.program_id(1)
    for span, *unused in spans:
        x_part = x_ref[0, :, span]
        here_gate = dot(x_part, grad_gate, (0, 0))
        here_up = dot(x_part, grad_up, (0, 0))
        here_down = dot(scaled, g_ref[0, :, span], (0, 0))
        if steps == 1:
            dgate_ref[0, span, :] = here_gate.astype(bf16)
            dup_ref[0, span, :] = here_up.astype(bf16)
            ddown_ref[0, :, span] = here_down
            continue

        @pl.when(step == 0)
        def _():
            sum_gate[span, :] = here_gate
            sum_up[span, :] = here_up
            ddown_ref[0, :, span] = here_down

        @pl.when(step > 0)
        def _():
            sum_gate[span, :] += here_gate
            sum_up[span, :] += here_up
            ddown_ref[0, :, span] += here_down

        @pl.when(step == steps - 1)
        def _():
            dgate_ref[0, span, :] = sum_gate[span, :].astype(bf16)
            dup_ref[0, span, :] = sum_up[span, :].astype(bf16)

    if n_pack:

        @pl.when((step == steps - 1) & (pl.program_id(0) < n_pack))
        def _():
            pack_ref = pack_refs[0]
            depth = pack_ref.shape[2]
            for plane in range(pack_ref.shape[0]):
                here = pl.ds(plane * depth, depth)
                pack_ref[plane, 0, :, :part] = dgate_ref[0, here, :]
                pack_ref[plane, 0, :, part:] = dup_ref[0, here, :]


def put_back(number, slots_ref, pairs):
    pick = jnp.concatenate(picks(slots_ref, number), axis=0).astype(jnp.bfloat16)
    piece = 512
    for source, target, first in pairs:
        width = source.shape[2]
        for at in range(0, width, piece):
            size = min(piece, width)
            part = source[:, :, at : at + size].reshape(-1, size)
            target[:, first + at : first + at + size] = dot(pick, part, (0, 0)).astype(
                jnp.bfloat16
            )


def place_back_kernel(number, slots_ref, dx_ref, probs_ref, back_ref):
    put_back(number, slots_ref, [(dx_ref, back_ref, 0), (probs_ref, back_ref, dx_ref.shape[2])])


def place_out_kernel(number, slots_ref, y_ref, out_ref):
    put_back(number, slots_ref, [(y_ref, out_ref, 0)])


def place_out(slots, y, out):
    pairs, number, pair = slots.shape
    pltpu.emit_pipeline(
        functools.partial(place_out_kernel, number),
        grid=(pairs,),
        in_specs=[
            pl.BlockSpec((1, number, pair), lambda p: (p, 0, 0)),
            pl.BlockSpec((number, 2 * CAP, D), lambda p: (0, p, 0)),
        ],
        out_specs=[pl.BlockSpec((pair, D), lambda p: (p, 0))],
    )(slots, y, out)


def pick_shapes(number, pairs):
    bf16 = jnp.bfloat16
    size = 2 * CAP
    return [
        jax.ShapeDtypeStruct((number, pairs * size, D), bf16),
        jax.ShapeDtypeStruct((number, pairs * size, D), bf16),
        jax.ShapeDtypeStruct((number, pairs * size, 128), jnp.float32),
    ]


def pick_rows(number, experts_all, slots, x_all, g_all, router, rows, grows, gates):
    pairs, _, pair = slots.shape
    size = 2 * CAP
    tokens = pl.BlockSpec((pair, D), lambda p: (p, 0))
    picked = pl.BlockSpec((number, size, D), lambda p: (0, p, 0))
    pltpu.emit_pipeline(
        functools.partial(pick_kernel, number, experts_all),
        grid=(pairs,),
        in_specs=[
            pl.BlockSpec((1, number, pair), lambda p: (p, 0, 0)),
            tokens,
            tokens,
            pl.BlockSpec(router.shape, lambda p: (0, 0)),
        ],
        out_specs=[picked, picked, pl.BlockSpec((number, size, 128), lambda p: (0, p, 0))],
    )(slots, x_all, g_all, router, rows, grows, gates)


def expert_call(names, half, low, number, rows, grows, gates, weights, down, into=(), pack=()):
    total, depth, _ = rows.shape
    part = down.shape[1]
    size = depth
    while size > 768:
        size //= 2
    steps = depth // size
    bf16 = jnp.bfloat16
    f32 = jnp.float32

    def from_rows(width):
        return pl.BlockSpec((1, size, width), lambda e, r: (e + low, r, 0))

    def whole(*shape):
        return pl.BlockSpec((1, *shape), lambda e, r: (e, 0, 0))

    def from_whole(*shape):
        return pl.BlockSpec((1, *shape), lambda e, r: (e + low, 0, 0))

    packed = [
        pl.BlockSpec(
            (planes, 1, D // planes, 2 * part),
            lambda e, r, n=n: (0, lax.min(e, n - 1), 0, 0),
        )
        for n, planes in ([pack] if pack else [])
    ]
    keep = (D, part) if steps > 1 else (16, 128)
    return pl.pallas_call(
        functools.partial(
            expert_kernel, steps, half, len(weights), len(into), pack[0] if pack else 0
        ),
        grid=(number, steps),
        in_specs=[
            pl.BlockSpec(memory_space=pltpu.SMEM),
            from_rows(D),
            from_rows(D),
            from_rows(128),
            *[(from_whole if len(weights) == 2 else whole)(*one.shape[1:]) for one in weights],
            from_whole(part, D),
            *[pl.BlockSpec(memory_space=pl.ANY)] * len(into),
        ],
        out_specs=[
            from_rows(D),
            from_rows(D),
            from_rows(128),
            whole(D, part),
            whole(D, part),
            from_whole(part, D),
            *packed,
        ],
        out_shape=[
            jax.ShapeDtypeStruct((total, depth, D), bf16),
            jax.ShapeDtypeStruct((total, depth, D), bf16),
            jax.ShapeDtypeStruct((total, depth, 128), bf16),
            jax.ShapeDtypeStruct((number, D, part), bf16),
            jax.ShapeDtypeStruct((number, D, part), bf16),
            jax.ShapeDtypeStruct((total, part, D), f32),
            *[
                jax.ShapeDtypeStruct((planes, n, D // planes, 2 * part), bf16)
                for n, planes in ([pack] if pack else [])
            ],
        ],
        input_output_aliases={
            5 + len(weights) + i: out for i, out in zip(range(len(into)), (0, 1, 2, 5))
        },
        scratch_shapes=[pltpu.VMEM(keep, f32), pltpu.VMEM(keep, f32)],
        compiler_params=pltpu.CompilerParams(vmem_limit_bytes=BIG),
    )(names, rows, grows, gates, *weights, down, *into)


def place_back(slots, dx, probs):
    pairs, number, pair = slots.shape
    size = 2 * CAP

    def rows(one):
        return pl.BlockSpec((number, size, one.shape[2]), lambda p: (0, p, 0))

    return pl.pallas_call(
        functools.partial(place_back_kernel, number),
        grid=(pairs,),
        in_specs=[pl.BlockSpec((1, number, pair), lambda p: (p, 0, 0)), rows(dx), rows(probs)],
        out_specs=pl.BlockSpec((pair, D + 128), lambda p: (p, 0)),
        out_shape=jax.ShapeDtypeStruct((pairs * pair, D + 128), jnp.bfloat16),
        compiler_params=pltpu.CompilerParams(vmem_limit_bytes=BIG),
    )(slots, dx, probs)


def widen_kernel(*refs):
    half = len(refs) // 2
    for source, target in zip(refs[:half], refs[half:]):
        target[...] = source[...].astype(jnp.float32)


def widen(spans, values):
    number, rows, columns = values[0].shape
    (low, high), (again, end) = spans

    def chosen(e):
        return (jnp.where(e < high - low, e + low, e - (high - low) + again), 0, 0)

    block = pl.BlockSpec((1, rows, columns), chosen)
    return pl.pallas_call(
        widen_kernel,
        grid=(high - low + end - again,),
        in_specs=[block] * len(values),
        out_specs=[block] * len(values),
        out_shape=[jax.ShapeDtypeStruct(one.shape, jnp.float32) for one in values],
        compiler_params=pltpu.CompilerParams(vmem_limit_bytes=BIG),
    )(*values)


def widen_pieces_kernel(low, n_pieces, offsets_ref, *refs):
    pieces, refs = refs[:n_pieces], refs[n_pieces + 2 :]
    targets, wide, sems = refs[:2], refs[2], refs[3]
    part = wide.shape[4]
    copies = []
    for k, piece in enumerate(pieces):
        columns = pl.ds(pl.multiple_of(offsets_ref[k], part), part)
        for n in range(2):
            wide[k, n] = piece[:, :, n * part : (n + 1) * part].astype(jnp.float32)
            copy = pltpu.make_async_copy(
                wide.at[k, n], targets[n].at[pl.ds(low, piece.shape[0]), :, columns], sems.at[k, n]
            )
            copy.start()
            copies.append(copy)
    for copy in copies:
        copy.wait()


def widen_pieces(offsets, low, pieces, into):
    size, rows, columns = pieces[0].shape
    anywhere = pl.BlockSpec(memory_space=pl.ANY)
    count = len(pieces)
    return pl.pallas_call(
        functools.partial(widen_pieces_kernel, low, count),
        in_specs=[
            pl.BlockSpec(memory_space=pltpu.SMEM),
            *[pl.BlockSpec(memory_space=pltpu.VMEM)] * count,
            anywhere,
            anywhere,
        ],
        out_specs=[anywhere, anywhere],
        out_shape=[jax.ShapeDtypeStruct(one.shape, one.dtype) for one in into],
        scratch_shapes=[
            pltpu.VMEM((count, 2, size, rows, columns // 2), jnp.float32),
            pltpu.SemaphoreType.DMA((count, 2)),
        ],
        input_output_aliases={1 + count: 0, 2 + count: 1},
        compiler_params=pltpu.CompilerParams(vmem_limit_bytes=BIG),
    )(offsets, *pieces, *into)


def shards(
    n_dp,
    n_expert,
    tokens,
    cotangent,
    lengths,
    routes,
    w_query,
    w_key,
    w_value,
    w_out,
    w_router,
    gain_attn,
    gain_query,
    gain_key,
    gain_mlp,
    w_gate,
    w_up,
    w_down,
):
    groups = n_dp * n_expert
    bf16 = jnp.bfloat16
    number = w_gate.shape[0]
    ff = w_gate.shape[2]
    part = ff // n_dp
    experts_all = w_router.shape[1]
    width = 128
    small = jnp.concatenate(
        [
            w_router,
            gain_attn[:, None],
            gain_query[:, None],
            gain_key[:, None],
            gain_mlp[:, None],
            jnp.zeros((w_router.shape[0], width - experts_all - 4), bf16),
        ],
        axis=1,
    )
    hits = jnp.any(
        routes[:, :, None] == jnp.arange(width, dtype=jnp.int32)[None, None, :], axis=1
    ).astype(bf16)
    count = tokens.shape[0]
    rows_each = w_query.shape[0]
    extras = jnp.concatenate([hits, jnp.pad(small, ((0, count - rows_each), (0, 0)))], axis=1)
    weights = jnp.stack([w_query, w_key, w_value, w_out])
    depth = w_gate.shape[1]
    early = number // 4
    beside = early + number // 8
    late = number - number // 4
    back_beside = number // 8
    back_third = back_beside + max(number // 4, 1)
    back_late = back_third + number // 4
    me = lax.axis_index("dp")
    cut_shape = jax.ShapeDtypeStruct((number, n_dp * depth, part), bf16)

    def row_block(size):
        return lambda ref, block: ref.at[pl.ds(pl.multiple_of(block * size, 16), size)]

    def columns_at(at):
        return pl.ds(pl.multiple_of(at * part, part), part)

    def rows_at(at):
        return pl.ds(pl.multiple_of(at * depth, depth), depth)

    def recut(low, high):
        def cuts(ins, outs):
            def pair(n):
                chosen = pl.ds(low, high - low)
                return (
                    lambda to: ins[n].at[chosen, :, columns_at(to)],
                    lambda at: outs[n].at[chosen, rows_at(at)],
                )

            return [pair(0), pair(1)]

        return cuts

    to_plane, from_plane = partners(me, n_dp)

    def permuted(pieces, chained=False):
        got = []
        for k, piece in enumerate(pieces, 1):
            if chained and got:
                piece, last = lax.optimization_barrier((piece, got.pop()))
                got.append(last)
            paths = [(i, partners(i, n_dp)[0](k)) for i in range(n_dp)]
            got.append(lax.ppermute(piece, "dp", paths))
        return got

    def cut_pieces(low, high, first_k, ins, outs):
        to, unused = partners(lax.axis_index("dp"), n_dp)
        pairs = []
        for k, piece in enumerate(outs, first_k):
            for n in range(2):
                source = ins[n].at[pl.ds(low, high - low), :, columns_at(to(k))]
                pairs.append((source, piece.at[:, :, pl.ds(n * part, part)]))
        return pairs

    def piece_shapes(size, first_k):
        shape = jax.ShapeDtypeStruct((size, depth, 2 * part), bf16)
        return [shape] * (n_dp - first_k if size else 0)

    def stages(*sizes):
        return [(size, depth, part) for size in sizes]

    soon_shapes = piece_shapes(beside - early, 1)
    late_shapes = piece_shapes(number - late, 0)
    n_soon = len(soon_shapes)

    weights_all, extras_all, gate_early, up_early, *pieces = gather_call(
        n_dp,
        n_expert,
        [weights, extras],
        [
            jax.ShapeDtypeStruct((4, groups * rows_each, D), bf16),
            jax.ShapeDtypeStruct((groups * count, 2 * width), bf16),
        ],
        [
            lambda ref, block: ref.at[
                :, pl.ds(pl.multiple_of(block * rows_each, 16), rows_each)
            ],
            row_block(count),
        ],
        [w_gate, w_up],
        [cut_shape, cut_shape, *soon_shapes, *late_shapes],
        recut(0, early),
        {},
        0,
        stages(
            *[early] * 2,
            *[beside - early] * (2 * n_soon),
            *[number - late] * (2 * n_dp),
        ),
        lambda ins, outs: cut_pieces(early, beside, 1, ins, outs[2 : 2 + n_soon])
        + cut_pieces(late, number, 0, ins, outs[2 + n_soon :]),
    )
    soon_pieces, late_pieces = pieces[:n_soon], pieces[n_soon:]
    query_weight, key_weight, value_weight, out_weight = (weights_all[i] for i in range(4))
    small_all = (
        extras_all[:, width:].reshape(groups, count, width)[:, :rows_each].reshape(-1, width)
    )
    hits_all = extras_all[:, :experts_all]
    router_weight = small_all[:, :experts_all]
    gains = small_all[:, experts_all : experts_all + 4].astype(jnp.float32)
    attn_gain, query_gain, key_gain, mlp_gain = (gains[:, i] for i in range(4))
    inputs = tokens.astype(jnp.float32)
    segment, position, places = layout(lengths[0], count)
    half = HD // 2
    freq = 10000.0 ** (-2.0 * jnp.arange(half, dtype=jnp.float32) / HD)
    angle = position.astype(jnp.float32)[:, None] * freq[None, :]
    cosine = jnp.cos(angle)[:, None, :]
    sine = jnp.sin(angle)[:, None, :]
    scale = HD ** (-0.5)
    normed, attn_inverse = rms_forward(inputs, attn_gain)
    normed_low = normed.astype(bf16)
    query_raw = product(normed_low, query_weight, "td,de->te")
    key_raw = product(normed_low, key_weight, "td,de->te")
    value_low = product(normed_low, value_weight, "td,de->te").astype(bf16)
    query_normed, query_inverse = rms_forward(query_raw, query_gain)
    key_normed, key_inverse = rms_forward(key_raw, key_gain)
    query_low = rotate(query_normed, cosine, sine).astype(bf16).reshape(count, HEADS, HD)
    key_low = rotate(key_normed, cosine, sine).astype(bf16).reshape(count, HEADS, HD)
    value_heads = value_low.reshape(count, HEADS, HD)
    allowed = (segment[:, None] == segment[None, :]) & (places[None, :] <= places[:, None])
    scores = product(query_low, key_low, "qhd,khd->hqk") * scale
    scores = jnp.where(allowed[None], scores, -1e30)
    probs = jax.nn.softmax(scores, axis=-1)
    probs_low = probs.astype(bf16)
    attended_low = product(probs_low, value_heads, "hqk,khd->qhd").reshape(count, D).astype(bf16)
    middle = inputs + product(attended_low, out_weight, "td,de->te")
    mlp_normed, mlp_inverse = rms_forward(middle, mlp_gain)
    mlp_low = mlp_normed.astype(bf16)
    router = jax.nn.softmax(product(mlp_low, router_weight, "td,de->te"), axis=-1)

    first = lax.axis_index("expert") * number
    hit = lax.dynamic_slice_in_dim(hits_all, first, number, 1).reshape(groups, count, number)
    before = jnp.tril(jnp.ones((count, count), bf16), -1)
    slot = product(before, hit, "ts,bse->bet").astype(jnp.int32)
    slot = jnp.where(jnp.transpose(hit, (0, 2, 1)) > 0, slot, -1)
    slot = slot.reshape(groups // 2, 2, number, count)
    shift = jnp.array([0, CAP], jnp.int32)[None, :, None, None]
    slots = jnp.transpose(jnp.where(slot < 0, -1, slot + shift), (0, 2, 1, 3))
    slots = slots.reshape(groups // 2, number, 2 * count)
    router_own = jnp.pad(
        jnp.roll(router_weight, -first, axis=1), ((0, 0), (0, width - experts_all))
    )
    if n_soon:
        mlp_low, *soon_pieces = lax.optimization_barrier((mlp_low, *permuted(soon_pieces)))

    def put_weights(ins, outs):
        chosen = pl.ds(early, beside - early)
        unused, heard = partners(lax.axis_index("dp"), n_dp)
        pairs = []
        if beside > early:
            own = lax.axis_index("dp")
            for n in range(2):
                source = ins[n].at[chosen, :, columns_at(own)]
                pairs.append((source, outs[n].at[chosen, rows_at(own)]))
        for k, piece in enumerate(ins[6:], 1):
            for n in range(2):
                columns = piece.at[:, :, pl.ds(n * part, part)]
                pairs.append((columns, outs[n].at[chosen, rows_at(heard(k))]))
        return pairs

    def pick_all(items, ins, outs):
        pick_rows(number, experts_all, ins[4], *items, ins[5], *outs[2:])

    unused, unused, gate_cut, up_cut, rows, grows, gates = gather_call(
        n_dp,
        n_expert,
        [mlp_low, cotangent],
        [jax.ShapeDtypeStruct((groups * count, D), bf16)] * 2,
        [row_block(count)] * 2,
        [w_gate, w_up, gate_early, up_early, slots, router_own, *soon_pieces],
        [cut_shape, cut_shape, *pick_shapes(number, groups // 2)],
        recut(beside, late),
        {4: 2, 5: 3},
        1,
        stages(*[late - beside] * 2, *[beside - early] * (2 * n_dp if n_soon else 0)),
        put_weights,
        pick_all,
    )
    *late_pieces, rows = lax.optimization_barrier((*late_pieces, rows))
    late_pieces = [late_pieces[0], *permuted(late_pieces[1:])]
    packing = back_beside > 0 and depth == 512
    *outs, gate_soon, up_soon, down_soon = expert_call(
        first[None],
        experts_all,
        0,
        late,
        rows,
        grows,
        gates,
        [gate_cut, up_cut],
        w_down,
        pack=(back_beside, n_dp) if packing else (),
    )
    if packing:
        *outs, gate_soon, up_soon, down_soon, packed = [*outs, gate_soon, up_soon, down_soon]
    offsets = [from_plane(k) * depth for k in range(n_dp)]
    weighted, grad_rows, grad_gates, gate_rest, up_rest, grad_down_part = expert_call(
        jnp.stack([first + late, *offsets]),
        experts_all,
        late,
        number - late,
        rows,
        grows,
        gates,
        late_pieces,
        w_down,
        [*outs, down_soon],
    )
    part_back = place_back(slots, grad_rows, grad_gates)

    def ways(low, high, at, ins, outs):
        def pair(e, n):
            return (
                lambda to: ins[n].at[pl.ds(e, 1), rows_at(to)],
                lambda here: outs[n].at[pl.ds(e + at, 1), :, columns_at(here)],
            )

        return [pair(e, n) for e in range(low, high) for n in range(2)]

    def cut_grads(low, high, ins, outs):
        to, unused = partners(lax.axis_index("dp"), n_dp)
        pairs = []
        for k, piece in enumerate(outs, 1):
            for n in range(2):
                source = ins[n].at[pl.ds(low, high - low), rows_at(to(k))]
                pairs.append((source, piece.at[:, :, pl.ds(n * part, part)]))
        return pairs

    pieces = []
    if back_beside:
        for k in range(1, n_dp):
            if packing:
                piece = lax.dynamic_index_in_dim(packed, to_plane(k), 0, False)
            else:
                piece = jnp.concatenate(
                    [
                        lax.dynamic_slice_in_dim(
                            one[:back_beside], to_plane(k) * depth, depth, 1
                        )
                        for one in (gate_soon, up_soon)
                    ],
                    axis=2,
                )
            pieces.append(piece)
        ahead = lax.optimization_barrier((*pieces, *late_pieces[1:]))
        pieces = permuted(ahead[: n_dp - 1])
        part_back, *pieces = lax.optimization_barrier((part_back, *pieces))
    way_shapes = [jax.ShapeDtypeStruct((number, depth, ff), bf16)] * 2
    piece_shape = jax.ShapeDtypeStruct((back_late - back_third, depth, 2 * part), bf16)
    (back,), (gate_third, up_third, part_out, *later_pieces) = scatter_all(
        n_dp,
        n_expert,
        [part_back.reshape(n_dp, n_expert, count, D + width)],
        [4],
        [gate_soon, up_soon, slots, weighted],
        [
            *way_shapes,
            jax.ShapeDtypeStruct((groups * count, D), bf16),
            *[piece_shape] * (n_dp - 1),
        ],
        lambda ins, outs: ways(back_beside, back_third, 0, ins, outs),
        8,
        (),
        stages(
            *[1] * (2 * (back_third - back_beside)),
            *[back_late - back_third] * (2 * (n_dp - 1)),
        ),
        lambda ins, outs: cut_grads(back_third, back_late, ins, outs[3:]),
        lambda ins, outs: place_out(ins[2], ins[3], outs[2]),
    )
    later_pieces = permuted(later_pieces)

    def attention_back(back):
        query_weight, key_weight, value_weight, out_weight = (weights_all[i] for i in range(4))
        grad_final = cotangent.astype(jnp.float32)
        grad_mlp = back[:, :D]
        grad_router_probs = back[:, D : D + experts_all] + back[:, D + experts_all :]
        grad_logits = router * (
            grad_router_probs - jnp.sum(router * grad_router_probs, axis=1, keepdims=True)
        )
        grad_logits_low = grad_logits.astype(bf16)
        grad_router_full = product(mlp_low, grad_logits_low, "td,te->de")
        grad_mlp = grad_mlp + product(grad_logits_low, router_weight, "te,de->td")
        grad_middle_part, grad_mlp_gain = rms_backward(middle, mlp_inverse, mlp_gain, grad_mlp)
        grad_middle = grad_final + grad_middle_part
        grad_branch_low = grad_middle.astype(bf16)
        grad_out_full = product(attended_low, grad_branch_low, "td,te->de")
        grad_attended = (
            product(grad_branch_low, out_weight, "te,de->td").astype(bf16).reshape(count, HEADS, HD)
        )
        grad_weights = product(grad_attended, value_heads, "qhd,khd->hqk")
        grad_scores = probs * (grad_weights - jnp.sum(probs * grad_weights, axis=-1, keepdims=True))
        grad_scores_low = grad_scores.astype(bf16)
        grad_query_turn = product(grad_scores_low, key_low, "hqk,khd->qhd").reshape(count, D) * scale
        grad_key_turn = product(grad_scores_low, query_low, "hqk,qhd->khd").reshape(count, D) * scale
        grad_value_low = (
            product(probs_low, grad_attended, "hqk,qhd->khd").reshape(count, D).astype(bf16)
        )
        grad_query_raw, grad_query_gain = rms_backward(
            query_raw, query_inverse, query_gain, rotate(grad_query_turn, cosine, -sine)
        )
        grad_key_raw, grad_key_gain = rms_backward(
            key_raw, key_inverse, key_gain, rotate(grad_key_turn, cosine, -sine)
        )
        grad_query_low = grad_query_raw.astype(bf16)
        grad_key_low = grad_key_raw.astype(bf16)
        grad_query_full = product(normed_low, grad_query_low, "td,te->de")
        grad_key_full = product(normed_low, grad_key_low, "td,te->de")
        grad_value_full = product(normed_low, grad_value_low, "td,te->de")
        grad_normed = (
            product(grad_query_low, query_weight, "te,de->td")
            + product(grad_key_low, key_weight, "te,de->td")
            + product(grad_value_low, value_weight, "te,de->td")
        )
        grad_inputs_part, grad_attn_gain = rms_backward(inputs, attn_inverse, attn_gain, grad_normed)
        grad_inputs = grad_middle + grad_inputs_part

        small_grads = jnp.concatenate(
            [
                grad_router_full,
                grad_attn_gain[:, None],
                grad_query_gain[:, None],
                grad_key_gain[:, None],
                grad_mlp_gain[:, None],
                jnp.zeros((D, width - experts_all - 4), jnp.float32),
            ],
            axis=1,
        )
        grads = (grad_out_full, grad_value_full, grad_key_full, grad_query_full, small_grads)
        return grad_inputs, *[one.astype(bf16) for one in grads]

    def unreached(back):
        shapes = [(count, D)] + [(D, D)] * 4 + [(D, width)]
        kinds = [jnp.float32] + [bf16] * 5
        return tuple(jnp.zeros(shape, kind) for shape, kind in zip(shapes, kinds))

    grad_inputs, *weight_grads = lax.cond(lengths[0, 0] > 0, attention_back, unreached, back)

    def blocks_of(value):
        return value.reshape(n_dp, n_expert, rows_each, -1)

    sums, (gate_back, up_back) = scatter_all(
        n_dp,
        n_expert,
        [part_out.reshape(n_dp, n_expert, count, D)]
        + [blocks_of(value) for value in weight_grads],
        [2, 1, 1, 1, 2 if rows_each > 16 else 1, 1],
        [gate_third, up_third, gate_soon, up_soon, gate_rest, up_rest],
        way_shapes,
        lambda ins, outs: ways(back_late, late, 0, ins[2:4], outs)
        + ways(0, number - late, late, ins[4:6], outs),
        16,
        ((0, 0), (1, 1)),
        [],
    )
    summed, grad_out_part, grad_value_part, grad_key_part, grad_query_part, small_part = sums
    output = (middle + summed).astype(bf16)
    grad_router_part = small_part[:, :experts_all]
    gain_parts = [small_part[:, experts_all + i] for i in range(4)]
    widened = widen([(back_beside, back_third), (back_late, number)], [gate_back, up_back])
    offsets = jnp.stack([from_plane(k) * part for k in range(n_dp)])
    for low, high, others in (
        (0, back_beside, pieces),
        (back_third, back_late, later_pieces),
    ):
        if high > low:
            own = jnp.concatenate(
                [
                    lax.dynamic_slice_in_dim(one[low:high], me * depth, depth, 1)
                    for one in (gate_soon, up_soon)
                ],
                axis=2,
            )
            widened = widen_pieces(offsets, low, [own, *others], widened)
    grad_gate_part, grad_up_part = widened
    return (
        output,
        grad_inputs,
        grad_query_part,
        grad_key_part,
        grad_value_part,
        grad_out_part,
        grad_router_part,
        gain_parts[0],
        gain_parts[1],
        gain_parts[2],
        gain_parts[3],
        grad_gate_part,
        grad_up_part,
        grad_down_part,
    )


def solution(mesh):
    return jax.shard_map(
        functools.partial(shards, mesh.shape["dp"], mesh.shape["expert"]),
        mesh=mesh,
        in_specs=(
            P(("dp", "expert"), None),
            P(("dp", "expert"), None),
            P(("dp", "expert"), None),
            P(("dp", "expert"), None),
            P(("dp", "expert"), None),
            P(("dp", "expert"), None),
            P(("dp", "expert"), None),
            P(("dp", "expert"), None),
            P(("dp", "expert"), None),
            P(("dp", "expert")),
            P(("dp", "expert")),
            P(("dp", "expert")),
            P(("dp", "expert")),
            P("expert", "dp", None),
            P("expert", "dp", None),
            P("expert", "dp", None),
        ),
        out_specs=(
            P(("dp", "expert"), None),
            P(("dp", "expert"), None),
            P(("dp", "expert"), None),
            P(("dp", "expert"), None),
            P(("dp", "expert"), None),
            P(("dp", "expert"), None),
            P(("dp", "expert"), None),
            P(("dp", "expert")),
            P(("dp", "expert")),
            P(("dp", "expert")),
            P(("dp", "expert")),
            P("expert", "dp", None),
            P("expert", "dp", None),
            P("expert", "dp", None),
        ),
        check_vma=False,
    )
```

```python
import functools

import jax
import jax.numpy as jnp
from jax import lax
from jax.experimental import pallas as pl
from jax.experimental.pallas import tpu as pltpu
from jax.sharding import PartitionSpec as P

D = 2048
HEADS = 16
HD = 128
TOPK = 8
CAP = 24


eps = 1e-05


def product(left, right, form):
    return jnp.einsum(form, left, right, preferred_element_type=jnp.float32)


def rms_forward(values, gain):
    inverse = lax.rsqrt(jnp.mean(values * values, axis=-1, keepdims=True) + eps)
    return (values * inverse * gain, inverse)


def rms_backward(values, inverse, gain, grad):
    scaled = grad * gain
    inner = jnp.mean(scaled * values, axis=-1, keepdims=True)
    grad_values = inverse * scaled - values * (inverse * inverse * inverse) * inner
    grad_gain = jnp.sum(grad * values * inverse, axis=0)
    return (grad_values, grad_gain)


def layout(lengths_row, count):
    places = jnp.arange(count, dtype=jnp.int32)
    ends = jnp.cumsum(lengths_row, dtype=jnp.int32)
    passed = (places[:, None] >= ends[None, :]).astype(jnp.int32)
    segment = jnp.sum(passed, axis=1, dtype=jnp.int32)
    start = jnp.sum(passed * lengths_row[None, :], axis=1, dtype=jnp.int32)
    return (segment, places - start, places)


def rotate(values, cosine, sine):
    count = values.shape[0]
    heads = values.reshape(count, HEADS, HD)
    half = HD // 2
    first = heads[..., :half]
    second = heads[..., half:]
    turned = jnp.concatenate(
        [first * cosine - second * sine, second * cosine + first * sine], axis=-1
    )
    return turned.reshape(count, D)


MESH = pl.DeviceIdType.MESH
BIG = 60 * 1024 * 1024


def place_of():
    z = lax.axis_index("dp")
    j = lax.axis_index("expert")
    return z, j, j // 2, j % 2


def other_chips(chip, chips):
    if chips == 4:
        square = [chip, chip + 1 - 2 * (chip % 2), chip + 2 - 4 * (chip // 2), 3 - chip]
        return lambda k: square[k], lambda k: square[k]
    return lambda k: (chip + k) % chips, lambda k: (chip + chips - k) % chips


def partners(z, n_dp):
    if n_dp == 4:
        pairs = [z, 3 - z, (z + 2) % 4, z + 1 - 2 * (z % 2)]
        return lambda k: pairs[k], lambda k: pairs[k]
    return lambda k: (z + k) % n_dp, lambda k: (z + n_dp - k) % n_dp


def greet(n_dp, n_expert):
    z, j, chip, core = place_of()
    chips = n_expert // 2
    barrier = pltpu.get_barrier_semaphore()
    for k in range(1, n_dp):
        pl.semaphore_signal(
            barrier, inc=1, device_id=((z + k) % n_dp, j), device_id_type=MESH
        )
    for k in range(1, chips):
        other = ((chip + k) % chips) * 2 + core
        pl.semaphore_signal(barrier, inc=1, device_id=(z, other), device_id_type=MESH)
    pl.semaphore_signal(
        barrier, inc=1, device_id=(z, chip * 2 + 1 - core), device_id_type=MESH
    )
    pl.semaphore_wait(barrier, n_dp - 1 + chips - 1 + 1)


def remote(source, target, send, receive, device):
    return pltpu.make_async_remote_copy(
        src_ref=source,
        dst_ref=target,
        send_sem=send,
        recv_sem=receive,
        device_id=device,
        device_id_type=MESH,
    )


def exchange(n_dp, pairs, send, receive):
    z, j, chip, core = place_of()
    to_plane, unused = partners(z, n_dp)
    copies = []
    for i, (source, target) in enumerate(pairs):
        for k in range(1, n_dp):
            to = to_plane(k)
            copies.append(
                remote(source(to), target(z), send.at[i, k], receive.at[i, k], (to, j))
            )
    return copies


def moves(pairs, stages, local):
    if not stages:
        copies = [
            pltpu.make_async_copy(source, target, local.at[i, 0])
            for i, (source, target) in enumerate(pairs)
        ]
        for copy in copies:
            copy.start()
        return [], copies
    bring = [
        pltpu.make_async_copy(source, stages[i], local.at[i, 0])
        for i, (source, target) in enumerate(pairs)
    ]
    put = [
        pltpu.make_async_copy(stages[i], target, local.at[i, 1])
        for i, (source, target) in enumerate(pairs)
    ]
    return bring, put


def nothing(ins, outs):
    return []


def gather_kernel(
    n_dp, n_expert, n_items, places, cuts, puts, finish, n_cut, n_out, n_stages, *refs
):
    z, j, chip, core = place_of()
    chips = n_expert // 2
    square = chips == 4
    to_chip, from_chip = other_chips(chip, chips)
    sources = refs[:n_items]
    cut_in = refs[n_items : n_items + n_cut]
    at = n_items + n_cut
    targets = refs[at : at + n_items]
    cut_out = refs[at + n_items : at + n_items + n_out]
    (
        send_c,
        recv_c,
        send_b,
        recv_b,
        send_a,
        recv_a,
        local,
        send_x,
        recv_x,
        local_y,
        *stages,
    ) = refs[at + n_items + n_out :]
    greet(n_dp, n_expert)
    mate = (z, chip * 2 + 1 - core)
    near = (1, 2) if square else tuple(range(1, chips))

    def slot(i, plane, column):
        return places[i](targets[i], plane * n_expert + column)

    def pass_on(i, plane, source, column, k, chip_to):
        return remote(
            source,
            slot(i, plane, column),
            send_b.at[i, plane, k],
            recv_b.at[i, plane, k],
            (z, chip_to * 2 + core),
        )

    def hand(i, plane, source):
        for k in near:
            pass_on(i, plane, source, j, k, to_chip(k)).start()
        remote(
            source, slot(i, plane, j), send_a.at[i, plane, 0], recv_a.at[i, plane, 0], mate
        ).start()

    def along(i, plane, source, way, step):
        return remote(
            source, slot(i, plane, j), send_c.at[i, way, plane], recv_c.at[i, plane], (z + step, j)
        )

    def at_distance(d, body):
        if d == 0:
            body(z, 0)
            return

        @pl.when(z >= d)
        def _():
            body(z - d, 0)

        @pl.when(z + d < n_dp)
        def _():
            body(z + d, 1)

    for i in range(n_items):

        @pl.when(z < n_dp - 1)
        def _():
            along(i, z, sources[i], 0, 1).start()

        @pl.when(z > 0)
        def _():
            along(i, z, sources[i], 1, -1).start()

        hand(i, z, sources[i])
        pltpu.make_async_copy(sources[i], slot(i, z, j), local.at[i]).start()

    def relay(plane, way):
        step = -1 if way else 1
        for i in range(n_items):
            block = slot(i, plane, j)
            along(i, plane, block, way, step).wait_recv()

            @pl.when(z > 0 if way else z < n_dp - 1)
            def _():
                along(i, plane, block, way, step).start()

            hand(i, plane, block)

    for d in range(1, n_dp):
        at_distance(d, relay)
    pairs = cuts(cut_in, cut_out)
    copies = exchange(n_dp, pairs, send_x, recv_x)
    for copy in copies:
        copy.start()
    own = [(source(z), target(z)) for source, target in pairs]
    bring, put = moves(own + puts(cut_in, cut_out), stages, local_y)
    for copy in bring:
        copy.start()
    for one, other in zip(bring, put):
        one.wait()
        other.start()

    def arrive(i, plane, k):
        column = from_chip(k) * 2 + core
        block = slot(i, plane, column)
        pass_on(i, plane, block, column, k, chip).wait_recv()
        remote(block, block, send_a.at[i, plane, k], recv_a.at[i, plane, k], mate).start()
        return block, column

    def arrived(plane, way):
        for i in range(n_items):
            for k in near:
                block, column = arrive(i, plane, k)
                if square:

                    @pl.when(plane % 2 == k - 1)
                    def _():
                        pass_on(i, plane, block, column, 3, to_chip(3 - k)).start()

    def crossed(plane, way):
        for i in range(n_items):
            arrive(i, plane, 3)

    for d in range(n_dp):
        at_distance(d, arrived)
    if square:
        for d in range(n_dp):
            at_distance(d, crossed)

    for i in range(n_items):
        for plane in range(n_dp):
            for k in range(chips):
                column = (from_chip(k) if k else chip) * 2 + 1 - core
                block = slot(i, plane, column)
                remote(
                    block, block, send_a.at[i, plane, k], recv_a.at[i, plane, k], mate
                ).wait_recv()
        pltpu.make_async_copy(sources[i], slot(i, z, j), local.at[i]).wait()
    finish(targets, cut_in, cut_out)
    for i in range(n_items):
        for plane in range(n_dp):
            block = slot(i, plane, j)
            for k in range(1, chips):
                pass_on(i, plane, block, j, k, chip).wait_send()
            for k in range(chips):
                remote(
                    block, block, send_a.at[i, plane, k], recv_a.at[i, plane, k], mate
                ).wait_send()

            @pl.when((z < n_dp - 1) & (z >= plane))
            def _():
                along(i, plane, block, 0, 1).wait_send()

            @pl.when((z > 0) & (z <= plane))
            def _():
                along(i, plane, block, 1, -1).wait_send()

    for copy in copies + put:
        copy.wait()


def gather_call(
    n_dp,
    n_expert,
    items,
    shapes,
    places,
    cut_in,
    cut_shapes,
    cuts,
    aliases,
    number,
    stages,
    puts=nothing,
    finish=lambda items, ins, outs: None,
):
    chips = n_expert // 2
    n, m = len(items), len(cut_shapes)
    dma = pltpu.SemaphoreType.DMA
    anywhere = pl.BlockSpec(memory_space=pl.ANY)
    return pl.pallas_call(
        functools.partial(
            gather_kernel,
            n_dp,
            n_expert,
            n,
            places,
            cuts,
            puts,
            finish,
            len(cut_in),
            m,
            len(stages),
        ),
        out_shape=[*shapes, *cut_shapes],
        in_specs=[anywhere] * (n + len(cut_in)),
        out_specs=[anywhere] * (n + m),
        scratch_shapes=[
            dma((n, 2, n_dp)),
            dma((n, n_dp)),
            dma((n, n_dp, chips)),
            dma((n, n_dp, chips)),
            dma((n, n_dp, chips)),
            dma((n, n_dp, chips)),
            dma((n,)),
            dma((4, n_dp)),
            dma((4, n_dp)),
            dma((max(len(stages), 4), 2)),
            *[pltpu.VMEM(stage, jnp.bfloat16) for stage in stages],
        ],
        input_output_aliases=aliases,
        compiler_params=pltpu.CompilerParams(
            collective_id=number, has_side_effects=True, vmem_limit_bytes=BIG
        ),
    )(*items, *cut_in)


def scatter_kernel(
    n_dp, n_expert, n_arrays, items, n_cut, n_out, cuts, puts, middle, rings, n_rings, *refs
):
    n_items = len(items)
    z, j, chip, core = place_of()
    chips = n_expert // 2
    square = chips == 4
    to_chip, from_chip = other_chips(chip, chips)
    refs = list(refs)

    def take(count):
        taken = refs[:count]
        del refs[:count]
        return taken

    sources, cut_in, targets, cut_out = take(n_arrays), take(n_cut), take(n_arrays), take(n_out)
    ring, got_a, got_b, got_c = take(n_rings), take(n_items), take(n_items), take(n_items)
    transit = take(n_items)
    (
        send_a,
        recv_a,
        send_b,
        recv_b,
        send_c,
        recv_c,
        send_t,
        recv_t,
        local,
        send_x,
        recv_x,
        local_y,
        *stages,
    ) = refs
    greet(n_dp, n_expert)
    mate = (z, chip * 2 + 1 - core)
    order = [3, 1, 2, 0] if square else [*range(1, chips), 0]
    half = n_dp // 2
    low, high = pl.ds(0, half), pl.ds(half, n_dp - half)

    def chip_of(k):
        return to_chip(k) if k else chip

    def source(i, column):
        array, first, rows = items[i]
        return sources[array].at[:, column, pl.ds(first, rows)]

    def to_mate(i, k):
        return remote(
            source(i, chip_of(k) * 2 + 1 - core),
            got_a[i].at[k],
            send_a.at[i, k],
            recv_a.at[i, k],
            mate,
        )

    turn = [0] * n_rings
    loads = []
    for i in range(n_items):
        for k in order:
            loads.append((i, k, turn[rings[i]] % 2))
            turn[rings[i]] += 1

    def load(i, k, at):
        return pltpu.make_async_copy(
            source(i, chip_of(k) * 2 + core), ring[rings[i]].at[at], local.at[rings[i], at]
        )

    def send_near(i, k, part, number):
        return remote(
            got_a[i].at[k, part],
            got_b[i].at[k - 1, part],
            send_b.at[i, number],
            recv_b.at[i, number],
            (z, to_chip(k) * 2 + core),
        )

    def send_over(i, k, part):
        return remote(
            got_a[i].at[3, part],
            transit[i].at[k - 1],
            send_t.at[i, k],
            recv_t.at[i, k],
            (z, to_chip(k) * 2 + core),
        )

    def send_far(i, k):
        return remote(
            got_a[i].at[k],
            got_b[i].at[k - 1],
            send_b.at[i, k],
            recv_b.at[i, k],
            (z, to_chip(k) * 2 + core),
        )

    def along(i, plane, way):
        slot = n_dp - (z - 1) + plane if way else plane - (z + 1)
        return remote(
            got_a[i].at[0, plane],
            got_c[i].at[slot],
            send_c.at[i, plane],
            recv_c.at[i, slot],
            (z - 1 if way else z + 1, j),
        )

    def from_along(i, slot):
        return remote(
            got_c[i].at[slot], got_c[i].at[slot], send_c.at[i, 0], recv_c.at[i, slot], mate
        )

    f32 = jnp.float32

    def add(i, planes, target, terms):
        rows = got_a[i].shape[2]
        per = rows // 16

        def step(n, unused):
            plane = n // per
            at = pl.ds(pl.multiple_of((n % per) * 16, 16), 16)
            total = terms[0](plane, at).astype(f32)
            for term in terms[1:]:
                total = total + term(plane, at).astype(f32)
            target(plane, at, total)
            return unused

        lax.fori_loop(0, planes * per, step, 0)

    def grow(i, k, first, planes, term):
        def target(plane, at, total):
            got_a[i][k, plane + first, at] = total.astype(got_a[i].dtype)

        add(i, planes, target, [lambda plane, at: got_a[i][k, plane + first, at], term])

    for i in range(n_items):
        for k in order:
            to_mate(i, k).start()
    started = 0
    ahead = [0] * n_rings
    for i, k, at in loads:
        if ahead[rings[i]] < 2:
            load(i, k, at).start()
            ahead[rings[i]] += 1
    pairs = cuts(cut_in, cut_out)
    copies = exchange(n_dp, pairs, send_x, recv_x)
    own = [(source(z), target(z)) for source, target in pairs]
    bring, put = moves(own + puts(cut_in, cut_out), stages, local_y)
    for copy in bring:
        copy.start()

    def over_cores(i):
        for n, (item, k, at) in enumerate(loads):
            if item != i:
                continue
            load(i, k, at).wait()
            to_mate(i, k).wait_recv()
            grow(i, k, 0, n_dp, lambda plane, rows: ring[rings[i]][at, plane, rows])
            later = [one for one in loads[n + 1 :] if rings[one[0]] == rings[i]]
            if len(later) >= 2:
                load(*later[1]).start()
            if not k:
                continue
            if not square:
                send_far(i, k).start()
            elif k == 3:
                send_over(i, 1, low).start()
                send_over(i, 2, high).start()
            elif k == 1:
                send_near(i, 1, low, 0).start()
            else:
                send_near(i, 2, high, 1).start()

    def pass_over(i):
        if not square:
            return
        send_over(i, 2, high).wait_recv()
        grow(i, 1, half, n_dp - half, lambda plane, rows: transit[i][1, plane, rows])
        send_near(i, 1, high, 2).start()
        send_over(i, 1, low).wait_recv()
        grow(i, 2, 0, half, lambda plane, rows: transit[i][0, plane, rows])
        send_near(i, 2, low, 3).start()

    def over_chips(i):
        if square:
            send_near(i, 1, low, 0).wait_recv()
            send_near(i, 2, high, 1).wait_recv()
            send_near(i, 1, high, 2).wait_recv()
            send_near(i, 2, low, 3).wait_recv()
        else:
            for k in range(1, chips):
                send_far(i, k).wait_recv()
        heard = 2 if square else chips - 1

        def target(plane, at, total):
            got_a[i][0, plane, at] = total.astype(got_a[i].dtype)

        terms = [lambda plane, at: got_a[i][0, plane, at]]
        for other in range(heard):
            terms.append(lambda plane, at, other=other: got_b[i][other, plane, at])
        add(i, n_dp, target, terms)
        for d in range(n_dp - 1, 0, -1):
            for way in (0, 1):
                plane = z - d if way else z + d

                @pl.when(z == (n_dp - 1 if way else 0))
                def _():
                    along(i, plane, way).start()

    def over_planes(i):
        for d in range(n_dp - 2, 0, -1):
            for way in (0, 1):
                plane = z - d if way else z + d
                slot = n_dp - d if way else d

                @pl.when((plane >= 0) & (z < n_dp - 1) if way else (plane < n_dp) & (z > 0))
                def _():
                    from_along(i, slot).wait_recv()
                    grow(i, 0, plane, 1, lambda unused, at: got_c[i][slot, at])
                    along(i, plane, way).start()

    def finish(i):
        array, first, rows = items[i]

        def here(at):
            return pl.ds(pl.multiple_of(first + at.start, 16), 16)

        def own(unused, at, total):
            targets[array][here(at)] = total

        add(i, 1, own, [lambda unused, at: got_a[i][0, z, at]])
        for slot, arrives in ((0, z > 0), (n_dp, z < n_dp - 1)):

            @pl.when(arrives)
            def _():
                from_along(i, slot).wait_recv()
                add(
                    i,
                    1,
                    own,
                    [
                        lambda unused, at: targets[array][here(at)],
                        lambda unused, at: got_c[i][slot, at],
                    ],
                )

    steps = (over_cores, pass_over, over_chips, over_planes, finish)
    share = -(-len(copies) // n_items)
    for n in range(n_items + len(steps) - 1):
        for copy in copies[n * share : (n + 1) * share]:
            copy.start()
        for late, step in enumerate(steps):
            if 0 <= n - late < n_items:
                step(n - late)
        if n == min(1, n_items - 1):
            for one, other in zip(bring, put):
                one.wait()
                other.start()
            middle(cut_in, cut_out)
    for i in range(n_items):
        for k in range(chips):
            to_mate(i, k).wait_send()
        if square:
            for k, part in ((1, low), (2, high)):
                send_over(i, k, part).wait_send()
            for k, part, number in ((1, low, 0), (2, high, 1), (1, high, 2), (2, low, 3)):
                send_near(i, k, part, number).wait_send()
        else:
            for k in range(1, chips):
                send_far(i, k).wait_send()
        for plane in range(n_dp):

            @pl.when(z != plane)
            def _():
                remote(
                    got_a[i].at[0, plane],
                    got_c[i].at[0],
                    send_c.at[i, plane],
                    recv_c.at[i, 0],
                    mate,
                ).wait_send()

    for copy in copies + put:
        copy.wait()


def scatter_call(
    n_dp,
    n_expert,
    arrays,
    splits,
    cut_in,
    cut_shapes,
    cuts,
    number,
    aliases,
    stages,
    puts=nothing,
    middle=nothing,
):
    chips = n_expert // 2
    square = chips == 4
    items = []
    for array, (one, split) in enumerate(zip(arrays, splits)):
        rows = one.shape[2] // split
        items += [(array, first, rows) for first in range(0, one.shape[2], rows)]
    n, m = len(items), len(cut_shapes)
    count = len(arrays)
    dma = pltpu.SemaphoreType.DMA
    anywhere = pl.BlockSpec(memory_space=pl.ANY)
    blocks = [(rows, arrays[array].shape[3]) for array, unused, rows in items]
    kinds = sorted(set(blocks))
    rings = [kinds.index(block) for block in blocks]
    bf16 = jnp.bfloat16
    heard = 2 if square else chips - 1
    return pl.pallas_call(
        functools.partial(
            scatter_kernel,
            n_dp,
            n_expert,
            count,
            items,
            len(cut_in),
            m,
            cuts,
            puts,
            middle,
            rings,
            len(kinds),
        ),
        out_shape=[
            *[jax.ShapeDtypeStruct(one.shape[2:], jnp.float32) for one in arrays],
            *cut_shapes,
        ],
        in_specs=[anywhere] * (count + len(cut_in)),
        out_specs=[pl.BlockSpec(memory_space=pltpu.VMEM)] * count + [anywhere] * m,
        scratch_shapes=[
            *[pltpu.VMEM((2, n_dp, *kind), bf16) for kind in kinds],
            *[pltpu.VMEM((chips, n_dp, *block), bf16) for block in blocks],
            *[pltpu.VMEM((heard, n_dp, *block), bf16) for block in blocks],
            *[pltpu.VMEM((n_dp + 1, *block), bf16) for block in blocks],
            *[pltpu.VMEM((2, n_dp // 2, *(block if square else (16, 128))), bf16) for block in blocks],
            dma((n, chips)),
            dma((n, chips)),
            dma((n, chips)),
            dma((n, chips)),
            dma((n, n_dp)),
            dma((n, n_dp + 1)),
            dma((n, 3)),
            dma((n, 3)),
            dma((len(kinds), 2)),
            dma((16, n_dp)),
            dma((16, n_dp)),
            dma((max(len(stages), 16), 2)),
            *[pltpu.VMEM(stage, jnp.bfloat16) for stage in stages],
        ],
        input_output_aliases=aliases,
        compiler_params=pltpu.CompilerParams(
            collective_id=number, has_side_effects=True, vmem_limit_bytes=62 * 1024 * 1024
        ),
    )(*arrays, *cut_in)


def scatter_all(
    n_dp,
    n_expert,
    items,
    splits,
    cut_in,
    cut_shapes,
    cuts,
    number,
    aliases,
    stages,
    puts=nothing,
    middle=nothing,
):
    chips = n_expert // 2
    blocks = (2 * chips - 1 if chips != 4 else 7) * n_dp + n_dp + 3
    need = sum(blocks * item.shape[2] * item.shape[3] * 2 for item in items)
    kinds = {(item.shape[2] // split, item.shape[3]) for item, split in zip(items, splits)}
    need += sum(2 * n_dp * kind[0] * kind[1] * 2 for kind in kinds)
    need += sum(stage[0] * stage[1] * stage[2] * 2 for stage in stages)
    pieces = -(-need // (61 * 1024 * 1024))
    tiles = [item.shape[3] // 128 for item in items]
    results = [[] for item in items]
    extra = []
    for piece in range(pieces):
        ends = [(t * piece // pieces * 128, t * (piece + 1) // pieces * 128) for t in tiles]
        used = [i for i, (low, high) in enumerate(ends) if high > low]
        first = piece == 0
        outs = scatter_call(
            n_dp,
            n_expert,
            [items[i][..., ends[i][0] : ends[i][1]] if pieces > 1 else items[i] for i in used],
            [splits[i] for i in used],
            cut_in if first else [],
            cut_shapes if first else [],
            cuts if first else nothing,
            number + piece,
            {len(used) + a: len(used) + b for a, b in aliases} if first else {},
            stages if first else [],
            puts if first else nothing,
            middle if first else nothing,
        )
        for i, out in zip(used, outs):
            results[i].append(out)
        if first:
            extra = outs[len(used) :]
    return [one[0] if len(one) == 1 else jnp.concatenate(one, axis=1) for one in results], extra


def dot(left, right, dims):
    return lax.dot_general(
        left, right, ((dims[:1], dims[1:]), ((), ())), preferred_element_type=jnp.float32
    )


def picks(slots_ref, number):
    pair = slots_ref.shape[2]
    rows = lax.broadcasted_iota(jnp.int32, (2 * CAP, pair), 0)
    return [slots_ref[0, e : e + 1, :] == rows for e in range(number)]


def pick_kernel(number, experts_all, slots_ref, x_ref, g_ref, router_ref, rows_ref, grows_ref, gates_ref):
    chosen = picks(slots_ref, number)
    pick = jnp.concatenate(chosen, axis=0).astype(jnp.bfloat16)
    size = 2 * CAP
    x = x_ref[...]
    logits = dot(router_ref[...], x, (0, 1))
    names = lax.broadcasted_iota(jnp.int32, logits.shape, 0)
    logits = jnp.where(names < experts_all, logits, -1e30)
    weights = jnp.exp(logits - jnp.max(logits, axis=0, keepdims=True))
    probs = weights / jnp.sum(weights, axis=0, keepdims=True)
    for e in range(number):
        gate = jnp.sum(jnp.where(chosen[e], probs[e : e + 1, :], 0.0), axis=1, keepdims=True)
        gates_ref[e] = jnp.broadcast_to(gate, (size, 128))
    picked = dot(pick, x, (1, 0)).astype(jnp.bfloat16)
    for e in range(number):
        rows_ref[e] = picked[e * size : (e + 1) * size]
    picked = dot(pick, g_ref[...], (1, 0)).astype(jnp.bfloat16)
    for e in range(number):
        grows_ref[e] = picked[e * size : (e + 1) * size]


def expert_kernel(steps, half, n_weights, n_into, n_pack, names_ref, x_ref, g_ref, gates_ref, *refs):
    weights, refs = refs[:n_weights], refs[n_weights:]
    down_ref, refs = refs[0], refs[1 + n_into :]
    (
        y_ref,
        dx_ref,
        probs_ref,
        dgate_ref,
        dup_ref,
        ddown_ref,
        *pack_refs,
        sum_gate,
        sum_up,
    ) = refs
    bf16 = jnp.bfloat16
    g = g_ref[0]
    rows, width = x_ref.shape[1:]
    part = dgate_ref.shape[2]
    gate = gates_ref[0][:, :1]
    if n_weights == 2:
        piece = 512
        gate_ref, up_ref = weights
        gate_mid = dot(x_ref[0], gate_ref[0], (1, 0))
        up_mid = dot(x_ref[0], up_ref[0], (1, 0))
        spans = [
            (pl.ds(at, piece), gate_ref, up_ref, pl.ds(at, piece), pl.ds(0, part), pl.ds(0, part))
            for at in range(0, width, piece)
        ]
    else:
        piece = width // n_weights
        spans = []
        gate_mid = up_mid = 0.0
        for n, ref in enumerate(weights):
            span = pl.ds(pl.multiple_of(names_ref[1 + n], piece), piece)
            x_part = x_ref[0, :, span]
            gate_mid = gate_mid + dot(x_part, ref[0, :, :part], (1, 0))
            up_mid = up_mid + dot(x_part, ref[0, :, part:], (1, 0))
            spans.append((span, ref, ref, pl.ds(0, piece), pl.ds(0, part), pl.ds(part, part)))
    sigmoid = 1.0 / (1.0 + jnp.exp(-gate_mid))
    silu = gate_mid * sigmoid
    hidden = silu * up_mid
    hidden_low = hidden.astype(bf16)
    grad_plain = dot(g, down_ref[0], (1, 1))
    grad_gates = jnp.sum(grad_plain * hidden_low.astype(jnp.float32), axis=1, keepdims=True)
    high = grad_gates.astype(bf16).astype(jnp.float32)
    lane = lax.broadcasted_iota(jnp.int32, (rows, 128), 1)
    name = names_ref[0] + pl.program_id(0)
    probs_ref[0] = (
        jnp.where(lane == name, high, 0.0) + jnp.where(lane == name + half, grad_gates - high, 0.0)
    ).astype(bf16)
    grad_hidden = grad_plain * gate
    grad_gate = (
        grad_hidden * up_mid * sigmoid * (1.0 + gate_mid * (1.0 - sigmoid))
    ).astype(bf16)
    grad_up = (grad_hidden * silu).astype(bf16)
    scaled = (hidden * gate).astype(bf16)
    for at in range(0, width, piece):
        y_ref[0, :, at : at + piece] = (
            dot(hidden_low, down_ref[0, :, at : at + piece], (1, 0)) * gate
        ).astype(bf16)
    for span, gate_ref, up_ref, here, gate_columns, up_columns in spans:
        dx_ref[0, :, span] = (
            dot(grad_gate, gate_ref[0, here, gate_columns], (1, 1))
            + dot(grad_up, up_ref[0, here, up_columns], (1, 1))
        ).astype(bf16)
    step = pl.program_id(1)
    for span, *unused in spans:
        x_part = x_ref[0, :, span]
        here_gate = dot(x_part, grad_gate, (0, 0))
        here_up = dot(x_part, grad_up, (0, 0))
        here_down = dot(scaled, g_ref[0, :, span], (0, 0))
        if steps == 1:
            dgate_ref[0, span, :] = here_gate.astype(bf16)
            dup_ref[0, span, :] = here_up.astype(bf16)
            ddown_ref[0, :, span] = here_down
            continue

        @pl.when(step == 0)
        def _():
            sum_gate[span, :] = here_gate
            sum_up[span, :] = here_up
            ddown_ref[0, :, span] = here_down

        @pl.when(step > 0)
        def _():
            sum_gate[span, :] += here_gate
            sum_up[span, :] += here_up
            ddown_ref[0, :, span] += here_down

        @pl.when(step == steps - 1)
        def _():
            dgate_ref[0, span, :] = sum_gate[span, :].astype(bf16)
            dup_ref[0, span, :] = sum_up[span, :].astype(bf16)

    if n_pack:

        @pl.when((step == steps - 1) & (pl.program_id(0) < n_pack))
        def _():
            pack_ref = pack_refs[0]
            depth = pack_ref.shape[2]
            for plane in range(pack_ref.shape[0]):
                here = pl.ds(plane * depth, depth)
                pack_ref[plane, 0, :, :part] = dgate_ref[0, here, :]
                pack_ref[plane, 0, :, part:] = dup_ref[0, here, :]


def put_back(number, slots_ref, pairs):
    pick = jnp.concatenate(picks(slots_ref, number), axis=0).astype(jnp.bfloat16)
    piece = 512
    for source, target, first in pairs:
        width = source.shape[2]
        for at in range(0, width, piece):
            size = min(piece, width)
            part = source[:, :, at : at + size].reshape(-1, size)
            target[:, first + at : first + at + size] = dot(pick, part, (0, 0)).astype(
                jnp.bfloat16
            )


def place_back_kernel(number, slots_ref, dx_ref, probs_ref, back_ref):
    put_back(number, slots_ref, [(dx_ref, back_ref, 0), (probs_ref, back_ref, dx_ref.shape[2])])


def place_out_kernel(number, slots_ref, y_ref, out_ref):
    put_back(number, slots_ref, [(y_ref, out_ref, 0)])


def place_out(slots, y, out):
    pairs, number, pair = slots.shape
    pltpu.emit_pipeline(
        functools.partial(place_out_kernel, number),
        grid=(pairs,),
        in_specs=[
            pl.BlockSpec((1, number, pair), lambda p: (p, 0, 0)),
            pl.BlockSpec((number, 2 * CAP, D), lambda p: (0, p, 0)),
        ],
        out_specs=[pl.BlockSpec((pair, D), lambda p: (p, 0))],
    )(slots, y, out)


def pick_shapes(number, pairs):
    bf16 = jnp.bfloat16
    size = 2 * CAP
    return [
        jax.ShapeDtypeStruct((number, pairs * size, D), bf16),
        jax.ShapeDtypeStruct((number, pairs * size, D), bf16),
        jax.ShapeDtypeStruct((number, pairs * size, 128), jnp.float32),
    ]


def pick_rows(number, experts_all, slots, x_all, g_all, router, rows, grows, gates):
    pairs, _, pair = slots.shape
    size = 2 * CAP
    tokens = pl.BlockSpec((pair, D), lambda p: (p, 0))
    picked = pl.BlockSpec((number, size, D), lambda p: (0, p, 0))
    pltpu.emit_pipeline(
        functools.partial(pick_kernel, number, experts_all),
        grid=(pairs,),
        in_specs=[
            pl.BlockSpec((1, number, pair), lambda p: (p, 0, 0)),
            tokens,
            tokens,
            pl.BlockSpec(router.shape, lambda p: (0, 0)),
        ],
        out_specs=[picked, picked, pl.BlockSpec((number, size, 128), lambda p: (0, p, 0))],
    )(slots, x_all, g_all, router, rows, grows, gates)


def expert_call(names, half, low, number, rows, grows, gates, weights, down, into=(), pack=()):
    total, depth, _ = rows.shape
    part = down.shape[1]
    size = depth
    while size > 768:
        size //= 2
    steps = depth // size
    bf16 = jnp.bfloat16
    f32 = jnp.float32

    def from_rows(width):
        return pl.BlockSpec((1, size, width), lambda e, r: (e + low, r, 0))

    def whole(*shape):
        return pl.BlockSpec((1, *shape), lambda e, r: (e, 0, 0))

    def from_whole(*shape):
        return pl.BlockSpec((1, *shape), lambda e, r: (e + low, 0, 0))

    packed = [
        pl.BlockSpec(
            (planes, 1, D // planes, 2 * part),
            lambda e, r, n=n: (0, lax.min(e, n - 1), 0, 0),
        )
        for n, planes in ([pack] if pack else [])
    ]
    keep = (D, part) if steps > 1 else (16, 128)
    return pl.pallas_call(
        functools.partial(
            expert_kernel, steps, half, len(weights), len(into), pack[0] if pack else 0
        ),
        grid=(number, steps),
        in_specs=[
            pl.BlockSpec(memory_space=pltpu.SMEM),
            from_rows(D),
            from_rows(D),
            from_rows(128),
            *[(from_whole if len(weights) == 2 else whole)(*one.shape[1:]) for one in weights],
            from_whole(part, D),
            *[pl.BlockSpec(memory_space=pl.ANY)] * len(into),
        ],
        out_specs=[
            from_rows(D),
            from_rows(D),
            from_rows(128),
            whole(D, part),
            whole(D, part),
            from_whole(part, D),
            *packed,
        ],
        out_shape=[
            jax.ShapeDtypeStruct((total, depth, D), bf16),
            jax.ShapeDtypeStruct((total, depth, D), bf16),
            jax.ShapeDtypeStruct((total, depth, 128), bf16),
            jax.ShapeDtypeStruct((number, D, part), bf16),
            jax.ShapeDtypeStruct((number, D, part), bf16),
            jax.ShapeDtypeStruct((total, part, D), f32),
            *[
                jax.ShapeDtypeStruct((planes, n, D // planes, 2 * part), bf16)
                for n, planes in ([pack] if pack else [])
            ],
        ],
        input_output_aliases={
            5 + len(weights) + i: out for i, out in zip(range(len(into)), (0, 1, 2, 5))
        },
        scratch_shapes=[pltpu.VMEM(keep, f32), pltpu.VMEM(keep, f32)],
        compiler_params=pltpu.CompilerParams(vmem_limit_bytes=BIG),
    )(names, rows, grows, gates, *weights, down, *into)


def place_back(slots, dx, probs):
    pairs, number, pair = slots.shape
    size = 2 * CAP

    def rows(one):
        return pl.BlockSpec((number, size, one.shape[2]), lambda p: (0, p, 0))

    return pl.pallas_call(
        functools.partial(place_back_kernel, number),
        grid=(pairs,),
        in_specs=[pl.BlockSpec((1, number, pair), lambda p: (p, 0, 0)), rows(dx), rows(probs)],
        out_specs=pl.BlockSpec((pair, D + 128), lambda p: (p, 0)),
        out_shape=jax.ShapeDtypeStruct((pairs * pair, D + 128), jnp.bfloat16),
        compiler_params=pltpu.CompilerParams(vmem_limit_bytes=BIG),
    )(slots, dx, probs)


def through_kernel(count, *refs):
    lefts, weight_ref, out_ref = refs[:count], refs[count], refs[count + 1]
    for i in range(count):

        @pl.when(pl.program_id(1) == i)
        def _():
            part = dot(lefts[i][...], weight_ref[0], (1, 1))
            if i:
                part = part + out_ref[...]
            out_ref[...] = part


def through(lefts, weights, first):
    count, (rows, depth) = len(lefts), lefts[0].shape
    piece = 512
    return pl.pallas_call(
        functools.partial(through_kernel, count),
        grid=(depth // piece, count),
        in_specs=[
            *[pl.BlockSpec((rows, depth), lambda c, i: (0, 0))] * count,
            pl.BlockSpec((1, piece, depth), lambda c, i: (i + first, c, 0)),
        ],
        out_specs=pl.BlockSpec((rows, piece), lambda c, i: (0, c)),
        out_shape=jax.ShapeDtypeStruct((rows, depth), jnp.float32),
        compiler_params=pltpu.CompilerParams(vmem_limit_bytes=BIG),
    )(*lefts, weights)


def outer_kernel(which, n_left, *refs):
    lefts, rights = refs[:n_left], refs[n_left : n_left + len(which)]
    piece = 512
    for left, right, out_ref in zip(which, rights, refs[n_left + len(which) :]):
        for at in range(0, out_ref.shape[1], piece):
            out_ref[:, at : at + piece] = dot(
                lefts[left][...], right[:, at : at + piece], (0, 0)
            ).astype(out_ref.dtype)


def outer(lefts, rights, which):
    rows, depth = lefts[0].shape
    piece = 256
    return pl.pallas_call(
        functools.partial(outer_kernel, which, len(lefts)),
        grid=(depth // piece,),
        in_specs=[
            *[pl.BlockSpec((rows, piece), lambda c: (0, c))] * len(lefts),
            *[pl.BlockSpec((rows, depth), lambda c: (0, 0))] * len(rights),
        ],
        out_specs=[pl.BlockSpec((piece, depth), lambda c: (c, 0))] * len(rights),
        out_shape=[jax.ShapeDtypeStruct((depth, depth), jnp.bfloat16)] * len(rights),
        compiler_params=pltpu.CompilerParams(vmem_limit_bytes=BIG),
    )(*lefts, *rights)


def widen_kernel(*refs):
    half = len(refs) // 2
    for source, target in zip(refs[:half], refs[half:]):
        target[...] = source[...].astype(jnp.float32)


def widen(spans, values):
    number, rows, columns = values[0].shape
    (low, high), (again, end) = spans

    def chosen(e):
        return (jnp.where(e < high - low, e + low, e - (high - low) + again), 0, 0)

    block = pl.BlockSpec((1, rows, columns), chosen)
    return pl.pallas_call(
        widen_kernel,
        grid=(high - low + end - again,),
        in_specs=[block] * len(values),
        out_specs=[block] * len(values),
        out_shape=[jax.ShapeDtypeStruct(one.shape, jnp.float32) for one in values],
        compiler_params=pltpu.CompilerParams(vmem_limit_bytes=BIG),
    )(*values)


def widen_pieces_kernel(low, n_pieces, offsets_ref, *refs):
    pieces, refs = refs[:n_pieces], refs[n_pieces + 2 :]
    targets, wide, sems = refs[:2], refs[2], refs[3]
    part = wide.shape[4]
    copies = []
    for k, piece in enumerate(pieces):
        columns = pl.ds(pl.multiple_of(offsets_ref[k], part), part)
        for n in range(2):
            wide[k, n] = piece[:, :, n * part : (n + 1) * part].astype(jnp.float32)
            copy = pltpu.make_async_copy(
                wide.at[k, n], targets[n].at[pl.ds(low, piece.shape[0]), :, columns], sems.at[k, n]
            )
            copy.start()
            copies.append(copy)
    for copy in copies:
        copy.wait()


def widen_pieces(offsets, low, pieces, into):
    size, rows, columns = pieces[0].shape
    anywhere = pl.BlockSpec(memory_space=pl.ANY)
    count = len(pieces)
    return pl.pallas_call(
        functools.partial(widen_pieces_kernel, low, count),
        in_specs=[
            pl.BlockSpec(memory_space=pltpu.SMEM),
            *[pl.BlockSpec(memory_space=pltpu.VMEM)] * count,
            anywhere,
            anywhere,
        ],
        out_specs=[anywhere, anywhere],
        out_shape=[jax.ShapeDtypeStruct(one.shape, one.dtype) for one in into],
        scratch_shapes=[
            pltpu.VMEM((count, 2, size, rows, columns // 2), jnp.float32),
            pltpu.SemaphoreType.DMA((count, 2)),
        ],
        input_output_aliases={1 + count: 0, 2 + count: 1},
        compiler_params=pltpu.CompilerParams(vmem_limit_bytes=BIG),
    )(offsets, *pieces, *into)


def shards(
    n_dp,
    n_expert,
    tokens,
    cotangent,
    lengths,
    routes,
    w_query,
    w_key,
    w_value,
    w_out,
    w_router,
    gain_attn,
    gain_query,
    gain_key,
    gain_mlp,
    w_gate,
    w_up,
    w_down,
):
    groups = n_dp * n_expert
    bf16 = jnp.bfloat16
    number = w_gate.shape[0]
    ff = w_gate.shape[2]
    part = ff // n_dp
    experts_all = w_router.shape[1]
    width = 128
    small = jnp.concatenate(
        [
            w_router,
            gain_attn[:, None],
            gain_query[:, None],
            gain_key[:, None],
            gain_mlp[:, None],
            jnp.zeros((w_router.shape[0], width - experts_all - 4), bf16),
        ],
        axis=1,
    )
    hits = jnp.any(
        routes[:, :, None] == jnp.arange(width, dtype=jnp.int32)[None, None, :], axis=1
    ).astype(bf16)
    count = tokens.shape[0]
    rows_each = w_query.shape[0]
    extras = jnp.concatenate([hits, jnp.pad(small, ((0, count - rows_each), (0, 0)))], axis=1)
    weights = jnp.stack([w_query, w_key, w_value, w_out])
    depth = w_gate.shape[1]
    early = number // 4
    beside = early + number // 8
    late = number - number // 4
    back_beside = number // 8
    back_third = back_beside + max(number // 4, 1)
    back_late = back_third + number // 4
    me = lax.axis_index("dp")
    cut_shape = jax.ShapeDtypeStruct((number, n_dp * depth, part), bf16)

    def row_block(size):
        return lambda ref, block: ref.at[pl.ds(pl.multiple_of(block * size, 16), size)]

    def columns_at(at):
        return pl.ds(pl.multiple_of(at * part, part), part)

    def rows_at(at):
        return pl.ds(pl.multiple_of(at * depth, depth), depth)

    def recut(low, high):
        def cuts(ins, outs):
            def pair(n):
                chosen = pl.ds(low, high - low)
                return (
                    lambda to: ins[n].at[chosen, :, columns_at(to)],
                    lambda at: outs[n].at[chosen, rows_at(at)],
                )

            return [pair(0), pair(1)]

        return cuts

    to_plane, from_plane = partners(me, n_dp)

    def permuted(pieces, chained=False):
        got = []
        for k, piece in enumerate(pieces, 1):
            if chained and got:
                piece, last = lax.optimization_barrier((piece, got.pop()))
                got.append(last)
            paths = [(i, partners(i, n_dp)[0](k)) for i in range(n_dp)]
            got.append(lax.ppermute(piece, "dp", paths))
        return got

    def cut_pieces(low, high, first_k, ins, outs):
        to, unused = partners(lax.axis_index("dp"), n_dp)
        pairs = []
        for k, piece in enumerate(outs, first_k):
            for n in range(2):
                source = ins[n].at[pl.ds(low, high - low), :, columns_at(to(k))]
                pairs.append((source, piece.at[:, :, pl.ds(n * part, part)]))
        return pairs

    def piece_shapes(size, first_k):
        shape = jax.ShapeDtypeStruct((size, depth, 2 * part), bf16)
        return [shape] * (n_dp - first_k if size else 0)

    def stages(*sizes):
        return [(size, depth, part) for size in sizes]

    soon_shapes = piece_shapes(beside - early, 1)
    late_shapes = piece_shapes(number - late, 0)
    n_soon = len(soon_shapes)

    weights_all, extras_all, gate_early, up_early, *pieces = gather_call(
        n_dp,
        n_expert,
        [weights, extras],
        [
            jax.ShapeDtypeStruct((4, groups * rows_each, D), bf16),
            jax.ShapeDtypeStruct((groups * count, 2 * width), bf16),
        ],
        [
            lambda ref, block: ref.at[
                :, pl.ds(pl.multiple_of(block * rows_each, 16), rows_each)
            ],
            row_block(count),
        ],
        [w_gate, w_up],
        [cut_shape, cut_shape, *soon_shapes, *late_shapes],
        recut(0, early),
        {},
        0,
        stages(
            *[early] * 2,
            *[beside - early] * (2 * n_soon),
            *[number - late] * (2 * n_dp),
        ),
        lambda ins, outs: cut_pieces(early, beside, 1, ins, outs[2 : 2 + n_soon])
        + cut_pieces(late, number, 0, ins, outs[2 + n_soon :]),
    )
    soon_pieces, late_pieces = pieces[:n_soon], pieces[n_soon:]
    query_weight, key_weight, value_weight, out_weight = (weights_all[i] for i in range(4))
    small_all = (
        extras_all[:, width:].reshape(groups, count, width)[:, :rows_each].reshape(-1, width)
    )
    hits_all = extras_all[:, :experts_all]
    router_weight = small_all[:, :experts_all]
    gains = small_all[:, experts_all : experts_all + 4].astype(jnp.float32)
    attn_gain, query_gain, key_gain, mlp_gain = (gains[:, i] for i in range(4))
    inputs = tokens.astype(jnp.float32)
    segment, position, places = layout(lengths[0], count)
    half = HD // 2
    freq = 10000.0 ** (-2.0 * jnp.arange(half, dtype=jnp.float32) / HD)
    angle = position.astype(jnp.float32)[:, None] * freq[None, :]
    cosine = jnp.cos(angle)[:, None, :]
    sine = jnp.sin(angle)[:, None, :]
    scale = HD ** (-0.5)
    normed, attn_inverse = rms_forward(inputs, attn_gain)
    normed_low = normed.astype(bf16)
    query_raw = product(normed_low, query_weight, "td,de->te")
    key_raw = product(normed_low, key_weight, "td,de->te")
    value_low = product(normed_low, value_weight, "td,de->te").astype(bf16)
    query_normed, query_inverse = rms_forward(query_raw, query_gain)
    key_normed, key_inverse = rms_forward(key_raw, key_gain)
    query_low = rotate(query_normed, cosine, sine).astype(bf16).reshape(count, HEADS, HD)
    key_low = rotate(key_normed, cosine, sine).astype(bf16).reshape(count, HEADS, HD)
    value_heads = value_low.reshape(count, HEADS, HD)
    allowed = (segment[:, None] == segment[None, :]) & (places[None, :] <= places[:, None])
    scores = product(query_low, key_low, "qhd,khd->hqk") * scale
    scores = jnp.where(allowed[None], scores, -1e30)
    probs = jax.nn.softmax(scores, axis=-1)
    probs_low = probs.astype(bf16)
    attended_low = product(probs_low, value_heads, "hqk,khd->qhd").reshape(count, D).astype(bf16)
    middle = inputs + product(attended_low, out_weight, "td,de->te")
    mlp_normed, mlp_inverse = rms_forward(middle, mlp_gain)
    mlp_low = mlp_normed.astype(bf16)
    router = jax.nn.softmax(product(mlp_low, router_weight, "td,de->te"), axis=-1)

    first = lax.axis_index("expert") * number
    hit = lax.dynamic_slice_in_dim(hits_all, first, number, 1).reshape(groups, count, number)
    before = jnp.tril(jnp.ones((count, count), bf16), -1)
    slot = product(before, hit, "ts,bse->bet").astype(jnp.int32)
    slot = jnp.where(jnp.transpose(hit, (0, 2, 1)) > 0, slot, -1)
    slot = slot.reshape(groups // 2, 2, number, count)
    shift = jnp.array([0, CAP], jnp.int32)[None, :, None, None]
    slots = jnp.transpose(jnp.where(slot < 0, -1, slot + shift), (0, 2, 1, 3))
    slots = slots.reshape(groups // 2, number, 2 * count)
    router_own = jnp.pad(
        jnp.roll(router_weight, -first, axis=1), ((0, 0), (0, width - experts_all))
    )
    if n_soon:
        mlp_low, *soon_pieces = lax.optimization_barrier((mlp_low, *permuted(soon_pieces)))

    def put_weights(ins, outs):
        chosen = pl.ds(early, beside - early)
        unused, heard = partners(lax.axis_index("dp"), n_dp)
        pairs = []
        if beside > early:
            own = lax.axis_index("dp")
            for n in range(2):
                source = ins[n].at[chosen, :, columns_at(own)]
                pairs.append((source, outs[n].at[chosen, rows_at(own)]))
        for k, piece in enumerate(ins[6:], 1):
            for n in range(2):
                columns = piece.at[:, :, pl.ds(n * part, part)]
                pairs.append((columns, outs[n].at[chosen, rows_at(heard(k))]))
        return pairs

    def pick_all(items, ins, outs):
        pick_rows(number, experts_all, ins[4], *items, ins[5], *outs[2:])

    unused, unused, gate_cut, up_cut, rows, grows, gates = gather_call(
        n_dp,
        n_expert,
        [mlp_low, cotangent],
        [jax.ShapeDtypeStruct((groups * count, D), bf16)] * 2,
        [row_block(count)] * 2,
        [w_gate, w_up, gate_early, up_early, slots, router_own, *soon_pieces],
        [cut_shape, cut_shape, *pick_shapes(number, groups // 2)],
        recut(beside, late),
        {4: 2, 5: 3},
        1,
        stages(*[late - beside] * 2, *[beside - early] * (2 * n_dp if n_soon else 0)),
        put_weights,
        pick_all,
    )
    *late_pieces, rows = lax.optimization_barrier((*late_pieces, rows))
    late_pieces = [late_pieces[0], *permuted(late_pieces[1:])]
    packing = back_beside > 0 and depth == 512
    *outs, gate_soon, up_soon, down_soon = expert_call(
        first[None],
        experts_all,
        0,
        late,
        rows,
        grows,
        gates,
        [gate_cut, up_cut],
        w_down,
        pack=(back_beside, n_dp) if packing else (),
    )
    if packing:
        *outs, gate_soon, up_soon, down_soon, packed = [*outs, gate_soon, up_soon, down_soon]
    offsets = [from_plane(k) * depth for k in range(n_dp)]
    weighted, grad_rows, grad_gates, gate_rest, up_rest, grad_down_part = expert_call(
        jnp.stack([first + late, *offsets]),
        experts_all,
        late,
        number - late,
        rows,
        grows,
        gates,
        late_pieces,
        w_down,
        [*outs, down_soon],
    )
    part_back = place_back(slots, grad_rows, grad_gates)

    def ways(low, high, at, ins, outs):
        def pair(e, n):
            return (
                lambda to: ins[n].at[pl.ds(e, 1), rows_at(to)],
                lambda here: outs[n].at[pl.ds(e + at, 1), :, columns_at(here)],
            )

        return [pair(e, n) for e in range(low, high) for n in range(2)]

    def cut_grads(low, high, ins, outs):
        to, unused = partners(lax.axis_index("dp"), n_dp)
        pairs = []
        for k, piece in enumerate(outs, 1):
            for n in range(2):
                source = ins[n].at[pl.ds(low, high - low), rows_at(to(k))]
                pairs.append((source, piece.at[:, :, pl.ds(n * part, part)]))
        return pairs

    pieces = []
    if back_beside:
        for k in range(1, n_dp):
            if packing:
                piece = lax.dynamic_index_in_dim(packed, to_plane(k), 0, False)
            else:
                piece = jnp.concatenate(
                    [
                        lax.dynamic_slice_in_dim(
                            one[:back_beside], to_plane(k) * depth, depth, 1
                        )
                        for one in (gate_soon, up_soon)
                    ],
                    axis=2,
                )
            pieces.append(piece)
        ahead = lax.optimization_barrier((*pieces, *late_pieces[1:]))
        pieces = permuted(ahead[: n_dp - 1])
        part_back, *pieces = lax.optimization_barrier((part_back, *pieces))
    way_shapes = [jax.ShapeDtypeStruct((number, depth, ff), bf16)] * 2
    piece_shape = jax.ShapeDtypeStruct((back_late - back_third, depth, 2 * part), bf16)
    (back,), (gate_third, up_third, part_out, *later_pieces) = scatter_all(
        n_dp,
        n_expert,
        [part_back.reshape(n_dp, n_expert, count, D + width)],
        [4],
        [gate_soon, up_soon, slots, weighted],
        [
            *way_shapes,
            jax.ShapeDtypeStruct((groups * count, D), bf16),
            *[piece_shape] * (n_dp - 1),
        ],
        lambda ins, outs: ways(back_beside, back_third, 0, ins, outs),
        8,
        (),
        stages(
            *[1] * (2 * (back_third - back_beside)),
            *[back_late - back_third] * (2 * (n_dp - 1)),
        ),
        lambda ins, outs: cut_grads(back_third, back_late, ins, outs[3:]),
        lambda ins, outs: place_out(ins[2], ins[3], outs[2]),
    )
    later_pieces = permuted(later_pieces)

    def attention_back(back):
        grad_final = cotangent.astype(jnp.float32)
        grad_mlp = back[:, :D]
        grad_router_probs = back[:, D : D + experts_all] + back[:, D + experts_all :]
        grad_logits = router * (
            grad_router_probs - jnp.sum(router * grad_router_probs, axis=1, keepdims=True)
        )
        grad_logits_low = grad_logits.astype(bf16)
        grad_router_full = product(
            mlp_low, jnp.pad(grad_logits_low, ((0, 0), (0, width - experts_all))), "td,te->de"
        )
        grad_mlp = grad_mlp + product(grad_logits_low, router_weight, "te,de->td")
        grad_middle_part, grad_mlp_gain = rms_backward(middle, mlp_inverse, mlp_gain, grad_mlp)
        grad_middle = grad_final + grad_middle_part
        grad_branch_low = grad_middle.astype(bf16)
        grad_attended = (
            through([grad_branch_low], weights_all, 3).astype(bf16).reshape(count, HEADS, HD)
        )
        grad_weights = product(grad_attended, value_heads, "qhd,khd->hqk")
        grad_scores = probs * (grad_weights - jnp.sum(probs * grad_weights, axis=-1, keepdims=True))
        grad_scores_low = grad_scores.astype(bf16)
        grad_query_turn = product(grad_scores_low, key_low, "hqk,khd->qhd").reshape(count, D) * scale
        grad_key_turn = product(grad_scores_low, query_low, "hqk,qhd->khd").reshape(count, D) * scale
        grad_value_low = (
            product(probs_low, grad_attended, "hqk,qhd->khd").reshape(count, D).astype(bf16)
        )
        grad_query_raw, grad_query_gain = rms_backward(
            query_raw, query_inverse, query_gain, rotate(grad_query_turn, cosine, -sine)
        )
        grad_key_raw, grad_key_gain = rms_backward(
            key_raw, key_inverse, key_gain, rotate(grad_key_turn, cosine, -sine)
        )
        grad_query_low = grad_query_raw.astype(bf16)
        grad_key_low = grad_key_raw.astype(bf16)
        full_grads = outer(
            [attended_low, normed_low],
            [grad_branch_low, grad_value_low, grad_key_low, grad_query_low],
            (0, 1, 1, 1),
        )
        grad_normed = through([grad_query_low, grad_key_low, grad_value_low], weights_all, 0)
        grad_inputs_part, grad_attn_gain = rms_backward(inputs, attn_inverse, attn_gain, grad_normed)
        grad_inputs = grad_middle + grad_inputs_part

        gain_grads = jnp.stack([grad_attn_gain, grad_query_gain, grad_key_gain, grad_mlp_gain])
        gain_grads = jnp.transpose(gain_grads.reshape(4, groups, rows_each), (1, 0, 2))
        gain_grads = jnp.pad(gain_grads, ((0, 0), (0, 12), (0, width - rows_each)))
        return (
            grad_inputs,
            *full_grads,
            grad_router_full.astype(bf16),
            gain_grads.astype(bf16).reshape(groups * 16, width),
        )

    def unreached(back):
        shapes = [(count, D)] + [(D, D)] * 4 + [(D, width), (groups * 16, width)]
        kinds = [jnp.float32] + [bf16] * 6
        return tuple(jnp.zeros(shape, kind) for shape, kind in zip(shapes, kinds))

    grad_inputs, *weight_grads = lax.cond(lengths[0, 0] > 0, attention_back, unreached, back)

    def blocks_of(value):
        return value.reshape(n_dp, n_expert, -1, value.shape[1])

    sums, (gate_back, up_back) = scatter_all(
        n_dp,
        n_expert,
        [part_out.reshape(n_dp, n_expert, count, D)]
        + [blocks_of(value) for value in weight_grads],
        [2, 1, 1, 1, 2 if rows_each > 16 else 1, 1, 1],
        [gate_third, up_third, gate_soon, up_soon, gate_rest, up_rest],
        way_shapes,
        lambda ins, outs: ways(back_late, late, 0, ins[2:4], outs)
        + ways(0, number - late, late, ins[4:6], outs),
        16,
        ((0, 0), (1, 1)),
        [],
    )
    summed, grad_out_part, grad_value_part, grad_key_part, grad_query_part, router_part, small = sums
    output = (middle + summed).astype(bf16)
    grad_router_part = router_part[:, :experts_all]
    gain_parts = [small[i, :rows_each] for i in range(4)]
    widened = widen([(back_beside, back_third), (back_late, number)], [gate_back, up_back])
    offsets = jnp.stack([from_plane(k) * part for k in range(n_dp)])
    for low, high, others in (
        (0, back_beside, pieces),
        (back_third, back_late, later_pieces),
    ):
        if high > low:
            own = jnp.concatenate(
                [
                    lax.dynamic_slice_in_dim(one[low:high], me * depth, depth, 1)
                    for one in (gate_soon, up_soon)
                ],
                axis=2,
            )
            widened = widen_pieces(offsets, low, [own, *others], widened)
    grad_gate_part, grad_up_part = widened
    return (
        output,
        grad_inputs,
        grad_query_part,
        grad_key_part,
        grad_value_part,
        grad_out_part,
        grad_router_part,
        gain_parts[0],
        gain_parts[1],
        gain_parts[2],
        gain_parts[3],
        grad_gate_part,
        grad_up_part,
        grad_down_part,
    )


def solution(mesh):
    return jax.shard_map(
        functools.partial(shards, mesh.shape["dp"], mesh.shape["expert"]),
        mesh=mesh,
        in_specs=(
            P(("dp", "expert"), None),
            P(("dp", "expert"), None),
            P(("dp", "expert"), None),
            P(("dp", "expert"), None),
            P(("dp", "expert"), None),
            P(("dp", "expert"), None),
            P(("dp", "expert"), None),
            P(("dp", "expert"), None),
            P(("dp", "expert"), None),
            P(("dp", "expert")),
            P(("dp", "expert")),
            P(("dp", "expert")),
            P(("dp", "expert")),
            P("expert", "dp", None),
            P("expert", "dp", None),
            P("expert", "dp", None),
        ),
        out_specs=(
            P(("dp", "expert"), None),
            P(("dp", "expert"), None),
            P(("dp", "expert"), None),
            P(("dp", "expert"), None),
            P(("dp", "expert"), None),
            P(("dp", "expert"), None),
            P(("dp", "expert"), None),
            P(("dp", "expert")),
            P(("dp", "expert")),
            P(("dp", "expert")),
            P(("dp", "expert")),
            P("expert", "dp", None),
            P("expert", "dp", None),
            P("expert", "dp", None),
        ),
        check_vma=False,
    )
```

```python
import functools

import jax
import jax.numpy as jnp
from jax import lax
from jax.experimental import pallas as pl
from jax.experimental.pallas import tpu as pltpu
from jax.sharding import PartitionSpec as P

D = 2048
HEADS = 16
HD = 128
TOPK = 8
CAP = 24


eps = 1e-05


def product(left, right, form):
    return jnp.einsum(form, left, right, preferred_element_type=jnp.float32)


def rms_forward(values, gain):
    inverse = lax.rsqrt(jnp.mean(values * values, axis=-1, keepdims=True) + eps)
    return (values * inverse * gain, inverse)


def rms_backward(values, inverse, gain, grad):
    scaled = grad * gain
    inner = jnp.mean(scaled * values, axis=-1, keepdims=True)
    grad_values = inverse * scaled - values * (inverse * inverse * inverse) * inner
    grad_gain = jnp.sum(grad * values * inverse, axis=0)
    return (grad_values, grad_gain)


def layout(lengths_row, count):
    places = jnp.arange(count, dtype=jnp.int32)
    ends = jnp.cumsum(lengths_row, dtype=jnp.int32)
    passed = (places[:, None] >= ends[None, :]).astype(jnp.int32)
    segment = jnp.sum(passed, axis=1, dtype=jnp.int32)
    start = jnp.sum(passed * lengths_row[None, :], axis=1, dtype=jnp.int32)
    return (segment, places - start, places)


def rotate(values, cosine, sine):
    count = values.shape[0]
    heads = values.reshape(count, HEADS, HD)
    half = HD // 2
    first = heads[..., :half]
    second = heads[..., half:]
    turned = jnp.concatenate(
        [first * cosine - second * sine, second * cosine + first * sine], axis=-1
    )
    return turned.reshape(count, D)


MESH = pl.DeviceIdType.MESH
BIG = 60 * 1024 * 1024


def place_of():
    z = lax.axis_index("dp")
    j = lax.axis_index("expert")
    return z, j, j // 2, j % 2


def other_chips(chip, chips):
    if chips == 4:
        square = [chip, chip + 1 - 2 * (chip % 2), chip + 2 - 4 * (chip // 2), 3 - chip]
        return lambda k: square[k], lambda k: square[k]
    return lambda k: (chip + k) % chips, lambda k: (chip + chips - k) % chips


def partners(z, n_dp):
    if n_dp == 4:
        pairs = [z, 3 - z, (z + 2) % 4, z + 1 - 2 * (z % 2)]
        return lambda k: pairs[k], lambda k: pairs[k]
    return lambda k: (z + k) % n_dp, lambda k: (z + n_dp - k) % n_dp


def greet(n_dp, n_expert):
    z, j, chip, core = place_of()
    chips = n_expert // 2
    barrier = pltpu.get_barrier_semaphore()
    for k in range(1, n_dp):
        pl.semaphore_signal(
            barrier, inc=1, device_id=((z + k) % n_dp, j), device_id_type=MESH
        )
    for k in range(1, chips):
        other = ((chip + k) % chips) * 2 + core
        pl.semaphore_signal(barrier, inc=1, device_id=(z, other), device_id_type=MESH)
    pl.semaphore_signal(
        barrier, inc=1, device_id=(z, chip * 2 + 1 - core), device_id_type=MESH
    )
    pl.semaphore_wait(barrier, n_dp - 1 + chips - 1 + 1)


def remote(source, target, send, receive, device):
    return pltpu.make_async_remote_copy(
        src_ref=source,
        dst_ref=target,
        send_sem=send,
        recv_sem=receive,
        device_id=device,
        device_id_type=MESH,
    )


def exchange(n_dp, pairs, send, receive):
    z, j, chip, core = place_of()
    to_plane, unused = partners(z, n_dp)
    copies = []
    for i, (source, target) in enumerate(pairs):
        for k in range(1, n_dp):
            to = to_plane(k)
            copies.append(
                remote(source(to), target(z), send.at[i, k], receive.at[i, k], (to, j))
            )
    return copies


def moves(pairs, stages, local):
    if not stages:
        copies = [
            pltpu.make_async_copy(source, target, local.at[i, 0])
            for i, (source, target) in enumerate(pairs)
        ]
        for copy in copies:
            copy.start()
        return [], copies
    bring = [
        pltpu.make_async_copy(source, stages[i], local.at[i, 0])
        for i, (source, target) in enumerate(pairs)
    ]
    put = [
        pltpu.make_async_copy(stages[i], target, local.at[i, 1])
        for i, (source, target) in enumerate(pairs)
    ]
    return bring, put


def nothing(ins, outs):
    return []


def gather_kernel(
    n_dp, n_expert, n_items, places, cuts, puts, finish, n_cut, n_out, n_stages, *refs
):
    z, j, chip, core = place_of()
    chips = n_expert // 2
    square = chips == 4
    to_chip, from_chip = other_chips(chip, chips)
    sources = refs[:n_items]
    cut_in = refs[n_items : n_items + n_cut]
    at = n_items + n_cut
    targets = refs[at : at + n_items]
    cut_out = refs[at + n_items : at + n_items + n_out]
    (
        send_c,
        recv_c,
        send_b,
        recv_b,
        send_a,
        recv_a,
        local,
        send_x,
        recv_x,
        local_y,
        *stages,
    ) = refs[at + n_items + n_out :]
    greet(n_dp, n_expert)
    mate = (z, chip * 2 + 1 - core)
    near = (1, 2) if square else tuple(range(1, chips))

    def slot(i, plane, column):
        return places[i](targets[i], plane * n_expert + column)

    def pass_on(i, plane, source, column, k, chip_to):
        return remote(
            source,
            slot(i, plane, column),
            send_b.at[i, plane, k],
            recv_b.at[i, plane, k],
            (z, chip_to * 2 + core),
        )

    def hand(i, plane, source):
        for k in near:
            pass_on(i, plane, source, j, k, to_chip(k)).start()
        remote(
            source, slot(i, plane, j), send_a.at[i, plane, 0], recv_a.at[i, plane, 0], mate
        ).start()

    def along(i, plane, source, way, step):
        return remote(
            source, slot(i, plane, j), send_c.at[i, way, plane], recv_c.at[i, plane], (z + step, j)
        )

    def at_distance(d, body):
        if d == 0:
            body(z, 0)
            return

        @pl.when(z >= d)
        def _():
            body(z - d, 0)

        @pl.when(z + d < n_dp)
        def _():
            body(z + d, 1)

    for i in range(n_items):

        @pl.when(z < n_dp - 1)
        def _():
            along(i, z, sources[i], 0, 1).start()

        @pl.when(z > 0)
        def _():
            along(i, z, sources[i], 1, -1).start()

        hand(i, z, sources[i])
        pltpu.make_async_copy(sources[i], slot(i, z, j), local.at[i]).start()

    def relay(plane, way):
        step = -1 if way else 1
        for i in range(n_items):
            block = slot(i, plane, j)
            along(i, plane, block, way, step).wait_recv()

            @pl.when(z > 0 if way else z < n_dp - 1)
            def _():
                along(i, plane, block, way, step).start()

            hand(i, plane, block)

    for d in range(1, n_dp):
        at_distance(d, relay)
    pairs = cuts(cut_in, cut_out)
    copies = exchange(n_dp, pairs, send_x, recv_x)
    for copy in copies:
        copy.start()
    own = [(source(z), target(z)) for source, target in pairs]
    bring, put = moves(own + puts(cut_in, cut_out), stages, local_y)
    for copy in bring:
        copy.start()
    for one, other in zip(bring, put):
        one.wait()
        other.start()

    def arrive(i, plane, k):
        column = from_chip(k) * 2 + core
        block = slot(i, plane, column)
        pass_on(i, plane, block, column, k, chip).wait_recv()
        remote(block, block, send_a.at[i, plane, k], recv_a.at[i, plane, k], mate).start()
        return block, column

    def arrived(plane, way):
        for i in range(n_items):
            for k in near:
                block, column = arrive(i, plane, k)
                if square:

                    @pl.when(plane % 2 == k - 1)
                    def _():
                        pass_on(i, plane, block, column, 3, to_chip(3 - k)).start()

    def crossed(plane, way):
        for i in range(n_items):
            arrive(i, plane, 3)

    for d in range(n_dp):
        at_distance(d, arrived)
    if square:
        for d in range(n_dp):
            at_distance(d, crossed)

    for i in range(n_items):
        for plane in range(n_dp):
            for k in range(chips):
                column = (from_chip(k) if k else chip) * 2 + 1 - core
                block = slot(i, plane, column)
                remote(
                    block, block, send_a.at[i, plane, k], recv_a.at[i, plane, k], mate
                ).wait_recv()
        pltpu.make_async_copy(sources[i], slot(i, z, j), local.at[i]).wait()
    finish(targets, cut_in, cut_out)
    for i in range(n_items):
        for plane in range(n_dp):
            block = slot(i, plane, j)
            for k in range(1, chips):
                pass_on(i, plane, block, j, k, chip).wait_send()
            for k in range(chips):
                remote(
                    block, block, send_a.at[i, plane, k], recv_a.at[i, plane, k], mate
                ).wait_send()

            @pl.when((z < n_dp - 1) & (z >= plane))
            def _():
                along(i, plane, block, 0, 1).wait_send()

            @pl.when((z > 0) & (z <= plane))
            def _():
                along(i, plane, block, 1, -1).wait_send()

    for copy in copies + put:
        copy.wait()


def gather_call(
    n_dp,
    n_expert,
    items,
    shapes,
    places,
    cut_in,
    cut_shapes,
    cuts,
    aliases,
    number,
    stages,
    puts=nothing,
    finish=lambda items, ins, outs: None,
):
    chips = n_expert // 2
    n, m = len(items), len(cut_shapes)
    dma = pltpu.SemaphoreType.DMA
    anywhere = pl.BlockSpec(memory_space=pl.ANY)
    return pl.pallas_call(
        functools.partial(
            gather_kernel,
            n_dp,
            n_expert,
            n,
            places,
            cuts,
            puts,
            finish,
            len(cut_in),
            m,
            len(stages),
        ),
        out_shape=[*shapes, *cut_shapes],
        in_specs=[anywhere] * (n + len(cut_in)),
        out_specs=[anywhere] * (n + m),
        scratch_shapes=[
            dma((n, 2, n_dp)),
            dma((n, n_dp)),
            dma((n, n_dp, chips)),
            dma((n, n_dp, chips)),
            dma((n, n_dp, chips)),
            dma((n, n_dp, chips)),
            dma((n,)),
            dma((4, n_dp)),
            dma((4, n_dp)),
            dma((max(len(stages), 4), 2)),
            *[pltpu.VMEM(stage, jnp.bfloat16) for stage in stages],
        ],
        input_output_aliases=aliases,
        compiler_params=pltpu.CompilerParams(
            collective_id=number, has_side_effects=True, vmem_limit_bytes=BIG
        ),
    )(*items, *cut_in)


def scatter_kernel(
    n_dp, n_expert, n_arrays, items, n_cut, n_out, cuts, puts, middle, rings, n_rings, *refs
):
    n_items = len(items)
    z, j, chip, core = place_of()
    chips = n_expert // 2
    square = chips == 4
    to_chip, from_chip = other_chips(chip, chips)
    refs = list(refs)

    def take(count):
        taken = refs[:count]
        del refs[:count]
        return taken

    sources, cut_in, targets, cut_out = take(n_arrays), take(n_cut), take(n_arrays), take(n_out)
    ring, got_a, got_b, got_c = take(n_rings), take(n_items), take(n_items), take(n_items)
    transit = take(n_items)
    (
        send_a,
        recv_a,
        send_b,
        recv_b,
        send_c,
        recv_c,
        send_t,
        recv_t,
        local,
        send_x,
        recv_x,
        local_y,
        *stages,
    ) = refs
    greet(n_dp, n_expert)
    mate = (z, chip * 2 + 1 - core)
    order = [3, 1, 2, 0] if square else [*range(1, chips), 0]
    half = n_dp // 2
    low, high = pl.ds(0, half), pl.ds(half, n_dp - half)

    def chip_of(k):
        return to_chip(k) if k else chip

    def source(i, column):
        array, first, rows = items[i]
        return sources[array].at[:, column, pl.ds(first, rows)]

    def to_mate(i, k):
        return remote(
            source(i, chip_of(k) * 2 + 1 - core),
            got_a[i].at[k],
            send_a.at[i, k],
            recv_a.at[i, k],
            mate,
        )

    turn = [0] * n_rings
    loads = []
    for i in range(n_items):
        for k in order:
            loads.append((i, k, turn[rings[i]] % 2))
            turn[rings[i]] += 1

    def load(i, k, at):
        return pltpu.make_async_copy(
            source(i, chip_of(k) * 2 + core), ring[rings[i]].at[at], local.at[rings[i], at]
        )

    def send_near(i, k, part, number):
        return remote(
            got_a[i].at[k, part],
            got_b[i].at[k - 1, part],
            send_b.at[i, number],
            recv_b.at[i, number],
            (z, to_chip(k) * 2 + core),
        )

    def send_over(i, k, part):
        return remote(
            got_a[i].at[3, part],
            transit[i].at[k - 1],
            send_t.at[i, k],
            recv_t.at[i, k],
            (z, to_chip(k) * 2 + core),
        )

    def send_far(i, k):
        return remote(
            got_a[i].at[k],
            got_b[i].at[k - 1],
            send_b.at[i, k],
            recv_b.at[i, k],
            (z, to_chip(k) * 2 + core),
        )

    def along(i, plane, way):
        slot = n_dp - (z - 1) + plane if way else plane - (z + 1)
        return remote(
            got_a[i].at[0, plane],
            got_c[i].at[slot],
            send_c.at[i, plane],
            recv_c.at[i, slot],
            (z - 1 if way else z + 1, j),
        )

    def from_along(i, slot):
        return remote(
            got_c[i].at[slot], got_c[i].at[slot], send_c.at[i, 0], recv_c.at[i, slot], mate
        )

    f32 = jnp.float32

    def add(i, planes, target, terms):
        rows = got_a[i].shape[2]
        per = rows // 16

        def step(n, unused):
            plane = n // per
            at = pl.ds(pl.multiple_of((n % per) * 16, 16), 16)
            total = terms[0](plane, at).astype(f32)
            for term in terms[1:]:
                total = total + term(plane, at).astype(f32)
            target(plane, at, total)
            return unused

        lax.fori_loop(0, planes * per, step, 0)

    def grow(i, k, first, planes, term):
        def target(plane, at, total):
            got_a[i][k, plane + first, at] = total.astype(got_a[i].dtype)

        add(i, planes, target, [lambda plane, at: got_a[i][k, plane + first, at], term])

    for i in range(n_items):
        for k in order:
            to_mate(i, k).start()
    started = 0
    ahead = [0] * n_rings
    for i, k, at in loads:
        if ahead[rings[i]] < 2:
            load(i, k, at).start()
            ahead[rings[i]] += 1
    pairs = cuts(cut_in, cut_out)
    copies = exchange(n_dp, pairs, send_x, recv_x)
    own = [(source(z), target(z)) for source, target in pairs]
    bring, put = moves(own + puts(cut_in, cut_out), stages, local_y)
    for copy in bring:
        copy.start()

    def over_cores(i):
        for n, (item, k, at) in enumerate(loads):
            if item != i:
                continue
            load(i, k, at).wait()
            to_mate(i, k).wait_recv()
            grow(i, k, 0, n_dp, lambda plane, rows: ring[rings[i]][at, plane, rows])
            later = [one for one in loads[n + 1 :] if rings[one[0]] == rings[i]]
            if len(later) >= 2:
                load(*later[1]).start()
            if not k:
                continue
            if not square:
                send_far(i, k).start()
            elif k == 3:
                send_over(i, 1, low).start()
                send_over(i, 2, high).start()
            elif k == 1:
                send_near(i, 1, low, 0).start()
            else:
                send_near(i, 2, high, 1).start()

    def pass_over(i):
        if not square:
            return
        send_over(i, 2, high).wait_recv()
        grow(i, 1, half, n_dp - half, lambda plane, rows: transit[i][1, plane, rows])
        send_near(i, 1, high, 2).start()
        send_over(i, 1, low).wait_recv()
        grow(i, 2, 0, half, lambda plane, rows: transit[i][0, plane, rows])
        send_near(i, 2, low, 3).start()

    def over_chips(i):
        if square:
            send_near(i, 1, low, 0).wait_recv()
            send_near(i, 2, high, 1).wait_recv()
            send_near(i, 1, high, 2).wait_recv()
            send_near(i, 2, low, 3).wait_recv()
        else:
            for k in range(1, chips):
                send_far(i, k).wait_recv()
        heard = 2 if square else chips - 1

        def target(plane, at, total):
            got_a[i][0, plane, at] = total.astype(got_a[i].dtype)

        terms = [lambda plane, at: got_a[i][0, plane, at]]
        for other in range(heard):
            terms.append(lambda plane, at, other=other: got_b[i][other, plane, at])
        add(i, n_dp, target, terms)
        for d in range(n_dp - 1, 0, -1):
            for way in (0, 1):
                plane = z - d if way else z + d

                @pl.when(z == (n_dp - 1 if way else 0))
                def _():
                    along(i, plane, way).start()

    def over_planes(i):
        for d in range(n_dp - 2, 0, -1):
            for way in (0, 1):
                plane = z - d if way else z + d
                slot = n_dp - d if way else d

                @pl.when((plane >= 0) & (z < n_dp - 1) if way else (plane < n_dp) & (z > 0))
                def _():
                    from_along(i, slot).wait_recv()
                    grow(i, 0, plane, 1, lambda unused, at: got_c[i][slot, at])
                    along(i, plane, way).start()

    def finish(i):
        array, first, rows = items[i]

        def here(at):
            return pl.ds(pl.multiple_of(first + at.start, 16), 16)

        def own(unused, at, total):
            targets[array][here(at)] = total

        add(i, 1, own, [lambda unused, at: got_a[i][0, z, at]])
        for slot, arrives in ((0, z > 0), (n_dp, z < n_dp - 1)):

            @pl.when(arrives)
            def _():
                from_along(i, slot).wait_recv()
                add(
                    i,
                    1,
                    own,
                    [
                        lambda unused, at: targets[array][here(at)],
                        lambda unused, at: got_c[i][slot, at],
                    ],
                )

    behind = min(4, n_items // 2)
    steps = (
        (0, over_cores),
        (1, pass_over),
        (2, over_chips),
        (2 + behind, over_planes),
        (3 + behind, finish),
    )
    share = -(-len(copies) // n_items)
    for n in range(n_items + 3 + behind):
        for copy in copies[n * share : (n + 1) * share]:
            copy.start()
        for late, step in steps:
            if 0 <= n - late < n_items:
                step(n - late)
        if n == min(1, n_items - 1):
            for one, other in zip(bring, put):
                one.wait()
                other.start()
            middle(cut_in, cut_out)
    for i in range(n_items):
        for k in range(chips):
            to_mate(i, k).wait_send()
        if square:
            for k, part in ((1, low), (2, high)):
                send_over(i, k, part).wait_send()
            for k, part, number in ((1, low, 0), (2, high, 1), (1, high, 2), (2, low, 3)):
                send_near(i, k, part, number).wait_send()
        else:
            for k in range(1, chips):
                send_far(i, k).wait_send()
        for plane in range(n_dp):

            @pl.when(z != plane)
            def _():
                remote(
                    got_a[i].at[0, plane],
                    got_c[i].at[0],
                    send_c.at[i, plane],
                    recv_c.at[i, 0],
                    mate,
                ).wait_send()

    for copy in copies + put:
        copy.wait()


def scatter_call(
    n_dp,
    n_expert,
    arrays,
    splits,
    cut_in,
    cut_shapes,
    cuts,
    number,
    aliases,
    stages,
    puts=nothing,
    middle=nothing,
):
    chips = n_expert // 2
    square = chips == 4
    items = []
    for array, (one, split) in enumerate(zip(arrays, splits)):
        rows = one.shape[2] // split
        items += [(array, first, rows) for first in range(0, one.shape[2], rows)]
    n, m = len(items), len(cut_shapes)
    count = len(arrays)
    dma = pltpu.SemaphoreType.DMA
    anywhere = pl.BlockSpec(memory_space=pl.ANY)
    blocks = [(rows, arrays[array].shape[3]) for array, unused, rows in items]
    kinds = sorted(set(blocks))
    rings = [kinds.index(block) for block in blocks]
    bf16 = jnp.bfloat16
    heard = 2 if square else chips - 1
    return pl.pallas_call(
        functools.partial(
            scatter_kernel,
            n_dp,
            n_expert,
            count,
            items,
            len(cut_in),
            m,
            cuts,
            puts,
            middle,
            rings,
            len(kinds),
        ),
        out_shape=[
            *[jax.ShapeDtypeStruct(one.shape[2:], jnp.float32) for one in arrays],
            *cut_shapes,
        ],
        in_specs=[anywhere] * (count + len(cut_in)),
        out_specs=[pl.BlockSpec(memory_space=pltpu.VMEM)] * count + [anywhere] * m,
        scratch_shapes=[
            *[pltpu.VMEM((2, n_dp, *kind), bf16) for kind in kinds],
            *[pltpu.VMEM((chips, n_dp, *block), bf16) for block in blocks],
            *[pltpu.VMEM((heard, n_dp, *block), bf16) for block in blocks],
            *[pltpu.VMEM((n_dp + 1, *block), bf16) for block in blocks],
            *[pltpu.VMEM((2, n_dp // 2, *(block if square else (16, 128))), bf16) for block in blocks],
            dma((n, chips)),
            dma((n, chips)),
            dma((n, chips)),
            dma((n, chips)),
            dma((n, n_dp)),
            dma((n, n_dp + 1)),
            dma((n, 3)),
            dma((n, 3)),
            dma((len(kinds), 2)),
            dma((16, n_dp)),
            dma((16, n_dp)),
            dma((max(len(stages), 16), 2)),
            *[pltpu.VMEM(stage, jnp.bfloat16) for stage in stages],
        ],
        input_output_aliases=aliases,
        compiler_params=pltpu.CompilerParams(
            collective_id=number, has_side_effects=True, vmem_limit_bytes=62 * 1024 * 1024
        ),
    )(*arrays, *cut_in)


def scatter_all(
    n_dp,
    n_expert,
    items,
    splits,
    cut_in,
    cut_shapes,
    cuts,
    number,
    aliases,
    stages,
    puts=nothing,
    middle=nothing,
):
    chips = n_expert // 2
    blocks = (2 * chips - 1 if chips != 4 else 7) * n_dp + n_dp + 3
    need = sum(blocks * item.shape[2] * item.shape[3] * 2 for item in items)
    kinds = {(item.shape[2] // split, item.shape[3]) for item, split in zip(items, splits)}
    need += sum(2 * n_dp * kind[0] * kind[1] * 2 for kind in kinds)
    need += sum(stage[0] * stage[1] * stage[2] * 2 for stage in stages)
    pieces = -(-need // (61 * 1024 * 1024))
    tiles = [item.shape[3] // 128 for item in items]
    results = [[] for item in items]
    extra = []
    for piece in range(pieces):
        ends = [(t * piece // pieces * 128, t * (piece + 1) // pieces * 128) for t in tiles]
        used = [i for i, (low, high) in enumerate(ends) if high > low]
        first = piece == 0
        outs = scatter_call(
            n_dp,
            n_expert,
            [items[i][..., ends[i][0] : ends[i][1]] if pieces > 1 else items[i] for i in used],
            [splits[i] for i in used],
            cut_in if first else [],
            cut_shapes if first else [],
            cuts if first else nothing,
            number + piece,
            {len(used) + a: len(used) + b for a, b in aliases} if first else {},
            stages if first else [],
            puts if first else nothing,
            middle if first else nothing,
        )
        for i, out in zip(used, outs):
            results[i].append(out)
        if first:
            extra = outs[len(used) :]
    return [one[0] if len(one) == 1 else jnp.concatenate(one, axis=1) for one in results], extra


def dot(left, right, dims):
    return lax.dot_general(
        left, right, ((dims[:1], dims[1:]), ((), ())), preferred_element_type=jnp.float32
    )


def picks(slots_ref, number):
    pair = slots_ref.shape[2]
    rows = lax.broadcasted_iota(jnp.int32, (2 * CAP, pair), 0)
    return [slots_ref[0, e : e + 1, :] == rows for e in range(number)]


def pick_kernel(number, experts_all, slots_ref, x_ref, g_ref, router_ref, rows_ref, grows_ref, gates_ref):
    chosen = picks(slots_ref, number)
    pick = jnp.concatenate(chosen, axis=0).astype(jnp.bfloat16)
    size = 2 * CAP
    x = x_ref[...]
    logits = dot(router_ref[...], x, (0, 1))
    names = lax.broadcasted_iota(jnp.int32, logits.shape, 0)
    logits = jnp.where(names < experts_all, logits, -1e30)
    weights = jnp.exp(logits - jnp.max(logits, axis=0, keepdims=True))
    probs = weights / jnp.sum(weights, axis=0, keepdims=True)
    for e in range(number):
        gate = jnp.sum(jnp.where(chosen[e], probs[e : e + 1, :], 0.0), axis=1, keepdims=True)
        gates_ref[e] = jnp.broadcast_to(gate, (size, 128))
    picked = dot(pick, x, (1, 0)).astype(jnp.bfloat16)
    for e in range(number):
        rows_ref[e] = picked[e * size : (e + 1) * size]
    picked = dot(pick, g_ref[...], (1, 0)).astype(jnp.bfloat16)
    for e in range(number):
        grows_ref[e] = picked[e * size : (e + 1) * size]


def expert_kernel(steps, half, n_weights, n_into, n_pack, names_ref, x_ref, g_ref, gates_ref, *refs):
    weights, refs = refs[:n_weights], refs[n_weights:]
    down_ref, refs = refs[0], refs[1 + n_into :]
    (
        y_ref,
        dx_ref,
        probs_ref,
        dgate_ref,
        dup_ref,
        ddown_ref,
        *pack_refs,
        sum_gate,
        sum_up,
    ) = refs
    bf16 = jnp.bfloat16
    g = g_ref[0]
    rows, width = x_ref.shape[1:]
    part = dgate_ref.shape[2]
    gate = gates_ref[0][:, :1]
    if n_weights == 2:
        piece = 512
        gate_ref, up_ref = weights
        gate_mid = dot(x_ref[0], gate_ref[0], (1, 0))
        up_mid = dot(x_ref[0], up_ref[0], (1, 0))
        spans = [
            (pl.ds(at, piece), gate_ref, up_ref, pl.ds(at, piece), pl.ds(0, part), pl.ds(0, part))
            for at in range(0, width, piece)
        ]
    else:
        piece = width // n_weights
        spans = []
        gate_mid = up_mid = 0.0
        for n, ref in enumerate(weights):
            span = pl.ds(pl.multiple_of(names_ref[1 + n], piece), piece)
            x_part = x_ref[0, :, span]
            gate_mid = gate_mid + dot(x_part, ref[0, :, :part], (1, 0))
            up_mid = up_mid + dot(x_part, ref[0, :, part:], (1, 0))
            spans.append((span, ref, ref, pl.ds(0, piece), pl.ds(0, part), pl.ds(part, part)))
    sigmoid = 1.0 / (1.0 + jnp.exp(-gate_mid))
    silu = gate_mid * sigmoid
    hidden = silu * up_mid
    hidden_low = hidden.astype(bf16)
    grad_plain = dot(g, down_ref[0], (1, 1))
    grad_gates = jnp.sum(grad_plain * hidden_low.astype(jnp.float32), axis=1, keepdims=True)
    high = grad_gates.astype(bf16).astype(jnp.float32)
    lane = lax.broadcasted_iota(jnp.int32, (rows, 128), 1)
    name = names_ref[0] + pl.program_id(0)
    probs_ref[0] = (
        jnp.where(lane == name, high, 0.0) + jnp.where(lane == name + half, grad_gates - high, 0.0)
    ).astype(bf16)
    grad_hidden = grad_plain * gate
    grad_gate = (
        grad_hidden * up_mid * sigmoid * (1.0 + gate_mid * (1.0 - sigmoid))
    ).astype(bf16)
    grad_up = (grad_hidden * silu).astype(bf16)
    scaled = (hidden * gate).astype(bf16)
    for at in range(0, width, piece):
        y_ref[0, :, at : at + piece] = (
            dot(hidden_low, down_ref[0, :, at : at + piece], (1, 0)) * gate
        ).astype(bf16)
    for span, gate_ref, up_ref, here, gate_columns, up_columns in spans:
        dx_ref[0, :, span] = (
            dot(grad_gate, gate_ref[0, here, gate_columns], (1, 1))
            + dot(grad_up, up_ref[0, here, up_columns], (1, 1))
        ).astype(bf16)
    step = pl.program_id(1)
    for span, *unused in spans:
        x_part = x_ref[0, :, span]
        here_gate = dot(x_part, grad_gate, (0, 0))
        here_up = dot(x_part, grad_up, (0, 0))
        here_down = dot(scaled, g_ref[0, :, span], (0, 0))
        if steps == 1:
            dgate_ref[0, span, :] = here_gate.astype(bf16)
            dup_ref[0, span, :] = here_up.astype(bf16)
            ddown_ref[0, :, span] = here_down
            continue

        @pl.when(step == 0)
        def _():
            sum_gate[span, :] = here_gate
            sum_up[span, :] = here_up
            ddown_ref[0, :, span] = here_down

        @pl.when(step > 0)
        def _():
            sum_gate[span, :] += here_gate
            sum_up[span, :] += here_up
            ddown_ref[0, :, span] += here_down

        @pl.when(step == steps - 1)
        def _():
            dgate_ref[0, span, :] = sum_gate[span, :].astype(bf16)
            dup_ref[0, span, :] = sum_up[span, :].astype(bf16)

    if n_pack:

        @pl.when((step == steps - 1) & (pl.program_id(0) < n_pack))
        def _():
            pack_ref = pack_refs[0]
            depth = pack_ref.shape[2]
            for plane in range(pack_ref.shape[0]):
                here = pl.ds(plane * depth, depth)
                pack_ref[plane, 0, :, :part] = dgate_ref[0, here, :]
                pack_ref[plane, 0, :, part:] = dup_ref[0, here, :]


def put_back(number, slots_ref, pairs):
    pick = jnp.concatenate(picks(slots_ref, number), axis=0).astype(jnp.bfloat16)
    piece = 512
    for source, target, first in pairs:
        width = source.shape[2]
        for at in range(0, width, piece):
            size = min(piece, width)
            part = source[:, :, at : at + size].reshape(-1, size)
            target[:, first + at : first + at + size] = dot(pick, part, (0, 0)).astype(
                jnp.bfloat16
            )


def place_back_kernel(number, slots_ref, dx_ref, probs_ref, back_ref):
    put_back(number, slots_ref, [(dx_ref, back_ref, 0), (probs_ref, back_ref, dx_ref.shape[2])])


def place_out_kernel(number, slots_ref, y_ref, out_ref):
    put_back(number, slots_ref, [(y_ref, out_ref, 0)])


def place_out(slots, y, out):
    pairs, number, pair = slots.shape
    pltpu.emit_pipeline(
        functools.partial(place_out_kernel, number),
        grid=(pairs,),
        in_specs=[
            pl.BlockSpec((1, number, pair), lambda p: (p, 0, 0)),
            pl.BlockSpec((number, 2 * CAP, D), lambda p: (0, p, 0)),
        ],
        out_specs=[pl.BlockSpec((pair, D), lambda p: (p, 0))],
    )(slots, y, out)


def pick_shapes(number, pairs):
    bf16 = jnp.bfloat16
    size = 2 * CAP
    return [
        jax.ShapeDtypeStruct((number, pairs * size, D), bf16),
        jax.ShapeDtypeStruct((number, pairs * size, D), bf16),
        jax.ShapeDtypeStruct((number, pairs * size, 128), jnp.float32),
    ]


def pick_rows(number, experts_all, slots, x_all, g_all, router, rows, grows, gates):
    pairs, _, pair = slots.shape
    size = 2 * CAP
    tokens = pl.BlockSpec((pair, D), lambda p: (p, 0))
    picked = pl.BlockSpec((number, size, D), lambda p: (0, p, 0))
    pltpu.emit_pipeline(
        functools.partial(pick_kernel, number, experts_all),
        grid=(pairs,),
        in_specs=[
            pl.BlockSpec((1, number, pair), lambda p: (p, 0, 0)),
            tokens,
            tokens,
            pl.BlockSpec(router.shape, lambda p: (0, 0)),
        ],
        out_specs=[picked, picked, pl.BlockSpec((number, size, 128), lambda p: (0, p, 0))],
    )(slots, x_all, g_all, router, rows, grows, gates)


def expert_call(names, half, low, number, rows, grows, gates, weights, down, into=(), pack=()):
    total, depth, _ = rows.shape
    part = down.shape[1]
    size = depth
    while size > 768:
        size //= 2
    steps = depth // size
    bf16 = jnp.bfloat16
    f32 = jnp.float32

    def from_rows(width):
        return pl.BlockSpec((1, size, width), lambda e, r: (e + low, r, 0))

    def whole(*shape):
        return pl.BlockSpec((1, *shape), lambda e, r: (e, 0, 0))

    def from_whole(*shape):
        return pl.BlockSpec((1, *shape), lambda e, r: (e + low, 0, 0))

    packed = [
        pl.BlockSpec(
            (planes, 1, D // planes, 2 * part),
            lambda e, r, n=n: (0, lax.min(e, n - 1), 0, 0),
        )
        for n, planes in ([pack] if pack else [])
    ]
    keep = (D, part) if steps > 1 else (16, 128)
    return pl.pallas_call(
        functools.partial(
            expert_kernel, steps, half, len(weights), len(into), pack[0] if pack else 0
        ),
        grid=(number, steps),
        in_specs=[
            pl.BlockSpec(memory_space=pltpu.SMEM),
            from_rows(D),
            from_rows(D),
            from_rows(128),
            *[(from_whole if len(weights) == 2 else whole)(*one.shape[1:]) for one in weights],
            from_whole(part, D),
            *[pl.BlockSpec(memory_space=pl.ANY)] * len(into),
        ],
        out_specs=[
            from_rows(D),
            from_rows(D),
            from_rows(128),
            whole(D, part),
            whole(D, part),
            from_whole(part, D),
            *packed,
        ],
        out_shape=[
            jax.ShapeDtypeStruct((total, depth, D), bf16),
            jax.ShapeDtypeStruct((total, depth, D), bf16),
            jax.ShapeDtypeStruct((total, depth, 128), bf16),
            jax.ShapeDtypeStruct((number, D, part), bf16),
            jax.ShapeDtypeStruct((number, D, part), bf16),
            jax.ShapeDtypeStruct((total, part, D), f32),
            *[
                jax.ShapeDtypeStruct((planes, n, D // planes, 2 * part), bf16)
                for n, planes in ([pack] if pack else [])
            ],
        ],
        input_output_aliases={
            5 + len(weights) + i: out for i, out in zip(range(len(into)), (0, 1, 2, 5))
        },
        scratch_shapes=[pltpu.VMEM(keep, f32), pltpu.VMEM(keep, f32)],
        compiler_params=pltpu.CompilerParams(vmem_limit_bytes=BIG),
    )(names, rows, grows, gates, *weights, down, *into)


def place_back(slots, dx, probs):
    pairs, number, pair = slots.shape
    size = 2 * CAP

    def rows(one):
        return pl.BlockSpec((number, size, one.shape[2]), lambda p: (0, p, 0))

    return pl.pallas_call(
        functools.partial(place_back_kernel, number),
        grid=(pairs,),
        in_specs=[pl.BlockSpec((1, number, pair), lambda p: (p, 0, 0)), rows(dx), rows(probs)],
        out_specs=pl.BlockSpec((pair, D + 128), lambda p: (p, 0)),
        out_shape=jax.ShapeDtypeStruct((pairs * pair, D + 128), jnp.bfloat16),
        compiler_params=pltpu.CompilerParams(vmem_limit_bytes=BIG),
    )(slots, dx, probs)


def through_kernel(count, *refs):
    lefts, weight_ref, out_ref = refs[:count], refs[count], refs[count + 1]
    for i in range(count):

        @pl.when(pl.program_id(1) == i)
        def _():
            part = dot(lefts[i][...], weight_ref[0], (1, 1))
            if i:
                part = part + out_ref[...]
            out_ref[...] = part


def through(lefts, weights, first):
    count, (rows, depth) = len(lefts), lefts[0].shape
    piece = 512
    return pl.pallas_call(
        functools.partial(through_kernel, count),
        grid=(depth // piece, count),
        in_specs=[
            *[pl.BlockSpec((rows, depth), lambda c, i: (0, 0))] * count,
            pl.BlockSpec((1, piece, depth), lambda c, i: (i + first, c, 0)),
        ],
        out_specs=pl.BlockSpec((rows, piece), lambda c, i: (0, c)),
        out_shape=jax.ShapeDtypeStruct((rows, depth), jnp.float32),
        compiler_params=pltpu.CompilerParams(vmem_limit_bytes=BIG),
    )(*lefts, weights)


def project_kernel(left_ref, weight_ref, out_ref):
    out_ref[0] = dot(left_ref[...], weight_ref[0], (1, 0))


def project(left, weights, first, count):
    rows, depth = left.shape
    piece = 512
    return pl.pallas_call(
        project_kernel,
        grid=(count, depth // piece),
        in_specs=[
            pl.BlockSpec((rows, depth), lambda i, c: (0, 0)),
            pl.BlockSpec((1, depth, piece), lambda i, c: (i + first, 0, c)),
        ],
        out_specs=pl.BlockSpec((1, rows, piece), lambda i, c: (i, 0, c)),
        out_shape=jax.ShapeDtypeStruct((count, rows, depth), jnp.float32),
        compiler_params=pltpu.CompilerParams(vmem_limit_bytes=BIG),
    )(left, weights)


def outer_kernel(which, n_left, *refs):
    lefts, rights = refs[:n_left], refs[n_left : n_left + len(which)]
    piece = 512
    for left, right, out_ref in zip(which, rights, refs[n_left + len(which) :]):
        for at in range(0, out_ref.shape[1], piece):
            out_ref[:, at : at + piece] = dot(
                lefts[left][...], right[:, at : at + piece], (0, 0)
            ).astype(out_ref.dtype)


def outer(lefts, rights, which):
    rows, depth = lefts[0].shape
    piece = 256
    return pl.pallas_call(
        functools.partial(outer_kernel, which, len(lefts)),
        grid=(depth // piece,),
        in_specs=[
            *[pl.BlockSpec((rows, piece), lambda c: (0, c))] * len(lefts),
            *[pl.BlockSpec((rows, depth), lambda c: (0, 0))] * len(rights),
        ],
        out_specs=[pl.BlockSpec((piece, depth), lambda c: (c, 0))] * len(rights),
        out_shape=[jax.ShapeDtypeStruct((depth, depth), jnp.bfloat16)] * len(rights),
        compiler_params=pltpu.CompilerParams(vmem_limit_bytes=BIG),
    )(*lefts, *rights)


def widen_kernel(*refs):
    half = len(refs) // 2
    for source, target in zip(refs[:half], refs[half:]):
        target[...] = source[...].astype(jnp.float32)


def widen(spans, values):
    number, rows, columns = values[0].shape
    (low, high), (again, end) = spans

    def chosen(e):
        return (jnp.where(e < high - low, e + low, e - (high - low) + again), 0, 0)

    block = pl.BlockSpec((1, rows, columns), chosen)
    return pl.pallas_call(
        widen_kernel,
        grid=(high - low + end - again,),
        in_specs=[block] * len(values),
        out_specs=[block] * len(values),
        out_shape=[jax.ShapeDtypeStruct(one.shape, jnp.float32) for one in values],
        compiler_params=pltpu.CompilerParams(vmem_limit_bytes=BIG),
    )(*values)


def widen_pieces_kernel(low, n_pieces, offsets_ref, *refs):
    pieces, refs = refs[:n_pieces], refs[n_pieces + 2 :]
    targets, wide, sems = refs[:2], refs[2], refs[3]
    part = wide.shape[4]
    copies = []
    for k, piece in enumerate(pieces):
        columns = pl.ds(pl.multiple_of(offsets_ref[k], part), part)
        for n in range(2):
            wide[k, n] = piece[:, :, n * part : (n + 1) * part].astype(jnp.float32)
            copy = pltpu.make_async_copy(
                wide.at[k, n], targets[n].at[pl.ds(low, piece.shape[0]), :, columns], sems.at[k, n]
            )
            copy.start()
            copies.append(copy)
    for copy in copies:
        copy.wait()


def widen_pieces(offsets, low, pieces, into):
    size, rows, columns = pieces[0].shape
    anywhere = pl.BlockSpec(memory_space=pl.ANY)
    count = len(pieces)
    return pl.pallas_call(
        functools.partial(widen_pieces_kernel, low, count),
        in_specs=[
            pl.BlockSpec(memory_space=pltpu.SMEM),
            *[pl.BlockSpec(memory_space=pltpu.VMEM)] * count,
            anywhere,
            anywhere,
        ],
        out_specs=[anywhere, anywhere],
        out_shape=[jax.ShapeDtypeStruct(one.shape, one.dtype) for one in into],
        scratch_shapes=[
            pltpu.VMEM((count, 2, size, rows, columns // 2), jnp.float32),
            pltpu.SemaphoreType.DMA((count, 2)),
        ],
        input_output_aliases={1 + count: 0, 2 + count: 1},
        compiler_params=pltpu.CompilerParams(vmem_limit_bytes=BIG),
    )(offsets, *pieces, *into)


def shards(
    n_dp,
    n_expert,
    tokens,
    cotangent,
    lengths,
    routes,
    w_query,
    w_key,
    w_value,
    w_out,
    w_router,
    gain_attn,
    gain_query,
    gain_key,
    gain_mlp,
    w_gate,
    w_up,
    w_down,
):
    groups = n_dp * n_expert
    bf16 = jnp.bfloat16
    number = w_gate.shape[0]
    ff = w_gate.shape[2]
    part = ff // n_dp
    experts_all = w_router.shape[1]
    width = 128
    small = jnp.concatenate(
        [
            w_router,
            gain_attn[:, None],
            gain_query[:, None],
            gain_key[:, None],
            gain_mlp[:, None],
            jnp.zeros((w_router.shape[0], width - experts_all - 4), bf16),
        ],
        axis=1,
    )
    hits = jnp.any(
        routes[:, :, None] == jnp.arange(width, dtype=jnp.int32)[None, None, :], axis=1
    ).astype(bf16)
    count = tokens.shape[0]
    rows_each = w_query.shape[0]
    extras = jnp.concatenate([hits, jnp.pad(small, ((0, count - rows_each), (0, 0)))], axis=1)
    weights = jnp.stack([w_query, w_key, w_value, w_out])
    depth = w_gate.shape[1]
    early = number // 4
    beside = early + number // 8
    late = number - number // 4
    back_beside = number // 8
    back_third = back_beside + max(number // 4, 1)
    back_late = back_third + number // 4
    me = lax.axis_index("dp")
    cut_shape = jax.ShapeDtypeStruct((number, n_dp * depth, part), bf16)

    def row_block(size):
        return lambda ref, block: ref.at[pl.ds(pl.multiple_of(block * size, 16), size)]

    def columns_at(at):
        return pl.ds(pl.multiple_of(at * part, part), part)

    def rows_at(at):
        return pl.ds(pl.multiple_of(at * depth, depth), depth)

    def recut(low, high):
        def cuts(ins, outs):
            def pair(n):
                chosen = pl.ds(low, high - low)
                return (
                    lambda to: ins[n].at[chosen, :, columns_at(to)],
                    lambda at: outs[n].at[chosen, rows_at(at)],
                )

            return [pair(0), pair(1)]

        return cuts

    to_plane, from_plane = partners(me, n_dp)

    def permuted(pieces, chained=False):
        got = []
        for k, piece in enumerate(pieces, 1):
            if chained and got:
                piece, last = lax.optimization_barrier((piece, got.pop()))
                got.append(last)
            paths = [(i, partners(i, n_dp)[0](k)) for i in range(n_dp)]
            got.append(lax.ppermute(piece, "dp", paths))
        return got

    def cut_pieces(low, high, first_k, ins, outs):
        to, unused = partners(lax.axis_index("dp"), n_dp)
        pairs = []
        for k, piece in enumerate(outs, first_k):
            for n in range(2):
                source = ins[n].at[pl.ds(low, high - low), :, columns_at(to(k))]
                pairs.append((source, piece.at[:, :, pl.ds(n * part, part)]))
        return pairs

    def piece_shapes(size, first_k):
        shape = jax.ShapeDtypeStruct((size, depth, 2 * part), bf16)
        return [shape] * (n_dp - first_k if size else 0)

    def stages(*sizes):
        return [(size, depth, part) for size in sizes]

    soon_shapes = piece_shapes(beside - early, 1)
    late_shapes = piece_shapes(number - late, 0)
    n_soon = len(soon_shapes)

    weights_all, extras_all, gate_early, up_early, *pieces = gather_call(
        n_dp,
        n_expert,
        [weights, extras],
        [
            jax.ShapeDtypeStruct((4, groups * rows_each, D), bf16),
            jax.ShapeDtypeStruct((groups * count, 2 * width), bf16),
        ],
        [
            lambda ref, block: ref.at[
                :, pl.ds(pl.multiple_of(block * rows_each, 16), rows_each)
            ],
            row_block(count),
        ],
        [w_gate, w_up],
        [cut_shape, cut_shape, *soon_shapes, *late_shapes],
        recut(0, early),
        {},
        0,
        stages(
            *[early] * 2,
            *[beside - early] * (2 * n_soon),
            *[number - late] * (2 * n_dp),
        ),
        lambda ins, outs: cut_pieces(early, beside, 1, ins, outs[2 : 2 + n_soon])
        + cut_pieces(late, number, 0, ins, outs[2 + n_soon :]),
    )
    soon_pieces, late_pieces = pieces[:n_soon], pieces[n_soon:]
    small_all = (
        extras_all[:, width:].reshape(groups, count, width)[:, :rows_each].reshape(-1, width)
    )
    hits_all = extras_all[:, :experts_all]
    router_weight = small_all[:, :experts_all]
    gains = small_all[:, experts_all : experts_all + 4].astype(jnp.float32)
    attn_gain, query_gain, key_gain, mlp_gain = (gains[:, i] for i in range(4))
    inputs = tokens.astype(jnp.float32)
    segment, position, places = layout(lengths[0], count)
    half = HD // 2
    freq = 10000.0 ** (-2.0 * jnp.arange(half, dtype=jnp.float32) / HD)
    angle = position.astype(jnp.float32)[:, None] * freq[None, :]
    cosine = jnp.cos(angle)[:, None, :]
    sine = jnp.sin(angle)[:, None, :]
    scale = HD ** (-0.5)
    normed, attn_inverse = rms_forward(inputs, attn_gain)
    normed_low = normed.astype(bf16)
    query_raw, key_raw, value_raw = project(normed_low, weights_all, 0, 3)
    value_low = value_raw.astype(bf16)
    query_normed, query_inverse = rms_forward(query_raw, query_gain)
    key_normed, key_inverse = rms_forward(key_raw, key_gain)
    query_low = rotate(query_normed, cosine, sine).astype(bf16).reshape(count, HEADS, HD)
    key_low = rotate(key_normed, cosine, sine).astype(bf16).reshape(count, HEADS, HD)
    value_heads = value_low.reshape(count, HEADS, HD)
    allowed = (segment[:, None] == segment[None, :]) & (places[None, :] <= places[:, None])
    scores = product(query_low, key_low, "qhd,khd->hqk") * scale
    scores = jnp.where(allowed[None], scores, -1e30)
    probs = jax.nn.softmax(scores, axis=-1)
    probs_low = probs.astype(bf16)
    attended_low = product(probs_low, value_heads, "hqk,khd->qhd").reshape(count, D).astype(bf16)
    middle = inputs + project(attended_low, weights_all, 3, 1)[0]
    mlp_normed, mlp_inverse = rms_forward(middle, mlp_gain)
    mlp_low = mlp_normed.astype(bf16)
    router = jax.nn.softmax(product(mlp_low, router_weight, "td,de->te"), axis=-1)

    first = lax.axis_index("expert") * number
    hit = lax.dynamic_slice_in_dim(hits_all, first, number, 1).reshape(groups, count, number)
    before = jnp.tril(jnp.ones((count, count), bf16), -1)
    slot = product(before, hit, "ts,bse->bet").astype(jnp.int32)
    slot = jnp.where(jnp.transpose(hit, (0, 2, 1)) > 0, slot, -1)
    slot = slot.reshape(groups // 2, 2, number, count)
    shift = jnp.array([0, CAP], jnp.int32)[None, :, None, None]
    slots = jnp.transpose(jnp.where(slot < 0, -1, slot + shift), (0, 2, 1, 3))
    slots = slots.reshape(groups // 2, number, 2 * count)
    router_own = jnp.pad(
        jnp.roll(router_weight, -first, axis=1), ((0, 0), (0, width - experts_all))
    )
    if n_soon:
        mlp_low, *soon_pieces = lax.optimization_barrier((mlp_low, *permuted(soon_pieces)))

    def put_weights(ins, outs):
        chosen = pl.ds(early, beside - early)
        unused, heard = partners(lax.axis_index("dp"), n_dp)
        pairs = []
        if beside > early:
            own = lax.axis_index("dp")
            for n in range(2):
                source = ins[n].at[chosen, :, columns_at(own)]
                pairs.append((source, outs[n].at[chosen, rows_at(own)]))
        for k, piece in enumerate(ins[6:], 1):
            for n in range(2):
                columns = piece.at[:, :, pl.ds(n * part, part)]
                pairs.append((columns, outs[n].at[chosen, rows_at(heard(k))]))
        return pairs

    def pick_all(items, ins, outs):
        pick_rows(number, experts_all, ins[4], *items, ins[5], *outs[2:])

    unused, unused, gate_cut, up_cut, rows, grows, gates = gather_call(
        n_dp,
        n_expert,
        [mlp_low, cotangent],
        [jax.ShapeDtypeStruct((groups * count, D), bf16)] * 2,
        [row_block(count)] * 2,
        [w_gate, w_up, gate_early, up_early, slots, router_own, *soon_pieces],
        [cut_shape, cut_shape, *pick_shapes(number, groups // 2)],
        recut(beside, late),
        {4: 2, 5: 3},
        1,
        stages(*[late - beside] * 2, *[beside - early] * (2 * n_dp if n_soon else 0)),
        put_weights,
        pick_all,
    )
    *late_pieces, rows = lax.optimization_barrier((*late_pieces, rows))
    late_pieces = [late_pieces[0], *permuted(late_pieces[1:])]
    packing = back_beside > 0 and depth == 512
    *outs, gate_soon, up_soon, down_soon = expert_call(
        first[None],
        experts_all,
        0,
        late,
        rows,
        grows,
        gates,
        [gate_cut, up_cut],
        w_down,
        pack=(back_beside, n_dp) if packing else (),
    )
    if packing:
        *outs, gate_soon, up_soon, down_soon, packed = [*outs, gate_soon, up_soon, down_soon]
    offsets = [from_plane(k) * depth for k in range(n_dp)]
    weighted, grad_rows, grad_gates, gate_rest, up_rest, grad_down_part = expert_call(
        jnp.stack([first + late, *offsets]),
        experts_all,
        late,
        number - late,
        rows,
        grows,
        gates,
        late_pieces,
        w_down,
        [*outs, down_soon],
    )
    part_back = place_back(slots, grad_rows, grad_gates)

    def ways(low, high, at, ins, outs):
        def pair(e, n):
            return (
                lambda to: ins[n].at[pl.ds(e, 1), rows_at(to)],
                lambda here: outs[n].at[pl.ds(e + at, 1), :, columns_at(here)],
            )

        return [pair(e, n) for e in range(low, high) for n in range(2)]

    def cut_grads(low, high, ins, outs):
        to, unused = partners(lax.axis_index("dp"), n_dp)
        pairs = []
        for k, piece in enumerate(outs):
            for n in range(2):
                source = ins[n].at[pl.ds(low, high - low), rows_at(to(k))]
                pairs.append((source, piece.at[:, :, pl.ds(n * part, part)]))
        return pairs

    pieces = []
    if back_beside:
        for k in range(n_dp):
            if packing:
                piece = lax.dynamic_index_in_dim(packed, to_plane(k), 0, False)
            else:
                piece = jnp.concatenate(
                    [
                        lax.dynamic_slice_in_dim(
                            one[:back_beside], to_plane(k) * depth, depth, 1
                        )
                        for one in (gate_soon, up_soon)
                    ],
                    axis=2,
                )
            pieces.append(piece)
        ahead = lax.optimization_barrier((*pieces[1:], *late_pieces[1:]))
        pieces = [pieces[0], *permuted(ahead[: n_dp - 1])]
        part_back, *pieces = lax.optimization_barrier((part_back, *pieces))
    way_shapes = [jax.ShapeDtypeStruct((number, depth, ff), bf16)] * 2
    piece_shape = jax.ShapeDtypeStruct((back_late - back_third, depth, 2 * part), bf16)
    (back,), (gate_third, up_third, part_out, *later_pieces) = scatter_all(
        n_dp,
        n_expert,
        [part_back.reshape(n_dp, n_expert, count, D + width)],
        [4],
        [gate_soon, up_soon, slots, weighted],
        [
            *way_shapes,
            jax.ShapeDtypeStruct((groups * count, D), bf16),
            *[piece_shape] * n_dp,
        ],
        lambda ins, outs: ways(back_beside, back_third, 0, ins, outs),
        8,
        (),
        stages(
            *[1] * (2 * (back_third - back_beside)),
            *[back_late - back_third] * (2 * n_dp),
        ),
        lambda ins, outs: cut_grads(back_third, back_late, ins, outs[3:]),
        lambda ins, outs: place_out(ins[2], ins[3], outs[2]),
    )
    later_pieces = [later_pieces[0], *permuted(later_pieces[1:])]

    def attention_back(back):
        grad_final = cotangent.astype(jnp.float32)
        grad_mlp = back[:, :D]
        grad_router_probs = back[:, D : D + experts_all] + back[:, D + experts_all :]
        grad_logits = router * (
            grad_router_probs - jnp.sum(router * grad_router_probs, axis=1, keepdims=True)
        )
        grad_logits_low = grad_logits.astype(bf16)
        grad_router_full = product(
            mlp_low, jnp.pad(grad_logits_low, ((0, 0), (0, width - experts_all))), "td,te->de"
        )
        grad_mlp = grad_mlp + product(grad_logits_low, router_weight, "te,de->td")
        grad_middle_part, grad_mlp_gain = rms_backward(middle, mlp_inverse, mlp_gain, grad_mlp)
        grad_middle = grad_final + grad_middle_part
        grad_branch_low = grad_middle.astype(bf16)
        grad_attended = (
            through([grad_branch_low], weights_all, 3).astype(bf16).reshape(count, HEADS, HD)
        )
        grad_weights = product(grad_attended, value_heads, "qhd,khd->hqk")
        grad_scores = probs * (grad_weights - jnp.sum(probs * grad_weights, axis=-1, keepdims=True))
        grad_scores_low = grad_scores.astype(bf16)
        grad_query_turn = product(grad_scores_low, key_low, "hqk,khd->qhd").reshape(count, D) * scale
        grad_key_turn = product(grad_scores_low, query_low, "hqk,qhd->khd").reshape(count, D) * scale
        grad_value_low = (
            product(probs_low, grad_attended, "hqk,qhd->khd").reshape(count, D).astype(bf16)
        )
        grad_query_raw, grad_query_gain = rms_backward(
            query_raw, query_inverse, query_gain, rotate(grad_query_turn, cosine, -sine)
        )
        grad_key_raw, grad_key_gain = rms_backward(
            key_raw, key_inverse, key_gain, rotate(grad_key_turn, cosine, -sine)
        )
        grad_query_low = grad_query_raw.astype(bf16)
        grad_key_low = grad_key_raw.astype(bf16)
        full_grads = outer(
            [attended_low, normed_low],
            [grad_branch_low, grad_value_low, grad_key_low, grad_query_low],
            (0, 1, 1, 1),
        )
        grad_normed = through([grad_query_low, grad_key_low, grad_value_low], weights_all, 0)
        grad_inputs_part, grad_attn_gain = rms_backward(inputs, attn_inverse, attn_gain, grad_normed)
        grad_inputs = grad_middle + grad_inputs_part

        gain_grads = jnp.stack([grad_attn_gain, grad_query_gain, grad_key_gain, grad_mlp_gain])
        gain_grads = jnp.transpose(gain_grads.reshape(4, groups, rows_each), (1, 0, 2))
        gain_grads = jnp.pad(gain_grads, ((0, 0), (0, 12), (0, width - rows_each)))
        return (
            grad_inputs,
            *full_grads,
            grad_router_full.astype(bf16),
            gain_grads.astype(bf16).reshape(groups * 16, width),
        )

    def unreached(back):
        shapes = [(count, D)] + [(D, D)] * 4 + [(D, width), (groups * 16, width)]
        kinds = [jnp.float32] + [bf16] * 6
        return tuple(jnp.zeros(shape, kind) for shape, kind in zip(shapes, kinds))

    grad_inputs, *weight_grads = lax.cond(lengths[0, 0] > 0, attention_back, unreached, back)

    def blocks_of(value):
        return value.reshape(n_dp, n_expert, -1, value.shape[1])

    sums, (gate_back, up_back) = scatter_all(
        n_dp,
        n_expert,
        [part_out.reshape(n_dp, n_expert, count, D)]
        + [blocks_of(value) for value in weight_grads],
        [2, 1, 1, 1, 2 if rows_each > 16 else 1, 1, 1],
        [gate_third, up_third, gate_soon, up_soon, gate_rest, up_rest],
        way_shapes,
        lambda ins, outs: ways(back_late, late, 0, ins[2:4], outs)
        + ways(0, number - late, late, ins[4:6], outs),
        16,
        ((0, 0), (1, 1)),
        [],
    )
    summed, grad_out_part, grad_value_part, grad_key_part, grad_query_part, router_part, small = sums
    output = (middle + summed).astype(bf16)
    grad_router_part = router_part[:, :experts_all]
    gain_parts = [small[i, :rows_each] for i in range(4)]
    widened = widen([(back_beside, back_third), (back_late, number)], [gate_back, up_back])
    offsets = jnp.stack([from_plane(k) * part for k in range(n_dp)])
    for low, high, others in (
        (0, back_beside, pieces),
        (back_third, back_late, later_pieces),
    ):
        if high > low:
            widened = widen_pieces(offsets, low, others, widened)
    grad_gate_part, grad_up_part = widened
    return (
        output,
        grad_inputs,
        grad_query_part,
        grad_key_part,
        grad_value_part,
        grad_out_part,
        grad_router_part,
        gain_parts[0],
        gain_parts[1],
        gain_parts[2],
        gain_parts[3],
        grad_gate_part,
        grad_up_part,
        grad_down_part,
    )


def solution(mesh):
    return jax.shard_map(
        functools.partial(shards, mesh.shape["dp"], mesh.shape["expert"]),
        mesh=mesh,
        in_specs=(
            P(("dp", "expert"), None),
            P(("dp", "expert"), None),
            P(("dp", "expert"), None),
            P(("dp", "expert"), None),
            P(("dp", "expert"), None),
            P(("dp", "expert"), None),
            P(("dp", "expert"), None),
            P(("dp", "expert"), None),
            P(("dp", "expert"), None),
            P(("dp", "expert")),
            P(("dp", "expert")),
            P(("dp", "expert")),
            P(("dp", "expert")),
            P("expert", "dp", None),
            P("expert", "dp", None),
            P("expert", "dp", None),
        ),
        out_specs=(
            P(("dp", "expert"), None),
            P(("dp", "expert"), None),
            P(("dp", "expert"), None),
            P(("dp", "expert"), None),
            P(("dp", "expert"), None),
            P(("dp", "expert"), None),
            P(("dp", "expert"), None),
            P(("dp", "expert")),
            P(("dp", "expert")),
            P(("dp", "expert")),
            P(("dp", "expert")),
            P("expert", "dp", None),
            P("expert", "dp", None),
            P("expert", "dp", None),
        ),
        check_vma=False,
    )
```

```python
import functools

import jax
import jax.numpy as jnp
from jax import lax
from jax.experimental import pallas as pl
from jax.experimental.pallas import tpu as pltpu
from jax.sharding import PartitionSpec as P

D = 2048
HEADS = 16
HD = 128
TOPK = 8
CAP = 24


eps = 1e-05


def product(left, right, form):
    return jnp.einsum(form, left, right, preferred_element_type=jnp.float32)


def rms_forward(values, gain):
    inverse = lax.rsqrt(jnp.mean(values * values, axis=-1, keepdims=True) + eps)
    return (values * inverse * gain, inverse)


def rms_backward(values, inverse, gain, grad):
    scaled = grad * gain
    inner = jnp.mean(scaled * values, axis=-1, keepdims=True)
    grad_values = inverse * scaled - values * (inverse * inverse * inverse) * inner
    grad_gain = jnp.sum(grad * values * inverse, axis=0)
    return (grad_values, grad_gain)


def layout(lengths_row, count):
    places = jnp.arange(count, dtype=jnp.int32)
    ends = jnp.cumsum(lengths_row, dtype=jnp.int32)
    passed = (places[:, None] >= ends[None, :]).astype(jnp.int32)
    segment = jnp.sum(passed, axis=1, dtype=jnp.int32)
    start = jnp.sum(passed * lengths_row[None, :], axis=1, dtype=jnp.int32)
    return (segment, places - start, places)


def rotate(values, cosine, sine):
    count = values.shape[0]
    heads = values.reshape(count, HEADS, HD)
    half = HD // 2
    first = heads[..., :half]
    second = heads[..., half:]
    turned = jnp.concatenate(
        [first * cosine - second * sine, second * cosine + first * sine], axis=-1
    )
    return turned.reshape(count, D)


MESH = pl.DeviceIdType.MESH
BIG = 60 * 1024 * 1024


def place_of():
    z = lax.axis_index("dp")
    j = lax.axis_index("expert")
    return z, j, j // 2, j % 2


def other_chips(chip, chips):
    if chips == 4:
        square = [chip, chip + 1 - 2 * (chip % 2), chip + 2 - 4 * (chip // 2), 3 - chip]
        return lambda k: square[k], lambda k: square[k]
    return lambda k: (chip + k) % chips, lambda k: (chip + chips - k) % chips


def partners(z, n_dp):
    if n_dp == 4:
        pairs = [z, 3 - z, (z + 2) % 4, z + 1 - 2 * (z % 2)]
        return lambda k: pairs[k], lambda k: pairs[k]
    return lambda k: (z + k) % n_dp, lambda k: (z + n_dp - k) % n_dp


def greet(n_dp, n_expert):
    z, j, chip, core = place_of()
    chips = n_expert // 2
    barrier = pltpu.get_barrier_semaphore()
    for k in range(1, n_dp):
        pl.semaphore_signal(
            barrier, inc=1, device_id=((z + k) % n_dp, j), device_id_type=MESH
        )
    for k in range(1, chips):
        other = ((chip + k) % chips) * 2 + core
        pl.semaphore_signal(barrier, inc=1, device_id=(z, other), device_id_type=MESH)
    pl.semaphore_signal(
        barrier, inc=1, device_id=(z, chip * 2 + 1 - core), device_id_type=MESH
    )
    pl.semaphore_wait(barrier, n_dp - 1 + chips - 1 + 1)


def remote(source, target, send, receive, device):
    return pltpu.make_async_remote_copy(
        src_ref=source,
        dst_ref=target,
        send_sem=send,
        recv_sem=receive,
        device_id=device,
        device_id_type=MESH,
    )


def exchange(n_dp, pairs, send, receive):
    z, j, chip, core = place_of()
    to_plane, unused = partners(z, n_dp)
    copies = []
    for i, (source, target) in enumerate(pairs):
        for k in range(1, n_dp):
            to = to_plane(k)
            copies.append(
                remote(source(to), target(z), send.at[i, k], receive.at[i, k], (to, j))
            )
    return copies


def moves(pairs, stages, local):
    if not stages:
        copies = [
            pltpu.make_async_copy(source, target, local.at[i, 0])
            for i, (source, target) in enumerate(pairs)
        ]
        for copy in copies:
            copy.start()
        return [], copies
    bring = [
        pltpu.make_async_copy(source, stages[i], local.at[i, 0])
        for i, (source, target) in enumerate(pairs)
    ]
    put = [
        pltpu.make_async_copy(stages[i], target, local.at[i, 1])
        for i, (source, target) in enumerate(pairs)
    ]
    return bring, put


def nothing(ins, outs):
    return []


def gather_kernel(
    n_dp, n_expert, n_items, places, cuts, puts, finish, n_cut, n_out, n_stages, *refs
):
    z, j, chip, core = place_of()
    chips = n_expert // 2
    square = chips == 4
    to_chip, from_chip = other_chips(chip, chips)
    sources = refs[:n_items]
    cut_in = refs[n_items : n_items + n_cut]
    at = n_items + n_cut
    targets = refs[at : at + n_items]
    cut_out = refs[at + n_items : at + n_items + n_out]
    (
        send_c,
        recv_c,
        send_b,
        recv_b,
        send_a,
        recv_a,
        local,
        send_x,
        recv_x,
        local_y,
        *stages,
    ) = refs[at + n_items + n_out :]
    greet(n_dp, n_expert)
    mate = (z, chip * 2 + 1 - core)
    near = (1, 2) if square else tuple(range(1, chips))

    def slot(i, plane, column):
        return places[i](targets[i], plane * n_expert + column)

    def pass_on(i, plane, source, column, k, chip_to):
        return remote(
            source,
            slot(i, plane, column),
            send_b.at[i, plane, k],
            recv_b.at[i, plane, k],
            (z, chip_to * 2 + core),
        )

    def hand(i, plane, source):
        for k in near:
            pass_on(i, plane, source, j, k, to_chip(k)).start()
        remote(
            source, slot(i, plane, j), send_a.at[i, plane, 0], recv_a.at[i, plane, 0], mate
        ).start()

    def along(i, plane, source, way, step):
        return remote(
            source, slot(i, plane, j), send_c.at[i, way, plane], recv_c.at[i, plane], (z + step, j)
        )

    def at_distance(d, body):
        if d == 0:
            body(z, 0)
            return

        @pl.when(z >= d)
        def _():
            body(z - d, 0)

        @pl.when(z + d < n_dp)
        def _():
            body(z + d, 1)

    for i in range(n_items):

        @pl.when(z < n_dp - 1)
        def _():
            along(i, z, sources[i], 0, 1).start()

        @pl.when(z > 0)
        def _():
            along(i, z, sources[i], 1, -1).start()

        hand(i, z, sources[i])
        pltpu.make_async_copy(sources[i], slot(i, z, j), local.at[i]).start()

    def relay(plane, way):
        step = -1 if way else 1
        for i in range(n_items):
            block = slot(i, plane, j)
            along(i, plane, block, way, step).wait_recv()

            @pl.when(z > 0 if way else z < n_dp - 1)
            def _():
                along(i, plane, block, way, step).start()

            hand(i, plane, block)

    for d in range(1, n_dp):
        at_distance(d, relay)
    pairs = cuts(cut_in, cut_out)
    copies = exchange(n_dp, pairs, send_x, recv_x)
    for copy in copies:
        copy.start()
    own = [(source(z), target(z)) for source, target in pairs]
    bring, put = moves(own + puts(cut_in, cut_out), stages, local_y)
    for copy in bring:
        copy.start()
    for one, other in zip(bring, put):
        one.wait()
        other.start()

    def arrive(i, plane, k):
        column = from_chip(k) * 2 + core
        block = slot(i, plane, column)
        pass_on(i, plane, block, column, k, chip).wait_recv()
        remote(block, block, send_a.at[i, plane, k], recv_a.at[i, plane, k], mate).start()
        return block, column

    def arrived(plane, way):
        for i in range(n_items):
            for k in near:
                block, column = arrive(i, plane, k)
                if square:

                    @pl.when(plane % 2 == k - 1)
                    def _():
                        pass_on(i, plane, block, column, 3, to_chip(3 - k)).start()

    def crossed(plane, way):
        for i in range(n_items):
            arrive(i, plane, 3)

    for d in range(n_dp):
        at_distance(d, arrived)
    if square:
        for d in range(n_dp):
            at_distance(d, crossed)

    for i in range(n_items):
        for plane in range(n_dp):
            for k in range(chips):
                column = (from_chip(k) if k else chip) * 2 + 1 - core
                block = slot(i, plane, column)
                remote(
                    block, block, send_a.at[i, plane, k], recv_a.at[i, plane, k], mate
                ).wait_recv()
        pltpu.make_async_copy(sources[i], slot(i, z, j), local.at[i]).wait()
    finish(targets, cut_in, cut_out)
    for i in range(n_items):
        for plane in range(n_dp):
            block = slot(i, plane, j)
            for k in range(1, chips):
                pass_on(i, plane, block, j, k, chip).wait_send()
            for k in range(chips):
                remote(
                    block, block, send_a.at[i, plane, k], recv_a.at[i, plane, k], mate
                ).wait_send()

            @pl.when((z < n_dp - 1) & (z >= plane))
            def _():
                along(i, plane, block, 0, 1).wait_send()

            @pl.when((z > 0) & (z <= plane))
            def _():
                along(i, plane, block, 1, -1).wait_send()

    for copy in copies + put:
        copy.wait()


def gather_call(
    n_dp,
    n_expert,
    items,
    shapes,
    places,
    cut_in,
    cut_shapes,
    cuts,
    aliases,
    number,
    stages,
    puts=nothing,
    finish=lambda items, ins, outs: None,
):
    chips = n_expert // 2
    n, m = len(items), len(cut_shapes)
    dma = pltpu.SemaphoreType.DMA
    anywhere = pl.BlockSpec(memory_space=pl.ANY)
    return pl.pallas_call(
        functools.partial(
            gather_kernel,
            n_dp,
            n_expert,
            n,
            places,
            cuts,
            puts,
            finish,
            len(cut_in),
            m,
            len(stages),
        ),
        out_shape=[*shapes, *cut_shapes],
        in_specs=[anywhere] * (n + len(cut_in)),
        out_specs=[anywhere] * (n + m),
        scratch_shapes=[
            dma((n, 2, n_dp)),
            dma((n, n_dp)),
            dma((n, n_dp, chips)),
            dma((n, n_dp, chips)),
            dma((n, n_dp, chips)),
            dma((n, n_dp, chips)),
            dma((n,)),
            dma((4, n_dp)),
            dma((4, n_dp)),
            dma((max(len(stages), 4), 2)),
            *[pltpu.VMEM(stage, jnp.bfloat16) for stage in stages],
        ],
        input_output_aliases=aliases,
        compiler_params=pltpu.CompilerParams(
            collective_id=number, has_side_effects=True, vmem_limit_bytes=BIG
        ),
    )(*items, *cut_in)


def scatter_kernel(
    n_dp, n_expert, n_arrays, items, n_cut, n_out, cuts, puts, middle, rings, n_rings, *refs
):
    n_items = len(items)
    z, j, chip, core = place_of()
    chips = n_expert // 2
    square = chips == 4
    to_chip, from_chip = other_chips(chip, chips)
    refs = list(refs)

    def take(count):
        taken = refs[:count]
        del refs[:count]
        return taken

    sources, cut_in, targets, cut_out = take(n_arrays), take(n_cut), take(n_arrays), take(n_out)
    ring, got_a, got_b, got_c = take(n_rings), take(n_items), take(n_items), take(n_items)
    transit = take(n_items)
    (
        send_a,
        recv_a,
        send_b,
        recv_b,
        send_c,
        recv_c,
        send_t,
        recv_t,
        local,
        send_x,
        recv_x,
        local_y,
        *stages,
    ) = refs
    greet(n_dp, n_expert)
    mate = (z, chip * 2 + 1 - core)
    order = [3, 1, 2, 0] if square else [*range(1, chips), 0]
    half = n_dp // 2
    low, high = pl.ds(0, half), pl.ds(half, n_dp - half)

    def chip_of(k):
        return to_chip(k) if k else chip

    def source(i, column):
        array, first, rows = items[i]
        return sources[array].at[:, column, pl.ds(first, rows)]

    def to_mate(i, k):
        return remote(
            source(i, chip_of(k) * 2 + 1 - core),
            got_a[i].at[k],
            send_a.at[i, k],
            recv_a.at[i, k],
            mate,
        )

    turn = [0] * n_rings
    loads = []
    for i in range(n_items):
        for k in order:
            loads.append((i, k, turn[rings[i]] % 2))
            turn[rings[i]] += 1

    def load(i, k, at):
        return pltpu.make_async_copy(
            source(i, chip_of(k) * 2 + core), ring[rings[i]].at[at], local.at[rings[i], at]
        )

    def send_near(i, k, part, number):
        return remote(
            got_a[i].at[k, part],
            got_b[i].at[k - 1, part],
            send_b.at[i, number],
            recv_b.at[i, number],
            (z, to_chip(k) * 2 + core),
        )

    def send_over(i, k, part):
        return remote(
            got_a[i].at[3, part],
            transit[i].at[k - 1],
            send_t.at[i, k],
            recv_t.at[i, k],
            (z, to_chip(k) * 2 + core),
        )

    def send_far(i, k):
        return remote(
            got_a[i].at[k],
            got_b[i].at[k - 1],
            send_b.at[i, k],
            recv_b.at[i, k],
            (z, to_chip(k) * 2 + core),
        )

    def along(i, plane, way):
        slot = n_dp - (z - 1) + plane if way else plane - (z + 1)
        return remote(
            got_a[i].at[0, plane],
            got_c[i].at[slot],
            send_c.at[i, plane],
            recv_c.at[i, slot],
            (z - 1 if way else z + 1, j),
        )

    def from_along(i, slot):
        return remote(
            got_c[i].at[slot], got_c[i].at[slot], send_c.at[i, 0], recv_c.at[i, slot], mate
        )

    f32 = jnp.float32

    def add(i, planes, target, terms):
        rows = got_a[i].shape[2]
        per = rows // 16

        def step(n, unused):
            plane = n // per
            at = pl.ds(pl.multiple_of((n % per) * 16, 16), 16)
            total = terms[0](plane, at).astype(f32)
            for term in terms[1:]:
                total = total + term(plane, at).astype(f32)
            target(plane, at, total)
            return unused

        lax.fori_loop(0, planes * per, step, 0)

    def grow(i, k, first, planes, term):
        def target(plane, at, total):
            got_a[i][k, plane + first, at] = total.astype(got_a[i].dtype)

        add(i, planes, target, [lambda plane, at: got_a[i][k, plane + first, at], term])

    for i in range(n_items):
        for k in order:
            to_mate(i, k).start()
    started = 0
    ahead = [0] * n_rings
    for i, k, at in loads:
        if ahead[rings[i]] < 2:
            load(i, k, at).start()
            ahead[rings[i]] += 1
    pairs = cuts(cut_in, cut_out)
    copies = exchange(n_dp, pairs, send_x, recv_x)
    own = [(source(z), target(z)) for source, target in pairs]
    bring, put = moves(own + puts(cut_in, cut_out), stages, local_y)
    for copy in bring:
        copy.start()

    def over_cores(i):
        for n, (item, k, at) in enumerate(loads):
            if item != i:
                continue
            load(i, k, at).wait()
            to_mate(i, k).wait_recv()
            grow(i, k, 0, n_dp, lambda plane, rows: ring[rings[i]][at, plane, rows])
            later = [one for one in loads[n + 1 :] if rings[one[0]] == rings[i]]
            if len(later) >= 2:
                load(*later[1]).start()
            if not k:
                continue
            if not square:
                send_far(i, k).start()
            elif k == 3:
                send_over(i, 1, low).start()
                send_over(i, 2, high).start()
            elif k == 1:
                send_near(i, 1, low, 0).start()
            else:
                send_near(i, 2, high, 1).start()

    def pass_over(i):
        if not square:
            return
        send_over(i, 2, high).wait_recv()
        grow(i, 1, half, n_dp - half, lambda plane, rows: transit[i][1, plane, rows])
        send_near(i, 1, high, 2).start()
        send_over(i, 1, low).wait_recv()
        grow(i, 2, 0, half, lambda plane, rows: transit[i][0, plane, rows])
        send_near(i, 2, low, 3).start()

    def over_chips(i):
        if square:
            send_near(i, 1, low, 0).wait_recv()
            send_near(i, 2, high, 1).wait_recv()
            send_near(i, 1, high, 2).wait_recv()
            send_near(i, 2, low, 3).wait_recv()
        else:
            for k in range(1, chips):
                send_far(i, k).wait_recv()
        heard = 2 if square else chips - 1

        def target(plane, at, total):
            got_a[i][0, plane, at] = total.astype(got_a[i].dtype)

        terms = [lambda plane, at: got_a[i][0, plane, at]]
        for other in range(heard):
            terms.append(lambda plane, at, other=other: got_b[i][other, plane, at])
        add(i, n_dp, target, terms)
        for d in range(n_dp - 1, 0, -1):
            for way in (0, 1):
                plane = z - d if way else z + d

                @pl.when(z == (n_dp - 1 if way else 0))
                def _():
                    along(i, plane, way).start()

    def over_planes(i):
        for d in range(n_dp - 2, 0, -1):
            for way in (0, 1):
                plane = z - d if way else z + d
                slot = n_dp - d if way else d

                @pl.when((plane >= 0) & (z < n_dp - 1) if way else (plane < n_dp) & (z > 0))
                def _():
                    from_along(i, slot).wait_recv()
                    grow(i, 0, plane, 1, lambda unused, at: got_c[i][slot, at])
                    along(i, plane, way).start()

    def finish(i):
        array, first, rows = items[i]

        def here(at):
            return pl.ds(pl.multiple_of(first + at.start, 16), 16)

        def own(unused, at, total):
            targets[array][here(at)] = total

        add(i, 1, own, [lambda unused, at: got_a[i][0, z, at]])
        for slot, arrives in ((0, z > 0), (n_dp, z < n_dp - 1)):

            @pl.when(arrives)
            def _():
                from_along(i, slot).wait_recv()
                add(
                    i,
                    1,
                    own,
                    [
                        lambda unused, at: targets[array][here(at)],
                        lambda unused, at: got_c[i][slot, at],
                    ],
                )

    steps = ((0, over_cores), (1, pass_over), (2, over_chips), (3, over_planes), (4, finish))
    if n_items >= 6:
        quotas = [-(-len(copies) * part // 9) for part in (2, 2, 2, 1, 1, 1)]
    else:
        quotas = [-(-len(copies) // n_items)] * n_items
    quotas += [0] * (n_items + len(steps) - len(quotas))
    for n in range(n_items + len(steps) - 1):
        for copy in copies[sum(quotas[:n]) : sum(quotas[: n + 1])]:
            copy.start()
        for late, step in steps:
            if 0 <= n - late < n_items:
                step(n - late)
        if n == min(1, n_items - 1):
            for one, other in zip(bring, put):
                one.wait()
                other.start()
            middle(cut_in, cut_out)
    for i in range(n_items):
        for k in range(chips):
            to_mate(i, k).wait_send()
        if square:
            for k, part in ((1, low), (2, high)):
                send_over(i, k, part).wait_send()
            for k, part, number in ((1, low, 0), (2, high, 1), (1, high, 2), (2, low, 3)):
                send_near(i, k, part, number).wait_send()
        else:
            for k in range(1, chips):
                send_far(i, k).wait_send()
        for plane in range(n_dp):

            @pl.when(z != plane)
            def _():
                remote(
                    got_a[i].at[0, plane],
                    got_c[i].at[0],
                    send_c.at[i, plane],
                    recv_c.at[i, 0],
                    mate,
                ).wait_send()

    for copy in copies + put:
        copy.wait()


def scatter_call(
    n_dp,
    n_expert,
    arrays,
    splits,
    cut_in,
    cut_shapes,
    cuts,
    number,
    aliases,
    stages,
    puts=nothing,
    middle=nothing,
):
    chips = n_expert // 2
    square = chips == 4
    items = []
    for array, (one, split) in enumerate(zip(arrays, splits)):
        rows = one.shape[2] // split
        items += [(array, first, rows) for first in range(0, one.shape[2], rows)]
    n, m = len(items), len(cut_shapes)
    count = len(arrays)
    dma = pltpu.SemaphoreType.DMA
    anywhere = pl.BlockSpec(memory_space=pl.ANY)
    blocks = [(rows, arrays[array].shape[3]) for array, unused, rows in items]
    kinds = sorted(set(blocks))
    rings = [kinds.index(block) for block in blocks]
    bf16 = jnp.bfloat16
    heard = 2 if square else chips - 1
    return pl.pallas_call(
        functools.partial(
            scatter_kernel,
            n_dp,
            n_expert,
            count,
            items,
            len(cut_in),
            m,
            cuts,
            puts,
            middle,
            rings,
            len(kinds),
        ),
        out_shape=[
            *[jax.ShapeDtypeStruct(one.shape[2:], jnp.float32) for one in arrays],
            *cut_shapes,
        ],
        in_specs=[anywhere] * (count + len(cut_in)),
        out_specs=[pl.BlockSpec(memory_space=pltpu.VMEM)] * count + [anywhere] * m,
        scratch_shapes=[
            *[pltpu.VMEM((2, n_dp, *kind), bf16) for kind in kinds],
            *[pltpu.VMEM((chips, n_dp, *block), bf16) for block in blocks],
            *[pltpu.VMEM((heard, n_dp, *block), bf16) for block in blocks],
            *[pltpu.VMEM((n_dp + 1, *block), bf16) for block in blocks],
            *[pltpu.VMEM((2, n_dp // 2, *(block if square else (16, 128))), bf16) for block in blocks],
            dma((n, chips)),
            dma((n, chips)),
            dma((n, chips)),
            dma((n, chips)),
            dma((n, n_dp)),
            dma((n, n_dp + 1)),
            dma((n, 3)),
            dma((n, 3)),
            dma((len(kinds), 2)),
            dma((16, n_dp)),
            dma((16, n_dp)),
            dma((max(len(stages), 16), 2)),
            *[pltpu.VMEM(stage, jnp.bfloat16) for stage in stages],
        ],
        input_output_aliases=aliases,
        compiler_params=pltpu.CompilerParams(
            collective_id=number, has_side_effects=True, vmem_limit_bytes=62 * 1024 * 1024
        ),
    )(*arrays, *cut_in)


def scatter_all(
    n_dp,
    n_expert,
    items,
    splits,
    cut_in,
    cut_shapes,
    cuts,
    number,
    aliases,
    stages,
    puts=nothing,
    middle=nothing,
):
    chips = n_expert // 2
    blocks = (2 * chips - 1 if chips != 4 else 7) * n_dp + n_dp + 3
    need = sum(blocks * item.shape[2] * item.shape[3] * 2 for item in items)
    kinds = {(item.shape[2] // split, item.shape[3]) for item, split in zip(items, splits)}
    need += sum(2 * n_dp * kind[0] * kind[1] * 2 for kind in kinds)
    need += sum(stage[0] * stage[1] * stage[2] * 2 for stage in stages)
    pieces = -(-need // (61 * 1024 * 1024))
    tiles = [item.shape[3] // 128 for item in items]
    results = [[] for item in items]
    extra = []
    for piece in range(pieces):
        ends = [(t * piece // pieces * 128, t * (piece + 1) // pieces * 128) for t in tiles]
        used = [i for i, (low, high) in enumerate(ends) if high > low]
        first = piece == 0
        outs = scatter_call(
            n_dp,
            n_expert,
            [items[i][..., ends[i][0] : ends[i][1]] if pieces > 1 else items[i] for i in used],
            [splits[i] for i in used],
            cut_in if first else [],
            cut_shapes if first else [],
            cuts if first else nothing,
            number + piece,
            {len(used) + a: len(used) + b for a, b in aliases} if first else {},
            stages if first else [],
            puts if first else nothing,
            middle if first else nothing,
        )
        for i, out in zip(used, outs):
            results[i].append(out)
        if first:
            extra = outs[len(used) :]
    return [one[0] if len(one) == 1 else jnp.concatenate(one, axis=1) for one in results], extra


def dot(left, right, dims):
    return lax.dot_general(
        left, right, ((dims[:1], dims[1:]), ((), ())), preferred_element_type=jnp.float32
    )


def picks(slots_ref, number):
    pair = slots_ref.shape[2]
    rows = lax.broadcasted_iota(jnp.int32, (2 * CAP, pair), 0)
    return [slots_ref[0, e : e + 1, :] == rows for e in range(number)]


def pick_kernel(number, experts_all, slots_ref, x_ref, g_ref, router_ref, rows_ref, grows_ref, gates_ref):
    chosen = picks(slots_ref, number)
    pick = jnp.concatenate(chosen, axis=0).astype(jnp.bfloat16)
    size = 2 * CAP
    x = x_ref[...]
    logits = dot(router_ref[...], x, (0, 1))
    names = lax.broadcasted_iota(jnp.int32, logits.shape, 0)
    logits = jnp.where(names < experts_all, logits, -1e30)
    weights = jnp.exp(logits - jnp.max(logits, axis=0, keepdims=True))
    probs = weights / jnp.sum(weights, axis=0, keepdims=True)
    for e in range(number):
        gate = jnp.sum(jnp.where(chosen[e], probs[e : e + 1, :], 0.0), axis=1, keepdims=True)
        gates_ref[e] = jnp.broadcast_to(gate, (size, 128))
    picked = dot(pick, x, (1, 0)).astype(jnp.bfloat16)
    for e in range(number):
        rows_ref[e] = picked[e * size : (e + 1) * size]
    picked = dot(pick, g_ref[...], (1, 0)).astype(jnp.bfloat16)
    for e in range(number):
        grows_ref[e] = picked[e * size : (e + 1) * size]


def expert_kernel(steps, half, n_weights, n_into, n_pack, names_ref, x_ref, g_ref, gates_ref, *refs):
    weights, refs = refs[:n_weights], refs[n_weights:]
    down_ref, refs = refs[0], refs[1 + n_into :]
    (
        y_ref,
        dx_ref,
        probs_ref,
        dgate_ref,
        dup_ref,
        ddown_ref,
        *pack_refs,
        sum_gate,
        sum_up,
    ) = refs
    bf16 = jnp.bfloat16
    g = g_ref[0]
    rows, width = x_ref.shape[1:]
    part = dgate_ref.shape[2]
    gate = gates_ref[0][:, :1]
    if n_weights == 2:
        piece = 512
        gate_ref, up_ref = weights
        gate_mid = dot(x_ref[0], gate_ref[0], (1, 0))
        up_mid = dot(x_ref[0], up_ref[0], (1, 0))
        spans = [
            (pl.ds(at, piece), gate_ref, up_ref, pl.ds(at, piece), pl.ds(0, part), pl.ds(0, part))
            for at in range(0, width, piece)
        ]
    else:
        piece = width // n_weights
        spans = []
        gate_mid = up_mid = 0.0
        for n, ref in enumerate(weights):
            span = pl.ds(pl.multiple_of(names_ref[1 + n], piece), piece)
            x_part = x_ref[0, :, span]
            gate_mid = gate_mid + dot(x_part, ref[0, :, :part], (1, 0))
            up_mid = up_mid + dot(x_part, ref[0, :, part:], (1, 0))
            spans.append((span, ref, ref, pl.ds(0, piece), pl.ds(0, part), pl.ds(part, part)))
    sigmoid = 1.0 / (1.0 + jnp.exp(-gate_mid))
    silu = gate_mid * sigmoid
    hidden = silu * up_mid
    hidden_low = hidden.astype(bf16)
    grad_plain = dot(g, down_ref[0], (1, 1))
    grad_gates = jnp.sum(grad_plain * hidden_low.astype(jnp.float32), axis=1, keepdims=True)
    high = grad_gates.astype(bf16).astype(jnp.float32)
    lane = lax.broadcasted_iota(jnp.int32, (rows, 128), 1)
    name = names_ref[0] + pl.program_id(0)
    probs_ref[0] = (
        jnp.where(lane == name, high, 0.0) + jnp.where(lane == name + half, grad_gates - high, 0.0)
    ).astype(bf16)
    grad_hidden = grad_plain * gate
    grad_gate = (
        grad_hidden * up_mid * sigmoid * (1.0 + gate_mid * (1.0 - sigmoid))
    ).astype(bf16)
    grad_up = (grad_hidden * silu).astype(bf16)
    scaled = (hidden * gate).astype(bf16)
    for at in range(0, width, piece):
        y_ref[0, :, at : at + piece] = (
            dot(hidden_low, down_ref[0, :, at : at + piece], (1, 0)) * gate
        ).astype(bf16)
    for span, gate_ref, up_ref, here, gate_columns, up_columns in spans:
        dx_ref[0, :, span] = (
            dot(grad_gate, gate_ref[0, here, gate_columns], (1, 1))
            + dot(grad_up, up_ref[0, here, up_columns], (1, 1))
        ).astype(bf16)
    step = pl.program_id(1)
    for span, *unused in spans:
        x_part = x_ref[0, :, span]
        here_gate = dot(x_part, grad_gate, (0, 0))
        here_up = dot(x_part, grad_up, (0, 0))
        here_down = dot(scaled, g_ref[0, :, span], (0, 0))
        if steps == 1:
            dgate_ref[0, span, :] = here_gate.astype(bf16)
            dup_ref[0, span, :] = here_up.astype(bf16)
            ddown_ref[0, :, span] = here_down
            continue

        @pl.when(step == 0)
        def _():
            sum_gate[span, :] = here_gate
            sum_up[span, :] = here_up
            ddown_ref[0, :, span] = here_down

        @pl.when(step > 0)
        def _():
            sum_gate[span, :] += here_gate
            sum_up[span, :] += here_up
            ddown_ref[0, :, span] += here_down

        @pl.when(step == steps - 1)
        def _():
            dgate_ref[0, span, :] = sum_gate[span, :].astype(bf16)
            dup_ref[0, span, :] = sum_up[span, :].astype(bf16)

    if n_pack:

        @pl.when((step == steps - 1) & (pl.program_id(0) < n_pack))
        def _():
            pack_ref = pack_refs[0]
            depth = pack_ref.shape[2]
            for plane in range(pack_ref.shape[0]):
                here = pl.ds(plane * depth, depth)
                pack_ref[plane, 0, :, :part] = dgate_ref[0, here, :]
                pack_ref[plane, 0, :, part:] = dup_ref[0, here, :]


def put_back(number, slots_ref, pairs):
    pick = jnp.concatenate(picks(slots_ref, number), axis=0).astype(jnp.bfloat16)
    piece = 512
    for source, target, first in pairs:
        width = source.shape[2]
        for at in range(0, width, piece):
            size = min(piece, width)
            part = source[:, :, at : at + size].reshape(-1, size)
            target[:, first + at : first + at + size] = dot(pick, part, (0, 0)).astype(
                jnp.bfloat16
            )


def place_back_kernel(number, slots_ref, dx_ref, probs_ref, back_ref):
    put_back(number, slots_ref, [(dx_ref, back_ref, 0), (probs_ref, back_ref, dx_ref.shape[2])])


def place_out_kernel(number, slots_ref, y_ref, out_ref):
    put_back(number, slots_ref, [(y_ref, out_ref, 0)])


def place_out(slots, y, out):
    pairs, number, pair = slots.shape
    pltpu.emit_pipeline(
        functools.partial(place_out_kernel, number),
        grid=(pairs,),
        in_specs=[
            pl.BlockSpec((1, number, pair), lambda p: (p, 0, 0)),
            pl.BlockSpec((number, 2 * CAP, D), lambda p: (0, p, 0)),
        ],
        out_specs=[pl.BlockSpec((pair, D), lambda p: (p, 0))],
    )(slots, y, out)


def pick_shapes(number, pairs):
    bf16 = jnp.bfloat16
    size = 2 * CAP
    return [
        jax.ShapeDtypeStruct((number, pairs * size, D), bf16),
        jax.ShapeDtypeStruct((number, pairs * size, D), bf16),
        jax.ShapeDtypeStruct((number, pairs * size, 128), jnp.float32),
    ]


def pick_rows(number, experts_all, slots, x_all, g_all, router, rows, grows, gates):
    pairs, _, pair = slots.shape
    size = 2 * CAP
    tokens = pl.BlockSpec((pair, D), lambda p: (p, 0))
    picked = pl.BlockSpec((number, size, D), lambda p: (0, p, 0))
    pltpu.emit_pipeline(
        functools.partial(pick_kernel, number, experts_all),
        grid=(pairs,),
        in_specs=[
            pl.BlockSpec((1, number, pair), lambda p: (p, 0, 0)),
            tokens,
            tokens,
            pl.BlockSpec(router.shape, lambda p: (0, 0)),
        ],
        out_specs=[picked, picked, pl.BlockSpec((number, size, 128), lambda p: (0, p, 0))],
    )(slots, x_all, g_all, router, rows, grows, gates)


def expert_call(names, half, low, number, rows, grows, gates, weights, down, into=(), pack=()):
    total, depth, _ = rows.shape
    part = down.shape[1]
    size = depth
    while size > 768:
        size //= 2
    steps = depth // size
    bf16 = jnp.bfloat16
    f32 = jnp.float32

    def from_rows(width):
        return pl.BlockSpec((1, size, width), lambda e, r: (e + low, r, 0))

    def whole(*shape):
        return pl.BlockSpec((1, *shape), lambda e, r: (e, 0, 0))

    def from_whole(*shape):
        return pl.BlockSpec((1, *shape), lambda e, r: (e + low, 0, 0))

    packed = [
        pl.BlockSpec(
            (planes, 1, D // planes, 2 * part),
            lambda e, r, n=n: (0, lax.min(e, n - 1), 0, 0),
        )
        for n, planes in ([pack] if pack else [])
    ]
    keep = (D, part) if steps > 1 else (16, 128)
    return pl.pallas_call(
        functools.partial(
            expert_kernel, steps, half, len(weights), len(into), pack[0] if pack else 0
        ),
        grid=(number, steps),
        in_specs=[
            pl.BlockSpec(memory_space=pltpu.SMEM),
            from_rows(D),
            from_rows(D),
            from_rows(128),
            *[(from_whole if len(weights) == 2 else whole)(*one.shape[1:]) for one in weights],
            from_whole(part, D),
            *[pl.BlockSpec(memory_space=pl.ANY)] * len(into),
        ],
        out_specs=[
            from_rows(D),
            from_rows(D),
            from_rows(128),
            whole(D, part),
            whole(D, part),
            from_whole(part, D),
            *packed,
        ],
        out_shape=[
            jax.ShapeDtypeStruct((total, depth, D), bf16),
            jax.ShapeDtypeStruct((total, depth, D), bf16),
            jax.ShapeDtypeStruct((total, depth, 128), bf16),
            jax.ShapeDtypeStruct((number, D, part), bf16),
            jax.ShapeDtypeStruct((number, D, part), bf16),
            jax.ShapeDtypeStruct((total, part, D), f32),
            *[
                jax.ShapeDtypeStruct((planes, n, D // planes, 2 * part), bf16)
                for n, planes in ([pack] if pack else [])
            ],
        ],
        input_output_aliases={
            5 + len(weights) + i: out for i, out in zip(range(len(into)), (0, 1, 2, 5))
        },
        scratch_shapes=[pltpu.VMEM(keep, f32), pltpu.VMEM(keep, f32)],
        compiler_params=pltpu.CompilerParams(vmem_limit_bytes=BIG),
    )(names, rows, grows, gates, *weights, down, *into)


def place_back(slots, dx, probs):
    pairs, number, pair = slots.shape
    size = 2 * CAP

    def rows(one):
        return pl.BlockSpec((number, size, one.shape[2]), lambda p: (0, p, 0))

    return pl.pallas_call(
        functools.partial(place_back_kernel, number),
        grid=(pairs,),
        in_specs=[pl.BlockSpec((1, number, pair), lambda p: (p, 0, 0)), rows(dx), rows(probs)],
        out_specs=pl.BlockSpec((pair, D + 128), lambda p: (p, 0)),
        out_shape=jax.ShapeDtypeStruct((pairs * pair, D + 128), jnp.bfloat16),
        compiler_params=pltpu.CompilerParams(vmem_limit_bytes=BIG),
    )(slots, dx, probs)


def through_kernel(count, *refs):
    lefts, weight_ref, out_ref = refs[:count], refs[count], refs[count + 1]
    for i in range(count):

        @pl.when(pl.program_id(1) == i)
        def _():
            part = dot(lefts[i][...], weight_ref[0], (1, 1))
            if i:
                part = part + out_ref[...]
            out_ref[...] = part


def through(lefts, weights, first):
    count, (rows, depth) = len(lefts), lefts[0].shape
    piece = 512
    return pl.pallas_call(
        functools.partial(through_kernel, count),
        grid=(depth // piece, count),
        in_specs=[
            *[pl.BlockSpec((rows, depth), lambda c, i: (0, 0))] * count,
            pl.BlockSpec((1, piece, depth), lambda c, i: (i + first, c, 0)),
        ],
        out_specs=pl.BlockSpec((rows, piece), lambda c, i: (0, c)),
        out_shape=jax.ShapeDtypeStruct((rows, depth), jnp.float32),
        compiler_params=pltpu.CompilerParams(vmem_limit_bytes=BIG),
    )(*lefts, weights)


def outer_kernel(which, n_left, *refs):
    lefts, rights = refs[:n_left], refs[n_left : n_left + len(which)]
    piece = 512
    for left, right, out_ref in zip(which, rights, refs[n_left + len(which) :]):
        for at in range(0, out_ref.shape[1], piece):
            out_ref[:, at : at + piece] = dot(
                lefts[left][...], right[:, at : at + piece], (0, 0)
            ).astype(out_ref.dtype)


def outer(lefts, rights, which):
    rows, depth = lefts[0].shape
    piece = 256
    return pl.pallas_call(
        functools.partial(outer_kernel, which, len(lefts)),
        grid=(depth // piece,),
        in_specs=[
            *[pl.BlockSpec((rows, piece), lambda c: (0, c))] * len(lefts),
            *[pl.BlockSpec((rows, depth), lambda c: (0, 0))] * len(rights),
        ],
        out_specs=[pl.BlockSpec((piece, depth), lambda c: (c, 0))] * len(rights),
        out_shape=[jax.ShapeDtypeStruct((depth, depth), jnp.bfloat16)] * len(rights),
        compiler_params=pltpu.CompilerParams(vmem_limit_bytes=BIG),
    )(*lefts, *rights)


def widen_kernel(*refs):
    for source, target in zip(refs[:2], refs[-2:]):
        target[...] = source[...].astype(jnp.float32)


def widen(low, high, values, into=()):
    number, rows, columns = values[0].shape
    block = pl.BlockSpec((1, rows, columns), lambda e: (e + low, 0, 0))
    return pl.pallas_call(
        widen_kernel,
        grid=(high - low,),
        in_specs=[block] * 2 + [pl.BlockSpec(memory_space=pl.ANY)] * len(into),
        out_specs=[block] * 2,
        out_shape=[jax.ShapeDtypeStruct(one.shape, jnp.float32) for one in values],
        input_output_aliases={2 + i: i for i in range(len(into))},
        compiler_params=pltpu.CompilerParams(vmem_limit_bytes=BIG),
    )(*values, *into)


def widen_pieces_kernel(low, n_pieces, offsets_ref, *refs):
    pieces, refs = refs[:n_pieces], refs[n_pieces + 2 :]
    targets, wide, sems = refs[:2], refs[2], refs[3]
    part = wide.shape[4]
    copies = []
    for k, piece in enumerate(pieces):
        columns = pl.ds(pl.multiple_of(offsets_ref[k], part), part)
        for n in range(2):
            wide[k, n] = piece[:, :, n * part : (n + 1) * part].astype(jnp.float32)
            copy = pltpu.make_async_copy(
                wide.at[k, n], targets[n].at[pl.ds(low, piece.shape[0]), :, columns], sems.at[k, n]
            )
            copy.start()
            copies.append(copy)
    for copy in copies:
        copy.wait()


def widen_pieces(offsets, low, pieces, into):
    size, rows, columns = pieces[0].shape
    anywhere = pl.BlockSpec(memory_space=pl.ANY)
    count = len(pieces)
    return pl.pallas_call(
        functools.partial(widen_pieces_kernel, low, count),
        in_specs=[
            pl.BlockSpec(memory_space=pltpu.SMEM),
            *[pl.BlockSpec(memory_space=pltpu.VMEM)] * count,
            anywhere,
            anywhere,
        ],
        out_specs=[anywhere, anywhere],
        out_shape=[jax.ShapeDtypeStruct(one.shape, one.dtype) for one in into],
        scratch_shapes=[
            pltpu.VMEM((count, 2, size, rows, columns // 2), jnp.float32),
            pltpu.SemaphoreType.DMA((count, 2)),
        ],
        input_output_aliases={1 + count: 0, 2 + count: 1},
        compiler_params=pltpu.CompilerParams(vmem_limit_bytes=BIG),
    )(offsets, *pieces, *into)


def shards(
    n_dp,
    n_expert,
    tokens,
    cotangent,
    lengths,
    routes,
    w_query,
    w_key,
    w_value,
    w_out,
    w_router,
    gain_attn,
    gain_query,
    gain_key,
    gain_mlp,
    w_gate,
    w_up,
    w_down,
):
    groups = n_dp * n_expert
    bf16 = jnp.bfloat16
    number = w_gate.shape[0]
    ff = w_gate.shape[2]
    part = ff // n_dp
    experts_all = w_router.shape[1]
    width = 128
    small = jnp.concatenate(
        [
            w_router,
            gain_attn[:, None],
            gain_query[:, None],
            gain_key[:, None],
            gain_mlp[:, None],
            jnp.zeros((w_router.shape[0], width - experts_all - 4), bf16),
        ],
        axis=1,
    )
    hits = jnp.any(
        routes[:, :, None] == jnp.arange(width, dtype=jnp.int32)[None, None, :], axis=1
    ).astype(bf16)
    count = tokens.shape[0]
    rows_each = w_query.shape[0]
    extras = jnp.concatenate([hits, jnp.pad(small, ((0, count - rows_each), (0, 0)))], axis=1)
    weights = jnp.stack([w_query, w_key, w_value, w_out])
    depth = w_gate.shape[1]
    early = number // 4
    beside = early + number // 8
    late = number - number // 4
    back_beside = number // 8
    back_third = back_beside + max(number // 4, 1)
    back_late = back_third + number // 4
    me = lax.axis_index("dp")
    cut_shape = jax.ShapeDtypeStruct((number, n_dp * depth, part), bf16)

    def row_block(size):
        return lambda ref, block: ref.at[pl.ds(pl.multiple_of(block * size, 16), size)]

    def columns_at(at):
        return pl.ds(pl.multiple_of(at * part, part), part)

    def rows_at(at):
        return pl.ds(pl.multiple_of(at * depth, depth), depth)

    def recut(low, high):
        def cuts(ins, outs):
            def pair(n):
                chosen = pl.ds(low, high - low)
                return (
                    lambda to: ins[n].at[chosen, :, columns_at(to)],
                    lambda at: outs[n].at[chosen, rows_at(at)],
                )

            return [pair(0), pair(1)]

        return cuts

    to_plane, from_plane = partners(me, n_dp)

    def permuted(pieces, chained=False):
        got = []
        for k, piece in enumerate(pieces, 1):
            if chained and got:
                piece, last = lax.optimization_barrier((piece, got.pop()))
                got.append(last)
            paths = [(i, partners(i, n_dp)[0](k)) for i in range(n_dp)]
            got.append(lax.ppermute(piece, "dp", paths))
        return got

    def cut_pieces(low, high, first_k, ins, outs):
        to, unused = partners(lax.axis_index("dp"), n_dp)
        pairs = []
        for k, piece in enumerate(outs, first_k):
            for n in range(2):
                source = ins[n].at[pl.ds(low, high - low), :, columns_at(to(k))]
                pairs.append((source, piece.at[:, :, pl.ds(n * part, part)]))
        return pairs

    def piece_shapes(size, first_k):
        shape = jax.ShapeDtypeStruct((size, depth, 2 * part), bf16)
        return [shape] * (n_dp - first_k if size else 0)

    def stages(*sizes):
        return [(size, depth, part) for size in sizes]

    soon_shapes = piece_shapes(beside - early, 1)
    late_shapes = piece_shapes(number - late, 0)
    n_soon = len(soon_shapes)

    weights_all, extras_all, gate_early, up_early, *pieces = gather_call(
        n_dp,
        n_expert,
        [weights, extras],
        [
            jax.ShapeDtypeStruct((4, groups * rows_each, D), bf16),
            jax.ShapeDtypeStruct((groups * count, 2 * width), bf16),
        ],
        [
            lambda ref, block: ref.at[
                :, pl.ds(pl.multiple_of(block * rows_each, 16), rows_each)
            ],
            row_block(count),
        ],
        [w_gate, w_up],
        [cut_shape, cut_shape, *soon_shapes, *late_shapes],
        recut(0, early),
        {},
        0,
        stages(
            *[early] * 2,
            *[beside - early] * (2 * n_soon),
            *[number - late] * (2 * n_dp),
        ),
        lambda ins, outs: cut_pieces(early, beside, 1, ins, outs[2 : 2 + n_soon])
        + cut_pieces(late, number, 0, ins, outs[2 + n_soon :]),
    )
    soon_pieces, late_pieces = pieces[:n_soon], pieces[n_soon:]
    small_all = (
        extras_all[:, width:].reshape(groups, count, width)[:, :rows_each].reshape(-1, width)
    )
    hits_all = extras_all[:, :experts_all]
    router_weight = small_all[:, :experts_all]
    gains = small_all[:, experts_all : experts_all + 4].astype(jnp.float32)
    attn_gain, query_gain, key_gain, mlp_gain = (gains[:, i] for i in range(4))
    inputs = tokens.astype(jnp.float32)
    segment, position, places = layout(lengths[0], count)
    half = HD // 2
    freq = 10000.0 ** (-2.0 * jnp.arange(half, dtype=jnp.float32) / HD)
    angle = position.astype(jnp.float32)[:, None] * freq[None, :]
    cosine = jnp.cos(angle)[:, None, :]
    sine = jnp.sin(angle)[:, None, :]
    scale = HD ** (-0.5)
    normed, attn_inverse = rms_forward(inputs, attn_gain)
    normed_low = normed.astype(bf16)
    query_raw = product(normed_low, weights_all[0], "td,de->te")
    key_raw = product(normed_low, weights_all[1], "td,de->te")
    value_low = product(normed_low, weights_all[2], "td,de->te").astype(bf16)
    query_normed, query_inverse = rms_forward(query_raw, query_gain)
    key_normed, key_inverse = rms_forward(key_raw, key_gain)
    query_low = rotate(query_normed, cosine, sine).astype(bf16).reshape(count, HEADS, HD)
    key_low = rotate(key_normed, cosine, sine).astype(bf16).reshape(count, HEADS, HD)
    value_heads = value_low.reshape(count, HEADS, HD)
    allowed = (segment[:, None] == segment[None, :]) & (places[None, :] <= places[:, None])
    scores = product(query_low, key_low, "qhd,khd->hqk") * scale
    scores = jnp.where(allowed[None], scores, -1e30)
    probs = jax.nn.softmax(scores, axis=-1)
    probs_low = probs.astype(bf16)
    attended_low = product(probs_low, value_heads, "hqk,khd->qhd").reshape(count, D).astype(bf16)
    middle = inputs + product(attended_low, weights_all[3], "td,de->te")
    mlp_normed, mlp_inverse = rms_forward(middle, mlp_gain)
    mlp_low = mlp_normed.astype(bf16)
    router = jax.nn.softmax(product(mlp_low, router_weight, "td,de->te"), axis=-1)

    first = lax.axis_index("expert") * number
    hit = lax.dynamic_slice_in_dim(hits_all, first, number, 1).reshape(groups, count, number)
    before = jnp.tril(jnp.ones((count, count), bf16), -1)
    slot = product(before, hit, "ts,bse->bet").astype(jnp.int32)
    slot = jnp.where(jnp.transpose(hit, (0, 2, 1)) > 0, slot, -1)
    slot = slot.reshape(groups // 2, 2, number, count)
    shift = jnp.array([0, CAP], jnp.int32)[None, :, None, None]
    slots = jnp.transpose(jnp.where(slot < 0, -1, slot + shift), (0, 2, 1, 3))
    slots = slots.reshape(groups // 2, number, 2 * count)
    router_own = jnp.pad(
        jnp.roll(router_weight, -first, axis=1), ((0, 0), (0, width - experts_all))
    )
    if n_soon:
        mlp_low, *soon_pieces = lax.optimization_barrier((mlp_low, *permuted(soon_pieces)))

    def put_weights(ins, outs):
        chosen = pl.ds(early, beside - early)
        unused, heard = partners(lax.axis_index("dp"), n_dp)
        pairs = []
        if beside > early:
            own = lax.axis_index("dp")
            for n in range(2):
                source = ins[n].at[chosen, :, columns_at(own)]
                pairs.append((source, outs[n].at[chosen, rows_at(own)]))
        for k, piece in enumerate(ins[6:], 1):
            for n in range(2):
                columns = piece.at[:, :, pl.ds(n * part, part)]
                pairs.append((columns, outs[n].at[chosen, rows_at(heard(k))]))
        return pairs

    def pick_all(items, ins, outs):
        pick_rows(number, experts_all, ins[4], *items, ins[5], *outs[2:])

    unused, unused, gate_cut, up_cut, rows, grows, gates = gather_call(
        n_dp,
        n_expert,
        [mlp_low, cotangent],
        [jax.ShapeDtypeStruct((groups * count, D), bf16)] * 2,
        [row_block(count)] * 2,
        [w_gate, w_up, gate_early, up_early, slots, router_own, *soon_pieces],
        [cut_shape, cut_shape, *pick_shapes(number, groups // 2)],
        recut(beside, late),
        {4: 2, 5: 3},
        1,
        stages(*[late - beside] * 2, *[beside - early] * (2 * n_dp if n_soon else 0)),
        put_weights,
        pick_all,
    )
    *late_pieces, rows = lax.optimization_barrier((*late_pieces, rows))
    late_pieces = [late_pieces[0], *permuted(late_pieces[1:])]
    packing = back_beside > 0 and depth == 512
    *outs, gate_soon, up_soon, down_soon = expert_call(
        first[None],
        experts_all,
        0,
        late,
        rows,
        grows,
        gates,
        [gate_cut, up_cut],
        w_down,
        pack=(back_beside, n_dp) if packing else (),
    )
    if packing:
        *outs, gate_soon, up_soon, down_soon, packed = [*outs, gate_soon, up_soon, down_soon]
    offsets = [from_plane(k) * depth for k in range(n_dp)]
    weighted, grad_rows, grad_gates, gate_rest, up_rest, grad_down_part = expert_call(
        jnp.stack([first + late, *offsets]),
        experts_all,
        late,
        number - late,
        rows,
        grows,
        gates,
        late_pieces,
        w_down,
        [*outs, down_soon],
    )
    part_back = place_back(slots, grad_rows, grad_gates)

    def ways(low, high, at, ins, outs):
        def pair(e, n):
            return (
                lambda to: ins[n].at[pl.ds(e, 1), rows_at(to)],
                lambda here: outs[n].at[pl.ds(e + at, 1), :, columns_at(here)],
            )

        return [pair(e, n) for e in range(low, high) for n in range(2)]

    def cut_grads(low, high, ins, outs):
        to, unused = partners(lax.axis_index("dp"), n_dp)
        pairs = []
        for k, piece in enumerate(outs):
            for n in range(2):
                source = ins[n].at[pl.ds(low, high - low), rows_at(to(k))]
                pairs.append((source, piece.at[:, :, pl.ds(n * part, part)]))
        return pairs

    pieces = []
    if back_beside:
        for k in range(n_dp):
            if packing:
                piece = lax.dynamic_index_in_dim(packed, to_plane(k), 0, False)
            else:
                piece = jnp.concatenate(
                    [
                        lax.dynamic_slice_in_dim(
                            one[:back_beside], to_plane(k) * depth, depth, 1
                        )
                        for one in (gate_soon, up_soon)
                    ],
                    axis=2,
                )
            pieces.append(piece)
        ahead = lax.optimization_barrier((*pieces[1:], *late_pieces[1:]))
        pieces = [pieces[0], *permuted(ahead[: n_dp - 1])]
        part_back, *pieces = lax.optimization_barrier((part_back, *pieces))
    way_shapes = [jax.ShapeDtypeStruct((number, depth, ff), bf16)] * 2
    piece_shape = jax.ShapeDtypeStruct((back_late - back_third, depth, 2 * part), bf16)
    (back,), (gate_third, up_third, part_out, *later_pieces) = scatter_all(
        n_dp,
        n_expert,
        [part_back.reshape(n_dp, n_expert, count, D + width)],
        [4],
        [gate_soon, up_soon, slots, weighted],
        [
            *way_shapes,
            jax.ShapeDtypeStruct((groups * count, D), bf16),
            *[piece_shape] * n_dp,
        ],
        lambda ins, outs: ways(back_beside, back_third, 0, ins, outs),
        8,
        (),
        stages(
            *[1] * (2 * (back_third - back_beside)),
            *[back_late - back_third] * (2 * n_dp),
        ),
        lambda ins, outs: cut_grads(back_third, back_late, ins, outs[3:]),
        lambda ins, outs: place_out(ins[2], ins[3], outs[2]),
    )
    later_pieces = [later_pieces[0], *permuted(later_pieces[1:])]

    offsets = jnp.stack([from_plane(k) * part for k in range(n_dp)])
    widened = widen(back_beside, back_third, [gate_third, up_third])
    if back_beside:
        widened = widen_pieces(offsets, 0, pieces, widened)
    part_out, *widened = lax.optimization_barrier((part_out, *widened))

    def attention_back(back):
        grad_final = cotangent.astype(jnp.float32)
        grad_mlp = back[:, :D]
        grad_router_probs = back[:, D : D + experts_all] + back[:, D + experts_all :]
        grad_logits = router * (
            grad_router_probs - jnp.sum(router * grad_router_probs, axis=1, keepdims=True)
        )
        grad_logits_low = grad_logits.astype(bf16)
        grad_router_full = product(
            mlp_low, jnp.pad(grad_logits_low, ((0, 0), (0, width - experts_all))), "td,te->de"
        )
        grad_mlp = grad_mlp + product(grad_logits_low, router_weight, "te,de->td")
        grad_middle_part, grad_mlp_gain = rms_backward(middle, mlp_inverse, mlp_gain, grad_mlp)
        grad_middle = grad_final + grad_middle_part
        grad_branch_low = grad_middle.astype(bf16)
        grad_attended = (
            through([grad_branch_low], weights_all, 3).astype(bf16).reshape(count, HEADS, HD)
        )
        grad_weights = product(grad_attended, value_heads, "qhd,khd->hqk")
        grad_scores = probs * (grad_weights - jnp.sum(probs * grad_weights, axis=-1, keepdims=True))
        grad_scores_low = grad_scores.astype(bf16)
        grad_query_turn = product(grad_scores_low, key_low, "hqk,khd->qhd").reshape(count, D) * scale
        grad_key_turn = product(grad_scores_low, query_low, "hqk,qhd->khd").reshape(count, D) * scale
        grad_value_low = (
            product(probs_low, grad_attended, "hqk,qhd->khd").reshape(count, D).astype(bf16)
        )
        grad_query_raw, grad_query_gain = rms_backward(
            query_raw, query_inverse, query_gain, rotate(grad_query_turn, cosine, -sine)
        )
        grad_key_raw, grad_key_gain = rms_backward(
            key_raw, key_inverse, key_gain, rotate(grad_key_turn, cosine, -sine)
        )
        grad_query_low = grad_query_raw.astype(bf16)
        grad_key_low = grad_key_raw.astype(bf16)
        full_grads = outer(
            [attended_low, normed_low],
            [grad_branch_low, grad_value_low, grad_key_low, grad_query_low],
            (0, 1, 1, 1),
        )
        grad_normed = through([grad_query_low, grad_key_low, grad_value_low], weights_all, 0)
        grad_inputs_part, grad_attn_gain = rms_backward(inputs, attn_inverse, attn_gain, grad_normed)
        grad_inputs = grad_middle + grad_inputs_part

        gain_grads = jnp.stack([grad_attn_gain, grad_query_gain, grad_key_gain, grad_mlp_gain])
        gain_grads = jnp.transpose(gain_grads.reshape(4, groups, rows_each), (1, 0, 2))
        gain_grads = jnp.pad(gain_grads, ((0, 0), (0, 12), (0, width - rows_each)))
        return (
            grad_inputs,
            *full_grads,
            grad_router_full.astype(bf16),
            gain_grads.astype(bf16).reshape(groups * 16, width),
        )

    def unreached(back):
        shapes = [(count, D)] + [(D, D)] * 4 + [(D, width), (groups * 16, width)]
        kinds = [jnp.float32] + [bf16] * 6
        return tuple(jnp.zeros(shape, kind) for shape, kind in zip(shapes, kinds))

    grad_inputs, *weight_grads = lax.cond(lengths[0, 0] > 0, attention_back, unreached, back)

    def blocks_of(value):
        return value.reshape(n_dp, n_expert, -1, value.shape[1])

    sums, (gate_back, up_back) = scatter_all(
        n_dp,
        n_expert,
        [part_out.reshape(n_dp, n_expert, count, D)]
        + [blocks_of(value) for value in weight_grads],
        [2, 1, 1, 1, 2 if rows_each > 16 else 1, 1, 1],
        [gate_soon, up_soon, gate_rest, up_rest],
        way_shapes,
        lambda ins, outs: ways(back_late, late, 0, ins[:2], outs)
        + ways(0, number - late, late, ins[2:], outs),
        16,
        (),
        [],
    )
    summed, grad_out_part, grad_value_part, grad_key_part, grad_query_part, router_part, small = sums
    output = (middle + summed).astype(bf16)
    grad_router_part = router_part[:, :experts_all]
    gain_parts = [small[i, :rows_each] for i in range(4)]
    widened = widen(back_late, number, [gate_back, up_back], widened)
    if back_late > back_third:
        widened = widen_pieces(offsets, back_third, later_pieces, widened)
    grad_gate_part, grad_up_part = widened
    return (
        output,
        grad_inputs,
        grad_query_part,
        grad_key_part,
        grad_value_part,
        grad_out_part,
        grad_router_part,
        gain_parts[0],
        gain_parts[1],
        gain_parts[2],
        gain_parts[3],
        grad_gate_part,
        grad_up_part,
        grad_down_part,
    )


def solution(mesh):
    return jax.shard_map(
        functools.partial(shards, mesh.shape["dp"], mesh.shape["expert"]),
        mesh=mesh,
        in_specs=(
            P(("dp", "expert"), None),
            P(("dp", "expert"), None),
            P(("dp", "expert"), None),
            P(("dp", "expert"), None),
            P(("dp", "expert"), None),
            P(("dp", "expert"), None),
            P(("dp", "expert"), None),
            P(("dp", "expert"), None),
            P(("dp", "expert"), None),
            P(("dp", "expert")),
            P(("dp", "expert")),
            P(("dp", "expert")),
            P(("dp", "expert")),
            P("expert", "dp", None),
            P("expert", "dp", None),
            P("expert", "dp", None),
        ),
        out_specs=(
            P(("dp", "expert"), None),
            P(("dp", "expert"), None),
            P(("dp", "expert"), None),
            P(("dp", "expert"), None),
            P(("dp", "expert"), None),
            P(("dp", "expert"), None),
            P(("dp", "expert"), None),
            P(("dp", "expert")),
            P(("dp", "expert")),
            P(("dp", "expert")),
            P(("dp", "expert")),
            P("expert", "dp", None),
            P("expert", "dp", None),
            P("expert", "dp", None),
        ),
        check_vma=False,
    )
```

```python
import functools

import jax
import jax.numpy as jnp
from jax import lax
from jax.experimental import pallas as pl
from jax.experimental.pallas import tpu as pltpu
from jax.sharding import PartitionSpec as P

D = 2048
HEADS = 16
HD = 128
TOPK = 8
CAP = 24


eps = 1e-05


def product(left, right, form):
    return jnp.einsum(form, left, right, preferred_element_type=jnp.float32)


def rms_forward(values, gain):
    inverse = lax.rsqrt(jnp.mean(values * values, axis=-1, keepdims=True) + eps)
    return (values * inverse * gain, inverse)


def rms_backward(values, inverse, gain, grad):
    scaled = grad * gain
    inner = jnp.mean(scaled * values, axis=-1, keepdims=True)
    grad_values = inverse * scaled - values * (inverse * inverse * inverse) * inner
    grad_gain = jnp.sum(grad * values * inverse, axis=0)
    return (grad_values, grad_gain)


def layout(lengths_row, count):
    places = jnp.arange(count, dtype=jnp.int32)
    ends = jnp.cumsum(lengths_row, dtype=jnp.int32)
    passed = (places[:, None] >= ends[None, :]).astype(jnp.int32)
    segment = jnp.sum(passed, axis=1, dtype=jnp.int32)
    start = jnp.sum(passed * lengths_row[None, :], axis=1, dtype=jnp.int32)
    return (segment, places - start, places)


def rotate(values, cosine, sine):
    count = values.shape[0]
    heads = values.reshape(count, HEADS, HD)
    half = HD // 2
    first = heads[..., :half]
    second = heads[..., half:]
    turned = jnp.concatenate(
        [first * cosine - second * sine, second * cosine + first * sine], axis=-1
    )
    return turned.reshape(count, D)


MESH = pl.DeviceIdType.MESH
BIG = 60 * 1024 * 1024


def place_of():
    z = lax.axis_index("dp")
    j = lax.axis_index("expert")
    return z, j, j // 2, j % 2


def other_chips(chip, chips):
    if chips == 4:
        square = [chip, chip + 1 - 2 * (chip % 2), chip + 2 - 4 * (chip // 2), 3 - chip]
        return lambda k: square[k], lambda k: square[k]
    return lambda k: (chip + k) % chips, lambda k: (chip + chips - k) % chips


def partners(z, n_dp):
    if n_dp == 4:
        pairs = [z, 3 - z, (z + 2) % 4, z + 1 - 2 * (z % 2)]
        return lambda k: pairs[k], lambda k: pairs[k]
    return lambda k: (z + k) % n_dp, lambda k: (z + n_dp - k) % n_dp


def greet(n_dp, n_expert):
    z, j, chip, core = place_of()
    chips = n_expert // 2
    barrier = pltpu.get_barrier_semaphore()
    for k in range(1, n_dp):
        pl.semaphore_signal(
            barrier, inc=1, device_id=((z + k) % n_dp, j), device_id_type=MESH
        )
    for k in range(1, chips):
        other = ((chip + k) % chips) * 2 + core
        pl.semaphore_signal(barrier, inc=1, device_id=(z, other), device_id_type=MESH)
    pl.semaphore_signal(
        barrier, inc=1, device_id=(z, chip * 2 + 1 - core), device_id_type=MESH
    )
    pl.semaphore_wait(barrier, n_dp - 1 + chips - 1 + 1)


def remote(source, target, send, receive, device):
    return pltpu.make_async_remote_copy(
        src_ref=source,
        dst_ref=target,
        send_sem=send,
        recv_sem=receive,
        device_id=device,
        device_id_type=MESH,
    )


def exchange(n_dp, pairs, send, receive):
    z, j, chip, core = place_of()
    to_plane, unused = partners(z, n_dp)
    copies = []
    for i, (source, target) in enumerate(pairs):
        for k in range(1, n_dp):
            to = to_plane(k)
            copies.append(
                remote(source(to), target(z), send.at[i, k], receive.at[i, k], (to, j))
            )
    return copies


def moves(pairs, stages, local):
    if not stages:
        copies = [
            pltpu.make_async_copy(source, target, local.at[i, 0])
            for i, (source, target) in enumerate(pairs)
        ]
        for copy in copies:
            copy.start()
        return [], copies
    bring = [
        pltpu.make_async_copy(source, stages[i], local.at[i, 0])
        for i, (source, target) in enumerate(pairs)
    ]
    put = [
        pltpu.make_async_copy(stages[i], target, local.at[i, 1])
        for i, (source, target) in enumerate(pairs)
    ]
    return bring, put


def nothing(ins, outs):
    return []


def gather_kernel(
    n_dp, n_expert, n_items, places, cuts, puts, finish, n_cut, n_out, n_stages, *refs
):
    z, j, chip, core = place_of()
    chips = n_expert // 2
    square = chips == 4
    to_chip, from_chip = other_chips(chip, chips)
    sources = refs[:n_items]
    cut_in = refs[n_items : n_items + n_cut]
    at = n_items + n_cut
    targets = refs[at : at + n_items]
    cut_out = refs[at + n_items : at + n_items + n_out]
    (
        send_c,
        recv_c,
        send_b,
        recv_b,
        send_a,
        recv_a,
        local,
        send_x,
        recv_x,
        local_y,
        *stages,
    ) = refs[at + n_items + n_out :]
    greet(n_dp, n_expert)
    mate = (z, chip * 2 + 1 - core)
    near = (1, 2) if square else tuple(range(1, chips))

    def slot(i, plane, column):
        return places[i](targets[i], plane * n_expert + column)

    def pass_on(i, plane, source, column, k, chip_to):
        return remote(
            source,
            slot(i, plane, column),
            send_b.at[i, plane, k],
            recv_b.at[i, plane, k],
            (z, chip_to * 2 + core),
        )

    def hand(i, plane, source):
        for k in near:
            pass_on(i, plane, source, j, k, to_chip(k)).start()
        remote(
            source, slot(i, plane, j), send_a.at[i, plane, 0], recv_a.at[i, plane, 0], mate
        ).start()

    def along(i, plane, source, way, step):
        return remote(
            source, slot(i, plane, j), send_c.at[i, way, plane], recv_c.at[i, plane], (z + step, j)
        )

    def at_distance(d, body):
        if d == 0:
            body(z, 0)
            return

        @pl.when(z >= d)
        def _():
            body(z - d, 0)

        @pl.when(z + d < n_dp)
        def _():
            body(z + d, 1)

    for i in range(n_items):

        @pl.when(z < n_dp - 1)
        def _():
            along(i, z, sources[i], 0, 1).start()

        @pl.when(z > 0)
        def _():
            along(i, z, sources[i], 1, -1).start()

        hand(i, z, sources[i])
        pltpu.make_async_copy(sources[i], slot(i, z, j), local.at[i]).start()

    def relay(plane, way):
        step = -1 if way else 1
        for i in range(n_items):
            block = slot(i, plane, j)
            along(i, plane, block, way, step).wait_recv()

            @pl.when(z > 0 if way else z < n_dp - 1)
            def _():
                along(i, plane, block, way, step).start()

            hand(i, plane, block)

    for d in range(1, n_dp):
        at_distance(d, relay)
    pairs = cuts(cut_in, cut_out)
    copies = exchange(n_dp, pairs, send_x, recv_x)
    for copy in copies:
        copy.start()
    own = [(source(z), target(z)) for source, target in pairs]
    bring, put = moves(own + puts(cut_in, cut_out), stages, local_y)
    for copy in bring:
        copy.start()
    for one, other in zip(bring, put):
        one.wait()
        other.start()

    def arrive(i, plane, k):
        column = from_chip(k) * 2 + core
        block = slot(i, plane, column)
        pass_on(i, plane, block, column, k, chip).wait_recv()
        remote(block, block, send_a.at[i, plane, k], recv_a.at[i, plane, k], mate).start()
        return block, column

    def arrived(plane, way):
        for i in range(n_items):
            for k in near:
                block, column = arrive(i, plane, k)
                if square:

                    @pl.when(plane % 2 == k - 1)
                    def _():
                        pass_on(i, plane, block, column, 3, to_chip(3 - k)).start()

    def crossed(plane, way):
        for i in range(n_items):
            arrive(i, plane, 3)

    for d in range(n_dp):
        at_distance(d, arrived)
    if square:
        for d in range(n_dp):
            at_distance(d, crossed)

    for i in range(n_items):
        for plane in range(n_dp):
            for k in range(chips):
                column = (from_chip(k) if k else chip) * 2 + 1 - core
                block = slot(i, plane, column)
                remote(
                    block, block, send_a.at[i, plane, k], recv_a.at[i, plane, k], mate
                ).wait_recv()
        pltpu.make_async_copy(sources[i], slot(i, z, j), local.at[i]).wait()
    finish(targets, cut_in, cut_out)
    for i in range(n_items):
        for plane in range(n_dp):
            block = slot(i, plane, j)
            for k in range(1, chips):
                pass_on(i, plane, block, j, k, chip).wait_send()
            for k in range(chips):
                remote(
                    block, block, send_a.at[i, plane, k], recv_a.at[i, plane, k], mate
                ).wait_send()

            @pl.when((z < n_dp - 1) & (z >= plane))
            def _():
                along(i, plane, block, 0, 1).wait_send()

            @pl.when((z > 0) & (z <= plane))
            def _():
                along(i, plane, block, 1, -1).wait_send()

    for copy in copies + put:
        copy.wait()


def gather_call(
    n_dp,
    n_expert,
    items,
    shapes,
    places,
    cut_in,
    cut_shapes,
    cuts,
    aliases,
    number,
    stages,
    puts=nothing,
    finish=lambda items, ins, outs: None,
):
    chips = n_expert // 2
    n, m = len(items), len(cut_shapes)
    dma = pltpu.SemaphoreType.DMA
    anywhere = pl.BlockSpec(memory_space=pl.ANY)
    return pl.pallas_call(
        functools.partial(
            gather_kernel,
            n_dp,
            n_expert,
            n,
            places,
            cuts,
            puts,
            finish,
            len(cut_in),
            m,
            len(stages),
        ),
        out_shape=[*shapes, *cut_shapes],
        in_specs=[anywhere] * (n + len(cut_in)),
        out_specs=[anywhere] * (n + m),
        scratch_shapes=[
            dma((n, 2, n_dp)),
            dma((n, n_dp)),
            dma((n, n_dp, chips)),
            dma((n, n_dp, chips)),
            dma((n, n_dp, chips)),
            dma((n, n_dp, chips)),
            dma((n,)),
            dma((4, n_dp)),
            dma((4, n_dp)),
            dma((max(len(stages), 4), 2)),
            *[pltpu.VMEM(stage, jnp.bfloat16) for stage in stages],
        ],
        input_output_aliases=aliases,
        compiler_params=pltpu.CompilerParams(
            collective_id=number, has_side_effects=True, vmem_limit_bytes=BIG
        ),
    )(*items, *cut_in)


def scatter_kernel(
    n_dp, n_expert, n_arrays, items, n_cut, n_out, cuts, puts, middle, rings, n_rings, *refs
):
    n_items = len(items)
    z, j, chip, core = place_of()
    chips = n_expert // 2
    square = chips == 4
    to_chip, from_chip = other_chips(chip, chips)
    refs = list(refs)

    def take(count):
        taken = refs[:count]
        del refs[:count]
        return taken

    sources, cut_in, targets, cut_out = take(n_arrays), take(n_cut), take(n_arrays), take(n_out)
    ring, got_a, got_b, got_c = take(n_rings), take(n_items), take(n_items), take(n_items)
    transit = take(n_items)
    (
        send_a,
        recv_a,
        send_b,
        recv_b,
        send_c,
        recv_c,
        send_t,
        recv_t,
        local,
        send_x,
        recv_x,
        local_y,
        *stages,
    ) = refs
    greet(n_dp, n_expert)
    mate = (z, chip * 2 + 1 - core)
    order = [3, 1, 2, 0] if square else [*range(1, chips), 0]
    half = n_dp // 2
    low, high = pl.ds(0, half), pl.ds(half, n_dp - half)

    def chip_of(k):
        return to_chip(k) if k else chip

    def source(i, column):
        array, first, rows = items[i]
        return sources[array].at[:, column, pl.ds(first, rows)]

    def to_mate(i, k):
        return remote(
            source(i, chip_of(k) * 2 + 1 - core),
            got_a[i].at[k],
            send_a.at[i, k],
            recv_a.at[i, k],
            mate,
        )

    turn = [0] * n_rings
    loads = []
    for i in range(n_items):
        for k in order:
            loads.append((i, k, turn[rings[i]] % 2))
            turn[rings[i]] += 1

    def load(i, k, at):
        return pltpu.make_async_copy(
            source(i, chip_of(k) * 2 + core), ring[rings[i]].at[at], local.at[rings[i], at]
        )

    def send_near(i, k, part, number):
        return remote(
            got_a[i].at[k, part],
            got_b[i].at[k - 1, part],
            send_b.at[i, number],
            recv_b.at[i, number],
            (z, to_chip(k) * 2 + core),
        )

    def send_over(i, k, part):
        return remote(
            got_a[i].at[3, part],
            transit[i].at[k - 1],
            send_t.at[i, k],
            recv_t.at[i, k],
            (z, to_chip(k) * 2 + core),
        )

    def send_far(i, k):
        return remote(
            got_a[i].at[k],
            got_b[i].at[k - 1],
            send_b.at[i, k],
            recv_b.at[i, k],
            (z, to_chip(k) * 2 + core),
        )

    def along(i, plane, way):
        slot = n_dp - (z - 1) + plane if way else plane - (z + 1)
        return remote(
            got_a[i].at[0, plane],
            got_c[i].at[slot],
            send_c.at[i, plane],
            recv_c.at[i, slot],
            (z - 1 if way else z + 1, j),
        )

    def from_along(i, slot):
        return remote(
            got_c[i].at[slot], got_c[i].at[slot], send_c.at[i, 0], recv_c.at[i, slot], mate
        )

    f32 = jnp.float32

    def add(i, planes, target, terms):
        rows = got_a[i].shape[2]
        per = rows // 16

        def step(n, unused):
            plane = n // per
            at = pl.ds(pl.multiple_of((n % per) * 16, 16), 16)
            total = terms[0](plane, at).astype(f32)
            for term in terms[1:]:
                total = total + term(plane, at).astype(f32)
            target(plane, at, total)
            return unused

        lax.fori_loop(0, planes * per, step, 0)

    def grow(i, k, first, planes, term):
        def target(plane, at, total):
            got_a[i][k, plane + first, at] = total.astype(got_a[i].dtype)

        add(i, planes, target, [lambda plane, at: got_a[i][k, plane + first, at], term])

    for i in range(n_items):
        for k in order:
            to_mate(i, k).start()
    started = 0
    ahead = [0] * n_rings
    for i, k, at in loads:
        if ahead[rings[i]] < 2:
            load(i, k, at).start()
            ahead[rings[i]] += 1
    pairs = cuts(cut_in, cut_out)
    copies = exchange(n_dp, pairs, send_x, recv_x)
    own = [(source(z), target(z)) for source, target in pairs]
    bring, put = moves(own + puts(cut_in, cut_out), stages, local_y)
    for copy in bring:
        copy.start()

    def over_cores(i):
        for n, (item, k, at) in enumerate(loads):
            if item != i:
                continue
            load(i, k, at).wait()
            to_mate(i, k).wait_recv()
            grow(i, k, 0, n_dp, lambda plane, rows: ring[rings[i]][at, plane, rows])
            later = [one for one in loads[n + 1 :] if rings[one[0]] == rings[i]]
            if len(later) >= 2:
                load(*later[1]).start()
            if not k:
                continue
            if not square:
                send_far(i, k).start()
            elif k == 3:
                send_over(i, 1, low).start()
                send_over(i, 2, high).start()
            elif k == 1:
                send_near(i, 1, low, 0).start()
            else:
                send_near(i, 2, high, 1).start()

    def pass_over(i):
        if not square:
            return
        send_over(i, 2, high).wait_recv()
        grow(i, 1, half, n_dp - half, lambda plane, rows: transit[i][1, plane, rows])
        send_near(i, 1, high, 2).start()
        send_over(i, 1, low).wait_recv()
        grow(i, 2, 0, half, lambda plane, rows: transit[i][0, plane, rows])
        send_near(i, 2, low, 3).start()

    def over_chips(i):
        if square:
            send_near(i, 1, low, 0).wait_recv()
            send_near(i, 2, high, 1).wait_recv()
            send_near(i, 1, high, 2).wait_recv()
            send_near(i, 2, low, 3).wait_recv()
        else:
            for k in range(1, chips):
                send_far(i, k).wait_recv()
        heard = 2 if square else chips - 1

        def target(plane, at, total):
            got_a[i][0, plane, at] = total.astype(got_a[i].dtype)

        terms = [lambda plane, at: got_a[i][0, plane, at]]
        for other in range(heard):
            terms.append(lambda plane, at, other=other: got_b[i][other, plane, at])
        add(i, n_dp, target, terms)
        for d in range(n_dp - 1, 0, -1):
            for way in (0, 1):
                plane = z - d if way else z + d

                @pl.when(z == (n_dp - 1 if way else 0))
                def _():
                    along(i, plane, way).start()

    def over_planes(i):
        for d in range(n_dp - 2, 0, -1):
            for way in (0, 1):
                plane = z - d if way else z + d
                slot = n_dp - d if way else d

                @pl.when((plane >= 0) & (z < n_dp - 1) if way else (plane < n_dp) & (z > 0))
                def _():
                    from_along(i, slot).wait_recv()
                    grow(i, 0, plane, 1, lambda unused, at: got_c[i][slot, at])
                    along(i, plane, way).start()

    def finish(i):
        array, first, rows = items[i]

        def here(at):
            return pl.ds(pl.multiple_of(first + at.start, 16), 16)

        def own(unused, at, total):
            targets[array][here(at)] = total

        add(i, 1, own, [lambda unused, at: got_a[i][0, z, at]])
        for slot, arrives in ((0, z > 0), (n_dp, z < n_dp - 1)):

            @pl.when(arrives)
            def _():
                from_along(i, slot).wait_recv()
                add(
                    i,
                    1,
                    own,
                    [
                        lambda unused, at: targets[array][here(at)],
                        lambda unused, at: got_c[i][slot, at],
                    ],
                )

    steps = ((0, over_cores), (1, pass_over), (2, over_chips), (3, over_planes), (4, finish))
    if n_items >= 6:
        quotas = [-(-len(copies) * part // 9) for part in (2, 2, 2, 1, 1, 1)]
    else:
        quotas = [-(-len(copies) // n_items)] * n_items
    quotas += [0] * (n_items + len(steps) - len(quotas))
    for n in range(n_items + len(steps) - 1):
        for copy in copies[sum(quotas[:n]) : sum(quotas[: n + 1])]:
            copy.start()
        for late, step in steps:
            if 0 <= n - late < n_items:
                step(n - late)
        if n == min(1, n_items - 1):
            for one, other in zip(bring, put):
                one.wait()
                other.start()
            middle(cut_in, cut_out)
    for i in range(n_items):
        for k in range(chips):
            to_mate(i, k).wait_send()
        if square:
            for k, part in ((1, low), (2, high)):
                send_over(i, k, part).wait_send()
            for k, part, number in ((1, low, 0), (2, high, 1), (1, high, 2), (2, low, 3)):
                send_near(i, k, part, number).wait_send()
        else:
            for k in range(1, chips):
                send_far(i, k).wait_send()
        for plane in range(n_dp):

            @pl.when(z != plane)
            def _():
                remote(
                    got_a[i].at[0, plane],
                    got_c[i].at[0],
                    send_c.at[i, plane],
                    recv_c.at[i, 0],
                    mate,
                ).wait_send()

    for copy in copies + put:
        copy.wait()


def scatter_call(
    n_dp,
    n_expert,
    arrays,
    splits,
    cut_in,
    cut_shapes,
    cuts,
    number,
    aliases,
    stages,
    puts=nothing,
    middle=nothing,
):
    chips = n_expert // 2
    square = chips == 4
    items = []
    for array, (one, split) in enumerate(zip(arrays, splits)):
        rows = one.shape[2] // split
        items += [(array, first, rows) for first in range(0, one.shape[2], rows)]
    n, m = len(items), len(cut_shapes)
    count = len(arrays)
    dma = pltpu.SemaphoreType.DMA
    anywhere = pl.BlockSpec(memory_space=pl.ANY)
    blocks = [(rows, arrays[array].shape[3]) for array, unused, rows in items]
    kinds = sorted(set(blocks))
    rings = [kinds.index(block) for block in blocks]
    bf16 = jnp.bfloat16
    heard = 2 if square else chips - 1
    return pl.pallas_call(
        functools.partial(
            scatter_kernel,
            n_dp,
            n_expert,
            count,
            items,
            len(cut_in),
            m,
            cuts,
            puts,
            middle,
            rings,
            len(kinds),
        ),
        out_shape=[
            *[jax.ShapeDtypeStruct(one.shape[2:], jnp.float32) for one in arrays],
            *cut_shapes,
        ],
        in_specs=[anywhere] * (count + len(cut_in)),
        out_specs=[pl.BlockSpec(memory_space=pltpu.VMEM)] * count + [anywhere] * m,
        scratch_shapes=[
            *[pltpu.VMEM((2, n_dp, *kind), bf16) for kind in kinds],
            *[pltpu.VMEM((chips, n_dp, *block), bf16) for block in blocks],
            *[pltpu.VMEM((heard, n_dp, *block), bf16) for block in blocks],
            *[pltpu.VMEM((n_dp + 1, *block), bf16) for block in blocks],
            *[pltpu.VMEM((2, n_dp // 2, *(block if square else (16, 128))), bf16) for block in blocks],
            dma((n, chips)),
            dma((n, chips)),
            dma((n, chips)),
            dma((n, chips)),
            dma((n, n_dp)),
            dma((n, n_dp + 1)),
            dma((n, 3)),
            dma((n, 3)),
            dma((len(kinds), 2)),
            dma((16, n_dp)),
            dma((16, n_dp)),
            dma((max(len(stages), 16), 2)),
            *[pltpu.VMEM(stage, jnp.bfloat16) for stage in stages],
        ],
        input_output_aliases=aliases,
        compiler_params=pltpu.CompilerParams(
            collective_id=number, has_side_effects=True, vmem_limit_bytes=62 * 1024 * 1024
        ),
    )(*arrays, *cut_in)


def scatter_all(
    n_dp,
    n_expert,
    items,
    splits,
    cut_in,
    cut_shapes,
    cuts,
    number,
    aliases,
    stages,
    puts=nothing,
    middle=nothing,
):
    chips = n_expert // 2
    blocks = (2 * chips - 1 if chips != 4 else 7) * n_dp + n_dp + 3
    need = sum(blocks * item.shape[2] * item.shape[3] * 2 for item in items)
    kinds = {(item.shape[2] // split, item.shape[3]) for item, split in zip(items, splits)}
    need += sum(2 * n_dp * kind[0] * kind[1] * 2 for kind in kinds)
    need += sum(stage[0] * stage[1] * stage[2] * 2 for stage in stages)
    pieces = -(-need // (61 * 1024 * 1024))
    tiles = [item.shape[3] // 128 for item in items]
    results = [[] for item in items]
    extra = []
    for piece in range(pieces):
        ends = [(t * piece // pieces * 128, t * (piece + 1) // pieces * 128) for t in tiles]
        used = [i for i, (low, high) in enumerate(ends) if high > low]
        first = piece == 0
        outs = scatter_call(
            n_dp,
            n_expert,
            [items[i][..., ends[i][0] : ends[i][1]] if pieces > 1 else items[i] for i in used],
            [splits[i] for i in used],
            cut_in if first else [],
            cut_shapes if first else [],
            cuts if first else nothing,
            number + piece,
            {len(used) + a: len(used) + b for a, b in aliases} if first else {},
            stages if first else [],
            puts if first else nothing,
            middle if first else nothing,
        )
        for i, out in zip(used, outs):
            results[i].append(out)
        if first:
            extra = outs[len(used) :]
    return [one[0] if len(one) == 1 else jnp.concatenate(one, axis=1) for one in results], extra


def dot(left, right, dims):
    return lax.dot_general(
        left, right, ((dims[:1], dims[1:]), ((), ())), preferred_element_type=jnp.float32
    )


def picks(slots_ref, number):
    pair = slots_ref.shape[2]
    rows = lax.broadcasted_iota(jnp.int32, (2 * CAP, pair), 0)
    return [slots_ref[0, e : e + 1, :] == rows for e in range(number)]


def pick_kernel(number, experts_all, slots_ref, x_ref, g_ref, router_ref, rows_ref, grows_ref, gates_ref):
    chosen = picks(slots_ref, number)
    pick = jnp.concatenate(chosen, axis=0).astype(jnp.bfloat16)
    size = 2 * CAP
    x = x_ref[...]
    logits = dot(router_ref[...], x, (0, 1))
    names = lax.broadcasted_iota(jnp.int32, logits.shape, 0)
    logits = jnp.where(names < experts_all, logits, -1e30)
    weights = jnp.exp(logits - jnp.max(logits, axis=0, keepdims=True))
    probs = weights / jnp.sum(weights, axis=0, keepdims=True)
    for e in range(number):
        gate = jnp.sum(jnp.where(chosen[e], probs[e : e + 1, :], 0.0), axis=1, keepdims=True)
        gates_ref[e] = jnp.broadcast_to(gate, (size, 128))
    picked = dot(pick, x, (1, 0)).astype(jnp.bfloat16)
    for e in range(number):
        rows_ref[e] = picked[e * size : (e + 1) * size]
    picked = dot(pick, g_ref[...], (1, 0)).astype(jnp.bfloat16)
    for e in range(number):
        grows_ref[e] = picked[e * size : (e + 1) * size]


def expert_kernel(steps, half, n_weights, n_into, n_pack, names_ref, x_ref, g_ref, gates_ref, *refs):
    weights, refs = refs[:n_weights], refs[n_weights:]
    down_ref, refs = refs[0], refs[1 + n_into :]
    (
        y_ref,
        dx_ref,
        probs_ref,
        dgate_ref,
        dup_ref,
        ddown_ref,
        *pack_refs,
        sum_gate,
        sum_up,
    ) = refs
    bf16 = jnp.bfloat16
    g = g_ref[0]
    rows, width = x_ref.shape[1:]
    part = dgate_ref.shape[2]
    gate = gates_ref[0][:, :1]
    if n_weights == 2:
        piece = 512
        gate_ref, up_ref = weights
        gate_mid = dot(x_ref[0], gate_ref[0], (1, 0))
        up_mid = dot(x_ref[0], up_ref[0], (1, 0))
        spans = [
            (pl.ds(at, piece), gate_ref, up_ref, pl.ds(at, piece), pl.ds(0, part), pl.ds(0, part))
            for at in range(0, width, piece)
        ]
    else:
        piece = width // n_weights
        spans = []
        gate_mid = up_mid = 0.0
        for n, ref in enumerate(weights):
            span = pl.ds(pl.multiple_of(names_ref[1 + n], piece), piece)
            x_part = x_ref[0, :, span]
            gate_mid = gate_mid + dot(x_part, ref[0, :, :part], (1, 0))
            up_mid = up_mid + dot(x_part, ref[0, :, part:], (1, 0))
            spans.append((span, ref, ref, pl.ds(0, piece), pl.ds(0, part), pl.ds(part, part)))
    sigmoid = 1.0 / (1.0 + jnp.exp(-gate_mid))
    silu = gate_mid * sigmoid
    hidden = silu * up_mid
    hidden_low = hidden.astype(bf16)
    grad_plain = dot(g, down_ref[0], (1, 1))
    grad_gates = jnp.sum(grad_plain * hidden_low.astype(jnp.float32), axis=1, keepdims=True)
    high = grad_gates.astype(bf16).astype(jnp.float32)
    lane = lax.broadcasted_iota(jnp.int32, (rows, 128), 1)
    name = names_ref[0] + pl.program_id(0)
    probs_ref[0] = (
        jnp.where(lane == name, high, 0.0) + jnp.where(lane == name + half, grad_gates - high, 0.0)
    ).astype(bf16)
    grad_hidden = grad_plain * gate
    grad_gate = (
        grad_hidden * up_mid * sigmoid * (1.0 + gate_mid * (1.0 - sigmoid))
    ).astype(bf16)
    grad_up = (grad_hidden * silu).astype(bf16)
    scaled = (hidden * gate).astype(bf16)
    for at in range(0, width, piece):
        y_ref[0, :, at : at + piece] = (
            dot(hidden_low, down_ref[0, :, at : at + piece], (1, 0)) * gate
        ).astype(bf16)
    for span, gate_ref, up_ref, here, gate_columns, up_columns in spans:
        dx_ref[0, :, span] = (
            dot(grad_gate, gate_ref[0, here, gate_columns], (1, 1))
            + dot(grad_up, up_ref[0, here, up_columns], (1, 1))
        ).astype(bf16)
    step = pl.program_id(1)
    for span, *unused in spans:
        x_part = x_ref[0, :, span]
        here_gate = dot(x_part, grad_gate, (0, 0))
        here_up = dot(x_part, grad_up, (0, 0))
        here_down = dot(scaled, g_ref[0, :, span], (0, 0))
        if steps == 1:
            dgate_ref[0, span, :] = here_gate.astype(bf16)
            dup_ref[0, span, :] = here_up.astype(bf16)
            ddown_ref[0, :, span] = here_down
            continue

        @pl.when(step == 0)
        def _():
            sum_gate[span, :] = here_gate
            sum_up[span, :] = here_up
            ddown_ref[0, :, span] = here_down

        @pl.when(step > 0)
        def _():
            sum_gate[span, :] += here_gate
            sum_up[span, :] += here_up
            ddown_ref[0, :, span] += here_down

        @pl.when(step == steps - 1)
        def _():
            dgate_ref[0, span, :] = sum_gate[span, :].astype(bf16)
            dup_ref[0, span, :] = sum_up[span, :].astype(bf16)

    if n_pack:

        @pl.when((step == steps - 1) & (pl.program_id(0) < n_pack))
        def _():
            pack_ref = pack_refs[0]
            depth = pack_ref.shape[2]
            for plane in range(pack_ref.shape[0]):
                here = pl.ds(plane * depth, depth)
                pack_ref[plane, 0, :, :part] = dgate_ref[0, here, :]
                pack_ref[plane, 0, :, part:] = dup_ref[0, here, :]


def put_back(number, slots_ref, pairs):
    pick = jnp.concatenate(picks(slots_ref, number), axis=0).astype(jnp.bfloat16)
    piece = 512
    for source, target, first in pairs:
        width = source.shape[2]
        for at in range(0, width, piece):
            size = min(piece, width)
            part = source[:, :, at : at + size].reshape(-1, size)
            target[:, first + at : first + at + size] = dot(pick, part, (0, 0)).astype(
                jnp.bfloat16
            )


def place_back_kernel(number, slots_ref, dx_ref, probs_ref, back_ref):
    put_back(number, slots_ref, [(dx_ref, back_ref, 0), (probs_ref, back_ref, dx_ref.shape[2])])


def place_out_kernel(number, slots_ref, y_ref, out_ref):
    put_back(number, slots_ref, [(y_ref, out_ref, 0)])


def place_out(slots, y, out):
    pairs, number, pair = slots.shape
    pltpu.emit_pipeline(
        functools.partial(place_out_kernel, number),
        grid=(pairs,),
        in_specs=[
            pl.BlockSpec((1, number, pair), lambda p: (p, 0, 0)),
            pl.BlockSpec((number, 2 * CAP, D), lambda p: (0, p, 0)),
        ],
        out_specs=[pl.BlockSpec((pair, D), lambda p: (p, 0))],
    )(slots, y, out)


def pick_shapes(number, pairs):
    bf16 = jnp.bfloat16
    size = 2 * CAP
    return [
        jax.ShapeDtypeStruct((number, pairs * size, D), bf16),
        jax.ShapeDtypeStruct((number, pairs * size, D), bf16),
        jax.ShapeDtypeStruct((number, pairs * size, 128), jnp.float32),
    ]


def pick_rows(number, experts_all, slots, x_all, g_all, router, rows, grows, gates):
    pairs, _, pair = slots.shape
    size = 2 * CAP
    tokens = pl.BlockSpec((pair, D), lambda p: (p, 0))
    picked = pl.BlockSpec((number, size, D), lambda p: (0, p, 0))
    pltpu.emit_pipeline(
        functools.partial(pick_kernel, number, experts_all),
        grid=(pairs,),
        in_specs=[
            pl.BlockSpec((1, number, pair), lambda p: (p, 0, 0)),
            tokens,
            tokens,
            pl.BlockSpec(router.shape, lambda p: (0, 0)),
        ],
        out_specs=[picked, picked, pl.BlockSpec((number, size, 128), lambda p: (0, p, 0))],
    )(slots, x_all, g_all, router, rows, grows, gates)


def expert_call(names, half, low, number, rows, grows, gates, weights, down, into=(), pack=()):
    total, depth, _ = rows.shape
    part = down.shape[1]
    size = depth
    while size > 768:
        size //= 2
    steps = depth // size
    bf16 = jnp.bfloat16
    f32 = jnp.float32

    def from_rows(width):
        return pl.BlockSpec((1, size, width), lambda e, r: (e + low, r, 0))

    def whole(*shape):
        return pl.BlockSpec((1, *shape), lambda e, r: (e, 0, 0))

    def from_whole(*shape):
        return pl.BlockSpec((1, *shape), lambda e, r: (e + low, 0, 0))

    packed = [
        pl.BlockSpec(
            (planes, 1, D // planes, 2 * part),
            lambda e, r, n=n: (0, lax.min(e, n - 1), 0, 0),
        )
        for n, planes in ([pack] if pack else [])
    ]
    keep = (D, part) if steps > 1 else (16, 128)
    return pl.pallas_call(
        functools.partial(
            expert_kernel, steps, half, len(weights), len(into), pack[0] if pack else 0
        ),
        grid=(number, steps),
        in_specs=[
            pl.BlockSpec(memory_space=pltpu.SMEM),
            from_rows(D),
            from_rows(D),
            from_rows(128),
            *[(from_whole if len(weights) == 2 else whole)(*one.shape[1:]) for one in weights],
            from_whole(part, D),
            *[pl.BlockSpec(memory_space=pl.ANY)] * len(into),
        ],
        out_specs=[
            from_rows(D),
            from_rows(D),
            from_rows(128),
            whole(D, part),
            whole(D, part),
            from_whole(part, D),
            *packed,
        ],
        out_shape=[
            jax.ShapeDtypeStruct((total, depth, D), bf16),
            jax.ShapeDtypeStruct((total, depth, D), bf16),
            jax.ShapeDtypeStruct((total, depth, 128), bf16),
            jax.ShapeDtypeStruct((number, D, part), bf16),
            jax.ShapeDtypeStruct((number, D, part), bf16),
            jax.ShapeDtypeStruct((total, part, D), f32),
            *[
                jax.ShapeDtypeStruct((planes, n, D // planes, 2 * part), bf16)
                for n, planes in ([pack] if pack else [])
            ],
        ],
        input_output_aliases={
            5 + len(weights) + i: out for i, out in zip(range(len(into)), (0, 1, 2, 5))
        },
        scratch_shapes=[pltpu.VMEM(keep, f32), pltpu.VMEM(keep, f32)],
        compiler_params=pltpu.CompilerParams(vmem_limit_bytes=BIG),
    )(names, rows, grows, gates, *weights, down, *into)


def place_back(slots, dx, probs):
    pairs, number, pair = slots.shape
    size = 2 * CAP

    def rows(one):
        return pl.BlockSpec((number, size, one.shape[2]), lambda p: (0, p, 0))

    return pl.pallas_call(
        functools.partial(place_back_kernel, number),
        grid=(pairs,),
        in_specs=[pl.BlockSpec((1, number, pair), lambda p: (p, 0, 0)), rows(dx), rows(probs)],
        out_specs=pl.BlockSpec((pair, D + 128), lambda p: (p, 0)),
        out_shape=jax.ShapeDtypeStruct((pairs * pair, D + 128), jnp.bfloat16),
        compiler_params=pltpu.CompilerParams(vmem_limit_bytes=BIG),
    )(slots, dx, probs)


def core_back_kernel(
    scale,
    q_ref,
    k_ref,
    v_ref,
    grad_ref,
    probs_ref,
    cos_ref,
    sin_ref,
    q_raw_ref,
    k_raw_ref,
    q_inverse_ref,
    k_inverse_ref,
    q_gain_ref,
    k_gain_ref,
    grad_q_ref,
    grad_k_ref,
    grad_v_ref,
    grad_q_gain_ref,
    grad_k_gain_ref,
    q_turned,
    k_turned,
):
    bf16 = jnp.bfloat16
    cosine, sine = cos_ref[...], sin_ref[...]
    for head in range(HEADS):
        at = slice(head * HD, (head + 1) * HD)
        probs, grad = probs_ref[head], grad_ref[:, at]
        weights = dot(grad, v_ref[:, at], (1, 1))
        scores = probs * (weights - jnp.sum(probs * weights, axis=1, keepdims=True))
        scores = scores.astype(bf16)
        grad_v_ref[:, at] = dot(probs.astype(bf16), grad, (0, 0)).astype(bf16)
        for other_ref, side, turned in ((k_ref, 1, q_turned), (q_ref, 0, k_turned)):
            rope = dot(scores, other_ref[:, at], (side, 0)) * scale
            turned[:, at] = rope * cosine + pltpu.roll(rope, HD // 2, 1) * sine
    for turned, raw_ref, inverse_ref, gain_ref, out_ref, out_gain_ref in (
        (q_turned, q_raw_ref, q_inverse_ref, q_gain_ref, grad_q_ref, grad_q_gain_ref),
        (k_turned, k_raw_ref, k_inverse_ref, k_gain_ref, grad_k_ref, grad_k_gain_ref),
    ):
        grad, raw, inverse = turned[...], raw_ref[...], inverse_ref[...]
        scaled = grad * gain_ref[...]
        inner = jnp.mean(scaled * raw, axis=1, keepdims=True)
        out_ref[...] = (inverse * scaled - raw * (inverse * inverse * inverse) * inner).astype(bf16)
        out_gain_ref[...] = jnp.sum(grad * raw * inverse, axis=0, keepdims=True)


def core_back(scale, q, k, v, grad, probs, cosine, sine, q_raw, k_raw, q_inverse, k_inverse, gains):
    count, depth = q.shape
    low = jax.ShapeDtypeStruct((count, depth), jnp.bfloat16)
    gain = jax.ShapeDtypeStruct((1, depth), jnp.float32)
    return pl.pallas_call(
        functools.partial(core_back_kernel, scale),
        out_shape=[low, low, low, gain, gain],
        scratch_shapes=[pltpu.VMEM((count, depth), jnp.float32)] * 2,
        compiler_params=pltpu.CompilerParams(vmem_limit_bytes=BIG),
    )(
        q,
        k,
        v,
        grad,
        probs,
        jnp.concatenate([cosine, cosine], axis=1),
        jnp.concatenate([sine, -sine], axis=1),
        q_raw,
        k_raw,
        q_inverse,
        k_inverse,
        *[one[None] for one in gains],
    )


def through_kernel(count, *refs):
    lefts, weight_ref, out_ref = refs[:count], refs[count], refs[count + 1]
    for i in range(count):

        @pl.when(pl.program_id(1) == i)
        def _():
            part = dot(lefts[i][...], weight_ref[0], (1, 1))
            if i:
                part = part + out_ref[...]
            out_ref[...] = part


def through(lefts, weights, first):
    count, (rows, depth) = len(lefts), lefts[0].shape
    piece = 512
    return pl.pallas_call(
        functools.partial(through_kernel, count),
        grid=(depth // piece, count),
        in_specs=[
            *[pl.BlockSpec((rows, depth), lambda c, i: (0, 0))] * count,
            pl.BlockSpec((1, piece, depth), lambda c, i: (i + first, c, 0)),
        ],
        out_specs=pl.BlockSpec((rows, piece), lambda c, i: (0, c)),
        out_shape=jax.ShapeDtypeStruct((rows, depth), jnp.float32),
        compiler_params=pltpu.CompilerParams(vmem_limit_bytes=BIG),
    )(*lefts, weights)


def outer_kernel(which, n_left, *refs):
    lefts, rights = refs[:n_left], refs[n_left : n_left + len(which)]
    piece = 512
    for left, right, out_ref in zip(which, rights, refs[n_left + len(which) :]):
        for at in range(0, out_ref.shape[1], piece):
            out_ref[:, at : at + piece] = dot(
                lefts[left][...], right[:, at : at + piece], (0, 0)
            ).astype(out_ref.dtype)


def outer(lefts, rights, which):
    rows, depth = lefts[0].shape
    piece = 256
    return pl.pallas_call(
        functools.partial(outer_kernel, which, len(lefts)),
        grid=(depth // piece,),
        in_specs=[
            *[pl.BlockSpec((rows, piece), lambda c: (0, c))] * len(lefts),
            *[pl.BlockSpec((rows, depth), lambda c: (0, 0))] * len(rights),
        ],
        out_specs=[pl.BlockSpec((piece, depth), lambda c: (c, 0))] * len(rights),
        out_shape=[jax.ShapeDtypeStruct((depth, depth), jnp.bfloat16)] * len(rights),
        compiler_params=pltpu.CompilerParams(vmem_limit_bytes=BIG),
    )(*lefts, *rights)


def widen_kernel(*refs):
    for source, target in zip(refs[:2], refs[-2:]):
        target[...] = source[...].astype(jnp.float32)


def widen(low, high, values, into=()):
    number, rows, columns = values[0].shape
    block = pl.BlockSpec((1, rows, columns), lambda e: (e + low, 0, 0))
    return pl.pallas_call(
        widen_kernel,
        grid=(high - low,),
        in_specs=[block] * 2 + [pl.BlockSpec(memory_space=pl.ANY)] * len(into),
        out_specs=[block] * 2,
        out_shape=[jax.ShapeDtypeStruct(one.shape, jnp.float32) for one in values],
        input_output_aliases={2 + i: i for i in range(len(into))},
        compiler_params=pltpu.CompilerParams(vmem_limit_bytes=BIG),
    )(*values, *into)


def widen_pieces_kernel(low, n_pieces, offsets_ref, *refs):
    pieces, refs = refs[:n_pieces], refs[n_pieces + 2 :]
    targets, wide, sems = refs[:2], refs[2], refs[3]
    part = wide.shape[4]
    copies = []
    for k, piece in enumerate(pieces):
        columns = pl.ds(pl.multiple_of(offsets_ref[k], part), part)
        for n in range(2):
            wide[k, n] = piece[:, :, n * part : (n + 1) * part].astype(jnp.float32)
            copy = pltpu.make_async_copy(
                wide.at[k, n], targets[n].at[pl.ds(low, piece.shape[0]), :, columns], sems.at[k, n]
            )
            copy.start()
            copies.append(copy)
    for copy in copies:
        copy.wait()


def widen_pieces(offsets, low, pieces, into):
    size, rows, columns = pieces[0].shape
    anywhere = pl.BlockSpec(memory_space=pl.ANY)
    count = len(pieces)
    return pl.pallas_call(
        functools.partial(widen_pieces_kernel, low, count),
        in_specs=[
            pl.BlockSpec(memory_space=pltpu.SMEM),
            *[pl.BlockSpec(memory_space=pltpu.VMEM)] * count,
            anywhere,
            anywhere,
        ],
        out_specs=[anywhere, anywhere],
        out_shape=[jax.ShapeDtypeStruct(one.shape, one.dtype) for one in into],
        scratch_shapes=[
            pltpu.VMEM((count, 2, size, rows, columns // 2), jnp.float32),
            pltpu.SemaphoreType.DMA((count, 2)),
        ],
        input_output_aliases={1 + count: 0, 2 + count: 1},
        compiler_params=pltpu.CompilerParams(vmem_limit_bytes=BIG),
    )(offsets, *pieces, *into)


def shards(
    n_dp,
    n_expert,
    tokens,
    cotangent,
    lengths,
    routes,
    w_query,
    w_key,
    w_value,
    w_out,
    w_router,
    gain_attn,
    gain_query,
    gain_key,
    gain_mlp,
    w_gate,
    w_up,
    w_down,
):
    groups = n_dp * n_expert
    bf16 = jnp.bfloat16
    number = w_gate.shape[0]
    ff = w_gate.shape[2]
    part = ff // n_dp
    experts_all = w_router.shape[1]
    width = 128
    small = jnp.concatenate(
        [
            w_router,
            gain_attn[:, None],
            gain_query[:, None],
            gain_key[:, None],
            gain_mlp[:, None],
            jnp.zeros((w_router.shape[0], width - experts_all - 4), bf16),
        ],
        axis=1,
    )
    hits = jnp.any(
        routes[:, :, None] == jnp.arange(width, dtype=jnp.int32)[None, None, :], axis=1
    ).astype(bf16)
    count = tokens.shape[0]
    rows_each = w_query.shape[0]
    extras = jnp.concatenate([hits, jnp.pad(small, ((0, count - rows_each), (0, 0)))], axis=1)
    weights = jnp.stack([w_query, w_key, w_value, w_out])
    depth = w_gate.shape[1]
    early = number // 4
    beside = early + number // 8
    late = number - number // 4
    back_beside = number // 8
    back_third = back_beside + max(number // 4, 1)
    back_late = back_third + number // 4
    me = lax.axis_index("dp")
    cut_shape = jax.ShapeDtypeStruct((number, n_dp * depth, part), bf16)

    def row_block(size):
        return lambda ref, block: ref.at[pl.ds(pl.multiple_of(block * size, 16), size)]

    def columns_at(at):
        return pl.ds(pl.multiple_of(at * part, part), part)

    def rows_at(at):
        return pl.ds(pl.multiple_of(at * depth, depth), depth)

    def recut(low, high):
        def cuts(ins, outs):
            def pair(n):
                chosen = pl.ds(low, high - low)
                return (
                    lambda to: ins[n].at[chosen, :, columns_at(to)],
                    lambda at: outs[n].at[chosen, rows_at(at)],
                )

            return [pair(0), pair(1)]

        return cuts

    to_plane, from_plane = partners(me, n_dp)

    def permuted(pieces, chained=False):
        got = []
        for k, piece in enumerate(pieces, 1):
            if chained and got:
                piece, last = lax.optimization_barrier((piece, got.pop()))
                got.append(last)
            paths = [(i, partners(i, n_dp)[0](k)) for i in range(n_dp)]
            got.append(lax.ppermute(piece, "dp", paths))
        return got

    def cut_pieces(low, high, first_k, ins, outs):
        to, unused = partners(lax.axis_index("dp"), n_dp)
        pairs = []
        for k, piece in enumerate(outs, first_k):
            for n in range(2):
                source = ins[n].at[pl.ds(low, high - low), :, columns_at(to(k))]
                pairs.append((source, piece.at[:, :, pl.ds(n * part, part)]))
        return pairs

    def piece_shapes(size, first_k):
        shape = jax.ShapeDtypeStruct((size, depth, 2 * part), bf16)
        return [shape] * (n_dp - first_k if size else 0)

    def stages(*sizes):
        return [(size, depth, part) for size in sizes]

    soon_shapes = piece_shapes(beside - early, 1)
    late_shapes = piece_shapes(number - late, 0)
    n_soon = len(soon_shapes)

    weights_all, extras_all, gate_early, up_early, *pieces = gather_call(
        n_dp,
        n_expert,
        [weights, extras],
        [
            jax.ShapeDtypeStruct((4, groups * rows_each, D), bf16),
            jax.ShapeDtypeStruct((groups * count, 2 * width), bf16),
        ],
        [
            lambda ref, block: ref.at[
                :, pl.ds(pl.multiple_of(block * rows_each, 16), rows_each)
            ],
            row_block(count),
        ],
        [w_gate, w_up],
        [cut_shape, cut_shape, *soon_shapes, *late_shapes],
        recut(0, early),
        {},
        0,
        stages(
            *[early] * 2,
            *[beside - early] * (2 * n_soon),
            *[number - late] * (2 * n_dp),
        ),
        lambda ins, outs: cut_pieces(early, beside, 1, ins, outs[2 : 2 + n_soon])
        + cut_pieces(late, number, 0, ins, outs[2 + n_soon :]),
    )
    soon_pieces, late_pieces = pieces[:n_soon], pieces[n_soon:]
    small_all = (
        extras_all[:, width:].reshape(groups, count, width)[:, :rows_each].reshape(-1, width)
    )
    hits_all = extras_all[:, :experts_all]
    router_weight = small_all[:, :experts_all]
    gains = small_all[:, experts_all : experts_all + 4].astype(jnp.float32)
    attn_gain, query_gain, key_gain, mlp_gain = (gains[:, i] for i in range(4))
    inputs = tokens.astype(jnp.float32)
    segment, position, places = layout(lengths[0], count)
    half = HD // 2
    freq = 10000.0 ** (-2.0 * jnp.arange(half, dtype=jnp.float32) / HD)
    angle = position.astype(jnp.float32)[:, None] * freq[None, :]
    cosine = jnp.cos(angle)[:, None, :]
    sine = jnp.sin(angle)[:, None, :]
    scale = HD ** (-0.5)
    normed, attn_inverse = rms_forward(inputs, attn_gain)
    normed_low = normed.astype(bf16)
    query_raw = product(normed_low, weights_all[0], "td,de->te")
    key_raw = product(normed_low, weights_all[1], "td,de->te")
    value_low = product(normed_low, weights_all[2], "td,de->te").astype(bf16)
    query_normed, query_inverse = rms_forward(query_raw, query_gain)
    key_normed, key_inverse = rms_forward(key_raw, key_gain)
    query_low = rotate(query_normed, cosine, sine).astype(bf16).reshape(count, HEADS, HD)
    key_low = rotate(key_normed, cosine, sine).astype(bf16).reshape(count, HEADS, HD)
    value_heads = value_low.reshape(count, HEADS, HD)
    allowed = (segment[:, None] == segment[None, :]) & (places[None, :] <= places[:, None])
    scores = product(query_low, key_low, "qhd,khd->hqk") * scale
    scores = jnp.where(allowed[None], scores, -1e30)
    probs = jax.nn.softmax(scores, axis=-1)
    probs_low = probs.astype(bf16)
    attended_low = product(probs_low, value_heads, "hqk,khd->qhd").reshape(count, D).astype(bf16)
    middle = inputs + product(attended_low, weights_all[3], "td,de->te")
    mlp_normed, mlp_inverse = rms_forward(middle, mlp_gain)
    mlp_low = mlp_normed.astype(bf16)
    router = jax.nn.softmax(product(mlp_low, router_weight, "td,de->te"), axis=-1)

    first = lax.axis_index("expert") * number
    hit = lax.dynamic_slice_in_dim(hits_all, first, number, 1).reshape(groups, count, number)
    before = jnp.tril(jnp.ones((count, count), bf16), -1)
    slot = product(before, hit, "ts,bse->bet").astype(jnp.int32)
    slot = jnp.where(jnp.transpose(hit, (0, 2, 1)) > 0, slot, -1)
    slot = slot.reshape(groups // 2, 2, number, count)
    shift = jnp.array([0, CAP], jnp.int32)[None, :, None, None]
    slots = jnp.transpose(jnp.where(slot < 0, -1, slot + shift), (0, 2, 1, 3))
    slots = slots.reshape(groups // 2, number, 2 * count)
    router_own = jnp.pad(
        jnp.roll(router_weight, -first, axis=1), ((0, 0), (0, width - experts_all))
    )
    if n_soon:
        mlp_low, *soon_pieces = lax.optimization_barrier((mlp_low, *permuted(soon_pieces)))

    def put_weights(ins, outs):
        chosen = pl.ds(early, beside - early)
        unused, heard = partners(lax.axis_index("dp"), n_dp)
        pairs = []
        if beside > early:
            own = lax.axis_index("dp")
            for n in range(2):
                source = ins[n].at[chosen, :, columns_at(own)]
                pairs.append((source, outs[n].at[chosen, rows_at(own)]))
        for k, piece in enumerate(ins[6:], 1):
            for n in range(2):
                columns = piece.at[:, :, pl.ds(n * part, part)]
                pairs.append((columns, outs[n].at[chosen, rows_at(heard(k))]))
        return pairs

    def pick_all(items, ins, outs):
        pick_rows(number, experts_all, ins[4], *items, ins[5], *outs[2:])

    unused, unused, gate_cut, up_cut, rows, grows, gates = gather_call(
        n_dp,
        n_expert,
        [mlp_low, cotangent],
        [jax.ShapeDtypeStruct((groups * count, D), bf16)] * 2,
        [row_block(count)] * 2,
        [w_gate, w_up, gate_early, up_early, slots, router_own, *soon_pieces],
        [cut_shape, cut_shape, *pick_shapes(number, groups // 2)],
        recut(beside, late),
        {4: 2, 5: 3},
        1,
        stages(*[late - beside] * 2, *[beside - early] * (2 * n_dp if n_soon else 0)),
        put_weights,
        pick_all,
    )
    *late_pieces, rows = lax.optimization_barrier((*late_pieces, rows))
    late_pieces = [late_pieces[0], *permuted(late_pieces[1:])]
    packing = back_beside > 0 and depth == 512
    *outs, gate_soon, up_soon, down_soon = expert_call(
        first[None],
        experts_all,
        0,
        late,
        rows,
        grows,
        gates,
        [gate_cut, up_cut],
        w_down,
        pack=(back_beside, n_dp) if packing else (),
    )
    if packing:
        *outs, gate_soon, up_soon, down_soon, packed = [*outs, gate_soon, up_soon, down_soon]
    offsets = [from_plane(k) * depth for k in range(n_dp)]
    weighted, grad_rows, grad_gates, gate_rest, up_rest, grad_down_part = expert_call(
        jnp.stack([first + late, *offsets]),
        experts_all,
        late,
        number - late,
        rows,
        grows,
        gates,
        late_pieces,
        w_down,
        [*outs, down_soon],
    )
    part_back = place_back(slots, grad_rows, grad_gates)

    def ways(low, high, at, ins, outs):
        def pair(e, n):
            return (
                lambda to: ins[n].at[pl.ds(e, 1), rows_at(to)],
                lambda here: outs[n].at[pl.ds(e + at, 1), :, columns_at(here)],
            )

        return [pair(e, n) for e in range(low, high) for n in range(2)]

    def cut_grads(low, high, ins, outs):
        to, unused = partners(lax.axis_index("dp"), n_dp)
        pairs = []
        for k, piece in enumerate(outs):
            for n in range(2):
                source = ins[n].at[pl.ds(low, high - low), rows_at(to(k))]
                pairs.append((source, piece.at[:, :, pl.ds(n * part, part)]))
        return pairs

    pieces = []
    if back_beside:
        for k in range(n_dp):
            if packing:
                piece = lax.dynamic_index_in_dim(packed, to_plane(k), 0, False)
            else:
                piece = jnp.concatenate(
                    [
                        lax.dynamic_slice_in_dim(
                            one[:back_beside], to_plane(k) * depth, depth, 1
                        )
                        for one in (gate_soon, up_soon)
                    ],
                    axis=2,
                )
            pieces.append(piece)
        ahead = lax.optimization_barrier((*pieces[1:], *late_pieces[1:]))
        pieces = [pieces[0], *permuted(ahead[: n_dp - 1])]
        part_back, *pieces = lax.optimization_barrier((part_back, *pieces))
    way_shapes = [jax.ShapeDtypeStruct((number, depth, ff), bf16)] * 2
    piece_shape = jax.ShapeDtypeStruct((back_late - back_third, depth, 2 * part), bf16)
    (back,), (gate_third, up_third, part_out, *later_pieces) = scatter_all(
        n_dp,
        n_expert,
        [part_back.reshape(n_dp, n_expert, count, D + width)],
        [4],
        [gate_soon, up_soon, slots, weighted],
        [
            *way_shapes,
            jax.ShapeDtypeStruct((groups * count, D), bf16),
            *[piece_shape] * n_dp,
        ],
        lambda ins, outs: ways(back_beside, back_third, 0, ins, outs),
        8,
        (),
        stages(
            *[1] * (2 * (back_third - back_beside)),
            *[back_late - back_third] * (2 * n_dp),
        ),
        lambda ins, outs: cut_grads(back_third, back_late, ins, outs[3:]),
        lambda ins, outs: place_out(ins[2], ins[3], outs[2]),
    )
    later_pieces = [later_pieces[0], *permuted(later_pieces[1:])]

    offsets = jnp.stack([from_plane(k) * part for k in range(n_dp)])
    widened = widen(back_beside, back_third, [gate_third, up_third])
    if back_beside:
        widened = widen_pieces(offsets, 0, pieces, widened)
    part_out, *widened = lax.optimization_barrier((part_out, *widened))

    def attention_back(back):
        grad_final = cotangent.astype(jnp.float32)
        grad_mlp = back[:, :D]
        grad_router_probs = back[:, D : D + experts_all] + back[:, D + experts_all :]
        grad_logits = router * (
            grad_router_probs - jnp.sum(router * grad_router_probs, axis=1, keepdims=True)
        )
        grad_logits_low = grad_logits.astype(bf16)
        grad_router_full = product(
            mlp_low, jnp.pad(grad_logits_low, ((0, 0), (0, width - experts_all))), "td,te->de"
        )
        grad_mlp = grad_mlp + product(grad_logits_low, router_weight, "te,de->td")
        grad_middle_part, grad_mlp_gain = rms_backward(middle, mlp_inverse, mlp_gain, grad_mlp)
        grad_middle = grad_final + grad_middle_part
        grad_branch_low = grad_middle.astype(bf16)
        grad_attended = through([grad_branch_low], weights_all, 3).astype(bf16)
        grad_query_low, grad_key_low, grad_value_low, grad_query_gain, grad_key_gain = core_back(
            scale,
            query_low.reshape(count, D),
            key_low.reshape(count, D),
            value_low,
            grad_attended,
            probs,
            cosine[:, 0],
            sine[:, 0],
            query_raw,
            key_raw,
            query_inverse,
            key_inverse,
            (query_gain, key_gain),
        )
        full_grads = outer(
            [attended_low, normed_low],
            [grad_branch_low, grad_value_low, grad_key_low, grad_query_low],
            (0, 1, 1, 1),
        )
        grad_normed = through([grad_query_low, grad_key_low, grad_value_low], weights_all, 0)
        grad_inputs_part, grad_attn_gain = rms_backward(inputs, attn_inverse, attn_gain, grad_normed)
        grad_inputs = grad_middle + grad_inputs_part

        gain_grads = jnp.stack(
            [grad_attn_gain, grad_query_gain[0], grad_key_gain[0], grad_mlp_gain]
        )
        gain_grads = jnp.transpose(gain_grads.reshape(4, groups, rows_each), (1, 0, 2))
        gain_grads = jnp.pad(gain_grads, ((0, 0), (0, 12), (0, width - rows_each)))
        return (
            grad_inputs,
            *full_grads,
            grad_router_full.astype(bf16),
            gain_grads.astype(bf16).reshape(groups * 16, width),
        )

    def unreached(back):
        shapes = [(count, D)] + [(D, D)] * 4 + [(D, width), (groups * 16, width)]
        kinds = [jnp.float32] + [bf16] * 6
        return tuple(jnp.zeros(shape, kind) for shape, kind in zip(shapes, kinds))

    grad_inputs, *weight_grads = lax.cond(lengths[0, 0] > 0, attention_back, unreached, back)

    def blocks_of(value):
        return value.reshape(n_dp, n_expert, -1, value.shape[1])

    sums, (gate_back, up_back) = scatter_all(
        n_dp,
        n_expert,
        [part_out.reshape(n_dp, n_expert, count, D)]
        + [blocks_of(value) for value in weight_grads],
        [2, 1, 1, 1, 2 if rows_each > 16 else 1, 1, 1],
        [gate_soon, up_soon, gate_rest, up_rest],
        way_shapes,
        lambda ins, outs: ways(back_late, late, 0, ins[:2], outs)
        + ways(0, number - late, late, ins[2:], outs),
        16,
        (),
        [],
    )
    summed, grad_out_part, grad_value_part, grad_key_part, grad_query_part, router_part, small = sums
    output = (middle + summed).astype(bf16)
    grad_router_part = router_part[:, :experts_all]
    gain_parts = [small[i, :rows_each] for i in range(4)]
    widened = widen(back_late, number, [gate_back, up_back], widened)
    if back_late > back_third:
        widened = widen_pieces(offsets, back_third, later_pieces, widened)
    grad_gate_part, grad_up_part = widened
    return (
        output,
        grad_inputs,
        grad_query_part,
        grad_key_part,
        grad_value_part,
        grad_out_part,
        grad_router_part,
        gain_parts[0],
        gain_parts[1],
        gain_parts[2],
        gain_parts[3],
        grad_gate_part,
        grad_up_part,
        grad_down_part,
    )


def solution(mesh):
    return jax.shard_map(
        functools.partial(shards, mesh.shape["dp"], mesh.shape["expert"]),
        mesh=mesh,
        in_specs=(
            P(("dp", "expert"), None),
            P(("dp", "expert"), None),
            P(("dp", "expert"), None),
            P(("dp", "expert"), None),
            P(("dp", "expert"), None),
            P(("dp", "expert"), None),
            P(("dp", "expert"), None),
            P(("dp", "expert"), None),
            P(("dp", "expert"), None),
            P(("dp", "expert")),
            P(("dp", "expert")),
            P(("dp", "expert")),
            P(("dp", "expert")),
            P("expert", "dp", None),
            P("expert", "dp", None),
            P("expert", "dp", None),
        ),
        out_specs=(
            P(("dp", "expert"), None),
            P(("dp", "expert"), None),
            P(("dp", "expert"), None),
            P(("dp", "expert"), None),
            P(("dp", "expert"), None),
            P(("dp", "expert"), None),
            P(("dp", "expert"), None),
            P(("dp", "expert")),
            P(("dp", "expert")),
            P(("dp", "expert")),
            P(("dp", "expert")),
            P("expert", "dp", None),
            P("expert", "dp", None),
            P("expert", "dp", None),
        ),
        check_vma=False,
    )
```

```python
import functools

import jax
import jax.numpy as jnp
from jax import lax
from jax.experimental import pallas as pl
from jax.experimental.pallas import tpu as pltpu
from jax.sharding import PartitionSpec as P

D = 2048
HEADS = 16
HD = 128
TOPK = 8
CAP = 24


eps = 1e-05


def product(left, right, form):
    return jnp.einsum(form, left, right, preferred_element_type=jnp.float32)


def rms_forward(values, gain):
    inverse = lax.rsqrt(jnp.mean(values * values, axis=-1, keepdims=True) + eps)
    return (values * inverse * gain, inverse)


def rms_backward(values, inverse, gain, grad):
    scaled = grad * gain
    inner = jnp.mean(scaled * values, axis=-1, keepdims=True)
    grad_values = inverse * scaled - values * (inverse * inverse * inverse) * inner
    grad_gain = jnp.sum(grad * values * inverse, axis=0)
    return (grad_values, grad_gain)


def layout(lengths_row, count):
    places = jnp.arange(count, dtype=jnp.int32)
    ends = jnp.cumsum(lengths_row, dtype=jnp.int32)
    passed = (places[:, None] >= ends[None, :]).astype(jnp.int32)
    segment = jnp.sum(passed, axis=1, dtype=jnp.int32)
    start = jnp.sum(passed * lengths_row[None, :], axis=1, dtype=jnp.int32)
    return (segment, places - start, places)


def rotate(values, cosine, sine):
    count = values.shape[0]
    heads = values.reshape(count, HEADS, HD)
    half = HD // 2
    first = heads[..., :half]
    second = heads[..., half:]
    turned = jnp.concatenate(
        [first * cosine - second * sine, second * cosine + first * sine], axis=-1
    )
    return turned.reshape(count, D)


MESH = pl.DeviceIdType.MESH
BIG = 60 * 1024 * 1024


def place_of():
    z = lax.axis_index("dp")
    j = lax.axis_index("expert")
    return z, j, j // 2, j % 2


def other_chips(chip, chips):
    if chips == 4:
        square = [chip, chip + 1 - 2 * (chip % 2), chip + 2 - 4 * (chip // 2), 3 - chip]
        return lambda k: square[k], lambda k: square[k]
    return lambda k: (chip + k) % chips, lambda k: (chip + chips - k) % chips


def partners(z, n_dp):
    if n_dp == 4:
        pairs = [z, 3 - z, (z + 2) % 4, z + 1 - 2 * (z % 2)]
        return lambda k: pairs[k], lambda k: pairs[k]
    return lambda k: (z + k) % n_dp, lambda k: (z + n_dp - k) % n_dp


def greet(n_dp, n_expert):
    z, j, chip, core = place_of()
    chips = n_expert // 2
    barrier = pltpu.get_barrier_semaphore()
    for k in range(1, n_dp):
        pl.semaphore_signal(
            barrier, inc=1, device_id=((z + k) % n_dp, j), device_id_type=MESH
        )
    for k in range(1, chips):
        other = ((chip + k) % chips) * 2 + core
        pl.semaphore_signal(barrier, inc=1, device_id=(z, other), device_id_type=MESH)
    pl.semaphore_signal(
        barrier, inc=1, device_id=(z, chip * 2 + 1 - core), device_id_type=MESH
    )
    pl.semaphore_wait(barrier, n_dp - 1 + chips - 1 + 1)


def remote(source, target, send, receive, device):
    return pltpu.make_async_remote_copy(
        src_ref=source,
        dst_ref=target,
        send_sem=send,
        recv_sem=receive,
        device_id=device,
        device_id_type=MESH,
    )


def exchange(n_dp, pairs, send, receive):
    z, j, chip, core = place_of()
    to_plane, unused = partners(z, n_dp)
    copies = []
    for i, (source, target) in enumerate(pairs):
        for k in range(1, n_dp):
            to = to_plane(k)
            copies.append(
                remote(source(to), target(z), send.at[i, k], receive.at[i, k], (to, j))
            )
    return copies


def moves(pairs, stages, local):
    if not stages:
        copies = [
            pltpu.make_async_copy(source, target, local.at[i, 0])
            for i, (source, target) in enumerate(pairs)
        ]
        for copy in copies:
            copy.start()
        return [], copies
    bring = [
        pltpu.make_async_copy(source, stages[i], local.at[i, 0])
        for i, (source, target) in enumerate(pairs)
    ]
    put = [
        pltpu.make_async_copy(stages[i], target, local.at[i, 1])
        for i, (source, target) in enumerate(pairs)
    ]
    return bring, put


def nothing(ins, outs):
    return []


def gather_kernel(
    n_dp, n_expert, n_items, places, cuts, puts, finish, n_cut, n_out, n_stages, *refs
):
    z, j, chip, core = place_of()
    chips = n_expert // 2
    square = chips == 4
    to_chip, from_chip = other_chips(chip, chips)
    sources = refs[:n_items]
    cut_in = refs[n_items : n_items + n_cut]
    at = n_items + n_cut
    targets = refs[at : at + n_items]
    cut_out = refs[at + n_items : at + n_items + n_out]
    (
        send_c,
        recv_c,
        send_b,
        recv_b,
        send_a,
        recv_a,
        local,
        send_x,
        recv_x,
        local_y,
        *stages,
    ) = refs[at + n_items + n_out :]
    greet(n_dp, n_expert)
    mate = (z, chip * 2 + 1 - core)
    near = (1, 2) if square else tuple(range(1, chips))

    def slot(i, plane, column):
        return places[i](targets[i], plane * n_expert + column)

    def pass_on(i, plane, source, column, k, chip_to):
        return remote(
            source,
            slot(i, plane, column),
            send_b.at[i, plane, k],
            recv_b.at[i, plane, k],
            (z, chip_to * 2 + core),
        )

    def hand(i, plane, source):
        for k in near:
            pass_on(i, plane, source, j, k, to_chip(k)).start()
        remote(
            source, slot(i, plane, j), send_a.at[i, plane, 0], recv_a.at[i, plane, 0], mate
        ).start()

    def along(i, plane, source, way, step):
        return remote(
            source, slot(i, plane, j), send_c.at[i, way, plane], recv_c.at[i, plane], (z + step, j)
        )

    def at_distance(d, body):
        if d == 0:
            body(z, 0)
            return

        @pl.when(z >= d)
        def _():
            body(z - d, 0)

        @pl.when(z + d < n_dp)
        def _():
            body(z + d, 1)

    for i in range(n_items):

        @pl.when(z < n_dp - 1)
        def _():
            along(i, z, sources[i], 0, 1).start()

        @pl.when(z > 0)
        def _():
            along(i, z, sources[i], 1, -1).start()

        hand(i, z, sources[i])
        pltpu.make_async_copy(sources[i], slot(i, z, j), local.at[i]).start()

    def relay(plane, way):
        step = -1 if way else 1
        for i in range(n_items):
            block = slot(i, plane, j)
            along(i, plane, block, way, step).wait_recv()

            @pl.when(z > 0 if way else z < n_dp - 1)
            def _():
                along(i, plane, block, way, step).start()

            hand(i, plane, block)

    for d in range(1, n_dp):
        at_distance(d, relay)
    pairs = cuts(cut_in, cut_out)
    copies = exchange(n_dp, pairs, send_x, recv_x)
    for copy in copies:
        copy.start()
    own = [(source(z), target(z)) for source, target in pairs]
    bring, put = moves(own + puts(cut_in, cut_out), stages, local_y)
    for copy in bring:
        copy.start()
    for one, other in zip(bring, put):
        one.wait()
        other.start()

    def arrive(i, plane, k):
        column = from_chip(k) * 2 + core
        block = slot(i, plane, column)
        pass_on(i, plane, block, column, k, chip).wait_recv()
        remote(block, block, send_a.at[i, plane, k], recv_a.at[i, plane, k], mate).start()
        return block, column

    def arrived(plane, way):
        for i in range(n_items):
            for k in near:
                block, column = arrive(i, plane, k)
                if square:

                    @pl.when(plane % 2 == k - 1)
                    def _():
                        pass_on(i, plane, block, column, 3, to_chip(3 - k)).start()

    def crossed(plane, way):
        for i in range(n_items):
            arrive(i, plane, 3)

    for d in range(n_dp):
        at_distance(d, arrived)
    if square:
        for d in range(n_dp):
            at_distance(d, crossed)

    for i in range(n_items):
        for plane in range(n_dp):
            for k in range(chips):
                column = (from_chip(k) if k else chip) * 2 + 1 - core
                block = slot(i, plane, column)
                remote(
                    block, block, send_a.at[i, plane, k], recv_a.at[i, plane, k], mate
                ).wait_recv()
        pltpu.make_async_copy(sources[i], slot(i, z, j), local.at[i]).wait()
    finish(targets, cut_in, cut_out)
    for i in range(n_items):
        for plane in range(n_dp):
            block = slot(i, plane, j)
            for k in range(1, chips):
                pass_on(i, plane, block, j, k, chip).wait_send()
            for k in range(chips):
                remote(
                    block, block, send_a.at[i, plane, k], recv_a.at[i, plane, k], mate
                ).wait_send()

            @pl.when((z < n_dp - 1) & (z >= plane))
            def _():
                along(i, plane, block, 0, 1).wait_send()

            @pl.when((z > 0) & (z <= plane))
            def _():
                along(i, plane, block, 1, -1).wait_send()

    for copy in copies + put:
        copy.wait()


def gather_call(
    n_dp,
    n_expert,
    items,
    shapes,
    places,
    cut_in,
    cut_shapes,
    cuts,
    aliases,
    number,
    stages,
    puts=nothing,
    finish=lambda items, ins, outs: None,
):
    chips = n_expert // 2
    n, m = len(items), len(cut_shapes)
    dma = pltpu.SemaphoreType.DMA
    anywhere = pl.BlockSpec(memory_space=pl.ANY)
    return pl.pallas_call(
        functools.partial(
            gather_kernel,
            n_dp,
            n_expert,
            n,
            places,
            cuts,
            puts,
            finish,
            len(cut_in),
            m,
            len(stages),
        ),
        out_shape=[*shapes, *cut_shapes],
        in_specs=[anywhere] * (n + len(cut_in)),
        out_specs=[anywhere] * (n + m),
        scratch_shapes=[
            dma((n, 2, n_dp)),
            dma((n, n_dp)),
            dma((n, n_dp, chips)),
            dma((n, n_dp, chips)),
            dma((n, n_dp, chips)),
            dma((n, n_dp, chips)),
            dma((n,)),
            dma((4, n_dp)),
            dma((4, n_dp)),
            dma((max(len(stages), 4), 2)),
            *[pltpu.VMEM(stage, jnp.bfloat16) for stage in stages],
        ],
        input_output_aliases=aliases,
        compiler_params=pltpu.CompilerParams(
            collective_id=number, has_side_effects=True, vmem_limit_bytes=BIG
        ),
    )(*items, *cut_in)


def scatter_kernel(
    n_dp, n_expert, n_arrays, items, n_cut, n_out, cuts, puts, middle, rings, n_rings, *refs
):
    n_items = len(items)
    z, j, chip, core = place_of()
    chips = n_expert // 2
    square = chips == 4
    to_chip, from_chip = other_chips(chip, chips)
    refs = list(refs)

    def take(count):
        taken = refs[:count]
        del refs[:count]
        return taken

    sources, cut_in, targets, cut_out = take(n_arrays), take(n_cut), take(n_arrays), take(n_out)
    ring, got_a, got_b, got_c = take(n_rings), take(n_items), take(n_items), take(n_items)
    transit = take(n_items)
    (
        send_a,
        recv_a,
        send_b,
        recv_b,
        send_c,
        recv_c,
        send_t,
        recv_t,
        local,
        send_x,
        recv_x,
        local_y,
        *stages,
    ) = refs
    greet(n_dp, n_expert)
    mate = (z, chip * 2 + 1 - core)
    order = [3, 1, 2, 0] if square else [*range(1, chips), 0]
    half = n_dp // 2
    low, high = pl.ds(0, half), pl.ds(half, n_dp - half)

    def chip_of(k):
        return to_chip(k) if k else chip

    def source(i, column):
        array, first, rows = items[i]
        return sources[array].at[:, column, pl.ds(first, rows)]

    def to_mate(i, k):
        return remote(
            source(i, chip_of(k) * 2 + 1 - core),
            got_a[i].at[k],
            send_a.at[i, k],
            recv_a.at[i, k],
            mate,
        )

    turn = [0] * n_rings
    loads = []
    for i in range(n_items):
        for k in order:
            loads.append((i, k, turn[rings[i]] % 2))
            turn[rings[i]] += 1

    def load(i, k, at):
        return pltpu.make_async_copy(
            source(i, chip_of(k) * 2 + core), ring[rings[i]].at[at], local.at[rings[i], at]
        )

    def send_near(i, k, part, number):
        return remote(
            got_a[i].at[k, part],
            got_b[i].at[k - 1, part],
            send_b.at[i, number],
            recv_b.at[i, number],
            (z, to_chip(k) * 2 + core),
        )

    def send_over(i, k, part):
        return remote(
            got_a[i].at[3, part],
            transit[i].at[k - 1],
            send_t.at[i, k],
            recv_t.at[i, k],
            (z, to_chip(k) * 2 + core),
        )

    def send_far(i, k):
        return remote(
            got_a[i].at[k],
            got_b[i].at[k - 1],
            send_b.at[i, k],
            recv_b.at[i, k],
            (z, to_chip(k) * 2 + core),
        )

    def along(i, plane, way):
        slot = n_dp - (z - 1) + plane if way else plane - (z + 1)
        return remote(
            got_a[i].at[0, plane],
            got_c[i].at[slot],
            send_c.at[i, plane],
            recv_c.at[i, slot],
            (z - 1 if way else z + 1, j),
        )

    def from_along(i, slot):
        return remote(
            got_c[i].at[slot], got_c[i].at[slot], send_c.at[i, 0], recv_c.at[i, slot], mate
        )

    f32 = jnp.float32

    def add(i, planes, target, terms):
        rows = got_a[i].shape[2]
        per = rows // 16

        def step(n, unused):
            plane = n // per
            at = pl.ds(pl.multiple_of((n % per) * 16, 16), 16)
            total = terms[0](plane, at).astype(f32)
            for term in terms[1:]:
                total = total + term(plane, at).astype(f32)
            target(plane, at, total)
            return unused

        lax.fori_loop(0, planes * per, step, 0)

    def grow(i, k, first, planes, term):
        def target(plane, at, total):
            got_a[i][k, plane + first, at] = total.astype(got_a[i].dtype)

        add(i, planes, target, [lambda plane, at: got_a[i][k, plane + first, at], term])

    for i in range(n_items):
        for k in order:
            to_mate(i, k).start()
    started = 0
    ahead = [0] * n_rings
    for i, k, at in loads:
        if ahead[rings[i]] < 2:
            load(i, k, at).start()
            ahead[rings[i]] += 1
    pairs = cuts(cut_in, cut_out)
    copies = exchange(n_dp, pairs, send_x, recv_x)
    own = [(source(z), target(z)) for source, target in pairs]
    bring, put = moves(own + puts(cut_in, cut_out), stages, local_y)
    for copy in bring:
        copy.start()

    def over_cores(i):
        for n, (item, k, at) in enumerate(loads):
            if item != i:
                continue
            load(i, k, at).wait()
            to_mate(i, k).wait_recv()
            grow(i, k, 0, n_dp, lambda plane, rows: ring[rings[i]][at, plane, rows])
            later = [one for one in loads[n + 1 :] if rings[one[0]] == rings[i]]
            if len(later) >= 2:
                load(*later[1]).start()
            if not k:
                continue
            if not square:
                send_far(i, k).start()
            elif k == 3:
                send_over(i, 1, low).start()
                send_over(i, 2, high).start()
            elif k == 1:
                send_near(i, 1, low, 0).start()
            else:
                send_near(i, 2, high, 1).start()

    def pass_over(i):
        if not square:
            return
        send_over(i, 2, high).wait_recv()
        grow(i, 1, half, n_dp - half, lambda plane, rows: transit[i][1, plane, rows])
        send_near(i, 1, high, 2).start()
        send_over(i, 1, low).wait_recv()
        grow(i, 2, 0, half, lambda plane, rows: transit[i][0, plane, rows])
        send_near(i, 2, low, 3).start()

    def over_chips(i):
        if square:
            send_near(i, 1, low, 0).wait_recv()
            send_near(i, 2, high, 1).wait_recv()
            send_near(i, 1, high, 2).wait_recv()
            send_near(i, 2, low, 3).wait_recv()
        else:
            for k in range(1, chips):
                send_far(i, k).wait_recv()
        heard = 2 if square else chips - 1

        def target(plane, at, total):
            got_a[i][0, plane, at] = total.astype(got_a[i].dtype)

        terms = [lambda plane, at: got_a[i][0, plane, at]]
        for other in range(heard):
            terms.append(lambda plane, at, other=other: got_b[i][other, plane, at])
        add(i, n_dp, target, terms)
        for d in range(n_dp - 1, 0, -1):
            for way in (0, 1):
                plane = z - d if way else z + d

                @pl.when(z == (n_dp - 1 if way else 0))
                def _():
                    along(i, plane, way).start()

    def over_planes(i):
        for d in range(n_dp - 2, 0, -1):
            for way in (0, 1):
                plane = z - d if way else z + d
                slot = n_dp - d if way else d

                @pl.when((plane >= 0) & (z < n_dp - 1) if way else (plane < n_dp) & (z > 0))
                def _():
                    from_along(i, slot).wait_recv()
                    grow(i, 0, plane, 1, lambda unused, at: got_c[i][slot, at])
                    along(i, plane, way).start()

    def finish(i):
        array, first, rows = items[i]

        def here(at):
            return pl.ds(pl.multiple_of(first + at.start, 16), 16)

        def own(unused, at, total):
            targets[array][here(at)] = total

        add(i, 1, own, [lambda unused, at: got_a[i][0, z, at]])
        for slot, arrives in ((0, z > 0), (n_dp, z < n_dp - 1)):

            @pl.when(arrives)
            def _():
                from_along(i, slot).wait_recv()
                add(
                    i,
                    1,
                    own,
                    [
                        lambda unused, at: targets[array][here(at)],
                        lambda unused, at: got_c[i][slot, at],
                    ],
                )

    steps = ((0, over_cores), (1, pass_over), (2, over_chips), (3, over_planes), (4, finish))
    if n_items >= 6:
        quotas = [-(-len(copies) * part // 9) for part in (2, 2, 2, 1, 1, 1)]
    else:
        quotas = [-(-len(copies) // n_items)] * n_items
    quotas += [0] * (n_items + len(steps) - len(quotas))
    for n in range(n_items + len(steps) - 1):
        for copy in copies[sum(quotas[:n]) : sum(quotas[: n + 1])]:
            copy.start()
        for late, step in steps:
            if 0 <= n - late < n_items:
                step(n - late)
        if n == min(1, n_items - 1):
            for one, other in zip(bring, put):
                one.wait()
                other.start()
            middle(cut_in, cut_out)
    for i in range(n_items):
        for k in range(chips):
            to_mate(i, k).wait_send()
        if square:
            for k, part in ((1, low), (2, high)):
                send_over(i, k, part).wait_send()
            for k, part, number in ((1, low, 0), (2, high, 1), (1, high, 2), (2, low, 3)):
                send_near(i, k, part, number).wait_send()
        else:
            for k in range(1, chips):
                send_far(i, k).wait_send()
        for plane in range(n_dp):

            @pl.when(z != plane)
            def _():
                remote(
                    got_a[i].at[0, plane],
                    got_c[i].at[0],
                    send_c.at[i, plane],
                    recv_c.at[i, 0],
                    mate,
                ).wait_send()

    for copy in copies + put:
        copy.wait()


def scatter_call(
    n_dp,
    n_expert,
    arrays,
    splits,
    cut_in,
    cut_shapes,
    cuts,
    number,
    aliases,
    stages,
    puts=nothing,
    middle=nothing,
):
    chips = n_expert // 2
    square = chips == 4
    items = []
    for array, (one, split) in enumerate(zip(arrays, splits)):
        rows = one.shape[2] // split
        items += [(array, first, rows) for first in range(0, one.shape[2], rows)]
    n, m = len(items), len(cut_shapes)
    count = len(arrays)
    dma = pltpu.SemaphoreType.DMA
    anywhere = pl.BlockSpec(memory_space=pl.ANY)
    blocks = [(rows, arrays[array].shape[3]) for array, unused, rows in items]
    kinds = sorted(set(blocks))
    rings = [kinds.index(block) for block in blocks]
    bf16 = jnp.bfloat16
    heard = 2 if square else chips - 1
    return pl.pallas_call(
        functools.partial(
            scatter_kernel,
            n_dp,
            n_expert,
            count,
            items,
            len(cut_in),
            m,
            cuts,
            puts,
            middle,
            rings,
            len(kinds),
        ),
        out_shape=[
            *[jax.ShapeDtypeStruct(one.shape[2:], jnp.float32) for one in arrays],
            *cut_shapes,
        ],
        in_specs=[anywhere] * (count + len(cut_in)),
        out_specs=[pl.BlockSpec(memory_space=pltpu.VMEM)] * count + [anywhere] * m,
        scratch_shapes=[
            *[pltpu.VMEM((2, n_dp, *kind), bf16) for kind in kinds],
            *[pltpu.VMEM((chips, n_dp, *block), bf16) for block in blocks],
            *[pltpu.VMEM((heard, n_dp, *block), bf16) for block in blocks],
            *[pltpu.VMEM((n_dp + 1, *block), bf16) for block in blocks],
            *[pltpu.VMEM((2, n_dp // 2, *(block if square else (16, 128))), bf16) for block in blocks],
            dma((n, chips)),
            dma((n, chips)),
            dma((n, chips)),
            dma((n, chips)),
            dma((n, n_dp)),
            dma((n, n_dp + 1)),
            dma((n, 3)),
            dma((n, 3)),
            dma((len(kinds), 2)),
            dma((16, n_dp)),
            dma((16, n_dp)),
            dma((max(len(stages), 16), 2)),
            *[pltpu.VMEM(stage, jnp.bfloat16) for stage in stages],
        ],
        input_output_aliases=aliases,
        compiler_params=pltpu.CompilerParams(
            collective_id=number, has_side_effects=True, vmem_limit_bytes=62 * 1024 * 1024
        ),
    )(*arrays, *cut_in)


def scatter_all(
    n_dp,
    n_expert,
    items,
    splits,
    cut_in,
    cut_shapes,
    cuts,
    number,
    aliases,
    stages,
    puts=nothing,
    middle=nothing,
):
    chips = n_expert // 2
    blocks = (2 * chips - 1 if chips != 4 else 7) * n_dp + n_dp + 3
    need = sum(blocks * item.shape[2] * item.shape[3] * 2 for item in items)
    kinds = {(item.shape[2] // split, item.shape[3]) for item, split in zip(items, splits)}
    need += sum(2 * n_dp * kind[0] * kind[1] * 2 for kind in kinds)
    need += sum(stage[0] * stage[1] * stage[2] * 2 for stage in stages)
    pieces = -(-need // (61 * 1024 * 1024))
    tiles = [item.shape[3] // 128 for item in items]
    results = [[] for item in items]
    extra = []
    for piece in range(pieces):
        ends = [(t * piece // pieces * 128, t * (piece + 1) // pieces * 128) for t in tiles]
        used = [i for i, (low, high) in enumerate(ends) if high > low]
        first = piece == 0
        outs = scatter_call(
            n_dp,
            n_expert,
            [items[i][..., ends[i][0] : ends[i][1]] if pieces > 1 else items[i] for i in used],
            [splits[i] for i in used],
            cut_in if first else [],
            cut_shapes if first else [],
            cuts if first else nothing,
            number + piece,
            {len(used) + a: len(used) + b for a, b in aliases} if first else {},
            stages if first else [],
            puts if first else nothing,
            middle if first else nothing,
        )
        for i, out in zip(used, outs):
            results[i].append(out)
        if first:
            extra = outs[len(used) :]
    return [one[0] if len(one) == 1 else jnp.concatenate(one, axis=1) for one in results], extra


def dot(left, right, dims):
    return lax.dot_general(
        left, right, ((dims[:1], dims[1:]), ((), ())), preferred_element_type=jnp.float32
    )


def picks(slots_ref, number):
    pair = slots_ref.shape[2]
    rows = lax.broadcasted_iota(jnp.int32, (2 * CAP, pair), 0)
    return [slots_ref[0, e : e + 1, :] == rows for e in range(number)]


def pick_kernel(number, experts_all, slots_ref, x_ref, g_ref, router_ref, rows_ref, grows_ref, gates_ref):
    chosen = picks(slots_ref, number)
    pick = jnp.concatenate(chosen, axis=0).astype(jnp.bfloat16)
    size = 2 * CAP
    x = x_ref[...]
    logits = dot(router_ref[...], x, (0, 1))
    names = lax.broadcasted_iota(jnp.int32, logits.shape, 0)
    logits = jnp.where(names < experts_all, logits, -1e30)
    weights = jnp.exp(logits - jnp.max(logits, axis=0, keepdims=True))
    probs = weights / jnp.sum(weights, axis=0, keepdims=True)
    for e in range(number):
        gate = jnp.sum(jnp.where(chosen[e], probs[e : e + 1, :], 0.0), axis=1, keepdims=True)
        gates_ref[e] = jnp.broadcast_to(gate, (size, 128))
    picked = dot(pick, x, (1, 0)).astype(jnp.bfloat16)
    for e in range(number):
        rows_ref[e] = picked[e * size : (e + 1) * size]
    picked = dot(pick, g_ref[...], (1, 0)).astype(jnp.bfloat16)
    for e in range(number):
        grows_ref[e] = picked[e * size : (e + 1) * size]


def expert_kernel(steps, half, n_weights, n_into, n_pack, names_ref, x_ref, g_ref, gates_ref, *refs):
    weights, refs = refs[:n_weights], refs[n_weights:]
    down_ref, refs = refs[0], refs[1 + n_into :]
    (
        y_ref,
        dx_ref,
        probs_ref,
        dgate_ref,
        dup_ref,
        ddown_ref,
        *pack_refs,
        sum_gate,
        sum_up,
    ) = refs
    bf16 = jnp.bfloat16
    g = g_ref[0]
    rows, width = x_ref.shape[1:]
    part = dgate_ref.shape[2]
    gate = gates_ref[0][:, :1]
    if n_weights == 2:
        piece = 512
        gate_ref, up_ref = weights
        gate_mid = dot(x_ref[0], gate_ref[0], (1, 0))
        up_mid = dot(x_ref[0], up_ref[0], (1, 0))
        spans = [
            (pl.ds(at, piece), gate_ref, up_ref, pl.ds(at, piece), pl.ds(0, part), pl.ds(0, part))
            for at in range(0, width, piece)
        ]
    else:
        piece = width // n_weights
        spans = []
        gate_mid = up_mid = 0.0
        for n, ref in enumerate(weights):
            span = pl.ds(pl.multiple_of(names_ref[1 + n], piece), piece)
            x_part = x_ref[0, :, span]
            gate_mid = gate_mid + dot(x_part, ref[0, :, :part], (1, 0))
            up_mid = up_mid + dot(x_part, ref[0, :, part:], (1, 0))
            spans.append((span, ref, ref, pl.ds(0, piece), pl.ds(0, part), pl.ds(part, part)))
    sigmoid = 1.0 / (1.0 + jnp.exp(-gate_mid))
    silu = gate_mid * sigmoid
    hidden = silu * up_mid
    hidden_low = hidden.astype(bf16)
    grad_plain = dot(g, down_ref[0], (1, 1))
    grad_gates = jnp.sum(grad_plain * hidden_low.astype(jnp.float32), axis=1, keepdims=True)
    high = grad_gates.astype(bf16).astype(jnp.float32)
    lane = lax.broadcasted_iota(jnp.int32, (rows, 128), 1)
    name = names_ref[0] + pl.program_id(0)
    probs_ref[0] = (
        jnp.where(lane == name, high, 0.0) + jnp.where(lane == name + half, grad_gates - high, 0.0)
    ).astype(bf16)
    grad_hidden = grad_plain * gate
    grad_gate = (
        grad_hidden * up_mid * sigmoid * (1.0 + gate_mid * (1.0 - sigmoid))
    ).astype(bf16)
    grad_up = (grad_hidden * silu).astype(bf16)
    scaled = (hidden * gate).astype(bf16)
    for at in range(0, width, piece):
        y_ref[0, :, at : at + piece] = (
            dot(hidden_low, down_ref[0, :, at : at + piece], (1, 0)) * gate
        ).astype(bf16)
    for span, gate_ref, up_ref, here, gate_columns, up_columns in spans:
        dx_ref[0, :, span] = (
            dot(grad_gate, gate_ref[0, here, gate_columns], (1, 1))
            + dot(grad_up, up_ref[0, here, up_columns], (1, 1))
        ).astype(bf16)
    step = pl.program_id(1)
    for span, *unused in spans:
        x_part = x_ref[0, :, span]
        here_gate = dot(x_part, grad_gate, (0, 0))
        here_up = dot(x_part, grad_up, (0, 0))
        here_down = dot(scaled, g_ref[0, :, span], (0, 0))
        if steps == 1:
            dgate_ref[0, span, :] = here_gate.astype(bf16)
            dup_ref[0, span, :] = here_up.astype(bf16)
            ddown_ref[0, :, span] = here_down
            continue

        @pl.when(step == 0)
        def _():
            sum_gate[span, :] = here_gate
            sum_up[span, :] = here_up
            ddown_ref[0, :, span] = here_down

        @pl.when(step > 0)
        def _():
            sum_gate[span, :] += here_gate
            sum_up[span, :] += here_up
            ddown_ref[0, :, span] += here_down

        @pl.when(step == steps - 1)
        def _():
            dgate_ref[0, span, :] = sum_gate[span, :].astype(bf16)
            dup_ref[0, span, :] = sum_up[span, :].astype(bf16)

    if n_pack:

        @pl.when((step == steps - 1) & (pl.program_id(0) < n_pack))
        def _():
            pack_ref = pack_refs[0]
            depth = pack_ref.shape[2]
            for plane in range(pack_ref.shape[0]):
                here = pl.ds(plane * depth, depth)
                pack_ref[plane, 0, :, :part] = dgate_ref[0, here, :]
                pack_ref[plane, 0, :, part:] = dup_ref[0, here, :]


def put_back(number, slots_ref, pairs):
    pick = jnp.concatenate(picks(slots_ref, number), axis=0).astype(jnp.bfloat16)
    piece = 512
    for source, target, first in pairs:
        width = source.shape[2]
        for at in range(0, width, piece):
            size = min(piece, width)
            part = source[:, :, at : at + size].reshape(-1, size)
            target[:, first + at : first + at + size] = dot(pick, part, (0, 0)).astype(
                jnp.bfloat16
            )


def place_back_kernel(number, slots_ref, dx_ref, probs_ref, back_ref):
    put_back(number, slots_ref, [(dx_ref, back_ref, 0), (probs_ref, back_ref, dx_ref.shape[2])])


def place_out_kernel(number, slots_ref, y_ref, out_ref):
    put_back(number, slots_ref, [(y_ref, out_ref, 0)])


def place_out(slots, y, out):
    pairs, number, pair = slots.shape
    pltpu.emit_pipeline(
        functools.partial(place_out_kernel, number),
        grid=(pairs,),
        in_specs=[
            pl.BlockSpec((1, number, pair), lambda p: (p, 0, 0)),
            pl.BlockSpec((number, 2 * CAP, D), lambda p: (0, p, 0)),
        ],
        out_specs=[pl.BlockSpec((pair, D), lambda p: (p, 0))],
    )(slots, y, out)


def pick_shapes(number, pairs):
    bf16 = jnp.bfloat16
    size = 2 * CAP
    return [
        jax.ShapeDtypeStruct((number, pairs * size, D), bf16),
        jax.ShapeDtypeStruct((number, pairs * size, D), bf16),
        jax.ShapeDtypeStruct((number, pairs * size, 128), jnp.float32),
    ]


def pick_rows(number, experts_all, slots, x_all, g_all, router, rows, grows, gates):
    pairs, _, pair = slots.shape
    size = 2 * CAP
    tokens = pl.BlockSpec((pair, D), lambda p: (p, 0))
    picked = pl.BlockSpec((number, size, D), lambda p: (0, p, 0))
    pltpu.emit_pipeline(
        functools.partial(pick_kernel, number, experts_all),
        grid=(pairs,),
        in_specs=[
            pl.BlockSpec((1, number, pair), lambda p: (p, 0, 0)),
            tokens,
            tokens,
            pl.BlockSpec(router.shape, lambda p: (0, 0)),
        ],
        out_specs=[picked, picked, pl.BlockSpec((number, size, 128), lambda p: (0, p, 0))],
    )(slots, x_all, g_all, router, rows, grows, gates)


def expert_call(names, half, low, number, rows, grows, gates, weights, down, into=(), pack=()):
    total, depth, _ = rows.shape
    part = down.shape[1]
    size = depth
    while size > 768:
        size //= 2
    steps = depth // size
    bf16 = jnp.bfloat16
    f32 = jnp.float32

    def from_rows(width):
        return pl.BlockSpec((1, size, width), lambda e, r: (e + low, r, 0))

    def whole(*shape):
        return pl.BlockSpec((1, *shape), lambda e, r: (e, 0, 0))

    def from_whole(*shape):
        return pl.BlockSpec((1, *shape), lambda e, r: (e + low, 0, 0))

    packed = [
        pl.BlockSpec(
            (planes, 1, D // planes, 2 * part),
            lambda e, r, n=n: (0, lax.min(e, n - 1), 0, 0),
        )
        for n, planes in ([pack] if pack else [])
    ]
    keep = (D, part) if steps > 1 else (16, 128)
    return pl.pallas_call(
        functools.partial(
            expert_kernel, steps, half, len(weights), len(into), pack[0] if pack else 0
        ),
        grid=(number, steps),
        in_specs=[
            pl.BlockSpec(memory_space=pltpu.SMEM),
            from_rows(D),
            from_rows(D),
            from_rows(128),
            *[(from_whole if len(weights) == 2 else whole)(*one.shape[1:]) for one in weights],
            from_whole(part, D),
            *[pl.BlockSpec(memory_space=pl.ANY)] * len(into),
        ],
        out_specs=[
            from_rows(D),
            from_rows(D),
            from_rows(128),
            whole(D, part),
            whole(D, part),
            from_whole(part, D),
            *packed,
        ],
        out_shape=[
            jax.ShapeDtypeStruct((total, depth, D), bf16),
            jax.ShapeDtypeStruct((total, depth, D), bf16),
            jax.ShapeDtypeStruct((total, depth, 128), bf16),
            jax.ShapeDtypeStruct((number, D, part), bf16),
            jax.ShapeDtypeStruct((number, D, part), bf16),
            jax.ShapeDtypeStruct((total, part, D), f32),
            *[
                jax.ShapeDtypeStruct((planes, n, D // planes, 2 * part), bf16)
                for n, planes in ([pack] if pack else [])
            ],
        ],
        input_output_aliases={
            5 + len(weights) + i: out for i, out in zip(range(len(into)), (0, 1, 2, 5))
        },
        scratch_shapes=[pltpu.VMEM(keep, f32), pltpu.VMEM(keep, f32)],
        compiler_params=pltpu.CompilerParams(vmem_limit_bytes=BIG),
    )(names, rows, grows, gates, *weights, down, *into)


def place_back(slots, dx, probs):
    pairs, number, pair = slots.shape
    size = 2 * CAP

    def rows(one):
        return pl.BlockSpec((number, size, one.shape[2]), lambda p: (0, p, 0))

    return pl.pallas_call(
        functools.partial(place_back_kernel, number),
        grid=(pairs,),
        in_specs=[pl.BlockSpec((1, number, pair), lambda p: (p, 0, 0)), rows(dx), rows(probs)],
        out_specs=pl.BlockSpec((pair, D + 128), lambda p: (p, 0)),
        out_shape=jax.ShapeDtypeStruct((pairs * pair, D + 128), jnp.bfloat16),
        compiler_params=pltpu.CompilerParams(vmem_limit_bytes=BIG),
    )(slots, dx, probs)


def core_back_kernel(
    scale,
    q_ref,
    k_ref,
    v_ref,
    grad_ref,
    probs_ref,
    cos_ref,
    sin_ref,
    q_raw_ref,
    k_raw_ref,
    q_inverse_ref,
    k_inverse_ref,
    q_gain_ref,
    k_gain_ref,
    grad_q_ref,
    grad_k_ref,
    grad_v_ref,
    grad_q_gain_ref,
    grad_k_gain_ref,
    q_turned,
    k_turned,
):
    bf16 = jnp.bfloat16
    cosine, sine = cos_ref[...], sin_ref[...]
    for head in range(HEADS):
        at = slice(head * HD, (head + 1) * HD)
        probs, grad = probs_ref[head], grad_ref[:, at]
        weights = dot(grad, v_ref[:, at], (1, 1))
        scores = probs * (weights - jnp.sum(probs * weights, axis=1, keepdims=True))
        scores = scores.astype(bf16)
        grad_v_ref[:, at] = dot(probs.astype(bf16), grad, (0, 0)).astype(bf16)
        for other_ref, side, turned in ((k_ref, 1, q_turned), (q_ref, 0, k_turned)):
            rope = dot(scores, other_ref[:, at], (side, 0)) * scale
            turned[:, at] = rope * cosine + pltpu.roll(rope, HD // 2, 1) * sine
    for turned, raw_ref, inverse_ref, gain_ref, out_ref, out_gain_ref in (
        (q_turned, q_raw_ref, q_inverse_ref, q_gain_ref, grad_q_ref, grad_q_gain_ref),
        (k_turned, k_raw_ref, k_inverse_ref, k_gain_ref, grad_k_ref, grad_k_gain_ref),
    ):
        grad, raw, inverse = turned[...], raw_ref[...], inverse_ref[...]
        scaled = grad * gain_ref[...]
        inner = jnp.mean(scaled * raw, axis=1, keepdims=True)
        out_ref[...] = (inverse * scaled - raw * (inverse * inverse * inverse) * inner).astype(bf16)
        out_gain_ref[...] = jnp.sum(grad * raw * inverse, axis=0, keepdims=True)


def core_back(scale, q, k, v, grad, probs, cosine, sine, q_raw, k_raw, q_inverse, k_inverse, gains):
    count, depth = q.shape
    low = jax.ShapeDtypeStruct((count, depth), jnp.bfloat16)
    gain = jax.ShapeDtypeStruct((1, depth), jnp.float32)
    return pl.pallas_call(
        functools.partial(core_back_kernel, scale),
        out_shape=[low, low, low, gain, gain],
        scratch_shapes=[pltpu.VMEM((count, depth), jnp.float32)] * 2,
        compiler_params=pltpu.CompilerParams(vmem_limit_bytes=BIG),
    )(
        q,
        k,
        v,
        grad,
        probs,
        jnp.concatenate([cosine, cosine], axis=1),
        jnp.concatenate([sine, -sine], axis=1),
        q_raw,
        k_raw,
        q_inverse,
        k_inverse,
        *[one[None] for one in gains],
    )


def through_kernel(count, *refs):
    lefts, weight_ref, out_ref = refs[:count], refs[count], refs[count + 1]
    for i in range(count):

        @pl.when(pl.program_id(1) == i)
        def _():
            part = dot(lefts[i][...], weight_ref[0], (1, 1))
            if i:
                part = part + out_ref[...]
            out_ref[...] = part.astype(out_ref.dtype)


def through(lefts, weights, first, kind=jnp.float32):
    count, (rows, depth) = len(lefts), lefts[0].shape
    piece = 512
    return pl.pallas_call(
        functools.partial(through_kernel, count),
        grid=(depth // piece, count),
        in_specs=[
            *[pl.BlockSpec((rows, depth), lambda c, i: (0, 0))] * count,
            pl.BlockSpec((1, piece, depth), lambda c, i: (i + first, c, 0)),
        ],
        out_specs=pl.BlockSpec((rows, piece), lambda c, i: (0, c)),
        out_shape=jax.ShapeDtypeStruct((rows, depth), kind),
        compiler_params=pltpu.CompilerParams(vmem_limit_bytes=BIG),
    )(*lefts, weights)


def outer_kernel(which, n_left, *refs):
    lefts, rights = refs[:n_left], refs[n_left : n_left + len(which)]
    piece = 512
    for left, right, out_ref in zip(which, rights, refs[n_left + len(which) :]):
        for at in range(0, out_ref.shape[1], piece):
            out_ref[:, at : at + piece] = dot(
                lefts[left][...], right[:, at : at + piece], (0, 0)
            ).astype(out_ref.dtype)


def outer(lefts, rights, which):
    rows, depth = lefts[0].shape
    piece = 256
    return pl.pallas_call(
        functools.partial(outer_kernel, which, len(lefts)),
        grid=(depth // piece,),
        in_specs=[
            *[pl.BlockSpec((rows, piece), lambda c: (0, c))] * len(lefts),
            *[pl.BlockSpec((rows, depth), lambda c: (0, 0))] * len(rights),
        ],
        out_specs=[pl.BlockSpec((piece, depth), lambda c: (c, 0))] * len(rights),
        out_shape=[jax.ShapeDtypeStruct((depth, depth), jnp.bfloat16)] * len(rights),
        compiler_params=pltpu.CompilerParams(vmem_limit_bytes=BIG),
    )(*lefts, *rights)


def widen_kernel(*refs):
    for source, target in zip(refs[:2], refs[-2:]):
        target[...] = source[...].astype(jnp.float32)


def widen(low, high, values, into=()):
    number, rows, columns = values[0].shape
    block = pl.BlockSpec((1, rows, columns), lambda e: (e + low, 0, 0))
    return pl.pallas_call(
        widen_kernel,
        grid=(high - low,),
        in_specs=[block] * 2 + [pl.BlockSpec(memory_space=pl.ANY)] * len(into),
        out_specs=[block] * 2,
        out_shape=[jax.ShapeDtypeStruct(one.shape, jnp.float32) for one in values],
        input_output_aliases={2 + i: i for i in range(len(into))},
        compiler_params=pltpu.CompilerParams(vmem_limit_bytes=BIG),
    )(*values, *into)


def widen_pieces_kernel(low, n_pieces, offsets_ref, *refs):
    pieces, refs = refs[:n_pieces], refs[n_pieces + 2 :]
    targets, wide, sems = refs[:2], refs[2], refs[3]
    part = wide.shape[4]
    copies = []
    for k, piece in enumerate(pieces):
        columns = pl.ds(pl.multiple_of(offsets_ref[k], part), part)
        for n in range(2):
            wide[k, n] = piece[:, :, n * part : (n + 1) * part].astype(jnp.float32)
            copy = pltpu.make_async_copy(
                wide.at[k, n], targets[n].at[pl.ds(low, piece.shape[0]), :, columns], sems.at[k, n]
            )
            copy.start()
            copies.append(copy)
    for copy in copies:
        copy.wait()


def widen_pieces(offsets, low, pieces, into):
    size, rows, columns = pieces[0].shape
    anywhere = pl.BlockSpec(memory_space=pl.ANY)
    count = len(pieces)
    return pl.pallas_call(
        functools.partial(widen_pieces_kernel, low, count),
        in_specs=[
            pl.BlockSpec(memory_space=pltpu.SMEM),
            *[pl.BlockSpec(memory_space=pltpu.VMEM)] * count,
            anywhere,
            anywhere,
        ],
        out_specs=[anywhere, anywhere],
        out_shape=[jax.ShapeDtypeStruct(one.shape, one.dtype) for one in into],
        scratch_shapes=[
            pltpu.VMEM((count, 2, size, rows, columns // 2), jnp.float32),
            pltpu.SemaphoreType.DMA((count, 2)),
        ],
        input_output_aliases={1 + count: 0, 2 + count: 1},
        compiler_params=pltpu.CompilerParams(vmem_limit_bytes=BIG),
    )(offsets, *pieces, *into)


def shards(
    n_dp,
    n_expert,
    tokens,
    cotangent,
    lengths,
    routes,
    w_query,
    w_key,
    w_value,
    w_out,
    w_router,
    gain_attn,
    gain_query,
    gain_key,
    gain_mlp,
    w_gate,
    w_up,
    w_down,
):
    groups = n_dp * n_expert
    bf16 = jnp.bfloat16
    number = w_gate.shape[0]
    ff = w_gate.shape[2]
    part = ff // n_dp
    experts_all = w_router.shape[1]
    width = 128
    small = jnp.concatenate(
        [
            w_router,
            gain_attn[:, None],
            gain_query[:, None],
            gain_key[:, None],
            gain_mlp[:, None],
            jnp.zeros((w_router.shape[0], width - experts_all - 4), bf16),
        ],
        axis=1,
    )
    hits = jnp.any(
        routes[:, :, None] == jnp.arange(width, dtype=jnp.int32)[None, None, :], axis=1
    ).astype(bf16)
    count = tokens.shape[0]
    rows_each = w_query.shape[0]
    extras = jnp.concatenate([hits, jnp.pad(small, ((0, count - rows_each), (0, 0)))], axis=1)
    weights = jnp.stack([w_query, w_key, w_value, w_out])
    depth = w_gate.shape[1]
    early = number // 4
    beside = early + number // 8
    late = number - number // 4
    back_beside = number // 8
    back_third = back_beside + max(number // 4, 1)
    back_late = back_third + number // 4
    me = lax.axis_index("dp")
    cut_shape = jax.ShapeDtypeStruct((number, n_dp * depth, part), bf16)

    def row_block(size):
        return lambda ref, block: ref.at[pl.ds(pl.multiple_of(block * size, 16), size)]

    def columns_at(at):
        return pl.ds(pl.multiple_of(at * part, part), part)

    def rows_at(at):
        return pl.ds(pl.multiple_of(at * depth, depth), depth)

    def recut(low, high):
        def cuts(ins, outs):
            def pair(n):
                chosen = pl.ds(low, high - low)
                return (
                    lambda to: ins[n].at[chosen, :, columns_at(to)],
                    lambda at: outs[n].at[chosen, rows_at(at)],
                )

            return [pair(0), pair(1)]

        return cuts

    to_plane, from_plane = partners(me, n_dp)

    def permuted(pieces, chained=False):
        got = []
        for k, piece in enumerate(pieces, 1):
            if chained and got:
                piece, last = lax.optimization_barrier((piece, got.pop()))
                got.append(last)
            paths = [(i, partners(i, n_dp)[0](k)) for i in range(n_dp)]
            got.append(lax.ppermute(piece, "dp", paths))
        return got

    def cut_pieces(low, high, first_k, ins, outs):
        to, unused = partners(lax.axis_index("dp"), n_dp)
        pairs = []
        for k, piece in enumerate(outs, first_k):
            for n in range(2):
                source = ins[n].at[pl.ds(low, high - low), :, columns_at(to(k))]
                pairs.append((source, piece.at[:, :, pl.ds(n * part, part)]))
        return pairs

    def piece_shapes(size, first_k):
        shape = jax.ShapeDtypeStruct((size, depth, 2 * part), bf16)
        return [shape] * (n_dp - first_k if size else 0)

    def stages(*sizes):
        return [(size, depth, part) for size in sizes]

    soon_shapes = piece_shapes(beside - early, 1)
    late_shapes = piece_shapes(number - late, 0)
    n_soon = len(soon_shapes)

    weights_all, extras_all, gate_early, up_early, *pieces = gather_call(
        n_dp,
        n_expert,
        [weights, extras],
        [
            jax.ShapeDtypeStruct((4, groups * rows_each, D), bf16),
            jax.ShapeDtypeStruct((groups * count, 2 * width), bf16),
        ],
        [
            lambda ref, block: ref.at[
                :, pl.ds(pl.multiple_of(block * rows_each, 16), rows_each)
            ],
            row_block(count),
        ],
        [w_gate, w_up],
        [cut_shape, cut_shape, *soon_shapes, *late_shapes],
        recut(0, early),
        {},
        0,
        stages(
            *[early] * 2,
            *[beside - early] * (2 * n_soon),
            *[number - late] * (2 * n_dp),
        ),
        lambda ins, outs: cut_pieces(early, beside, 1, ins, outs[2 : 2 + n_soon])
        + cut_pieces(late, number, 0, ins, outs[2 + n_soon :]),
    )
    soon_pieces, late_pieces = pieces[:n_soon], pieces[n_soon:]
    small_all = (
        extras_all[:, width:].reshape(groups, count, width)[:, :rows_each].reshape(-1, width)
    )
    hits_all = extras_all[:, :experts_all]
    router_weight = small_all[:, :experts_all]
    gains = small_all[:, experts_all : experts_all + 4].astype(jnp.float32)
    gains = lax.optimization_barrier(jnp.transpose(gains))
    attn_gain, query_gain, key_gain, mlp_gain = (gains[i] for i in range(4))
    inputs = tokens.astype(jnp.float32)
    segment, position, places = layout(lengths[0], count)
    half = HD // 2
    freq = 10000.0 ** (-2.0 * jnp.arange(half, dtype=jnp.float32) / HD)
    angle = position.astype(jnp.float32)[:, None] * freq[None, :]
    cosine = jnp.cos(angle)[:, None, :]
    sine = jnp.sin(angle)[:, None, :]
    scale = HD ** (-0.5)
    normed, attn_inverse = rms_forward(inputs, attn_gain)
    normed_low = normed.astype(bf16)
    query_raw = product(normed_low, weights_all[0], "td,de->te")
    key_raw = product(normed_low, weights_all[1], "td,de->te")
    value_low = product(normed_low, weights_all[2], "td,de->te").astype(bf16)
    query_normed, query_inverse = rms_forward(query_raw, query_gain)
    key_normed, key_inverse = rms_forward(key_raw, key_gain)
    query_low = rotate(query_normed, cosine, sine).astype(bf16).reshape(count, HEADS, HD)
    key_low = rotate(key_normed, cosine, sine).astype(bf16).reshape(count, HEADS, HD)
    value_heads = value_low.reshape(count, HEADS, HD)
    allowed = (segment[:, None] == segment[None, :]) & (places[None, :] <= places[:, None])
    scores = product(query_low, key_low, "qhd,khd->hqk") * scale
    scores = jnp.where(allowed[None], scores, -1e30)
    probs = jax.nn.softmax(scores, axis=-1)
    probs_low = probs.astype(bf16)
    attended_low = product(probs_low, value_heads, "hqk,khd->qhd").reshape(count, D).astype(bf16)
    middle = inputs + product(attended_low, weights_all[3], "td,de->te")
    mlp_normed, mlp_inverse = rms_forward(middle, mlp_gain)
    mlp_low = mlp_normed.astype(bf16)
    router = jax.nn.softmax(product(mlp_low, router_weight, "td,de->te"), axis=-1)

    first = lax.axis_index("expert") * number
    hit = lax.dynamic_slice_in_dim(hits_all, first, number, 1).reshape(groups, count, number)
    before = jnp.tril(jnp.ones((count, count), bf16), -1)
    slot = product(before, hit, "ts,bse->bet").astype(jnp.int32)
    slot = jnp.where(jnp.transpose(hit, (0, 2, 1)) > 0, slot, -1)
    slot = slot.reshape(groups // 2, 2, number, count)
    shift = jnp.array([0, CAP], jnp.int32)[None, :, None, None]
    slots = jnp.transpose(jnp.where(slot < 0, -1, slot + shift), (0, 2, 1, 3))
    slots = slots.reshape(groups // 2, number, 2 * count)
    router_own = jnp.pad(
        jnp.roll(router_weight, -first, axis=1), ((0, 0), (0, width - experts_all))
    )
    if n_soon:
        mlp_low, *soon_pieces = lax.optimization_barrier((mlp_low, *permuted(soon_pieces)))

    def put_weights(ins, outs):
        chosen = pl.ds(early, beside - early)
        unused, heard = partners(lax.axis_index("dp"), n_dp)
        pairs = []
        if beside > early:
            own = lax.axis_index("dp")
            for n in range(2):
                source = ins[n].at[chosen, :, columns_at(own)]
                pairs.append((source, outs[n].at[chosen, rows_at(own)]))
        for k, piece in enumerate(ins[6:], 1):
            for n in range(2):
                columns = piece.at[:, :, pl.ds(n * part, part)]
                pairs.append((columns, outs[n].at[chosen, rows_at(heard(k))]))
        return pairs

    def pick_all(items, ins, outs):
        pick_rows(number, experts_all, ins[4], *items, ins[5], *outs[2:])

    unused, unused, gate_cut, up_cut, rows, grows, gates = gather_call(
        n_dp,
        n_expert,
        [mlp_low, cotangent],
        [jax.ShapeDtypeStruct((groups * count, D), bf16)] * 2,
        [row_block(count)] * 2,
        [w_gate, w_up, gate_early, up_early, slots, router_own, *soon_pieces],
        [cut_shape, cut_shape, *pick_shapes(number, groups // 2)],
        recut(beside, late),
        {4: 2, 5: 3},
        1,
        stages(*[late - beside] * 2, *[beside - early] * (2 * n_dp if n_soon else 0)),
        put_weights,
        pick_all,
    )
    *late_pieces, rows = lax.optimization_barrier((*late_pieces, rows))
    late_pieces = [late_pieces[0], *permuted(late_pieces[1:])]
    packing = back_beside > 0 and depth == 512
    *outs, gate_soon, up_soon, down_soon = expert_call(
        first[None],
        experts_all,
        0,
        late,
        rows,
        grows,
        gates,
        [gate_cut, up_cut],
        w_down,
        pack=(back_beside, n_dp) if packing else (),
    )
    if packing:
        *outs, gate_soon, up_soon, down_soon, packed = [*outs, gate_soon, up_soon, down_soon]
    offsets = [from_plane(k) * depth for k in range(n_dp)]
    weighted, grad_rows, grad_gates, gate_rest, up_rest, grad_down_part = expert_call(
        jnp.stack([first + late, *offsets]),
        experts_all,
        late,
        number - late,
        rows,
        grows,
        gates,
        late_pieces,
        w_down,
        [*outs, down_soon],
    )
    part_back = place_back(slots, grad_rows, grad_gates)

    def ways(low, high, at, ins, outs):
        def pair(e, n):
            return (
                lambda to: ins[n].at[pl.ds(e, 1), rows_at(to)],
                lambda here: outs[n].at[pl.ds(e + at, 1), :, columns_at(here)],
            )

        return [pair(e, n) for e in range(low, high) for n in range(2)]

    def cut_grads(low, high, ins, outs):
        to, unused = partners(lax.axis_index("dp"), n_dp)
        pairs = []
        for k, piece in enumerate(outs):
            for n in range(2):
                source = ins[n].at[pl.ds(low, high - low), rows_at(to(k))]
                pairs.append((source, piece.at[:, :, pl.ds(n * part, part)]))
        return pairs

    pieces = []
    if back_beside:
        for k in range(n_dp):
            if packing:
                piece = lax.dynamic_index_in_dim(packed, to_plane(k), 0, False)
            else:
                piece = jnp.concatenate(
                    [
                        lax.dynamic_slice_in_dim(
                            one[:back_beside], to_plane(k) * depth, depth, 1
                        )
                        for one in (gate_soon, up_soon)
                    ],
                    axis=2,
                )
            pieces.append(piece)
        ahead = lax.optimization_barrier((*pieces[1:], *late_pieces[1:]))
        pieces = [pieces[0], *permuted(ahead[: n_dp - 1])]
        part_back, *pieces = lax.optimization_barrier((part_back, *pieces))
    way_shapes = [jax.ShapeDtypeStruct((number, depth, ff), bf16)] * 2
    piece_shape = jax.ShapeDtypeStruct((back_late - back_third, depth, 2 * part), bf16)
    (back,), (gate_third, up_third, part_out, *later_pieces) = scatter_all(
        n_dp,
        n_expert,
        [part_back.reshape(n_dp, n_expert, count, D + width)],
        [4],
        [gate_soon, up_soon, slots, weighted],
        [
            *way_shapes,
            jax.ShapeDtypeStruct((groups * count, D), bf16),
            *[piece_shape] * n_dp,
        ],
        lambda ins, outs: ways(back_beside, back_third, 0, ins, outs),
        8,
        (),
        stages(
            *[1] * (2 * (back_third - back_beside)),
            *[back_late - back_third] * (2 * n_dp),
        ),
        lambda ins, outs: cut_grads(back_third, back_late, ins, outs[3:]),
        lambda ins, outs: place_out(ins[2], ins[3], outs[2]),
    )
    later_pieces = [later_pieces[0], *permuted(later_pieces[1:])]

    offsets = jnp.stack([from_plane(k) * part for k in range(n_dp)])
    widened = widen(back_beside, back_third, [gate_third, up_third])
    if back_beside:
        widened = widen_pieces(offsets, 0, pieces, widened)
    part_out, *widened = lax.optimization_barrier((part_out, *widened))

    def attention_back(back):
        grad_final = cotangent.astype(jnp.float32)
        grad_mlp = back[:, :D]
        grad_router_probs = back[:, D : D + experts_all] + back[:, D + experts_all :]
        grad_logits = router * (
            grad_router_probs - jnp.sum(router * grad_router_probs, axis=1, keepdims=True)
        )
        grad_logits_low = grad_logits.astype(bf16)
        grad_router_full = product(
            mlp_low, jnp.pad(grad_logits_low, ((0, 0), (0, width - experts_all))), "td,te->de"
        )
        grad_mlp = grad_mlp + product(grad_logits_low, router_weight, "te,de->td")
        grad_middle_part, grad_mlp_gain = rms_backward(middle, mlp_inverse, mlp_gain, grad_mlp)
        grad_middle = grad_final + grad_middle_part
        grad_branch_low = grad_middle.astype(bf16)
        grad_attended = through([grad_branch_low], weights_all, 3, bf16)
        grad_query_low, grad_key_low, grad_value_low, grad_query_gain, grad_key_gain = core_back(
            scale,
            query_low.reshape(count, D),
            key_low.reshape(count, D),
            value_low,
            grad_attended,
            probs,
            cosine[:, 0],
            sine[:, 0],
            query_raw,
            key_raw,
            query_inverse,
            key_inverse,
            (query_gain, key_gain),
        )
        full_grads = outer(
            [attended_low, normed_low],
            [grad_branch_low, grad_value_low, grad_key_low, grad_query_low],
            (0, 1, 1, 1),
        )
        grad_normed = through([grad_query_low, grad_key_low, grad_value_low], weights_all, 0)
        grad_inputs_part, grad_attn_gain = rms_backward(inputs, attn_inverse, attn_gain, grad_normed)
        grad_inputs = grad_middle + grad_inputs_part

        gain_grads = jnp.stack(
            [grad_attn_gain, grad_query_gain[0], grad_key_gain[0], grad_mlp_gain]
        )
        gain_grads = jnp.transpose(gain_grads.reshape(4, groups, rows_each), (1, 0, 2))
        gain_grads = jnp.pad(gain_grads, ((0, 0), (0, 12), (0, width - rows_each)))
        return (
            grad_inputs,
            *full_grads,
            grad_router_full.astype(bf16),
            gain_grads.astype(bf16).reshape(groups * 16, width),
        )

    def unreached(back):
        shapes = [(count, D)] + [(D, D)] * 4 + [(D, width), (groups * 16, width)]
        kinds = [jnp.float32] + [bf16] * 6
        return tuple(jnp.zeros(shape, kind) for shape, kind in zip(shapes, kinds))

    grad_inputs, *weight_grads = lax.cond(lengths[0, 0] > 0, attention_back, unreached, back)

    def blocks_of(value):
        return value.reshape(n_dp, n_expert, -1, value.shape[1])

    sums, (gate_back, up_back) = scatter_all(
        n_dp,
        n_expert,
        [part_out.reshape(n_dp, n_expert, count, D)]
        + [blocks_of(value) for value in weight_grads],
        [2, 1, 1, 1, 2 if rows_each > 16 else 1, 1, 1],
        [gate_soon, up_soon, gate_rest, up_rest],
        way_shapes,
        lambda ins, outs: ways(back_late, late, 0, ins[:2], outs)
        + ways(0, number - late, late, ins[2:], outs),
        16,
        (),
        [],
    )
    summed, grad_out_part, grad_value_part, grad_key_part, grad_query_part, router_part, small = sums
    output = (middle + summed).astype(bf16)
    grad_router_part = router_part[:, :experts_all]
    gain_parts = [small[i, :rows_each] for i in range(4)]
    widened = widen(back_late, number, [gate_back, up_back], widened)
    if back_late > back_third:
        widened = widen_pieces(offsets, back_third, later_pieces, widened)
    grad_gate_part, grad_up_part = widened
    return (
        output,
        grad_inputs,
        grad_query_part,
        grad_key_part,
        grad_value_part,
        grad_out_part,
        grad_router_part,
        gain_parts[0],
        gain_parts[1],
        gain_parts[2],
        gain_parts[3],
        grad_gate_part,
        grad_up_part,
        grad_down_part,
    )


def solution(mesh):
    return jax.shard_map(
        functools.partial(shards, mesh.shape["dp"], mesh.shape["expert"]),
        mesh=mesh,
        in_specs=(
            P(("dp", "expert"), None),
            P(("dp", "expert"), None),
            P(("dp", "expert"), None),
            P(("dp", "expert"), None),
            P(("dp", "expert"), None),
            P(("dp", "expert"), None),
            P(("dp", "expert"), None),
            P(("dp", "expert"), None),
            P(("dp", "expert"), None),
            P(("dp", "expert")),
            P(("dp", "expert")),
            P(("dp", "expert")),
            P(("dp", "expert")),
            P("expert", "dp", None),
            P("expert", "dp", None),
            P("expert", "dp", None),
        ),
        out_specs=(
            P(("dp", "expert"), None),
            P(("dp", "expert"), None),
            P(("dp", "expert"), None),
            P(("dp", "expert"), None),
            P(("dp", "expert"), None),
            P(("dp", "expert"), None),
            P(("dp", "expert"), None),
            P(("dp", "expert")),
            P(("dp", "expert")),
            P(("dp", "expert")),
            P(("dp", "expert")),
            P("expert", "dp", None),
            P("expert", "dp", None),
            P("expert", "dp", None),
        ),
        check_vma=False,
    )
```
